32 devices in a mesh: grp: 8 (over y, x, core), shard: 4 (over z).
Axes of the slice: x: 2, y: 2, z: 4, core: 2. Of those that a mesh axis runs over, the one named last changes fastest.
Arguments:
- x_in: bfloat16 [7168, 2048], P(('grp', 'shard')), may hold values from -6 to 6
- d_out: bfloat16 [7168, 2048], P(('grp', 'shard')), may hold values from -6 to 6
- w_qkv: bfloat16 [2048, 6144], P(('grp', 'shard')), may hold values from -0.125 to 0.125
- w_dense: bfloat16 [2048, 2048], P(('grp', 'shard')), may hold values from -6 to 6
- w_in: bfloat16 [2048, 10922], P(('grp', 'shard')), may hold values from -0.125 to 0.125
- w_out: bfloat16 [2048, 5461], P(('grp', 'shard')), may hold values from -1 to 1
- gain_one: bfloat16 [2048], P(('grp', 'shard')), may hold values from 0.5 to 1.5
- bias_one: bfloat16 [2048], P(('grp', 'shard')), may hold values from -1 to 1
- gain_two: bfloat16 [2048], P(('grp', 'shard')), may hold values from 0.5 to 1.5
- bias_two: bfloat16 [2048], P(('grp', 'shard')), may hold values from -1 to 1
- mlm_flags: int32 [7168], P(('grp', 'shard')), may hold values from 0 to 1, as said below
- span_start: int32 [32], P(('grp', 'shard')), may hold values from 0 to 111, as said below
- span_len: int32 [32], P(('grp', 'shard')), may hold values from 28 to 112, as said below
Outputs:
- layer_out: bfloat16 [7168, 2048], P(('grp', 'shard'))
- d_input: bfloat16 [7168, 2048], P(('grp', 'shard'))
- d_w_qkv: float32 [2048, 6144], P(('grp', 'shard'))
- d_w_dense: float32 [2048, 2048], P(('grp', 'shard'))
- d_w_in: float32 [2048, 10922], P(('grp', 'shard'))
- d_w_out: float32 [2048, 5461], P(('grp', 'shard'))
- d_gain_one: float32 [2048], P(('grp', 'shard'))
- d_bias_one: float32 [2048], P(('grp', 'shard'))
- d_gain_two: float32 [2048], P(('grp', 'shard'))
- d_bias_two: float32 [2048], P(('grp', 'shard'))
The draws below stay inside these ranges and needn't reach their ends.
Inputs may be any that keep to these rules, and one draw needn't show every extreme that they name: `mlm_flags`: flags are 1 only in max(1, 6) sequences, the MLM ones, and there the first token's flag is always 1. `span_len`: the most is reached in every draw. `span_start`: below the sequence's prefix; the most is reached in every draw.
All inputs are finite; a program needn't handle non-finite values.
Results may differ from the reference program's by a relative error of at most 0.02.
Values may be sent and summed in bfloat16 or wider, within the bound.
A program may use at most 512 MiB of HBM per device.

```python
import math
import jax
import jax.numpy as jnp
from jax import lax

D = 2048
HEADS = 16
HEAD = 128
FF = 5461
SEQ_LEN = 224
SEQS = 32
TOKENS = 7168


def draw_mlm_flags(key, part):
    key = jax.random.fold_in(key, 11)
    pick_key, token_key = jax.random.split(key)
    order = jax.random.permutation(pick_key, SEQS)
    chosen = order < max(1, SEQS // 5)
    marks = jax.random.randint(token_key, (SEQS, SEQ_LEN), 0, 20) < 3
    leading = jnp.arange(SEQ_LEN) == 0
    flags = (marks | leading[None, :]) & chosen[:, None]
    return flags.astype(jnp.int32).reshape(TOKENS)


def draw_span_len(key, part):
    key = jax.random.fold_in(key, 23)
    value_key, pick_key = jax.random.split(key)
    least = max(1, SEQ_LEN // 8)
    most = SEQ_LEN // 2
    lengths = jax.random.randint(value_key, (SEQS,), least, most + 1)
    which = jax.random.randint(pick_key, (), 0, SEQS)
    return jnp.where(jnp.arange(SEQS) == which, most, lengths).astype(jnp.int32)


def draw_span_start(key, part):
    key = jax.random.fold_in(key, 37)
    value_key, pick_key = jax.random.split(key)
    most = SEQ_LEN - SEQ_LEN // 2 - 1
    starts = jax.random.randint(value_key, (SEQS,), 0, most + 1)
    which = jax.random.randint(pick_key, (), 0, SEQS)
    return jnp.where(jnp.arange(SEQS) == which, most, starts).astype(jnp.int32)


def with_spikes(values, own_key, source, target, blocks, factor):
    def block_of(dim):
        return (jnp.arange(values.shape[dim]) // (values.shape[dim] // blocks)).reshape((-1,) + (1,) * (values.ndim - 1 - dim))

    near = jax.random.permutation(own_key, blocks)[block_of(target)]
    other_side = (block_of(target) + blocks // 2) % blocks
    return jnp.where((block_of(source) == near) | (block_of(source) == other_side), factor * values, values)


def block_levels(own_key, extent, cuts, low, top_value):
    loudness, own = 1.0, jax.random.fold_in(own_key, 6)
    for dim, shards_of in cuts:
        steps = jnp.exp(jax.random.uniform(jax.random.fold_in(own, dim), (shards_of,), jnp.float32, low / len(cuts), top_value / len(cuts)))
        loudness = loudness * jnp.repeat(steps, extent[dim] // shards_of).reshape([-1 if axis == dim else 1 for axis in range(len(extent))])
    return loudness


def scatter_about(key, dims, scale, limit, shards=(), kind=jnp.bfloat16):
    values = scale * jax.random.normal(key, dims, jnp.float32)
    if shards:
        values = values * block_levels(key, dims, shards, -0.22, 0.18)
    return jnp.clip(values, -limit, limit).astype(kind)


def noise_with(rng, extent, scale, reach, cuts, heavy, held_as=jnp.bfloat16):
    drawn = scale * jax.random.normal(rng, extent, jnp.float32)
    if cuts:
        drawn = drawn * block_levels(rng, extent, cuts, -0.22, 0.18)
    return jnp.clip(with_spikes(drawn, jax.random.fold_in(rng, 3), *heavy), -reach, reach).astype(held_as)


def setup_inputs(seed: int = 0) -> dict:
    splits = jax.random.split(jax.random.key(seed), 14)
    x_in = noise_with(splits[0], (TOKENS, D), 1.0, 6.0, ((0, 32),), (0, 1, 32, 2.75))
    d_out = scatter_about(splits[1], (TOKENS, D), 1.0, 6.0, ((0, 32),))
    w_qkv = scatter_about(splits[2], (D, 3 * D), D ** -0.5, 0.125, ((0, 32),))
    w_dense = scatter_about(splits[3], (D, D), 1 ** -0.5, 6.0, ((0, 32),))
    w_in = scatter_about(splits[4], (D, 2 * FF), D ** -0.5, 0.125, ((0, 32),))
    w_out = scatter_about(splits[5], (D, FF), (max(1, FF // 128)) ** -0.5, 1.0, ((0, 32),))
    gain_one = jnp.clip(1.0 + 0.1 * jax.random.normal(splits[6], (D,), jnp.float32), 0.5, 1.5).astype(jnp.bfloat16)
    bias_one = scatter_about(splits[7], (D,), 0.2, 1.0, ((0, 32),))
    gain_two = jnp.clip(1.0 + 0.1 * jax.random.normal(splits[8], (D,), jnp.float32), 0.5, 1.5).astype(jnp.bfloat16)
    bias_two = scatter_about(splits[9], (D,), 0.2, 1.0, ((0, 32),))
    mlm_flags = draw_mlm_flags(jax.random.fold_in(splits[13], 71), 0)
    span_start = draw_span_start(jax.random.fold_in(splits[13], 71), 0)
    span_len = draw_span_len(jax.random.fold_in(splits[13], 71), 0)
    return dict(x_in=x_in, d_out=d_out, w_qkv=w_qkv, w_dense=w_dense, w_in=w_in, w_out=w_out, gain_one=gain_one, bias_one=bias_one, gain_two=gain_two, bias_two=bias_two, mlm_flags=mlm_flags, span_start=span_start, span_len=span_len)


deep_alpha = 6.928203230275509
norm_eps = 1e-05
far_below = -1e+30

@jax.custom_vjp
def low(v):
    return lax.optimization_barrier(v.astype(jnp.bfloat16)).astype(jnp.float32)

@jax.custom_vjp
def low_back(v):
    return v

def low_keep(v):
    return (low(v), None)

def low_pass(kept, grad):
    return (grad,)

def back_keep(v):
    return (v, None)

def back_low(kept, grad):
    return (low(grad),)
low.defvjp(low_keep, low_pass)
low_back.defvjp(back_keep, back_low)

def matmul(left, right):
    return jnp.dot(left, right, precision=lax.Precision.HIGHEST, preferred_element_type=jnp.float32)

def layer_norm(values, gain, bias):
    center = values - lax.optimization_barrier(jnp.mean(values, axis=-1, keepdims=True))
    spread = lax.optimization_barrier(jnp.mean(center * center, axis=-1, keepdims=True))
    return center * lax.rsqrt(spread + norm_eps) * gain + bias

def rotate(block, position):
    width = block.shape[-1]
    quarter = width // 2
    freqs = 10000.0 ** (-2.0 * jnp.arange(quarter, dtype=jnp.float32) / width)
    angles = position.astype(jnp.float32)[..., None, None] * freqs
    cosine = jnp.cos(angles)
    sine = jnp.sin(angles)
    first_half = block[..., :quarter]
    second_half = block[..., quarter:]
    return jnp.concatenate([first_half * cosine - second_half * sine, second_half * cosine + first_half * sine], axis=-1)

def rotary(block, pos_one, pos_two):
    half = block.shape[-1] // 2
    return jnp.concatenate([rotate(block[..., :half], pos_one), rotate(block[..., half:], pos_two)], axis=-1)

def layout(flags, starts, lengths):
    seq_len = flags.shape[1]
    places = jnp.arange(seq_len, dtype=jnp.int32)
    masked = lax.optimization_barrier(jnp.max(flags, axis=1)) > 0
    prefix = jnp.where(masked, seq_len, seq_len - lengths).astype(jnp.int32)
    in_span = places[None, :] >= prefix[:, None]
    pos_one = jnp.where(in_span, starts[:, None], places[None, :]).astype(jnp.int32)
    pos_two = jnp.where(in_span, places[None, :] - prefix[:, None] + 1, 0).astype(jnp.int32)
    visible = (places[None, None, :] < prefix[:, None, None]) | (places[None, None, :] <= places[None, :, None])
    return (visible, pos_one, pos_two)

def attend(queries, key_rows, values, visible):
    scores = jnp.einsum('sqhd,skhd->shqk', queries, key_rows, precision=lax.Precision.HIGHEST)
    scores = low_back(scores)
    scores = jnp.where(visible[:, None], scores, far_below)
    row_max = lax.optimization_barrier(jnp.max(scores, axis=-1, keepdims=True))
    weights = jnp.exp(scores - row_max)
    probs = weights / lax.optimization_barrier(jnp.sum(weights, axis=-1, keepdims=True))
    probs = low(probs)
    return jnp.einsum('shqk,skhd->sqhd', probs, values, precision=lax.Precision.HIGHEST)

def attend_pack(packed_group):
    return attend(packed_group[0], packed_group[1], packed_group[2], packed_group[3])

def forward(x_vals, wqkv, wdense, win, wout, gone, bone, gtwo, btwo, visible, pos_one, pos_two):
    rows = x_vals.shape[0]
    seqs = rows // SEQ_LEN
    width = HEADS * HEAD
    scale = HEAD ** (-0.5)
    shape_four = (seqs, SEQ_LEN, HEADS, HEAD)
    packed = low_back(matmul(x_vals, wqkv))
    queries = low(rotary(packed[:, :width].reshape(shape_four), pos_one, pos_two) * scale)
    key_rows = low(rotary(packed[:, width:2 * width].reshape(shape_four), pos_one, pos_two))
    values = low(packed[:, 2 * width:].reshape(shape_four))
    group = math.gcd(seqs, max(1, 4096 // SEQ_LEN))
    count = seqs // group

    def blocked(array):
        return array.reshape((count, group) + array.shape[1:])
    context = lax.map(jax.checkpoint(attend_pack), (blocked(queries), blocked(key_rows), blocked(values), blocked(visible)))
    context = low(low_back(context.reshape(rows, width)))
    attn = low_back(matmul(context, wdense))
    first = layer_norm(deep_alpha * x_vals + attn, gone, bone)
    projected = low_back(matmul(low(first), win))
    hidden = low(jax.nn.gelu(projected[:, :FF], approximate=False) * projected[:, FF:])
    branch = low_back(matmul(hidden, wout.T))
    return layer_norm(deep_alpha * first + branch, gtwo, btwo)

def reference(x_in, d_out, w_qkv, w_dense, w_in, w_out, gain_one, bias_one, gain_two, bias_two, mlm_flags, span_start, span_len):
    visible, pos_one, pos_two = layout(mlm_flags.reshape(SEQS, SEQ_LEN), span_start, span_len)

    def run(x_vals, wqkv, wdense, win, wout, gone, bone, gtwo, btwo):
        return forward(x_vals, wqkv, wdense, win, wout, gone, bone, gtwo, btwo, visible, pos_one, pos_two)
    floats = [a.astype(jnp.float32) for a in (x_in, w_qkv, w_dense, w_in, w_out, gain_one, bias_one, gain_two, bias_two)]
    result, pull = jax.vjp(run, *floats)
    grads = pull(d_out.astype(jnp.float32))
    return (result.astype(jnp.bfloat16), grads[0].astype(jnp.bfloat16), grads[1], grads[2], grads[3], grads[4], grads[5], grads[6], grads[7], grads[8])
```

```python
import functools

import jax
import jax.numpy as jnp
from jax import lax
from jax.experimental import pallas as pl
from jax.experimental.pallas import tpu as pltpu
from jax.sharding import Mesh
from jax.sharding import PartitionSpec as P

HEADS = 16
HEAD = 128
SEQ_LEN = 224
D = HEADS * HEAD
deep_alpha = 6.928203230275509
norm_eps = 1e-05
far_below = -1e30
scale = HEAD ** (-0.5)

ALL = ("gy", "gx", "core", "z")
CHIPS = ("gy", "gx", "z")
F32 = jnp.float32
BF16 = jnp.bfloat16


def dot(left, right):
    return jnp.dot(left, right, preferred_element_type=F32)


def dot_rows(left, right):
    return lax.dot_general(left, right, (((0,), (0,)), ((), ())), preferred_element_type=F32)


def dot_cols(left, right):
    return lax.dot_general(left, right, (((1,), (1,)), ((), ())), preferred_element_type=F32)


def swap_halves(block):
    lane = lax.broadcasted_iota(jnp.int32, block.shape, 1)
    return jnp.where((lane & 32) == 0, pltpu.roll(block, 96, 1), pltpu.roll(block, 32, 1))


def seen(prefix):
    row = lax.broadcasted_iota(jnp.int32, (SEQ_LEN, SEQ_LEN), 0)
    col = lax.broadcasted_iota(jnp.int32, (SEQ_LEN, SEQ_LEN), 1)
    return (col < prefix) | (col <= row)


def softmax(queries, keys, visible):
    scores = jnp.where(visible, dot_cols(queries, keys), far_below)
    weights = jnp.exp(scores - jnp.max(scores, axis=1, keepdims=True))
    return weights / jnp.sum(weights, axis=1, keepdims=True)


def attend_kernel(prefix_ref, packed_ref, cos_ref, sin_ref, qkv_ref, context_ref):
    width = context_ref.shape[1]
    visible = seen(prefix_ref[pl.program_id(0)])
    cosine = cos_ref[0]
    sine = sin_ref[0]
    for head in range(width // HEAD):
        at = pl.ds(head * HEAD, HEAD)
        at_k = pl.ds(width + head * HEAD, HEAD)
        at_v = pl.ds(2 * width + head * HEAD, HEAD)
        raw = packed_ref[:, at]
        queries = ((raw * cosine + swap_halves(raw) * sine) * scale).astype(BF16)
        raw = packed_ref[:, at_k]
        keys = (raw * cosine + swap_halves(raw) * sine).astype(BF16)
        values = packed_ref[:, at_v].astype(BF16)
        qkv_ref[:, at] = queries
        qkv_ref[:, at_k] = keys
        qkv_ref[:, at_v] = values
        probs = softmax(queries, keys, visible).astype(BF16)
        context_ref[:, at] = dot(probs, values).astype(BF16)


def attend_back_kernel(prefix_ref, qkv_ref, d_context_ref, cos_ref, sin_ref, d_packed_ref):
    width = d_context_ref.shape[1]
    visible = seen(prefix_ref[pl.program_id(0)])
    cosine = cos_ref[0]
    sine = sin_ref[0]
    for head in range(width // HEAD):
        at = pl.ds(head * HEAD, HEAD)
        at_k = pl.ds(width + head * HEAD, HEAD)
        at_v = pl.ds(2 * width + head * HEAD, HEAD)
        queries = qkv_ref[:, at]
        keys = qkv_ref[:, at_k]
        values = qkv_ref[:, at_v]
        d_context = d_context_ref[:, at]
        probs = softmax(queries, keys, visible)
        d_packed_ref[:, at_v] = dot_rows(probs.astype(BF16), d_context).astype(BF16)
        d_probs = dot_cols(d_context, values)
        inner = jnp.sum(probs * d_probs, axis=1, keepdims=True)
        d_scores = (probs * (d_probs - inner)).astype(BF16)
        grad = dot(d_scores, keys) * scale
        d_packed_ref[:, at] = (grad * cosine - swap_halves(grad) * sine).astype(BF16)
        grad = dot_rows(d_scores, queries)
        d_packed_ref[:, at_k] = (grad * cosine - swap_halves(grad) * sine).astype(BF16)


def by_sequence(width):
    return pl.BlockSpec((SEQ_LEN, width), lambda s: (s, 0))


TABLE = pl.BlockSpec((1, SEQ_LEN, HEAD), lambda s: (s, 0, 0))
SCALARS = pl.BlockSpec(memory_space=pltpu.SMEM)
PARAMS = pltpu.CompilerParams(vmem_limit_bytes=48 * 2**20)


def attend(prefix, packed, cosine, sine):
    rows, width = packed.shape[0], packed.shape[1] // 3
    return pl.pallas_call(
        attend_kernel,
        grid=(rows // SEQ_LEN,),
        in_specs=[SCALARS, by_sequence(3 * width), TABLE, TABLE],
        out_specs=[by_sequence(3 * width), by_sequence(width)],
        out_shape=[
            jax.ShapeDtypeStruct((rows, 3 * width), BF16),
            jax.ShapeDtypeStruct((rows, width), BF16),
        ],
        compiler_params=PARAMS,
    )(prefix, packed, cosine, sine)


def attend_back(prefix, qkv, d_context, cosine, sine):
    rows, width = d_context.shape
    return pl.pallas_call(
        attend_back_kernel,
        grid=(rows // SEQ_LEN,),
        in_specs=[SCALARS, by_sequence(3 * width), by_sequence(width), TABLE, TABLE],
        out_specs=by_sequence(3 * width),
        out_shape=jax.ShapeDtypeStruct((rows, 3 * width), BF16),
        compiler_params=PARAMS,
    )(prefix, qkv, d_context, cosine, sine)


def tables(prefix, start):
    place = jnp.arange(SEQ_LEN, dtype=jnp.int32)
    in_span = place[None, :] >= prefix[:, None]
    pos_one = jnp.where(in_span, start[:, None], place[None, :])
    pos_two = jnp.where(in_span, place[None, :] - prefix[:, None] + 1, 0)
    lane = jnp.arange(HEAD)
    freqs = 10000.0 ** (-2.0 * (lane % 32).astype(F32) / 64)
    place_of = jnp.where(lane[None, None, :] < 64, pos_one[:, :, None], pos_two[:, :, None])
    angles = place_of.astype(F32) * freqs
    sign = jnp.where(lane % 64 < 32, -1.0, 1.0)
    return jnp.cos(angles), jnp.sin(angles) * sign


def norm_parts(values):
    center = values - jnp.mean(values, axis=-1, keepdims=True)
    inverse = lax.rsqrt(jnp.mean(center * center, axis=-1, keepdims=True) + norm_eps)
    return center * inverse, inverse


def norm_back(normal, inverse, gain, grad):
    scaled = gain * grad
    return inverse * (
        scaled
        - jnp.mean(scaled, axis=-1, keepdims=True)
        - normal * jnp.mean(scaled * normal, axis=-1, keepdims=True)
    )


def gate_parts(gate):
    phi = 0.5 * (1.0 + lax.erf(gate * 0.7071067811865476))
    slope = phi + gate * jnp.exp(-0.5 * gate * gate) * 0.3989422804014327
    return gate * phi, slope


def on_device(sizes, x_in, d_out, w_qkv, w_dense, w_in, w_out, gone, bone, gtwo, btwo, flags, span_start, span_len):
    gy, gx, cores, zs = sizes
    piece = w_qkv.shape[0]
    ff = w_out.shape[1]
    chips = gy * gx * zs
    pairs = gy * gx
    me = lax.axis_index("core")
    half = D // 2
    group = half // pairs
    tile = -(-ff // 256) * 128

    def other(array):
        return lax.ppermute(array, "core", [(0, 1), (1, 0)])

    def in_order(mine, theirs):
        return jnp.where(me == 0, jnp.stack([mine, theirs]), jnp.stack([theirs, mine]))

    def permute(array):
        lead = array.shape[:-1]
        split = array.reshape(lead + (gy, gx, cores, zs, piece))
        return jnp.swapaxes(split, -3, -2).reshape(lead + (D,))

    def restore(array):
        lead = array.shape[:-1]
        split = array.reshape(lead + (gy, gx, zs, cores, piece))
        return jnp.swapaxes(split, -3, -2).reshape(lead + (D,))

    def take(array, core):
        return lax.dynamic_index_in_dim(array, core, 0, keepdims=False)

    def share(halves):
        return in_order(take(halves, me), other(take(halves, 1 - me)))

    def gather(block):
        return lax.all_gather(block, CHIPS, axis=0, tiled=True)

    def scatter(partial):
        return lax.psum_scatter(partial.astype(BF16), CHIPS, scatter_dimension=0, tiled=True)

    def both(block):
        return jnp.concatenate([block, other(block)], axis=0)

    def fold(partial):
        return partial[:SEQ_LEN] + other(partial[SEQ_LEN:].astype(BF16)).astype(F32)

    def pad_ff(array):
        return jnp.pad(array, ((0, 0), (0, 2 * tile - ff))).reshape(piece, 2, tile)

    qkv_halves = jnp.moveaxis(w_qkv.reshape(piece, 3, pairs, 2, group), 3, 0).reshape(2, piece, 3 * half)
    w_qkv_half = gather(share(qkv_halves).reshape(2 * piece, 3 * half))

    gains = jnp.stack([gone, bone, gtwo, btwo], axis=1)
    extra = jnp.concatenate([gains, other(gains), jnp.zeros((piece, 120), BF16)], axis=1)
    dense_block = gather(jnp.concatenate([permute(w_dense), extra], axis=1))
    w_dense_half = dense_block[:, :D]
    ends = dense_block[:, D : D + 8].astype(F32)
    gains = in_order(ends[:, :4], ends[:, 4:]).reshape(2, chips, piece, 4)
    gains = jnp.transpose(gains, (3, 1, 0, 2)).reshape(4, D)
    gone_full, bone_full, gtwo_full, btwo_full = gains[0], gains[1], gains[2], gains[3]

    in_halves = jnp.stack([pad_ff(w_in[:, :ff]), pad_ff(w_in[:, ff:])], axis=1)
    in_halves = jnp.moveaxis(in_halves, 2, 0).reshape(2, piece, 2 * tile)
    w_in_half = gather(share(in_halves).reshape(2 * piece, 2 * tile))
    out_halves = jnp.moveaxis(pad_ff(w_out), 1, 0)
    w_out_half = gather(share(out_halves).reshape(2 * piece, tile))

    masked = jnp.max(flags) > 0
    prefix = jnp.where(masked, SEQ_LEN, SEQ_LEN - span_len[0])
    info = both(jnp.stack([prefix, span_start[0]])[None, :])
    prefix, start = info[:, 0], info[:, 1]
    cosine, sine = tables(prefix, start)

    x_perm = permute(x_in)
    x_all = both(x_perm)
    packed = dot(x_all, w_qkv_half)
    qkv, context = attend(prefix, packed, cosine, sine)
    attn = fold(dot(context, w_dense_half))
    normal_one, inverse_one = norm_parts(deep_alpha * x_perm.astype(F32) + attn)
    first = normal_one * gone_full + bone_full
    first_all = both(first.astype(BF16))
    projected = dot(first_all, w_in_half)
    gate, up = projected[:, :tile], projected[:, tile:]
    act, slope = gate_parts(gate)
    hidden = (act * up).astype(BF16)
    branch = fold(dot_cols(hidden, w_out_half))
    normal_two, inverse_two = norm_parts(deep_alpha * first + branch)
    layer_out = restore((normal_two * gtwo_full + btwo_full).astype(BF16))

    grad = permute(d_out).astype(F32)
    d_gtwo = jnp.sum(grad * normal_two, axis=0)
    d_btwo = jnp.sum(grad, axis=0)
    d_pre_two = norm_back(normal_two, inverse_two, gtwo_full, grad)
    d_branch = both(d_pre_two.astype(BF16))
    d_w_out = scatter(dot_rows(d_branch, hidden))
    d_hidden = dot(d_branch, w_out_half)
    d_projected = jnp.concatenate([d_hidden * up * slope, d_hidden * act], axis=1).astype(BF16)
    d_w_in = scatter(dot_rows(first_all, d_projected))
    d_first = deep_alpha * d_pre_two + fold(dot_cols(d_projected, w_in_half))

    d_gone = jnp.sum(d_first * normal_one, axis=0)
    d_bone = jnp.sum(d_first, axis=0)
    d_pre_one = norm_back(normal_one, inverse_one, gone_full, d_first)
    d_attn = both(d_pre_one.astype(BF16))
    sums = jnp.stack([d_gone, d_bone, d_gtwo, d_btwo])
    sums = sums + other(sums)
    sums = lax.dynamic_index_in_dim(sums.reshape(4, chips, 2, piece), me, 2, keepdims=False)
    sums = jnp.pad(sums.reshape(4, half).T, ((0, 0), (0, 124)))
    d_dense = scatter(jnp.concatenate([dot_rows(context, d_attn), sums], axis=1))
    d_context = dot_cols(d_attn, w_dense_half).astype(BF16)
    d_packed = attend_back(prefix, qkv, d_context, cosine, sine)
    d_w_qkv = scatter(dot_rows(x_all, d_packed))
    d_input = deep_alpha * d_pre_one + fold(dot_cols(d_packed, w_qkv_half))
    d_input = restore(d_input.astype(BF16))

    def settle(summed):
        blocks = summed.reshape((2, piece) + summed.shape[1:])
        return in_order(take(blocks, me), other(take(blocks, 1 - me))).astype(F32)

    out_qkv = settle(d_w_qkv).reshape(2, piece, 3, pairs, group)
    out_qkv = jnp.transpose(out_qkv, (1, 2, 3, 0, 4)).reshape(piece, 3 * D)
    out_in = jnp.transpose(settle(d_w_in).reshape(2, piece, 2, tile), (1, 2, 0, 3)).reshape(piece, 2, 2 * tile)
    out_in = jnp.concatenate([out_in[:, 0, :ff], out_in[:, 1, :ff]], axis=1)
    out_out = jnp.moveaxis(settle(d_w_out), 0, 1).reshape(piece, 2 * tile)[:, :ff]
    out_dense = restore(d_dense[:, :D]).astype(F32)
    ends = d_dense[:, D : D + 4].astype(F32)
    return layer_out, d_input, out_qkv, out_dense, out_in, out_out, ends[:, 0], ends[:, 1], ends[:, 2], ends[:, 3]


def solution(mesh):
    grp, shard = mesh.shape["grp"], mesh.shape["shard"]
    sizes = (grp // 4, 2, 2, shard)
    inner = Mesh(mesh.devices.reshape(sizes), ALL)
    rows, flat = P(ALL, None), P(ALL)
    return jax.shard_map(
        functools.partial(on_device, sizes),
        mesh=inner,
        in_specs=(rows,) * 6 + (flat,) * 7,
        out_specs=(rows,) * 6 + (flat,) * 4,
        check_vma=False,
    )
```

```python
import functools

import jax
import jax.numpy as jnp
from jax import lax
from jax.experimental import pallas as pl
from jax.experimental.pallas import tpu as pltpu
from jax.sharding import Mesh
from jax.sharding import PartitionSpec as P

HEADS = 16
HEAD = 128
SEQ_LEN = 224
D = HEADS * HEAD
deep_alpha = 6.928203230275509
norm_eps = 1e-05
far_below = -1e30
scale = HEAD ** (-0.5)

ALL = ("gy", "gx", "core", "z")
GROUP = ("gy", "gx", "core")
MESH = pl.DeviceIdType.MESH
F32 = jnp.float32
BF16 = jnp.bfloat16


def dot(left, right):
    return jnp.dot(left, right, preferred_element_type=F32)


def dot_rows(left, right):
    return lax.dot_general(left, right, (((0,), (0,)), ((), ())), preferred_element_type=F32)


def dot_cols(left, right):
    return lax.dot_general(left, right, (((1,), (1,)), ((), ())), preferred_element_type=F32)


def swap_halves(block):
    lane = lax.broadcasted_iota(jnp.int32, block.shape, 1)
    return jnp.where((lane & 32) == 0, pltpu.roll(block, 96, 1), pltpu.roll(block, 32, 1))


def seen(prefix):
    row = lax.broadcasted_iota(jnp.int32, (SEQ_LEN, SEQ_LEN), 0)
    col = lax.broadcasted_iota(jnp.int32, (SEQ_LEN, SEQ_LEN), 1)
    return (col < prefix) | (col <= row)


def softmax(queries, keys, visible):
    scores = jnp.where(visible, dot_cols(queries, keys), far_below)
    weights = jnp.exp(scores - jnp.max(scores, axis=1, keepdims=True))
    return weights / jnp.sum(weights, axis=1, keepdims=True)


def attend_kernel(prefix_ref, packed_ref, cos_ref, sin_ref, qkv_ref, context_ref):
    width = context_ref.shape[1]
    visible = seen(prefix_ref[pl.program_id(0)])
    cosine = cos_ref[0]
    sine = sin_ref[0]
    for head in range(width // HEAD):
        at = pl.ds(head * HEAD, HEAD)
        at_k = pl.ds(width + head * HEAD, HEAD)
        at_v = pl.ds(2 * width + head * HEAD, HEAD)
        raw = packed_ref[:, at]
        queries = ((raw * cosine + swap_halves(raw) * sine) * scale).astype(BF16)
        raw = packed_ref[:, at_k]
        keys = (raw * cosine + swap_halves(raw) * sine).astype(BF16)
        values = packed_ref[:, at_v].astype(BF16)
        qkv_ref[:, at] = queries
        qkv_ref[:, at_k] = keys
        qkv_ref[:, at_v] = values
        probs = softmax(queries, keys, visible).astype(BF16)
        context_ref[:, at] = dot(probs, values).astype(BF16)


def attend_back_kernel(prefix_ref, qkv_ref, d_context_ref, cos_ref, sin_ref, d_packed_ref):
    width = d_context_ref.shape[1]
    visible = seen(prefix_ref[pl.program_id(0)])
    cosine = cos_ref[0]
    sine = sin_ref[0]
    for head in range(width // HEAD):
        at = pl.ds(head * HEAD, HEAD)
        at_k = pl.ds(width + head * HEAD, HEAD)
        at_v = pl.ds(2 * width + head * HEAD, HEAD)
        queries = qkv_ref[:, at]
        keys = qkv_ref[:, at_k]
        values = qkv_ref[:, at_v]
        d_context = d_context_ref[:, at]
        probs = softmax(queries, keys, visible)
        d_packed_ref[:, at_v] = dot_rows(probs.astype(BF16), d_context).astype(BF16)
        d_probs = dot_cols(d_context, values)
        inner = jnp.sum(probs * d_probs, axis=1, keepdims=True)
        d_scores = (probs * (d_probs - inner)).astype(BF16)
        grad = dot(d_scores, keys) * scale
        d_packed_ref[:, at] = (grad * cosine - swap_halves(grad) * sine).astype(BF16)
        grad = dot_rows(d_scores, queries)
        d_packed_ref[:, at_k] = (grad * cosine - swap_halves(grad) * sine).astype(BF16)


def by_sequence(width):
    return pl.BlockSpec((SEQ_LEN, width), lambda s: (s, 0))


TABLE = pl.BlockSpec((1, SEQ_LEN, HEAD), lambda s: (s, 0, 0))
SCALARS = pl.BlockSpec(memory_space=pltpu.SMEM)
PARAMS = pltpu.CompilerParams(vmem_limit_bytes=48 * 2**20)


def attend(prefix, packed, cosine, sine):
    rows, width = packed.shape[0], packed.shape[1] // 3
    return pl.pallas_call(
        attend_kernel,
        grid=(rows // SEQ_LEN,),
        in_specs=[SCALARS, by_sequence(3 * width), TABLE, TABLE],
        out_specs=[by_sequence(3 * width), by_sequence(width)],
        out_shape=[
            jax.ShapeDtypeStruct((rows, 3 * width), BF16),
            jax.ShapeDtypeStruct((rows, width), BF16),
        ],
        compiler_params=PARAMS,
    )(prefix, packed, cosine, sine)


def attend_back(prefix, qkv, d_context, cosine, sine):
    rows, width = d_context.shape
    return pl.pallas_call(
        attend_back_kernel,
        grid=(rows // SEQ_LEN,),
        in_specs=[SCALARS, by_sequence(3 * width), by_sequence(width), TABLE, TABLE],
        out_specs=by_sequence(3 * width),
        out_shape=jax.ShapeDtypeStruct((rows, 3 * width), BF16),
        compiler_params=PARAMS,
    )(prefix, qkv, d_context, cosine, sine)


def tables(prefix, start):
    place = jnp.arange(SEQ_LEN, dtype=jnp.int32)
    in_span = place[None, :] >= prefix[:, None]
    pos_one = jnp.where(in_span, start[:, None], place[None, :])
    pos_two = jnp.where(in_span, place[None, :] - prefix[:, None] + 1, 0)
    lane = jnp.arange(HEAD)
    freqs = 10000.0 ** (-2.0 * (lane % 32).astype(F32) / 64)
    place_of = jnp.where(lane[None, None, :] < 64, pos_one[:, :, None], pos_two[:, :, None])
    angles = place_of.astype(F32) * freqs
    sign = jnp.where(lane % 64 < 32, -1.0, 1.0)
    return jnp.cos(angles), jnp.sin(angles) * sign


def norm_parts(values):
    center = values - jnp.mean(values, axis=-1, keepdims=True)
    inverse = lax.rsqrt(jnp.mean(center * center, axis=-1, keepdims=True) + norm_eps)
    return center * inverse, inverse


def norm_back(normal, inverse, gain, grad):
    scaled = gain * grad
    return inverse * (
        scaled
        - jnp.mean(scaled, axis=-1, keepdims=True)
        - normal * jnp.mean(scaled * normal, axis=-1, keepdims=True)
    )


def gate_parts(gate):
    phi = 0.5 * (1.0 + lax.erf(gate * 0.7071067811865476))
    slope = phi + gate * jnp.exp(-0.5 * gate * gate) * 0.3989422804014327
    return gate * phi, slope


def here():
    return lax.axis_index("gy"), lax.axis_index("gx"), lax.axis_index("core")


def place(y, x, c):
    return (y * 2 + x) * 2 + c


def greet(peers):
    barrier = pltpu.get_barrier_semaphore()
    for peer in peers:
        pl.semaphore_signal(barrier, inc=1, device_id=peer, device_id_type=MESH)
    pl.semaphore_wait(barrier, len(peers))


def gather_kernel(cut, block_ref, out_ref, send, recv, local):
    rows = block_ref.shape[0]
    y, x, c = here()
    to_x, to_y, to_c = {"gx": 1 - x}, {"gy": 1 - y}, {"core": 1 - c}
    me, by_x, by_y, far = place(y, x, c), place(y, 1 - x, c), place(1 - y, x, c), place(1 - y, 1 - x, c)
    low, high = pl.ds(0, cut), pl.ds(cut, rows - cut)

    def push(k, src, dst, to):
        copy = pltpu.make_async_remote_copy(
            src_ref=src, dst_ref=dst, send_sem=send.at[k], recv_sem=recv.at[k], device_id=to, device_id_type=MESH
        )
        copy.start()
        return copy

    def landed(k, dst):
        pltpu.make_async_remote_copy(
            src_ref=dst, dst_ref=dst, send_sem=send.at[k], recv_sem=recv.at[k], device_id=to_c, device_id_type=MESH
        ).wait_recv()

    greet([to_x, to_y, to_c])
    sent = [
        push(0, block_ref.at[low], out_ref.at[me, low], to_x),
        push(1, block_ref.at[high], out_ref.at[me, high], to_y),
        push(2, block_ref.at[high], out_ref.at[me, high], to_x),
        push(3, block_ref.at[low], out_ref.at[me, low], to_y),
        push(4, block_ref, out_ref.at[me], to_c),
    ]
    keep = pltpu.make_async_copy(block_ref, out_ref.at[me], local)
    keep.start()
    landed(0, out_ref.at[by_x, low])
    sent.append(push(5, out_ref.at[by_x, low], out_ref.at[by_x, low], to_y))
    sent.append(push(7, out_ref.at[by_x, low], out_ref.at[by_x, low], to_c))
    landed(1, out_ref.at[by_y, high])
    sent.append(push(6, out_ref.at[by_y, high], out_ref.at[by_y, high], to_x))
    sent.append(push(8, out_ref.at[by_y, high], out_ref.at[by_y, high], to_c))
    landed(2, out_ref.at[by_x, high])
    sent.append(push(9, out_ref.at[by_x, high], out_ref.at[by_x, high], to_c))
    landed(3, out_ref.at[by_y, low])
    sent.append(push(10, out_ref.at[by_y, low], out_ref.at[by_y, low], to_c))
    landed(5, out_ref.at[far, low])
    sent.append(push(11, out_ref.at[far, low], out_ref.at[far, low], to_c))
    landed(6, out_ref.at[far, high])
    sent.append(push(12, out_ref.at[far, high], out_ref.at[far, high], to_c))
    other, other_x, other_y, other_far = (
        place(y, x, 1 - c),
        place(y, 1 - x, 1 - c),
        place(1 - y, x, 1 - c),
        place(1 - y, 1 - x, 1 - c),
    )
    landed(4, out_ref.at[other])
    landed(7, out_ref.at[other_x, low])
    landed(8, out_ref.at[other_y, high])
    landed(9, out_ref.at[other_x, high])
    landed(10, out_ref.at[other_y, low])
    landed(11, out_ref.at[other_far, low])
    landed(12, out_ref.at[other_far, high])
    keep.wait()
    for copy in sent:
        copy.wait_send()


ANY = pl.BlockSpec(memory_space=pl.ANY)


def group_gather(block):
    rows, width = block.shape
    return pl.pallas_call(
        functools.partial(gather_kernel, rows // 2),
        out_shape=jax.ShapeDtypeStruct((8, rows, width), block.dtype),
        in_specs=[ANY],
        out_specs=ANY,
        scratch_shapes=[pltpu.SemaphoreType.DMA((13,)), pltpu.SemaphoreType.DMA((13,)), pltpu.SemaphoreType.DMA],
        compiler_params=pltpu.CompilerParams(collective_id=0, has_side_effects=True),
        cost_estimate=pl.CostEstimate(flops=0, bytes_accessed=100 * 2**20, transcendentals=0),
    )(block)


SLAB = 16


def sum_kernel(
    cut, partial_ref, out_ref, mine, got, near_x, near_y, from_x, from_y, send, recv, local
):
    rows = out_ref.shape[0]
    y, x, c = here()
    to_x, to_y, to_c = {"gx": 1 - x}, {"gy": 1 - y}, {"core": 1 - c}
    chips = [(1 - y, 1 - x), (y, 1 - x), (1 - y, x), (y, x)]
    low, high = pl.ds(0, cut), pl.ds(cut, rows - cut)

    def push(k, src, dst, to):
        copy = pltpu.make_async_remote_copy(
            src_ref=src, dst_ref=dst, send_sem=send.at[k], recv_sem=recv.at[k], device_id=to, device_id_type=MESH
        )
        copy.start()
        return copy

    def add(into, extra, start, size, offset=0):
        @pl.loop(0, size // SLAB)
        def _(step):
            at = pl.ds(pl.multiple_of(start + step * SLAB, SLAB), SLAB)
            of = pl.ds(pl.multiple_of(start - offset + step * SLAB, SLAB), SLAB)
            into[at] = (into[at].astype(F32) + extra[of].astype(F32)).astype(into.dtype)

    loads = [
        pltpu.make_async_copy(partial_ref.at[place(*chip, c)], mine.at[k], local.at[k])
        for k, chip in enumerate(chips)
    ]
    for load in loads:
        load.start()
    greet([to_x, to_y, to_c])
    sent = [push(k, partial_ref.at[place(*chip, 1 - c)], got.at[k], to_c) for k, chip in enumerate(chips)]

    def chip_sum(k):
        loads[k].wait()
        sent[k].wait_recv()
        add(mine.at[k], got.at[k], 0, rows)

    chip_sum(0)
    far_x = push(4, mine.at[0, low], near_x, to_x)
    far_y = push(5, mine.at[0, high], near_y, to_y)
    chip_sum(1)
    plain_x = push(6, mine.at[1, low], from_x.at[low], to_x)
    chip_sum(2)
    plain_y = push(7, mine.at[2, high], from_y.at[high], to_y)
    chip_sum(3)
    far_y.wait_recv()
    add(mine.at[1], near_y, cut, rows - cut, cut)
    more_x = push(8, mine.at[1, high], from_x.at[high], to_x)
    far_x.wait_recv()
    add(mine.at[2], near_x, 0, cut)
    more_y = push(9, mine.at[2, low], from_y.at[low], to_y)
    plain_x.wait_recv()
    plain_y.wait_recv()
    more_x.wait_recv()
    more_y.wait_recv()

    @pl.loop(0, rows // SLAB)
    def _(step):
        at = pl.ds(pl.multiple_of(step * SLAB, SLAB), SLAB)
        out_ref[at] = mine[3, at].astype(F32) + from_x[at].astype(F32) + from_y[at].astype(F32)

    for copy in sent + [far_x, far_y, plain_x, plain_y, more_x, more_y]:
        copy.wait_send()


def group_sum(partial):
    rows, width = partial.shape[0] // 8, partial.shape[1]
    cut = rows // 2
    return pl.pallas_call(
        functools.partial(sum_kernel, cut),
        out_shape=jax.ShapeDtypeStruct((rows, width), F32),
        in_specs=[ANY],
        out_specs=pl.BlockSpec(memory_space=pltpu.VMEM),
        scratch_shapes=[
            pltpu.VMEM((4, rows, width), BF16),
            pltpu.VMEM((4, rows, width), BF16),
            pltpu.VMEM((cut, width), BF16),
            pltpu.VMEM((rows - cut, width), BF16),
            pltpu.VMEM((rows, width), BF16),
            pltpu.VMEM((rows, width), BF16),
            pltpu.SemaphoreType.DMA((10,)),
            pltpu.SemaphoreType.DMA((10,)),
            pltpu.SemaphoreType.DMA((4,)),
        ],
        compiler_params=pltpu.CompilerParams(
            collective_id=1, has_side_effects=True, vmem_limit_bytes=40 * 2**20
        ),
        cost_estimate=pl.CostEstimate(flops=0, bytes_accessed=100 * 2**20, transcendentals=0),
    )(partial.reshape(8, rows, width))


def swap_kernel(spread, *refs):
    n = len(spread)
    blocks, outs = refs[:n], refs[n : 2 * n]
    send, recv, local = refs[2 * n :]
    y, x, c = here()
    me = place(y, x, c)
    peers = [((y + k // 4) % 2, (x + k // 2 % 2) % 2, (c + k % 2) % 2) for k in range(1, 8)]
    names = [{"gy": p[0], "gx": p[1], "core": p[2]} for p in peers]
    greet(names)
    copies, comes, keeps = [], [], []
    for i in range(n):
        for k, (peer, name) in enumerate(zip(peers, names)):
            src = blocks[i] if spread[i] else blocks[i].at[place(*peer)]
            landing = outs[i].at[place(*peer)]
            sems = dict(send_sem=send.at[i, k], recv_sem=recv.at[i, k], device_id=name, device_id_type=MESH)
            copies.append(pltpu.make_async_remote_copy(src_ref=src, dst_ref=outs[i].at[me], **sems))
            comes.append(pltpu.make_async_remote_copy(src_ref=landing, dst_ref=landing, **sems))
            copies[-1].start()
        keeps.append(
            pltpu.make_async_copy(blocks[i] if spread[i] else blocks[i].at[me], outs[i].at[me], local.at[i])
        )
        keeps[-1].start()
    for come in comes:
        come.wait_recv()
    for copy in copies:
        copy.wait_send()
    for keep in keeps:
        keep.wait()


def group_swap(name, arrays, spread):
    n = len(arrays)
    shapes = [((8,) if s else ()) + a.shape for a, s in zip(arrays, spread)]
    return pl.pallas_call(
        functools.partial(swap_kernel, spread),
        out_shape=[jax.ShapeDtypeStruct(s, a.dtype) for a, s in zip(arrays, shapes)],
        in_specs=[ANY] * n,
        out_specs=[ANY] * n,
        scratch_shapes=[
            pltpu.SemaphoreType.DMA((n, 7)),
            pltpu.SemaphoreType.DMA((n, 7)),
            pltpu.SemaphoreType.DMA((n,)),
        ],
        compiler_params=pltpu.CompilerParams(collective_id=name, has_side_effects=True),
        cost_estimate=pl.CostEstimate(flops=0, bytes_accessed=50 * 2**20, transcendentals=0),
    )(*arrays)


def on_device(sizes, x_in, d_out, w_qkv, w_dense, w_in, w_out, gone, bone, gtwo, btwo, flags, span_start, span_len):
    gy, gx, cores, zs = sizes
    piece = w_qkv.shape[0]
    ff = w_out.shape[1]
    group = gy * gx * cores
    width = D // group
    tile = -(-ff // (group * 128)) * 128
    own = gy == 2

    def permute(array):
        lead = array.shape[:-1]
        return jnp.swapaxes(array.reshape(lead + (group, zs, piece)), -3, -2).reshape(lead + (D,))

    def restore(array):
        lead = array.shape[:-1]
        return jnp.swapaxes(array.reshape(lead + (zs, group, piece)), -3, -2).reshape(lead + (D,))

    def swap(name, arrays, spread):
        if own:
            return group_swap(name, arrays, spread)
        return [
            lax.all_gather(a, GROUP, axis=0) if s else lax.all_to_all(a, GROUP, 0, 0, tiled=True)
            for a, s in zip(arrays, spread)
        ]

    def spread_rows(block):
        whole = group_gather(block) if own else lax.all_gather(block, GROUP, axis=0)
        return whole.reshape(group * block.shape[0], block.shape[1])

    def fold(partial):
        partial = partial.astype(BF16)
        if own:
            return group_sum(partial)
        return lax.psum_scatter(partial, GROUP, scatter_dimension=0, tiled=True).astype(F32)

    def gather(block):
        return lax.all_gather(block, "z", axis=0, tiled=True)

    def scatter(partial):
        return lax.psum_scatter(partial.astype(BF16), "z", scatter_dimension=0, tiled=True)

    def pad_ff(array):
        return jnp.pad(array, ((0, 0), (0, group * tile - ff))).reshape(piece, group, tile)

    masked = jnp.max(flags) > 0
    prefix = jnp.where(masked, SEQ_LEN, SEQ_LEN - span_len[0])
    info = jnp.concatenate([gone, bone, gtwo, btwo, jnp.stack([prefix, span_start[0]]).astype(BF16)])
    info = jnp.pad(info[None, :], ((0, 15), (0, -info.shape[0] % 128)))

    qkv_blocks = jnp.moveaxis(w_qkv.reshape(piece, 3, group, width), 2, 0).reshape(group, piece, 3 * width)
    qkv_blocks, info = swap(2, [qkv_blocks, info], (False, True))
    w_qkv_part = gather(qkv_blocks.reshape(group * piece, 3 * width))
    info = info[:, 0, :]
    place_info = info[:, 4 * piece : 4 * piece + 2].astype(jnp.int32)
    prefix, start = place_info[:, 0], place_info[:, 1]
    ends = info[:, : 4 * piece].reshape(group, 4, piece)
    ends = jnp.transpose(ends, (2, 0, 1)).reshape(piece, 4 * group)
    ends = jnp.pad(ends, ((0, 0), (0, 128 - 4 * group)))
    dense_block = gather(jnp.concatenate([permute(w_dense), ends], axis=1))
    w_dense_part = dense_block[:, :D]
    ends = dense_block[:, D : D + 4 * group].astype(F32).reshape(zs, piece, group, 4)
    ends = jnp.transpose(ends, (3, 0, 2, 1)).reshape(4, D)
    gone_full, bone_full, gtwo_full, btwo_full = ends[0], ends[1], ends[2], ends[3]

    x_perm = permute(x_in)
    x_all = spread_rows(x_perm)
    in_blocks = jnp.stack([pad_ff(w_in[:, :ff]), pad_ff(w_in[:, ff:])], axis=2)
    in_blocks = jnp.moveaxis(in_blocks, 1, 0).reshape(group, piece, 2 * tile)
    out_blocks = jnp.moveaxis(pad_ff(w_out), 1, 0)
    in_blocks, out_blocks = swap(3, [in_blocks, out_blocks], (False, False))
    w_in_part = gather(in_blocks.reshape(group * piece, 2 * tile))
    w_out_part = gather(out_blocks.reshape(group * piece, tile))

    cosine, sine = tables(prefix, start)
    packed = dot(x_all, w_qkv_part)
    qkv, context = attend(prefix, packed, cosine, sine)
    attn = fold(dot(context, w_dense_part))
    normal_one, inverse_one = norm_parts(deep_alpha * x_perm.astype(F32) + attn)
    first = normal_one * gone_full + bone_full
    first_all = spread_rows(first.astype(BF16))
    projected = dot(first_all, w_in_part)
    gate, up = projected[:, :tile], projected[:, tile:]
    act, slope = gate_parts(gate)
    hidden = (act * up).astype(BF16)
    branch = fold(dot_cols(hidden, w_out_part))
    normal_two, inverse_two = norm_parts(deep_alpha * first + branch)
    layer_out = restore((normal_two * gtwo_full + btwo_full).astype(BF16))

    grad = permute(d_out).astype(F32)
    d_gtwo = jnp.sum(grad * normal_two, axis=0)
    d_btwo = jnp.sum(grad, axis=0)
    d_pre_two = norm_back(normal_two, inverse_two, gtwo_full, grad)
    d_branch = spread_rows(d_pre_two.astype(BF16))
    d_w_out = scatter(dot_rows(d_branch, hidden))
    d_hidden = dot(d_branch, w_out_part)
    d_projected = jnp.concatenate([d_hidden * up * slope, d_hidden * act], axis=1).astype(BF16)
    d_w_in = scatter(dot_rows(first_all, d_projected))
    d_first = deep_alpha * d_pre_two + fold(dot_cols(d_projected, w_in_part))

    d_gone = jnp.sum(d_first * normal_one, axis=0)
    d_bone = jnp.sum(d_first, axis=0)
    d_pre_one = norm_back(normal_one, inverse_one, gone_full, d_first)
    d_attn = spread_rows(d_pre_one.astype(BF16))
    (sums,) = swap(4, [jnp.pad(jnp.stack([d_gone, d_bone, d_gtwo, d_btwo]), ((0, 4), (0, 0)))], (True,))
    sums = jnp.sum(sums, axis=0)[:4].reshape(4, zs, group, piece)
    mine = lax.axis_index(GROUP)
    sums = lax.dynamic_index_in_dim(sums, mine, 2, keepdims=False).reshape(4, width)
    sums = jnp.pad(sums.T, ((0, 0), (0, 124)))
    d_dense = scatter(jnp.concatenate([dot_rows(context, d_attn), sums], axis=1))
    d_context = dot_cols(d_attn, w_dense_part).astype(BF16)
    d_packed = attend_back(prefix, qkv, d_context, cosine, sine)
    d_w_qkv = scatter(dot_rows(x_all, d_packed))
    d_input = deep_alpha * d_pre_one + fold(dot_cols(d_packed, w_qkv_part))
    d_input = restore(d_input.astype(BF16))

    def settle(name, summed):
        (blocks,) = swap(name, [summed.reshape(group, piece, summed.shape[1])], (False,))
        return blocks.astype(F32)

    out_out = jnp.moveaxis(settle(5, d_w_out), 0, 1).reshape(piece, group * tile)[:, :ff]
    out_in = jnp.transpose(settle(6, d_w_in).reshape(group, piece, 2, tile), (1, 2, 0, 3))
    out_in = out_in.reshape(piece, 2, group * tile)
    out_in = jnp.concatenate([out_in[:, 0, :ff], out_in[:, 1, :ff]], axis=1)
    out_qkv = jnp.transpose(settle(5, d_w_qkv).reshape(group, piece, 3, width), (1, 2, 0, 3)).reshape(piece, 3 * D)
    out_dense = restore(d_dense[:, :D]).astype(F32)
    ends = d_dense[:, D : D + 4].astype(F32)
    return layer_out, d_input, out_qkv, out_dense, out_in, out_out, ends[:, 0], ends[:, 1], ends[:, 2], ends[:, 3]


def solution(mesh):
    grp, shard = mesh.shape["grp"], mesh.shape["shard"]
    sizes = (grp // 4, 2, 2, shard)
    inner = Mesh(mesh.devices.reshape(sizes), ALL)
    rows, flat = P(ALL, None), P(ALL)
    return jax.shard_map(
        functools.partial(on_device, sizes),
        mesh=inner,
        in_specs=(rows,) * 6 + (flat,) * 7,
        out_specs=(rows,) * 6 + (flat,) * 4,
        check_vma=False,
    )
```

```python
import functools

import jax
import jax.numpy as jnp
from jax import lax
from jax.experimental import pallas as pl
from jax.experimental.pallas import tpu as pltpu
from jax.sharding import Mesh
from jax.sharding import PartitionSpec as P

HEADS = 16
HEAD = 128
SEQ_LEN = 224
D = HEADS * HEAD
deep_alpha = 6.928203230275509
norm_eps = 1e-05
far_below = -1e30
scale = HEAD ** (-0.5)

ALL = ("gy", "gx", "core", "z")
GROUP = ("gy", "gx", "core")
MESH = pl.DeviceIdType.MESH
F32 = jnp.float32
BF16 = jnp.bfloat16


def dot(left, right):
    return jnp.dot(left, right, preferred_element_type=F32)


def dot_rows(left, right):
    return lax.dot_general(left, right, (((0,), (0,)), ((), ())), preferred_element_type=F32)


def dot_cols(left, right):
    return lax.dot_general(left, right, (((1,), (1,)), ((), ())), preferred_element_type=F32)


def swap_halves(block):
    lane = lax.broadcasted_iota(jnp.int32, block.shape, 1)
    return jnp.where((lane & 32) == 0, pltpu.roll(block, 96, 1), pltpu.roll(block, 32, 1))


def seen(prefix):
    row = lax.broadcasted_iota(jnp.int32, (SEQ_LEN, SEQ_LEN), 0)
    col = lax.broadcasted_iota(jnp.int32, (SEQ_LEN, SEQ_LEN), 1)
    return (col < prefix) | (col <= row)


def softmax(queries, keys, visible):
    scores = jnp.where(visible, dot_cols(queries, keys), far_below)
    weights = jnp.exp(scores - jnp.max(scores, axis=1, keepdims=True))
    return weights / jnp.sum(weights, axis=1, keepdims=True)


def attend_kernel(prefix_ref, packed_ref, cos_ref, sin_ref, qkv_ref, context_ref):
    width = context_ref.shape[1]
    visible = seen(prefix_ref[pl.program_id(0)])
    cosine = cos_ref[0]
    sine = sin_ref[0]
    for head in range(width // HEAD):
        at = pl.ds(head * HEAD, HEAD)
        at_k = pl.ds(width + head * HEAD, HEAD)
        at_v = pl.ds(2 * width + head * HEAD, HEAD)
        raw = packed_ref[:, at]
        queries = ((raw * cosine + swap_halves(raw) * sine) * scale).astype(BF16)
        raw = packed_ref[:, at_k]
        keys = (raw * cosine + swap_halves(raw) * sine).astype(BF16)
        values = packed_ref[:, at_v].astype(BF16)
        qkv_ref[:, at] = queries
        qkv_ref[:, at_k] = keys
        qkv_ref[:, at_v] = values
        probs = softmax(queries, keys, visible).astype(BF16)
        context_ref[:, at] = dot(probs, values).astype(BF16)


def attend_back_kernel(prefix_ref, qkv_ref, d_context_ref, cos_ref, sin_ref, d_packed_ref):
    width = d_context_ref.shape[1]
    visible = seen(prefix_ref[pl.program_id(0)])
    cosine = cos_ref[0]
    sine = sin_ref[0]
    for head in range(width // HEAD):
        at = pl.ds(head * HEAD, HEAD)
        at_k = pl.ds(width + head * HEAD, HEAD)
        at_v = pl.ds(2 * width + head * HEAD, HEAD)
        queries = qkv_ref[:, at]
        keys = qkv_ref[:, at_k]
        values = qkv_ref[:, at_v]
        d_context = d_context_ref[:, at]
        probs = softmax(queries, keys, visible)
        d_packed_ref[:, at_v] = dot_rows(probs.astype(BF16), d_context).astype(BF16)
        d_probs = dot_cols(d_context, values)
        inner = jnp.sum(probs * d_probs, axis=1, keepdims=True)
        d_scores = (probs * (d_probs - inner)).astype(BF16)
        grad = dot(d_scores, keys) * scale
        d_packed_ref[:, at] = (grad * cosine - swap_halves(grad) * sine).astype(BF16)
        grad = dot_rows(d_scores, queries)
        d_packed_ref[:, at_k] = (grad * cosine - swap_halves(grad) * sine).astype(BF16)


def by_sequence(width):
    return pl.BlockSpec((SEQ_LEN, width), lambda s: (s, 0))


TABLE = pl.BlockSpec((1, SEQ_LEN, HEAD), lambda s: (s, 0, 0))
SCALARS = pl.BlockSpec(memory_space=pltpu.SMEM)
PARAMS = pltpu.CompilerParams(vmem_limit_bytes=48 * 2**20)


def attend(prefix, packed, cosine, sine):
    rows, width = packed.shape[0], packed.shape[1] // 3
    return pl.pallas_call(
        attend_kernel,
        grid=(rows // SEQ_LEN,),
        in_specs=[SCALARS, by_sequence(3 * width), TABLE, TABLE],
        out_specs=[by_sequence(3 * width), by_sequence(width)],
        out_shape=[
            jax.ShapeDtypeStruct((rows, 3 * width), BF16),
            jax.ShapeDtypeStruct((rows, width), BF16),
        ],
        compiler_params=PARAMS,
    )(prefix, packed, cosine, sine)


def attend_back(prefix, qkv, d_context, cosine, sine):
    rows, width = d_context.shape
    return pl.pallas_call(
        attend_back_kernel,
        grid=(rows // SEQ_LEN,),
        in_specs=[SCALARS, by_sequence(3 * width), by_sequence(width), TABLE, TABLE],
        out_specs=by_sequence(3 * width),
        out_shape=jax.ShapeDtypeStruct((rows, 3 * width), BF16),
        compiler_params=PARAMS,
    )(prefix, qkv, d_context, cosine, sine)


def tables(prefix, start):
    place = jnp.arange(SEQ_LEN, dtype=jnp.int32)
    in_span = place[None, :] >= prefix[:, None]
    pos_one = jnp.where(in_span, start[:, None], place[None, :])
    pos_two = jnp.where(in_span, place[None, :] - prefix[:, None] + 1, 0)
    lane = jnp.arange(HEAD)
    freqs = 10000.0 ** (-2.0 * (lane % 32).astype(F32) / 64)
    place_of = jnp.where(lane[None, None, :] < 64, pos_one[:, :, None], pos_two[:, :, None])
    angles = place_of.astype(F32) * freqs
    sign = jnp.where(lane % 64 < 32, -1.0, 1.0)
    return jnp.cos(angles), jnp.sin(angles) * sign


def norm_parts(values):
    center = values - jnp.mean(values, axis=-1, keepdims=True)
    inverse = lax.rsqrt(jnp.mean(center * center, axis=-1, keepdims=True) + norm_eps)
    return center * inverse, inverse


def norm_back(normal, inverse, gain, grad):
    scaled = gain * grad
    return inverse * (
        scaled
        - jnp.mean(scaled, axis=-1, keepdims=True)
        - normal * jnp.mean(scaled * normal, axis=-1, keepdims=True)
    )


def gate_parts(gate):
    phi = 0.5 * (1.0 + lax.erf(gate * 0.7071067811865476))
    slope = phi + gate * jnp.exp(-0.5 * gate * gate) * 0.3989422804014327
    return gate * phi, slope


def here():
    return lax.axis_index("gy"), lax.axis_index("gx"), lax.axis_index("core")


def place(y, x, c):
    return (y * 2 + x) * 2 + c


def greet(peers):
    barrier = pltpu.get_barrier_semaphore()
    for peer in peers:
        pl.semaphore_signal(barrier, inc=1, device_id=peer, device_id_type=MESH)
    pl.semaphore_wait(barrier, len(peers))


def gather_kernel(cut, block_ref, out_ref, send, recv, local):
    rows = block_ref.shape[0]
    y, x, c = here()
    to_x, to_y, to_c = {"gx": 1 - x}, {"gy": 1 - y}, {"core": 1 - c}
    me, by_x, by_y, far = place(y, x, c), place(y, 1 - x, c), place(1 - y, x, c), place(1 - y, 1 - x, c)
    low, high = pl.ds(0, cut), pl.ds(cut, rows - cut)

    def push(k, src, dst, to):
        copy = pltpu.make_async_remote_copy(
            src_ref=src, dst_ref=dst, send_sem=send.at[k], recv_sem=recv.at[k], device_id=to, device_id_type=MESH
        )
        copy.start()
        return copy

    def landed(k, dst):
        pltpu.make_async_remote_copy(
            src_ref=dst, dst_ref=dst, send_sem=send.at[k], recv_sem=recv.at[k], device_id=to_c, device_id_type=MESH
        ).wait_recv()

    greet([to_x, to_y, to_c])
    sent = [
        push(0, block_ref.at[low], out_ref.at[me, low], to_x),
        push(1, block_ref.at[high], out_ref.at[me, high], to_y),
        push(2, block_ref.at[high], out_ref.at[me, high], to_x),
        push(3, block_ref.at[low], out_ref.at[me, low], to_y),
        push(4, block_ref, out_ref.at[me], to_c),
    ]
    keep = pltpu.make_async_copy(block_ref, out_ref.at[me], local)
    keep.start()
    landed(0, out_ref.at[by_x, low])
    sent.append(push(5, out_ref.at[by_x, low], out_ref.at[by_x, low], to_y))
    sent.append(push(7, out_ref.at[by_x, low], out_ref.at[by_x, low], to_c))
    landed(1, out_ref.at[by_y, high])
    sent.append(push(6, out_ref.at[by_y, high], out_ref.at[by_y, high], to_x))
    sent.append(push(8, out_ref.at[by_y, high], out_ref.at[by_y, high], to_c))
    landed(2, out_ref.at[by_x, high])
    sent.append(push(9, out_ref.at[by_x, high], out_ref.at[by_x, high], to_c))
    landed(3, out_ref.at[by_y, low])
    sent.append(push(10, out_ref.at[by_y, low], out_ref.at[by_y, low], to_c))
    landed(5, out_ref.at[far, low])
    sent.append(push(11, out_ref.at[far, low], out_ref.at[far, low], to_c))
    landed(6, out_ref.at[far, high])
    sent.append(push(12, out_ref.at[far, high], out_ref.at[far, high], to_c))
    other, other_x, other_y, other_far = (
        place(y, x, 1 - c),
        place(y, 1 - x, 1 - c),
        place(1 - y, x, 1 - c),
        place(1 - y, 1 - x, 1 - c),
    )
    landed(4, out_ref.at[other])
    landed(7, out_ref.at[other_x, low])
    landed(8, out_ref.at[other_y, high])
    landed(9, out_ref.at[other_x, high])
    landed(10, out_ref.at[other_y, low])
    landed(11, out_ref.at[other_far, low])
    landed(12, out_ref.at[other_far, high])
    keep.wait()
    for copy in sent:
        copy.wait_send()


ANY = pl.BlockSpec(memory_space=pl.ANY)


def group_gather(block):
    rows, width = block.shape
    return pl.pallas_call(
        functools.partial(gather_kernel, rows // 2),
        out_shape=jax.ShapeDtypeStruct((8, rows, width), block.dtype),
        in_specs=[ANY],
        out_specs=ANY,
        scratch_shapes=[pltpu.SemaphoreType.DMA((13,)), pltpu.SemaphoreType.DMA((13,)), pltpu.SemaphoreType.DMA],
        compiler_params=pltpu.CompilerParams(collective_id=0, has_side_effects=True),
        cost_estimate=pl.CostEstimate(flops=0, bytes_accessed=100 * 2**20, transcendentals=0),
    )(block)


SLAB = 16


def sum_kernel(
    cut, partial_ref, out_ref, mine, got, near_x, near_y, from_x, from_y, send, recv, local
):
    rows = out_ref.shape[0]
    y, x, c = here()
    to_x, to_y, to_c = {"gx": 1 - x}, {"gy": 1 - y}, {"core": 1 - c}
    chips = [(1 - y, 1 - x), (y, 1 - x), (1 - y, x), (y, x)]
    low, high = pl.ds(0, cut), pl.ds(cut, rows - cut)

    def push(k, src, dst, to):
        copy = pltpu.make_async_remote_copy(
            src_ref=src, dst_ref=dst, send_sem=send.at[k], recv_sem=recv.at[k], device_id=to, device_id_type=MESH
        )
        copy.start()
        return copy

    def add(into, extra, start, size, offset=0):
        @pl.loop(0, size // SLAB)
        def _(step):
            at = pl.ds(pl.multiple_of(start + step * SLAB, SLAB), SLAB)
            of = pl.ds(pl.multiple_of(start - offset + step * SLAB, SLAB), SLAB)
            into[at] = (into[at].astype(F32) + extra[of].astype(F32)).astype(into.dtype)

    loads = [
        pltpu.make_async_copy(partial_ref.at[place(*chip, c)], mine.at[k], local.at[k])
        for k, chip in enumerate(chips)
    ]
    for load in loads:
        load.start()
    greet([to_x, to_y, to_c])
    sent = [push(k, partial_ref.at[place(*chip, 1 - c)], got.at[k], to_c) for k, chip in enumerate(chips)]

    def chip_sum(k):
        loads[k].wait()
        sent[k].wait_recv()
        add(mine.at[k], got.at[k], 0, rows)

    chip_sum(0)
    far_x = push(4, mine.at[0, low], near_x, to_x)
    far_y = push(5, mine.at[0, high], near_y, to_y)
    chip_sum(1)
    plain_x = push(6, mine.at[1, low], from_x.at[low], to_x)
    chip_sum(2)
    plain_y = push(7, mine.at[2, high], from_y.at[high], to_y)
    chip_sum(3)
    far_y.wait_recv()
    add(mine.at[1], near_y, cut, rows - cut, cut)
    more_x = push(8, mine.at[1, high], from_x.at[high], to_x)
    far_x.wait_recv()
    add(mine.at[2], near_x, 0, cut)
    more_y = push(9, mine.at[2, low], from_y.at[low], to_y)
    plain_x.wait_recv()
    plain_y.wait_recv()
    more_x.wait_recv()
    more_y.wait_recv()

    @pl.loop(0, rows // SLAB)
    def _(step):
        at = pl.ds(pl.multiple_of(step * SLAB, SLAB), SLAB)
        out_ref[at] = mine[3, at].astype(F32) + from_x[at].astype(F32) + from_y[at].astype(F32)

    for copy in sent + [far_x, far_y, plain_x, plain_y, more_x, more_y]:
        copy.wait_send()


def group_sum(partial):
    rows, width = partial.shape[0] // 8, partial.shape[1]
    cut = rows // 2
    return pl.pallas_call(
        functools.partial(sum_kernel, cut),
        out_shape=jax.ShapeDtypeStruct((rows, width), F32),
        in_specs=[ANY],
        out_specs=pl.BlockSpec(memory_space=pltpu.VMEM),
        scratch_shapes=[
            pltpu.VMEM((4, rows, width), BF16),
            pltpu.VMEM((4, rows, width), BF16),
            pltpu.VMEM((cut, width), BF16),
            pltpu.VMEM((rows - cut, width), BF16),
            pltpu.VMEM((rows, width), BF16),
            pltpu.VMEM((rows, width), BF16),
            pltpu.SemaphoreType.DMA((10,)),
            pltpu.SemaphoreType.DMA((10,)),
            pltpu.SemaphoreType.DMA((4,)),
        ],
        compiler_params=pltpu.CompilerParams(
            collective_id=1, has_side_effects=True, vmem_limit_bytes=40 * 2**20
        ),
        cost_estimate=pl.CostEstimate(flops=0, bytes_accessed=100 * 2**20, transcendentals=0),
    )(partial.reshape(8, rows, width))


def swap_kernel(spread, *refs):
    n = len(spread)
    blocks, outs = refs[:n], refs[n : 2 * n]
    send, recv, local = refs[2 * n :]
    y, x, c = here()
    me = place(y, x, c)
    peers = [((y + k // 4) % 2, (x + k // 2 % 2) % 2, (c + k % 2) % 2) for k in range(1, 8)]
    names = [{"gy": p[0], "gx": p[1], "core": p[2]} for p in peers]
    greet(names)
    copies, comes, keeps = [], [], []
    for i in range(n):
        for k, (peer, name) in enumerate(zip(peers, names)):
            src = blocks[i] if spread[i] else blocks[i].at[place(*peer)]
            landing = outs[i].at[place(*peer)]
            sems = dict(send_sem=send.at[i, k], recv_sem=recv.at[i, k], device_id=name, device_id_type=MESH)
            copies.append(pltpu.make_async_remote_copy(src_ref=src, dst_ref=outs[i].at[me], **sems))
            comes.append(pltpu.make_async_remote_copy(src_ref=landing, dst_ref=landing, **sems))
            copies[-1].start()
        keeps.append(
            pltpu.make_async_copy(blocks[i] if spread[i] else blocks[i].at[me], outs[i].at[me], local.at[i])
        )
        keeps[-1].start()
    for come in comes:
        come.wait_recv()
    for copy in copies:
        copy.wait_send()
    for keep in keeps:
        keep.wait()


def group_swap(name, arrays, spread):
    n = len(arrays)
    shapes = [((8,) if s else ()) + a.shape for a, s in zip(arrays, spread)]
    return pl.pallas_call(
        functools.partial(swap_kernel, spread),
        out_shape=[jax.ShapeDtypeStruct(s, a.dtype) for a, s in zip(arrays, shapes)],
        in_specs=[ANY] * n,
        out_specs=[ANY] * n,
        scratch_shapes=[
            pltpu.SemaphoreType.DMA((n, 7)),
            pltpu.SemaphoreType.DMA((n, 7)),
            pltpu.SemaphoreType.DMA((n,)),
        ],
        compiler_params=pltpu.CompilerParams(collective_id=name, has_side_effects=True),
        cost_estimate=pl.CostEstimate(flops=0, bytes_accessed=50 * 2**20, transcendentals=0),
    )(*arrays)


def on_device(sizes, x_in, d_out, w_qkv, w_dense, w_in, w_out, gone, bone, gtwo, btwo, flags, span_start, span_len):
    gy, gx, cores, zs = sizes
    piece = w_qkv.shape[0]
    ff = w_out.shape[1]
    group = gy * gx * cores
    width = D // group
    tile = -(-ff // (group * 128)) * 128
    own = gy == 2

    def permute(array):
        lead = array.shape[:-1]
        return jnp.swapaxes(array.reshape(lead + (group, zs, piece)), -3, -2).reshape(lead + (D,))

    def restore(array):
        lead = array.shape[:-1]
        return jnp.swapaxes(array.reshape(lead + (zs, group, piece)), -3, -2).reshape(lead + (D,))

    def swap(name, arrays, spread):
        if own:
            return group_swap(name, arrays, spread)
        return [
            lax.all_gather(a, GROUP, axis=0) if s else lax.all_to_all(a, GROUP, 0, 0, tiled=True)
            for a, s in zip(arrays, spread)
        ]

    def spread_rows(block):
        whole = group_gather(block) if own else lax.all_gather(block, GROUP, axis=0)
        return whole.reshape(group * block.shape[0], block.shape[1])

    def fold(partial):
        partial = partial.astype(BF16)
        if own:
            return group_sum(partial)
        return lax.psum_scatter(partial, GROUP, scatter_dimension=0, tiled=True).astype(F32)

    def gather(block):
        return lax.all_gather(block, "z", axis=0, tiled=True)

    def scatter(partial):
        return lax.psum_scatter(partial.astype(BF16), "z", scatter_dimension=0, tiled=True)

    def pad_ff(array):
        return jnp.pad(array, ((0, 0), (0, group * tile - ff))).reshape(piece, group, tile)

    masked = jnp.max(flags) > 0
    prefix = jnp.where(masked, SEQ_LEN, SEQ_LEN - span_len[0])
    info = jnp.pad(jnp.stack([prefix, span_start[0]]).astype(BF16)[None, :], ((0, 15), (0, 126)))

    ends = jnp.pad(jnp.stack([gone, bone, gtwo, btwo], axis=1), ((0, 0), (0, 124)))
    dense_block = gather(jnp.concatenate([permute(w_dense), ends], axis=1))
    w_dense_part = dense_block[:, :D]
    qkv_blocks = jnp.moveaxis(w_qkv.reshape(piece, 3, group, width), 2, 0).reshape(group, piece, 3 * width)
    qkv_blocks, info = swap(2, [qkv_blocks, info], (False, True))
    w_qkv_part = gather(qkv_blocks.reshape(group * piece, 3 * width))
    prefix, start = info[:, 0, 0].astype(jnp.int32), info[:, 0, 1].astype(jnp.int32)

    x_perm = permute(x_in)
    x_all = spread_rows(x_perm)
    in_blocks = jnp.stack([pad_ff(w_in[:, :ff]), pad_ff(w_in[:, ff:])], axis=2)
    in_blocks = jnp.moveaxis(in_blocks, 1, 0).reshape(group, piece, 2 * tile)
    out_blocks = jnp.moveaxis(pad_ff(w_out), 1, 0)
    ends = jnp.pad(dense_block[:, D : D + 4].T, ((0, 12), (0, 0)))
    in_blocks, out_blocks, ends = swap(3, [in_blocks, out_blocks, ends], (False, False, True))
    ends = ends[:, :4].astype(F32).reshape(group, 4, zs, piece)
    ends = jnp.transpose(ends, (1, 2, 0, 3)).reshape(4, D)
    gone_full, bone_full, gtwo_full, btwo_full = ends[0], ends[1], ends[2], ends[3]
    w_in_part = gather(in_blocks.reshape(group * piece, 2 * tile))
    w_out_part = gather(out_blocks.reshape(group * piece, tile))

    cosine, sine = tables(prefix, start)
    packed = dot(x_all, w_qkv_part)
    qkv, context = attend(prefix, packed, cosine, sine)
    attn = fold(dot(context, w_dense_part))
    normal_one, inverse_one = norm_parts(deep_alpha * x_perm.astype(F32) + attn)
    first = normal_one * gone_full + bone_full
    first_all = spread_rows(first.astype(BF16))
    projected = dot(first_all, w_in_part)
    gate, up = projected[:, :tile], projected[:, tile:]
    act, slope = gate_parts(gate)
    hidden = (act * up).astype(BF16)
    branch = fold(dot_cols(hidden, w_out_part))
    normal_two, inverse_two = norm_parts(deep_alpha * first + branch)
    layer_out = restore((normal_two * gtwo_full + btwo_full).astype(BF16))

    grad = permute(d_out).astype(F32)
    d_gtwo = jnp.sum(grad * normal_two, axis=0)
    d_btwo = jnp.sum(grad, axis=0)
    d_pre_two = norm_back(normal_two, inverse_two, gtwo_full, grad)
    d_branch = spread_rows(d_pre_two.astype(BF16))
    d_w_out = dot_rows(d_branch, hidden).astype(BF16)
    d_w_out, d_branch = lax.optimization_barrier((d_w_out, d_branch))
    d_w_out = scatter(d_w_out)
    d_hidden = dot(d_branch, w_out_part)
    d_projected = jnp.concatenate([d_hidden * up * slope, d_hidden * act], axis=1).astype(BF16)
    d_w_in = dot_rows(first_all, d_projected).astype(BF16)
    d_w_in, d_projected = lax.optimization_barrier((d_w_in, d_projected))
    d_w_in = scatter(d_w_in)
    d_first = deep_alpha * d_pre_two + fold(dot_cols(d_projected, w_in_part))
    d_first, d_w_out = lax.optimization_barrier((d_first, d_w_out))

    d_gone = jnp.sum(d_first * normal_one, axis=0)
    d_bone = jnp.sum(d_first, axis=0)
    d_pre_one = norm_back(normal_one, inverse_one, gone_full, d_first)
    d_attn = spread_rows(d_pre_one.astype(BF16))
    (sums,) = swap(4, [jnp.pad(jnp.stack([d_gone, d_bone, d_gtwo, d_btwo]), ((0, 4), (0, 0)))], (True,))
    sums = jnp.sum(sums, axis=0)[:4].reshape(4, zs, group, piece)
    mine = lax.axis_index(GROUP)
    sums = lax.dynamic_index_in_dim(sums, mine, 2, keepdims=False).reshape(4, width)
    sums = jnp.pad(sums.T, ((0, 0), (0, 124)))
    d_context = dot_cols(d_attn, w_dense_part).astype(BF16)
    d_packed = attend_back(prefix, qkv, d_context, cosine, sine)
    d_w_qkv = dot_rows(x_all, d_packed).astype(BF16)
    d_w_qkv, d_packed, d_attn = lax.optimization_barrier((d_w_qkv, d_packed, d_attn))
    d_w_qkv = scatter(d_w_qkv)
    d_dense = jnp.concatenate([dot_rows(context, d_attn), sums], axis=1).astype(BF16)
    d_dense, d_packed, d_w_in = lax.optimization_barrier((d_dense, d_packed, d_w_in))
    d_dense, d_w_qkv = lax.optimization_barrier((d_dense, d_w_qkv))
    d_dense = scatter(d_dense)
    d_input = deep_alpha * d_pre_one + fold(dot_cols(d_packed, w_qkv_part))
    d_input = restore(d_input.astype(BF16))

    def settle(name, summed):
        (blocks,) = swap(name, [summed.reshape(group, piece, summed.shape[1])], (False,))
        return blocks.astype(F32)

    out_out = jnp.moveaxis(settle(5, d_w_out), 0, 1).reshape(piece, group * tile)[:, :ff]
    out_in = jnp.transpose(settle(6, d_w_in).reshape(group, piece, 2, tile), (1, 2, 0, 3))
    out_in = out_in.reshape(piece, 2, group * tile)
    out_in = jnp.concatenate([out_in[:, 0, :ff], out_in[:, 1, :ff]], axis=1)
    out_qkv = jnp.transpose(settle(5, d_w_qkv).reshape(group, piece, 3, width), (1, 2, 0, 3)).reshape(piece, 3 * D)
    out_dense = restore(d_dense[:, :D]).astype(F32)
    ends = d_dense[:, D : D + 4].astype(F32)
    return layer_out, d_input, out_qkv, out_dense, out_in, out_out, ends[:, 0], ends[:, 1], ends[:, 2], ends[:, 3]


def solution(mesh):
    grp, shard = mesh.shape["grp"], mesh.shape["shard"]
    sizes = (grp // 4, 2, 2, shard)
    inner = Mesh(mesh.devices.reshape(sizes), ALL)
    rows, flat = P(ALL, None), P(ALL)
    return jax.shard_map(
        functools.partial(on_device, sizes),
        mesh=inner,
        in_specs=(rows,) * 6 + (flat,) * 7,
        out_specs=(rows,) * 6 + (flat,) * 4,
        check_vma=False,
    )
```

```python
import functools

import jax
import jax.numpy as jnp
from jax import lax
from jax.experimental import pallas as pl
from jax.experimental.pallas import tpu as pltpu
from jax.sharding import Mesh
from jax.sharding import PartitionSpec as P

HEADS = 16
HEAD = 128
SEQ_LEN = 224
D = HEADS * HEAD
deep_alpha = 6.928203230275509
norm_eps = 1e-05
far_below = -1e30
scale = HEAD ** (-0.5)

ALL = ("gy", "gx", "core", "z")
GROUP = ("gy", "gx", "core")
MESH = pl.DeviceIdType.MESH
F32 = jnp.float32
BF16 = jnp.bfloat16


def dot(left, right):
    return jnp.dot(left, right, preferred_element_type=F32)


def dot_rows(left, right):
    return lax.dot_general(left, right, (((0,), (0,)), ((), ())), preferred_element_type=F32)


def dot_cols(left, right):
    return lax.dot_general(left, right, (((1,), (1,)), ((), ())), preferred_element_type=F32)


def swap_halves(block):
    lane = lax.broadcasted_iota(jnp.int32, block.shape, 1)
    return jnp.where((lane & 32) == 0, pltpu.roll(block, 96, 1), pltpu.roll(block, 32, 1))


def seen(prefix):
    row = lax.broadcasted_iota(jnp.int32, (SEQ_LEN, SEQ_LEN), 0)
    col = lax.broadcasted_iota(jnp.int32, (SEQ_LEN, SEQ_LEN), 1)
    return (col < prefix) | (col <= row)


def softmax(queries, keys, visible):
    scores = jnp.where(visible, dot_cols(queries, keys), far_below)
    weights = jnp.exp(scores - jnp.max(scores, axis=1, keepdims=True))
    return weights / jnp.sum(weights, axis=1, keepdims=True)


def attend_kernel(prefix_ref, packed_ref, cos_ref, sin_ref, qkv_ref, context_ref):
    width = context_ref.shape[1]
    visible = seen(prefix_ref[pl.program_id(0)])
    cosine = cos_ref[0]
    sine = sin_ref[0]
    for head in range(width // HEAD):
        at = pl.ds(head * HEAD, HEAD)
        at_k = pl.ds(width + head * HEAD, HEAD)
        at_v = pl.ds(2 * width + head * HEAD, HEAD)
        raw = packed_ref[:, at]
        queries = ((raw * cosine + swap_halves(raw) * sine) * scale).astype(BF16)
        raw = packed_ref[:, at_k]
        keys = (raw * cosine + swap_halves(raw) * sine).astype(BF16)
        values = packed_ref[:, at_v].astype(BF16)
        qkv_ref[:, at] = queries
        qkv_ref[:, at_k] = keys
        qkv_ref[:, at_v] = values
        probs = softmax(queries, keys, visible).astype(BF16)
        context_ref[:, at] = dot(probs, values).astype(BF16)


def attend_back_kernel(prefix_ref, qkv_ref, d_context_ref, cos_ref, sin_ref, d_packed_ref):
    width = d_context_ref.shape[1]
    visible = seen(prefix_ref[pl.program_id(0)])
    cosine = cos_ref[0]
    sine = sin_ref[0]
    for head in range(width // HEAD):
        at = pl.ds(head * HEAD, HEAD)
        at_k = pl.ds(width + head * HEAD, HEAD)
        at_v = pl.ds(2 * width + head * HEAD, HEAD)
        queries = qkv_ref[:, at]
        keys = qkv_ref[:, at_k]
        values = qkv_ref[:, at_v]
        d_context = d_context_ref[:, at]
        probs = softmax(queries, keys, visible)
        d_packed_ref[:, at_v] = dot_rows(probs.astype(BF16), d_context).astype(BF16)
        d_probs = dot_cols(d_context, values)
        inner = jnp.sum(probs * d_probs, axis=1, keepdims=True)
        d_scores = (probs * (d_probs - inner)).astype(BF16)
        grad = dot(d_scores, keys) * scale
        d_packed_ref[:, at] = (grad * cosine - swap_halves(grad) * sine).astype(BF16)
        grad = dot_rows(d_scores, queries)
        d_packed_ref[:, at_k] = (grad * cosine - swap_halves(grad) * sine).astype(BF16)


def by_sequence(width):
    return pl.BlockSpec((SEQ_LEN, width), lambda s: (s, 0))


TABLE = pl.BlockSpec((1, SEQ_LEN, HEAD), lambda s: (s, 0, 0))
SCALARS = pl.BlockSpec(memory_space=pltpu.SMEM)
PARAMS = pltpu.CompilerParams(vmem_limit_bytes=48 * 2**20)


def attend(prefix, packed, cosine, sine):
    rows, width = packed.shape[0], packed.shape[1] // 3
    return pl.pallas_call(
        attend_kernel,
        grid=(rows // SEQ_LEN,),
        in_specs=[SCALARS, by_sequence(3 * width), TABLE, TABLE],
        out_specs=[by_sequence(3 * width), by_sequence(width)],
        out_shape=[
            jax.ShapeDtypeStruct((rows, 3 * width), BF16),
            jax.ShapeDtypeStruct((rows, width), BF16),
        ],
        compiler_params=PARAMS,
    )(prefix, packed, cosine, sine)


def attend_back(prefix, qkv, d_context, cosine, sine):
    rows, width = d_context.shape
    return pl.pallas_call(
        attend_back_kernel,
        grid=(rows // SEQ_LEN,),
        in_specs=[SCALARS, by_sequence(3 * width), by_sequence(width), TABLE, TABLE],
        out_specs=by_sequence(3 * width),
        out_shape=jax.ShapeDtypeStruct((rows, 3 * width), BF16),
        compiler_params=PARAMS,
    )(prefix, qkv, d_context, cosine, sine)


def tables(prefix, start):
    place = jnp.arange(SEQ_LEN, dtype=jnp.int32)
    in_span = place[None, :] >= prefix[:, None]
    pos_one = jnp.where(in_span, start[:, None], place[None, :])
    pos_two = jnp.where(in_span, place[None, :] - prefix[:, None] + 1, 0)
    lane = jnp.arange(HEAD)
    freqs = 10000.0 ** (-2.0 * (lane % 32).astype(F32) / 64)
    place_of = jnp.where(lane[None, None, :] < 64, pos_one[:, :, None], pos_two[:, :, None])
    angles = place_of.astype(F32) * freqs
    sign = jnp.where(lane % 64 < 32, -1.0, 1.0)
    return jnp.cos(angles), jnp.sin(angles) * sign


def norm_parts(values):
    center = values - jnp.mean(values, axis=-1, keepdims=True)
    inverse = lax.rsqrt(jnp.mean(center * center, axis=-1, keepdims=True) + norm_eps)
    return center * inverse, inverse


def norm_back(normal, inverse, gain, grad):
    scaled = gain * grad
    return inverse * (
        scaled
        - jnp.mean(scaled, axis=-1, keepdims=True)
        - normal * jnp.mean(scaled * normal, axis=-1, keepdims=True)
    )


def gate_parts(gate):
    phi = 0.5 * (1.0 + lax.erf(gate * 0.7071067811865476))
    slope = phi + gate * jnp.exp(-0.5 * gate * gate) * 0.3989422804014327
    return gate * phi, slope


def here():
    return lax.axis_index("gy"), lax.axis_index("gx"), lax.axis_index("core")


def place(y, x, c):
    return (y * 2 + x) * 2 + c


def greet(peers):
    barrier = pltpu.get_barrier_semaphore()
    for peer in peers:
        pl.semaphore_signal(barrier, inc=1, device_id=peer, device_id_type=MESH)
    pl.semaphore_wait(barrier, len(peers))


def spread_block(cut, base, block_ref, out_ref, send, recv, local):
    rows = block_ref.shape[0]
    y, x, c = here()
    to_x, to_y, to_c = {"gx": 1 - x}, {"gy": 1 - y}, {"core": 1 - c}
    me, by_x, by_y, far = place(y, x, c), place(y, 1 - x, c), place(1 - y, x, c), place(1 - y, 1 - x, c)
    low, high = pl.ds(0, cut), pl.ds(cut, rows - cut)

    def push(k, src, dst, to):
        copy = pltpu.make_async_remote_copy(
            src_ref=src, dst_ref=dst, send_sem=send.at[base + k], recv_sem=recv.at[base + k], device_id=to, device_id_type=MESH
        )
        copy.start()
        return copy

    def landed(k, dst):
        pltpu.make_async_remote_copy(
            src_ref=dst, dst_ref=dst, send_sem=send.at[base + k], recv_sem=recv.at[base + k], device_id=to_c, device_id_type=MESH
        ).wait_recv()

    sent = [
        push(0, block_ref.at[low], out_ref.at[me, low], to_x),
        push(1, block_ref.at[high], out_ref.at[me, high], to_y),
        push(2, block_ref.at[high], out_ref.at[me, high], to_x),
        push(3, block_ref.at[low], out_ref.at[me, low], to_y),
        push(4, block_ref, out_ref.at[me], to_c),
    ]
    keep = pltpu.make_async_copy(block_ref, out_ref.at[me], local)
    keep.start()
    landed(0, out_ref.at[by_x, low])
    sent.append(push(5, out_ref.at[by_x, low], out_ref.at[by_x, low], to_y))
    sent.append(push(7, out_ref.at[by_x, low], out_ref.at[by_x, low], to_c))
    landed(1, out_ref.at[by_y, high])
    sent.append(push(6, out_ref.at[by_y, high], out_ref.at[by_y, high], to_x))
    sent.append(push(8, out_ref.at[by_y, high], out_ref.at[by_y, high], to_c))
    landed(2, out_ref.at[by_x, high])
    sent.append(push(9, out_ref.at[by_x, high], out_ref.at[by_x, high], to_c))
    landed(3, out_ref.at[by_y, low])
    sent.append(push(10, out_ref.at[by_y, low], out_ref.at[by_y, low], to_c))
    landed(5, out_ref.at[far, low])
    sent.append(push(11, out_ref.at[far, low], out_ref.at[far, low], to_c))
    landed(6, out_ref.at[far, high])
    sent.append(push(12, out_ref.at[far, high], out_ref.at[far, high], to_c))
    other, other_x, other_y, other_far = (
        place(y, x, 1 - c),
        place(y, 1 - x, 1 - c),
        place(1 - y, x, 1 - c),
        place(1 - y, 1 - x, 1 - c),
    )
    landed(4, out_ref.at[other])
    landed(7, out_ref.at[other_x, low])
    landed(8, out_ref.at[other_y, high])
    landed(9, out_ref.at[other_x, high])
    landed(10, out_ref.at[other_y, low])
    landed(11, out_ref.at[other_far, low])
    landed(12, out_ref.at[other_far, high])
    keep.wait()
    for copy in sent:
        copy.wait_send()


def gather_kernel(cut, block_ref, out_ref, send, recv, local):
    y, x, c = here()
    greet([{"gx": 1 - x}, {"gy": 1 - y}, {"core": 1 - c}])
    spread_block(cut, 0, block_ref, out_ref, send, recv, local)


ANY = pl.BlockSpec(memory_space=pl.ANY)


def group_gather(block):
    rows, width = block.shape
    return pl.pallas_call(
        functools.partial(gather_kernel, rows // 2),
        out_shape=jax.ShapeDtypeStruct((8, rows, width), block.dtype),
        in_specs=[ANY],
        out_specs=ANY,
        scratch_shapes=[pltpu.SemaphoreType.DMA((13,)), pltpu.SemaphoreType.DMA((13,)), pltpu.SemaphoreType.DMA],
        compiler_params=pltpu.CompilerParams(collective_id=9, has_side_effects=True),
        cost_estimate=pl.CostEstimate(flops=0, bytes_accessed=100 * 2**20, transcendentals=0),
    )(block)


SLAB = 16
ROWS = pl.BlockSpec(memory_space=pltpu.VMEM)
CHIP_COLS = 256


def first_norm(total, x, gains):
    normal, inverse = norm_parts(deep_alpha * x + total)
    first = normal * gains[0:1] + gains[1:2]
    return first, normal, inverse


def second_norm(total, first, grad, gains):
    normal, inverse = norm_parts(deep_alpha * first + total)
    return normal * gains[2:3] + gains[3:4], norm_back(normal, inverse, gains[2:3], grad), grad * normal


def first_back(total, d_pre_two, normal, inverse, gains):
    d_first = deep_alpha * d_pre_two + total
    return norm_back(normal, inverse, gains[0:1], d_first), d_first * normal, d_first


def fold_kernel(mode, across, n_aux, n_out, *refs):
    left_ref, right_ref, gains_ref = refs[:3]
    aux_refs = refs[3 : 3 + n_aux]
    refs = refs[3 + n_aux :]
    spread = mode != "last"
    if spread:
        all_ref, refs = refs[0], refs[1:]
    outs, refs = refs[:n_out], refs[n_out:]
    aux, refs = refs[:n_aux], refs[n_aux:]
    left, right, part, got, near_x, near_y, from_x, from_y, block, acc, send, recv, local = refs
    rows, width = block.shape
    cut = near_x.shape[0]
    y, x, c = here()
    to_x, to_y, to_c = {"gx": 1 - x}, {"gy": 1 - y}, {"core": 1 - c}
    chips = [(1 - y, 1 - x), (y, 1 - x), (1 - y, x), (y, x)]
    low, high = pl.ds(0, cut), pl.ds(cut, rows - cut)

    def push(k, src, dst, to):
        copy = pltpu.make_async_remote_copy(
            src_ref=src, dst_ref=dst, send_sem=send.at[k], recv_sem=recv.at[k], device_id=to, device_id_type=MESH
        )
        copy.start()
        return copy

    def add(k, extra, start, size, offset=0):
        @pl.loop(0, size // SLAB)
        def _(step):
            at = pl.ds(pl.multiple_of(start + step * SLAB, SLAB), SLAB)
            of = pl.ds(pl.multiple_of(start - offset + step * SLAB, SLAB), SLAB)
            part[k, c, at] = (part[k, c, at].astype(F32) + extra[of].astype(F32)).astype(BF16)

    loads = [pltpu.make_async_copy(left_ref.at[a * 2 + b], left.at[k], local.at[k]) for k, (a, b) in enumerate(chips)]
    load_right = pltpu.make_async_copy(right_ref, right, local.at[4])
    load_aux = [pltpu.make_async_copy(r, v, local.at[5 + k]) for k, (r, v) in enumerate(zip(aux_refs, aux))]
    loads[0].start()
    load_right.start()
    for load in loads[1:] + load_aux:
        load.start()
    greet([to_x, to_y, to_c])

    def product(k):
        loads[k].wait()

        @pl.loop(0, width // CHIP_COLS)
        def _(step):
            at = pl.ds(pl.multiple_of(step * CHIP_COLS, CHIP_COLS), CHIP_COLS)
            here_part = dot_cols(left[k], right[at]) if across else dot(left[k], right[:, at])
            part[k, 0, :, at] = here_part[:rows].astype(BF16)
            part[k, 1, :, at] = here_part[rows:].astype(BF16)

        return push(k, part.at[k, 1 - c], got.at[k], to_c)

    load_right.wait()
    sent = [product(0), product(1)]
    sent[0].wait_recv()
    add(0, got.at[0], 0, rows)
    far_x = push(4, part.at[0, c, low], near_x, to_x)
    far_y = push(5, part.at[0, c, high], near_y, to_y)
    sent.append(product(2))
    sent[1].wait_recv()
    add(1, got.at[1], 0, rows)
    plain_x = push(6, part.at[1, c, low], from_x.at[low], to_x)
    sent[2].wait_recv()
    add(2, got.at[2], 0, rows)
    plain_y = push(7, part.at[2, c, high], from_y.at[high], to_y)
    sent.append(product(3))
    far_y.wait_recv()
    add(1, near_y, cut, rows - cut, cut)
    more_x = push(8, part.at[1, c, high], from_x.at[high], to_x)
    far_x.wait_recv()
    add(2, near_x, 0, cut)
    more_y = push(9, part.at[2, c, low], from_y.at[low], to_y)
    sent[3].wait_recv()
    for load in load_aux:
        load.wait()
    plain_x.wait_recv()
    plain_y.wait_recv()
    more_x.wait_recv()
    more_y.wait_recv()
    gains = gains_ref[...]
    acc[...] = jnp.zeros_like(acc)

    @pl.loop(0, rows // SLAB)
    def _(step):
        at = pl.ds(pl.multiple_of(step * SLAB, SLAB), SLAB)
        total = part[3, c, at].astype(F32) + got[3, at].astype(F32) + from_x[at].astype(F32) + from_y[at].astype(F32)
        held = [a[at].astype(F32) for a in aux]
        if mode == "one":
            first, normal, inverse = first_norm(total, held[0], gains)
            outs[0][at] = first
            outs[1][at] = normal
            outs[2][at] = jnp.broadcast_to(inverse, (SLAB, 128))
            block[at] = first.astype(BF16)
        elif mode == "two":
            result, d_pre, terms = second_norm(total, held[0], held[1], gains)
            outs[0][at] = result.astype(BF16)
            outs[1][at] = d_pre
            block[at] = d_pre.astype(BF16)
            acc[0] += terms
            acc[1] += held[1]
        elif mode == "back":
            d_pre, terms, d_first = first_back(total, held[0], held[1], held[2][:, 0:1], gains)
            outs[0][at] = d_pre
            block[at] = d_pre.astype(BF16)
            acc[0] += terms
            acc[1] += d_first
        else:
            outs[0][at] = (deep_alpha * held[0] + total).astype(BF16)

    if mode in ("two", "back"):
        outs[-1][0:1] = jnp.sum(acc[0], axis=0, keepdims=True)
        outs[-1][1:2] = jnp.sum(acc[1], axis=0, keepdims=True)
    for copy in sent + [far_x, far_y, plain_x, plain_y, more_x, more_y]:
        copy.wait_send()
    if spread:
        spread_block(cut, 10, block, all_ref, send, recv, local.at[4])


def group_fold(name, mode, left, right, gains, aux, out_types):
    across = mode != "one"
    rows, depth = left.shape[0] // 8, left.shape[1]
    width = gains.shape[1]
    cut = rows // 2
    spread = mode != "last"
    out_shape = [jax.ShapeDtypeStruct((8, rows, width), BF16)] * spread + out_types
    n = len(aux)
    n_sems = 23 if spread else 10
    return pl.pallas_call(
        functools.partial(fold_kernel, mode, across, n, len(out_types)),
        out_shape=out_shape,
        in_specs=[ANY, ANY, ROWS] + [ANY] * n,
        out_specs=[ANY] * spread + [ROWS] * len(out_types),
        scratch_shapes=[pltpu.VMEM(a.shape, a.dtype) for a in aux]
        + [
            pltpu.VMEM((4, 2 * rows, depth), BF16),
            pltpu.VMEM(right.shape, BF16),
            pltpu.VMEM((4, 2, rows, width), BF16),
            pltpu.VMEM((4, rows, width), BF16),
            pltpu.VMEM((cut, width), BF16),
            pltpu.VMEM((rows - cut, width), BF16),
            pltpu.VMEM((rows, width), BF16),
            pltpu.VMEM((rows, width), BF16),
            pltpu.VMEM((rows, width), BF16),
            pltpu.VMEM((2, SLAB, width), F32),
            pltpu.SemaphoreType.DMA((n_sems,)),
            pltpu.SemaphoreType.DMA((n_sems,)),
            pltpu.SemaphoreType.DMA((5 + n,)),
        ],
        compiler_params=pltpu.CompilerParams(
            collective_id=name, has_side_effects=True, vmem_limit_bytes=50 * 2**20
        ),
        cost_estimate=pl.CostEstimate(flops=0, bytes_accessed=(200 if spread else 110) * 2**20, transcendentals=0),
    )(left.reshape(4, 2 * rows, depth), right, gains, *aux)


def swap_kernel(spread, *refs):
    n = len(spread)
    blocks, outs = refs[:n], refs[n : 2 * n]
    send, recv, local = refs[2 * n :]
    y, x, c = here()
    me = place(y, x, c)
    peers = [((y + k // 4) % 2, (x + k // 2 % 2) % 2, (c + k % 2) % 2) for k in range(1, 8)]
    names = [{"gy": p[0], "gx": p[1], "core": p[2]} for p in peers]
    greet(names)
    copies, comes, keeps = [], [], []
    for i in range(n):
        for k, (peer, name) in enumerate(zip(peers, names)):
            src = blocks[i] if spread[i] else blocks[i].at[place(*peer)]
            landing = outs[i].at[place(*peer)]
            sems = dict(send_sem=send.at[i, k], recv_sem=recv.at[i, k], device_id=name, device_id_type=MESH)
            copies.append(pltpu.make_async_remote_copy(src_ref=src, dst_ref=outs[i].at[me], **sems))
            comes.append(pltpu.make_async_remote_copy(src_ref=landing, dst_ref=landing, **sems))
            copies[-1].start()
        keeps.append(
            pltpu.make_async_copy(blocks[i] if spread[i] else blocks[i].at[me], outs[i].at[me], local.at[i])
        )
        keeps[-1].start()
    for come in comes:
        come.wait_recv()
    for copy in copies:
        copy.wait_send()
    for keep in keeps:
        keep.wait()


def group_swap(name, arrays, spread):
    n = len(arrays)
    shapes = [((8,) if s else ()) + a.shape for a, s in zip(arrays, spread)]
    return pl.pallas_call(
        functools.partial(swap_kernel, spread),
        out_shape=[jax.ShapeDtypeStruct(s, a.dtype) for a, s in zip(arrays, shapes)],
        in_specs=[ANY] * n,
        out_specs=[ANY] * n,
        scratch_shapes=[
            pltpu.SemaphoreType.DMA((n, 7)),
            pltpu.SemaphoreType.DMA((n, 7)),
            pltpu.SemaphoreType.DMA((n,)),
        ],
        compiler_params=pltpu.CompilerParams(collective_id=name, has_side_effects=True),
        cost_estimate=pl.CostEstimate(flops=0, bytes_accessed=50 * 2**20, transcendentals=0),
    )(*arrays)


def on_device(sizes, x_in, d_out, w_qkv, w_dense, w_in, w_out, gone, bone, gtwo, btwo, flags, span_start, span_len):
    gy, gx, cores, zs = sizes
    piece = w_qkv.shape[0]
    ff = w_out.shape[1]
    group = gy * gx * cores
    width = D // group
    tile = -(-ff // (group * 128)) * 128
    own = gy == 2

    def permute(array):
        lead = array.shape[:-1]
        return jnp.swapaxes(array.reshape(lead + (group, zs, piece)), -3, -2).reshape(lead + (D,))

    def restore(array):
        lead = array.shape[:-1]
        return jnp.swapaxes(array.reshape(lead + (zs, group, piece)), -3, -2).reshape(lead + (D,))

    def swap(name, arrays, spread):
        if own:
            return group_swap(name, arrays, spread)
        return [
            lax.all_gather(a, GROUP, axis=0) if s else lax.all_to_all(a, GROUP, 0, 0, tiled=True)
            for a, s in zip(arrays, spread)
        ]

    def spread_rows(block):
        whole = group_gather(block) if own else lax.all_gather(block, GROUP, axis=0)
        return whole.reshape(group * block.shape[0], block.shape[1])

    rows_f32 = jax.ShapeDtypeStruct((SEQ_LEN, D), F32)
    rows_low = jax.ShapeDtypeStruct((SEQ_LEN, D), BF16)
    sums_type = jax.ShapeDtypeStruct((8, D), F32)

    def fold(partial):
        return lax.psum_scatter(partial.astype(BF16), GROUP, scatter_dimension=0, tiled=True).astype(F32)

    def stack_sums(*arrays):
        return jnp.pad(jnp.stack([jnp.sum(a, axis=0) for a in arrays]), ((0, 6), (0, 0)))

    def fold_one(left, right, x, gains):
        if own:
            kinds = [rows_f32, rows_f32, jax.ShapeDtypeStruct((SEQ_LEN, 128), F32)]
            whole, first, normal, inverse = group_fold(0, "one", left, right, gains, [x], kinds)
            return whole.reshape(left.shape[0], D), first, normal, inverse
        first, normal, inverse = first_norm(fold(dot(left, right)), x.astype(F32), gains)
        return spread_rows(first.astype(BF16)), first, normal, inverse

    def fold_two(left, right, first, grad, gains):
        if own:
            kinds = [rows_low, rows_f32, sums_type]
            whole, result, d_pre, sums = group_fold(1, "two", left, right, gains, [first, grad], kinds)
            return whole.reshape(left.shape[0], D), result, d_pre, sums
        grad = grad.astype(F32)
        result, d_pre, terms = second_norm(fold(dot_cols(left, right)), first, grad, gains)
        return spread_rows(d_pre.astype(BF16)), result.astype(BF16), d_pre, stack_sums(terms, grad)

    def fold_back(left, right, d_pre_two, normal, inverse, gains):
        if own:
            kinds = [rows_f32, sums_type]
            whole, d_pre, sums = group_fold(7, "back", left, right, gains, [d_pre_two, normal, inverse], kinds)
            return whole.reshape(left.shape[0], D), d_pre, sums
        d_pre, terms, d_first = first_back(fold(dot_cols(left, right)), d_pre_two, normal, inverse, gains)
        return spread_rows(d_pre.astype(BF16)), d_pre, stack_sums(terms, d_first)

    def fold_last(left, right, d_pre, gains):
        if own:
            (out,) = group_fold(8, "last", left, right, gains, [d_pre], [rows_low])
            return out
        return (deep_alpha * d_pre + fold(dot_cols(left, right))).astype(BF16)

    def gather(block):
        return lax.all_gather(block, "z", axis=0, tiled=True)

    def scatter(partial):
        return lax.psum_scatter(partial.astype(BF16), "z", scatter_dimension=0, tiled=True)

    def pad_ff(array):
        return jnp.pad(array, ((0, 0), (0, group * tile - ff))).reshape(piece, group, tile)

    masked = jnp.max(flags) > 0
    prefix = jnp.where(masked, SEQ_LEN, SEQ_LEN - span_len[0])
    info = jnp.pad(jnp.stack([prefix, span_start[0]]).astype(BF16)[None, :], ((0, 15), (0, 126)))

    ends = jnp.pad(jnp.stack([gone, bone, gtwo, btwo], axis=1), ((0, 0), (0, 124)))
    dense_block = gather(jnp.concatenate([permute(w_dense), ends], axis=1))
    w_dense_part = dense_block[:, :D]
    qkv_blocks = jnp.moveaxis(w_qkv.reshape(piece, 3, group, width), 2, 0).reshape(group, piece, 3 * width)
    qkv_blocks, info = swap(2, [qkv_blocks, info], (False, True))
    w_qkv_part = gather(qkv_blocks.reshape(group * piece, 3 * width))
    prefix, start = info[:, 0, 0].astype(jnp.int32), info[:, 0, 1].astype(jnp.int32)

    x_perm = permute(x_in)
    x_all = spread_rows(x_perm)
    in_blocks = jnp.stack([pad_ff(w_in[:, :ff]), pad_ff(w_in[:, ff:])], axis=2)
    in_blocks = jnp.moveaxis(in_blocks, 1, 0).reshape(group, piece, 2 * tile)
    out_blocks = jnp.moveaxis(pad_ff(w_out), 1, 0)
    ends = jnp.pad(dense_block[:, D : D + 4].T, ((0, 12), (0, 0)))
    in_blocks, out_blocks, ends = swap(3, [in_blocks, out_blocks, ends], (False, False, True))
    ends = ends[:, :4].astype(F32).reshape(group, 4, zs, piece)
    gains = jnp.pad(jnp.transpose(ends, (1, 2, 0, 3)).reshape(4, D), ((0, 4), (0, 0)))
    w_in_part = gather(in_blocks.reshape(group * piece, 2 * tile))
    out_blocks, w_in_part = lax.optimization_barrier((out_blocks, w_in_part))
    w_out_part = gather(out_blocks.reshape(group * piece, tile))

    cosine, sine = tables(prefix, start)
    packed = dot(x_all, w_qkv_part)
    qkv, context = attend(prefix, packed, cosine, sine)
    first_all, first, normal_one, inverse_one = fold_one(context, w_dense_part, x_perm, gains)
    projected = dot(first_all, w_in_part)
    gate, up = projected[:, :tile], projected[:, tile:]
    act, slope = gate_parts(gate)
    hidden = (act * up).astype(BF16)
    d_branch, layer_out, d_pre_two, sums_two = fold_two(hidden, w_out_part, first, permute(d_out), gains)
    layer_out = restore(layer_out)
    d_w_out = dot_rows(d_branch, hidden).astype(BF16)
    d_w_out, d_branch = lax.optimization_barrier((d_w_out, d_branch))
    d_w_out = scatter(d_w_out)
    d_hidden = dot(d_branch, w_out_part)
    d_projected = jnp.concatenate([d_hidden * up * slope, d_hidden * act], axis=1).astype(BF16)
    d_w_in = dot_rows(first_all, d_projected).astype(BF16)
    d_w_in, d_projected = lax.optimization_barrier((d_w_in, d_projected))
    d_w_in = scatter(d_w_in)
    d_attn, d_pre_one, sums_one = fold_back(d_projected, w_in_part, d_pre_two, normal_one, inverse_one, gains)
    d_attn, d_w_out = lax.optimization_barrier((d_attn, d_w_out))
    (sums,) = swap(4, [jnp.concatenate([sums_one[:2], sums_two[:2], jnp.zeros((4, D), F32)])], (True,))
    sums = jnp.sum(sums, axis=0)[:4].reshape(4, zs, group, piece)
    mine = lax.axis_index(GROUP)
    sums = lax.dynamic_index_in_dim(sums, mine, 2, keepdims=False).reshape(4, width)
    sums = jnp.pad(sums.T, ((0, 0), (0, 124)))
    d_context = dot_cols(d_attn, w_dense_part).astype(BF16)
    d_packed = attend_back(prefix, qkv, d_context, cosine, sine)
    d_w_qkv = dot_rows(x_all, d_packed).astype(BF16)
    d_w_qkv, d_packed, d_attn = lax.optimization_barrier((d_w_qkv, d_packed, d_attn))
    d_w_qkv = scatter(d_w_qkv)
    d_dense = jnp.concatenate([dot_rows(context, d_attn), sums], axis=1).astype(BF16)
    d_dense, d_packed, d_w_in = lax.optimization_barrier((d_dense, d_packed, d_w_in))
    d_dense = scatter(d_dense)
    d_input = restore(fold_last(d_packed, w_qkv_part, d_pre_one, gains))

    def settle(name, summed):
        (blocks,) = swap(name, [summed.reshape(group, piece, summed.shape[1])], (False,))
        return blocks.astype(F32)

    out_out = jnp.moveaxis(settle(5, d_w_out), 0, 1).reshape(piece, group * tile)[:, :ff]
    out_in = jnp.transpose(settle(6, d_w_in).reshape(group, piece, 2, tile), (1, 2, 0, 3))
    out_in = out_in.reshape(piece, 2, group * tile)
    out_in = jnp.concatenate([out_in[:, 0, :ff], out_in[:, 1, :ff]], axis=1)
    out_qkv = jnp.transpose(settle(5, d_w_qkv).reshape(group, piece, 3, width), (1, 2, 0, 3)).reshape(piece, 3 * D)
    out_dense = restore(d_dense[:, :D]).astype(F32)
    ends = d_dense[:, D : D + 4].astype(F32)
    return layer_out, d_input, out_qkv, out_dense, out_in, out_out, ends[:, 0], ends[:, 1], ends[:, 2], ends[:, 3]


def solution(mesh):
    grp, shard = mesh.shape["grp"], mesh.shape["shard"]
    sizes = (grp // 4, 2, 2, shard)
    inner = Mesh(mesh.devices.reshape(sizes), ALL)
    rows, flat = P(ALL, None), P(ALL)
    return jax.shard_map(
        functools.partial(on_device, sizes),
        mesh=inner,
        in_specs=(rows,) * 6 + (flat,) * 7,
        out_specs=(rows,) * 6 + (flat,) * 4,
        check_vma=False,
    )
```

```python
import functools

import jax
import jax.numpy as jnp
from jax import lax
from jax.experimental import pallas as pl
from jax.experimental.pallas import tpu as pltpu
from jax.sharding import Mesh
from jax.sharding import PartitionSpec as P

HEADS = 16
HEAD = 128
SEQ_LEN = 224
D = HEADS * HEAD
deep_alpha = 6.928203230275509
norm_eps = 1e-05
far_below = -1e30
scale = HEAD ** (-0.5)

ALL = ("gy", "gx", "core", "z")
GROUP = ("gy", "gx", "core")
MESH = pl.DeviceIdType.MESH
F32 = jnp.float32
BF16 = jnp.bfloat16


def dot(left, right):
    return jnp.dot(left, right, preferred_element_type=F32)


def dot_rows(left, right):
    return lax.dot_general(left, right, (((0,), (0,)), ((), ())), preferred_element_type=F32)


def dot_cols(left, right):
    return lax.dot_general(left, right, (((1,), (1,)), ((), ())), preferred_element_type=F32)


def swap_halves(block):
    lane = lax.broadcasted_iota(jnp.int32, block.shape, 1)
    return jnp.where((lane & 32) == 0, pltpu.roll(block, 96, 1), pltpu.roll(block, 32, 1))


def seen(prefix):
    row = lax.broadcasted_iota(jnp.int32, (SEQ_LEN, SEQ_LEN), 0)
    col = lax.broadcasted_iota(jnp.int32, (SEQ_LEN, SEQ_LEN), 1)
    return (col < prefix) | (col <= row)


def softmax(queries, keys, visible):
    scores = jnp.where(visible, dot_cols(queries, keys), far_below)
    weights = jnp.exp(scores - jnp.max(scores, axis=1, keepdims=True))
    return weights / jnp.sum(weights, axis=1, keepdims=True)


def attend_kernel(prefix_ref, packed_ref, cos_ref, sin_ref, qkv_ref, context_ref):
    width = context_ref.shape[1]
    visible = seen(prefix_ref[pl.program_id(0)])
    cosine = cos_ref[0]
    sine = sin_ref[0]
    for head in range(width // HEAD):
        at = pl.ds(head * HEAD, HEAD)
        at_k = pl.ds(width + head * HEAD, HEAD)
        at_v = pl.ds(2 * width + head * HEAD, HEAD)
        raw = packed_ref[:, at]
        queries = ((raw * cosine + swap_halves(raw) * sine) * scale).astype(BF16)
        raw = packed_ref[:, at_k]
        keys = (raw * cosine + swap_halves(raw) * sine).astype(BF16)
        values = packed_ref[:, at_v].astype(BF16)
        qkv_ref[:, at] = queries
        qkv_ref[:, at_k] = keys
        qkv_ref[:, at_v] = values
        probs = softmax(queries, keys, visible).astype(BF16)
        context_ref[:, at] = dot(probs, values).astype(BF16)


def attend_back_kernel(prefix_ref, qkv_ref, d_context_ref, cos_ref, sin_ref, d_packed_ref):
    width = d_context_ref.shape[1]
    visible = seen(prefix_ref[pl.program_id(0)])
    cosine = cos_ref[0]
    sine = sin_ref[0]
    for head in range(width // HEAD):
        at = pl.ds(head * HEAD, HEAD)
        at_k = pl.ds(width + head * HEAD, HEAD)
        at_v = pl.ds(2 * width + head * HEAD, HEAD)
        queries = qkv_ref[:, at]
        keys = qkv_ref[:, at_k]
        values = qkv_ref[:, at_v]
        d_context = d_context_ref[:, at]
        probs = softmax(queries, keys, visible)
        d_packed_ref[:, at_v] = dot_rows(probs.astype(BF16), d_context).astype(BF16)
        d_probs = dot_cols(d_context, values)
        inner = jnp.sum(probs * d_probs, axis=1, keepdims=True)
        d_scores = (probs * (d_probs - inner)).astype(BF16)
        grad = dot(d_scores, keys) * scale
        d_packed_ref[:, at] = (grad * cosine - swap_halves(grad) * sine).astype(BF16)
        grad = dot_rows(d_scores, queries)
        d_packed_ref[:, at_k] = (grad * cosine - swap_halves(grad) * sine).astype(BF16)


def by_sequence(width):
    return pl.BlockSpec((SEQ_LEN, width), lambda s: (s, 0))


TABLE = pl.BlockSpec((1, SEQ_LEN, HEAD), lambda s: (s, 0, 0))
SCALARS = pl.BlockSpec(memory_space=pltpu.SMEM)
PARAMS = pltpu.CompilerParams(vmem_limit_bytes=48 * 2**20)


def attend(prefix, packed, cosine, sine):
    rows, width = packed.shape[0], packed.shape[1] // 3
    return pl.pallas_call(
        attend_kernel,
        grid=(rows // SEQ_LEN,),
        in_specs=[SCALARS, by_sequence(3 * width), TABLE, TABLE],
        out_specs=[by_sequence(3 * width), by_sequence(width)],
        out_shape=[
            jax.ShapeDtypeStruct((rows, 3 * width), BF16),
            jax.ShapeDtypeStruct((rows, width), BF16),
        ],
        compiler_params=PARAMS,
    )(prefix, packed, cosine, sine)


def attend_back(prefix, qkv, d_context, cosine, sine):
    rows, width = d_context.shape
    return pl.pallas_call(
        attend_back_kernel,
        grid=(rows // SEQ_LEN,),
        in_specs=[SCALARS, by_sequence(3 * width), by_sequence(width), TABLE, TABLE],
        out_specs=by_sequence(3 * width),
        out_shape=jax.ShapeDtypeStruct((rows, 3 * width), BF16),
        compiler_params=PARAMS,
    )(prefix, qkv, d_context, cosine, sine)


def tables(prefix, start):
    place = jnp.arange(SEQ_LEN, dtype=jnp.int32)
    in_span = place[None, :] >= prefix[:, None]
    pos_one = jnp.where(in_span, start[:, None], place[None, :])
    pos_two = jnp.where(in_span, place[None, :] - prefix[:, None] + 1, 0)
    lane = jnp.arange(HEAD)
    freqs = 10000.0 ** (-2.0 * (lane % 32).astype(F32) / 64)
    place_of = jnp.where(lane[None, None, :] < 64, pos_one[:, :, None], pos_two[:, :, None])
    angles = place_of.astype(F32) * freqs
    sign = jnp.where(lane % 64 < 32, -1.0, 1.0)
    return jnp.cos(angles), jnp.sin(angles) * sign


def norm_parts(values):
    center = values - jnp.mean(values, axis=-1, keepdims=True)
    inverse = lax.rsqrt(jnp.mean(center * center, axis=-1, keepdims=True) + norm_eps)
    return center * inverse, inverse


def norm_back(normal, inverse, gain, grad):
    scaled = gain * grad
    return inverse * (
        scaled
        - jnp.mean(scaled, axis=-1, keepdims=True)
        - normal * jnp.mean(scaled * normal, axis=-1, keepdims=True)
    )


def gate_parts(gate):
    phi = 0.5 * (1.0 + lax.erf(gate * 0.7071067811865476))
    slope = phi + gate * jnp.exp(-0.5 * gate * gate) * 0.3989422804014327
    return gate * phi, slope


def here():
    return lax.axis_index("gy"), lax.axis_index("gx"), lax.axis_index("core")


def place(y, x, c):
    return (y * 2 + x) * 2 + c


def greet(peers):
    barrier = pltpu.get_barrier_semaphore()
    for peer in peers:
        pl.semaphore_signal(barrier, inc=1, device_id=peer, device_id_type=MESH)
    pl.semaphore_wait(barrier, len(peers))


def spread_block(cut, base, block_ref, out_ref, send, recv, local, between=()):
    rows = block_ref.shape[0]
    y, x, c = here()
    to_x, to_y, to_c = {"gx": 1 - x}, {"gy": 1 - y}, {"core": 1 - c}
    me, by_x, by_y, far = place(y, x, c), place(y, 1 - x, c), place(1 - y, x, c), place(1 - y, 1 - x, c)
    low, high = pl.ds(0, cut), pl.ds(cut, rows - cut)

    def push(k, src, dst, to):
        copy = pltpu.make_async_remote_copy(
            src_ref=src, dst_ref=dst, send_sem=send.at[base + k], recv_sem=recv.at[base + k], device_id=to, device_id_type=MESH
        )
        copy.start()
        return copy

    def landed(k, dst):
        pltpu.make_async_remote_copy(
            src_ref=dst, dst_ref=dst, send_sem=send.at[base + k], recv_sem=recv.at[base + k], device_id=to_c, device_id_type=MESH
        ).wait_recv()

    sent = [
        push(0, block_ref.at[low], out_ref.at[me, low], to_x),
        push(1, block_ref.at[high], out_ref.at[me, high], to_y),
        push(2, block_ref.at[high], out_ref.at[me, high], to_x),
        push(3, block_ref.at[low], out_ref.at[me, low], to_y),
        push(4, block_ref, out_ref.at[me], to_c),
    ]
    keep = pltpu.make_async_copy(block_ref, out_ref.at[me], local)
    keep.start()
    landed(0, out_ref.at[by_x, low])
    sent.append(push(5, out_ref.at[by_x, low], out_ref.at[by_x, low], to_y))
    sent.append(push(7, out_ref.at[by_x, low], out_ref.at[by_x, low], to_c))
    landed(1, out_ref.at[by_y, high])
    sent.append(push(6, out_ref.at[by_y, high], out_ref.at[by_y, high], to_x))
    sent.append(push(8, out_ref.at[by_y, high], out_ref.at[by_y, high], to_c))
    for service in between:
        service()
    landed(2, out_ref.at[by_x, high])
    sent.append(push(9, out_ref.at[by_x, high], out_ref.at[by_x, high], to_c))
    landed(3, out_ref.at[by_y, low])
    sent.append(push(10, out_ref.at[by_y, low], out_ref.at[by_y, low], to_c))
    landed(5, out_ref.at[far, low])
    sent.append(push(11, out_ref.at[far, low], out_ref.at[far, low], to_c))
    landed(6, out_ref.at[far, high])
    sent.append(push(12, out_ref.at[far, high], out_ref.at[far, high], to_c))
    other, other_x, other_y, other_far = (
        place(y, x, 1 - c),
        place(y, 1 - x, 1 - c),
        place(1 - y, x, 1 - c),
        place(1 - y, 1 - x, 1 - c),
    )
    landed(4, out_ref.at[other])
    landed(7, out_ref.at[other_x, low])
    landed(8, out_ref.at[other_y, high])
    landed(9, out_ref.at[other_x, high])
    landed(10, out_ref.at[other_y, low])
    landed(11, out_ref.at[other_far, low])
    landed(12, out_ref.at[other_far, high])
    keep.wait()
    for copy in sent:
        copy.wait_send()


ANY = pl.BlockSpec(memory_space=pl.ANY)


SLAB = 16
ROWS = pl.BlockSpec(memory_space=pltpu.VMEM)
CHIP_COLS = 256


def first_norm(total, x, gains):
    normal, inverse = norm_parts(deep_alpha * x + total)
    first = normal * gains[0:1] + gains[1:2]
    return first, normal, inverse


def second_norm(total, first, grad, gains):
    normal, inverse = norm_parts(deep_alpha * first + total)
    return normal * gains[2:3] + gains[3:4], norm_back(normal, inverse, gains[2:3], grad), grad * normal


def first_back(total, d_pre_two, normal, inverse, gains):
    d_first = deep_alpha * d_pre_two + total
    return norm_back(normal, inverse, gains[0:1], d_first), d_first * normal, d_first


def fold_kernel(mode, across, n_aux, n_out, *refs):
    left_ref, right_ref, gains_ref = refs[:3]
    aux_refs = refs[3 : 3 + n_aux]
    refs = refs[3 + n_aux :]
    spread = mode != "last"
    if spread:
        all_ref, refs = refs[0], refs[1:]
    outs, refs = refs[:n_out], refs[n_out:]
    aux, refs = refs[:n_aux], refs[n_aux:]
    left, right, part, got, near_x, near_y, from_x, from_y, block, acc, send, recv, local = refs
    rows, width = block.shape
    cut = near_x.shape[0]
    y, x, c = here()
    to_x, to_y, to_c = {"gx": 1 - x}, {"gy": 1 - y}, {"core": 1 - c}
    chips = [(1 - y, 1 - x), (y, 1 - x), (1 - y, x), (y, x)]
    low, high = pl.ds(0, cut), pl.ds(cut, rows - cut)

    def push(k, src, dst, to):
        copy = pltpu.make_async_remote_copy(
            src_ref=src, dst_ref=dst, send_sem=send.at[k], recv_sem=recv.at[k], device_id=to, device_id_type=MESH
        )
        copy.start()
        return copy

    def add(k, extra, start, size, offset=0):
        @pl.loop(0, size // SLAB)
        def _(step):
            at = pl.ds(pl.multiple_of(start + step * SLAB, SLAB), SLAB)
            of = pl.ds(pl.multiple_of(start - offset + step * SLAB, SLAB), SLAB)
            part[k, c, at] = (part[k, c, at].astype(F32) + extra[of].astype(F32)).astype(BF16)

    loads = [pltpu.make_async_copy(left_ref.at[a * 2 + b], left.at[k], local.at[k]) for k, (a, b) in enumerate(chips)]
    load_right = pltpu.make_async_copy(right_ref, right, local.at[4])
    load_aux = [pltpu.make_async_copy(r, v, local.at[5 + k]) for k, (r, v) in enumerate(zip(aux_refs, aux))]
    loads[0].start()
    load_right.start()
    for load in loads[1:] + load_aux:
        load.start()
    greet([to_x, to_y, to_c])

    def product(k):
        loads[k].wait()

        @pl.loop(0, width // CHIP_COLS)
        def _(step):
            at = pl.ds(pl.multiple_of(step * CHIP_COLS, CHIP_COLS), CHIP_COLS)
            here_part = dot_cols(left[k], right[at]) if across else dot(left[k], right[:, at])
            part[k, 0, :, at] = here_part[:rows].astype(BF16)
            part[k, 1, :, at] = here_part[rows:].astype(BF16)

        return push(k, part.at[k, 1 - c], got.at[k], to_c)

    load_right.wait()
    sent = [product(0), product(1)]
    sent[0].wait_recv()
    add(0, got.at[0], 0, rows)
    far_x = push(4, part.at[0, c, low], near_x, to_x)
    far_y = push(5, part.at[0, c, high], near_y, to_y)
    sent.append(product(2))
    sent[1].wait_recv()
    add(1, got.at[1], 0, rows)
    plain_x = push(6, part.at[1, c, low], from_x.at[low], to_x)
    sent[2].wait_recv()
    add(2, got.at[2], 0, rows)
    plain_y = push(7, part.at[2, c, high], from_y.at[high], to_y)
    sent.append(product(3))
    far_y.wait_recv()
    add(1, near_y, cut, rows - cut, cut)
    more_x = push(8, part.at[1, c, high], from_x.at[high], to_x)
    far_x.wait_recv()
    add(2, near_x, 0, cut)
    more_y = push(9, part.at[2, c, low], from_y.at[low], to_y)
    sent[3].wait_recv()
    for load in load_aux:
        load.wait()
    plain_x.wait_recv()
    plain_y.wait_recv()
    more_x.wait_recv()
    more_y.wait_recv()
    gains = gains_ref[...]
    acc[...] = jnp.zeros_like(acc)

    @pl.loop(0, rows // SLAB)
    def _(step):
        at = pl.ds(pl.multiple_of(step * SLAB, SLAB), SLAB)
        total = part[3, c, at].astype(F32) + got[3, at].astype(F32) + from_x[at].astype(F32) + from_y[at].astype(F32)
        held = [a[at].astype(F32) for a in aux]
        if mode == "one":
            first, normal, inverse = first_norm(total, held[0], gains)
            outs[0][at] = first
            outs[1][at] = normal
            outs[2][at] = jnp.broadcast_to(inverse, (SLAB, 128))
            block[at] = first.astype(BF16)
        elif mode == "two":
            result, d_pre, terms = second_norm(total, held[0], held[1], gains)
            outs[0][at] = result.astype(BF16)
            outs[1][at] = d_pre
            block[at] = d_pre.astype(BF16)
            acc[0] += terms
            acc[1] += held[1]
        elif mode == "back":
            d_pre, terms, d_first = first_back(total, held[0], held[1], held[2][:, 0:1], gains)
            outs[0][at] = d_pre
            block[at] = d_pre.astype(BF16)
            acc[0] += terms
            acc[1] += d_first
        else:
            outs[0][at] = (deep_alpha * held[0] + total).astype(BF16)

    if mode in ("two", "back"):
        outs[-1][0:1] = jnp.sum(acc[0], axis=0, keepdims=True)
        outs[-1][1:2] = jnp.sum(acc[1], axis=0, keepdims=True)
    for copy in sent + [far_x, far_y, plain_x, plain_y, more_x, more_y]:
        copy.wait_send()
    if spread:
        spread_block(cut, 10, block, all_ref, send, recv, local.at[4])


def group_fold(name, mode, left, right, gains, aux, out_types):
    across = mode != "one"
    rows, depth = left.shape[0] // 8, left.shape[1]
    width = gains.shape[1]
    cut = rows // 2
    spread = mode != "last"
    out_shape = [jax.ShapeDtypeStruct((8, rows, width), BF16)] * spread + out_types
    n = len(aux)
    n_sems = 23 if spread else 10
    return pl.pallas_call(
        functools.partial(fold_kernel, mode, across, n, len(out_types)),
        out_shape=out_shape,
        in_specs=[ANY, ANY, ROWS] + [ANY] * n,
        out_specs=[ANY] * spread + [ROWS] * len(out_types),
        scratch_shapes=[pltpu.VMEM(a.shape, a.dtype) for a in aux]
        + [
            pltpu.VMEM((4, 2 * rows, depth), BF16),
            pltpu.VMEM(right.shape, BF16),
            pltpu.VMEM((4, 2, rows, width), BF16),
            pltpu.VMEM((4, rows, width), BF16),
            pltpu.VMEM((cut, width), BF16),
            pltpu.VMEM((rows - cut, width), BF16),
            pltpu.VMEM((rows, width), BF16),
            pltpu.VMEM((rows, width), BF16),
            pltpu.VMEM((rows, width), BF16),
            pltpu.VMEM((2, SLAB, width), F32),
            pltpu.SemaphoreType.DMA((n_sems,)),
            pltpu.SemaphoreType.DMA((n_sems,)),
            pltpu.SemaphoreType.DMA((5 + n,)),
        ],
        compiler_params=pltpu.CompilerParams(
            collective_id=name, has_side_effects=True, vmem_limit_bytes=50 * 2**20
        ),
        cost_estimate=pl.CostEstimate(flops=0, bytes_accessed=(200 if spread else 110) * 2**20, transcendentals=0),
    )(left.reshape(4, 2 * rows, depth), right, gains, *aux)


def swap_kernel(spread, *refs):
    n = len(spread)
    blocks, outs = refs[:n], refs[n : 2 * n]
    send, recv, local = refs[2 * n :]
    y, x, c = here()
    me = place(y, x, c)
    peers = [((y + k // 4) % 2, (x + k // 2 % 2) % 2, (c + k % 2) % 2) for k in range(1, 8)]
    names = [{"gy": p[0], "gx": p[1], "core": p[2]} for p in peers]
    greet(names)
    copies, comes, keeps = [], [], []
    for i in range(n):
        for k, (peer, name) in enumerate(zip(peers, names)):
            src = blocks[i] if spread[i] else blocks[i].at[place(*peer)]
            landing = outs[i].at[place(*peer)]
            sems = dict(send_sem=send.at[i, k], recv_sem=recv.at[i, k], device_id=name, device_id_type=MESH)
            copies.append(pltpu.make_async_remote_copy(src_ref=src, dst_ref=outs[i].at[me], **sems))
            comes.append(pltpu.make_async_remote_copy(src_ref=landing, dst_ref=landing, **sems))
            copies[-1].start()
        keeps.append(
            pltpu.make_async_copy(blocks[i] if spread[i] else blocks[i].at[me], outs[i].at[me], local.at[i])
        )
        keeps[-1].start()
    for come in comes:
        come.wait_recv()
    for copy in copies:
        copy.wait_send()
    for keep in keeps:
        keep.wait()


def group_swap(name, arrays, spread):
    n = len(arrays)
    shapes = [((8,) if s else ()) + a.shape for a, s in zip(arrays, spread)]
    return pl.pallas_call(
        functools.partial(swap_kernel, spread),
        out_shape=[jax.ShapeDtypeStruct(s, a.dtype) for a, s in zip(arrays, shapes)],
        in_specs=[ANY] * n,
        out_specs=[ANY] * n,
        scratch_shapes=[
            pltpu.SemaphoreType.DMA((n, 7)),
            pltpu.SemaphoreType.DMA((n, 7)),
            pltpu.SemaphoreType.DMA((n,)),
        ],
        compiler_params=pltpu.CompilerParams(collective_id=name, has_side_effects=True),
        cost_estimate=pl.CostEstimate(flops=0, bytes_accessed=50 * 2**20, transcendentals=0),
    )(*arrays)


def opening_kernel(
    zs, qkv_ref, dense_ref, info_ref, in_ref, out_ref, x_ref, *refs
):
    qkv_all, dense_all, info_all, in_all, out_all, x_all = refs[:6]
    swap_send, swap_recv, line_send, line_recv, x_send, x_recv, local = refs[6:]
    y, x, c = here()
    z = lax.axis_index("z")
    me = place(y, x, c)
    peers = [((y + k // 4) % 2, (x + k // 2 % 2) % 2, (c + k % 2) % 2) for k in range(1, 8)]
    names = [{"gy": p[0], "gx": p[1], "core": p[2]} for p in peers]
    lines = [dense_all, qkv_all, info_all]
    barrier = pltpu.get_barrier_semaphore()
    for name in names:
        pl.semaphore_signal(barrier, inc=1, device_id=name, device_id_type=MESH)

    @pl.when(z > 0)
    def _():
        pl.semaphore_signal(barrier, inc=1, device_id={"z": z - 1}, device_id_type=MESH)

    @pl.when(z < zs - 1)
    def _():
        pl.semaphore_signal(barrier, inc=1, device_id={"z": z + 1}, device_id_type=MESH)

    inside = (z > 0) & (z < zs - 1)

    @pl.when(inside)
    def _():
        pl.semaphore_wait(barrier, 9)

    @pl.when(jnp.logical_not(inside))
    def _():
        pl.semaphore_wait(barrier, 8)

    def hop(a, step, up):
        shard = z - step if up else z + step
        to = z + 1 if up else z - 1
        k = 2 * step + (0 if up else 1)
        ref = lines[a].at[shard]
        return pltpu.make_async_remote_copy(
            src_ref=ref,
            dst_ref=ref,
            send_sem=line_send.at[a, k],
            recv_sem=line_recv.at[a, k],
            device_id={"z": to},
            device_id_type=MESH,
        )

    def comes(a, step, up):
        shard = z - 1 - step if up else z + 1 + step
        k = 2 * step + (0 if up else 1)
        ref = lines[a].at[shard]
        return pltpu.make_async_remote_copy(
            src_ref=ref,
            dst_ref=ref,
            send_sem=line_send.at[a, k],
            recv_sem=line_recv.at[a, k],
            device_id={"core": 1 - c},
            device_id_type=MESH,
        )

    def sends(step, up):
        return (z >= step) & (z < zs - 1) if up else (z <= zs - 1 - step) & (z > 0)

    def gets(step, up):
        return z >= step + 1 if up else z <= zs - 2 - step

    def line_step(a, step):
        for up in (True, False):
            if step > 0:

                @pl.when(gets(step - 1, up))
                def _(up=up):
                    comes(a, step - 1, up).wait_recv()

            @pl.when(sends(step, up))
            def _(up=up):
                hop(a, step, up).start()

    def line_end(a):
        for up in (True, False):

            @pl.when(gets(zs - 2, up))
            def _(up=up):
                comes(a, zs - 2, up).wait_recv()

            for step in range(zs - 1):

                @pl.when(sends(step, up))
                def _(step=step, up=up):
                    hop(a, step, up).wait_send()

    swaps = [
        (qkv_ref, qkv_all.at[z], False),
        (info_ref, info_all.at[z], True),
        (in_ref, in_all, False),
        (out_ref, out_all, False),
    ]

    def swap_copies(i):
        src, dst, spread = swaps[i]
        out, back = [], []
        for k, (peer, name) in enumerate(zip(peers, names)):
            sems = dict(
                send_sem=swap_send.at[i, k], recv_sem=swap_recv.at[i, k], device_id=name, device_id_type=MESH
            )
            out.append(
                pltpu.make_async_remote_copy(
                    src_ref=src if spread else src.at[place(*peer)], dst_ref=dst.at[me], **sems
                )
            )
            landing = dst.at[place(*peer)]
            back.append(pltpu.make_async_remote_copy(src_ref=landing, dst_ref=landing, **sems))
        return out, back, pltpu.make_async_copy(src if spread else src.at[me], dst.at[me], local.at[i])

    all_swaps = [swap_copies(i) for i in range(4)]

    def swap_start(i):
        for copy in all_swaps[i][0]:
            copy.start()
        all_swaps[i][2].start()

    def swap_landed(i):
        for copy in all_swaps[i][1]:
            copy.wait_recv()
        all_swaps[i][2].wait()

    keep_dense = pltpu.make_async_copy(dense_ref, dense_all.at[z], local.at[4])
    keep_dense.start()
    swap_start(0)
    swap_start(1)
    keep_dense.wait()
    line_step(0, 0)
    swap_landed(0)
    line_step(1, 0)
    swap_landed(1)
    line_step(2, 0)
    swap_start(2)
    swap_start(3)
    for step in range(1, zs - 1):
        line_step(0, step)
        line_step(2, step)
    spread_block(
        x_ref.shape[0] // 2, 0, x_ref, x_all, x_send, x_recv, local.at[5],
        [functools.partial(line_step, 1, step) for step in range(1, zs - 1)],
    )
    swap_landed(2)
    swap_landed(3)
    for a in range(3):
        line_end(a)
    for i in range(4):
        for copy in all_swaps[i][0]:
            copy.wait_send()


def opening(zs, qkv_blocks, dense, info, in_blocks, out_blocks, x):
    def whole(lead, a):
        return jax.ShapeDtypeStruct(lead + a.shape, a.dtype)

    out_shape = [
        whole((zs,), qkv_blocks),
        whole((zs,), dense),
        whole((zs, 8), info),
        whole((), in_blocks),
        whole((), out_blocks),
        whole((8,), x),
    ]
    return pl.pallas_call(
        functools.partial(opening_kernel, zs),
        out_shape=out_shape,
        in_specs=[ANY] * 6,
        out_specs=[ANY] * 6,
        scratch_shapes=[
            pltpu.SemaphoreType.DMA((4, 7)),
            pltpu.SemaphoreType.DMA((4, 7)),
            pltpu.SemaphoreType.DMA((3, 2 * (zs - 1))),
            pltpu.SemaphoreType.DMA((3, 2 * (zs - 1))),
            pltpu.SemaphoreType.DMA((13,)),
            pltpu.SemaphoreType.DMA((13,)),
            pltpu.SemaphoreType.DMA((6,)),
        ],
        compiler_params=pltpu.CompilerParams(collective_id=9, has_side_effects=True),
        cost_estimate=pl.CostEstimate(flops=0, bytes_accessed=200 * 2**20, transcendentals=0),
    )(qkv_blocks, dense, info, in_blocks, out_blocks, x)


def on_device(sizes, x_in, d_out, w_qkv, w_dense, w_in, w_out, gone, bone, gtwo, btwo, flags, span_start, span_len):
    gy, gx, cores, zs = sizes
    piece = w_qkv.shape[0]
    ff = w_out.shape[1]
    group = gy * gx * cores
    width = D // group
    tile = -(-ff // (group * 128)) * 128
    own = gy == 2

    def permute(array):
        lead = array.shape[:-1]
        return jnp.swapaxes(array.reshape(lead + (group, zs, piece)), -3, -2).reshape(lead + (D,))

    def restore(array):
        lead = array.shape[:-1]
        return jnp.swapaxes(array.reshape(lead + (zs, group, piece)), -3, -2).reshape(lead + (D,))

    def swap(name, arrays, spread):
        if own:
            return group_swap(name, arrays, spread)
        return [
            lax.all_gather(a, GROUP, axis=0) if s else lax.all_to_all(a, GROUP, 0, 0, tiled=True)
            for a, s in zip(arrays, spread)
        ]

    def spread_rows(block):
        return lax.all_gather(block, GROUP, axis=0, tiled=True)

    rows_f32 = jax.ShapeDtypeStruct((SEQ_LEN, D), F32)
    rows_low = jax.ShapeDtypeStruct((SEQ_LEN, D), BF16)
    sums_type = jax.ShapeDtypeStruct((8, D), F32)

    def fold(partial):
        return lax.psum_scatter(partial.astype(BF16), GROUP, scatter_dimension=0, tiled=True).astype(F32)

    def stack_sums(*arrays):
        return jnp.pad(jnp.stack([jnp.sum(a, axis=0) for a in arrays]), ((0, 6), (0, 0)))

    def fold_one(left, right, x, gains):
        if own:
            kinds = [rows_f32, rows_f32, jax.ShapeDtypeStruct((SEQ_LEN, 128), F32)]
            whole, first, normal, inverse = group_fold(0, "one", left, right, gains, [x], kinds)
            return whole.reshape(left.shape[0], D), first, normal, inverse
        first, normal, inverse = first_norm(fold(dot(left, right)), x.astype(F32), gains)
        return spread_rows(first.astype(BF16)), first, normal, inverse

    def fold_two(left, right, first, grad, gains):
        if own:
            kinds = [rows_low, rows_f32, sums_type]
            whole, result, d_pre, sums = group_fold(1, "two", left, right, gains, [first, grad], kinds)
            return whole.reshape(left.shape[0], D), result, d_pre, sums
        grad = grad.astype(F32)
        result, d_pre, terms = second_norm(fold(dot_cols(left, right)), first, grad, gains)
        return spread_rows(d_pre.astype(BF16)), result.astype(BF16), d_pre, stack_sums(terms, grad)

    def fold_back(left, right, d_pre_two, normal, inverse, gains):
        if own:
            kinds = [rows_f32, sums_type]
            whole, d_pre, sums = group_fold(7, "back", left, right, gains, [d_pre_two, normal, inverse], kinds)
            return whole.reshape(left.shape[0], D), d_pre, sums
        d_pre, terms, d_first = first_back(fold(dot_cols(left, right)), d_pre_two, normal, inverse, gains)
        return spread_rows(d_pre.astype(BF16)), d_pre, stack_sums(terms, d_first)

    def fold_last(left, right, d_pre, gains):
        if own:
            (out,) = group_fold(8, "last", left, right, gains, [d_pre], [rows_low])
            return out
        return (deep_alpha * d_pre + fold(dot_cols(left, right))).astype(BF16)

    def gather(block):
        return lax.all_gather(block, "z", axis=0, tiled=True)

    def scatter(partial):
        return lax.psum_scatter(partial.astype(BF16), "z", scatter_dimension=0, tiled=True)

    def pad_ff(array):
        return jnp.pad(array, ((0, 0), (0, group * tile - ff))).reshape(piece, group, tile)

    masked = jnp.max(flags) > 0
    prefix = jnp.where(masked, SEQ_LEN, SEQ_LEN - span_len[0])
    info = jnp.concatenate([gone, bone, gtwo, btwo, jnp.stack([prefix, span_start[0]]).astype(BF16)])
    info = jnp.pad(info[None, :], ((0, 15), (0, -info.shape[0] % 128)))

    x_perm = permute(x_in)
    qkv_blocks = jnp.moveaxis(w_qkv.reshape(piece, 3, group, width), 2, 0).reshape(group, piece, 3 * width)
    in_blocks = jnp.stack([pad_ff(w_in[:, :ff]), pad_ff(w_in[:, ff:])], axis=2)
    in_blocks = jnp.moveaxis(in_blocks, 1, 0).reshape(group, piece, 2 * tile)
    out_blocks = jnp.moveaxis(pad_ff(w_out), 1, 0)
    w_dense = permute(w_dense)
    if own:
        w_qkv_part, w_dense_part, info, in_blocks, out_blocks, x_all = opening(
            zs, qkv_blocks, w_dense, info, in_blocks, out_blocks, x_perm
        )
        x_all = x_all.reshape(group * SEQ_LEN, D)
        w_qkv_part = w_qkv_part.reshape(D, 3 * width)
        w_dense_part = w_dense_part.reshape(zs * piece, D)
    else:
        qkv_blocks, in_blocks, out_blocks = swap(2, [qkv_blocks, in_blocks, out_blocks], (False,) * 3)
        w_qkv_part = gather(qkv_blocks.reshape(group * piece, 3 * width))
        w_dense_part = gather(w_dense)
        info = lax.all_gather(lax.all_gather(info, GROUP, axis=0), "z", axis=0)
        x_all = spread_rows(x_perm)
    w_in_part = gather(in_blocks.reshape(group * piece, 2 * tile))
    out_blocks, w_in_part = lax.optimization_barrier((out_blocks, w_in_part))
    w_out_part = gather(out_blocks.reshape(group * piece, tile))
    info = info[:, :, 0]
    place_info = info[lax.axis_index("z"), :, 4 * piece : 4 * piece + 2].astype(jnp.int32)
    prefix, start = place_info[:, 0], place_info[:, 1]
    gains = info[:, :, : 4 * piece].astype(F32).reshape(zs, group, 4, piece)
    gains = jnp.pad(jnp.transpose(gains, (2, 0, 1, 3)).reshape(4, D), ((0, 4), (0, 0)))

    cosine, sine = tables(prefix, start)
    packed = dot(x_all, w_qkv_part)
    qkv, context = attend(prefix, packed, cosine, sine)
    first_all, first, normal_one, inverse_one = fold_one(context, w_dense_part, x_perm, gains)
    projected = dot(first_all, w_in_part)
    gate, up = projected[:, :tile], projected[:, tile:]
    act, slope = gate_parts(gate)
    hidden = (act * up).astype(BF16)
    d_branch, layer_out, d_pre_two, sums_two = fold_two(hidden, w_out_part, first, permute(d_out), gains)
    layer_out = restore(layer_out)
    d_w_out = dot_rows(d_branch, hidden).astype(BF16)
    d_w_out, d_branch = lax.optimization_barrier((d_w_out, d_branch))
    d_w_out = scatter(d_w_out)
    d_hidden = dot(d_branch, w_out_part)
    d_projected = jnp.concatenate([d_hidden * up * slope, d_hidden * act], axis=1).astype(BF16)
    d_w_in = dot_rows(first_all, d_projected).astype(BF16)
    d_w_in, d_projected = lax.optimization_barrier((d_w_in, d_projected))
    d_w_in = scatter(d_w_in)
    d_attn, d_pre_one, sums_one = fold_back(d_projected, w_in_part, d_pre_two, normal_one, inverse_one, gains)
    d_attn, d_w_out = lax.optimization_barrier((d_attn, d_w_out))
    sums = jnp.concatenate([sums_one[:2], sums_two[:2], jnp.zeros((4, D), F32)])
    d_w_out, sums = swap(4, [d_w_out.reshape(group, piece, tile), sums], (False, True))
    sums = jnp.sum(sums, axis=0)[:4].reshape(4, zs, group, piece)
    mine = lax.axis_index(GROUP)
    sums = lax.dynamic_index_in_dim(sums, mine, 2, keepdims=False).reshape(4, width)
    sums = jnp.pad(sums.T, ((0, 0), (0, 124)))
    d_context = dot_cols(d_attn, w_dense_part).astype(BF16)
    d_packed = attend_back(prefix, qkv, d_context, cosine, sine)
    d_w_qkv = dot_rows(x_all, d_packed).astype(BF16)
    d_w_qkv, d_packed, d_attn = lax.optimization_barrier((d_w_qkv, d_packed, d_attn))
    d_w_qkv = scatter(d_w_qkv)
    d_dense = jnp.concatenate([dot_rows(context, d_attn), sums], axis=1).astype(BF16)
    d_dense, d_packed, d_w_in = lax.optimization_barrier((d_dense, d_packed, d_w_in))
    d_dense = scatter(d_dense)
    d_input = restore(fold_last(d_packed, w_qkv_part, d_pre_one, gains))

    def settle(name, summed):
        (blocks,) = swap(name, [summed.reshape(group, piece, summed.shape[1])], (False,))
        return blocks.astype(F32)

    out_out = jnp.moveaxis(d_w_out.astype(F32), 0, 1).reshape(piece, group * tile)[:, :ff]
    out_in = jnp.transpose(settle(6, d_w_in).reshape(group, piece, 2, tile), (1, 2, 0, 3))
    out_in = out_in.reshape(piece, 2, group * tile)
    out_in = jnp.concatenate([out_in[:, 0, :ff], out_in[:, 1, :ff]], axis=1)
    out_qkv = jnp.transpose(settle(5, d_w_qkv).reshape(group, piece, 3, width), (1, 2, 0, 3)).reshape(piece, 3 * D)
    out_dense = restore(d_dense[:, :D]).astype(F32)
    ends = d_dense[:, D : D + 4].astype(F32)
    return layer_out, d_input, out_qkv, out_dense, out_in, out_out, ends[:, 0], ends[:, 1], ends[:, 2], ends[:, 3]


def solution(mesh):
    grp, shard = mesh.shape["grp"], mesh.shape["shard"]
    sizes = (grp // 4, 2, 2, shard)
    inner = Mesh(mesh.devices.reshape(sizes), ALL)
    rows, flat = P(ALL, None), P(ALL)
    return jax.shard_map(
        functools.partial(on_device, sizes),
        mesh=inner,
        in_specs=(rows,) * 6 + (flat,) * 7,
        out_specs=(rows,) * 6 + (flat,) * 4,
        check_vma=False,
    )
```

```python
import functools

import jax
import jax.numpy as jnp
from jax import lax
from jax.experimental import pallas as pl
from jax.experimental.pallas import tpu as pltpu
from jax.sharding import Mesh
from jax.sharding import PartitionSpec as P

HEADS = 16
HEAD = 128
SEQ_LEN = 224
D = HEADS * HEAD
deep_alpha = 6.928203230275509
norm_eps = 1e-05
far_below = -1e30
scale = HEAD ** (-0.5)

ALL = ("gy", "gx", "core", "z")
GROUP = ("gy", "gx", "core")
MESH = pl.DeviceIdType.MESH
F32 = jnp.float32
BF16 = jnp.bfloat16


def dot(left, right):
    return jnp.dot(left, right, preferred_element_type=F32)


def dot_rows(left, right):
    return lax.dot_general(left, right, (((0,), (0,)), ((), ())), preferred_element_type=F32)


def dot_cols(left, right):
    return lax.dot_general(left, right, (((1,), (1,)), ((), ())), preferred_element_type=F32)


def swap_halves(block):
    lane = lax.broadcasted_iota(jnp.int32, block.shape, 1)
    return jnp.where((lane & 32) == 0, pltpu.roll(block, 96, 1), pltpu.roll(block, 32, 1))


def seen(prefix):
    row = lax.broadcasted_iota(jnp.int32, (SEQ_LEN, SEQ_LEN), 0)
    col = lax.broadcasted_iota(jnp.int32, (SEQ_LEN, SEQ_LEN), 1)
    return (col < prefix) | (col <= row)


def softmax(queries, keys, visible):
    scores = jnp.where(visible, dot_cols(queries, keys), far_below)
    weights = jnp.exp(scores - jnp.max(scores, axis=1, keepdims=True))
    return weights / jnp.sum(weights, axis=1, keepdims=True)


def attend_kernel(prefix_ref, packed_ref, cos_ref, sin_ref, qkv_ref, context_ref):
    width = context_ref.shape[1]
    visible = seen(prefix_ref[pl.program_id(0)])
    cosine = cos_ref[0]
    sine = sin_ref[0]
    for head in range(width // HEAD):
        at = pl.ds(head * HEAD, HEAD)
        at_k = pl.ds(width + head * HEAD, HEAD)
        at_v = pl.ds(2 * width + head * HEAD, HEAD)
        raw = packed_ref[:, at]
        queries = ((raw * cosine + swap_halves(raw) * sine) * scale).astype(BF16)
        raw = packed_ref[:, at_k]
        keys = (raw * cosine + swap_halves(raw) * sine).astype(BF16)
        values = packed_ref[:, at_v].astype(BF16)
        qkv_ref[:, at] = queries
        qkv_ref[:, at_k] = keys
        qkv_ref[:, at_v] = values
        probs = softmax(queries, keys, visible).astype(BF16)
        context_ref[:, at] = dot(probs, values).astype(BF16)


def attend_back_kernel(prefix_ref, qkv_ref, d_context_ref, cos_ref, sin_ref, d_packed_ref):
    width = d_context_ref.shape[1]
    visible = seen(prefix_ref[pl.program_id(0)])
    cosine = cos_ref[0]
    sine = sin_ref[0]
    for head in range(width // HEAD):
        at = pl.ds(head * HEAD, HEAD)
        at_k = pl.ds(width + head * HEAD, HEAD)
        at_v = pl.ds(2 * width + head * HEAD, HEAD)
        queries = qkv_ref[:, at]
        keys = qkv_ref[:, at_k]
        values = qkv_ref[:, at_v]
        d_context = d_context_ref[:, at]
        probs = softmax(queries, keys, visible)
        d_packed_ref[:, at_v] = dot_rows(probs.astype(BF16), d_context).astype(BF16)
        d_probs = dot_cols(d_context, values)
        inner = jnp.sum(probs * d_probs, axis=1, keepdims=True)
        d_scores = (probs * (d_probs - inner)).astype(BF16)
        grad = dot(d_scores, keys) * scale
        d_packed_ref[:, at] = (grad * cosine - swap_halves(grad) * sine).astype(BF16)
        grad = dot_rows(d_scores, queries)
        d_packed_ref[:, at_k] = (grad * cosine - swap_halves(grad) * sine).astype(BF16)


def by_sequence(width):
    return pl.BlockSpec((SEQ_LEN, width), lambda s: (s, 0))


TABLE = pl.BlockSpec((1, SEQ_LEN, HEAD), lambda s: (s, 0, 0))
SCALARS = pl.BlockSpec(memory_space=pltpu.SMEM)
PARAMS = pltpu.CompilerParams(vmem_limit_bytes=48 * 2**20)


def attend(prefix, packed, cosine, sine):
    rows, width = packed.shape[0], packed.shape[1] // 3
    return pl.pallas_call(
        attend_kernel,
        grid=(rows // SEQ_LEN,),
        in_specs=[SCALARS, by_sequence(3 * width), TABLE, TABLE],
        out_specs=[by_sequence(3 * width), by_sequence(width)],
        out_shape=[
            jax.ShapeDtypeStruct((rows, 3 * width), BF16),
            jax.ShapeDtypeStruct((rows, width), BF16),
        ],
        compiler_params=PARAMS,
    )(prefix, packed, cosine, sine)


def attend_back(prefix, qkv, d_context, cosine, sine):
    rows, width = d_context.shape
    return pl.pallas_call(
        attend_back_kernel,
        grid=(rows // SEQ_LEN,),
        in_specs=[SCALARS, by_sequence(3 * width), by_sequence(width), TABLE, TABLE],
        out_specs=by_sequence(3 * width),
        out_shape=jax.ShapeDtypeStruct((rows, 3 * width), BF16),
        compiler_params=PARAMS,
    )(prefix, qkv, d_context, cosine, sine)


def tables(prefix, start):
    place = jnp.arange(SEQ_LEN, dtype=jnp.int32)
    in_span = place[None, :] >= prefix[:, None]
    pos_one = jnp.where(in_span, start[:, None], place[None, :])
    pos_two = jnp.where(in_span, place[None, :] - prefix[:, None] + 1, 0)
    lane = jnp.arange(HEAD)
    freqs = 10000.0 ** (-2.0 * (lane % 32).astype(F32) / 64)
    place_of = jnp.where(lane[None, None, :] < 64, pos_one[:, :, None], pos_two[:, :, None])
    angles = place_of.astype(F32) * freqs
    sign = jnp.where(lane % 64 < 32, -1.0, 1.0)
    return jnp.cos(angles), jnp.sin(angles) * sign


def norm_parts(values):
    center = values - jnp.mean(values, axis=-1, keepdims=True)
    inverse = lax.rsqrt(jnp.mean(center * center, axis=-1, keepdims=True) + norm_eps)
    return center * inverse, inverse


def norm_back(normal, inverse, gain, grad):
    scaled = gain * grad
    return inverse * (
        scaled
        - jnp.mean(scaled, axis=-1, keepdims=True)
        - normal * jnp.mean(scaled * normal, axis=-1, keepdims=True)
    )


def gate_parts(gate):
    phi = 0.5 * (1.0 + lax.erf(gate * 0.7071067811865476))
    slope = phi + gate * jnp.exp(-0.5 * gate * gate) * 0.3989422804014327
    return gate * phi, slope


def here():
    return lax.axis_index("gy"), lax.axis_index("gx"), lax.axis_index("core")


def place(y, x, c):
    return (y * 2 + x) * 2 + c


def greet(peers):
    barrier = pltpu.get_barrier_semaphore()
    for peer in peers:
        pl.semaphore_signal(barrier, inc=1, device_id=peer, device_id_type=MESH)
    pl.semaphore_wait(barrier, len(peers))


def spread_block(cut, base, block_ref, out_ref, send, recv, local):
    rows = block_ref.shape[0]
    y, x, c = here()
    to_x, to_y, to_c = {"gx": 1 - x}, {"gy": 1 - y}, {"core": 1 - c}
    me, by_x, by_y, far = place(y, x, c), place(y, 1 - x, c), place(1 - y, x, c), place(1 - y, 1 - x, c)
    low, high = pl.ds(0, cut), pl.ds(cut, rows - cut)

    def push(k, src, dst, to):
        copy = pltpu.make_async_remote_copy(
            src_ref=src, dst_ref=dst, send_sem=send.at[base + k], recv_sem=recv.at[base + k], device_id=to, device_id_type=MESH
        )
        copy.start()
        return copy

    def landed(k, dst):
        pltpu.make_async_remote_copy(
            src_ref=dst, dst_ref=dst, send_sem=send.at[base + k], recv_sem=recv.at[base + k], device_id=to_c, device_id_type=MESH
        ).wait_recv()

    sent = [
        push(0, block_ref.at[low], out_ref.at[me, low], to_x),
        push(1, block_ref.at[high], out_ref.at[me, high], to_y),
        push(2, block_ref.at[high], out_ref.at[me, high], to_x),
        push(3, block_ref.at[low], out_ref.at[me, low], to_y),
        push(4, block_ref, out_ref.at[me], to_c),
    ]
    keep = pltpu.make_async_copy(block_ref, out_ref.at[me], local)
    keep.start()
    landed(0, out_ref.at[by_x, low])
    sent.append(push(5, out_ref.at[by_x, low], out_ref.at[by_x, low], to_y))
    sent.append(push(7, out_ref.at[by_x, low], out_ref.at[by_x, low], to_c))
    landed(1, out_ref.at[by_y, high])
    sent.append(push(6, out_ref.at[by_y, high], out_ref.at[by_y, high], to_x))
    sent.append(push(8, out_ref.at[by_y, high], out_ref.at[by_y, high], to_c))
    landed(2, out_ref.at[by_x, high])
    sent.append(push(9, out_ref.at[by_x, high], out_ref.at[by_x, high], to_c))
    landed(3, out_ref.at[by_y, low])
    sent.append(push(10, out_ref.at[by_y, low], out_ref.at[by_y, low], to_c))
    landed(5, out_ref.at[far, low])
    sent.append(push(11, out_ref.at[far, low], out_ref.at[far, low], to_c))
    landed(6, out_ref.at[far, high])
    sent.append(push(12, out_ref.at[far, high], out_ref.at[far, high], to_c))
    other, other_x, other_y, other_far = (
        place(y, x, 1 - c),
        place(y, 1 - x, 1 - c),
        place(1 - y, x, 1 - c),
        place(1 - y, 1 - x, 1 - c),
    )
    landed(4, out_ref.at[other])
    landed(7, out_ref.at[other_x, low])
    landed(8, out_ref.at[other_y, high])
    landed(9, out_ref.at[other_x, high])
    landed(10, out_ref.at[other_y, low])
    landed(11, out_ref.at[other_far, low])
    landed(12, out_ref.at[other_far, high])
    keep.wait()
    for copy in sent:
        copy.wait_send()


def gather_kernel(cut, block_ref, out_ref, send, recv, local):
    y, x, c = here()
    greet([{"gx": 1 - x}, {"gy": 1 - y}, {"core": 1 - c}])
    spread_block(cut, 0, block_ref, out_ref, send, recv, local)


ANY = pl.BlockSpec(memory_space=pl.ANY)


def group_gather(block):
    rows, width = block.shape
    return pl.pallas_call(
        functools.partial(gather_kernel, rows // 2),
        out_shape=jax.ShapeDtypeStruct((8, rows, width), block.dtype),
        in_specs=[ANY],
        out_specs=ANY,
        scratch_shapes=[pltpu.SemaphoreType.DMA((13,)), pltpu.SemaphoreType.DMA((13,)), pltpu.SemaphoreType.DMA],
        compiler_params=pltpu.CompilerParams(collective_id=9, has_side_effects=True),
        cost_estimate=pl.CostEstimate(flops=0, bytes_accessed=100 * 2**20, transcendentals=0),
    )(block)


SLAB = 16
ROWS = pl.BlockSpec(memory_space=pltpu.VMEM)
CHIP_COLS = 256


def first_norm(total, x, gains):
    normal, inverse = norm_parts(deep_alpha * x + total)
    first = normal * gains[0:1] + gains[1:2]
    return first, normal, inverse


def second_norm(total, first, grad, gains):
    normal, inverse = norm_parts(deep_alpha * first + total)
    return normal * gains[2:3] + gains[3:4], norm_back(normal, inverse, gains[2:3], grad), grad * normal


def first_back(total, d_pre_two, normal, inverse, gains):
    d_first = deep_alpha * d_pre_two + total
    return norm_back(normal, inverse, gains[0:1], d_first), d_first * normal, d_first


def fold_kernel(mode, across, n_aux, n_out, *refs):
    left_ref, right_ref, gains_ref = refs[:3]
    aux_refs = refs[3 : 3 + n_aux]
    refs = refs[3 + n_aux :]
    spread = mode != "last"
    if spread:
        all_ref, refs = refs[0], refs[1:]
    outs, refs = refs[:n_out], refs[n_out:]
    aux, refs = refs[:n_aux], refs[n_aux:]
    left, right, part, got, near_x, near_y, from_x, from_y, block, acc, send, recv, local = refs
    rows, width = block.shape
    cut = near_x.shape[0]
    y, x, c = here()
    to_x, to_y, to_c = {"gx": 1 - x}, {"gy": 1 - y}, {"core": 1 - c}
    chips = [(1 - y, 1 - x), (y, 1 - x), (1 - y, x), (y, x)]
    low, high = pl.ds(0, cut), pl.ds(cut, rows - cut)

    def push(k, src, dst, to):
        copy = pltpu.make_async_remote_copy(
            src_ref=src, dst_ref=dst, send_sem=send.at[k], recv_sem=recv.at[k], device_id=to, device_id_type=MESH
        )
        copy.start()
        return copy

    def add(k, extra, start, size, offset=0):
        @pl.loop(0, size // SLAB)
        def _(step):
            at = pl.ds(pl.multiple_of(start + step * SLAB, SLAB), SLAB)
            of = pl.ds(pl.multiple_of(start - offset + step * SLAB, SLAB), SLAB)
            part[k, c, at] = (part[k, c, at].astype(F32) + extra[of].astype(F32)).astype(BF16)

    loads = [pltpu.make_async_copy(left_ref.at[a * 2 + b], left.at[k], local.at[k]) for k, (a, b) in enumerate(chips)]
    load_right = pltpu.make_async_copy(right_ref, right, local.at[4])
    load_aux = [pltpu.make_async_copy(r, v, local.at[5 + k]) for k, (r, v) in enumerate(zip(aux_refs, aux))]
    loads[0].start()
    load_right.start()
    for load in loads[1:] + load_aux:
        load.start()
    greet([to_x, to_y, to_c])

    def product(k):
        loads[k].wait()

        @pl.loop(0, width // CHIP_COLS)
        def _(step):
            at = pl.ds(pl.multiple_of(step * CHIP_COLS, CHIP_COLS), CHIP_COLS)
            here_part = dot_cols(left[k], right[at]) if across else dot(left[k], right[:, at])
            part[k, 0, :, at] = here_part[:rows].astype(BF16)
            part[k, 1, :, at] = here_part[rows:].astype(BF16)

        return push(k, part.at[k, 1 - c], got.at[k], to_c)

    load_right.wait()
    sent = [product(0), product(1)]
    sent[0].wait_recv()
    add(0, got.at[0], 0, rows)
    far_x = push(4, part.at[0, c, low], near_x, to_x)
    far_y = push(5, part.at[0, c, high], near_y, to_y)
    sent.append(product(2))
    sent[1].wait_recv()
    add(1, got.at[1], 0, rows)
    plain_x = push(6, part.at[1, c, low], from_x.at[low], to_x)
    sent[2].wait_recv()
    add(2, got.at[2], 0, rows)
    plain_y = push(7, part.at[2, c, high], from_y.at[high], to_y)
    sent.append(product(3))
    far_y.wait_recv()
    add(1, near_y, cut, rows - cut, cut)
    more_x = push(8, part.at[1, c, high], from_x.at[high], to_x)
    far_x.wait_recv()
    add(2, near_x, 0, cut)
    more_y = push(9, part.at[2, c, low], from_y.at[low], to_y)
    sent[3].wait_recv()
    for load in load_aux:
        load.wait()
    plain_x.wait_recv()
    plain_y.wait_recv()
    more_x.wait_recv()
    more_y.wait_recv()
    gains = gains_ref[...]
    acc[...] = jnp.zeros_like(acc)

    @pl.loop(0, rows // SLAB)
    def _(step):
        at = pl.ds(pl.multiple_of(step * SLAB, SLAB), SLAB)
        total = part[3, c, at].astype(F32) + got[3, at].astype(F32) + from_x[at].astype(F32) + from_y[at].astype(F32)
        held = [a[at].astype(F32) for a in aux]
        if mode == "one":
            first, normal, inverse = first_norm(total, held[0], gains)
            outs[0][at] = first
            outs[1][at] = normal
            outs[2][at] = jnp.broadcast_to(inverse, (SLAB, 128))
            block[at] = first.astype(BF16)
        elif mode == "two":
            result, d_pre, terms = second_norm(total, held[0], held[1], gains)
            outs[0][at] = result.astype(BF16)
            outs[1][at] = d_pre
            block[at] = d_pre.astype(BF16)
            acc[0] += terms
            acc[1] += held[1]
        elif mode == "back":
            d_pre, terms, d_first = first_back(total, held[0], held[1], held[2][:, 0:1], gains)
            outs[0][at] = d_pre
            block[at] = d_pre.astype(BF16)
            acc[0] += terms
            acc[1] += d_first
        else:
            outs[0][at] = (deep_alpha * held[0] + total).astype(BF16)

    if mode in ("two", "back"):
        outs[-1][0:1] = jnp.sum(acc[0], axis=0, keepdims=True)
        outs[-1][1:2] = jnp.sum(acc[1], axis=0, keepdims=True)
    for copy in sent + [far_x, far_y, plain_x, plain_y, more_x, more_y]:
        copy.wait_send()
    if spread:
        spread_block(cut, 10, block, all_ref, send, recv, local.at[4])


def group_fold(name, mode, left, right, gains, aux, out_types):
    across = mode != "one"
    rows, depth = left.shape[0] // 8, left.shape[1]
    width = gains.shape[1]
    cut = rows // 2
    spread = mode != "last"
    out_shape = [jax.ShapeDtypeStruct((8, rows, width), BF16)] * spread + out_types
    n = len(aux)
    n_sems = 23 if spread else 10
    return pl.pallas_call(
        functools.partial(fold_kernel, mode, across, n, len(out_types)),
        out_shape=out_shape,
        in_specs=[ANY, ANY, ROWS] + [ANY] * n,
        out_specs=[ANY] * spread + [ROWS] * len(out_types),
        scratch_shapes=[pltpu.VMEM(a.shape, a.dtype) for a in aux]
        + [
            pltpu.VMEM((4, 2 * rows, depth), BF16),
            pltpu.VMEM(right.shape, BF16),
            pltpu.VMEM((4, 2, rows, width), BF16),
            pltpu.VMEM((4, rows, width), BF16),
            pltpu.VMEM((cut, width), BF16),
            pltpu.VMEM((rows - cut, width), BF16),
            pltpu.VMEM((rows, width), BF16),
            pltpu.VMEM((rows, width), BF16),
            pltpu.VMEM((rows, width), BF16),
            pltpu.VMEM((2, SLAB, width), F32),
            pltpu.SemaphoreType.DMA((n_sems,)),
            pltpu.SemaphoreType.DMA((n_sems,)),
            pltpu.SemaphoreType.DMA((5 + n,)),
        ],
        compiler_params=pltpu.CompilerParams(
            collective_id=name, has_side_effects=True, vmem_limit_bytes=50 * 2**20
        ),
        cost_estimate=pl.CostEstimate(flops=0, bytes_accessed=(200 if spread else 110) * 2**20, transcendentals=0),
    )(left.reshape(4, 2 * rows, depth), right, gains, *aux)


def swap_kernel(spread, *refs):
    n = len(spread)
    blocks, outs = refs[:n], refs[n : 2 * n]
    send, recv, local = refs[2 * n :]
    y, x, c = here()
    me = place(y, x, c)
    peers = [((y + k // 4) % 2, (x + k // 2 % 2) % 2, (c + k % 2) % 2) for k in range(1, 8)]
    names = [{"gy": p[0], "gx": p[1], "core": p[2]} for p in peers]
    greet(names)
    copies, comes, keeps = [], [], []
    for i in range(n):
        for k, (peer, name) in enumerate(zip(peers, names)):
            src = blocks[i] if spread[i] else blocks[i].at[place(*peer)]
            landing = outs[i].at[place(*peer)]
            sems = dict(send_sem=send.at[i, k], recv_sem=recv.at[i, k], device_id=name, device_id_type=MESH)
            copies.append(pltpu.make_async_remote_copy(src_ref=src, dst_ref=outs[i].at[me], **sems))
            comes.append(pltpu.make_async_remote_copy(src_ref=landing, dst_ref=landing, **sems))
            copies[-1].start()
        keeps.append(
            pltpu.make_async_copy(blocks[i] if spread[i] else blocks[i].at[me], outs[i].at[me], local.at[i])
        )
        keeps[-1].start()
    for come in comes:
        come.wait_recv()
    for copy in copies:
        copy.wait_send()
    for keep in keeps:
        keep.wait()


def group_swap(name, arrays, spread):
    n = len(arrays)
    shapes = [((8,) if s else ()) + a.shape for a, s in zip(arrays, spread)]
    return pl.pallas_call(
        functools.partial(swap_kernel, spread),
        out_shape=[jax.ShapeDtypeStruct(s, a.dtype) for a, s in zip(arrays, shapes)],
        in_specs=[ANY] * n,
        out_specs=[ANY] * n,
        scratch_shapes=[
            pltpu.SemaphoreType.DMA((n, 7)),
            pltpu.SemaphoreType.DMA((n, 7)),
            pltpu.SemaphoreType.DMA((n,)),
        ],
        compiler_params=pltpu.CompilerParams(collective_id=name, has_side_effects=True),
        cost_estimate=pl.CostEstimate(flops=0, bytes_accessed=50 * 2**20, transcendentals=0),
    )(*arrays)


def on_device(sizes, x_in, d_out, w_qkv, w_dense, w_in, w_out, gone, bone, gtwo, btwo, flags, span_start, span_len):
    gy, gx, cores, zs = sizes
    piece = w_qkv.shape[0]
    ff = w_out.shape[1]
    group = gy * gx * cores
    width = D // group
    tile = -(-ff // (group * 128)) * 128
    own = gy == 2

    def permute(array):
        lead = array.shape[:-1]
        return jnp.swapaxes(array.reshape(lead + (group, zs, piece)), -3, -2).reshape(lead + (D,))

    def restore(array):
        lead = array.shape[:-1]
        return jnp.swapaxes(array.reshape(lead + (zs, group, piece)), -3, -2).reshape(lead + (D,))

    def swap(name, arrays, spread):
        if own:
            return group_swap(name, arrays, spread)
        return [
            lax.all_gather(a, GROUP, axis=0) if s else lax.all_to_all(a, GROUP, 0, 0, tiled=True)
            for a, s in zip(arrays, spread)
        ]

    def spread_rows(block):
        whole = group_gather(block) if own else lax.all_gather(block, GROUP, axis=0)
        return whole.reshape(group * block.shape[0], block.shape[1])

    rows_f32 = jax.ShapeDtypeStruct((SEQ_LEN, D), F32)
    rows_low = jax.ShapeDtypeStruct((SEQ_LEN, D), BF16)
    sums_type = jax.ShapeDtypeStruct((8, D), F32)

    def fold(partial):
        return lax.psum_scatter(partial.astype(BF16), GROUP, scatter_dimension=0, tiled=True).astype(F32)

    def stack_sums(*arrays):
        return jnp.pad(jnp.stack([jnp.sum(a, axis=0) for a in arrays]), ((0, 6), (0, 0)))

    def fold_one(left, right, x, gains):
        if own:
            kinds = [rows_f32, rows_f32, jax.ShapeDtypeStruct((SEQ_LEN, 128), F32)]
            whole, first, normal, inverse = group_fold(0, "one", left, right, gains, [x], kinds)
            return whole.reshape(left.shape[0], D), first, normal, inverse
        first, normal, inverse = first_norm(fold(dot(left, right)), x.astype(F32), gains)
        return spread_rows(first.astype(BF16)), first, normal, inverse

    def fold_two(left, right, first, grad, gains):
        if own:
            kinds = [rows_low, rows_f32, sums_type]
            whole, result, d_pre, sums = group_fold(1, "two", left, right, gains, [first, grad], kinds)
            return whole.reshape(left.shape[0], D), result, d_pre, sums
        grad = grad.astype(F32)
        result, d_pre, terms = second_norm(fold(dot_cols(left, right)), first, grad, gains)
        return spread_rows(d_pre.astype(BF16)), result.astype(BF16), d_pre, stack_sums(terms, grad)

    def fold_back(left, right, d_pre_two, normal, inverse, gains):
        if own:
            kinds = [rows_f32, sums_type]
            whole, d_pre, sums = group_fold(7, "back", left, right, gains, [d_pre_two, normal, inverse], kinds)
            return whole.reshape(left.shape[0], D), d_pre, sums
        d_pre, terms, d_first = first_back(fold(dot_cols(left, right)), d_pre_two, normal, inverse, gains)
        return spread_rows(d_pre.astype(BF16)), d_pre, stack_sums(terms, d_first)

    def fold_last(left, right, d_pre, gains):
        if own:
            (out,) = group_fold(8, "last", left, right, gains, [d_pre], [rows_low])
            return out
        return (deep_alpha * d_pre + fold(dot_cols(left, right))).astype(BF16)

    def gather(block):
        return lax.all_gather(block, "z", axis=0, tiled=True)

    def scatter(partial):
        return lax.psum_scatter(partial.astype(BF16), "z", scatter_dimension=0, tiled=True)

    def pad_ff(array):
        return jnp.pad(array, ((0, 0), (0, group * tile - ff))).reshape(piece, group, tile)

    masked = jnp.max(flags) > 0
    prefix = jnp.where(masked, SEQ_LEN, SEQ_LEN - span_len[0])
    info = jnp.pad(jnp.stack([prefix, span_start[0]]).astype(BF16)[None, :], ((0, 15), (0, 126)))

    ends = jnp.pad(jnp.stack([gone, bone, gtwo, btwo], axis=1), ((0, 0), (0, 124)))
    dense_block = gather(jnp.concatenate([permute(w_dense), ends], axis=1))
    w_dense_part = dense_block[:, :D]
    qkv_blocks = jnp.moveaxis(w_qkv.reshape(piece, 3, group, width), 2, 0).reshape(group, piece, 3 * width)
    qkv_blocks, info = swap(2, [qkv_blocks, info], (False, True))
    w_qkv_part = gather(qkv_blocks.reshape(group * piece, 3 * width))
    prefix, start = info[:, 0, 0].astype(jnp.int32), info[:, 0, 1].astype(jnp.int32)

    x_perm = permute(x_in)
    x_all = spread_rows(x_perm)
    in_blocks = jnp.stack([pad_ff(w_in[:, :ff]), pad_ff(w_in[:, ff:])], axis=2)
    in_blocks = jnp.moveaxis(in_blocks, 1, 0).reshape(group, piece, 2 * tile)
    out_blocks = jnp.moveaxis(pad_ff(w_out), 1, 0)
    ends = jnp.pad(dense_block[:, D : D + 4].T, ((0, 12), (0, 0)))
    in_blocks, out_blocks, ends = swap(3, [in_blocks, out_blocks, ends], (False, False, True))
    ends = ends[:, :4].astype(F32).reshape(group, 4, zs, piece)
    gains = jnp.pad(jnp.transpose(ends, (1, 2, 0, 3)).reshape(4, D), ((0, 4), (0, 0)))

    cosine, sine = tables(prefix, start)
    in_blocks, w_qkv_part, x_all, cosine, sine, gains = lax.optimization_barrier(
        (in_blocks, w_qkv_part, x_all, cosine, sine, gains)
    )
    w_in_part = gather(in_blocks.reshape(group * piece, 2 * tile))
    packed = dot(x_all, w_qkv_part)
    qkv, context = attend(prefix, packed, cosine, sine)
    first_all, first, normal_one, inverse_one = fold_one(context, w_dense_part, x_perm, gains)
    out_blocks, first_all, w_in_part = lax.optimization_barrier((out_blocks, first_all, w_in_part))
    w_out_part = gather(out_blocks.reshape(group * piece, tile))
    projected = dot(first_all, w_in_part)
    gate, up = projected[:, :tile], projected[:, tile:]
    act, slope = gate_parts(gate)
    hidden = (act * up).astype(BF16)
    d_branch, layer_out, d_pre_two, sums_two = fold_two(hidden, w_out_part, first, permute(d_out), gains)
    layer_out = restore(layer_out)
    d_w_out = dot_rows(d_branch, hidden).astype(BF16)
    d_w_out, d_branch = lax.optimization_barrier((d_w_out, d_branch))
    d_w_out = scatter(d_w_out)
    d_hidden = dot(d_branch, w_out_part)
    d_projected = jnp.concatenate([d_hidden * up * slope, d_hidden * act], axis=1).astype(BF16)
    d_w_in = dot_rows(first_all, d_projected).astype(BF16)
    d_w_in, d_projected = lax.optimization_barrier((d_w_in, d_projected))
    d_w_in = scatter(d_w_in)
    d_attn, d_pre_one, sums_one = fold_back(d_projected, w_in_part, d_pre_two, normal_one, inverse_one, gains)
    d_attn, d_w_out = lax.optimization_barrier((d_attn, d_w_out))
    d_context = dot_cols(d_attn, w_dense_part).astype(BF16)
    d_packed = attend_back(prefix, qkv, d_context, cosine, sine)
    d_w_qkv = dot_rows(x_all, d_packed).astype(BF16)
    sums = jnp.concatenate([sums_one[:2], sums_two[:2], jnp.zeros((4, D), F32)])
    d_w_out, sums = swap(4, [d_w_out.reshape(group, piece, tile), sums], (False, True))
    sums = jnp.sum(sums, axis=0)[:4].reshape(4, zs, group, piece)
    mine = lax.axis_index(GROUP)
    sums = lax.dynamic_index_in_dim(sums, mine, 2, keepdims=False).reshape(4, width)
    sums = jnp.pad(sums.T, ((0, 0), (0, 124)))
    d_dense = jnp.concatenate([dot_rows(context, d_attn), sums], axis=1).astype(BF16)
    d_dense, d_packed, d_w_qkv, d_w_in = lax.optimization_barrier((d_dense, d_packed, d_w_qkv, d_w_in))
    d_w_qkv = scatter(d_w_qkv)
    d_input = fold_last(d_packed, w_qkv_part, d_pre_one, gains)
    (d_w_in,) = swap(6, [d_w_in.reshape(group, piece, 2 * tile)], (False,))
    d_dense, d_input, d_w_in, d_w_qkv = lax.optimization_barrier((d_dense, d_input, d_w_in, d_w_qkv))
    d_dense = scatter(d_dense)
    (d_w_qkv,) = swap(5, [d_w_qkv.reshape(group, piece, 3 * width)], (False,))
    d_input = restore(d_input)

    out_out = jnp.moveaxis(d_w_out.astype(F32), 0, 1).reshape(piece, group * tile)[:, :ff]
    out_in = jnp.transpose(d_w_in.astype(F32).reshape(group, piece, 2, tile), (1, 2, 0, 3))
    out_in = out_in.reshape(piece, 2, group * tile)
    out_in = jnp.concatenate([out_in[:, 0, :ff], out_in[:, 1, :ff]], axis=1)
    out_qkv = jnp.transpose(d_w_qkv.astype(F32).reshape(group, piece, 3, width), (1, 2, 0, 3)).reshape(piece, 3 * D)
    out_dense = restore(d_dense[:, :D]).astype(F32)
    ends = d_dense[:, D : D + 4].astype(F32)
    return layer_out, d_input, out_qkv, out_dense, out_in, out_out, ends[:, 0], ends[:, 1], ends[:, 2], ends[:, 3]


def solution(mesh):
    grp, shard = mesh.shape["grp"], mesh.shape["shard"]
    sizes = (grp // 4, 2, 2, shard)
    inner = Mesh(mesh.devices.reshape(sizes), ALL)
    rows, flat = P(ALL, None), P(ALL)
    return jax.shard_map(
        functools.partial(on_device, sizes),
        mesh=inner,
        in_specs=(rows,) * 6 + (flat,) * 7,
        out_specs=(rows,) * 6 + (flat,) * 4,
        check_vma=False,
    )
```

```python
import functools

import jax
import jax.numpy as jnp
from jax import lax
from jax.experimental import pallas as pl
from jax.experimental.pallas import tpu as pltpu
from jax.sharding import Mesh
from jax.sharding import PartitionSpec as P

HEADS = 16
HEAD = 128
SEQ_LEN = 224
D = HEADS * HEAD
deep_alpha = 6.928203230275509
norm_eps = 1e-05
far_below = -1e30
scale = HEAD ** (-0.5)

ALL = ("gy", "gx", "core", "z")
GROUP = ("gy", "gx", "core")
MESH = pl.DeviceIdType.MESH
F32 = jnp.float32
BF16 = jnp.bfloat16


def dot(left, right):
    return jnp.dot(left, right, preferred_element_type=F32)


def dot_rows(left, right):
    return lax.dot_general(left, right, (((0,), (0,)), ((), ())), preferred_element_type=F32)


def dot_cols(left, right):
    return lax.dot_general(left, right, (((1,), (1,)), ((), ())), preferred_element_type=F32)


def swap_halves(block):
    lane = lax.broadcasted_iota(jnp.int32, block.shape, 1)
    return jnp.where((lane & 32) == 0, pltpu.roll(block, 96, 1), pltpu.roll(block, 32, 1))


def seen(prefix):
    row = lax.broadcasted_iota(jnp.int32, (SEQ_LEN, SEQ_LEN), 0)
    col = lax.broadcasted_iota(jnp.int32, (SEQ_LEN, SEQ_LEN), 1)
    return (col < prefix) | (col <= row)


def softmax(queries, keys, visible):
    scores = jnp.where(visible, dot_cols(queries, keys), far_below)
    weights = jnp.exp(scores - jnp.max(scores, axis=1, keepdims=True))
    return weights / jnp.sum(weights, axis=1, keepdims=True)


def attend_kernel(prefix_ref, packed_ref, cos_ref, sin_ref, qkv_ref, context_ref):
    width = context_ref.shape[1]
    visible = seen(prefix_ref[pl.program_id(0)])
    cosine = cos_ref[0]
    sine = sin_ref[0]
    for head in range(width // HEAD):
        at = pl.ds(head * HEAD, HEAD)
        at_k = pl.ds(width + head * HEAD, HEAD)
        at_v = pl.ds(2 * width + head * HEAD, HEAD)
        raw = packed_ref[:, at]
        queries = ((raw * cosine + swap_halves(raw) * sine) * scale).astype(BF16)
        raw = packed_ref[:, at_k]
        keys = (raw * cosine + swap_halves(raw) * sine).astype(BF16)
        values = packed_ref[:, at_v].astype(BF16)
        qkv_ref[:, at] = queries
        qkv_ref[:, at_k] = keys
        qkv_ref[:, at_v] = values
        probs = softmax(queries, keys, visible).astype(BF16)
        context_ref[:, at] = dot(probs, values).astype(BF16)


def attend_back_kernel(prefix_ref, qkv_ref, d_context_ref, cos_ref, sin_ref, d_packed_ref):
    width = d_context_ref.shape[1]
    visible = seen(prefix_ref[pl.program_id(0)])
    cosine = cos_ref[0]
    sine = sin_ref[0]
    for head in range(width // HEAD):
        at = pl.ds(head * HEAD, HEAD)
        at_k = pl.ds(width + head * HEAD, HEAD)
        at_v = pl.ds(2 * width + head * HEAD, HEAD)
        queries = qkv_ref[:, at]
        keys = qkv_ref[:, at_k]
        values = qkv_ref[:, at_v]
        d_context = d_context_ref[:, at]
        probs = softmax(queries, keys, visible)
        d_packed_ref[:, at_v] = dot_rows(probs.astype(BF16), d_context).astype(BF16)
        d_probs = dot_cols(d_context, values)
        inner = jnp.sum(probs * d_probs, axis=1, keepdims=True)
        d_scores = (probs * (d_probs - inner)).astype(BF16)
        grad = dot(d_scores, keys) * scale
        d_packed_ref[:, at] = (grad * cosine - swap_halves(grad) * sine).astype(BF16)
        grad = dot_rows(d_scores, queries)
        d_packed_ref[:, at_k] = (grad * cosine - swap_halves(grad) * sine).astype(BF16)


def by_sequence(width):
    return pl.BlockSpec((SEQ_LEN, width), lambda s: (s, 0))


TABLE = pl.BlockSpec((1, SEQ_LEN, HEAD), lambda s: (s, 0, 0))
SCALARS = pl.BlockSpec(memory_space=pltpu.SMEM)
PARAMS = pltpu.CompilerParams(vmem_limit_bytes=48 * 2**20)


def attend(prefix, packed, cosine, sine):
    rows, width = packed.shape[0], packed.shape[1] // 3
    return pl.pallas_call(
        attend_kernel,
        grid=(rows // SEQ_LEN,),
        in_specs=[SCALARS, by_sequence(3 * width), TABLE, TABLE],
        out_specs=[by_sequence(3 * width), by_sequence(width)],
        out_shape=[
            jax.ShapeDtypeStruct((rows, 3 * width), BF16),
            jax.ShapeDtypeStruct((rows, width), BF16),
        ],
        compiler_params=PARAMS,
    )(prefix, packed, cosine, sine)


def attend_back(prefix, qkv, d_context, cosine, sine):
    rows, width = d_context.shape
    return pl.pallas_call(
        attend_back_kernel,
        grid=(rows // SEQ_LEN,),
        in_specs=[SCALARS, by_sequence(3 * width), by_sequence(width), TABLE, TABLE],
        out_specs=by_sequence(3 * width),
        out_shape=jax.ShapeDtypeStruct((rows, 3 * width), BF16),
        compiler_params=PARAMS,
    )(prefix, qkv, d_context, cosine, sine)


def tables(prefix, start):
    place = jnp.arange(SEQ_LEN, dtype=jnp.int32)
    in_span = place[None, :] >= prefix[:, None]
    pos_one = jnp.where(in_span, start[:, None], place[None, :])
    pos_two = jnp.where(in_span, place[None, :] - prefix[:, None] + 1, 0)
    lane = jnp.arange(HEAD)
    freqs = 10000.0 ** (-2.0 * (lane % 32).astype(F32) / 64)
    place_of = jnp.where(lane[None, None, :] < 64, pos_one[:, :, None], pos_two[:, :, None])
    angles = place_of.astype(F32) * freqs
    sign = jnp.where(lane % 64 < 32, -1.0, 1.0)
    return jnp.cos(angles), jnp.sin(angles) * sign


def norm_parts(values):
    center = values - jnp.mean(values, axis=-1, keepdims=True)
    inverse = lax.rsqrt(jnp.mean(center * center, axis=-1, keepdims=True) + norm_eps)
    return center * inverse, inverse


def norm_back(normal, inverse, gain, grad):
    scaled = gain * grad
    return inverse * (
        scaled
        - jnp.mean(scaled, axis=-1, keepdims=True)
        - normal * jnp.mean(scaled * normal, axis=-1, keepdims=True)
    )


def gate_parts(gate):
    phi = 0.5 * (1.0 + lax.erf(gate * 0.7071067811865476))
    slope = phi + gate * jnp.exp(-0.5 * gate * gate) * 0.3989422804014327
    return gate * phi, slope


def here():
    return lax.axis_index("gy"), lax.axis_index("gx"), lax.axis_index("core")


def place(y, x, c):
    return (y * 2 + x) * 2 + c


def greet(peers):
    barrier = pltpu.get_barrier_semaphore()
    for peer in peers:
        pl.semaphore_signal(barrier, inc=1, device_id=peer, device_id_type=MESH)
    pl.semaphore_wait(barrier, len(peers))


def spread_block(cut, base, block_ref, out_ref, send, recv, local):
    rows = block_ref.shape[0]
    y, x, c = here()
    to_x, to_y, to_c = {"gx": 1 - x}, {"gy": 1 - y}, {"core": 1 - c}
    me, by_x, by_y, far = place(y, x, c), place(y, 1 - x, c), place(1 - y, x, c), place(1 - y, 1 - x, c)
    low, high = pl.ds(0, cut), pl.ds(cut, rows - cut)

    def push(k, src, dst, to):
        copy = pltpu.make_async_remote_copy(
            src_ref=src, dst_ref=dst, send_sem=send.at[base + k], recv_sem=recv.at[base + k], device_id=to, device_id_type=MESH
        )
        copy.start()
        return copy

    def landed(k, dst):
        pltpu.make_async_remote_copy(
            src_ref=dst, dst_ref=dst, send_sem=send.at[base + k], recv_sem=recv.at[base + k], device_id=to_c, device_id_type=MESH
        ).wait_recv()

    sent = [
        push(0, block_ref.at[low], out_ref.at[me, low], to_x),
        push(1, block_ref.at[high], out_ref.at[me, high], to_y),
        push(2, block_ref.at[high], out_ref.at[me, high], to_x),
        push(3, block_ref.at[low], out_ref.at[me, low], to_y),
        push(4, block_ref, out_ref.at[me], to_c),
    ]
    keep = pltpu.make_async_copy(block_ref, out_ref.at[me], local)
    keep.start()
    landed(0, out_ref.at[by_x, low])
    sent.append(push(5, out_ref.at[by_x, low], out_ref.at[by_x, low], to_y))
    sent.append(push(7, out_ref.at[by_x, low], out_ref.at[by_x, low], to_c))
    landed(1, out_ref.at[by_y, high])
    sent.append(push(6, out_ref.at[by_y, high], out_ref.at[by_y, high], to_x))
    sent.append(push(8, out_ref.at[by_y, high], out_ref.at[by_y, high], to_c))
    landed(2, out_ref.at[by_x, high])
    sent.append(push(9, out_ref.at[by_x, high], out_ref.at[by_x, high], to_c))
    landed(3, out_ref.at[by_y, low])
    sent.append(push(10, out_ref.at[by_y, low], out_ref.at[by_y, low], to_c))
    landed(5, out_ref.at[far, low])
    sent.append(push(11, out_ref.at[far, low], out_ref.at[far, low], to_c))
    landed(6, out_ref.at[far, high])
    sent.append(push(12, out_ref.at[far, high], out_ref.at[far, high], to_c))
    other, other_x, other_y, other_far = (
        place(y, x, 1 - c),
        place(y, 1 - x, 1 - c),
        place(1 - y, x, 1 - c),
        place(1 - y, 1 - x, 1 - c),
    )
    landed(4, out_ref.at[other])
    landed(7, out_ref.at[other_x, low])
    landed(8, out_ref.at[other_y, high])
    landed(9, out_ref.at[other_x, high])
    landed(10, out_ref.at[other_y, low])
    landed(11, out_ref.at[other_far, low])
    landed(12, out_ref.at[other_far, high])
    keep.wait()
    for copy in sent:
        copy.wait_send()


def gather_kernel(cut, block_ref, out_ref, send, recv, local):
    y, x, c = here()
    greet([{"gx": 1 - x}, {"gy": 1 - y}, {"core": 1 - c}])
    spread_block(cut, 0, block_ref, out_ref, send, recv, local)


ANY = pl.BlockSpec(memory_space=pl.ANY)


def group_gather(block):
    rows, width = block.shape
    return pl.pallas_call(
        functools.partial(gather_kernel, rows // 2),
        out_shape=jax.ShapeDtypeStruct((8, rows, width), block.dtype),
        in_specs=[ANY],
        out_specs=ANY,
        scratch_shapes=[pltpu.SemaphoreType.DMA((13,)), pltpu.SemaphoreType.DMA((13,)), pltpu.SemaphoreType.DMA],
        compiler_params=pltpu.CompilerParams(collective_id=9, has_side_effects=True),
        cost_estimate=pl.CostEstimate(flops=0, bytes_accessed=100 * 2**20, transcendentals=0),
    )(block)


SLAB = 16
ROWS = pl.BlockSpec(memory_space=pltpu.VMEM)
CHIP_COLS = 256


def first_norm(total, x, gains):
    normal, inverse = norm_parts(deep_alpha * x + total)
    first = normal * gains[0:1] + gains[1:2]
    return first, normal, inverse


def second_norm(total, first, grad, gains):
    normal, inverse = norm_parts(deep_alpha * first + total)
    return normal * gains[2:3] + gains[3:4], norm_back(normal, inverse, gains[2:3], grad), grad * normal


def first_back(total, d_pre_two, normal, inverse, gains):
    d_first = deep_alpha * d_pre_two + total
    return norm_back(normal, inverse, gains[0:1], d_first), d_first * normal, d_first


def fold_kernel(mode, across, n_aux, n_out, *refs):
    left_ref, right_ref, gains_ref = refs[:3]
    aux_refs = refs[3 : 3 + n_aux]
    refs = refs[3 + n_aux :]
    spread = mode != "last"
    if spread:
        all_ref, refs = refs[0], refs[1:]
    outs, refs = refs[:n_out], refs[n_out:]
    aux, refs = refs[:n_aux], refs[n_aux:]
    left, right, part, got, near_x, near_y, from_x, from_y, block, acc, send, recv, local = refs
    rows, width = block.shape
    cut = near_x.shape[0]
    y, x, c = here()
    to_x, to_y, to_c = {"gx": 1 - x}, {"gy": 1 - y}, {"core": 1 - c}
    chips = [(1 - y, 1 - x), (y, 1 - x), (1 - y, x), (y, x)]
    low, high = pl.ds(0, cut), pl.ds(cut, rows - cut)

    def push(k, src, dst, to):
        copy = pltpu.make_async_remote_copy(
            src_ref=src, dst_ref=dst, send_sem=send.at[k], recv_sem=recv.at[k], device_id=to, device_id_type=MESH
        )
        copy.start()
        return copy

    def add(k, extra, start, size, offset=0):
        @pl.loop(0, size // SLAB)
        def _(step):
            at = pl.ds(pl.multiple_of(start + step * SLAB, SLAB), SLAB)
            of = pl.ds(pl.multiple_of(start - offset + step * SLAB, SLAB), SLAB)
            part[k, c, at] = (part[k, c, at].astype(F32) + extra[of].astype(F32)).astype(BF16)

    loads = [pltpu.make_async_copy(left_ref.at[a * 2 + b], left.at[k], local.at[k]) for k, (a, b) in enumerate(chips)]
    load_right = pltpu.make_async_copy(right_ref, right, local.at[4])
    load_aux = [pltpu.make_async_copy(r, v, local.at[5 + k]) for k, (r, v) in enumerate(zip(aux_refs, aux))]
    loads[0].start()
    load_right.start()
    for load in loads[1:] + load_aux:
        load.start()
    greet([to_x, to_y, to_c])

    def product(k):
        loads[k].wait()

        @pl.loop(0, width // CHIP_COLS)
        def _(step):
            at = pl.ds(pl.multiple_of(step * CHIP_COLS, CHIP_COLS), CHIP_COLS)
            here_part = dot_cols(left[k], right[at]) if across else dot(left[k], right[:, at])
            part[k, 0, :, at] = here_part[:rows].astype(BF16)
            part[k, 1, :, at] = here_part[rows:].astype(BF16)

        return push(k, part.at[k, 1 - c], got.at[k], to_c)

    load_right.wait()
    sent = [product(0), product(1)]
    sent[0].wait_recv()
    add(0, got.at[0], 0, rows)
    far_x = push(4, part.at[0, c, low], near_x, to_x)
    far_y = push(5, part.at[0, c, high], near_y, to_y)
    sent.append(product(2))
    sent[1].wait_recv()
    add(1, got.at[1], 0, rows)
    plain_x = push(6, part.at[1, c, low], from_x.at[low], to_x)
    sent[2].wait_recv()
    add(2, got.at[2], 0, rows)
    plain_y = push(7, part.at[2, c, high], from_y.at[high], to_y)
    sent.append(product(3))
    far_y.wait_recv()
    add(1, near_y, cut, rows - cut, cut)
    more_x = push(8, part.at[1, c, high], from_x.at[high], to_x)
    far_x.wait_recv()
    add(2, near_x, 0, cut)
    more_y = push(9, part.at[2, c, low], from_y.at[low], to_y)
    sent[3].wait_recv()
    for load in load_aux:
        load.wait()
    plain_x.wait_recv()
    plain_y.wait_recv()
    more_x.wait_recv()
    more_y.wait_recv()
    gains = gains_ref[...]
    acc[...] = jnp.zeros_like(acc)

    @pl.loop(0, rows // SLAB)
    def _(step):
        at = pl.ds(pl.multiple_of(step * SLAB, SLAB), SLAB)
        total = part[3, c, at].astype(F32) + got[3, at].astype(F32) + from_x[at].astype(F32) + from_y[at].astype(F32)
        held = [a[at].astype(F32) for a in aux]
        if mode == "one":
            first, normal, inverse = first_norm(total, held[0], gains)
            outs[0][at] = first
            outs[1][at] = normal
            outs[2][at] = jnp.broadcast_to(inverse, (SLAB, 128))
            block[at] = first.astype(BF16)
        elif mode == "two":
            result, d_pre, terms = second_norm(total, held[0], held[1], gains)
            outs[0][at] = result.astype(BF16)
            outs[1][at] = d_pre
            block[at] = d_pre.astype(BF16)
            acc[0] += terms
            acc[1] += held[1]
        elif mode == "back":
            d_pre, terms, d_first = first_back(total, held[0], held[1], held[2][:, 0:1], gains)
            outs[0][at] = d_pre
            block[at] = d_pre.astype(BF16)
            acc[0] += terms
            acc[1] += d_first
        else:
            outs[0][at] = (deep_alpha * held[0] + total).astype(BF16)

    if mode in ("two", "back"):
        outs[-1][0:1] = jnp.sum(acc[0], axis=0, keepdims=True)
        outs[-1][1:2] = jnp.sum(acc[1], axis=0, keepdims=True)
    for copy in sent + [far_x, far_y, plain_x, plain_y, more_x, more_y]:
        copy.wait_send()
    if spread:
        spread_block(cut, 10, block, all_ref, send, recv, local.at[4])


def group_fold(name, mode, left, right, gains, aux, out_types):
    across = mode != "one"
    rows, depth = left.shape[0] // 8, left.shape[1]
    width = gains.shape[1]
    cut = rows // 2
    spread = mode != "last"
    out_shape = [jax.ShapeDtypeStruct((8, rows, width), BF16)] * spread + out_types
    n = len(aux)
    n_sems = 23 if spread else 10
    return pl.pallas_call(
        functools.partial(fold_kernel, mode, across, n, len(out_types)),
        out_shape=out_shape,
        in_specs=[ANY, ANY, ROWS] + [ANY] * n,
        out_specs=[ANY] * spread + [ROWS] * len(out_types),
        scratch_shapes=[pltpu.VMEM(a.shape, a.dtype) for a in aux]
        + [
            pltpu.VMEM((4, 2 * rows, depth), BF16),
            pltpu.VMEM(right.shape, BF16),
            pltpu.VMEM((4, 2, rows, width), BF16),
            pltpu.VMEM((4, rows, width), BF16),
            pltpu.VMEM((cut, width), BF16),
            pltpu.VMEM((rows - cut, width), BF16),
            pltpu.VMEM((rows, width), BF16),
            pltpu.VMEM((rows, width), BF16),
            pltpu.VMEM((rows, width), BF16),
            pltpu.VMEM((2, SLAB, width), F32),
            pltpu.SemaphoreType.DMA((n_sems,)),
            pltpu.SemaphoreType.DMA((n_sems,)),
            pltpu.SemaphoreType.DMA((5 + n,)),
        ],
        compiler_params=pltpu.CompilerParams(
            collective_id=name, has_side_effects=True, vmem_limit_bytes=50 * 2**20
        ),
        cost_estimate=pl.CostEstimate(flops=0, bytes_accessed=(200 if spread else 110) * 2**20, transcendentals=0),
    )(left.reshape(4, 2 * rows, depth), right, gains, *aux)


def group_peers(y, x, c):
    peers = [((y + k // 4) % 2, (x + k // 2 % 2) % 2, (c + k % 2) % 2) for k in range(1, 8)]
    return peers, [{"gy": p[0], "gx": p[1], "core": p[2]} for p in peers]


def swap_kernel(zs, kinds, *refs):
    n = len(kinds)
    blocks, outs = refs[:n], refs[n : 2 * n]
    send, recv, local = refs[2 * n :]
    y, x, c = here()
    z = lax.axis_index("z")
    peers, names = group_peers(y, x, c)
    in_group = [(place(*peer), name) for peer, name in zip(peers, names)]
    in_line = [((z + k) % zs, {"z": (z + k) % zs}) for k in range(1, zs)]
    greet(names + [name for _, name in in_line] * ("line" in kinds))
    copies, comes, keeps = [], [], []
    for i, kind in enumerate(kinds):
        me = z if kind == "line" else place(y, x, c)
        for k, (peer, name) in enumerate(in_line if kind == "line" else in_group):
            src = blocks[i].at[peer] if kind == "swap" else blocks[i]
            landing = outs[i].at[peer]
            sems = dict(send_sem=send.at[i, k], recv_sem=recv.at[i, k], device_id=name, device_id_type=MESH)
            copies.append(pltpu.make_async_remote_copy(src_ref=src, dst_ref=outs[i].at[me], **sems))
            comes.append(pltpu.make_async_remote_copy(src_ref=landing, dst_ref=landing, **sems))
            copies[-1].start()
        own = blocks[i].at[me] if kind == "swap" else blocks[i]
        keeps.append(pltpu.make_async_copy(own, outs[i].at[me], local.at[i]))
        keeps[-1].start()
    for come in comes:
        come.wait_recv()
    for copy in copies:
        copy.wait_send()
    for keep in keeps:
        keep.wait()


def group_swap(name, zs, arrays, kinds):
    n = len(arrays)
    most = max(7, zs - 1)
    lead = {"swap": (), "group": (8,), "line": (zs,)}
    return pl.pallas_call(
        functools.partial(swap_kernel, zs, kinds),
        out_shape=[jax.ShapeDtypeStruct(lead[k] + a.shape, a.dtype) for a, k in zip(arrays, kinds)],
        in_specs=[ANY] * n,
        out_specs=[ANY] * n,
        scratch_shapes=[
            pltpu.SemaphoreType.DMA((n, most)),
            pltpu.SemaphoreType.DMA((n, most)),
            pltpu.SemaphoreType.DMA((n,)),
        ],
        compiler_params=pltpu.CompilerParams(collective_id=name, has_side_effects=True),
        cost_estimate=pl.CostEstimate(flops=0, bytes_accessed=50 * 2**20, transcendentals=0),
    )(*arrays)


def opening_kernel(zs, qkv_ref, dense_ref, info_ref, qkv_all, dense_all, info_all, *refs):
    swap_send, swap_recv, line_send, line_recv, local = refs
    y, x, c = here()
    z = lax.axis_index("z")
    me = place(y, x, c)
    peers, names = group_peers(y, x, c)
    lines = [dense_all, info_all]
    barrier = pltpu.get_barrier_semaphore()
    for name in names:
        pl.semaphore_signal(barrier, inc=1, device_id=name, device_id_type=MESH)

    @pl.when(z > 0)
    def _():
        pl.semaphore_signal(barrier, inc=1, device_id={"z": z - 1}, device_id_type=MESH)

    @pl.when(z < zs - 1)
    def _():
        pl.semaphore_signal(barrier, inc=1, device_id={"z": z + 1}, device_id_type=MESH)

    inside = (z > 0) & (z < zs - 1)

    @pl.when(inside)
    def _():
        pl.semaphore_wait(barrier, 9)

    @pl.when(jnp.logical_not(inside))
    def _():
        pl.semaphore_wait(barrier, 8)

    def hop(a, step, up, to):
        shard = z - step if up else z + step
        k = 2 * step + (0 if up else 1)
        ref = lines[a].at[shard]
        return pltpu.make_async_remote_copy(
            src_ref=ref,
            dst_ref=ref,
            send_sem=line_send.at[a, k],
            recv_sem=line_recv.at[a, k],
            device_id=to,
            device_id_type=MESH,
        )

    def sends(step, up):
        return (z >= step) & (z < zs - 1) if up else (z <= zs - 1 - step) & (z > 0)

    def gets(step, up):
        return z >= step + 1 if up else z <= zs - 2 - step

    def arrive(a, step, up):
        @pl.when(gets(step, up))
        def _():
            shard = z - 1 - step if up else z + 1 + step
            k = 2 * step + (0 if up else 1)
            ref = lines[a].at[shard]
            pltpu.make_async_remote_copy(
                src_ref=ref,
                dst_ref=ref,
                send_sem=line_send.at[a, k],
                recv_sem=line_recv.at[a, k],
                device_id={"core": 1 - c},
                device_id_type=MESH,
            ).wait_recv()

    def line_step(a, step):
        for up in (True, False):
            if step > 0:
                arrive(a, step - 1, up)

            @pl.when(sends(step, up))
            def _(up=up):
                hop(a, step, up, {"z": z + 1 if up else z - 1}).start()

    def line_end(a):
        for up in (True, False):
            arrive(a, zs - 2, up)
            for step in range(zs - 1):

                @pl.when(sends(step, up))
                def _(step=step, up=up):
                    hop(a, step, up, {"z": z + 1 if up else z - 1}).wait_send()

    def swap_copies(i, src, dst, spread):
        out, back = [], []
        for k, (peer, name) in enumerate(zip(peers, names)):
            sems = dict(
                send_sem=swap_send.at[i, k], recv_sem=swap_recv.at[i, k], device_id=name, device_id_type=MESH
            )
            out.append(
                pltpu.make_async_remote_copy(
                    src_ref=src if spread else src.at[place(*peer)], dst_ref=dst.at[me], **sems
                )
            )
            landing = dst.at[place(*peer)]
            back.append(pltpu.make_async_remote_copy(src_ref=landing, dst_ref=landing, **sems))
        keep = pltpu.make_async_copy(src if spread else src.at[me], dst.at[me], local.at[i])
        keep.start()
        for copy in out:
            copy.start()
        return out, back, keep

    def landed(copies):
        for copy in copies[1]:
            copy.wait_recv()
        copies[2].wait()

    keep_dense = pltpu.make_async_copy(dense_ref, dense_all.at[z], local.at[2])
    keep_dense.start()
    small = swap_copies(1, info_ref, info_all.at[z], True)
    blocks = swap_copies(0, qkv_ref, qkv_all, False)
    keep_dense.wait()
    line_step(0, 0)
    landed(small)
    line_step(1, 0)
    for step in range(1, zs - 1):
        line_step(0, step)
        line_step(1, step)
    landed(blocks)
    line_end(0)
    line_end(1)
    for copy in blocks[0] + small[0]:
        copy.wait_send()


def opening(zs, qkv_blocks, dense, info):
    return pl.pallas_call(
        functools.partial(opening_kernel, zs),
        out_shape=[
            jax.ShapeDtypeStruct(qkv_blocks.shape, BF16),
            jax.ShapeDtypeStruct((zs,) + dense.shape, BF16),
            jax.ShapeDtypeStruct((zs, 8) + info.shape, BF16),
        ],
        in_specs=[ANY] * 3,
        out_specs=[ANY] * 3,
        scratch_shapes=[
            pltpu.SemaphoreType.DMA((2, 7)),
            pltpu.SemaphoreType.DMA((2, 7)),
            pltpu.SemaphoreType.DMA((2, 2 * (zs - 1))),
            pltpu.SemaphoreType.DMA((2, 2 * (zs - 1))),
            pltpu.SemaphoreType.DMA((3,)),
        ],
        compiler_params=pltpu.CompilerParams(collective_id=2, has_side_effects=True),
        cost_estimate=pl.CostEstimate(flops=0, bytes_accessed=50 * 2**20, transcendentals=0),
    )(qkv_blocks, dense, info)


def on_device(sizes, x_in, d_out, w_qkv, w_dense, w_in, w_out, gone, bone, gtwo, btwo, flags, span_start, span_len):
    gy, gx, cores, zs = sizes
    piece = w_qkv.shape[0]
    ff = w_out.shape[1]
    group = gy * gx * cores
    width = D // group
    tile = -(-ff // (group * 128)) * 128
    own = gy == 2

    def permute(array):
        lead = array.shape[:-1]
        return jnp.swapaxes(array.reshape(lead + (group, zs, piece)), -3, -2).reshape(lead + (D,))

    def restore(array):
        lead = array.shape[:-1]
        return jnp.swapaxes(array.reshape(lead + (zs, group, piece)), -3, -2).reshape(lead + (D,))

    def swap(name, arrays, kinds):
        if own:
            return group_swap(name, zs, arrays, kinds)
        ways = {
            "swap": lambda a: lax.all_to_all(a, GROUP, 0, 0, tiled=True),
            "group": lambda a: lax.all_gather(a, GROUP, axis=0),
            "line": lambda a: lax.all_gather(a, "z", axis=0),
        }
        return [ways[k](a) for a, k in zip(arrays, kinds)]

    def spread_rows(block):
        whole = group_gather(block) if own else lax.all_gather(block, GROUP, axis=0)
        return whole.reshape(group * block.shape[0], block.shape[1])

    rows_f32 = jax.ShapeDtypeStruct((SEQ_LEN, D), F32)
    rows_low = jax.ShapeDtypeStruct((SEQ_LEN, D), BF16)
    sums_type = jax.ShapeDtypeStruct((8, D), F32)

    def fold(partial):
        return lax.psum_scatter(partial.astype(BF16), GROUP, scatter_dimension=0, tiled=True).astype(F32)

    def stack_sums(*arrays):
        return jnp.pad(jnp.stack([jnp.sum(a, axis=0) for a in arrays]), ((0, 6), (0, 0)))

    def fold_one(left, right, x, gains):
        if own:
            kinds = [rows_f32, rows_f32, jax.ShapeDtypeStruct((SEQ_LEN, 128), F32)]
            whole, first, normal, inverse = group_fold(0, "one", left, right, gains, [x], kinds)
            return whole.reshape(left.shape[0], D), first, normal, inverse
        first, normal, inverse = first_norm(fold(dot(left, right)), x.astype(F32), gains)
        return spread_rows(first.astype(BF16)), first, normal, inverse

    def fold_two(left, right, first, grad, gains):
        if own:
            kinds = [rows_low, rows_f32, sums_type]
            whole, result, d_pre, sums = group_fold(1, "two", left, right, gains, [first, grad], kinds)
            return whole.reshape(left.shape[0], D), result, d_pre, sums
        grad = grad.astype(F32)
        result, d_pre, terms = second_norm(fold(dot_cols(left, right)), first, grad, gains)
        return spread_rows(d_pre.astype(BF16)), result.astype(BF16), d_pre, stack_sums(terms, grad)

    def fold_back(left, right, d_pre_two, normal, inverse, gains):
        if own:
            kinds = [rows_f32, sums_type]
            whole, d_pre, sums = group_fold(7, "back", left, right, gains, [d_pre_two, normal, inverse], kinds)
            return whole.reshape(left.shape[0], D), d_pre, sums
        d_pre, terms, d_first = first_back(fold(dot_cols(left, right)), d_pre_two, normal, inverse, gains)
        return spread_rows(d_pre.astype(BF16)), d_pre, stack_sums(terms, d_first)

    def fold_last(left, right, d_pre, gains):
        if own:
            (out,) = group_fold(8, "last", left, right, gains, [d_pre], [rows_low])
            return out
        return (deep_alpha * d_pre + fold(dot_cols(left, right))).astype(BF16)

    def gather(block):
        return lax.all_gather(block, "z", axis=0, tiled=True)

    def scatter(partial):
        return lax.psum_scatter(partial.astype(BF16), "z", scatter_dimension=0, tiled=True)

    def pad_ff(array):
        return jnp.pad(array, ((0, 0), (0, group * tile - ff))).reshape(piece, group, tile)

    masked = jnp.max(flags) > 0
    prefix = jnp.where(masked, SEQ_LEN, SEQ_LEN - span_len[0])
    info = jnp.concatenate([gone, bone, gtwo, btwo, jnp.stack([prefix, span_start[0]]).astype(BF16)])
    info = jnp.pad(info[None, :], ((0, 15), (0, -info.shape[0] % 128)))

    qkv_blocks = jnp.moveaxis(w_qkv.reshape(piece, 3, group, width), 2, 0).reshape(group, piece, 3 * width)
    if own:
        qkv_blocks, w_dense_part, info = opening(zs, qkv_blocks, permute(w_dense), info)
        w_dense_part = w_dense_part.reshape(zs * piece, D)
    else:
        (qkv_blocks,) = swap(2, [qkv_blocks], ("swap",))
        w_dense_part = gather(permute(w_dense))
        info = lax.all_gather(lax.all_gather(info, GROUP, axis=0), "z", axis=0)
    w_qkv_part = gather(qkv_blocks.reshape(group * piece, 3 * width))
    in_blocks = jnp.stack([pad_ff(w_in[:, :ff]), pad_ff(w_in[:, ff:])], axis=2)
    in_blocks = jnp.moveaxis(in_blocks, 1, 0).reshape(group, piece, 2 * tile)
    out_blocks = jnp.moveaxis(pad_ff(w_out), 1, 0)
    in_blocks, out_blocks, qkv_blocks = lax.optimization_barrier((in_blocks, out_blocks, qkv_blocks))
    in_blocks, out_blocks = swap(3, [in_blocks, out_blocks], ("swap", "swap"))
    w_in_part = gather(in_blocks.reshape(group * piece, 2 * tile))
    x_perm = permute(x_in)
    x_next, in_blocks = lax.optimization_barrier((x_perm, in_blocks))
    x_all = spread_rows(x_next)

    info = info[:, :, 0]
    place_info = info[lax.axis_index("z"), :, 4 * piece : 4 * piece + 2].astype(jnp.int32)
    prefix, start = place_info[:, 0], place_info[:, 1]
    gains = info[:, :, : 4 * piece].astype(F32).reshape(zs, group, 4, piece)
    gains = jnp.pad(jnp.transpose(gains, (2, 0, 1, 3)).reshape(4, D), ((0, 4), (0, 0)))
    cosine, sine = tables(prefix, start)
    w_qkv_part, x_all, cosine, sine, gains = lax.optimization_barrier((w_qkv_part, x_all, cosine, sine, gains))
    packed = dot(x_all, w_qkv_part)
    qkv, context = attend(prefix, packed, cosine, sine)
    first_all, first, normal_one, inverse_one = fold_one(context, w_dense_part, x_perm, gains)
    out_blocks, first_all, w_in_part = lax.optimization_barrier((out_blocks, first_all, w_in_part))
    w_out_part = gather(out_blocks.reshape(group * piece, tile))
    projected = dot(first_all, w_in_part)
    gate, up = projected[:, :tile], projected[:, tile:]
    act, slope = gate_parts(gate)
    hidden = (act * up).astype(BF16)
    d_branch, layer_out, d_pre_two, sums_two = fold_two(hidden, w_out_part, first, permute(d_out), gains)
    layer_out = restore(layer_out)
    d_w_out = dot_rows(d_branch, hidden).astype(BF16)
    d_w_out, d_branch = lax.optimization_barrier((d_w_out, d_branch))
    d_w_out = scatter(d_w_out)
    d_hidden = dot(d_branch, w_out_part)
    d_projected = jnp.concatenate([d_hidden * up * slope, d_hidden * act], axis=1).astype(BF16)
    d_w_in = dot_rows(first_all, d_projected).astype(BF16)
    d_w_in, d_projected = lax.optimization_barrier((d_w_in, d_projected))
    d_w_in = scatter(d_w_in)
    d_attn, d_pre_one, sums_one = fold_back(d_projected, w_in_part, d_pre_two, normal_one, inverse_one, gains)
    d_attn, d_w_out = lax.optimization_barrier((d_attn, d_w_out))
    d_context = dot_cols(d_attn, w_dense_part).astype(BF16)
    d_packed = attend_back(prefix, qkv, d_context, cosine, sine)
    d_w_qkv = dot_rows(x_all, d_packed).astype(BF16)
    sums = jnp.concatenate([sums_one[:2], sums_two[:2], jnp.zeros((4, D), F32)])
    d_w_out, sums = swap(4, [d_w_out.reshape(group, piece, tile), sums], ("swap", "group"))
    sums = jnp.sum(sums, axis=0).reshape(8, zs, group, piece)
    sums = lax.dynamic_index_in_dim(sums, lax.axis_index(GROUP), 2, keepdims=False).reshape(8, width)
    d_dense = dot_rows(context, d_attn).astype(BF16).reshape(zs, piece, group, width)
    d_dense = jnp.swapaxes(d_dense, 1, 2).reshape(D, width)
    d_w_qkv = jnp.concatenate([d_w_qkv, d_dense], axis=1)
    d_packed, d_w_qkv, d_w_in, sums = lax.optimization_barrier((d_packed, d_w_qkv, d_w_in, sums))
    d_w_qkv = scatter(d_w_qkv)
    d_w_in, sums = swap(6, [d_w_in.reshape(group, piece, 2 * tile), sums], ("swap", "line"))
    d_input = restore(fold_last(d_packed, w_qkv_part, d_pre_one, gains))
    sums = jnp.sum(sums, axis=0).reshape(8, zs, piece)
    sums = lax.dynamic_index_in_dim(sums, lax.axis_index("z"), 1, keepdims=False)
    out_in = jnp.transpose(d_w_in.astype(F32).reshape(group, piece, 2, tile), (1, 2, 0, 3))
    out_in = out_in.reshape(piece, 2, group * tile)
    out_in = jnp.concatenate([out_in[:, 0, :ff], out_in[:, 1, :ff]], axis=1)
    out_out = jnp.moveaxis(d_w_out.astype(F32), 0, 1).reshape(piece, group * tile)[:, :ff]
    out_in, out_out, d_input, d_w_qkv = lax.optimization_barrier((out_in, out_out, d_input, d_w_qkv))
    out_dense = d_w_qkv[:, 3 * width :].reshape(group, piece, width)
    out_dense = restore(jnp.swapaxes(out_dense, 0, 1).reshape(piece, D)).astype(F32)
    (d_w_qkv,) = swap(5, [d_w_qkv[:, : 3 * width].reshape(group, piece, 3 * width)], ("swap",))
    out_qkv = jnp.transpose(d_w_qkv.astype(F32).reshape(group, piece, 3, width), (1, 2, 0, 3)).reshape(piece, 3 * D)
    return layer_out, d_input, out_qkv, out_dense, out_in, out_out, sums[0], sums[1], sums[2], sums[3]


def solution(mesh):
    grp, shard = mesh.shape["grp"], mesh.shape["shard"]
    sizes = (grp // 4, 2, 2, shard)
    inner = Mesh(mesh.devices.reshape(sizes), ALL)
    rows, flat = P(ALL, None), P(ALL)
    return jax.shard_map(
        functools.partial(on_device, sizes),
        mesh=inner,
        in_specs=(rows,) * 6 + (flat,) * 7,
        out_specs=(rows,) * 6 + (flat,) * 4,
        check_vma=False,
    )
```

```python
import functools

import jax
import jax.numpy as jnp
from jax import lax
from jax.experimental import pallas as pl
from jax.experimental.pallas import tpu as pltpu
from jax.sharding import Mesh
from jax.sharding import PartitionSpec as P

HEADS = 16
HEAD = 128
SEQ_LEN = 224
D = HEADS * HEAD
deep_alpha = 6.928203230275509
norm_eps = 1e-05
far_below = -1e30
scale = HEAD ** (-0.5)

ALL = ("gy", "gx", "core", "z")
GROUP = ("gy", "gx", "core")
MESH = pl.DeviceIdType.MESH
F32 = jnp.float32
BF16 = jnp.bfloat16


def dot(left, right):
    return jnp.dot(left, right, preferred_element_type=F32)


def dot_rows(left, right):
    return lax.dot_general(left, right, (((0,), (0,)), ((), ())), preferred_element_type=F32)


def dot_cols(left, right):
    return lax.dot_general(left, right, (((1,), (1,)), ((), ())), preferred_element_type=F32)


def swap_halves(block):
    lane = lax.broadcasted_iota(jnp.int32, block.shape, 1)
    return jnp.where((lane & 32) == 0, pltpu.roll(block, 96, 1), pltpu.roll(block, 32, 1))


def seen(prefix):
    row = lax.broadcasted_iota(jnp.int32, (SEQ_LEN, SEQ_LEN), 0)
    col = lax.broadcasted_iota(jnp.int32, (SEQ_LEN, SEQ_LEN), 1)
    return (col < prefix) | (col <= row)


def softmax(queries, keys, visible):
    scores = jnp.where(visible, dot_cols(queries, keys), far_below)
    weights = jnp.exp(scores - jnp.max(scores, axis=1, keepdims=True))
    return weights / jnp.sum(weights, axis=1, keepdims=True)


def attend_kernel(prefix_ref, packed_ref, cos_ref, sin_ref, qkv_ref, context_ref):
    width = context_ref.shape[1]
    visible = seen(prefix_ref[pl.program_id(0)])
    cosine = cos_ref[0]
    sine = sin_ref[0]
    for head in range(width // HEAD):
        at = pl.ds(head * HEAD, HEAD)
        at_k = pl.ds(width + head * HEAD, HEAD)
        at_v = pl.ds(2 * width + head * HEAD, HEAD)
        raw = packed_ref[:, at]
        queries = ((raw * cosine + swap_halves(raw) * sine) * scale).astype(BF16)
        raw = packed_ref[:, at_k]
        keys = (raw * cosine + swap_halves(raw) * sine).astype(BF16)
        values = packed_ref[:, at_v].astype(BF16)
        qkv_ref[:, at] = queries
        qkv_ref[:, at_k] = keys
        qkv_ref[:, at_v] = values
        probs = softmax(queries, keys, visible).astype(BF16)
        context_ref[:, at] = dot(probs, values).astype(BF16)


def attend_back_kernel(prefix_ref, qkv_ref, d_context_ref, cos_ref, sin_ref, d_packed_ref):
    width = d_context_ref.shape[1]
    visible = seen(prefix_ref[pl.program_id(0)])
    cosine = cos_ref[0]
    sine = sin_ref[0]
    for head in range(width // HEAD):
        at = pl.ds(head * HEAD, HEAD)
        at_k = pl.ds(width + head * HEAD, HEAD)
        at_v = pl.ds(2 * width + head * HEAD, HEAD)
        queries = qkv_ref[:, at]
        keys = qkv_ref[:, at_k]
        values = qkv_ref[:, at_v]
        d_context = d_context_ref[:, at]
        probs = softmax(queries, keys, visible)
        d_packed_ref[:, at_v] = dot_rows(probs.astype(BF16), d_context).astype(BF16)
        d_probs = dot_cols(d_context, values)
        inner = jnp.sum(probs * d_probs, axis=1, keepdims=True)
        d_scores = (probs * (d_probs - inner)).astype(BF16)
        grad = dot(d_scores, keys) * scale
        d_packed_ref[:, at] = (grad * cosine - swap_halves(grad) * sine).astype(BF16)
        grad = dot_rows(d_scores, queries)
        d_packed_ref[:, at_k] = (grad * cosine - swap_halves(grad) * sine).astype(BF16)


def by_sequence(width):
    return pl.BlockSpec((SEQ_LEN, width), lambda s: (s, 0))


TABLE = pl.BlockSpec((1, SEQ_LEN, HEAD), lambda s: (s, 0, 0))
SCALARS = pl.BlockSpec(memory_space=pltpu.SMEM)
PARAMS = pltpu.CompilerParams(vmem_limit_bytes=48 * 2**20)


def attend(prefix, packed, cosine, sine):
    rows, width = packed.shape[0], packed.shape[1] // 3
    return pl.pallas_call(
        attend_kernel,
        grid=(rows // SEQ_LEN,),
        in_specs=[SCALARS, by_sequence(3 * width), TABLE, TABLE],
        out_specs=[by_sequence(3 * width), by_sequence(width)],
        out_shape=[
            jax.ShapeDtypeStruct((rows, 3 * width), BF16),
            jax.ShapeDtypeStruct((rows, width), BF16),
        ],
        compiler_params=PARAMS,
    )(prefix, packed, cosine, sine)


def attend_back(prefix, qkv, d_context, cosine, sine):
    rows, width = d_context.shape
    return pl.pallas_call(
        attend_back_kernel,
        grid=(rows // SEQ_LEN,),
        in_specs=[SCALARS, by_sequence(3 * width), by_sequence(width), TABLE, TABLE],
        out_specs=by_sequence(3 * width),
        out_shape=jax.ShapeDtypeStruct((rows, 3 * width), BF16),
        compiler_params=PARAMS,
    )(prefix, qkv, d_context, cosine, sine)


def tables(prefix, start):
    place = jnp.arange(SEQ_LEN, dtype=jnp.int32)
    in_span = place[None, :] >= prefix[:, None]
    pos_one = jnp.where(in_span, start[:, None], place[None, :])
    pos_two = jnp.where(in_span, place[None, :] - prefix[:, None] + 1, 0)
    lane = jnp.arange(HEAD)
    freqs = 10000.0 ** (-2.0 * (lane % 32).astype(F32) / 64)
    place_of = jnp.where(lane[None, None, :] < 64, pos_one[:, :, None], pos_two[:, :, None])
    angles = place_of.astype(F32) * freqs
    sign = jnp.where(lane % 64 < 32, -1.0, 1.0)
    return jnp.cos(angles), jnp.sin(angles) * sign


def norm_parts(values):
    center = values - jnp.mean(values, axis=-1, keepdims=True)
    inverse = lax.rsqrt(jnp.mean(center * center, axis=-1, keepdims=True) + norm_eps)
    return center * inverse, inverse


def norm_back(normal, inverse, gain, grad):
    scaled = gain * grad
    return inverse * (
        scaled
        - jnp.mean(scaled, axis=-1, keepdims=True)
        - normal * jnp.mean(scaled * normal, axis=-1, keepdims=True)
    )


def gate_parts(gate):
    phi = 0.5 * (1.0 + lax.erf(gate * 0.7071067811865476))
    slope = phi + gate * jnp.exp(-0.5 * gate * gate) * 0.3989422804014327
    return gate * phi, slope


def here():
    return lax.axis_index("gy"), lax.axis_index("gx"), lax.axis_index("core")


def place(y, x, c):
    return (y * 2 + x) * 2 + c


def greet(peers):
    barrier = pltpu.get_barrier_semaphore()
    for peer in peers:
        pl.semaphore_signal(barrier, inc=1, device_id=peer, device_id_type=MESH)
    pl.semaphore_wait(barrier, len(peers))


def spread_block(cut, base, block_ref, out_ref, send, recv, local):
    rows = block_ref.shape[0]
    y, x, c = here()
    to_x, to_y, to_c = {"gx": 1 - x}, {"gy": 1 - y}, {"core": 1 - c}
    me, by_x, by_y, far = place(y, x, c), place(y, 1 - x, c), place(1 - y, x, c), place(1 - y, 1 - x, c)
    low, high = pl.ds(0, cut), pl.ds(cut, rows - cut)

    def push(k, src, dst, to):
        copy = pltpu.make_async_remote_copy(
            src_ref=src, dst_ref=dst, send_sem=send.at[base + k], recv_sem=recv.at[base + k], device_id=to, device_id_type=MESH
        )
        copy.start()
        return copy

    def landed(k, dst):
        pltpu.make_async_remote_copy(
            src_ref=dst, dst_ref=dst, send_sem=send.at[base + k], recv_sem=recv.at[base + k], device_id=to_c, device_id_type=MESH
        ).wait_recv()

    sent = [
        push(0, block_ref.at[low], out_ref.at[me, low], to_x),
        push(1, block_ref.at[high], out_ref.at[me, high], to_y),
        push(2, block_ref.at[high], out_ref.at[me, high], to_x),
        push(3, block_ref.at[low], out_ref.at[me, low], to_y),
        push(4, block_ref, out_ref.at[me], to_c),
    ]
    keep = pltpu.make_async_copy(block_ref, out_ref.at[me], local)
    keep.start()
    landed(0, out_ref.at[by_x, low])
    sent.append(push(5, out_ref.at[by_x, low], out_ref.at[by_x, low], to_y))
    sent.append(push(7, out_ref.at[by_x, low], out_ref.at[by_x, low], to_c))
    landed(1, out_ref.at[by_y, high])
    sent.append(push(6, out_ref.at[by_y, high], out_ref.at[by_y, high], to_x))
    sent.append(push(8, out_ref.at[by_y, high], out_ref.at[by_y, high], to_c))
    landed(2, out_ref.at[by_x, high])
    sent.append(push(9, out_ref.at[by_x, high], out_ref.at[by_x, high], to_c))
    landed(3, out_ref.at[by_y, low])
    sent.append(push(10, out_ref.at[by_y, low], out_ref.at[by_y, low], to_c))
    landed(5, out_ref.at[far, low])
    sent.append(push(11, out_ref.at[far, low], out_ref.at[far, low], to_c))
    landed(6, out_ref.at[far, high])
    sent.append(push(12, out_ref.at[far, high], out_ref.at[far, high], to_c))
    other, other_x, other_y, other_far = (
        place(y, x, 1 - c),
        place(y, 1 - x, 1 - c),
        place(1 - y, x, 1 - c),
        place(1 - y, 1 - x, 1 - c),
    )
    landed(4, out_ref.at[other])
    landed(7, out_ref.at[other_x, low])
    landed(8, out_ref.at[other_y, high])
    landed(9, out_ref.at[other_x, high])
    landed(10, out_ref.at[other_y, low])
    landed(11, out_ref.at[other_far, low])
    landed(12, out_ref.at[other_far, high])
    keep.wait()
    for copy in sent:
        copy.wait_send()


def gather_kernel(cut, block_ref, out_ref, send, recv, local):
    y, x, c = here()
    greet([{"gx": 1 - x}, {"gy": 1 - y}, {"core": 1 - c}])
    spread_block(cut, 0, block_ref, out_ref, send, recv, local)


ANY = pl.BlockSpec(memory_space=pl.ANY)


def group_gather(block):
    rows, width = block.shape
    return pl.pallas_call(
        functools.partial(gather_kernel, rows // 2),
        out_shape=jax.ShapeDtypeStruct((8, rows, width), block.dtype),
        in_specs=[ANY],
        out_specs=ANY,
        scratch_shapes=[pltpu.SemaphoreType.DMA((13,)), pltpu.SemaphoreType.DMA((13,)), pltpu.SemaphoreType.DMA],
        compiler_params=pltpu.CompilerParams(collective_id=9, has_side_effects=True),
        cost_estimate=pl.CostEstimate(flops=0, bytes_accessed=100 * 2**20, transcendentals=0),
    )(block)


def swap_peers(zs, kinds):
    y, x, c = here()
    z = lax.axis_index("z")
    found = []
    for k in range(1, 8):
        peer = ((y + k // 4) % 2, (x + k // 2 % 2) % 2, (c + k % 2) % 2)
        found.append((place(*peer), {"gy": peer[0], "gx": peer[1], "core": peer[2]}))
    if "line" in kinds:
        found += [((z + k) % zs, {"z": (z + k) % zs}) for k in range(1, zs)]
    return found


def swap_begin(zs, kinds, blocks, outs, send, recv, local):
    copies, comes, keeps = [], [], []
    found = swap_peers(zs, kinds)
    for i, kind in enumerate(kinds):
        me = lax.axis_index("z") if kind == "line" else place(*here())
        for k, (peer, name) in enumerate(found[7:] if kind == "line" else found[:7]):
            src = blocks[i].at[peer] if kind == "swap" else blocks[i]
            landing = outs[i].at[peer]
            sems = dict(send_sem=send.at[i, k], recv_sem=recv.at[i, k], device_id=name, device_id_type=MESH)
            copies.append(pltpu.make_async_remote_copy(src_ref=src, dst_ref=outs[i].at[me], **sems))
            comes.append(pltpu.make_async_remote_copy(src_ref=landing, dst_ref=landing, **sems))
            copies[-1].start()
        own = blocks[i].at[me] if kind == "swap" else blocks[i]
        keeps.append(pltpu.make_async_copy(own, outs[i].at[me], local.at[i]))
        keeps[-1].start()

    def finish():
        for come in comes:
            come.wait_recv()
        for copy in copies:
            copy.wait_send()
        for keep in keeps:
            keep.wait()

    return finish


SWAP_LEAD = {"swap": lambda zs: (), "group": lambda zs: (8,), "line": lambda zs: (zs,)}


def swap_shapes(zs, arrays, kinds):
    return [jax.ShapeDtypeStruct(SWAP_LEAD[k](zs) + a.shape, a.dtype) for a, k in zip(arrays, kinds)]


def swap_scratch(zs, kinds):
    n, most = len(kinds), max(7, zs - 1)
    return [
        pltpu.SemaphoreType.DMA((n, most)),
        pltpu.SemaphoreType.DMA((n, most)),
        pltpu.SemaphoreType.DMA((n,)),
    ]


SLAB = 16
ROWS = pl.BlockSpec(memory_space=pltpu.VMEM)
CHIP_COLS = 256


def first_norm(total, x, gains):
    normal, inverse = norm_parts(deep_alpha * x + total)
    first = normal * gains[0:1] + gains[1:2]
    return first, normal, inverse


def second_norm(total, first, grad, gains):
    normal, inverse = norm_parts(deep_alpha * first + total)
    return normal * gains[2:3] + gains[3:4], norm_back(normal, inverse, gains[2:3], grad), grad * normal


def first_back(total, d_pre_two, normal, inverse, gains):
    d_first = deep_alpha * d_pre_two + total
    return norm_back(normal, inverse, gains[0:1], d_first), d_first * normal, d_first


def fold_kernel(mode, across, n_aux, n_out, kinds, *refs):
    left_ref, right_ref, gains_ref = refs[:3]
    aux_refs = refs[3 : 3 + n_aux]
    refs = refs[3 + n_aux :]
    n_swap = len(kinds)
    swap_in, refs = refs[:n_swap], refs[n_swap:]
    spread = mode != "last"
    if spread:
        all_ref, refs = refs[0], refs[1:]
    outs, refs = refs[:n_out], refs[n_out:]
    swap_out, refs = refs[:n_swap], refs[n_swap:]
    aux, refs = refs[:n_aux], refs[n_aux:]
    left, right, part, got, near_x, near_y, from_x, from_y, block, acc, send, recv, local = refs[:13]
    rows, width = block.shape
    cut = near_x.shape[0]
    y, x, c = here()
    to_x, to_y, to_c = {"gx": 1 - x}, {"gy": 1 - y}, {"core": 1 - c}
    chips = [(1 - y, 1 - x), (y, 1 - x), (1 - y, x), (y, x)]
    low, high = pl.ds(0, cut), pl.ds(cut, rows - cut)

    def push(k, src, dst, to):
        copy = pltpu.make_async_remote_copy(
            src_ref=src, dst_ref=dst, send_sem=send.at[k], recv_sem=recv.at[k], device_id=to, device_id_type=MESH
        )
        copy.start()
        return copy

    def add(k, extra, start, size, offset=0):
        @pl.loop(0, size // SLAB)
        def _(step):
            at = pl.ds(pl.multiple_of(start + step * SLAB, SLAB), SLAB)
            of = pl.ds(pl.multiple_of(start - offset + step * SLAB, SLAB), SLAB)
            part[k, c, at] = (part[k, c, at].astype(F32) + extra[of].astype(F32)).astype(BF16)

    loads = [pltpu.make_async_copy(left_ref.at[a * 2 + b], left.at[k], local.at[k]) for k, (a, b) in enumerate(chips)]
    load_right = pltpu.make_async_copy(right_ref, right, local.at[4])
    load_aux = [pltpu.make_async_copy(r, v, local.at[5 + k]) for k, (r, v) in enumerate(zip(aux_refs, aux))]
    loads[0].start()
    load_right.start()
    for load in loads[1:] + load_aux:
        load.start()
    if n_swap:
        greet([name for _, name in swap_peers(1, kinds)])
        swap_finish = swap_begin(1, kinds, swap_in, swap_out, *refs[13:])
    else:
        greet([to_x, to_y, to_c])

    def product(k):
        loads[k].wait()

        @pl.loop(0, width // CHIP_COLS)
        def _(step):
            at = pl.ds(pl.multiple_of(step * CHIP_COLS, CHIP_COLS), CHIP_COLS)
            here_part = dot_cols(left[k], right[at]) if across else dot(left[k], right[:, at])
            part[k, 0, :, at] = here_part[:rows].astype(BF16)
            part[k, 1, :, at] = here_part[rows:].astype(BF16)

        return push(k, part.at[k, 1 - c], got.at[k], to_c)

    load_right.wait()
    sent = [product(0), product(1)]
    sent[0].wait_recv()
    add(0, got.at[0], 0, rows)
    far_x = push(4, part.at[0, c, low], near_x, to_x)
    far_y = push(5, part.at[0, c, high], near_y, to_y)
    sent.append(product(2))
    sent[1].wait_recv()
    add(1, got.at[1], 0, rows)
    plain_x = push(6, part.at[1, c, low], from_x.at[low], to_x)
    sent[2].wait_recv()
    add(2, got.at[2], 0, rows)
    plain_y = push(7, part.at[2, c, high], from_y.at[high], to_y)
    sent.append(product(3))
    far_y.wait_recv()
    add(1, near_y, cut, rows - cut, cut)
    more_x = push(8, part.at[1, c, high], from_x.at[high], to_x)
    far_x.wait_recv()
    add(2, near_x, 0, cut)
    more_y = push(9, part.at[2, c, low], from_y.at[low], to_y)
    sent[3].wait_recv()
    for load in load_aux:
        load.wait()
    plain_x.wait_recv()
    plain_y.wait_recv()
    more_x.wait_recv()
    more_y.wait_recv()
    gains = gains_ref[...]
    acc[...] = jnp.zeros_like(acc)

    @pl.loop(0, rows // SLAB)
    def _(step):
        at = pl.ds(pl.multiple_of(step * SLAB, SLAB), SLAB)
        total = part[3, c, at].astype(F32) + got[3, at].astype(F32) + from_x[at].astype(F32) + from_y[at].astype(F32)
        held = [a[at].astype(F32) for a in aux]
        if mode == "one":
            first, normal, inverse = first_norm(total, held[0], gains)
            outs[0][at] = first
            outs[1][at] = normal
            outs[2][at] = jnp.broadcast_to(inverse, (SLAB, 128))
            block[at] = first.astype(BF16)
        elif mode == "two":
            result, d_pre, terms = second_norm(total, held[0], held[1], gains)
            outs[0][at] = result.astype(BF16)
            outs[1][at] = d_pre
            block[at] = d_pre.astype(BF16)
            acc[0] += terms
            acc[1] += held[1]
        elif mode == "back":
            d_pre, terms, d_first = first_back(total, held[0], held[1], held[2][:, 0:1], gains)
            outs[0][at] = d_pre
            block[at] = d_pre.astype(BF16)
            acc[0] += terms
            acc[1] += d_first
        else:
            outs[0][at] = (deep_alpha * held[0] + total).astype(BF16)

    if mode in ("two", "back"):
        outs[-1][0:1] = jnp.sum(acc[0], axis=0, keepdims=True)
        outs[-1][1:2] = jnp.sum(acc[1], axis=0, keepdims=True)
    for copy in sent + [far_x, far_y, plain_x, plain_y, more_x, more_y]:
        copy.wait_send()
    if n_swap:
        swap_finish()
    if spread:
        spread_block(cut, 10, block, all_ref, send, recv, local.at[4])


def group_fold(name, mode, left, right, gains, aux, out_types, extras=(), kinds=()):
    across = mode != "one"
    rows, depth = left.shape[0] // 8, left.shape[1]
    width = gains.shape[1]
    cut = rows // 2
    spread = mode != "last"
    out_shape = [jax.ShapeDtypeStruct((8, rows, width), BF16)] * spread + out_types
    n, n_swap = len(aux), len(extras)
    n_sems = 23 if spread else 10
    return pl.pallas_call(
        functools.partial(fold_kernel, mode, across, n, len(out_types), kinds),
        out_shape=out_shape + swap_shapes(1, extras, kinds),
        in_specs=[ANY, ANY, ROWS] + [ANY] * (n + n_swap),
        out_specs=[ANY] * spread + [ROWS] * len(out_types) + [ANY] * n_swap,
        scratch_shapes=[pltpu.VMEM(a.shape, a.dtype) for a in aux]
        + [
            pltpu.VMEM((4, 2 * rows, depth), BF16),
            pltpu.VMEM(right.shape, BF16),
            pltpu.VMEM((4, 2, rows, width), BF16),
            pltpu.VMEM((4, rows, width), BF16),
            pltpu.VMEM((cut, width), BF16),
            pltpu.VMEM((rows - cut, width), BF16),
            pltpu.VMEM((rows, width), BF16),
            pltpu.VMEM((rows, width), BF16),
            pltpu.VMEM((rows, width), BF16),
            pltpu.VMEM((2, SLAB, width), F32),
            pltpu.SemaphoreType.DMA((n_sems,)),
            pltpu.SemaphoreType.DMA((n_sems,)),
            pltpu.SemaphoreType.DMA((5 + n,)),
        ]
        + (swap_scratch(1, kinds) if n_swap else []),
        compiler_params=pltpu.CompilerParams(
            collective_id=name, has_side_effects=True, vmem_limit_bytes=50 * 2**20
        ),
        cost_estimate=pl.CostEstimate(flops=0, bytes_accessed=(200 if spread else 110) * 2**20, transcendentals=0),
    )(left.reshape(4, 2 * rows, depth), right, gains, *aux, *extras)


def swap_kernel(zs, kinds, *refs):
    n = len(kinds)
    greet([name for _, name in swap_peers(zs, kinds)])
    swap_begin(zs, kinds, refs[:n], refs[n : 2 * n], *refs[2 * n :])()


def group_swap(name, zs, arrays, kinds):
    n = len(arrays)
    return pl.pallas_call(
        functools.partial(swap_kernel, zs, kinds),
        out_shape=swap_shapes(zs, arrays, kinds),
        in_specs=[ANY] * n,
        out_specs=[ANY] * n,
        scratch_shapes=swap_scratch(zs, kinds),
        compiler_params=pltpu.CompilerParams(collective_id=name, has_side_effects=True),
        cost_estimate=pl.CostEstimate(flops=0, bytes_accessed=50 * 2**20, transcendentals=0),
    )(*arrays)


def cut_kernel(in_ref, out_ref, in_blocks, out_blocks, wide):
    group, _, double = in_blocks.shape
    tile, ff = double // 2, out_ref.shape[1]
    span = group * tile
    odd = ff % 128
    live = lax.broadcasted_iota(jnp.int32, (in_ref.shape[0], span), 1) < ff
    wide[...] = jnp.zeros_like(wide)
    wide[:, : 2 * ff] = in_ref[...].astype(F32)
    gate = jnp.where(live, wide[:, :span], 0.0).astype(BF16)
    up = pltpu.roll(wide[:, ff - odd : ff - odd + span], span - odd, 1)
    up = jnp.where(live, up, 0.0).astype(BF16)
    wide[:, :span] = jnp.zeros_like(live, F32)
    wide[:, :ff] = out_ref[...].astype(F32)
    down = wide[:, :span].astype(BF16)
    for g in range(group):
        in_blocks[g, :, :tile] = gate[:, g * tile : (g + 1) * tile]
        in_blocks[g, :, tile:] = up[:, g * tile : (g + 1) * tile]
        out_blocks[g] = down[:, g * tile : (g + 1) * tile]


def cut_ff(w_in, w_out, group, tile):
    rows, ff = w_out.shape
    return pl.pallas_call(
        cut_kernel,
        grid=(rows // 16,),
        in_specs=[pl.BlockSpec((16, 2 * ff), lambda i: (i, 0)), pl.BlockSpec((16, ff), lambda i: (i, 0))],
        out_specs=[
            pl.BlockSpec((group, 16, 2 * tile), lambda i: (0, i, 0)),
            pl.BlockSpec((group, 16, tile), lambda i: (0, i, 0)),
        ],
        out_shape=[
            jax.ShapeDtypeStruct((group, rows, 2 * tile), BF16),
            jax.ShapeDtypeStruct((group, rows, tile), BF16),
        ],
        scratch_shapes=[pltpu.VMEM((16, -(-(ff + group * tile) // 128) * 128), F32)],
        compiler_params=PARAMS,
    )(w_in, w_out)


def join_kernel(in_blocks, out_blocks, in_ref, out_ref):
    group, _, double = in_blocks.shape
    tile, ff = double // 2, out_ref.shape[1]
    odd = ff % 128
    gate = jnp.concatenate([in_blocks[g, :, :tile] for g in range(group)], axis=1).astype(F32)
    up = jnp.concatenate([in_blocks[g, :, tile:] for g in range(group)], axis=1).astype(F32)
    up = pltpu.roll(up, odd, 1)
    lane = lax.broadcasted_iota(jnp.int32, (up.shape[0], 128), 1)
    in_ref[:, : ff - odd] = gate[:, : ff - odd]
    in_ref[:, ff - odd : ff - odd + 128] = jnp.where(lane < odd, gate[:, ff - odd : ff - odd + 128], up[:, :128])
    in_ref[:, ff - odd + 128 :] = up[:, 128 : ff + odd]
    down = jnp.concatenate([out_blocks[g] for g in range(group)], axis=1).astype(F32)
    out_ref[...] = down[:, :ff]


def join_ff(in_blocks, out_blocks, ff):
    group, rows, tile = out_blocks.shape
    return pl.pallas_call(
        join_kernel,
        grid=(rows // 16,),
        in_specs=[
            pl.BlockSpec((group, 16, 2 * tile), lambda i: (0, i, 0)),
            pl.BlockSpec((group, 16, tile), lambda i: (0, i, 0)),
        ],
        out_specs=[pl.BlockSpec((16, 2 * ff), lambda i: (i, 0)), pl.BlockSpec((16, ff), lambda i: (i, 0))],
        out_shape=[jax.ShapeDtypeStruct((rows, 2 * ff), F32), jax.ShapeDtypeStruct((rows, ff), F32)],
        compiler_params=PARAMS,
    )(in_blocks, out_blocks)


def on_device(sizes, x_in, d_out, w_qkv, w_dense, w_in, w_out, gone, bone, gtwo, btwo, flags, span_start, span_len):
    gy, gx, cores, zs = sizes
    piece = w_qkv.shape[0]
    ff = w_out.shape[1]
    group = gy * gx * cores
    width = D // group
    tile = -(-ff // (group * 128)) * 128
    own = gy == 2

    def permute(array):
        lead = array.shape[:-1]
        return jnp.swapaxes(array.reshape(lead + (group, zs, piece)), -3, -2).reshape(lead + (D,))

    def restore(array):
        lead = array.shape[:-1]
        return jnp.swapaxes(array.reshape(lead + (zs, group, piece)), -3, -2).reshape(lead + (D,))

    def swap(name, arrays, kinds):
        if own:
            return group_swap(name, zs, arrays, kinds)
        ways = {
            "swap": lambda a: lax.all_to_all(a, GROUP, 0, 0, tiled=True),
            "group": lambda a: lax.all_gather(a, GROUP, axis=0),
            "line": lambda a: lax.all_gather(a, "z", axis=0),
        }
        return [ways[k](a) for a, k in zip(arrays, kinds)]

    def spread_rows(block):
        whole = group_gather(block) if own else lax.all_gather(block, GROUP, axis=0)
        return whole.reshape(group * block.shape[0], block.shape[1])

    rows_f32 = jax.ShapeDtypeStruct((SEQ_LEN, D), F32)
    rows_low = jax.ShapeDtypeStruct((SEQ_LEN, D), BF16)
    sums_type = jax.ShapeDtypeStruct((8, D), F32)

    def fold(partial):
        return lax.psum_scatter(partial.astype(BF16), GROUP, scatter_dimension=0, tiled=True).astype(F32)

    def stack_sums(*arrays):
        return jnp.pad(jnp.stack([jnp.sum(a, axis=0) for a in arrays]), ((0, 6), (0, 0)))

    def fold_one(left, right, x, gains):
        if own:
            kinds = [rows_f32, rows_f32, jax.ShapeDtypeStruct((SEQ_LEN, 128), F32)]
            whole, first, normal, inverse = group_fold(0, "one", left, right, gains, [x], kinds)
            return whole.reshape(left.shape[0], D), first, normal, inverse
        first, normal, inverse = first_norm(fold(dot(left, right)), x.astype(F32), gains)
        return spread_rows(first.astype(BF16)), first, normal, inverse

    def fold_two(left, right, first, grad, gains):
        if own:
            kinds = [rows_low, rows_f32, sums_type]
            whole, result, d_pre, sums = group_fold(1, "two", left, right, gains, [first, grad], kinds)
            return whole.reshape(left.shape[0], D), result, d_pre, sums
        grad = grad.astype(F32)
        result, d_pre, terms = second_norm(fold(dot_cols(left, right)), first, grad, gains)
        return spread_rows(d_pre.astype(BF16)), result.astype(BF16), d_pre, stack_sums(terms, grad)

    def fold_back(left, right, d_pre_two, normal, inverse, gains):
        if own:
            kinds = [rows_f32, sums_type]
            whole, d_pre, sums = group_fold(7, "back", left, right, gains, [d_pre_two, normal, inverse], kinds)
            return whole.reshape(left.shape[0], D), d_pre, sums
        d_pre, terms, d_first = first_back(fold(dot_cols(left, right)), d_pre_two, normal, inverse, gains)
        return spread_rows(d_pre.astype(BF16)), d_pre, stack_sums(terms, d_first)

    def fold_last(left, right, d_pre, gains, extras, kinds):
        if own:
            return group_fold(8, "last", left, right, gains, [d_pre], [rows_low], extras, kinds)
        out = (deep_alpha * d_pre + fold(dot_cols(left, right))).astype(BF16)
        return [out] + swap(8, extras, kinds)

    def gather(block):
        return lax.all_gather(block, "z", axis=0, tiled=True)

    def scatter(partial):
        return lax.psum_scatter(partial.astype(BF16), "z", scatter_dimension=0, tiled=True)

    masked = jnp.max(flags) > 0
    prefix = jnp.where(masked, SEQ_LEN, SEQ_LEN - span_len[0])
    info = jnp.concatenate([gone, bone, gtwo, btwo, jnp.stack([prefix, span_start[0]]).astype(BF16)])
    info = jnp.pad(info[None, :], ((0, 15), (0, -info.shape[0] % 128)))

    qkv_blocks = jnp.moveaxis(w_qkv.reshape(piece, 3, group, width), 2, 0).reshape(group, piece, 3 * width)
    w_dense_part = gather(permute(w_dense))
    qkv_blocks, info = swap(2, [qkv_blocks, info], ("swap", "group"))
    w_qkv_part = gather(qkv_blocks.reshape(group * piece, 3 * width))
    in_blocks, out_blocks = cut_ff(w_in, w_out, group, tile)
    in_blocks, out_blocks, qkv_blocks = lax.optimization_barrier((in_blocks, out_blocks, qkv_blocks))
    in_blocks, out_blocks, info = swap(3, [in_blocks, out_blocks, info], ("swap", "swap", "line"))
    w_in_part = gather(in_blocks.reshape(group * piece, 2 * tile))
    x_perm = permute(x_in)
    x_next, in_blocks = lax.optimization_barrier((x_perm, in_blocks))
    x_all = spread_rows(x_next)

    info = info[:, :, 0]
    place_info = info[lax.axis_index("z"), :, 4 * piece : 4 * piece + 2].astype(jnp.int32)
    prefix, start = place_info[:, 0], place_info[:, 1]
    gains = info[:, :, : 4 * piece].astype(F32).reshape(zs, group, 4, piece)
    gains = jnp.pad(jnp.transpose(gains, (2, 0, 1, 3)).reshape(4, D), ((0, 4), (0, 0)))
    cosine, sine = tables(prefix, start)
    w_qkv_part, x_all, cosine, sine, gains = lax.optimization_barrier((w_qkv_part, x_all, cosine, sine, gains))
    packed = dot(x_all, w_qkv_part)
    qkv, context = attend(prefix, packed, cosine, sine)
    first_all, first, normal_one, inverse_one = fold_one(context, w_dense_part, x_perm, gains)
    out_blocks, first_all, w_in_part = lax.optimization_barrier((out_blocks, first_all, w_in_part))
    w_out_part = gather(out_blocks.reshape(group * piece, tile))
    projected = dot(first_all, w_in_part)
    gate, up = projected[:, :tile], projected[:, tile:]
    act, slope = gate_parts(gate)
    hidden = (act * up).astype(BF16)
    d_branch, layer_out, d_pre_two, sums_two = fold_two(hidden, w_out_part, first, permute(d_out), gains)
    layer_out = restore(layer_out)
    d_w_out = dot_rows(d_branch, hidden).astype(BF16)
    d_w_out, d_branch = lax.optimization_barrier((d_w_out, d_branch))
    d_w_out = scatter(d_w_out)
    d_hidden = dot(d_branch, w_out_part)
    d_projected = jnp.concatenate([d_hidden * up * slope, d_hidden * act], axis=1).astype(BF16)
    d_w_in = dot_rows(first_all, d_projected).astype(BF16)
    d_w_in, d_projected = lax.optimization_barrier((d_w_in, d_projected))
    d_w_in = scatter(d_w_in)
    d_attn, d_pre_one, sums_one = fold_back(d_projected, w_in_part, d_pre_two, normal_one, inverse_one, gains)
    d_attn, d_w_out = lax.optimization_barrier((d_attn, d_w_out))
    d_context = dot_cols(d_attn, w_dense_part).astype(BF16)
    d_packed = attend_back(prefix, qkv, d_context, cosine, sine)
    d_w_qkv = dot_rows(x_all, d_packed).astype(BF16)
    d_dense = dot_rows(context, d_attn).astype(BF16).reshape(zs, piece, group, width)
    d_dense = jnp.swapaxes(d_dense, 1, 2).reshape(D, width)
    d_w_qkv = jnp.concatenate([d_w_qkv, d_dense], axis=1)
    sums = jnp.concatenate([sums_one[:2], sums_two[:2], jnp.zeros((4, D), F32)])
    d_packed, d_w_qkv, d_w_in, sums = lax.optimization_barrier((d_packed, d_w_qkv, d_w_in, sums))
    d_w_qkv = scatter(d_w_qkv)
    d_w_in, d_w_out = d_w_in.reshape(group, piece, 2 * tile), d_w_out.reshape(group, piece, tile)
    d_input, d_w_in, d_w_out, sums = fold_last(
        d_packed, w_qkv_part, d_pre_one, gains, [d_w_in, d_w_out, sums], ("swap", "swap", "group")
    )
    d_input = restore(d_input)
    sums = jnp.sum(sums, axis=0).reshape(8, zs, group, piece)
    sums = lax.dynamic_index_in_dim(sums, lax.axis_index(GROUP), 2, keepdims=False).reshape(8, width)
    out_in, out_out = join_ff(d_w_in, d_w_out, ff)
    out_in, out_out, d_input, d_w_qkv, sums = lax.optimization_barrier((out_in, out_out, d_input, d_w_qkv, sums))
    out_dense = d_w_qkv[:, 3 * width :].reshape(group, piece, width)
    out_dense = restore(jnp.swapaxes(out_dense, 0, 1).reshape(piece, D)).astype(F32)
    d_w_qkv, sums = swap(5, [d_w_qkv[:, : 3 * width].reshape(group, piece, 3 * width), sums], ("swap", "line"))
    out_qkv = jnp.transpose(d_w_qkv.astype(F32).reshape(group, piece, 3, width), (1, 2, 0, 3)).reshape(piece, 3 * D)
    sums = jnp.sum(sums, axis=0).reshape(8, zs, piece)
    sums = lax.dynamic_index_in_dim(sums, lax.axis_index("z"), 1, keepdims=False)
    return layer_out, d_input, out_qkv, out_dense, out_in, out_out, sums[0], sums[1], sums[2], sums[3]


def solution(mesh):
    grp, shard = mesh.shape["grp"], mesh.shape["shard"]
    sizes = (grp // 4, 2, 2, shard)
    inner = Mesh(mesh.devices.reshape(sizes), ALL)
    rows, flat = P(ALL, None), P(ALL)
    return jax.shard_map(
        functools.partial(on_device, sizes),
        mesh=inner,
        in_specs=(rows,) * 6 + (flat,) * 7,
        out_specs=(rows,) * 6 + (flat,) * 4,
        check_vma=False,
    )
```

```python
import functools

import jax
import jax.numpy as jnp
from jax import lax
from jax.experimental import pallas as pl
from jax.experimental.pallas import tpu as pltpu
from jax.sharding import Mesh
from jax.sharding import PartitionSpec as P

HEADS = 16
HEAD = 128
SEQ_LEN = 224
D = HEADS * HEAD
deep_alpha = 6.928203230275509
norm_eps = 1e-05
far_below = -1e30
scale = HEAD ** (-0.5)

ALL = ("gy", "gx", "core", "z")
GROUP = ("gy", "gx", "core")
MESH = pl.DeviceIdType.MESH
F32 = jnp.float32
BF16 = jnp.bfloat16


def dot(left, right):
    return jnp.dot(left, right, preferred_element_type=F32)


def dot_rows(left, right):
    return lax.dot_general(left, right, (((0,), (0,)), ((), ())), preferred_element_type=F32)


def dot_cols(left, right):
    return lax.dot_general(left, right, (((1,), (1,)), ((), ())), preferred_element_type=F32)


def swap_halves(block):
    lane = lax.broadcasted_iota(jnp.int32, block.shape, 1)
    return jnp.where((lane & 32) == 0, pltpu.roll(block, 96, 1), pltpu.roll(block, 32, 1))


def seen(prefix):
    row = lax.broadcasted_iota(jnp.int32, (SEQ_LEN, SEQ_LEN), 0)
    col = lax.broadcasted_iota(jnp.int32, (SEQ_LEN, SEQ_LEN), 1)
    return (col < prefix) | (col <= row)


def softmax(queries, keys, visible):
    scores = jnp.where(visible, dot_cols(queries, keys), far_below)
    weights = jnp.exp(scores - jnp.max(scores, axis=1, keepdims=True))
    return weights / jnp.sum(weights, axis=1, keepdims=True)


def attend_kernel(prefix_ref, packed_ref, cos_ref, sin_ref, qkv_ref, context_ref):
    width = context_ref.shape[1]
    visible = seen(prefix_ref[pl.program_id(0)])
    cosine = cos_ref[0]
    sine = sin_ref[0]
    for head in range(width // HEAD):
        at = pl.ds(head * HEAD, HEAD)
        at_k = pl.ds(width + head * HEAD, HEAD)
        at_v = pl.ds(2 * width + head * HEAD, HEAD)
        raw = packed_ref[:, at]
        queries = ((raw * cosine + swap_halves(raw) * sine) * scale).astype(BF16)
        raw = packed_ref[:, at_k]
        keys = (raw * cosine + swap_halves(raw) * sine).astype(BF16)
        values = packed_ref[:, at_v].astype(BF16)
        qkv_ref[:, at] = queries
        qkv_ref[:, at_k] = keys
        qkv_ref[:, at_v] = values
        probs = softmax(queries, keys, visible).astype(BF16)
        context_ref[:, at] = dot(probs, values).astype(BF16)


def attend_back_kernel(prefix_ref, qkv_ref, d_context_ref, cos_ref, sin_ref, d_packed_ref):
    width = d_context_ref.shape[1]
    visible = seen(prefix_ref[pl.program_id(0)])
    cosine = cos_ref[0]
    sine = sin_ref[0]
    for head in range(width // HEAD):
        at = pl.ds(head * HEAD, HEAD)
        at_k = pl.ds(width + head * HEAD, HEAD)
        at_v = pl.ds(2 * width + head * HEAD, HEAD)
        queries = qkv_ref[:, at]
        keys = qkv_ref[:, at_k]
        values = qkv_ref[:, at_v]
        d_context = d_context_ref[:, at]
        probs = softmax(queries, keys, visible)
        d_packed_ref[:, at_v] = dot_rows(probs.astype(BF16), d_context).astype(BF16)
        d_probs = dot_cols(d_context, values)
        inner = jnp.sum(probs * d_probs, axis=1, keepdims=True)
        d_scores = (probs * (d_probs - inner)).astype(BF16)
        grad = dot(d_scores, keys) * scale
        d_packed_ref[:, at] = (grad * cosine - swap_halves(grad) * sine).astype(BF16)
        grad = dot_rows(d_scores, queries)
        d_packed_ref[:, at_k] = (grad * cosine - swap_halves(grad) * sine).astype(BF16)


def by_sequence(width):
    return pl.BlockSpec((SEQ_LEN, width), lambda s: (s, 0))


TABLE = pl.BlockSpec((1, SEQ_LEN, HEAD), lambda s: (s, 0, 0))
SCALARS = pl.BlockSpec(memory_space=pltpu.SMEM)
PARAMS = pltpu.CompilerParams(vmem_limit_bytes=48 * 2**20)


def attend(prefix, packed, cosine, sine):
    rows, width = packed.shape[0], packed.shape[1] // 3
    return pl.pallas_call(
        attend_kernel,
        grid=(rows // SEQ_LEN,),
        in_specs=[SCALARS, by_sequence(3 * width), TABLE, TABLE],
        out_specs=[by_sequence(3 * width), by_sequence(width)],
        out_shape=[
            jax.ShapeDtypeStruct((rows, 3 * width), BF16),
            jax.ShapeDtypeStruct((rows, width), BF16),
        ],
        compiler_params=PARAMS,
    )(prefix, packed, cosine, sine)


def attend_back(prefix, qkv, d_context, cosine, sine):
    rows, width = d_context.shape
    return pl.pallas_call(
        attend_back_kernel,
        grid=(rows // SEQ_LEN,),
        in_specs=[SCALARS, by_sequence(3 * width), by_sequence(width), TABLE, TABLE],
        out_specs=by_sequence(3 * width),
        out_shape=jax.ShapeDtypeStruct((rows, 3 * width), BF16),
        compiler_params=PARAMS,
    )(prefix, qkv, d_context, cosine, sine)


def tables(prefix, start):
    place = jnp.arange(SEQ_LEN, dtype=jnp.int32)
    in_span = place[None, :] >= prefix[:, None]
    pos_one = jnp.where(in_span, start[:, None], place[None, :])
    pos_two = jnp.where(in_span, place[None, :] - prefix[:, None] + 1, 0)
    lane = jnp.arange(HEAD)
    freqs = 10000.0 ** (-2.0 * (lane % 32).astype(F32) / 64)
    place_of = jnp.where(lane[None, None, :] < 64, pos_one[:, :, None], pos_two[:, :, None])
    angles = place_of.astype(F32) * freqs
    sign = jnp.where(lane % 64 < 32, -1.0, 1.0)
    return jnp.cos(angles), jnp.sin(angles) * sign


def norm_parts(values):
    center = values - jnp.mean(values, axis=-1, keepdims=True)
    inverse = lax.rsqrt(jnp.mean(center * center, axis=-1, keepdims=True) + norm_eps)
    return center * inverse, inverse


def norm_back(normal, inverse, gain, grad):
    scaled = gain * grad
    return inverse * (
        scaled
        - jnp.mean(scaled, axis=-1, keepdims=True)
        - normal * jnp.mean(scaled * normal, axis=-1, keepdims=True)
    )


def gate_parts(gate):
    phi = 0.5 * (1.0 + lax.erf(gate * 0.7071067811865476))
    slope = phi + gate * jnp.exp(-0.5 * gate * gate) * 0.3989422804014327
    return gate * phi, slope


def here():
    return lax.axis_index("gy"), lax.axis_index("gx"), lax.axis_index("core")


def place(y, x, c):
    return (y * 2 + x) * 2 + c


def greet(peers):
    barrier = pltpu.get_barrier_semaphore()
    for peer in peers:
        pl.semaphore_signal(barrier, inc=1, device_id=peer, device_id_type=MESH)
    pl.semaphore_wait(barrier, len(peers))


def spread_block(cut, base, block_ref, out_ref, send, recv, local):
    rows = block_ref.shape[0]
    y, x, c = here()
    to_x, to_y, to_c = {"gx": 1 - x}, {"gy": 1 - y}, {"core": 1 - c}
    me, by_x, by_y, far = place(y, x, c), place(y, 1 - x, c), place(1 - y, x, c), place(1 - y, 1 - x, c)
    low, high = pl.ds(0, cut), pl.ds(cut, rows - cut)

    def push(k, src, dst, to):
        copy = pltpu.make_async_remote_copy(
            src_ref=src, dst_ref=dst, send_sem=send.at[base + k], recv_sem=recv.at[base + k], device_id=to, device_id_type=MESH
        )
        copy.start()
        return copy

    def landed(k, dst):
        pltpu.make_async_remote_copy(
            src_ref=dst, dst_ref=dst, send_sem=send.at[base + k], recv_sem=recv.at[base + k], device_id=to_c, device_id_type=MESH
        ).wait_recv()

    sent = [
        push(0, block_ref.at[low], out_ref.at[me, low], to_x),
        push(1, block_ref.at[high], out_ref.at[me, high], to_y),
        push(2, block_ref.at[high], out_ref.at[me, high], to_x),
        push(3, block_ref.at[low], out_ref.at[me, low], to_y),
        push(4, block_ref, out_ref.at[me], to_c),
    ]
    keep = pltpu.make_async_copy(block_ref, out_ref.at[me], local)
    keep.start()
    landed(0, out_ref.at[by_x, low])
    sent.append(push(5, out_ref.at[by_x, low], out_ref.at[by_x, low], to_y))
    sent.append(push(7, out_ref.at[by_x, low], out_ref.at[by_x, low], to_c))
    landed(1, out_ref.at[by_y, high])
    sent.append(push(6, out_ref.at[by_y, high], out_ref.at[by_y, high], to_x))
    sent.append(push(8, out_ref.at[by_y, high], out_ref.at[by_y, high], to_c))
    landed(2, out_ref.at[by_x, high])
    sent.append(push(9, out_ref.at[by_x, high], out_ref.at[by_x, high], to_c))
    landed(3, out_ref.at[by_y, low])
    sent.append(push(10, out_ref.at[by_y, low], out_ref.at[by_y, low], to_c))
    landed(5, out_ref.at[far, low])
    sent.append(push(11, out_ref.at[far, low], out_ref.at[far, low], to_c))
    landed(6, out_ref.at[far, high])
    sent.append(push(12, out_ref.at[far, high], out_ref.at[far, high], to_c))
    other, other_x, other_y, other_far = (
        place(y, x, 1 - c),
        place(y, 1 - x, 1 - c),
        place(1 - y, x, 1 - c),
        place(1 - y, 1 - x, 1 - c),
    )
    landed(4, out_ref.at[other])
    landed(7, out_ref.at[other_x, low])
    landed(8, out_ref.at[other_y, high])
    landed(9, out_ref.at[other_x, high])
    landed(10, out_ref.at[other_y, low])
    landed(11, out_ref.at[other_far, low])
    landed(12, out_ref.at[other_far, high])
    keep.wait()
    for copy in sent:
        copy.wait_send()


def gather_kernel(cut, block_ref, out_ref, send, recv, local):
    y, x, c = here()
    greet([{"gx": 1 - x}, {"gy": 1 - y}, {"core": 1 - c}])
    spread_block(cut, 0, block_ref, out_ref, send, recv, local)


ANY = pl.BlockSpec(memory_space=pl.ANY)


def group_gather(block):
    rows, width = block.shape
    return pl.pallas_call(
        functools.partial(gather_kernel, rows // 2),
        out_shape=jax.ShapeDtypeStruct((8, rows, width), block.dtype),
        in_specs=[ANY],
        out_specs=ANY,
        scratch_shapes=[pltpu.SemaphoreType.DMA((13,)), pltpu.SemaphoreType.DMA((13,)), pltpu.SemaphoreType.DMA],
        compiler_params=pltpu.CompilerParams(collective_id=9, has_side_effects=True),
        cost_estimate=pl.CostEstimate(flops=0, bytes_accessed=100 * 2**20, transcendentals=0),
    )(block)


def swap_peers(zs, kinds):
    y, x, c = here()
    z = lax.axis_index("z")
    found = []
    for k in range(1, 8):
        peer = ((y + k // 4) % 2, (x + k // 2 % 2) % 2, (c + k % 2) % 2)
        found.append((place(*peer), {"gy": peer[0], "gx": peer[1], "core": peer[2]}))
    if "line" in kinds:
        found += [((z + k) % zs, {"z": (z + k) % zs}) for k in range(1, zs)]
    return found


def swap_begin(zs, kinds, blocks, outs, send, recv, local):
    copies, comes, keeps = [], [], []
    found = swap_peers(zs, kinds)
    for i, kind in enumerate(kinds):
        me = lax.axis_index("z") if kind == "line" else place(*here())
        for k, (peer, name) in enumerate(found[7:] if kind == "line" else found[:7]):
            src = blocks[i].at[peer] if kind == "swap" else blocks[i]
            landing = outs[i].at[peer]
            sems = dict(send_sem=send.at[i, k], recv_sem=recv.at[i, k], device_id=name, device_id_type=MESH)
            copies.append(pltpu.make_async_remote_copy(src_ref=src, dst_ref=outs[i].at[me], **sems))
            comes.append(pltpu.make_async_remote_copy(src_ref=landing, dst_ref=landing, **sems))
            copies[-1].start()
        own = blocks[i].at[me] if kind == "swap" else blocks[i]
        keeps.append(pltpu.make_async_copy(own, outs[i].at[me], local.at[i]))
        keeps[-1].start()

    def finish():
        for come in comes:
            come.wait_recv()
        for copy in copies:
            copy.wait_send()
        for keep in keeps:
            keep.wait()

    return finish


SWAP_LEAD = {"swap": lambda zs: (), "group": lambda zs: (8,), "line": lambda zs: (zs,)}


def swap_shapes(zs, arrays, kinds):
    return [jax.ShapeDtypeStruct(SWAP_LEAD[k](zs) + a.shape, a.dtype) for a, k in zip(arrays, kinds)]


def swap_scratch(zs, kinds):
    n, most = len(kinds), max(7, zs - 1)
    return [
        pltpu.SemaphoreType.DMA((n, most)),
        pltpu.SemaphoreType.DMA((n, most)),
        pltpu.SemaphoreType.DMA((n,)),
    ]


SLAB = 16
ROWS = pl.BlockSpec(memory_space=pltpu.VMEM)
CHIP_COLS = 256


def in_order(value, zs, piece):
    group = D // (zs * piece)
    order = [z * group + g for g in range(group) for z in range(zs)]
    return jnp.concatenate([value[:, m * piece : (m + 1) * piece] for m in order], axis=1)


def first_norm(total, x, gains):
    normal, inverse = norm_parts(deep_alpha * x + total)
    first = normal * gains[0:1] + gains[1:2]
    return first, normal, inverse


def second_norm(total, first, grad, gains):
    normal, inverse = norm_parts(deep_alpha * first + total)
    return normal * gains[2:3] + gains[3:4], norm_back(normal, inverse, gains[2:3], grad), grad * normal


def first_back(total, d_pre_two, normal, inverse, gains):
    d_first = deep_alpha * d_pre_two + total
    return norm_back(normal, inverse, gains[0:1], d_first), d_first * normal, d_first


def fold_kernel(mode, across, zs, piece, n_aux, n_out, kinds, *refs):
    left_ref, right_ref, gains_ref = refs[:3]
    aux_refs = refs[3 : 3 + n_aux]
    refs = refs[3 + n_aux :]
    n_swap = len(kinds)
    swap_in, refs = refs[:n_swap], refs[n_swap:]
    spread = mode != "last"
    if spread:
        all_ref, refs = refs[0], refs[1:]
    outs, refs = refs[:n_out], refs[n_out:]
    swap_out, refs = refs[:n_swap], refs[n_swap:]
    aux, refs = refs[:n_aux], refs[n_aux:]
    left, right, part, got, near_x, near_y, from_x, from_y, block, acc, send, recv, local = refs[:13]
    rows, width = block.shape
    cut = near_x.shape[0]
    y, x, c = here()
    to_x, to_y, to_c = {"gx": 1 - x}, {"gy": 1 - y}, {"core": 1 - c}
    chips = [(1 - y, 1 - x), (y, 1 - x), (1 - y, x), (y, x)]
    low, high = pl.ds(0, cut), pl.ds(cut, rows - cut)

    def push(k, src, dst, to):
        copy = pltpu.make_async_remote_copy(
            src_ref=src, dst_ref=dst, send_sem=send.at[k], recv_sem=recv.at[k], device_id=to, device_id_type=MESH
        )
        copy.start()
        return copy

    def add(k, extra, start, size, offset=0):
        @pl.loop(0, size // SLAB)
        def _(step):
            at = pl.ds(pl.multiple_of(start + step * SLAB, SLAB), SLAB)
            of = pl.ds(pl.multiple_of(start - offset + step * SLAB, SLAB), SLAB)
            part[k, c, at] = (part[k, c, at].astype(F32) + extra[of].astype(F32)).astype(BF16)

    loads = [pltpu.make_async_copy(left_ref.at[a * 2 + b], left.at[k], local.at[k]) for k, (a, b) in enumerate(chips)]
    load_right = pltpu.make_async_copy(right_ref, right, local.at[4])
    load_aux = [pltpu.make_async_copy(r, v, local.at[5 + k]) for k, (r, v) in enumerate(zip(aux_refs, aux))]
    loads[0].start()
    load_right.start()
    for load in loads[1:] + load_aux:
        load.start()
    if n_swap:
        greet([name for _, name in swap_peers(1, kinds)])
        swap_finish = swap_begin(1, kinds, swap_in, swap_out, *refs[13:])
    else:
        greet([to_x, to_y, to_c])

    def product(k):
        loads[k].wait()

        @pl.loop(0, width // CHIP_COLS)
        def _(step):
            at = pl.ds(pl.multiple_of(step * CHIP_COLS, CHIP_COLS), CHIP_COLS)
            here_part = dot_cols(left[k], right[at]) if across else dot(left[k], right[:, at])
            part[k, 0, :, at] = here_part[:rows].astype(BF16)
            part[k, 1, :, at] = here_part[rows:].astype(BF16)

        return push(k, part.at[k, 1 - c], got.at[k], to_c)

    load_right.wait()
    sent = [product(0), product(1)]
    sent[0].wait_recv()
    add(0, got.at[0], 0, rows)
    far_x = push(4, part.at[0, c, low], near_x, to_x)
    far_y = push(5, part.at[0, c, high], near_y, to_y)
    sent.append(product(2))
    sent[1].wait_recv()
    add(1, got.at[1], 0, rows)
    plain_x = push(6, part.at[1, c, low], from_x.at[low], to_x)
    sent[2].wait_recv()
    add(2, got.at[2], 0, rows)
    plain_y = push(7, part.at[2, c, high], from_y.at[high], to_y)
    sent.append(product(3))
    far_y.wait_recv()
    add(1, near_y, cut, rows - cut, cut)
    more_x = push(8, part.at[1, c, high], from_x.at[high], to_x)
    far_x.wait_recv()
    add(2, near_x, 0, cut)
    more_y = push(9, part.at[2, c, low], from_y.at[low], to_y)
    sent[3].wait_recv()
    for load in load_aux:
        load.wait()
    plain_x.wait_recv()
    plain_y.wait_recv()
    more_x.wait_recv()
    more_y.wait_recv()
    gains = gains_ref[...]
    acc[...] = jnp.zeros_like(acc)

    @pl.loop(0, rows // SLAB)
    def _(step):
        at = pl.ds(pl.multiple_of(step * SLAB, SLAB), SLAB)
        total = part[3, c, at].astype(F32) + got[3, at].astype(F32) + from_x[at].astype(F32) + from_y[at].astype(F32)
        held = [a[at].astype(F32) for a in aux]
        if mode == "one":
            first, normal, inverse = first_norm(total, held[0], gains)
            outs[0][at] = first
            outs[1][at] = normal
            outs[2][at] = jnp.broadcast_to(inverse, (SLAB, 128))
            block[at] = first.astype(BF16)
        elif mode == "two":
            result, d_pre, terms = second_norm(total, held[0], held[1], gains)
            outs[0][at] = in_order(result, zs, piece).astype(BF16)
            outs[1][at] = d_pre
            block[at] = d_pre.astype(BF16)
            acc[0] += terms
            acc[1] += held[1]
        elif mode == "back":
            d_pre, terms, d_first = first_back(total, held[0], held[1], held[2][:, 0:1], gains)
            outs[0][at] = d_pre
            block[at] = d_pre.astype(BF16)
            acc[0] += terms
            acc[1] += d_first
        else:
            outs[0][at] = in_order(deep_alpha * held[0] + total, zs, piece).astype(BF16)

    if mode in ("two", "back"):
        outs[-1][0:1] = jnp.sum(acc[0], axis=0, keepdims=True)
        outs[-1][1:2] = jnp.sum(acc[1], axis=0, keepdims=True)
    for copy in sent + [far_x, far_y, plain_x, plain_y, more_x, more_y]:
        copy.wait_send()
    if n_swap:
        swap_finish()
    if spread:
        spread_block(cut, 10, block, all_ref, send, recv, local.at[4])


def group_fold(name, zs, mode, left, right, gains, aux, out_types, extras=(), kinds=()):
    across = mode != "one"
    rows, depth = left.shape[0] // 8, left.shape[1]
    width = gains.shape[1]
    cut = rows // 2
    spread = mode != "last"
    out_shape = [jax.ShapeDtypeStruct((8, rows, width), BF16)] * spread + out_types
    n, n_swap = len(aux), len(extras)
    n_sems = 23 if spread else 10
    return pl.pallas_call(
        functools.partial(fold_kernel, mode, across, zs, width // (8 * zs), n, len(out_types), kinds),
        out_shape=out_shape + swap_shapes(1, extras, kinds),
        in_specs=[ANY, ANY, ROWS] + [ANY] * (n + n_swap),
        out_specs=[ANY] * spread + [ROWS] * len(out_types) + [ANY] * n_swap,
        scratch_shapes=[pltpu.VMEM(a.shape, a.dtype) for a in aux]
        + [
            pltpu.VMEM((4, 2 * rows, depth), BF16),
            pltpu.VMEM(right.shape, BF16),
            pltpu.VMEM((4, 2, rows, width), BF16),
            pltpu.VMEM((4, rows, width), BF16),
            pltpu.VMEM((cut, width), BF16),
            pltpu.VMEM((rows - cut, width), BF16),
            pltpu.VMEM((rows, width), BF16),
            pltpu.VMEM((rows, width), BF16),
            pltpu.VMEM((rows, width), BF16),
            pltpu.VMEM((2, SLAB, width), F32),
            pltpu.SemaphoreType.DMA((n_sems,)),
            pltpu.SemaphoreType.DMA((n_sems,)),
            pltpu.SemaphoreType.DMA((5 + n,)),
        ]
        + (swap_scratch(1, kinds) if n_swap else []),
        compiler_params=pltpu.CompilerParams(
            collective_id=name, has_side_effects=True, vmem_limit_bytes=50 * 2**20
        ),
        cost_estimate=pl.CostEstimate(flops=0, bytes_accessed=(200 if spread else 110) * 2**20, transcendentals=0),
    )(left.reshape(4, 2 * rows, depth), right, gains, *aux, *extras)


def swap_kernel(zs, kinds, *refs):
    n = len(kinds)
    greet([name for _, name in swap_peers(zs, kinds)])
    swap_begin(zs, kinds, refs[:n], refs[n : 2 * n], *refs[2 * n :])()


def group_swap(name, zs, arrays, kinds):
    n = len(arrays)
    return pl.pallas_call(
        functools.partial(swap_kernel, zs, kinds),
        out_shape=swap_shapes(zs, arrays, kinds),
        in_specs=[ANY] * n,
        out_specs=[ANY] * n,
        scratch_shapes=swap_scratch(zs, kinds),
        compiler_params=pltpu.CompilerParams(collective_id=name, has_side_effects=True),
        cost_estimate=pl.CostEstimate(flops=0, bytes_accessed=50 * 2**20, transcendentals=0),
    )(*arrays)


def cut_kernel(in_ref, out_ref, in_blocks, out_blocks, wide):
    group, _, double = in_blocks.shape
    tile, ff = double // 2, out_ref.shape[1]
    span = group * tile
    odd = ff % 128
    live = lax.broadcasted_iota(jnp.int32, (in_ref.shape[0], span), 1) < ff
    wide[...] = jnp.zeros_like(wide)
    wide[:, : 2 * ff] = in_ref[...].astype(F32)
    gate = jnp.where(live, wide[:, :span], 0.0).astype(BF16)
    up = pltpu.roll(wide[:, ff - odd : ff - odd + span], span - odd, 1)
    up = jnp.where(live, up, 0.0).astype(BF16)
    wide[:, :span] = jnp.zeros_like(live, F32)
    wide[:, :ff] = out_ref[...].astype(F32)
    down = wide[:, :span].astype(BF16)
    for g in range(group):
        in_blocks[g, :, :tile] = gate[:, g * tile : (g + 1) * tile]
        in_blocks[g, :, tile:] = up[:, g * tile : (g + 1) * tile]
        out_blocks[g] = down[:, g * tile : (g + 1) * tile]


def cut_ff(w_in, w_out, group, tile):
    rows, ff = w_out.shape
    return pl.pallas_call(
        cut_kernel,
        grid=(rows // 16,),
        in_specs=[pl.BlockSpec((16, 2 * ff), lambda i: (i, 0)), pl.BlockSpec((16, ff), lambda i: (i, 0))],
        out_specs=[
            pl.BlockSpec((group, 16, 2 * tile), lambda i: (0, i, 0)),
            pl.BlockSpec((group, 16, tile), lambda i: (0, i, 0)),
        ],
        out_shape=[
            jax.ShapeDtypeStruct((group, rows, 2 * tile), BF16),
            jax.ShapeDtypeStruct((group, rows, tile), BF16),
        ],
        scratch_shapes=[pltpu.VMEM((16, -(-(ff + group * tile) // 128) * 128), F32)],
        compiler_params=PARAMS,
    )(w_in, w_out)


def join_kernel(in_blocks, out_blocks, in_ref, out_ref):
    group, _, double = in_blocks.shape
    tile, ff = double // 2, out_ref.shape[1]
    odd = ff % 128
    gate = jnp.concatenate([in_blocks[g, :, :tile] for g in range(group)], axis=1).astype(F32)
    up = jnp.concatenate([in_blocks[g, :, tile:] for g in range(group)], axis=1).astype(F32)
    up = pltpu.roll(up, odd, 1)
    lane = lax.broadcasted_iota(jnp.int32, (up.shape[0], 128), 1)
    in_ref[:, : ff - odd] = gate[:, : ff - odd]
    in_ref[:, ff - odd : ff - odd + 128] = jnp.where(lane < odd, gate[:, ff - odd : ff - odd + 128], up[:, :128])
    in_ref[:, ff - odd + 128 :] = up[:, 128 : ff + odd]
    down = jnp.concatenate([out_blocks[g] for g in range(group)], axis=1).astype(F32)
    out_ref[...] = down[:, :ff]


def join_ff(in_blocks, out_blocks, ff):
    group, rows, tile = out_blocks.shape
    return pl.pallas_call(
        join_kernel,
        grid=(rows // 16,),
        in_specs=[
            pl.BlockSpec((group, 16, 2 * tile), lambda i: (0, i, 0)),
            pl.BlockSpec((group, 16, tile), lambda i: (0, i, 0)),
        ],
        out_specs=[pl.BlockSpec((16, 2 * ff), lambda i: (i, 0)), pl.BlockSpec((16, ff), lambda i: (i, 0))],
        out_shape=[jax.ShapeDtypeStruct((rows, 2 * ff), F32), jax.ShapeDtypeStruct((rows, ff), F32)],
        compiler_params=PARAMS,
    )(in_blocks, out_blocks)


def closing_kernel(zs, sum_ref, rows_ref, qkv_ref, dense_ref, total_ref, got, mine, lines, *refs):
    send, recv, local, line_send, line_recv = refs
    y, x, c = here()
    z = lax.axis_index("z")
    me = place(y, x, c)
    wide = got.shape[2]
    width = wide // 3
    piece = got.shape[1]
    found = swap_peers(zs, ("line",))
    greet([name for _, name in found])
    copies, comes = [], []
    for k, (peer, name) in enumerate(found[:7]):
        sems = dict(send_sem=send.at[k], recv_sem=recv.at[k], device_id=name, device_id_type=MESH)
        src = rows_ref.at[peer, :, pl.ds(0, wide)]
        copies.append(pltpu.make_async_remote_copy(src_ref=src, dst_ref=got.at[me], **sems))
        comes.append(pltpu.make_async_remote_copy(src_ref=got.at[peer], dst_ref=got.at[peer], **sems))
    for k, (peer, name) in enumerate(found[7:]):
        sems = dict(send_sem=line_send.at[k], recv_sem=line_recv.at[k], device_id=name, device_id_type=MESH)
        copies.append(pltpu.make_async_remote_copy(src_ref=sum_ref, dst_ref=lines.at[z], **sems))
        comes.append(pltpu.make_async_remote_copy(src_ref=lines.at[peer], dst_ref=lines.at[peer], **sems))
    for copy in copies:
        copy.start()
    keeps = [
        pltpu.make_async_copy(rows_ref.at[me, :, pl.ds(0, wide)], got.at[me], local.at[0]),
        pltpu.make_async_copy(sum_ref, lines.at[z], local.at[1]),
        pltpu.make_async_copy(rows_ref.at[:, :, pl.ds(wide, width)], mine, local.at[2]),
    ]
    for keep in keeps:
        keep.start()
    keeps[2].wait()
    for at in range(0, piece, 16):
        rows = jnp.concatenate([mine[g, at : at + 16] for g in range(8)], axis=1).astype(F32)
        dense_ref[at : at + 16] = in_order(rows, zs, piece)
    for come in comes:
        come.wait_recv()
    for keep in keeps[:2]:
        keep.wait()
    for g in range(8):
        for j in range(3):
            at = pl.ds(j * D + g * width, width)
            qkv_ref[:, at] = got[g, :, j * width : (j + 1) * width].astype(F32)
    total = lines[0]
    for k in range(1, zs):
        total += lines[k]
    part = total[:, :piece]
    for k in range(1, zs):
        part = jnp.where(z == k, total[:, k * piece : (k + 1) * piece], part)
    total_ref[...] = part
    for copy in copies:
        copy.wait_send()


def closing(zs, sums, rows):
    _, piece, columns = rows.shape
    width = columns // 4
    return pl.pallas_call(
        functools.partial(closing_kernel, zs),
        out_shape=[
            jax.ShapeDtypeStruct((piece, 3 * D), F32),
            jax.ShapeDtypeStruct((piece, D), F32),
            jax.ShapeDtypeStruct((8, piece), F32),
        ],
        in_specs=[ROWS, ANY],
        out_specs=[ROWS] * 3,
        scratch_shapes=[
            pltpu.VMEM((8, piece, 3 * width), BF16),
            pltpu.VMEM((8, piece, width), BF16),
            pltpu.VMEM((zs, 8, width), F32),
            pltpu.SemaphoreType.DMA((7,)),
            pltpu.SemaphoreType.DMA((7,)),
            pltpu.SemaphoreType.DMA((3,)),
            pltpu.SemaphoreType.DMA((zs - 1,)),
            pltpu.SemaphoreType.DMA((zs - 1,)),
        ],
        compiler_params=pltpu.CompilerParams(collective_id=5, has_side_effects=True, vmem_limit_bytes=24 * 2**20),
        cost_estimate=pl.CostEstimate(flops=0, bytes_accessed=50 * 2**20, transcendentals=0),
    )(sums, rows)


def on_device(sizes, x_in, d_out, w_qkv, w_dense, w_in, w_out, gone, bone, gtwo, btwo, flags, span_start, span_len):
    gy, gx, cores, zs = sizes
    piece = w_qkv.shape[0]
    ff = w_out.shape[1]
    group = gy * gx * cores
    width = D // group
    tile = -(-ff // (group * 128)) * 128
    own = gy == 2

    def permute(array):
        lead = array.shape[:-1]
        return jnp.swapaxes(array.reshape(lead + (group, zs, piece)), -3, -2).reshape(lead + (D,))

    def restore(array):
        lead = array.shape[:-1]
        return jnp.swapaxes(array.reshape(lead + (zs, group, piece)), -3, -2).reshape(lead + (D,))

    def swap(name, arrays, kinds):
        if own:
            return group_swap(name, zs, arrays, kinds)
        ways = {
            "swap": lambda a: lax.all_to_all(a, GROUP, 0, 0, tiled=True),
            "group": lambda a: lax.all_gather(a, GROUP, axis=0),
            "line": lambda a: lax.all_gather(a, "z", axis=0),
        }
        return [ways[k](a) for a, k in zip(arrays, kinds)]

    def spread_rows(block):
        whole = group_gather(block) if own else lax.all_gather(block, GROUP, axis=0)
        return whole.reshape(group * block.shape[0], block.shape[1])

    rows_f32 = jax.ShapeDtypeStruct((SEQ_LEN, D), F32)
    rows_low = jax.ShapeDtypeStruct((SEQ_LEN, D), BF16)
    sums_type = jax.ShapeDtypeStruct((8, D), F32)

    def fold(partial):
        return lax.psum_scatter(partial.astype(BF16), GROUP, scatter_dimension=0, tiled=True).astype(F32)

    def stack_sums(*arrays):
        return jnp.pad(jnp.stack([jnp.sum(a, axis=0) for a in arrays]), ((0, 6), (0, 0)))

    def fold_one(left, right, x, gains):
        if own:
            kinds = [rows_f32, rows_f32, jax.ShapeDtypeStruct((SEQ_LEN, 128), F32)]
            whole, first, normal, inverse = group_fold(0, zs, "one", left, right, gains, [x], kinds)
            return whole.reshape(left.shape[0], D), first, normal, inverse
        first, normal, inverse = first_norm(fold(dot(left, right)), x.astype(F32), gains)
        return spread_rows(first.astype(BF16)), first, normal, inverse

    def fold_two(left, right, first, grad, gains):
        if own:
            kinds = [rows_low, rows_f32, sums_type]
            whole, result, d_pre, sums = group_fold(1, zs, "two", left, right, gains, [first, grad], kinds)
            return whole.reshape(left.shape[0], D), result, d_pre, sums
        grad = grad.astype(F32)
        result, d_pre, terms = second_norm(fold(dot_cols(left, right)), first, grad, gains)
        return spread_rows(d_pre.astype(BF16)), restore(result.astype(BF16)), d_pre, stack_sums(terms, grad)

    def fold_back(left, right, d_pre_two, normal, inverse, gains):
        if own:
            kinds = [rows_f32, sums_type]
            whole, d_pre, sums = group_fold(7, zs, "back", left, right, gains, [d_pre_two, normal, inverse], kinds)
            return whole.reshape(left.shape[0], D), d_pre, sums
        d_pre, terms, d_first = first_back(fold(dot_cols(left, right)), d_pre_two, normal, inverse, gains)
        return spread_rows(d_pre.astype(BF16)), d_pre, stack_sums(terms, d_first)

    def fold_last(left, right, d_pre, gains, extras, kinds):
        if own:
            return group_fold(8, zs, "last", left, right, gains, [d_pre], [rows_low], extras, kinds)
        out = restore((deep_alpha * d_pre + fold(dot_cols(left, right))).astype(BF16))
        return [out] + swap(8, extras, kinds)

    def gather(block):
        return lax.all_gather(block, "z", axis=0, tiled=True)

    def scatter(partial):
        return lax.psum_scatter(partial.astype(BF16), "z", scatter_dimension=0, tiled=True)

    masked = jnp.max(flags) > 0
    prefix = jnp.where(masked, SEQ_LEN, SEQ_LEN - span_len[0])
    info = jnp.concatenate([gone, bone, gtwo, btwo, jnp.stack([prefix, span_start[0]]).astype(BF16)])
    info = jnp.pad(info[None, :], ((0, 15), (0, -info.shape[0] % 128)))

    qkv_blocks = jnp.moveaxis(w_qkv.reshape(piece, 3, group, width), 2, 0).reshape(group, piece, 3 * width)
    w_dense, qkv_blocks = lax.optimization_barrier((permute(w_dense), qkv_blocks))
    w_dense_part = gather(w_dense)
    qkv_blocks, info = swap(2, [qkv_blocks, info], ("swap", "group"))
    w_qkv_part = gather(qkv_blocks.reshape(group * piece, 3 * width))
    in_blocks, out_blocks = cut_ff(w_in, w_out, group, tile)
    in_blocks, out_blocks, qkv_blocks, w_dense_part = lax.optimization_barrier(
        (in_blocks, out_blocks, qkv_blocks, w_dense_part)
    )
    in_blocks, out_blocks, info = swap(3, [in_blocks, out_blocks, info], ("swap", "swap", "line"))
    w_in_part = gather(in_blocks.reshape(group * piece, 2 * tile))
    x_perm = permute(x_in)
    x_next, in_blocks = lax.optimization_barrier((x_perm, in_blocks))
    x_all = spread_rows(x_next)

    info = info[:, :, 0]
    place_info = info[lax.axis_index("z"), :, 4 * piece : 4 * piece + 2].astype(jnp.int32)
    prefix, start = place_info[:, 0], place_info[:, 1]
    gains = info[:, :, : 4 * piece].astype(F32).reshape(zs, group, 4, piece)
    gains = jnp.pad(jnp.transpose(gains, (2, 0, 1, 3)).reshape(4, D), ((0, 4), (0, 0)))
    cosine, sine = tables(prefix, start)
    w_qkv_part, x_all, cosine, sine, gains = lax.optimization_barrier((w_qkv_part, x_all, cosine, sine, gains))
    packed = dot(x_all, w_qkv_part)
    qkv, context = attend(prefix, packed, cosine, sine)
    first_all, first, normal_one, inverse_one = fold_one(context, w_dense_part, x_perm, gains)
    out_blocks, first_all, w_in_part = lax.optimization_barrier((out_blocks, first_all, w_in_part))
    w_out_part = gather(out_blocks.reshape(group * piece, tile))
    projected = dot(first_all, w_in_part)
    gate, up = projected[:, :tile], projected[:, tile:]
    act, slope = gate_parts(gate)
    hidden = (act * up).astype(BF16)
    d_branch, layer_out, d_pre_two, sums_two = fold_two(hidden, w_out_part, first, permute(d_out), gains)
    d_w_out = dot_rows(d_branch, hidden).astype(BF16)
    d_w_out, d_branch = lax.optimization_barrier((d_w_out, d_branch))
    d_w_out = scatter(d_w_out)
    d_hidden = dot(d_branch, w_out_part)
    d_projected = jnp.concatenate([d_hidden * up * slope, d_hidden * act], axis=1).astype(BF16)
    d_w_in = dot_rows(first_all, d_projected).astype(BF16)
    d_w_in, d_projected = lax.optimization_barrier((d_w_in, d_projected))
    d_w_in = scatter(d_w_in)
    d_attn, d_pre_one, sums_one = fold_back(d_projected, w_in_part, d_pre_two, normal_one, inverse_one, gains)
    d_attn, d_w_out = lax.optimization_barrier((d_attn, d_w_out))
    d_context = dot_cols(d_attn, w_dense_part).astype(BF16)
    d_packed = attend_back(prefix, qkv, d_context, cosine, sine)
    d_w_qkv = dot_rows(x_all, d_packed).astype(BF16)
    d_dense = dot_rows(context, d_attn).astype(BF16).reshape(zs, piece, group, width)
    d_dense = jnp.swapaxes(d_dense, 1, 2).reshape(D, width)
    d_w_qkv = jnp.concatenate([d_w_qkv, d_dense], axis=1)
    sums = jnp.concatenate([sums_one[:2], sums_two[:2], jnp.zeros((4, D), F32)])
    d_packed, d_w_qkv, d_w_in, sums = lax.optimization_barrier((d_packed, d_w_qkv, d_w_in, sums))
    d_w_qkv = scatter(d_w_qkv)
    d_w_in, d_w_out = d_w_in.reshape(group, piece, 2 * tile), d_w_out.reshape(group, piece, tile)
    d_input, d_w_in, d_w_out, sums = fold_last(
        d_packed, w_qkv_part, d_pre_one, gains, [d_w_in, d_w_out, sums], ("swap", "swap", "group")
    )
    sums = jnp.sum(sums, axis=0).reshape(8, zs, group, piece)
    sums = lax.dynamic_index_in_dim(sums, lax.axis_index(GROUP), 2, keepdims=False).reshape(8, width)
    out_in, out_out = join_ff(d_w_in, d_w_out, ff)
    out_in, out_out, d_input, d_w_qkv, sums = lax.optimization_barrier((out_in, out_out, d_input, d_w_qkv, sums))
    if own:
        out_qkv, out_dense, sums = closing(zs, sums, d_w_qkv.reshape(group, piece, 4 * width))
    else:
        out_dense = d_w_qkv[:, 3 * width :].reshape(group, piece, width)
        out_dense = restore(jnp.swapaxes(out_dense, 0, 1).reshape(piece, D)).astype(F32)
        d_w_qkv = d_w_qkv[:, : 3 * width].reshape(group, piece, 3 * width)
        d_w_qkv, sums = swap(5, [d_w_qkv, sums], ("swap", "line"))
        out_qkv = jnp.transpose(d_w_qkv.astype(F32).reshape(group, piece, 3, width), (1, 2, 0, 3))
        out_qkv = out_qkv.reshape(piece, 3 * D)
        sums = jnp.sum(sums, axis=0).reshape(8, zs, piece)
        sums = lax.dynamic_index_in_dim(sums, lax.axis_index("z"), 1, keepdims=False)
    return layer_out, d_input, out_qkv, out_dense, out_in, out_out, sums[0], sums[1], sums[2], sums[3]


def solution(mesh):
    grp, shard = mesh.shape["grp"], mesh.shape["shard"]
    sizes = (grp // 4, 2, 2, shard)
    inner = Mesh(mesh.devices.reshape(sizes), ALL)
    rows, flat = P(ALL, None), P(ALL)
    return jax.shard_map(
        functools.partial(on_device, sizes),
        mesh=inner,
        in_specs=(rows,) * 6 + (flat,) * 7,
        out_specs=(rows,) * 6 + (flat,) * 4,
        check_vma=False,
    )
```

```python
import functools

import jax
import jax.numpy as jnp
from jax import lax
from jax.experimental import pallas as pl
from jax.experimental.pallas import tpu as pltpu
from jax.sharding import Mesh
from jax.sharding import PartitionSpec as P

HEADS = 16
HEAD = 128
SEQ_LEN = 224
D = HEADS * HEAD
deep_alpha = 6.928203230275509
norm_eps = 1e-05
far_below = -1e30
scale = HEAD ** (-0.5)

ALL = ("gy", "gx", "core", "z")
GROUP = ("gy", "gx", "core")
MESH = pl.DeviceIdType.MESH
F32 = jnp.float32
BF16 = jnp.bfloat16


def dot(left, right):
    return jnp.dot(left, right, preferred_element_type=F32)


def dot_rows(left, right):
    return lax.dot_general(left, right, (((0,), (0,)), ((), ())), preferred_element_type=F32)


def dot_cols(left, right):
    return lax.dot_general(left, right, (((1,), (1,)), ((), ())), preferred_element_type=F32)


def swap_halves(block):
    lane = lax.broadcasted_iota(jnp.int32, block.shape, 1)
    return jnp.where((lane & 32) == 0, pltpu.roll(block, 96, 1), pltpu.roll(block, 32, 1))


def seen(prefix):
    row = lax.broadcasted_iota(jnp.int32, (SEQ_LEN, SEQ_LEN), 0)
    col = lax.broadcasted_iota(jnp.int32, (SEQ_LEN, SEQ_LEN), 1)
    return (col < prefix) | (col <= row)


def softmax(queries, keys, visible):
    scores = jnp.where(visible, dot_cols(queries, keys), far_below)
    weights = jnp.exp(scores - jnp.max(scores, axis=1, keepdims=True))
    return weights / jnp.sum(weights, axis=1, keepdims=True)


def attend_kernel(prefix_ref, packed_ref, cos_ref, sin_ref, qkv_ref, context_ref):
    width = context_ref.shape[1]
    visible = seen(prefix_ref[pl.program_id(0)])
    cosine = cos_ref[0]
    sine = sin_ref[0]
    for head in range(width // HEAD):
        at = pl.ds(head * HEAD, HEAD)
        at_k = pl.ds(width + head * HEAD, HEAD)
        at_v = pl.ds(2 * width + head * HEAD, HEAD)
        raw = packed_ref[:, at]
        queries = ((raw * cosine + swap_halves(raw) * sine) * scale).astype(BF16)
        raw = packed_ref[:, at_k]
        keys = (raw * cosine + swap_halves(raw) * sine).astype(BF16)
        values = packed_ref[:, at_v].astype(BF16)
        qkv_ref[:, at] = queries
        qkv_ref[:, at_k] = keys
        qkv_ref[:, at_v] = values
        probs = softmax(queries, keys, visible).astype(BF16)
        context_ref[:, at] = dot(probs, values).astype(BF16)


def attend_back_kernel(prefix_ref, qkv_ref, d_context_ref, cos_ref, sin_ref, d_packed_ref):
    width = d_context_ref.shape[1]
    visible = seen(prefix_ref[pl.program_id(0)])
    cosine = cos_ref[0]
    sine = sin_ref[0]
    for head in range(width // HEAD):
        at = pl.ds(head * HEAD, HEAD)
        at_k = pl.ds(width + head * HEAD, HEAD)
        at_v = pl.ds(2 * width + head * HEAD, HEAD)
        queries = qkv_ref[:, at]
        keys = qkv_ref[:, at_k]
        values = qkv_ref[:, at_v]
        d_context = d_context_ref[:, at]
        probs = softmax(queries, keys, visible)
        d_packed_ref[:, at_v] = dot_rows(probs.astype(BF16), d_context).astype(BF16)
        d_probs = dot_cols(d_context, values)
        inner = jnp.sum(probs * d_probs, axis=1, keepdims=True)
        d_scores = (probs * (d_probs - inner)).astype(BF16)
        grad = dot(d_scores, keys) * scale
        d_packed_ref[:, at] = (grad * cosine - swap_halves(grad) * sine).astype(BF16)
        grad = dot_rows(d_scores, queries)
        d_packed_ref[:, at_k] = (grad * cosine - swap_halves(grad) * sine).astype(BF16)


def by_sequence(width):
    return pl.BlockSpec((SEQ_LEN, width), lambda s: (s, 0))


TABLE = pl.BlockSpec((1, SEQ_LEN, HEAD), lambda s: (s, 0, 0))
SCALARS = pl.BlockSpec(memory_space=pltpu.SMEM)
PARAMS = pltpu.CompilerParams(vmem_limit_bytes=48 * 2**20)


def attend(prefix, packed, cosine, sine):
    rows, width = packed.shape[0], packed.shape[1] // 3
    return pl.pallas_call(
        attend_kernel,
        grid=(rows // SEQ_LEN,),
        in_specs=[SCALARS, by_sequence(3 * width), TABLE, TABLE],
        out_specs=[by_sequence(3 * width), by_sequence(width)],
        out_shape=[
            jax.ShapeDtypeStruct((rows, 3 * width), BF16),
            jax.ShapeDtypeStruct((rows, width), BF16),
        ],
        compiler_params=PARAMS,
    )(prefix, packed, cosine, sine)


def attend_back(prefix, qkv, d_context, cosine, sine):
    rows, width = d_context.shape
    return pl.pallas_call(
        attend_back_kernel,
        grid=(rows // SEQ_LEN,),
        in_specs=[SCALARS, by_sequence(3 * width), by_sequence(width), TABLE, TABLE],
        out_specs=by_sequence(3 * width),
        out_shape=jax.ShapeDtypeStruct((rows, 3 * width), BF16),
        compiler_params=PARAMS,
    )(prefix, qkv, d_context, cosine, sine)


def tables(prefix, start):
    place = jnp.arange(SEQ_LEN, dtype=jnp.int32)
    in_span = place[None, :] >= prefix[:, None]
    pos_one = jnp.where(in_span, start[:, None], place[None, :])
    pos_two = jnp.where(in_span, place[None, :] - prefix[:, None] + 1, 0)
    lane = jnp.arange(HEAD)
    freqs = 10000.0 ** (-2.0 * (lane % 32).astype(F32) / 64)
    place_of = jnp.where(lane[None, None, :] < 64, pos_one[:, :, None], pos_two[:, :, None])
    angles = place_of.astype(F32) * freqs
    sign = jnp.where(lane % 64 < 32, -1.0, 1.0)
    return jnp.cos(angles), jnp.sin(angles) * sign


def norm_parts(values):
    center = values - jnp.mean(values, axis=-1, keepdims=True)
    inverse = lax.rsqrt(jnp.mean(center * center, axis=-1, keepdims=True) + norm_eps)
    return center * inverse, inverse


def norm_back(normal, inverse, gain, grad):
    scaled = gain * grad
    return inverse * (
        scaled
        - jnp.mean(scaled, axis=-1, keepdims=True)
        - normal * jnp.mean(scaled * normal, axis=-1, keepdims=True)
    )


def gate_parts(gate):
    phi = 0.5 * (1.0 + lax.erf(gate * 0.7071067811865476))
    slope = phi + gate * jnp.exp(-0.5 * gate * gate) * 0.3989422804014327
    return gate * phi, slope


def here():
    return lax.axis_index("gy"), lax.axis_index("gx"), lax.axis_index("core")


def place(y, x, c):
    return (y * 2 + x) * 2 + c


def greet(peers):
    barrier = pltpu.get_barrier_semaphore()
    for peer in peers:
        pl.semaphore_signal(barrier, inc=1, device_id=peer, device_id_type=MESH)
    pl.semaphore_wait(barrier, len(peers))


def spread_block(cut, base, block_ref, out_ref, send, recv, local):
    rows = block_ref.shape[0]
    y, x, c = here()
    to_x, to_y, to_c = {"gx": 1 - x}, {"gy": 1 - y}, {"core": 1 - c}
    me, by_x, by_y, far = place(y, x, c), place(y, 1 - x, c), place(1 - y, x, c), place(1 - y, 1 - x, c)
    low, high = pl.ds(0, cut), pl.ds(cut, rows - cut)

    def push(k, src, dst, to):
        copy = pltpu.make_async_remote_copy(
            src_ref=src, dst_ref=dst, send_sem=send.at[base + k], recv_sem=recv.at[base + k], device_id=to, device_id_type=MESH
        )
        copy.start()
        return copy

    def landed(k, dst):
        pltpu.make_async_remote_copy(
            src_ref=dst, dst_ref=dst, send_sem=send.at[base + k], recv_sem=recv.at[base + k], device_id=to_c, device_id_type=MESH
        ).wait_recv()

    sent = [
        push(0, block_ref.at[low], out_ref.at[me, low], to_x),
        push(1, block_ref.at[high], out_ref.at[me, high], to_y),
        push(2, block_ref.at[high], out_ref.at[me, high], to_x),
        push(3, block_ref.at[low], out_ref.at[me, low], to_y),
        push(4, block_ref, out_ref.at[me], to_c),
    ]
    keep = pltpu.make_async_copy(block_ref, out_ref.at[me], local)
    keep.start()
    landed(0, out_ref.at[by_x, low])
    sent.append(push(5, out_ref.at[by_x, low], out_ref.at[by_x, low], to_y))
    sent.append(push(7, out_ref.at[by_x, low], out_ref.at[by_x, low], to_c))
    landed(1, out_ref.at[by_y, high])
    sent.append(push(6, out_ref.at[by_y, high], out_ref.at[by_y, high], to_x))
    sent.append(push(8, out_ref.at[by_y, high], out_ref.at[by_y, high], to_c))
    landed(2, out_ref.at[by_x, high])
    sent.append(push(9, out_ref.at[by_x, high], out_ref.at[by_x, high], to_c))
    landed(3, out_ref.at[by_y, low])
    sent.append(push(10, out_ref.at[by_y, low], out_ref.at[by_y, low], to_c))
    landed(5, out_ref.at[far, low])
    sent.append(push(11, out_ref.at[far, low], out_ref.at[far, low], to_c))
    landed(6, out_ref.at[far, high])
    sent.append(push(12, out_ref.at[far, high], out_ref.at[far, high], to_c))
    other, other_x, other_y, other_far = (
        place(y, x, 1 - c),
        place(y, 1 - x, 1 - c),
        place(1 - y, x, 1 - c),
        place(1 - y, 1 - x, 1 - c),
    )
    landed(4, out_ref.at[other])
    landed(7, out_ref.at[other_x, low])
    landed(8, out_ref.at[other_y, high])
    landed(9, out_ref.at[other_x, high])
    landed(10, out_ref.at[other_y, low])
    landed(11, out_ref.at[other_far, low])
    landed(12, out_ref.at[other_far, high])
    keep.wait()
    for copy in sent:
        copy.wait_send()


def gather_kernel(cut, block_ref, out_ref, send, recv, local):
    y, x, c = here()
    greet([{"gx": 1 - x}, {"gy": 1 - y}, {"core": 1 - c}])
    spread_block(cut, 0, block_ref, out_ref, send, recv, local)


ANY = pl.BlockSpec(memory_space=pl.ANY)


def group_gather(block):
    rows, width = block.shape
    return pl.pallas_call(
        functools.partial(gather_kernel, rows // 2),
        out_shape=jax.ShapeDtypeStruct((8, rows, width), block.dtype),
        in_specs=[ANY],
        out_specs=ANY,
        scratch_shapes=[pltpu.SemaphoreType.DMA((13,)), pltpu.SemaphoreType.DMA((13,)), pltpu.SemaphoreType.DMA],
        compiler_params=pltpu.CompilerParams(collective_id=9, has_side_effects=True),
        cost_estimate=pl.CostEstimate(flops=0, bytes_accessed=100 * 2**20, transcendentals=0),
    )(block)


def swap_peers(zs, kinds):
    y, x, c = here()
    z = lax.axis_index("z")
    found = []
    for k in range(1, 8):
        peer = ((y + k // 4) % 2, (x + k // 2 % 2) % 2, (c + k % 2) % 2)
        found.append((place(*peer), {"gy": peer[0], "gx": peer[1], "core": peer[2]}))
    if "line" in kinds:
        found += [((z + k) % zs, {"z": (z + k) % zs}) for k in range(1, zs)]
    return found


def swap_begin(zs, kinds, blocks, outs, send, recv, local):
    copies, comes, keeps = [], [], []
    found = swap_peers(zs, kinds)
    for i, kind in enumerate(kinds):
        me = lax.axis_index("z") if kind == "line" else place(*here())
        for k, (peer, name) in enumerate(found[7:] if kind == "line" else found[:7]):
            src = blocks[i].at[peer] if kind == "swap" else blocks[i]
            landing = outs[i].at[peer]
            sems = dict(send_sem=send.at[i, k], recv_sem=recv.at[i, k], device_id=name, device_id_type=MESH)
            copies.append(pltpu.make_async_remote_copy(src_ref=src, dst_ref=outs[i].at[me], **sems))
            comes.append(pltpu.make_async_remote_copy(src_ref=landing, dst_ref=landing, **sems))
            copies[-1].start()
        own = blocks[i].at[me] if kind == "swap" else blocks[i]
        keeps.append(pltpu.make_async_copy(own, outs[i].at[me], local.at[i]))
        keeps[-1].start()

    def finish():
        for come in comes:
            come.wait_recv()
        for copy in copies:
            copy.wait_send()
        for keep in keeps:
            keep.wait()

    return finish


SWAP_LEAD = {"swap": lambda zs: (), "group": lambda zs: (8,), "line": lambda zs: (zs,)}


def swap_shapes(zs, arrays, kinds):
    return [jax.ShapeDtypeStruct(SWAP_LEAD[k](zs) + a.shape, a.dtype) for a, k in zip(arrays, kinds)]


def swap_scratch(zs, kinds):
    n, most = len(kinds), max(7, zs - 1)
    return [
        pltpu.SemaphoreType.DMA((n, most)),
        pltpu.SemaphoreType.DMA((n, most)),
        pltpu.SemaphoreType.DMA((n,)),
    ]


SLAB = 16
ROWS = pl.BlockSpec(memory_space=pltpu.VMEM)
CHIP_COLS = 256


def by_rows(value, zs, piece):
    group = D // (zs * piece)
    order = [g * zs + z for z in range(zs) for g in range(group)]
    return jnp.concatenate([value[:, m * piece : (m + 1) * piece] for m in order], axis=1)


def in_order(value, zs, piece):
    group = D // (zs * piece)
    order = [z * group + g for g in range(group) for z in range(zs)]
    return jnp.concatenate([value[:, m * piece : (m + 1) * piece] for m in order], axis=1)


def first_norm(total, x, gains):
    normal, inverse = norm_parts(deep_alpha * x + total)
    first = normal * gains[0:1] + gains[1:2]
    return first, normal, inverse


def second_norm(total, first, grad, gains):
    normal, inverse = norm_parts(deep_alpha * first + total)
    return normal * gains[2:3] + gains[3:4], norm_back(normal, inverse, gains[2:3], grad), grad * normal


def first_back(total, d_pre_two, normal, inverse, gains):
    d_first = deep_alpha * d_pre_two + total
    return norm_back(normal, inverse, gains[0:1], d_first), d_first * normal, d_first


def fold_kernel(mode, across, zs, piece, n_aux, n_out, kinds, *refs):
    left_ref, right_ref, gains_ref = refs[:3]
    aux_refs = refs[3 : 3 + n_aux]
    refs = refs[3 + n_aux :]
    n_swap = len(kinds)
    swap_in, refs = refs[:n_swap], refs[n_swap:]
    spread = mode != "last"
    if spread:
        all_ref, refs = refs[0], refs[1:]
    outs, refs = refs[:n_out], refs[n_out:]
    swap_out, refs = refs[:n_swap], refs[n_swap:]
    aux, refs = refs[:n_aux], refs[n_aux:]
    left, right, part, got, near_x, near_y, from_x, from_y, block, acc, send, recv, local = refs[:13]
    rows, width = block.shape
    cut = near_x.shape[0]
    y, x, c = here()
    to_x, to_y, to_c = {"gx": 1 - x}, {"gy": 1 - y}, {"core": 1 - c}
    chips = [(1 - y, 1 - x), (y, 1 - x), (1 - y, x), (y, x)]
    low, high = pl.ds(0, cut), pl.ds(cut, rows - cut)

    def push(k, src, dst, to):
        copy = pltpu.make_async_remote_copy(
            src_ref=src, dst_ref=dst, send_sem=send.at[k], recv_sem=recv.at[k], device_id=to, device_id_type=MESH
        )
        copy.start()
        return copy

    def add(k, extra, start, size, offset=0):
        @pl.loop(0, size // SLAB)
        def _(step):
            at = pl.ds(pl.multiple_of(start + step * SLAB, SLAB), SLAB)
            of = pl.ds(pl.multiple_of(start - offset + step * SLAB, SLAB), SLAB)
            part[k, c, at] = (part[k, c, at].astype(F32) + extra[of].astype(F32)).astype(BF16)

    loads = [pltpu.make_async_copy(left_ref.at[a * 2 + b], left.at[k], local.at[k]) for k, (a, b) in enumerate(chips)]
    load_right = pltpu.make_async_copy(right_ref, right, local.at[4])
    load_aux = [pltpu.make_async_copy(r, v, local.at[5 + k]) for k, (r, v) in enumerate(zip(aux_refs, aux))]
    loads[0].start()
    load_right.start()
    for load in loads[1:] + load_aux:
        load.start()
    if n_swap:
        greet([name for _, name in swap_peers(1, kinds)])
        swap_finish = swap_begin(1, kinds, swap_in, swap_out, *refs[13:])
    else:
        greet([to_x, to_y, to_c])

    def product(k):
        loads[k].wait()

        @pl.loop(0, width // CHIP_COLS)
        def _(step):
            at = pl.ds(pl.multiple_of(step * CHIP_COLS, CHIP_COLS), CHIP_COLS)
            here_part = dot_cols(left[k], right[at]) if across else dot(left[k], right[:, at])
            part[k, 0, :, at] = here_part[:rows].astype(BF16)
            part[k, 1, :, at] = here_part[rows:].astype(BF16)

        return push(k, part.at[k, 1 - c], got.at[k], to_c)

    load_right.wait()
    sent = [product(0), product(1)]
    sent[0].wait_recv()
    add(0, got.at[0], 0, rows)
    far_x = push(4, part.at[0, c, low], near_x, to_x)
    far_y = push(5, part.at[0, c, high], near_y, to_y)
    sent.append(product(2))
    sent[1].wait_recv()
    add(1, got.at[1], 0, rows)
    plain_x = push(6, part.at[1, c, low], from_x.at[low], to_x)
    sent[2].wait_recv()
    add(2, got.at[2], 0, rows)
    plain_y = push(7, part.at[2, c, high], from_y.at[high], to_y)
    sent.append(product(3))
    far_y.wait_recv()
    add(1, near_y, cut, rows - cut, cut)
    more_x = push(8, part.at[1, c, high], from_x.at[high], to_x)
    far_x.wait_recv()
    add(2, near_x, 0, cut)
    more_y = push(9, part.at[2, c, low], from_y.at[low], to_y)
    sent[3].wait_recv()
    for load in load_aux:
        load.wait()
    plain_x.wait_recv()
    plain_y.wait_recv()
    more_x.wait_recv()
    more_y.wait_recv()
    gains = gains_ref[...]
    acc[...] = jnp.zeros_like(acc)

    @pl.loop(0, rows // SLAB)
    def _(step):
        at = pl.ds(pl.multiple_of(step * SLAB, SLAB), SLAB)
        total = part[3, c, at].astype(F32) + got[3, at].astype(F32) + from_x[at].astype(F32) + from_y[at].astype(F32)
        held = [a[at].astype(F32) for a in aux]
        if mode == "one":
            first, normal, inverse = first_norm(by_rows(total, zs, piece), held[0], gains)
            outs[0][at] = first
            outs[1][at] = normal
            outs[2][at] = jnp.broadcast_to(inverse, (SLAB, 128))
            block[at] = first.astype(BF16)
        elif mode == "two":
            result, d_pre, terms = second_norm(total, held[0], held[1], gains)
            outs[0][at] = in_order(result, zs, piece).astype(BF16)
            outs[1][at] = d_pre
            block[at] = d_pre.astype(BF16)
            acc[0] += terms
            acc[1] += held[1]
        elif mode == "back":
            d_pre, terms, d_first = first_back(total, held[0], held[1], held[2][:, 0:1], gains)
            outs[0][at] = d_pre
            block[at] = in_order(d_pre, zs, piece).astype(BF16)
            acc[0] += terms
            acc[1] += d_first
        else:
            outs[0][at] = in_order(deep_alpha * held[0] + total, zs, piece).astype(BF16)

    if mode in ("two", "back"):
        outs[-1][0:1] = jnp.sum(acc[0], axis=0, keepdims=True)
        outs[-1][1:2] = jnp.sum(acc[1], axis=0, keepdims=True)
    for copy in sent + [far_x, far_y, plain_x, plain_y, more_x, more_y]:
        copy.wait_send()
    if n_swap:
        swap_finish()
    if spread:
        spread_block(cut, 10, block, all_ref, send, recv, local.at[4])


def group_fold(name, zs, mode, left, right, gains, aux, out_types, extras=(), kinds=()):
    across = mode != "one"
    rows, depth = left.shape[0] // 8, left.shape[1]
    width = gains.shape[1]
    cut = rows // 2
    spread = mode != "last"
    out_shape = [jax.ShapeDtypeStruct((8, rows, width), BF16)] * spread + out_types
    n, n_swap = len(aux), len(extras)
    n_sems = 23 if spread else 10
    return pl.pallas_call(
        functools.partial(fold_kernel, mode, across, zs, width // (8 * zs), n, len(out_types), kinds),
        out_shape=out_shape + swap_shapes(1, extras, kinds),
        in_specs=[ANY, ANY, ROWS] + [ANY] * (n + n_swap),
        out_specs=[ANY] * spread + [ROWS] * len(out_types) + [ANY] * n_swap,
        scratch_shapes=[pltpu.VMEM(a.shape, a.dtype) for a in aux]
        + [
            pltpu.VMEM((4, 2 * rows, depth), BF16),
            pltpu.VMEM(right.shape, BF16),
            pltpu.VMEM((4, 2, rows, width), BF16),
            pltpu.VMEM((4, rows, width), BF16),
            pltpu.VMEM((cut, width), BF16),
            pltpu.VMEM((rows - cut, width), BF16),
            pltpu.VMEM((rows, width), BF16),
            pltpu.VMEM((rows, width), BF16),
            pltpu.VMEM((rows, width), BF16),
            pltpu.VMEM((2, SLAB, width), F32),
            pltpu.SemaphoreType.DMA((n_sems,)),
            pltpu.SemaphoreType.DMA((n_sems,)),
            pltpu.SemaphoreType.DMA((5 + n,)),
        ]
        + (swap_scratch(1, kinds) if n_swap else []),
        compiler_params=pltpu.CompilerParams(
            collective_id=name, has_side_effects=True, vmem_limit_bytes=50 * 2**20
        ),
        cost_estimate=pl.CostEstimate(flops=0, bytes_accessed=(200 if spread else 110) * 2**20, transcendentals=0),
    )(left.reshape(4, 2 * rows, depth), right, gains, *aux, *extras)


def swap_kernel(zs, kinds, *refs):
    n = len(kinds)
    greet([name for _, name in swap_peers(zs, kinds)])
    swap_begin(zs, kinds, refs[:n], refs[n : 2 * n], *refs[2 * n :])()


def group_swap(name, zs, arrays, kinds):
    n = len(arrays)
    return pl.pallas_call(
        functools.partial(swap_kernel, zs, kinds),
        out_shape=swap_shapes(zs, arrays, kinds),
        in_specs=[ANY] * n,
        out_specs=[ANY] * n,
        scratch_shapes=swap_scratch(zs, kinds),
        compiler_params=pltpu.CompilerParams(collective_id=name, has_side_effects=True),
        cost_estimate=pl.CostEstimate(flops=0, bytes_accessed=50 * 2**20, transcendentals=0),
    )(*arrays)


def ff_kernel(x_ref, w_ref, hidden_ref, kept_ref):
    tile = hidden_ref.shape[1]
    projected = dot(x_ref[...], w_ref[...])
    gate, up = projected[:, :tile], projected[:, tile:]
    act, slope = gate_parts(gate)
    hidden_ref[...] = (act * up).astype(BF16)
    kept_ref[...] = jnp.concatenate([up * slope, act], axis=1).astype(BF16)


def ff_back_kernel(grad_ref, w_ref, kept_ref, out_ref):
    d_hidden = dot(grad_ref[...], w_ref[...])
    out_ref[...] = (jnp.concatenate([d_hidden, d_hidden], axis=1) * kept_ref[...].astype(F32)).astype(BF16)


FF_ROWS = 256


def ff_rows(width):
    return pl.BlockSpec((FF_ROWS, width), lambda i: (i, 0))


def ff_forward(x, w):
    rows, depth = x.shape
    wide = w.shape[1]
    return pl.pallas_call(
        ff_kernel,
        grid=(rows // FF_ROWS,),
        in_specs=[ff_rows(depth), pl.BlockSpec((depth, wide), lambda i: (0, 0))],
        out_specs=[ff_rows(wide // 2), ff_rows(wide)],
        out_shape=[jax.ShapeDtypeStruct((rows, wide // 2), BF16), jax.ShapeDtypeStruct((rows, wide), BF16)],
        compiler_params=PARAMS,
        cost_estimate=pl.CostEstimate(flops=2 * rows * depth * wide, bytes_accessed=20 * 2**20, transcendentals=0),
    )(x, w)


def ff_backward(grad, w, kept):
    rows, depth = grad.shape
    wide = kept.shape[1]
    return pl.pallas_call(
        ff_back_kernel,
        grid=(rows // FF_ROWS,),
        in_specs=[ff_rows(depth), pl.BlockSpec((depth, wide // 2), lambda i: (0, 0)), ff_rows(wide)],
        out_specs=ff_rows(wide),
        out_shape=jax.ShapeDtypeStruct((rows, wide), BF16),
        compiler_params=PARAMS,
        cost_estimate=pl.CostEstimate(flops=rows * depth * wide, bytes_accessed=20 * 2**20, transcendentals=0),
    )(grad, w, kept)


def cut_kernel(in_ref, out_ref, in_blocks, out_blocks, wide):
    group, _, double = in_blocks.shape
    tile, ff = double // 2, out_ref.shape[1]
    span = group * tile
    odd = ff % 128
    live = lax.broadcasted_iota(jnp.int32, (in_ref.shape[0], span), 1) < ff
    wide[...] = jnp.zeros_like(wide)
    wide[:, : 2 * ff] = in_ref[...].astype(F32)
    gate = jnp.where(live, wide[:, :span], 0.0)
    up = pltpu.roll(wide[:, ff - odd : ff - odd + span], span - odd, 1)
    up = jnp.where(live, up, 0.0)
    wide[:, :span] = jnp.zeros_like(live, F32)
    wide[:, :ff] = out_ref[...].astype(F32)
    down = wide[:, :span]
    for g in range(group):
        at = slice(g * tile, (g + 1) * tile)
        in_blocks[g] = jnp.concatenate([gate[:, at], up[:, at]], axis=1).astype(BF16)
        out_blocks[g] = down[:, at].astype(BF16)


def cut_ff(w_in, w_out, group, tile):
    rows, ff = w_out.shape
    return pl.pallas_call(
        cut_kernel,
        grid=(rows // 16,),
        in_specs=[pl.BlockSpec((16, 2 * ff), lambda i: (i, 0)), pl.BlockSpec((16, ff), lambda i: (i, 0))],
        out_specs=[
            pl.BlockSpec((group, 16, 2 * tile), lambda i: (0, i, 0)),
            pl.BlockSpec((group, 16, tile), lambda i: (0, i, 0)),
        ],
        out_shape=[
            jax.ShapeDtypeStruct((group, rows, 2 * tile), BF16),
            jax.ShapeDtypeStruct((group, rows, tile), BF16),
        ],
        scratch_shapes=[pltpu.VMEM((16, -(-(ff + group * tile) // 128) * 128), F32)],
        compiler_params=PARAMS,
    )(w_in, w_out)


def join_kernel(in_blocks, out_blocks, in_ref, out_ref):
    group, _, double = in_blocks.shape
    tile, ff = double // 2, out_ref.shape[1]
    odd = ff % 128
    blocks = [in_blocks[g].astype(F32) for g in range(group)]
    gate = jnp.concatenate([block[:, :tile] for block in blocks], axis=1)
    up = jnp.concatenate([block[:, tile:] for block in blocks], axis=1)
    up = pltpu.roll(up, odd, 1)
    lane = lax.broadcasted_iota(jnp.int32, (up.shape[0], 128), 1)
    in_ref[:, : ff - odd] = gate[:, : ff - odd]
    in_ref[:, ff - odd : ff - odd + 128] = jnp.where(lane < odd, gate[:, ff - odd : ff - odd + 128], up[:, :128])
    in_ref[:, ff - odd + 128 :] = up[:, 128 : ff + odd]
    down = jnp.concatenate([out_blocks[g].astype(F32) for g in range(group)], axis=1)
    out_ref[...] = down[:, :ff]


def join_ff(in_blocks, out_blocks, ff):
    group, rows, tile = out_blocks.shape
    return pl.pallas_call(
        join_kernel,
        grid=(rows // 16,),
        in_specs=[
            pl.BlockSpec((group, 16, 2 * tile), lambda i: (0, i, 0)),
            pl.BlockSpec((group, 16, tile), lambda i: (0, i, 0)),
        ],
        out_specs=[pl.BlockSpec((16, 2 * ff), lambda i: (i, 0)), pl.BlockSpec((16, ff), lambda i: (i, 0))],
        out_shape=[jax.ShapeDtypeStruct((rows, 2 * ff), F32), jax.ShapeDtypeStruct((rows, ff), F32)],
        compiler_params=PARAMS,
    )(in_blocks, out_blocks)


def closing_kernel(zs, sum_ref, rows_ref, qkv_ref, dense_ref, total_ref, got, mine, lines, *refs):
    send, recv, local, line_send, line_recv = refs
    y, x, c = here()
    z = lax.axis_index("z")
    me = place(y, x, c)
    wide = got.shape[2]
    width = wide // 3
    piece = got.shape[1]
    found = swap_peers(zs, ("line",))
    greet([name for _, name in found])
    copies, comes = [], []
    for k, (peer, name) in enumerate(found[:7]):
        sems = dict(send_sem=send.at[k], recv_sem=recv.at[k], device_id=name, device_id_type=MESH)
        src = rows_ref.at[peer, :, pl.ds(0, wide)]
        copies.append(pltpu.make_async_remote_copy(src_ref=src, dst_ref=got.at[me], **sems))
        comes.append(pltpu.make_async_remote_copy(src_ref=got.at[peer], dst_ref=got.at[peer], **sems))
    for k, (peer, name) in enumerate(found[7:]):
        sems = dict(send_sem=line_send.at[k], recv_sem=line_recv.at[k], device_id=name, device_id_type=MESH)
        copies.append(pltpu.make_async_remote_copy(src_ref=sum_ref, dst_ref=lines.at[z], **sems))
        comes.append(pltpu.make_async_remote_copy(src_ref=lines.at[peer], dst_ref=lines.at[peer], **sems))
    for copy in copies:
        copy.start()
    keeps = [
        pltpu.make_async_copy(rows_ref.at[me, :, pl.ds(0, wide)], got.at[me], local.at[0]),
        pltpu.make_async_copy(sum_ref, lines.at[z], local.at[1]),
        pltpu.make_async_copy(rows_ref.at[:, :, pl.ds(wide, width)], mine, local.at[2]),
    ]
    for keep in keeps:
        keep.start()
    keeps[2].wait()
    for at in range(0, piece, 16):
        rows = jnp.concatenate([mine[g, at : at + 16] for g in range(8)], axis=1).astype(F32)
        dense_ref[at : at + 16] = rows
    for come in comes:
        come.wait_recv()
    for keep in keeps[:2]:
        keep.wait()
    for g in range(8):
        for j in range(3):
            at = pl.ds(j * D + g * width, width)
            qkv_ref[:, at] = got[g, :, j * width : (j + 1) * width].astype(F32)
    total = lines[0]
    for k in range(1, zs):
        total += lines[k]
    part = total[:, :piece]
    for k in range(1, zs):
        part = jnp.where(z == k, total[:, k * piece : (k + 1) * piece], part)
    total_ref[...] = part
    for copy in copies:
        copy.wait_send()


def closing(zs, sums, rows):
    _, piece, columns = rows.shape
    width = columns // 4
    return pl.pallas_call(
        functools.partial(closing_kernel, zs),
        out_shape=[
            jax.ShapeDtypeStruct((piece, 3 * D), F32),
            jax.ShapeDtypeStruct((piece, D), F32),
            jax.ShapeDtypeStruct((8, piece), F32),
        ],
        in_specs=[ROWS, ANY],
        out_specs=[ROWS] * 3,
        scratch_shapes=[
            pltpu.VMEM((8, piece, 3 * width), BF16),
            pltpu.VMEM((8, piece, width), BF16),
            pltpu.VMEM((zs, 8, width), F32),
            pltpu.SemaphoreType.DMA((7,)),
            pltpu.SemaphoreType.DMA((7,)),
            pltpu.SemaphoreType.DMA((3,)),
            pltpu.SemaphoreType.DMA((zs - 1,)),
            pltpu.SemaphoreType.DMA((zs - 1,)),
        ],
        compiler_params=pltpu.CompilerParams(collective_id=5, has_side_effects=True, vmem_limit_bytes=24 * 2**20),
        cost_estimate=pl.CostEstimate(flops=0, bytes_accessed=50 * 2**20, transcendentals=0),
    )(sums, rows)


def on_device(sizes, x_in, d_out, w_qkv, w_dense, w_in, w_out, gone, bone, gtwo, btwo, flags, span_start, span_len):
    gy, gx, cores, zs = sizes
    piece = w_qkv.shape[0]
    ff = w_out.shape[1]
    group = gy * gx * cores
    width = D // group
    tile = -(-ff // (group * 64)) * 64
    own = gy == 2

    def permute(array):
        lead = array.shape[:-1]
        return jnp.swapaxes(array.reshape(lead + (group, zs, piece)), -3, -2).reshape(lead + (D,))

    def restore(array):
        lead = array.shape[:-1]
        return jnp.swapaxes(array.reshape(lead + (zs, group, piece)), -3, -2).reshape(lead + (D,))

    def swap(name, arrays, kinds):
        if own:
            return group_swap(name, zs, arrays, kinds)
        ways = {
            "swap": lambda a: lax.all_to_all(a, GROUP, 0, 0, tiled=True),
            "group": lambda a: lax.all_gather(a, GROUP, axis=0),
            "line": lambda a: lax.all_gather(a, "z", axis=0),
        }
        return [ways[k](a) for a, k in zip(arrays, kinds)]

    def spread_rows(block):
        whole = group_gather(block) if own else lax.all_gather(block, GROUP, axis=0)
        return whole.reshape(group * block.shape[0], block.shape[1])

    rows_f32 = jax.ShapeDtypeStruct((SEQ_LEN, D), F32)
    rows_low = jax.ShapeDtypeStruct((SEQ_LEN, D), BF16)
    sums_type = jax.ShapeDtypeStruct((8, D), F32)

    def fold(partial):
        return lax.psum_scatter(partial.astype(BF16), GROUP, scatter_dimension=0, tiled=True).astype(F32)

    def stack_sums(*arrays):
        return jnp.pad(jnp.stack([jnp.sum(a, axis=0) for a in arrays]), ((0, 6), (0, 0)))

    def fold_one(left, right, x, gains):
        if own:
            kinds = [rows_f32, rows_f32, jax.ShapeDtypeStruct((SEQ_LEN, 128), F32)]
            whole, first, normal, inverse = group_fold(0, zs, "one", left, right, gains, [x], kinds)
            return whole.reshape(left.shape[0], D), first, normal, inverse
        first, normal, inverse = first_norm(permute(fold(dot(left, right))), x.astype(F32), gains)
        return spread_rows(first.astype(BF16)), first, normal, inverse

    def fold_two(left, right, first, grad, gains):
        if own:
            kinds = [rows_low, rows_f32, sums_type]
            whole, result, d_pre, sums = group_fold(1, zs, "two", left, right, gains, [first, grad], kinds)
            return whole.reshape(left.shape[0], D), result, d_pre, sums
        grad = grad.astype(F32)
        result, d_pre, terms = second_norm(fold(dot_cols(left, right)), first, grad, gains)
        return spread_rows(d_pre.astype(BF16)), restore(result.astype(BF16)), d_pre, stack_sums(terms, grad)

    def fold_back(left, right, d_pre_two, normal, inverse, gains):
        if own:
            kinds = [rows_f32, sums_type]
            whole, d_pre, sums = group_fold(7, zs, "back", left, right, gains, [d_pre_two, normal, inverse], kinds)
            return whole.reshape(left.shape[0], D), d_pre, sums
        d_pre, terms, d_first = first_back(fold(dot_cols(left, right)), d_pre_two, normal, inverse, gains)
        return spread_rows(restore(d_pre).astype(BF16)), d_pre, stack_sums(terms, d_first)

    def fold_last(left, right, d_pre, gains, extras, kinds):
        if own:
            return group_fold(8, zs, "last", left, right, gains, [d_pre], [rows_low], extras, kinds)
        out = restore((deep_alpha * d_pre + fold(dot_cols(left, right))).astype(BF16))
        return [out] + swap(8, extras, kinds)

    def gather(block):
        return lax.all_gather(block, "z", axis=0, tiled=True)

    def scatter(partial):
        return lax.psum_scatter(partial.astype(BF16), "z", scatter_dimension=0, tiled=True)

    masked = jnp.max(flags) > 0
    prefix = jnp.where(masked, SEQ_LEN, SEQ_LEN - span_len[0])
    info = jnp.concatenate([gone, bone, gtwo, btwo, jnp.stack([prefix, span_start[0]]).astype(BF16)])
    info = jnp.pad(info[None, :], ((0, 15), (0, -info.shape[0] % 128)))

    qkv_blocks = jnp.moveaxis(w_qkv.reshape(piece, 3, group, width), 2, 0).reshape(group, piece, 3 * width)
    w_dense_part = gather(w_dense)
    qkv_blocks, info = swap(2, [qkv_blocks, info], ("swap", "group"))
    w_qkv_part = gather(qkv_blocks.reshape(group * piece, 3 * width))
    in_blocks, out_blocks = cut_ff(w_in, w_out, group, tile)
    in_blocks, out_blocks, qkv_blocks, w_dense_part = lax.optimization_barrier(
        (in_blocks, out_blocks, qkv_blocks, w_dense_part)
    )
    in_blocks, out_blocks, info = swap(3, [in_blocks, out_blocks, info], ("swap", "swap", "line"))
    w_in_part = gather(in_blocks.reshape(group * piece, 2 * tile))
    x_perm = permute(x_in)
    x_next, in_blocks = lax.optimization_barrier((x_perm, in_blocks))
    x_all = spread_rows(x_next)

    info = info[:, :, 0]
    place_info = info[lax.axis_index("z"), :, 4 * piece : 4 * piece + 2].astype(jnp.int32)
    prefix, start = place_info[:, 0], place_info[:, 1]
    gains = info[:, :, : 4 * piece].astype(F32).reshape(zs, group, 4, piece)
    gains = jnp.pad(jnp.transpose(gains, (2, 0, 1, 3)).reshape(4, D), ((0, 4), (0, 0)))
    cosine, sine = tables(prefix, start)
    w_qkv_part, x_all, cosine, sine, gains = lax.optimization_barrier((w_qkv_part, x_all, cosine, sine, gains))
    packed = dot(x_all, w_qkv_part)
    qkv, context = attend(prefix, packed, cosine, sine)
    first_all, first, normal_one, inverse_one = fold_one(context, w_dense_part, x_perm, gains)
    out_blocks, first_all, w_in_part = lax.optimization_barrier((out_blocks, first_all, w_in_part))
    w_out_part = gather(out_blocks.reshape(group * piece, tile))
    hidden, kept = ff_forward(first_all, w_in_part)
    d_branch, layer_out, d_pre_two, sums_two = fold_two(hidden, w_out_part, first, permute(d_out), gains)
    d_w_out = dot_rows(d_branch, hidden).astype(BF16)
    d_w_out, d_branch = lax.optimization_barrier((d_w_out, d_branch))
    d_w_out = scatter(d_w_out)
    d_projected = ff_backward(d_branch, w_out_part, kept)
    d_w_in = dot_rows(first_all, d_projected).astype(BF16)
    d_w_in, d_projected = lax.optimization_barrier((d_w_in, d_projected))
    d_w_in = scatter(d_w_in)
    d_attn, d_pre_one, sums_one = fold_back(d_projected, w_in_part, d_pre_two, normal_one, inverse_one, gains)
    d_attn, d_w_out = lax.optimization_barrier((d_attn, d_w_out))
    d_context = dot_cols(d_attn, w_dense_part).astype(BF16)
    d_packed = attend_back(prefix, qkv, d_context, cosine, sine)
    d_w_qkv = dot_rows(x_all, d_packed).astype(BF16)
    d_dense = dot_rows(context, d_attn).astype(BF16).reshape(zs, piece, group, width)
    d_dense = jnp.swapaxes(d_dense, 1, 2).reshape(D, width)
    d_w_qkv = jnp.concatenate([d_w_qkv, d_dense], axis=1)
    sums = jnp.concatenate([sums_one[:2], sums_two[:2], jnp.zeros((4, D), F32)])
    d_packed, d_w_qkv, d_w_in, sums = lax.optimization_barrier((d_packed, d_w_qkv, d_w_in, sums))
    d_w_qkv = scatter(d_w_qkv)
    d_w_in, d_w_out = d_w_in.reshape(group, piece, 2 * tile), d_w_out.reshape(group, piece, tile)
    d_input, d_w_in, d_w_out, sums = fold_last(
        d_packed, w_qkv_part, d_pre_one, gains, [d_w_in, d_w_out, sums], ("swap", "swap", "group")
    )
    sums = jnp.sum(sums, axis=0).reshape(8, zs, group, piece)
    sums = lax.dynamic_index_in_dim(sums, lax.axis_index(GROUP), 2, keepdims=False).reshape(8, width)
    out_in, out_out = join_ff(d_w_in, d_w_out, ff)
    out_in, out_out, d_input, d_w_qkv, sums = lax.optimization_barrier((out_in, out_out, d_input, d_w_qkv, sums))
    if own:
        out_qkv, out_dense, sums = closing(zs, sums, d_w_qkv.reshape(group, piece, 4 * width))
    else:
        out_dense = d_w_qkv[:, 3 * width :].reshape(group, piece, width)
        out_dense = jnp.swapaxes(out_dense, 0, 1).reshape(piece, D).astype(F32)
        d_w_qkv = d_w_qkv[:, : 3 * width].reshape(group, piece, 3 * width)
        d_w_qkv, sums = swap(5, [d_w_qkv, sums], ("swap", "line"))
        out_qkv = jnp.transpose(d_w_qkv.astype(F32).reshape(group, piece, 3, width), (1, 2, 0, 3))
        out_qkv = out_qkv.reshape(piece, 3 * D)
        sums = jnp.sum(sums, axis=0).reshape(8, zs, piece)
        sums = lax.dynamic_index_in_dim(sums, lax.axis_index("z"), 1, keepdims=False)
    return layer_out, d_input, out_qkv, out_dense, out_in, out_out, sums[0], sums[1], sums[2], sums[3]


def solution(mesh):
    grp, shard = mesh.shape["grp"], mesh.shape["shard"]
    sizes = (grp // 4, 2, 2, shard)
    inner = Mesh(mesh.devices.reshape(sizes), ALL)
    rows, flat = P(ALL, None), P(ALL)
    return jax.shard_map(
        functools.partial(on_device, sizes),
        mesh=inner,
        in_specs=(rows,) * 6 + (flat,) * 7,
        out_specs=(rows,) * 6 + (flat,) * 4,
        check_vma=False,
    )
```

```python
import functools

import jax
import jax.numpy as jnp
from jax import lax
from jax.experimental import pallas as pl
from jax.experimental.pallas import tpu as pltpu
from jax.sharding import Mesh
from jax.sharding import PartitionSpec as P

HEADS = 16
HEAD = 128
SEQ_LEN = 224
D = HEADS * HEAD
deep_alpha = 6.928203230275509
norm_eps = 1e-05
far_below = -1e30
scale = HEAD ** (-0.5)

ALL = ("gy", "gx", "core", "z")
GROUP = ("gy", "gx", "core")
MESH = pl.DeviceIdType.MESH
F32 = jnp.float32
BF16 = jnp.bfloat16


def dot(left, right):
    return jnp.dot(left, right, preferred_element_type=F32)


def dot_rows(left, right):
    return lax.dot_general(left, right, (((0,), (0,)), ((), ())), preferred_element_type=F32)


def dot_cols(left, right):
    return lax.dot_general(left, right, (((1,), (1,)), ((), ())), preferred_element_type=F32)


def swap_halves(block):
    lane = lax.broadcasted_iota(jnp.int32, block.shape, 1)
    return jnp.where((lane & 32) == 0, pltpu.roll(block, 96, 1), pltpu.roll(block, 32, 1))


def seen(prefix):
    row = lax.broadcasted_iota(jnp.int32, (SEQ_LEN, SEQ_LEN), 0)
    col = lax.broadcasted_iota(jnp.int32, (SEQ_LEN, SEQ_LEN), 1)
    return (col < prefix) | (col <= row)


def softmax(queries, keys, visible):
    scores = jnp.where(visible, dot_cols(queries, keys), far_below)
    weights = jnp.exp(scores - jnp.max(scores, axis=1, keepdims=True))
    return weights / jnp.sum(weights, axis=1, keepdims=True)


def attend_kernel(prefix_ref, packed_ref, cos_ref, sin_ref, qkv_ref, context_ref):
    width = context_ref.shape[1]
    visible = seen(prefix_ref[pl.program_id(0)])
    cosine = cos_ref[0]
    sine = sin_ref[0]
    for head in range(width // HEAD):
        at = pl.ds(head * HEAD, HEAD)
        at_k = pl.ds(width + head * HEAD, HEAD)
        at_v = pl.ds(2 * width + head * HEAD, HEAD)
        raw = packed_ref[:, at]
        queries = ((raw * cosine + swap_halves(raw) * sine) * scale).astype(BF16)
        raw = packed_ref[:, at_k]
        keys = (raw * cosine + swap_halves(raw) * sine).astype(BF16)
        values = packed_ref[:, at_v].astype(BF16)
        qkv_ref[:, at] = queries
        qkv_ref[:, at_k] = keys
        qkv_ref[:, at_v] = values
        probs = softmax(queries, keys, visible).astype(BF16)
        context_ref[:, at] = dot(probs, values).astype(BF16)


def attend_back_kernel(prefix_ref, qkv_ref, d_context_ref, cos_ref, sin_ref, d_packed_ref):
    width = d_context_ref.shape[1]
    visible = seen(prefix_ref[pl.program_id(0)])
    cosine = cos_ref[0]
    sine = sin_ref[0]
    for head in range(width // HEAD):
        at = pl.ds(head * HEAD, HEAD)
        at_k = pl.ds(width + head * HEAD, HEAD)
        at_v = pl.ds(2 * width + head * HEAD, HEAD)
        queries = qkv_ref[:, at]
        keys = qkv_ref[:, at_k]
        values = qkv_ref[:, at_v]
        d_context = d_context_ref[:, at]
        probs = softmax(queries, keys, visible)
        d_packed_ref[:, at_v] = dot_rows(probs.astype(BF16), d_context).astype(BF16)
        d_probs = dot_cols(d_context, values)
        inner = jnp.sum(probs * d_probs, axis=1, keepdims=True)
        d_scores = (probs * (d_probs - inner)).astype(BF16)
        grad = dot(d_scores, keys) * scale
        d_packed_ref[:, at] = (grad * cosine - swap_halves(grad) * sine).astype(BF16)
        grad = dot_rows(d_scores, queries)
        d_packed_ref[:, at_k] = (grad * cosine - swap_halves(grad) * sine).astype(BF16)


def by_sequence(width):
    return pl.BlockSpec((SEQ_LEN, width), lambda s: (s, 0))


TABLE = pl.BlockSpec((1, SEQ_LEN, HEAD), lambda s: (s, 0, 0))
SCALARS = pl.BlockSpec(memory_space=pltpu.SMEM)
PARAMS = pltpu.CompilerParams(vmem_limit_bytes=48 * 2**20)


def attend(prefix, packed, cosine, sine):
    rows, width = packed.shape[0], packed.shape[1] // 3
    return pl.pallas_call(
        attend_kernel,
        grid=(rows // SEQ_LEN,),
        in_specs=[SCALARS, by_sequence(3 * width), TABLE, TABLE],
        out_specs=[by_sequence(3 * width), by_sequence(width)],
        out_shape=[
            jax.ShapeDtypeStruct((rows, 3 * width), BF16),
            jax.ShapeDtypeStruct((rows, width), BF16),
        ],
        compiler_params=PARAMS,
    )(prefix, packed, cosine, sine)


def attend_back(prefix, qkv, d_context, cosine, sine):
    rows, width = d_context.shape
    return pl.pallas_call(
        attend_back_kernel,
        grid=(rows // SEQ_LEN,),
        in_specs=[SCALARS, by_sequence(3 * width), by_sequence(width), TABLE, TABLE],
        out_specs=by_sequence(3 * width),
        out_shape=jax.ShapeDtypeStruct((rows, 3 * width), BF16),
        compiler_params=PARAMS,
    )(prefix, qkv, d_context, cosine, sine)


def tables(prefix, start):
    place = jnp.arange(SEQ_LEN, dtype=jnp.int32)
    in_span = place[None, :] >= prefix[:, None]
    pos_one = jnp.where(in_span, start[:, None], place[None, :])
    pos_two = jnp.where(in_span, place[None, :] - prefix[:, None] + 1, 0)
    lane = jnp.arange(HEAD)
    freqs = 10000.0 ** (-2.0 * (lane % 32).astype(F32) / 64)
    place_of = jnp.where(lane[None, None, :] < 64, pos_one[:, :, None], pos_two[:, :, None])
    angles = place_of.astype(F32) * freqs
    sign = jnp.where(lane % 64 < 32, -1.0, 1.0)
    return jnp.cos(angles), jnp.sin(angles) * sign


def norm_parts(values):
    center = values - jnp.mean(values, axis=-1, keepdims=True)
    inverse = lax.rsqrt(jnp.mean(center * center, axis=-1, keepdims=True) + norm_eps)
    return center * inverse, inverse


def norm_back(normal, inverse, gain, grad):
    scaled = gain * grad
    return inverse * (
        scaled
        - jnp.mean(scaled, axis=-1, keepdims=True)
        - normal * jnp.mean(scaled * normal, axis=-1, keepdims=True)
    )


def gate_parts(gate):
    phi = 0.5 * (1.0 + lax.erf(gate * 0.7071067811865476))
    slope = phi + gate * jnp.exp(-0.5 * gate * gate) * 0.3989422804014327
    return gate * phi, slope


def here():
    return lax.axis_index("gy"), lax.axis_index("gx"), lax.axis_index("core")


def place(y, x, c):
    return (y * 2 + x) * 2 + c


def greet(peers):
    barrier = pltpu.get_barrier_semaphore()
    for peer in peers:
        pl.semaphore_signal(barrier, inc=1, device_id=peer, device_id_type=MESH)
    pl.semaphore_wait(barrier, len(peers))


def spread_block(cut, base, block_ref, out_ref, send, recv, local):
    rows = block_ref.shape[0]
    y, x, c = here()
    to_x, to_y, to_c = {"gx": 1 - x}, {"gy": 1 - y}, {"core": 1 - c}
    me, by_x, by_y, far = place(y, x, c), place(y, 1 - x, c), place(1 - y, x, c), place(1 - y, 1 - x, c)
    low, high = pl.ds(0, cut), pl.ds(cut, rows - cut)

    def push(k, src, dst, to):
        copy = pltpu.make_async_remote_copy(
            src_ref=src, dst_ref=dst, send_sem=send.at[base + k], recv_sem=recv.at[base + k], device_id=to, device_id_type=MESH
        )
        copy.start()
        return copy

    def landed(k, dst):
        pltpu.make_async_remote_copy(
            src_ref=dst, dst_ref=dst, send_sem=send.at[base + k], recv_sem=recv.at[base + k], device_id=to_c, device_id_type=MESH
        ).wait_recv()

    sent = [
        push(0, block_ref.at[low], out_ref.at[me, low], to_x),
        push(1, block_ref.at[high], out_ref.at[me, high], to_y),
        push(2, block_ref.at[high], out_ref.at[me, high], to_x),
        push(3, block_ref.at[low], out_ref.at[me, low], to_y),
        push(4, block_ref, out_ref.at[me], to_c),
    ]
    keep = pltpu.make_async_copy(block_ref, out_ref.at[me], local)
    keep.start()
    landed(0, out_ref.at[by_x, low])
    sent.append(push(5, out_ref.at[by_x, low], out_ref.at[by_x, low], to_y))
    sent.append(push(7, out_ref.at[by_x, low], out_ref.at[by_x, low], to_c))
    landed(1, out_ref.at[by_y, high])
    sent.append(push(6, out_ref.at[by_y, high], out_ref.at[by_y, high], to_x))
    sent.append(push(8, out_ref.at[by_y, high], out_ref.at[by_y, high], to_c))
    landed(2, out_ref.at[by_x, high])
    sent.append(push(9, out_ref.at[by_x, high], out_ref.at[by_x, high], to_c))
    landed(3, out_ref.at[by_y, low])
    sent.append(push(10, out_ref.at[by_y, low], out_ref.at[by_y, low], to_c))
    landed(5, out_ref.at[far, low])
    sent.append(push(11, out_ref.at[far, low], out_ref.at[far, low], to_c))
    landed(6, out_ref.at[far, high])
    sent.append(push(12, out_ref.at[far, high], out_ref.at[far, high], to_c))
    other, other_x, other_y, other_far = (
        place(y, x, 1 - c),
        place(y, 1 - x, 1 - c),
        place(1 - y, x, 1 - c),
        place(1 - y, 1 - x, 1 - c),
    )
    landed(4, out_ref.at[other])
    landed(7, out_ref.at[other_x, low])
    landed(8, out_ref.at[other_y, high])
    landed(9, out_ref.at[other_x, high])
    landed(10, out_ref.at[other_y, low])
    landed(11, out_ref.at[other_far, low])
    landed(12, out_ref.at[other_far, high])
    keep.wait()
    for copy in sent:
        copy.wait_send()


def gather_kernel(cut, block_ref, out_ref, send, recv, local):
    y, x, c = here()
    greet([{"gx": 1 - x}, {"gy": 1 - y}, {"core": 1 - c}])
    spread_block(cut, 0, block_ref, out_ref, send, recv, local)


ANY = pl.BlockSpec(memory_space=pl.ANY)


def group_gather(block):
    rows, width = block.shape
    return pl.pallas_call(
        functools.partial(gather_kernel, rows // 2),
        out_shape=jax.ShapeDtypeStruct((8, rows, width), block.dtype),
        in_specs=[ANY],
        out_specs=ANY,
        scratch_shapes=[pltpu.SemaphoreType.DMA((13,)), pltpu.SemaphoreType.DMA((13,)), pltpu.SemaphoreType.DMA],
        compiler_params=pltpu.CompilerParams(collective_id=9, has_side_effects=True),
        cost_estimate=pl.CostEstimate(flops=0, bytes_accessed=100 * 2**20, transcendentals=0),
    )(block)


def swap_peers(zs, kinds):
    y, x, c = here()
    z = lax.axis_index("z")
    found = []
    for k in range(1, 8):
        peer = ((y + k // 4) % 2, (x + k // 2 % 2) % 2, (c + k % 2) % 2)
        found.append((place(*peer), {"gy": peer[0], "gx": peer[1], "core": peer[2]}))
    if "line" in kinds:
        found += [((z + k) % zs, {"z": (z + k) % zs}) for k in range(1, zs)]
    return found


def swap_begin(zs, kinds, blocks, outs, send, recv, local):
    copies, comes, keeps = [], [], []
    found = swap_peers(zs, kinds)
    for i, kind in enumerate(kinds):
        me = lax.axis_index("z") if kind == "line" else place(*here())
        for k, (peer, name) in enumerate(found[7:] if kind == "line" else found[:7]):
            src = blocks[i].at[peer] if kind == "swap" else blocks[i]
            landing = outs[i].at[peer]
            sems = dict(send_sem=send.at[i, k], recv_sem=recv.at[i, k], device_id=name, device_id_type=MESH)
            copies.append(pltpu.make_async_remote_copy(src_ref=src, dst_ref=outs[i].at[me], **sems))
            comes.append(pltpu.make_async_remote_copy(src_ref=landing, dst_ref=landing, **sems))
            copies[-1].start()
        own = blocks[i].at[me] if kind == "swap" else blocks[i]
        keeps.append(pltpu.make_async_copy(own, outs[i].at[me], local.at[i]))
        keeps[-1].start()

    def finish():
        for come in comes:
            come.wait_recv()
        for copy in copies:
            copy.wait_send()
        for keep in keeps:
            keep.wait()

    return finish


SWAP_LEAD = {"swap": lambda zs: (), "group": lambda zs: (8,), "line": lambda zs: (zs,)}


def swap_shapes(zs, arrays, kinds):
    return [jax.ShapeDtypeStruct(SWAP_LEAD[k](zs) + a.shape, a.dtype) for a, k in zip(arrays, kinds)]


def swap_scratch(zs, kinds):
    n, most = len(kinds), max(7, zs - 1)
    return [
        pltpu.SemaphoreType.DMA((n, most)),
        pltpu.SemaphoreType.DMA((n, most)),
        pltpu.SemaphoreType.DMA((n,)),
    ]


SLAB = 16
ROWS = pl.BlockSpec(memory_space=pltpu.VMEM)
CHIP_COLS = 256


def by_rows(value, zs, piece):
    group = D // (zs * piece)
    order = [g * zs + z for z in range(zs) for g in range(group)]
    return jnp.concatenate([value[:, m * piece : (m + 1) * piece] for m in order], axis=1)


def in_order(value, zs, piece):
    group = D // (zs * piece)
    order = [z * group + g for g in range(group) for z in range(zs)]
    return jnp.concatenate([value[:, m * piece : (m + 1) * piece] for m in order], axis=1)


def first_norm(total, x, gains):
    normal, inverse = norm_parts(deep_alpha * x + total)
    first = normal * gains[0:1] + gains[1:2]
    return first, normal, inverse


def second_norm(total, first, grad, gains):
    normal, inverse = norm_parts(deep_alpha * first + total)
    return normal * gains[2:3] + gains[3:4], norm_back(normal, inverse, gains[2:3], grad), grad * normal


def first_back(total, d_pre_two, normal, inverse, gains):
    d_first = deep_alpha * d_pre_two + total
    return norm_back(normal, inverse, gains[0:1], d_first), d_first * normal, d_first


def fold_kernel(mode, across, zs, piece, n_aux, n_out, kinds, *refs):
    left_ref, right_ref, gains_ref = refs[:3]
    aux_refs = refs[3 : 3 + n_aux]
    refs = refs[3 + n_aux :]
    n_swap = len(kinds)
    swap_in, refs = refs[:n_swap], refs[n_swap:]
    spread = mode != "last"
    if spread:
        all_ref, refs = refs[0], refs[1:]
    outs, refs = refs[:n_out], refs[n_out:]
    swap_out, refs = refs[:n_swap], refs[n_swap:]
    aux, refs = refs[:n_aux], refs[n_aux:]
    left, right, part, got, near_x, near_y, from_x, from_y, block, acc, send, recv, local = refs[:13]
    rows, width = block.shape
    cut = near_x.shape[0]
    y, x, c = here()
    to_x, to_y, to_c = {"gx": 1 - x}, {"gy": 1 - y}, {"core": 1 - c}
    chips = [(1 - y, 1 - x), (y, 1 - x), (1 - y, x), (y, x)]
    low, high = pl.ds(0, cut), pl.ds(cut, rows - cut)

    def push(k, src, dst, to):
        copy = pltpu.make_async_remote_copy(
            src_ref=src, dst_ref=dst, send_sem=send.at[k], recv_sem=recv.at[k], device_id=to, device_id_type=MESH
        )
        copy.start()
        return copy

    def add(k, extra, start, size, offset=0):
        @pl.loop(0, size // SLAB)
        def _(step):
            at = pl.ds(pl.multiple_of(start + step * SLAB, SLAB), SLAB)
            of = pl.ds(pl.multiple_of(start - offset + step * SLAB, SLAB), SLAB)
            part[k, c, at] = (part[k, c, at].astype(F32) + extra[of].astype(F32)).astype(BF16)

    loads = [pltpu.make_async_copy(left_ref.at[a * 2 + b], left.at[k], local.at[k]) for k, (a, b) in enumerate(chips)]
    load_right = pltpu.make_async_copy(right_ref, right, local.at[4])
    load_aux = [pltpu.make_async_copy(r, v, local.at[5 + k]) for k, (r, v) in enumerate(zip(aux_refs, aux))]
    loads[0].start()
    load_right.start()
    for load in loads[1:] + load_aux:
        load.start()
    if n_swap:
        greet([name for _, name in swap_peers(1, kinds)])
        swap_finish = swap_begin(1, kinds, swap_in, swap_out, *refs[13:])
    else:
        greet([to_x, to_y, to_c])

    def product(k):
        loads[k].wait()

        @pl.loop(0, width // CHIP_COLS)
        def _(step):
            at = pl.ds(pl.multiple_of(step * CHIP_COLS, CHIP_COLS), CHIP_COLS)
            here_part = dot_cols(left[k], right[at]) if across else dot(left[k], right[:, at])
            part[k, 0, :, at] = here_part[:rows].astype(BF16)
            part[k, 1, :, at] = here_part[rows:].astype(BF16)

        return push(k, part.at[k, 1 - c], got.at[k], to_c)

    load_right.wait()
    sent = [product(0), product(1)]
    sent[0].wait_recv()
    add(0, got.at[0], 0, rows)
    far_x = push(4, part.at[0, c, low], near_x, to_x)
    far_y = push(5, part.at[0, c, high], near_y, to_y)
    sent.append(product(2))
    sent[1].wait_recv()
    add(1, got.at[1], 0, rows)
    plain_x = push(6, part.at[1, c, low], from_x.at[low], to_x)
    sent[2].wait_recv()
    add(2, got.at[2], 0, rows)
    plain_y = push(7, part.at[2, c, high], from_y.at[high], to_y)
    sent.append(product(3))
    far_y.wait_recv()
    add(1, near_y, cut, rows - cut, cut)
    more_x = push(8, part.at[1, c, high], from_x.at[high], to_x)
    far_x.wait_recv()
    add(2, near_x, 0, cut)
    more_y = push(9, part.at[2, c, low], from_y.at[low], to_y)
    sent[3].wait_recv()
    for load in load_aux:
        load.wait()
    plain_x.wait_recv()
    plain_y.wait_recv()
    more_x.wait_recv()
    more_y.wait_recv()
    gains = gains_ref[...]
    acc[...] = jnp.zeros_like(acc)

    @pl.loop(0, rows // SLAB)
    def _(step):
        at = pl.ds(pl.multiple_of(step * SLAB, SLAB), SLAB)
        total = part[3, c, at].astype(F32) + got[3, at].astype(F32) + from_x[at].astype(F32) + from_y[at].astype(F32)
        held = [a[at].astype(F32) for a in aux]
        if mode == "one":
            first, normal, inverse = first_norm(by_rows(total, zs, piece), held[0], gains)
            outs[0][at] = first
            outs[1][at] = normal
            outs[2][at] = jnp.broadcast_to(inverse, (SLAB, 128))
            block[at] = first.astype(BF16)
        elif mode == "back":
            d_pre, terms, d_first = first_back(total, held[0], held[1], held[2][:, 0:1], gains)
            outs[0][at] = d_pre
            block[at] = in_order(d_pre, zs, piece).astype(BF16)
            acc[0] += terms
            acc[1] += d_first
        else:
            outs[0][at] = in_order(deep_alpha * held[0] + total, zs, piece).astype(BF16)

    if mode == "back":
        outs[-1][0:1] = jnp.sum(acc[0], axis=0, keepdims=True)
        outs[-1][1:2] = jnp.sum(acc[1], axis=0, keepdims=True)
    for copy in sent + [far_x, far_y, plain_x, plain_y, more_x, more_y]:
        copy.wait_send()
    if n_swap:
        swap_finish()
    if spread:
        spread_block(cut, 10, block, all_ref, send, recv, local.at[4])


def group_fold(name, zs, mode, left, right, gains, aux, out_types, extras=(), kinds=()):
    across = mode != "one"
    rows, depth = left.shape[0] // 8, left.shape[1]
    width = gains.shape[1]
    cut = rows // 2
    spread = mode != "last"
    out_shape = [jax.ShapeDtypeStruct((8, rows, width), BF16)] * spread + out_types
    n, n_swap = len(aux), len(extras)
    n_sems = 23 if spread else 10
    return pl.pallas_call(
        functools.partial(fold_kernel, mode, across, zs, width // (8 * zs), n, len(out_types), kinds),
        out_shape=out_shape + swap_shapes(1, extras, kinds),
        in_specs=[ANY, ANY, ROWS] + [ANY] * (n + n_swap),
        out_specs=[ANY] * spread + [ROWS] * len(out_types) + [ANY] * n_swap,
        scratch_shapes=[pltpu.VMEM(a.shape, a.dtype) for a in aux]
        + [
            pltpu.VMEM((4, 2 * rows, depth), BF16),
            pltpu.VMEM(right.shape, BF16),
            pltpu.VMEM((4, 2, rows, width), BF16),
            pltpu.VMEM((4, rows, width), BF16),
            pltpu.VMEM((cut, width), BF16),
            pltpu.VMEM((rows - cut, width), BF16),
            pltpu.VMEM((rows, width), BF16),
            pltpu.VMEM((rows, width), BF16),
            pltpu.VMEM((rows, width), BF16),
            pltpu.VMEM((2, SLAB, width), F32),
            pltpu.SemaphoreType.DMA((n_sems,)),
            pltpu.SemaphoreType.DMA((n_sems,)),
            pltpu.SemaphoreType.DMA((5 + n,)),
        ]
        + (swap_scratch(1, kinds) if n_swap else []),
        compiler_params=pltpu.CompilerParams(
            collective_id=name, has_side_effects=True, vmem_limit_bytes=50 * 2**20
        ),
        cost_estimate=pl.CostEstimate(flops=0, bytes_accessed=(200 if spread else 110) * 2**20, transcendentals=0),
    )(left.reshape(4, 2 * rows, depth), right, gains, *aux, *extras)


def turn_kernel(
    zs, piece, left_ref, right_ref, gains_ref, first_ref, grad_ref, all_ref, result_ref, d_pre_ref, sums_ref, dw_ref,
    first, grad, left, right, part, got, near_x, near_y, from_x, from_y, whole, dw, acc, send, recv, local
):
    rows = first.shape[0]
    y, x, c = here()
    to_x, to_y, to_c = {"gx": 1 - x}, {"gy": 1 - y}, {"core": 1 - c}
    chips = [(1 - y, 1 - x), (y, 1 - x), (1 - y, x), (y, x)]
    me, by_x, by_y, far = place(y, x, c), place(y, 1 - x, c), place(1 - y, x, c), place(1 - y, 1 - x, c)
    other, other_x, other_y, other_far = (
        place(y, x, 1 - c),
        place(y, 1 - x, 1 - c),
        place(1 - y, x, 1 - c),
        place(1 - y, 1 - x, 1 - c),
    )
    half = rows // 2
    most = -(-half // (2 * SLAB)) * SLAB
    lows = [(0, most), (half, half - most)]
    highs = [(most, half - most), (2 * half - most, most)]
    near_low, near_high = [0, most], [0, half - most]
    sent = []

    def push(k, src, dst, to):
        copy = pltpu.make_async_remote_copy(
            src_ref=src, dst_ref=dst, send_sem=send.at[k], recv_sem=recv.at[k], device_id=to, device_id_type=MESH
        )
        copy.start()
        sent.append(copy)

    def landed(k, dst):
        pltpu.make_async_remote_copy(
            src_ref=dst, dst_ref=dst, send_sem=send.at[k], recv_sem=recv.at[k], device_id=to_c, device_id_type=MESH
        ).wait_recv()

    def add(k, extra, start, size, offset=0):
        @pl.loop(0, size // SLAB)
        def _(step):
            at = pl.ds(pl.multiple_of(start + step * SLAB, SLAB), SLAB)
            of = pl.ds(pl.multiple_of(start - offset + step * SLAB, SLAB), SLAB)
            part[k, c, at] = (part[k, c, at].astype(F32) + extra[of].astype(F32)).astype(BF16)

    loads = [pltpu.make_async_copy(left_ref.at[a * 2 + b], left.at[k], local.at[k]) for k, (a, b) in enumerate(chips)]
    load_right = pltpu.make_async_copy(right_ref, right, local.at[4])
    load_first = pltpu.make_async_copy(first_ref, first, local.at[5])
    load_grad = pltpu.make_async_copy(grad_ref, grad, local.at[6])
    loads[0].start()
    load_right.start()
    for load in loads[1:] + [load_first, load_grad]:
        load.start()
    greet([to_x, to_y, to_c])

    def span(i):
        return pl.ds(i * half, half)

    def product(k):
        loads[k].wait()

        @pl.loop(0, zs)
        def _(z):
            wide = right.shape[2]
            at = pl.ds(pl.multiple_of(z * wide, wide), wide)
            found = dot(left[k], right[z])
            part[k, 0, :, at] = found[:rows].astype(BF16)
            part[k, 1, :, at] = found[rows:].astype(BF16)

        for i in (0, 1):
            push(10 * i + k, part.at[k, 1 - c, span(i)], got.at[k, span(i)], to_c)

    def chip_sum(i, k):
        landed(10 * i + k, got.at[k, span(i)])
        add(k, got.at[k], i * half, half)

    def low(i):
        return pl.ds(*lows[i])

    def high(i):
        return pl.ds(*highs[i])

    def near(i):
        return near_x.at[pl.ds(near_low[i], lows[i][1])], near_y.at[pl.ds(near_high[i], highs[i][1])]

    def fold_far(i):
        chip_sum(i, 0)
        push(10 * i + 4, part.at[0, c, low(i)], near(i)[0], to_x)
        push(10 * i + 5, part.at[0, c, high(i)], near(i)[1], to_y)

    def fold_plain(i, k):
        chip_sum(i, k)
        if k == 1:
            push(10 * i + 6, part.at[1, c, low(i)], from_x.at[low(i)], to_x)
        else:
            push(10 * i + 7, part.at[2, c, high(i)], from_y.at[high(i)], to_y)

    def fold_more(i):
        landed(10 * i + 5, near(i)[1])
        add(1, near_y, *highs[i], highs[i][0] - near_high[i])
        push(10 * i + 8, part.at[1, c, high(i)], from_x.at[high(i)], to_x)
        landed(10 * i + 4, near(i)[0])
        add(2, near_x, *lows[i], lows[i][0] - near_low[i])
        push(10 * i + 9, part.at[2, c, low(i)], from_y.at[low(i)], to_y)

    gains = gains_ref[...]

    def norm(i):
        landed(10 * i + 3, got.at[3, span(i)])
        landed(10 * i + 6, from_x.at[low(i)])
        landed(10 * i + 7, from_y.at[high(i)])
        landed(10 * i + 8, from_x.at[high(i)])
        landed(10 * i + 9, from_y.at[low(i)])

        @pl.loop(0, half // SLAB)
        def _(step):
            at = pl.ds(pl.multiple_of(i * half + step * SLAB, SLAB), SLAB)
            total = part[3, c, at].astype(F32) + got[3, at].astype(F32)
            total += from_x[at].astype(F32) + from_y[at].astype(F32)
            dy = grad[at].astype(F32)
            result, d_pre, terms = second_norm(total, first[at], dy, gains)
            result_ref[at] = in_order(result, zs, piece).astype(BF16)
            d_pre_ref[at] = d_pre
            whole[me, at] = d_pre.astype(BF16)
            acc[0] += terms
            acc[1] += dy

        b = 20 + 13 * i
        push(b, whole.at[me, low(i)], whole.at[me, low(i)], to_x)
        push(b + 1, whole.at[me, high(i)], whole.at[me, high(i)], to_y)
        push(b + 2, whole.at[me, high(i)], whole.at[me, high(i)], to_x)
        push(b + 3, whole.at[me, low(i)], whole.at[me, low(i)], to_y)
        push(b + 4, whole.at[me, span(i)], whole.at[me, span(i)], to_c)

    def pass_on(i, k, slot, at, onward):
        b = 20 + 13 * i
        ref = whole.at[slot, at]
        landed(b + k, ref)
        for where, to in onward:
            push(b + where, ref, ref, to)

    def spread_first(i):
        pass_on(i, 0, by_x, low(i), [(5, to_y), (7, to_c)])
        pass_on(i, 1, by_y, high(i), [(6, to_x), (8, to_c)])

    def spread_rest(i):
        pass_on(i, 2, by_x, high(i), [(9, to_c)])
        pass_on(i, 3, by_y, low(i), [(10, to_c)])

    def spread_far(i):
        pass_on(i, 5, far, low(i), [(11, to_c)])
        pass_on(i, 6, far, high(i), [(12, to_c)])

    outward = []

    def gradient(k, last=False, first_one=False):
        a, b = chips[k]
        slot = (a * 2 + b) * 2
        pair = pl.ds(slot, 2)
        outward.append(pltpu.make_async_copy(whole.at[pair], all_ref.at[pair], local.at[7 + k]))
        outward[-1].start()

        @pl.loop(0, zs)
        def _(z):
            wide = right.shape[2]
            at = pl.ds(pl.multiple_of(z * wide, wide), wide)
            found = dot_rows(left[k], whole[pair, :, at].reshape(2 * rows, wide))
            if first_one:
                dw[z] = found
            elif last:
                dw_ref[z] = (dw[z] + found).astype(BF16)
            else:
                dw[z] += found

    load_right.wait()
    product(0)
    product(1)
    fold_far(0)
    fold_far(1)
    product(2)
    fold_plain(0, 1)
    fold_plain(0, 2)
    fold_more(0)
    product(3)
    fold_plain(1, 1)
    fold_plain(1, 2)
    fold_more(1)
    load_first.wait()
    load_grad.wait()
    acc[...] = jnp.zeros_like(acc)
    norm(0)
    norm(1)
    spread_first(0)
    for i in (0, 1):
        landed(20 + 13 * i + 4, whole.at[other, span(i)])
    gradient(3, first_one=True)
    spread_rest(0)
    spread_first(1)
    spread_rest(1)
    for i in (0, 1):
        landed(20 + 13 * i + 7, whole.at[other_x, low(i)])
        landed(20 + 13 * i + 9, whole.at[other_x, high(i)])
    gradient(1)
    spread_far(0)
    for i in (0, 1):
        landed(20 + 13 * i + 8, whole.at[other_y, high(i)])
        landed(20 + 13 * i + 10, whole.at[other_y, low(i)])
    gradient(2)
    sums_ref[0:1] = jnp.sum(acc[0], axis=0, keepdims=True)
    sums_ref[1:2] = jnp.sum(acc[1], axis=0, keepdims=True)
    spread_far(1)
    for i in (0, 1):
        landed(20 + 13 * i + 11, whole.at[other_far, low(i)])
        landed(20 + 13 * i + 12, whole.at[other_far, high(i)])
    gradient(0, last=True)
    for copy in outward:
        copy.wait()
    for copy in sent:
        copy.wait_send()


def turn(zs, left, right, gains, first, grad):
    rows, units = left.shape[0] // 8, left.shape[1]
    width = gains.shape[1]
    half = rows // 2
    return pl.pallas_call(
        functools.partial(turn_kernel, zs, width // (8 * zs)),
        out_shape=[
            jax.ShapeDtypeStruct((8, rows, width), BF16),
            jax.ShapeDtypeStruct((rows, width), BF16),
            jax.ShapeDtypeStruct((rows, width), F32),
            jax.ShapeDtypeStruct((8, width), F32),
            jax.ShapeDtypeStruct(right.shape, BF16),
        ],
        in_specs=[ANY, ANY, ROWS, ANY, ANY],
        out_specs=[ANY] + [ROWS] * 4,
        scratch_shapes=[
            pltpu.VMEM((rows, width), F32),
            pltpu.VMEM((rows, width), BF16),
            pltpu.VMEM((4, 2 * rows, units), BF16),
            pltpu.VMEM(right.shape, BF16),
            pltpu.VMEM((4, 2, rows, width), BF16),
            pltpu.VMEM((4, rows, width), BF16),
            pltpu.VMEM((half, width), BF16),
            pltpu.VMEM((half, width), BF16),
            pltpu.VMEM((rows, width), BF16),
            pltpu.VMEM((rows, width), BF16),
            pltpu.VMEM((8, rows, width), BF16),
            pltpu.VMEM(right.shape, F32),
            pltpu.VMEM((2, SLAB, width), F32),
            pltpu.SemaphoreType.DMA((46,)),
            pltpu.SemaphoreType.DMA((46,)),
            pltpu.SemaphoreType.DMA((11,)),
        ],
        compiler_params=pltpu.CompilerParams(collective_id=1, has_side_effects=True, vmem_limit_bytes=56 * 2**20),
        cost_estimate=pl.CostEstimate(flops=0, bytes_accessed=220 * 2**20, transcendentals=0),
    )(left.reshape(4, 2 * rows, units), right, gains, first, grad)


def swap_kernel(zs, kinds, *refs):
    n = len(kinds)
    greet([name for _, name in swap_peers(zs, kinds)])
    swap_begin(zs, kinds, refs[:n], refs[n : 2 * n], *refs[2 * n :])()


def group_swap(name, zs, arrays, kinds):
    n = len(arrays)
    return pl.pallas_call(
        functools.partial(swap_kernel, zs, kinds),
        out_shape=swap_shapes(zs, arrays, kinds),
        in_specs=[ANY] * n,
        out_specs=[ANY] * n,
        scratch_shapes=swap_scratch(zs, kinds),
        compiler_params=pltpu.CompilerParams(collective_id=name, has_side_effects=True),
        cost_estimate=pl.CostEstimate(flops=0, bytes_accessed=50 * 2**20, transcendentals=0),
    )(*arrays)


def ff_kernel(x_ref, w_ref, hidden_ref, kept_ref):
    tile = hidden_ref.shape[1]
    projected = dot(x_ref[...], w_ref[...])
    gate, up = projected[:, :tile], projected[:, tile:]
    act, slope = gate_parts(gate)
    hidden_ref[...] = (act * up).astype(BF16)
    kept_ref[...] = jnp.concatenate([up * slope, act], axis=1).astype(BF16)


def ff_back_kernel(grad_ref, w_ref, kept_ref, out_ref):
    zs, _, wide = w_ref.shape
    d_hidden = dot_cols(grad_ref[:, :wide], w_ref[0])
    for z in range(1, zs):
        d_hidden += dot_cols(grad_ref[:, z * wide : (z + 1) * wide], w_ref[z])
    out_ref[...] = (jnp.concatenate([d_hidden, d_hidden], axis=1) * kept_ref[...].astype(F32)).astype(BF16)


FF_ROWS = 256


def ff_rows(width):
    return pl.BlockSpec((FF_ROWS, width), lambda i: (i, 0))


def ff_forward(x, w):
    rows, depth = x.shape
    wide = w.shape[1]
    return pl.pallas_call(
        ff_kernel,
        grid=(rows // FF_ROWS,),
        in_specs=[ff_rows(depth), pl.BlockSpec((depth, wide), lambda i: (0, 0))],
        out_specs=[ff_rows(wide // 2), ff_rows(wide)],
        out_shape=[jax.ShapeDtypeStruct((rows, wide // 2), BF16), jax.ShapeDtypeStruct((rows, wide), BF16)],
        compiler_params=PARAMS,
        cost_estimate=pl.CostEstimate(flops=2 * rows * depth * wide, bytes_accessed=20 * 2**20, transcendentals=0),
    )(x, w)


def ff_backward(grad, w, kept):
    rows, depth = grad.shape
    wide = kept.shape[1]
    return pl.pallas_call(
        ff_back_kernel,
        grid=(rows // FF_ROWS,),
        in_specs=[ff_rows(depth), pl.BlockSpec(w.shape, lambda i: (0, 0, 0)), ff_rows(wide)],
        out_specs=ff_rows(wide),
        out_shape=jax.ShapeDtypeStruct((rows, wide), BF16),
        compiler_params=PARAMS,
        cost_estimate=pl.CostEstimate(flops=rows * depth * wide, bytes_accessed=20 * 2**20, transcendentals=0),
    )(grad, w, kept)


def cut_kernel(in_ref, out_ref, in_blocks, out_blocks, wide):
    group, _, double = in_blocks.shape
    tile, ff = double // 2, out_ref.shape[1]
    span = group * tile
    odd = ff % 128
    live = lax.broadcasted_iota(jnp.int32, (in_ref.shape[0], span), 1) < ff
    wide[...] = jnp.zeros_like(wide)
    wide[:, : 2 * ff] = in_ref[...].astype(F32)
    gate = jnp.where(live, wide[:, :span], 0.0)
    up = pltpu.roll(wide[:, ff - odd : ff - odd + span], span - odd, 1)
    up = jnp.where(live, up, 0.0)
    wide[:, :span] = jnp.zeros_like(live, F32)
    wide[:, :ff] = out_ref[...].astype(F32)
    down = wide[:, :span]
    for g in range(group):
        at = slice(g * tile, (g + 1) * tile)
        in_blocks[g] = jnp.concatenate([gate[:, at], up[:, at]], axis=1).astype(BF16)
        out_blocks[g] = down[:, at].astype(BF16)


def cut_ff(w_in, w_out, group, tile):
    rows, ff = w_out.shape
    return pl.pallas_call(
        cut_kernel,
        grid=(rows // 16,),
        in_specs=[pl.BlockSpec((16, 2 * ff), lambda i: (i, 0)), pl.BlockSpec((16, ff), lambda i: (i, 0))],
        out_specs=[
            pl.BlockSpec((group, 16, 2 * tile), lambda i: (0, i, 0)),
            pl.BlockSpec((group, 16, tile), lambda i: (0, i, 0)),
        ],
        out_shape=[
            jax.ShapeDtypeStruct((group, rows, 2 * tile), BF16),
            jax.ShapeDtypeStruct((group, rows, tile), BF16),
        ],
        scratch_shapes=[pltpu.VMEM((16, -(-(ff + group * tile) // 128) * 128), F32)],
        compiler_params=PARAMS,
    )(w_in, w_out)


def join_kernel(in_blocks, out_blocks, in_ref, out_ref):
    group, _, double = in_blocks.shape
    tile, ff = double // 2, out_ref.shape[1]
    odd = ff % 128
    blocks = [in_blocks[g].astype(F32) for g in range(group)]
    gate = jnp.concatenate([block[:, :tile] for block in blocks], axis=1)
    up = jnp.concatenate([block[:, tile:] for block in blocks], axis=1)
    up = pltpu.roll(up, odd, 1)
    lane = lax.broadcasted_iota(jnp.int32, (up.shape[0], 128), 1)
    in_ref[:, : ff - odd] = gate[:, : ff - odd]
    in_ref[:, ff - odd : ff - odd + 128] = jnp.where(lane < odd, gate[:, ff - odd : ff - odd + 128], up[:, :128])
    in_ref[:, ff - odd + 128 :] = up[:, 128 : ff + odd]
    down = jnp.concatenate([out_blocks[g].astype(F32) for g in range(group)], axis=1)
    out_ref[...] = down[:, :ff]


def join_ff(in_blocks, out_blocks, ff):
    group, rows, tile = out_blocks.shape
    return pl.pallas_call(
        join_kernel,
        grid=(rows // 16,),
        in_specs=[
            pl.BlockSpec((group, 16, 2 * tile), lambda i: (0, i, 0)),
            pl.BlockSpec((group, 16, tile), lambda i: (0, i, 0)),
        ],
        out_specs=[pl.BlockSpec((16, 2 * ff), lambda i: (i, 0)), pl.BlockSpec((16, ff), lambda i: (i, 0))],
        out_shape=[jax.ShapeDtypeStruct((rows, 2 * ff), F32), jax.ShapeDtypeStruct((rows, ff), F32)],
        compiler_params=PARAMS,
    )(in_blocks, out_blocks)


def closing_kernel(zs, sum_ref, rows_ref, qkv_ref, dense_ref, total_ref, got, mine, lines, *refs):
    send, recv, local, line_send, line_recv = refs
    y, x, c = here()
    z = lax.axis_index("z")
    me = place(y, x, c)
    wide = got.shape[2]
    width = wide // 3
    piece = got.shape[1]
    found = swap_peers(zs, ("line",))
    greet([name for _, name in found])
    copies, comes = [], []
    for k, (peer, name) in enumerate(found[:7]):
        sems = dict(send_sem=send.at[k], recv_sem=recv.at[k], device_id=name, device_id_type=MESH)
        src = rows_ref.at[peer, :, pl.ds(0, wide)]
        copies.append(pltpu.make_async_remote_copy(src_ref=src, dst_ref=got.at[me], **sems))
        comes.append(pltpu.make_async_remote_copy(src_ref=got.at[peer], dst_ref=got.at[peer], **sems))
    for k, (peer, name) in enumerate(found[7:]):
        sems = dict(send_sem=line_send.at[k], recv_sem=line_recv.at[k], device_id=name, device_id_type=MESH)
        copies.append(pltpu.make_async_remote_copy(src_ref=sum_ref, dst_ref=lines.at[z], **sems))
        comes.append(pltpu.make_async_remote_copy(src_ref=lines.at[peer], dst_ref=lines.at[peer], **sems))
    for copy in copies:
        copy.start()
    keeps = [
        pltpu.make_async_copy(rows_ref.at[me, :, pl.ds(0, wide)], got.at[me], local.at[0]),
        pltpu.make_async_copy(sum_ref, lines.at[z], local.at[1]),
        pltpu.make_async_copy(rows_ref.at[:, :, pl.ds(wide, width)], mine, local.at[2]),
    ]
    for keep in keeps:
        keep.start()
    keeps[2].wait()
    for at in range(0, piece, 16):
        rows = jnp.concatenate([mine[g, at : at + 16] for g in range(8)], axis=1).astype(F32)
        dense_ref[at : at + 16] = rows
    for come in comes:
        come.wait_recv()
    for keep in keeps[:2]:
        keep.wait()
    for g in range(8):
        for j in range(3):
            at = pl.ds(j * D + g * width, width)
            qkv_ref[:, at] = got[g, :, j * width : (j + 1) * width].astype(F32)
    total = lines[0]
    for k in range(1, zs):
        total += lines[k]
    part = total[:, :piece]
    for k in range(1, zs):
        part = jnp.where(z == k, total[:, k * piece : (k + 1) * piece], part)
    total_ref[...] = part
    for copy in copies:
        copy.wait_send()


def closing(zs, sums, rows):
    _, piece, columns = rows.shape
    width = columns // 4
    return pl.pallas_call(
        functools.partial(closing_kernel, zs),
        out_shape=[
            jax.ShapeDtypeStruct((piece, 3 * D), F32),
            jax.ShapeDtypeStruct((piece, D), F32),
            jax.ShapeDtypeStruct((8, piece), F32),
        ],
        in_specs=[ROWS, ANY],
        out_specs=[ROWS] * 3,
        scratch_shapes=[
            pltpu.VMEM((8, piece, 3 * width), BF16),
            pltpu.VMEM((8, piece, width), BF16),
            pltpu.VMEM((zs, 8, width), F32),
            pltpu.SemaphoreType.DMA((7,)),
            pltpu.SemaphoreType.DMA((7,)),
            pltpu.SemaphoreType.DMA((3,)),
            pltpu.SemaphoreType.DMA((zs - 1,)),
            pltpu.SemaphoreType.DMA((zs - 1,)),
        ],
        compiler_params=pltpu.CompilerParams(collective_id=5, has_side_effects=True, vmem_limit_bytes=24 * 2**20),
        cost_estimate=pl.CostEstimate(flops=0, bytes_accessed=50 * 2**20, transcendentals=0),
    )(sums, rows)


def on_device(sizes, x_in, d_out, w_qkv, w_dense, w_in, w_out, gone, bone, gtwo, btwo, flags, span_start, span_len):
    gy, gx, cores, zs = sizes
    piece = w_qkv.shape[0]
    ff = w_out.shape[1]
    group = gy * gx * cores
    width = D // group
    tile = -(-ff // (group * 64)) * 64
    own = gy == 2

    def permute(array):
        lead = array.shape[:-1]
        return jnp.swapaxes(array.reshape(lead + (group, zs, piece)), -3, -2).reshape(lead + (D,))

    def restore(array):
        lead = array.shape[:-1]
        return jnp.swapaxes(array.reshape(lead + (zs, group, piece)), -3, -2).reshape(lead + (D,))

    def swap(name, arrays, kinds):
        if own:
            return group_swap(name, zs, arrays, kinds)
        ways = {
            "swap": lambda a: lax.all_to_all(a, GROUP, 0, 0, tiled=True),
            "group": lambda a: lax.all_gather(a, GROUP, axis=0),
            "line": lambda a: lax.all_gather(a, "z", axis=0),
        }
        return [ways[k](a) for a, k in zip(arrays, kinds)]

    def spread_rows(block):
        whole = group_gather(block) if own else lax.all_gather(block, GROUP, axis=0)
        return whole.reshape(group * block.shape[0], block.shape[1])

    rows_f32 = jax.ShapeDtypeStruct((SEQ_LEN, D), F32)
    rows_low = jax.ShapeDtypeStruct((SEQ_LEN, D), BF16)
    sums_type = jax.ShapeDtypeStruct((8, D), F32)

    def fold(partial):
        return lax.psum_scatter(partial.astype(BF16), GROUP, scatter_dimension=0, tiled=True).astype(F32)

    def stack_sums(*arrays):
        return jnp.pad(jnp.stack([jnp.sum(a, axis=0) for a in arrays]), ((0, 6), (0, 0)))

    def fold_one(left, right, x, gains):
        if own:
            kinds = [rows_f32, rows_f32, jax.ShapeDtypeStruct((SEQ_LEN, 128), F32)]
            whole, first, normal, inverse = group_fold(0, zs, "one", left, right, gains, [x], kinds)
            return whole.reshape(left.shape[0], D), first, normal, inverse
        first, normal, inverse = first_norm(permute(fold(dot(left, right))), x.astype(F32), gains)
        return spread_rows(first.astype(BF16)), first, normal, inverse

    def fold_two(left, right, first, grad, gains):
        if own:
            whole, result, d_pre, sums, d_right = turn(zs, left, right, gains, first, grad)
            return whole.reshape(left.shape[0], D), result, d_pre, sums, d_right
        grad = grad.astype(F32)
        right = jnp.swapaxes(right, 0, 1).reshape(right.shape[1], D)
        result, d_pre, terms = second_norm(fold(dot(left, right)), first, grad, gains)
        whole = spread_rows(d_pre.astype(BF16))
        d_right = jnp.swapaxes(dot_rows(left, whole).reshape(right.shape[0], zs, D // zs), 0, 1).astype(BF16)
        return whole, restore(result.astype(BF16)), d_pre, stack_sums(terms, grad), d_right

    def fold_back(left, right, d_pre_two, normal, inverse, gains):
        if own:
            kinds = [rows_f32, sums_type]
            whole, d_pre, sums = group_fold(7, zs, "back", left, right, gains, [d_pre_two, normal, inverse], kinds)
            return whole.reshape(left.shape[0], D), d_pre, sums
        d_pre, terms, d_first = first_back(fold(dot_cols(left, right)), d_pre_two, normal, inverse, gains)
        return spread_rows(restore(d_pre).astype(BF16)), d_pre, stack_sums(terms, d_first)

    def fold_last(left, right, d_pre, gains, extras, kinds):
        if own:
            return group_fold(8, zs, "last", left, right, gains, [d_pre], [rows_low], extras, kinds)
        out = restore((deep_alpha * d_pre + fold(dot_cols(left, right))).astype(BF16))
        return [out] + swap(8, extras, kinds)

    def gather(block):
        return lax.all_gather(block, "z", axis=0, tiled=True)

    def scatter(partial):
        return lax.psum_scatter(partial.astype(BF16), "z", scatter_dimension=0, tiled=True)

    masked = jnp.max(flags) > 0
    prefix = jnp.where(masked, SEQ_LEN, SEQ_LEN - span_len[0])
    info = jnp.concatenate([gone, bone, gtwo, btwo, jnp.stack([prefix, span_start[0]]).astype(BF16)])
    info = jnp.pad(info[None, :], ((0, 15), (0, -info.shape[0] % 128)))

    qkv_blocks = jnp.moveaxis(w_qkv.reshape(piece, 3, group, width), 2, 0).reshape(group, piece, 3 * width)
    w_dense_part = gather(w_dense)
    qkv_blocks, info = swap(2, [qkv_blocks, info], ("swap", "group"))
    w_qkv_part = gather(qkv_blocks.reshape(group * piece, 3 * width))
    in_blocks, out_blocks = cut_ff(w_in, w_out, group, tile)
    in_blocks, out_blocks, qkv_blocks, w_dense_part = lax.optimization_barrier(
        (in_blocks, out_blocks, qkv_blocks, w_dense_part)
    )
    in_blocks, out_blocks, info = swap(3, [in_blocks, out_blocks, info], ("swap", "swap", "line"))
    w_in_part = gather(in_blocks.reshape(group * piece, 2 * tile))
    x_perm = permute(x_in)
    x_next, in_blocks = lax.optimization_barrier((x_perm, in_blocks))
    x_all = spread_rows(x_next)

    info = info[:, :, 0]
    place_info = info[lax.axis_index("z"), :, 4 * piece : 4 * piece + 2].astype(jnp.int32)
    prefix, start = place_info[:, 0], place_info[:, 1]
    gains = info[:, :, : 4 * piece].astype(F32).reshape(zs, group, 4, piece)
    gains = jnp.pad(jnp.transpose(gains, (2, 0, 1, 3)).reshape(4, D), ((0, 4), (0, 0)))
    cosine, sine = tables(prefix, start)
    w_qkv_part, x_all, cosine, sine, gains = lax.optimization_barrier((w_qkv_part, x_all, cosine, sine, gains))
    packed = dot(x_all, w_qkv_part)
    qkv, context = attend(prefix, packed, cosine, sine)
    first_all, first, normal_one, inverse_one = fold_one(context, w_dense_part, x_perm, gains)
    out_blocks, first_all, w_in_part = lax.optimization_barrier((out_blocks, first_all, w_in_part))
    w_out_part = lax.all_gather(out_blocks.reshape(group * piece, tile).T, "z", axis=0)
    hidden, kept = ff_forward(first_all, w_in_part)
    d_branch, layer_out, d_pre_two, sums_two, d_w_out = fold_two(hidden, w_out_part, first, permute(d_out), gains)
    d_w_out = lax.psum_scatter(d_w_out, "z", scatter_dimension=0)
    d_projected = ff_backward(d_branch, w_out_part, kept)
    d_w_in = dot_rows(first_all, d_projected).astype(BF16)
    d_w_in, d_projected = lax.optimization_barrier((d_w_in, d_projected))
    d_w_in = scatter(d_w_in)
    d_attn, d_pre_one, sums_one = fold_back(d_projected, w_in_part, d_pre_two, normal_one, inverse_one, gains)
    d_attn, d_w_out = lax.optimization_barrier((d_attn, d_w_out))
    d_context = dot_cols(d_attn, w_dense_part).astype(BF16)
    d_packed = attend_back(prefix, qkv, d_context, cosine, sine)
    d_w_qkv = dot_rows(x_all, d_packed).astype(BF16)
    d_dense = dot_rows(context, d_attn).astype(BF16).reshape(zs, piece, group, width)
    d_dense = jnp.swapaxes(d_dense, 1, 2).reshape(D, width)
    d_w_qkv = jnp.concatenate([d_w_qkv, d_dense], axis=1)
    sums = jnp.concatenate([sums_one[:2], sums_two[:2], jnp.zeros((4, D), F32)])
    d_packed, d_w_qkv, d_w_in, sums = lax.optimization_barrier((d_packed, d_w_qkv, d_w_in, sums))
    d_w_qkv = scatter(d_w_qkv)
    d_w_in, d_w_out = d_w_in.reshape(group, piece, 2 * tile), d_w_out.T.reshape(group, piece, tile)
    d_input, d_w_in, d_w_out, sums = fold_last(
        d_packed, w_qkv_part, d_pre_one, gains, [d_w_in, d_w_out, sums], ("swap", "swap", "group")
    )
    sums = jnp.sum(sums, axis=0).reshape(8, zs, group, piece)
    sums = lax.dynamic_index_in_dim(sums, lax.axis_index(GROUP), 2, keepdims=False).reshape(8, width)
    out_in, out_out = join_ff(d_w_in, d_w_out, ff)
    out_in, out_out, d_input, d_w_qkv, sums = lax.optimization_barrier((out_in, out_out, d_input, d_w_qkv, sums))
    if own:
        out_qkv, out_dense, sums = closing(zs, sums, d_w_qkv.reshape(group, piece, 4 * width))
    else:
        out_dense = d_w_qkv[:, 3 * width :].reshape(group, piece, width)
        out_dense = jnp.swapaxes(out_dense, 0, 1).reshape(piece, D).astype(F32)
        d_w_qkv = d_w_qkv[:, : 3 * width].reshape(group, piece, 3 * width)
        d_w_qkv, sums = swap(5, [d_w_qkv, sums], ("swap", "line"))
        out_qkv = jnp.transpose(d_w_qkv.astype(F32).reshape(group, piece, 3, width), (1, 2, 0, 3))
        out_qkv = out_qkv.reshape(piece, 3 * D)
        sums = jnp.sum(sums, axis=0).reshape(8, zs, piece)
        sums = lax.dynamic_index_in_dim(sums, lax.axis_index("z"), 1, keepdims=False)
    return layer_out, d_input, out_qkv, out_dense, out_in, out_out, sums[0], sums[1], sums[2], sums[3]


def solution(mesh):
    grp, shard = mesh.shape["grp"], mesh.shape["shard"]
    sizes = (grp // 4, 2, 2, shard)
    inner = Mesh(mesh.devices.reshape(sizes), ALL)
    rows, flat = P(ALL, None), P(ALL)
    return jax.shard_map(
        functools.partial(on_device, sizes),
        mesh=inner,
        in_specs=(rows,) * 6 + (flat,) * 7,
        out_specs=(rows,) * 6 + (flat,) * 4,
        check_vma=False,
    )
```

```python
import functools

import jax
import jax.numpy as jnp
from jax import lax
from jax.experimental import pallas as pl
from jax.experimental.pallas import tpu as pltpu
from jax.sharding import Mesh
from jax.sharding import PartitionSpec as P

HEADS = 16
HEAD = 128
SEQ_LEN = 224
D = HEADS * HEAD
deep_alpha = 6.928203230275509
norm_eps = 1e-05
far_below = -1e30
scale = HEAD ** (-0.5)

ALL = ("gy", "gx", "core", "z")
GROUP = ("gy", "gx", "core")
MESH = pl.DeviceIdType.MESH
F32 = jnp.float32
BF16 = jnp.bfloat16


def dot(left, right):
    return jnp.dot(left, right, preferred_element_type=F32)


def dot_rows(left, right):
    return lax.dot_general(left, right, (((0,), (0,)), ((), ())), preferred_element_type=F32)


def dot_cols(left, right):
    return lax.dot_general(left, right, (((1,), (1,)), ((), ())), preferred_element_type=F32)


def swap_halves(block):
    lane = lax.broadcasted_iota(jnp.int32, block.shape, 1)
    return jnp.where((lane & 32) == 0, pltpu.roll(block, 96, 1), pltpu.roll(block, 32, 1))


def seen(prefix):
    row = lax.broadcasted_iota(jnp.int32, (SEQ_LEN, SEQ_LEN), 0)
    col = lax.broadcasted_iota(jnp.int32, (SEQ_LEN, SEQ_LEN), 1)
    return (col < prefix) | (col <= row)


def softmax(queries, keys, visible):
    scores = jnp.where(visible, dot_cols(queries, keys), far_below)
    weights = jnp.exp(scores - jnp.max(scores, axis=1, keepdims=True))
    return weights / jnp.sum(weights, axis=1, keepdims=True)


def attend_kernel(prefix_ref, packed_ref, cos_ref, sin_ref, qkv_ref, context_ref):
    width = context_ref.shape[1]
    visible = seen(prefix_ref[pl.program_id(0)])
    cosine = cos_ref[0]
    sine = sin_ref[0]
    for head in range(width // HEAD):
        at = pl.ds(head * HEAD, HEAD)
        at_k = pl.ds(width + head * HEAD, HEAD)
        at_v = pl.ds(2 * width + head * HEAD, HEAD)
        raw = packed_ref[:, at]
        queries = ((raw * cosine + swap_halves(raw) * sine) * scale).astype(BF16)
        raw = packed_ref[:, at_k]
        keys = (raw * cosine + swap_halves(raw) * sine).astype(BF16)
        values = packed_ref[:, at_v].astype(BF16)
        qkv_ref[:, at] = queries
        qkv_ref[:, at_k] = keys
        qkv_ref[:, at_v] = values
        probs = softmax(queries, keys, visible).astype(BF16)
        context_ref[:, at] = dot(probs, values).astype(BF16)


def attend_back_kernel(prefix_ref, qkv_ref, d_context_ref, cos_ref, sin_ref, d_packed_ref):
    width = d_context_ref.shape[1]
    visible = seen(prefix_ref[pl.program_id(0)])
    cosine = cos_ref[0]
    sine = sin_ref[0]
    for head in range(width // HEAD):
        at = pl.ds(head * HEAD, HEAD)
        at_k = pl.ds(width + head * HEAD, HEAD)
        at_v = pl.ds(2 * width + head * HEAD, HEAD)
        queries = qkv_ref[:, at]
        keys = qkv_ref[:, at_k]
        values = qkv_ref[:, at_v]
        d_context = d_context_ref[:, at]
        probs = softmax(queries, keys, visible)
        d_packed_ref[:, at_v] = dot_rows(probs.astype(BF16), d_context).astype(BF16)
        d_probs = dot_cols(d_context, values)
        inner = jnp.sum(probs * d_probs, axis=1, keepdims=True)
        d_scores = (probs * (d_probs - inner)).astype(BF16)
        grad = dot(d_scores, keys) * scale
        d_packed_ref[:, at] = (grad * cosine - swap_halves(grad) * sine).astype(BF16)
        grad = dot_rows(d_scores, queries)
        d_packed_ref[:, at_k] = (grad * cosine - swap_halves(grad) * sine).astype(BF16)


def by_sequence(width):
    return pl.BlockSpec((SEQ_LEN, width), lambda s: (s, 0))


TABLE = pl.BlockSpec((1, SEQ_LEN, HEAD), lambda s: (s, 0, 0))
SCALARS = pl.BlockSpec(memory_space=pltpu.SMEM)
PARAMS = pltpu.CompilerParams(vmem_limit_bytes=48 * 2**20)


def attend(prefix, packed, cosine, sine):
    rows, width = packed.shape[0], packed.shape[1] // 3
    return pl.pallas_call(
        attend_kernel,
        grid=(rows // SEQ_LEN,),
        in_specs=[SCALARS, by_sequence(3 * width), TABLE, TABLE],
        out_specs=[by_sequence(3 * width), by_sequence(width)],
        out_shape=[
            jax.ShapeDtypeStruct((rows, 3 * width), BF16),
            jax.ShapeDtypeStruct((rows, width), BF16),
        ],
        compiler_params=PARAMS,
    )(prefix, packed, cosine, sine)


def attend_back(prefix, qkv, d_context, cosine, sine):
    rows, width = d_context.shape
    return pl.pallas_call(
        attend_back_kernel,
        grid=(rows // SEQ_LEN,),
        in_specs=[SCALARS, by_sequence(3 * width), by_sequence(width), TABLE, TABLE],
        out_specs=by_sequence(3 * width),
        out_shape=jax.ShapeDtypeStruct((rows, 3 * width), BF16),
        compiler_params=PARAMS,
    )(prefix, qkv, d_context, cosine, sine)


def tables(prefix, start):
    place = jnp.arange(SEQ_LEN, dtype=jnp.int32)
    in_span = place[None, :] >= prefix[:, None]
    pos_one = jnp.where(in_span, start[:, None], place[None, :])
    pos_two = jnp.where(in_span, place[None, :] - prefix[:, None] + 1, 0)
    lane = jnp.arange(HEAD)
    freqs = 10000.0 ** (-2.0 * (lane % 32).astype(F32) / 64)
    place_of = jnp.where(lane[None, None, :] < 64, pos_one[:, :, None], pos_two[:, :, None])
    angles = place_of.astype(F32) * freqs
    sign = jnp.where(lane % 64 < 32, -1.0, 1.0)
    return jnp.cos(angles), jnp.sin(angles) * sign


def norm_parts(values):
    center = values - jnp.mean(values, axis=-1, keepdims=True)
    inverse = lax.rsqrt(jnp.mean(center * center, axis=-1, keepdims=True) + norm_eps)
    return center * inverse, inverse


def norm_back(normal, inverse, gain, grad):
    scaled = gain * grad
    return inverse * (
        scaled
        - jnp.mean(scaled, axis=-1, keepdims=True)
        - normal * jnp.mean(scaled * normal, axis=-1, keepdims=True)
    )


def gate_parts(gate):
    phi = 0.5 * (1.0 + lax.erf(gate * 0.7071067811865476))
    slope = phi + gate * jnp.exp(-0.5 * gate * gate) * 0.3989422804014327
    return gate * phi, slope


def here():
    return lax.axis_index("gy"), lax.axis_index("gx"), lax.axis_index("core")


def place(y, x, c):
    return (y * 2 + x) * 2 + c


def greet(peers):
    barrier = pltpu.get_barrier_semaphore()
    for peer in peers:
        pl.semaphore_signal(barrier, inc=1, device_id=peer, device_id_type=MESH)
    pl.semaphore_wait(barrier, len(peers))


def spread_block(cut, base, block_ref, out_ref, send, recv, local):
    rows = block_ref.shape[0]
    y, x, c = here()
    to_x, to_y, to_c = {"gx": 1 - x}, {"gy": 1 - y}, {"core": 1 - c}
    me, by_x, by_y, far = place(y, x, c), place(y, 1 - x, c), place(1 - y, x, c), place(1 - y, 1 - x, c)
    low, high = pl.ds(0, cut), pl.ds(cut, rows - cut)

    def push(k, src, dst, to):
        copy = pltpu.make_async_remote_copy(
            src_ref=src, dst_ref=dst, send_sem=send.at[base + k], recv_sem=recv.at[base + k], device_id=to, device_id_type=MESH
        )
        copy.start()
        return copy

    def landed(k, dst):
        pltpu.make_async_remote_copy(
            src_ref=dst, dst_ref=dst, send_sem=send.at[base + k], recv_sem=recv.at[base + k], device_id=to_c, device_id_type=MESH
        ).wait_recv()

    sent = [
        push(0, block_ref.at[low], out_ref.at[me, low], to_x),
        push(1, block_ref.at[high], out_ref.at[me, high], to_y),
        push(2, block_ref.at[high], out_ref.at[me, high], to_x),
        push(3, block_ref.at[low], out_ref.at[me, low], to_y),
        push(4, block_ref, out_ref.at[me], to_c),
    ]
    keep = pltpu.make_async_copy(block_ref, out_ref.at[me], local)
    keep.start()
    landed(0, out_ref.at[by_x, low])
    sent.append(push(5, out_ref.at[by_x, low], out_ref.at[by_x, low], to_y))
    sent.append(push(7, out_ref.at[by_x, low], out_ref.at[by_x, low], to_c))
    landed(1, out_ref.at[by_y, high])
    sent.append(push(6, out_ref.at[by_y, high], out_ref.at[by_y, high], to_x))
    sent.append(push(8, out_ref.at[by_y, high], out_ref.at[by_y, high], to_c))
    landed(2, out_ref.at[by_x, high])
    sent.append(push(9, out_ref.at[by_x, high], out_ref.at[by_x, high], to_c))
    landed(3, out_ref.at[by_y, low])
    sent.append(push(10, out_ref.at[by_y, low], out_ref.at[by_y, low], to_c))
    landed(5, out_ref.at[far, low])
    sent.append(push(11, out_ref.at[far, low], out_ref.at[far, low], to_c))
    landed(6, out_ref.at[far, high])
    sent.append(push(12, out_ref.at[far, high], out_ref.at[far, high], to_c))
    other, other_x, other_y, other_far = (
        place(y, x, 1 - c),
        place(y, 1 - x, 1 - c),
        place(1 - y, x, 1 - c),
        place(1 - y, 1 - x, 1 - c),
    )
    landed(4, out_ref.at[other])
    landed(7, out_ref.at[other_x, low])
    landed(8, out_ref.at[other_y, high])
    landed(9, out_ref.at[other_x, high])
    landed(10, out_ref.at[other_y, low])
    landed(11, out_ref.at[other_far, low])
    landed(12, out_ref.at[other_far, high])
    keep.wait()
    for copy in sent:
        copy.wait_send()


def gather_kernel(cut, block_ref, out_ref, send, recv, local):
    y, x, c = here()
    greet([{"gx": 1 - x}, {"gy": 1 - y}, {"core": 1 - c}])
    spread_block(cut, 0, block_ref, out_ref, send, recv, local)


ANY = pl.BlockSpec(memory_space=pl.ANY)


def group_gather(block):
    rows, width = block.shape
    return pl.pallas_call(
        functools.partial(gather_kernel, rows // 2),
        out_shape=jax.ShapeDtypeStruct((8, rows, width), block.dtype),
        in_specs=[ANY],
        out_specs=ANY,
        scratch_shapes=[pltpu.SemaphoreType.DMA((13,)), pltpu.SemaphoreType.DMA((13,)), pltpu.SemaphoreType.DMA],
        compiler_params=pltpu.CompilerParams(collective_id=9, has_side_effects=True),
        cost_estimate=pl.CostEstimate(flops=0, bytes_accessed=100 * 2**20, transcendentals=0),
    )(block)


def swap_peers(zs, kinds):
    y, x, c = here()
    z = lax.axis_index("z")
    found = []
    for k in range(1, 8):
        peer = ((y + k // 4) % 2, (x + k // 2 % 2) % 2, (c + k % 2) % 2)
        found.append((place(*peer), {"gy": peer[0], "gx": peer[1], "core": peer[2]}))
    if "line" in kinds:
        found += [((z + k) % zs, {"z": (z + k) % zs}) for k in range(1, zs)]
    return found


def swap_begin(zs, kinds, blocks, outs, send, recv, local):
    copies, comes, keeps = [], [], []
    found = swap_peers(zs, kinds)
    for i, kind in enumerate(kinds):
        me = lax.axis_index("z") if kind == "line" else place(*here())
        for k, (peer, name) in enumerate(found[7:] if kind == "line" else found[:7]):
            src = blocks[i].at[peer] if kind == "swap" else blocks[i]
            landing = outs[i].at[peer]
            sems = dict(send_sem=send.at[i, k], recv_sem=recv.at[i, k], device_id=name, device_id_type=MESH)
            copies.append(pltpu.make_async_remote_copy(src_ref=src, dst_ref=outs[i].at[me], **sems))
            comes.append(pltpu.make_async_remote_copy(src_ref=landing, dst_ref=landing, **sems))
            copies[-1].start()
        own = blocks[i].at[me] if kind == "swap" else blocks[i]
        keeps.append(pltpu.make_async_copy(own, outs[i].at[me], local.at[i]))
        keeps[-1].start()

    def finish():
        for come in comes:
            come.wait_recv()
        for copy in copies:
            copy.wait_send()
        for keep in keeps:
            keep.wait()

    return finish


SWAP_LEAD = {"swap": lambda zs: (), "group": lambda zs: (8,), "line": lambda zs: (zs,)}


def swap_shapes(zs, arrays, kinds):
    return [jax.ShapeDtypeStruct(SWAP_LEAD[k](zs) + a.shape, a.dtype) for a, k in zip(arrays, kinds)]


def swap_scratch(zs, kinds):
    n, most = len(kinds), max(7, zs - 1)
    return [
        pltpu.SemaphoreType.DMA((n, most)),
        pltpu.SemaphoreType.DMA((n, most)),
        pltpu.SemaphoreType.DMA((n,)),
    ]


SLAB = 16
ROWS = pl.BlockSpec(memory_space=pltpu.VMEM)
CHIP_COLS = 256


def by_rows(value, zs, piece):
    group = D // (zs * piece)
    order = [g * zs + z for z in range(zs) for g in range(group)]
    return jnp.concatenate([value[:, m * piece : (m + 1) * piece] for m in order], axis=1)


def in_order(value, zs, piece):
    group = D // (zs * piece)
    order = [z * group + g for g in range(group) for z in range(zs)]
    return jnp.concatenate([value[:, m * piece : (m + 1) * piece] for m in order], axis=1)


def first_norm(total, x, gains):
    normal, inverse = norm_parts(deep_alpha * x + total)
    first = normal * gains[0:1] + gains[1:2]
    return first, normal, inverse


def second_norm(total, first, grad, gains):
    normal, inverse = norm_parts(deep_alpha * first + total)
    return normal * gains[2:3] + gains[3:4], norm_back(normal, inverse, gains[2:3], grad), grad * normal


def first_back(total, d_pre_two, normal, inverse, gains):
    d_first = deep_alpha * d_pre_two + total
    return norm_back(normal, inverse, gains[0:1], d_first), d_first * normal, d_first


def fold_kernel(mode, across, zs, piece, n_aux, n_out, kinds, *refs):
    left_ref, right_ref, gains_ref = refs[:3]
    aux_refs = refs[3 : 3 + n_aux]
    refs = refs[3 + n_aux :]
    n_swap = len(kinds)
    swap_in, refs = refs[:n_swap], refs[n_swap:]
    spread = mode != "last"
    if spread:
        all_ref, refs = refs[0], refs[1:]
    outs, refs = refs[:n_out], refs[n_out:]
    swap_out, refs = refs[:n_swap], refs[n_swap:]
    aux, refs = refs[:n_aux], refs[n_aux:]
    left, right, part, got, near_x, near_y, from_x, from_y, block, acc, send, recv, local = refs[:13]
    rows, width = block.shape
    cut = near_x.shape[0]
    y, x, c = here()
    to_x, to_y, to_c = {"gx": 1 - x}, {"gy": 1 - y}, {"core": 1 - c}
    chips = [(1 - y, 1 - x), (y, 1 - x), (1 - y, x), (y, x)]
    low, high = pl.ds(0, cut), pl.ds(cut, rows - cut)

    def push(k, src, dst, to):
        copy = pltpu.make_async_remote_copy(
            src_ref=src, dst_ref=dst, send_sem=send.at[k], recv_sem=recv.at[k], device_id=to, device_id_type=MESH
        )
        copy.start()
        return copy

    def add(k, extra, start, size, offset=0):
        @pl.loop(0, size // SLAB)
        def _(step):
            at = pl.ds(pl.multiple_of(start + step * SLAB, SLAB), SLAB)
            of = pl.ds(pl.multiple_of(start - offset + step * SLAB, SLAB), SLAB)
            part[k, c, at] = (part[k, c, at].astype(F32) + extra[of].astype(F32)).astype(BF16)

    loads = [pltpu.make_async_copy(left_ref.at[a * 2 + b], left.at[k], local.at[k]) for k, (a, b) in enumerate(chips)]
    load_right = pltpu.make_async_copy(right_ref, right, local.at[4])
    load_aux = [pltpu.make_async_copy(r, v, local.at[5 + k]) for k, (r, v) in enumerate(zip(aux_refs, aux))]
    loads[0].start()
    load_right.start()
    for load in loads[1:] + load_aux:
        load.start()
    if n_swap:
        greet([name for _, name in swap_peers(1, kinds)])
        swap_finish = swap_begin(1, kinds, swap_in, swap_out, *refs[13:])
    else:
        greet([to_x, to_y, to_c])

    def product(k):
        loads[k].wait()

        @pl.loop(0, width // CHIP_COLS)
        def _(step):
            at = pl.ds(pl.multiple_of(step * CHIP_COLS, CHIP_COLS), CHIP_COLS)
            here_part = dot_cols(left[k], right[at]) if across else dot(left[k], right[:, at])
            part[k, 0, :, at] = here_part[:rows].astype(BF16)
            part[k, 1, :, at] = here_part[rows:].astype(BF16)

        return push(k, part.at[k, 1 - c], got.at[k], to_c)

    load_right.wait()
    sent = [product(0), product(1)]
    sent[0].wait_recv()
    add(0, got.at[0], 0, rows)
    far_x = push(4, part.at[0, c, low], near_x, to_x)
    far_y = push(5, part.at[0, c, high], near_y, to_y)
    sent.append(product(2))
    sent[1].wait_recv()
    add(1, got.at[1], 0, rows)
    plain_x = push(6, part.at[1, c, low], from_x.at[low], to_x)
    sent[2].wait_recv()
    add(2, got.at[2], 0, rows)
    plain_y = push(7, part.at[2, c, high], from_y.at[high], to_y)
    sent.append(product(3))
    far_y.wait_recv()
    add(1, near_y, cut, rows - cut, cut)
    more_x = push(8, part.at[1, c, high], from_x.at[high], to_x)
    far_x.wait_recv()
    add(2, near_x, 0, cut)
    more_y = push(9, part.at[2, c, low], from_y.at[low], to_y)
    sent[3].wait_recv()
    for load in load_aux:
        load.wait()
    plain_x.wait_recv()
    plain_y.wait_recv()
    more_x.wait_recv()
    more_y.wait_recv()
    gains = gains_ref[...]
    acc[...] = jnp.zeros_like(acc)

    @pl.loop(0, rows // SLAB)
    def _(step):
        at = pl.ds(pl.multiple_of(step * SLAB, SLAB), SLAB)
        total = part[3, c, at].astype(F32) + got[3, at].astype(F32) + from_x[at].astype(F32) + from_y[at].astype(F32)
        held = [a[at].astype(F32) for a in aux]
        if mode == "one":
            first, normal, inverse = first_norm(by_rows(total, zs, piece), held[0], gains)
            outs[0][at] = first
            outs[1][at] = normal
            outs[2][at] = jnp.broadcast_to(inverse, (SLAB, 128))
            block[at] = first.astype(BF16)
        elif mode == "back":
            d_pre, terms, d_first = first_back(total, held[0], held[1], held[2][:, 0:1], gains)
            outs[0][at] = d_pre
            block[at] = in_order(d_pre, zs, piece).astype(BF16)
            acc[0] += terms
            acc[1] += d_first
        else:
            outs[0][at] = in_order(deep_alpha * held[0] + total, zs, piece).astype(BF16)

    if mode == "back":
        outs[-1][0:1] = jnp.sum(acc[0], axis=0, keepdims=True)
        outs[-1][1:2] = jnp.sum(acc[1], axis=0, keepdims=True)
    for copy in sent + [far_x, far_y, plain_x, plain_y, more_x, more_y]:
        copy.wait_send()
    if n_swap:
        swap_finish()
    if spread:
        spread_block(cut, 10, block, all_ref, send, recv, local.at[4])


def group_fold(name, zs, mode, left, right, gains, aux, out_types, extras=(), kinds=()):
    across = mode != "one"
    rows, depth = left.shape[0] // 8, left.shape[1]
    width = gains.shape[1]
    cut = rows // 2
    spread = mode != "last"
    out_shape = [jax.ShapeDtypeStruct((8, rows, width), BF16)] * spread + out_types
    n, n_swap = len(aux), len(extras)
    n_sems = 23 if spread else 10
    return pl.pallas_call(
        functools.partial(fold_kernel, mode, across, zs, width // (8 * zs), n, len(out_types), kinds),
        out_shape=out_shape + swap_shapes(1, extras, kinds),
        in_specs=[ANY, ANY, ROWS] + [ANY] * (n + n_swap),
        out_specs=[ANY] * spread + [ROWS] * len(out_types) + [ANY] * n_swap,
        scratch_shapes=[pltpu.VMEM(a.shape, a.dtype) for a in aux]
        + [
            pltpu.VMEM((4, 2 * rows, depth), BF16),
            pltpu.VMEM(right.shape, BF16),
            pltpu.VMEM((4, 2, rows, width), BF16),
            pltpu.VMEM((4, rows, width), BF16),
            pltpu.VMEM((cut, width), BF16),
            pltpu.VMEM((rows - cut, width), BF16),
            pltpu.VMEM((rows, width), BF16),
            pltpu.VMEM((rows, width), BF16),
            pltpu.VMEM((rows, width), BF16),
            pltpu.VMEM((2, SLAB, width), F32),
            pltpu.SemaphoreType.DMA((n_sems,)),
            pltpu.SemaphoreType.DMA((n_sems,)),
            pltpu.SemaphoreType.DMA((5 + n,)),
        ]
        + (swap_scratch(1, kinds) if n_swap else []),
        compiler_params=pltpu.CompilerParams(
            collective_id=name, has_side_effects=True, vmem_limit_bytes=50 * 2**20
        ),
        cost_estimate=pl.CostEstimate(flops=0, bytes_accessed=(200 if spread else 110) * 2**20, transcendentals=0),
    )(left.reshape(4, 2 * rows, depth), right, gains, *aux, *extras)


def turn_kernel(
    zs, piece, x_ref, in_ref, out_ref, gains_ref, first_ref, grad_ref,
    all_ref, kept_ref, right_ref, result_ref, d_pre_ref, sums_ref, dw_ref,
    first, grad, w_in, kept, left, right, part, got, near_x, near_y, from_x, from_y, whole, dw, acc,
    fold_send, fold_recv, all_send, all_recv, line_send, line_recv, local, x_local
):
    rows = first.shape[0]
    tile = left.shape[2]
    wide = right.shape[2]
    y, x, c = here()
    z = lax.axis_index("z")
    to_x, to_y, to_c = {"gx": 1 - x}, {"gy": 1 - y}, {"core": 1 - c}
    chips = [(1 - y) * 2 + 1 - x, y * 2 + 1 - x, (1 - y) * 2 + x, y * 2 + x]
    me, by_x, by_y, far = place(y, x, c), place(y, 1 - x, c), place(1 - y, x, c), place(1 - y, 1 - x, c)
    other, other_x, other_y, other_far = (
        place(y, x, 1 - c),
        place(y, 1 - x, 1 - c),
        place(1 - y, x, 1 - c),
        place(1 - y, 1 - x, 1 - c),
    )
    half = rows // 2
    most = -(-half // (2 * SLAB)) * SLAB
    lows = [(0, most), (half, half - most)]
    highs = [(most, half - most), (2 * half - most, most)]
    top, bottom = pl.ds(0, half), pl.ds(half, half)
    sent = []

    def remote(sems, k, src, dst, to):
        return pltpu.make_async_remote_copy(
            src_ref=src,
            dst_ref=dst,
            send_sem=sems[0].at[k],
            recv_sem=sems[1].at[k],
            device_id=to,
            device_id_type=MESH,
        )

    def push(sems, k, src, dst, to):
        copy = remote(sems, k, src, dst, to)
        copy.start()
        sent.append(copy)

    def landed(sems, k, dst):
        remote(sems, k, dst, dst, to_c).wait_recv()

    folds, alls, lines = (fold_send, fold_recv), (all_send, all_recv), (line_send, line_recv)

    load_out = pltpu.make_async_copy(out_ref, right.at[z], local.at[0])
    load_in = pltpu.make_async_copy(in_ref, w_in, local.at[1])
    load_first = pltpu.make_async_copy(first_ref, first, local.at[2])
    load_grad = pltpu.make_async_copy(grad_ref, grad, local.at[3])

    def load_x(g):
        return pltpu.make_async_copy(x_ref.at[g], whole.at[g], x_local.at[g])

    load_out.start()
    load_in.start()
    for g in range(8):
        load_x(g).start()
    load_first.start()
    load_grad.start()

    barrier = pltpu.get_barrier_semaphore()
    for to in (to_x, to_y, to_c):
        pl.semaphore_signal(barrier, inc=1, device_id=to, device_id_type=MESH)

    @pl.when(z > 0)
    def _():
        pl.semaphore_signal(barrier, inc=1, device_id={"z": z - 1}, device_id_type=MESH)

    @pl.when(z < zs - 1)
    def _():
        pl.semaphore_signal(barrier, inc=1, device_id={"z": z + 1}, device_id_type=MESH)

    inside = (z > 0) & (z < zs - 1)

    @pl.when(inside)
    def _():
        pl.semaphore_wait(barrier, 5)

    @pl.when(jnp.logical_not(inside))
    def _():
        pl.semaphore_wait(barrier, 4)

    def shard_of(step, up):
        return z - step if up else z + step

    def hop(step, up):
        ref = right.at[shard_of(step, up)]
        return remote(lines, 2 * step + (0 if up else 1), ref, ref, {"z": z + 1 if up else z - 1})

    def sends(step, up):
        return (z >= step) & (z < zs - 1) if up else (z <= zs - 1 - step) & (z > 0)

    def gets(step, up):
        return z >= step + 1 if up else z <= zs - 2 - step

    def line_serve(step):
        for up in (True, False):

            @pl.when(gets(step - 1, up) & sends(step, up))
            def _(up=up):
                landed(lines, 2 * (step - 1) + (0 if up else 1), right.at[shard_of(step, up)])
                hop(step, up).start()

    def line_take(step):
        for up in (True, False):

            @pl.when(gets(step - 1, up) & jnp.logical_not(sends(step, up)))
            def _(up=up):
                landed(lines, 2 * (step - 1) + (0 if up else 1), right.at[shard_of(step, up)])

    load_out.wait()
    for up in (True, False):

        @pl.when(sends(0, up))
        def _(up=up):
            hop(0, up).start()


    load_in.wait()

    @pl.loop(0, 8)
    def _(g):
        @pl.when(g == 6)
        def _():
            line_serve(1)

        load_x(g).wait()
        projected = dot(whole[g], w_in[...])
        gate, up = projected[:, :tile], projected[:, tile:]
        act, slope = gate_parts(gate)
        left[g] = (act * up).astype(BF16)
        kept[g] = jnp.concatenate([up * slope, act], axis=1).astype(BF16)

    keep = pltpu.make_async_copy(kept, kept_ref, local.at[4])
    keep.start()

    def add(k, extra, start, offset, at):
        @pl.loop(0, half // SLAB)
        def _(step):
            row = pl.ds(pl.multiple_of(start + step * SLAB, SLAB), SLAB)
            of = pl.ds(pl.multiple_of(start - offset + step * SLAB, SLAB), SLAB)
            part[k, c, row, at] = (part[k, c, row, at].astype(F32) + extra[of, at].astype(F32)).astype(BF16)

    def chip_sum(k, at):
        add(k, got.at[k], 0, 0, at)
        add(k, got.at[k], half, 0, at)

    def product(k, block, at):
        found = dot(left[pl.ds(2 * chips[k], 2)].reshape(2 * rows, tile), right[block])
        part[k, 0, :, at] = found[:rows].astype(BF16)
        part[k, 1, :, at] = found[rows:].astype(BF16)

    def block_at(i):
        if i == 0:
            return z
        below = z < zs // 2
        near = jnp.where(below, z, zs - 1 - z)
        spot = jnp.where(i <= 2 * near, jnp.where(i % 2 == 1, near - (i + 1) // 2, near + i // 2), i)
        return jnp.where(below, spot, zs - 1 - spot)

    def block_cols(i):
        return pl.ds(pl.multiple_of(block_at(i) * wide, wide), wide)

    def fold_start(i):
        b, block, at = 8 * i, block_at(i), block_cols(i)
        rest = pl.ds(1, 3)
        product(0, block, at)
        push(folds, b, part.at[0, 1 - c, :, at], got.at[0, :, at], to_c)
        for k in (1, 2, 3):
            product(k, block, at)
        push(folds, b + 1, part.at[rest, 1 - c, :, at], got.at[rest, :, at], to_c)
        landed(folds, b, got.at[0, :, at])
        chip_sum(0, at)
        push(folds, b + 2, part.at[0, c, top, at], near_x.at[:, at], to_x)
        push(folds, b + 3, part.at[0, c, bottom, at], near_y.at[:, at], to_y)
        landed(folds, b + 1, got.at[rest, :, at])
        chip_sum(1, at)
        push(folds, b + 4, part.at[1, c, top, at], from_x.at[top, at], to_x)
        chip_sum(2, at)
        push(folds, b + 5, part.at[2, c, bottom, at], from_y.at[bottom, at], to_y)

    def fold_end(i):
        b, at = 8 * i, block_cols(i)
        landed(folds, b + 3, near_y.at[:, at])
        add(1, near_y, half, half, at)
        push(folds, b + 6, part.at[1, c, bottom, at], from_x.at[bottom, at], to_x)
        landed(folds, b + 2, near_x.at[:, at])
        add(2, near_x, 0, 0, at)
        push(folds, b + 7, part.at[2, c, top, at], from_y.at[top, at], to_y)

    gains = gains_ref[...]
    line_take(1)
    fold_start(0)
    fold_start(1)
    fold_end(0)
    for i in range(2, zs):
        if i < zs - 1:
            line_serve(i)
        fold_end(i - 1)
        line_take(i)
        fold_start(i)
    fold_end(zs - 1)
    carry = pltpu.make_async_copy(right, right_ref, local.at[5])
    carry.start()
    load_first.wait()
    load_grad.wait()
    acc[...] = jnp.zeros_like(acc)
    for i in range(zs):
        at = block_cols(i)
        landed(folds, 8 * i + 4, from_x.at[top, at])
        landed(folds, 8 * i + 5, from_y.at[bottom, at])
        landed(folds, 8 * i + 6, from_x.at[bottom, at])
        landed(folds, 8 * i + 7, from_y.at[top, at])

    def low(i):
        return pl.ds(*lows[i])

    def high(i):
        return pl.ds(*highs[i])

    def span(i):
        return pl.ds(i * half, half)

    def norm(i):
        @pl.loop(0, half // SLAB)
        def _(step):
            at = pl.ds(pl.multiple_of(i * half + step * SLAB, SLAB), SLAB)
            total = part[3, c, at].astype(F32) + got[3, at].astype(F32)
            total += from_x[at].astype(F32) + from_y[at].astype(F32)
            dy = grad[at].astype(F32)
            result, d_pre, terms = second_norm(total, first[at], dy, gains)
            result_ref[at] = in_order(result, zs, piece).astype(BF16)
            d_pre_ref[at] = d_pre
            whole[me, at] = d_pre.astype(BF16)
            acc[0] += terms
            acc[1] += dy

        b = 13 * i
        push(alls, b, whole.at[me, low(i)], whole.at[me, low(i)], to_x)
        push(alls, b + 1, whole.at[me, high(i)], whole.at[me, high(i)], to_y)
        push(alls, b + 2, whole.at[me, high(i)], whole.at[me, high(i)], to_x)
        push(alls, b + 3, whole.at[me, low(i)], whole.at[me, low(i)], to_y)
        push(alls, b + 4, whole.at[me, span(i)], whole.at[me, span(i)], to_c)

    def pass_on(i, k, slot, at, onward):
        ref = whole.at[slot, at]
        landed(alls, 13 * i + k, ref)
        for where, to in onward:
            push(alls, 13 * i + where, ref, ref, to)

    def spread_first(i):
        pass_on(i, 0, by_x, low(i), [(5, to_y), (7, to_c)])
        pass_on(i, 1, by_y, high(i), [(6, to_x), (8, to_c)])

    def spread_rest(i):
        pass_on(i, 2, by_x, high(i), [(9, to_c)])
        pass_on(i, 3, by_y, low(i), [(10, to_c)])

    def spread_far(i):
        pass_on(i, 5, far, low(i), [(11, to_c)])
        pass_on(i, 6, far, high(i), [(12, to_c)])

    outward = []

    def gradient(k, last=False, first_one=False):
        pair = pl.ds(2 * chips[k], 2)
        outward.append(pltpu.make_async_copy(whole.at[pair], all_ref.at[pair], local.at[6 + k]))
        outward[-1].start()

        @pl.loop(0, zs)
        def _(block):
            at = pl.ds(pl.multiple_of(block * wide, wide), wide)
            found = dot_rows(left[pair].reshape(2 * rows, tile), whole[pair, :, at].reshape(2 * rows, wide))
            if first_one:
                dw[block] = found
            elif last:
                dw_ref[block] = (dw[block] + found).astype(BF16)
            else:
                dw[block] += found

    norm(0)
    norm(1)
    spread_first(0)
    for i in (0, 1):
        landed(alls, 13 * i + 4, whole.at[other, span(i)])
    gradient(3, first_one=True)
    spread_rest(0)
    spread_first(1)
    spread_rest(1)
    for i in (0, 1):
        landed(alls, 13 * i + 7, whole.at[other_x, low(i)])
        landed(alls, 13 * i + 9, whole.at[other_x, high(i)])
    gradient(1)
    spread_far(0)
    for i in (0, 1):
        landed(alls, 13 * i + 8, whole.at[other_y, high(i)])
        landed(alls, 13 * i + 10, whole.at[other_y, low(i)])
    gradient(2)
    sums_ref[0:1] = jnp.sum(acc[0], axis=0, keepdims=True)
    sums_ref[1:2] = jnp.sum(acc[1], axis=0, keepdims=True)
    spread_far(1)
    for i in (0, 1):
        landed(alls, 13 * i + 11, whole.at[other_far, low(i)])
        landed(alls, 13 * i + 12, whole.at[other_far, high(i)])
    gradient(0, last=True)
    for copy in outward + [keep, carry]:
        copy.wait()
    for copy in sent:
        copy.wait_send()
    for step in range(zs - 1):
        for up in (True, False):

            @pl.when(sends(step, up))
            def _(step=step, up=up):
                hop(step, up).wait_send()


def turn(zs, x, w_in, w_out, gains, first, grad):
    rows = x.shape[0] // 8
    units, wide = w_out.shape
    width = gains.shape[1]
    half = rows // 2
    by_z = (zs, units, wide)
    return pl.pallas_call(
        functools.partial(turn_kernel, zs, width // (8 * zs)),
        out_shape=[
            jax.ShapeDtypeStruct((8, rows, width), BF16),
            jax.ShapeDtypeStruct((8, rows, 2 * units), BF16),
            jax.ShapeDtypeStruct(by_z, BF16),
            jax.ShapeDtypeStruct((rows, width), BF16),
            jax.ShapeDtypeStruct((rows, width), F32),
            jax.ShapeDtypeStruct((8, width), F32),
            jax.ShapeDtypeStruct(by_z, BF16),
        ],
        in_specs=[ANY, ANY, ANY, ROWS, ANY, ANY],
        out_specs=[ANY] * 3 + [ROWS] * 4,
        scratch_shapes=[
            pltpu.VMEM((rows, width), F32),
            pltpu.VMEM((rows, width), BF16),
            pltpu.VMEM(w_in.shape, BF16),
            pltpu.VMEM((8, rows, 2 * units), BF16),
            pltpu.VMEM((8, rows, units), BF16),
            pltpu.VMEM(by_z, BF16),
            pltpu.VMEM((4, 2, rows, width), BF16),
            pltpu.VMEM((4, rows, width), BF16),
            pltpu.VMEM((half, width), BF16),
            pltpu.VMEM((half, width), BF16),
            pltpu.VMEM((rows, width), BF16),
            pltpu.VMEM((rows, width), BF16),
            pltpu.VMEM((8, rows, width), BF16),
            pltpu.VMEM(by_z, F32),
            pltpu.VMEM((2, SLAB, width), F32),
            pltpu.SemaphoreType.DMA((8 * zs,)),
            pltpu.SemaphoreType.DMA((8 * zs,)),
            pltpu.SemaphoreType.DMA((26,)),
            pltpu.SemaphoreType.DMA((26,)),
            pltpu.SemaphoreType.DMA((2 * (zs - 1),)),
            pltpu.SemaphoreType.DMA((2 * (zs - 1),)),
            pltpu.SemaphoreType.DMA((10,)),
            pltpu.SemaphoreType.DMA((8,)),
        ],
        compiler_params=pltpu.CompilerParams(collective_id=1, has_side_effects=True, vmem_limit_bytes=60 * 2**20),
        cost_estimate=pl.CostEstimate(flops=0, bytes_accessed=380 * 2**20, transcendentals=0),
    )(x.reshape(8, rows, width), w_in, w_out, gains, first, grad)


def swap_kernel(zs, kinds, *refs):
    n = len(kinds)
    greet([name for _, name in swap_peers(zs, kinds)])
    swap_begin(zs, kinds, refs[:n], refs[n : 2 * n], *refs[2 * n :])()


def group_swap(name, zs, arrays, kinds):
    n = len(arrays)
    return pl.pallas_call(
        functools.partial(swap_kernel, zs, kinds),
        out_shape=swap_shapes(zs, arrays, kinds),
        in_specs=[ANY] * n,
        out_specs=[ANY] * n,
        scratch_shapes=swap_scratch(zs, kinds),
        compiler_params=pltpu.CompilerParams(collective_id=name, has_side_effects=True),
        cost_estimate=pl.CostEstimate(flops=0, bytes_accessed=50 * 2**20, transcendentals=0),
    )(*arrays)


def ff_kernel(x_ref, w_ref, hidden_ref, kept_ref):
    tile = hidden_ref.shape[1]
    projected = dot(x_ref[...], w_ref[...])
    gate, up = projected[:, :tile], projected[:, tile:]
    act, slope = gate_parts(gate)
    hidden_ref[...] = (act * up).astype(BF16)
    kept_ref[...] = jnp.concatenate([up * slope, act], axis=1).astype(BF16)


def ff_back_kernel(grad_ref, w_ref, kept_ref, out_ref):
    zs, _, wide = w_ref.shape
    d_hidden = dot_cols(grad_ref[:, :wide], w_ref[0])
    for z in range(1, zs):
        d_hidden += dot_cols(grad_ref[:, z * wide : (z + 1) * wide], w_ref[z])
    out_ref[...] = (jnp.concatenate([d_hidden, d_hidden], axis=1) * kept_ref[...].astype(F32)).astype(BF16)


FF_ROWS = 256


def ff_rows(width):
    return pl.BlockSpec((FF_ROWS, width), lambda i: (i, 0))


def ff_forward(x, w):
    rows, depth = x.shape
    wide = w.shape[1]
    return pl.pallas_call(
        ff_kernel,
        grid=(rows // FF_ROWS,),
        in_specs=[ff_rows(depth), pl.BlockSpec((depth, wide), lambda i: (0, 0))],
        out_specs=[ff_rows(wide // 2), ff_rows(wide)],
        out_shape=[jax.ShapeDtypeStruct((rows, wide // 2), BF16), jax.ShapeDtypeStruct((rows, wide), BF16)],
        compiler_params=PARAMS,
        cost_estimate=pl.CostEstimate(flops=2 * rows * depth * wide, bytes_accessed=20 * 2**20, transcendentals=0),
    )(x, w)


def ff_backward(grad, w, kept):
    rows, depth = grad.shape
    wide = kept.shape[1]
    return pl.pallas_call(
        ff_back_kernel,
        grid=(rows // FF_ROWS,),
        in_specs=[ff_rows(depth), pl.BlockSpec(w.shape, lambda i: (0, 0, 0)), ff_rows(wide)],
        out_specs=ff_rows(wide),
        out_shape=jax.ShapeDtypeStruct((rows, wide), BF16),
        compiler_params=PARAMS,
        cost_estimate=pl.CostEstimate(flops=rows * depth * wide, bytes_accessed=20 * 2**20, transcendentals=0),
    )(grad, w, kept)


def cut_kernel(in_ref, out_ref, in_blocks, out_blocks, wide):
    group, _, double = in_blocks.shape
    tile, ff = double // 2, out_ref.shape[1]
    span = group * tile
    odd = ff % 128
    live = lax.broadcasted_iota(jnp.int32, (in_ref.shape[0], span), 1) < ff
    wide[...] = jnp.zeros_like(wide)
    wide[:, : 2 * ff] = in_ref[...].astype(F32)
    gate = jnp.where(live, wide[:, :span], 0.0)
    up = pltpu.roll(wide[:, ff - odd : ff - odd + span], span - odd, 1)
    up = jnp.where(live, up, 0.0)
    wide[:, :span] = jnp.zeros_like(live, F32)
    wide[:, :ff] = out_ref[...].astype(F32)
    down = wide[:, :span]
    for g in range(group):
        at = slice(g * tile, (g + 1) * tile)
        in_blocks[g] = jnp.concatenate([gate[:, at], up[:, at]], axis=1).astype(BF16)
        out_blocks[g] = down[:, at].astype(BF16)


def cut_ff(w_in, w_out, group, tile):
    rows, ff = w_out.shape
    return pl.pallas_call(
        cut_kernel,
        grid=(rows // 16,),
        in_specs=[pl.BlockSpec((16, 2 * ff), lambda i: (i, 0)), pl.BlockSpec((16, ff), lambda i: (i, 0))],
        out_specs=[
            pl.BlockSpec((group, 16, 2 * tile), lambda i: (0, i, 0)),
            pl.BlockSpec((group, 16, tile), lambda i: (0, i, 0)),
        ],
        out_shape=[
            jax.ShapeDtypeStruct((group, rows, 2 * tile), BF16),
            jax.ShapeDtypeStruct((group, rows, tile), BF16),
        ],
        scratch_shapes=[pltpu.VMEM((16, -(-(ff + group * tile) // 128) * 128), F32)],
        compiler_params=PARAMS,
    )(w_in, w_out)


def join_kernel(in_blocks, out_blocks, in_ref, out_ref):
    group, _, double = in_blocks.shape
    tile, ff = double // 2, out_ref.shape[1]
    odd = ff % 128
    blocks = [in_blocks[g].astype(F32) for g in range(group)]
    gate = jnp.concatenate([block[:, :tile] for block in blocks], axis=1)
    up = jnp.concatenate([block[:, tile:] for block in blocks], axis=1)
    up = pltpu.roll(up, odd, 1)
    lane = lax.broadcasted_iota(jnp.int32, (up.shape[0], 128), 1)
    in_ref[:, : ff - odd] = gate[:, : ff - odd]
    in_ref[:, ff - odd : ff - odd + 128] = jnp.where(lane < odd, gate[:, ff - odd : ff - odd + 128], up[:, :128])
    in_ref[:, ff - odd + 128 :] = up[:, 128 : ff + odd]
    down = jnp.concatenate([out_blocks[g].astype(F32) for g in range(group)], axis=1)
    out_ref[...] = down[:, :ff]


def join_ff(in_blocks, out_blocks, ff):
    group, rows, tile = out_blocks.shape
    return pl.pallas_call(
        join_kernel,
        grid=(rows // 16,),
        in_specs=[
            pl.BlockSpec((group, 16, 2 * tile), lambda i: (0, i, 0)),
            pl.BlockSpec((group, 16, tile), lambda i: (0, i, 0)),
        ],
        out_specs=[pl.BlockSpec((16, 2 * ff), lambda i: (i, 0)), pl.BlockSpec((16, ff), lambda i: (i, 0))],
        out_shape=[jax.ShapeDtypeStruct((rows, 2 * ff), F32), jax.ShapeDtypeStruct((rows, ff), F32)],
        compiler_params=PARAMS,
    )(in_blocks, out_blocks)


def closing_kernel(zs, sum_ref, rows_ref, qkv_ref, dense_ref, total_ref, got, mine, lines, *refs):
    send, recv, local, line_send, line_recv = refs
    y, x, c = here()
    z = lax.axis_index("z")
    me = place(y, x, c)
    wide = got.shape[2]
    width = wide // 3
    piece = got.shape[1]
    found = swap_peers(zs, ("line",))
    greet([name for _, name in found])
    copies, comes = [], []
    for k, (peer, name) in enumerate(found[:7]):
        sems = dict(send_sem=send.at[k], recv_sem=recv.at[k], device_id=name, device_id_type=MESH)
        src = rows_ref.at[peer, :, pl.ds(0, wide)]
        copies.append(pltpu.make_async_remote_copy(src_ref=src, dst_ref=got.at[me], **sems))
        comes.append(pltpu.make_async_remote_copy(src_ref=got.at[peer], dst_ref=got.at[peer], **sems))
    for k, (peer, name) in enumerate(found[7:]):
        sems = dict(send_sem=line_send.at[k], recv_sem=line_recv.at[k], device_id=name, device_id_type=MESH)
        copies.append(pltpu.make_async_remote_copy(src_ref=sum_ref, dst_ref=lines.at[z], **sems))
        comes.append(pltpu.make_async_remote_copy(src_ref=lines.at[peer], dst_ref=lines.at[peer], **sems))
    for copy in copies:
        copy.start()
    keeps = [
        pltpu.make_async_copy(rows_ref.at[me, :, pl.ds(0, wide)], got.at[me], local.at[0]),
        pltpu.make_async_copy(sum_ref, lines.at[z], local.at[1]),
        pltpu.make_async_copy(rows_ref.at[:, :, pl.ds(wide, width)], mine, local.at[2]),
    ]
    for keep in keeps:
        keep.start()
    keeps[2].wait()
    for at in range(0, piece, 16):
        rows = jnp.concatenate([mine[g, at : at + 16] for g in range(8)], axis=1).astype(F32)
        dense_ref[at : at + 16] = rows
    for come in comes:
        come.wait_recv()
    for keep in keeps[:2]:
        keep.wait()
    for g in range(8):
        for j in range(3):
            at = pl.ds(j * D + g * width, width)
            qkv_ref[:, at] = got[g, :, j * width : (j + 1) * width].astype(F32)
    total = lines[0]
    for k in range(1, zs):
        total += lines[k]
    part = total[:, :piece]
    for k in range(1, zs):
        part = jnp.where(z == k, total[:, k * piece : (k + 1) * piece], part)
    total_ref[...] = part
    for copy in copies:
        copy.wait_send()


def closing(zs, sums, rows):
    _, piece, columns = rows.shape
    width = columns // 4
    return pl.pallas_call(
        functools.partial(closing_kernel, zs),
        out_shape=[
            jax.ShapeDtypeStruct((piece, 3 * D), F32),
            jax.ShapeDtypeStruct((piece, D), F32),
            jax.ShapeDtypeStruct((8, piece), F32),
        ],
        in_specs=[ROWS, ANY],
        out_specs=[ROWS] * 3,
        scratch_shapes=[
            pltpu.VMEM((8, piece, 3 * width), BF16),
            pltpu.VMEM((8, piece, width), BF16),
            pltpu.VMEM((zs, 8, width), F32),
            pltpu.SemaphoreType.DMA((7,)),
            pltpu.SemaphoreType.DMA((7,)),
            pltpu.SemaphoreType.DMA((3,)),
            pltpu.SemaphoreType.DMA((zs - 1,)),
            pltpu.SemaphoreType.DMA((zs - 1,)),
        ],
        compiler_params=pltpu.CompilerParams(collective_id=5, has_side_effects=True, vmem_limit_bytes=24 * 2**20),
        cost_estimate=pl.CostEstimate(flops=0, bytes_accessed=50 * 2**20, transcendentals=0),
    )(sums, rows)


def on_device(sizes, x_in, d_out, w_qkv, w_dense, w_in, w_out, gone, bone, gtwo, btwo, flags, span_start, span_len):
    gy, gx, cores, zs = sizes
    piece = w_qkv.shape[0]
    ff = w_out.shape[1]
    group = gy * gx * cores
    width = D // group
    tile = -(-ff // (group * 64)) * 64
    own = gy == 2

    def permute(array):
        lead = array.shape[:-1]
        return jnp.swapaxes(array.reshape(lead + (group, zs, piece)), -3, -2).reshape(lead + (D,))

    def restore(array):
        lead = array.shape[:-1]
        return jnp.swapaxes(array.reshape(lead + (zs, group, piece)), -3, -2).reshape(lead + (D,))

    def swap(name, arrays, kinds):
        if own:
            return group_swap(name, zs, arrays, kinds)
        ways = {
            "swap": lambda a: lax.all_to_all(a, GROUP, 0, 0, tiled=True),
            "group": lambda a: lax.all_gather(a, GROUP, axis=0),
            "line": lambda a: lax.all_gather(a, "z", axis=0),
        }
        return [ways[k](a) for a, k in zip(arrays, kinds)]

    def spread_rows(block):
        whole = group_gather(block) if own else lax.all_gather(block, GROUP, axis=0)
        return whole.reshape(group * block.shape[0], block.shape[1])

    rows_f32 = jax.ShapeDtypeStruct((SEQ_LEN, D), F32)
    rows_low = jax.ShapeDtypeStruct((SEQ_LEN, D), BF16)
    sums_type = jax.ShapeDtypeStruct((8, D), F32)

    def fold(partial):
        return lax.psum_scatter(partial.astype(BF16), GROUP, scatter_dimension=0, tiled=True).astype(F32)

    def stack_sums(*arrays):
        return jnp.pad(jnp.stack([jnp.sum(a, axis=0) for a in arrays]), ((0, 6), (0, 0)))

    def fold_one(left, right, x, gains):
        if own:
            kinds = [rows_f32, rows_f32, jax.ShapeDtypeStruct((SEQ_LEN, 128), F32)]
            whole, first, normal, inverse = group_fold(0, zs, "one", left, right, gains, [x], kinds)
            return whole.reshape(left.shape[0], D), first, normal, inverse
        first, normal, inverse = first_norm(permute(fold(dot(left, right))), x.astype(F32), gains)
        return spread_rows(first.astype(BF16)), first, normal, inverse

    def ff_turn(x, w_in, w_out, first, grad, gains):
        if own:
            whole, kept, w_out, result, d_pre, sums, d_out = turn(zs, x, w_in, w_out, gains, first, grad)
            rows = x.shape[0]
            return whole.reshape(rows, D), kept.reshape(rows, -1), w_out, result, d_pre, sums, d_out
        w_out = lax.all_gather(w_out, "z", axis=0)
        hidden, kept = ff_forward(x, w_in)
        grad = grad.astype(F32)
        right = jnp.swapaxes(w_out, 0, 1).reshape(-1, D)
        result, d_pre, terms = second_norm(fold(dot(hidden, right)), first, grad, gains)
        whole = spread_rows(d_pre.astype(BF16))
        d_out = jnp.swapaxes(dot_rows(hidden, whole).reshape(-1, zs, D // zs), 0, 1).astype(BF16)
        return whole, kept, w_out, restore(result.astype(BF16)), d_pre, stack_sums(terms, grad), d_out

    def fold_back(left, right, d_pre_two, normal, inverse, gains):
        if own:
            kinds = [rows_f32, sums_type]
            whole, d_pre, sums = group_fold(7, zs, "back", left, right, gains, [d_pre_two, normal, inverse], kinds)
            return whole.reshape(left.shape[0], D), d_pre, sums
        d_pre, terms, d_first = first_back(fold(dot_cols(left, right)), d_pre_two, normal, inverse, gains)
        return spread_rows(restore(d_pre).astype(BF16)), d_pre, stack_sums(terms, d_first)

    def fold_last(left, right, d_pre, gains, extras, kinds):
        if own:
            return group_fold(8, zs, "last", left, right, gains, [d_pre], [rows_low], extras, kinds)
        out = restore((deep_alpha * d_pre + fold(dot_cols(left, right))).astype(BF16))
        return [out] + swap(8, extras, kinds)

    def gather(block):
        return lax.all_gather(block, "z", axis=0, tiled=True)

    def scatter(partial):
        return lax.psum_scatter(partial.astype(BF16), "z", scatter_dimension=0, tiled=True)

    masked = jnp.max(flags) > 0
    prefix = jnp.where(masked, SEQ_LEN, SEQ_LEN - span_len[0])
    info = jnp.concatenate([gone, bone, gtwo, btwo, jnp.stack([prefix, span_start[0]]).astype(BF16)])
    info = jnp.pad(info[None, :], ((0, 15), (0, -info.shape[0] % 128)))

    qkv_blocks = jnp.moveaxis(w_qkv.reshape(piece, 3, group, width), 2, 0).reshape(group, piece, 3 * width)
    w_dense_part = gather(w_dense)
    qkv_blocks, info = swap(2, [qkv_blocks, info], ("swap", "group"))
    w_qkv_part = gather(qkv_blocks.reshape(group * piece, 3 * width))
    place_info = info[:, 0, 4 * piece : 4 * piece + 2].astype(jnp.int32)
    prefix, start = place_info[:, 0], place_info[:, 1]
    cosine, sine = tables(prefix, start)
    in_blocks, out_blocks = cut_ff(w_in, w_out, group, tile)
    x_perm = permute(x_in)
    x_next, qkv_blocks = lax.optimization_barrier((x_perm, qkv_blocks))
    x_all = spread_rows(x_next)
    in_blocks, out_blocks, x_all, w_dense_part = lax.optimization_barrier((in_blocks, out_blocks, x_all, w_dense_part))
    in_blocks, out_blocks, info = swap(3, [in_blocks, out_blocks, info], ("swap", "swap", "line"))
    w_in_part = gather(in_blocks.reshape(group * piece, 2 * tile))
    out_rows = out_blocks.reshape(group * piece, tile).T
    gains = info[:, :, 0, : 4 * piece].astype(F32).reshape(zs, group, 4, piece)
    gains = jnp.pad(jnp.transpose(gains, (2, 0, 1, 3)).reshape(4, D), ((0, 4), (0, 0)))
    w_qkv_part, x_all, cosine, sine, gains, out_rows = lax.optimization_barrier(
        (w_qkv_part, x_all, cosine, sine, gains, out_rows)
    )
    packed = dot(x_all, w_qkv_part)
    qkv, context = attend(prefix, packed, cosine, sine)
    first_all, first, normal_one, inverse_one = fold_one(context, w_dense_part, x_perm, gains)
    d_branch, kept, w_out_part, layer_out, d_pre_two, sums_two, d_w_out = ff_turn(
        first_all, w_in_part, out_rows, first, permute(d_out), gains
    )
    d_w_out = lax.psum_scatter(d_w_out, "z", scatter_dimension=0)
    d_projected = ff_backward(d_branch, w_out_part, kept)
    d_w_in = dot_rows(first_all, d_projected).astype(BF16)
    d_w_in, d_projected = lax.optimization_barrier((d_w_in, d_projected))
    d_w_in = scatter(d_w_in)
    d_attn, d_pre_one, sums_one = fold_back(d_projected, w_in_part, d_pre_two, normal_one, inverse_one, gains)
    d_attn, d_w_out = lax.optimization_barrier((d_attn, d_w_out))
    d_context = dot_cols(d_attn, w_dense_part).astype(BF16)
    d_packed = attend_back(prefix, qkv, d_context, cosine, sine)
    d_w_qkv = dot_rows(x_all, d_packed).astype(BF16)
    d_dense = dot_rows(context, d_attn).astype(BF16).reshape(zs, piece, group, width)
    d_dense = jnp.swapaxes(d_dense, 1, 2).reshape(D, width)
    d_w_qkv = jnp.concatenate([d_w_qkv, d_dense], axis=1)
    sums = jnp.concatenate([sums_one[:2], sums_two[:2], jnp.zeros((4, D), F32)])
    d_packed, d_w_qkv, d_w_in, sums = lax.optimization_barrier((d_packed, d_w_qkv, d_w_in, sums))
    d_w_qkv = scatter(d_w_qkv)
    d_w_in, d_w_out = d_w_in.reshape(group, piece, 2 * tile), d_w_out.T.reshape(group, piece, tile)
    d_input, d_w_in, d_w_out, sums = fold_last(
        d_packed, w_qkv_part, d_pre_one, gains, [d_w_in, d_w_out, sums], ("swap", "swap", "group")
    )
    sums = jnp.sum(sums, axis=0).reshape(8, zs, group, piece)
    sums = lax.dynamic_index_in_dim(sums, lax.axis_index(GROUP), 2, keepdims=False).reshape(8, width)
    out_in, out_out = join_ff(d_w_in, d_w_out, ff)
    out_in, out_out, d_input, d_w_qkv, sums = lax.optimization_barrier((out_in, out_out, d_input, d_w_qkv, sums))
    if own:
        out_qkv, out_dense, sums = closing(zs, sums, d_w_qkv.reshape(group, piece, 4 * width))
    else:
        out_dense = d_w_qkv[:, 3 * width :].reshape(group, piece, width)
        out_dense = jnp.swapaxes(out_dense, 0, 1).reshape(piece, D).astype(F32)
        d_w_qkv = d_w_qkv[:, : 3 * width].reshape(group, piece, 3 * width)
        d_w_qkv, sums = swap(5, [d_w_qkv, sums], ("swap", "line"))
        out_qkv = jnp.transpose(d_w_qkv.astype(F32).reshape(group, piece, 3, width), (1, 2, 0, 3))
        out_qkv = out_qkv.reshape(piece, 3 * D)
        sums = jnp.sum(sums, axis=0).reshape(8, zs, piece)
        sums = lax.dynamic_index_in_dim(sums, lax.axis_index("z"), 1, keepdims=False)
    return layer_out, d_input, out_qkv, out_dense, out_in, out_out, sums[0], sums[1], sums[2], sums[3]


def solution(mesh):
    grp, shard = mesh.shape["grp"], mesh.shape["shard"]
    sizes = (grp // 4, 2, 2, shard)
    inner = Mesh(mesh.devices.reshape(sizes), ALL)
    rows, flat = P(ALL, None), P(ALL)
    return jax.shard_map(
        functools.partial(on_device, sizes),
        mesh=inner,
        in_specs=(rows,) * 6 + (flat,) * 7,
        out_specs=(rows,) * 6 + (flat,) * 4,
        check_vma=False,
    )
```

```python
import functools

import jax
import jax.numpy as jnp
from jax import lax
from jax.experimental import pallas as pl
from jax.experimental.pallas import tpu as pltpu
from jax.sharding import Mesh
from jax.sharding import PartitionSpec as P

HEADS = 16
HEAD = 128
SEQ_LEN = 224
D = HEADS * HEAD
deep_alpha = 6.928203230275509
norm_eps = 1e-05
far_below = -1e30
scale = HEAD ** (-0.5)

ALL = ("gy", "gx", "core", "z")
GROUP = ("gy", "gx", "core")
MESH = pl.DeviceIdType.MESH
F32 = jnp.float32
BF16 = jnp.bfloat16


def dot(left, right):
    return jnp.dot(left, right, preferred_element_type=F32)


def dot_rows(left, right):
    return lax.dot_general(left, right, (((0,), (0,)), ((), ())), preferred_element_type=F32)


def dot_cols(left, right):
    return lax.dot_general(left, right, (((1,), (1,)), ((), ())), preferred_element_type=F32)


def swap_halves(block):
    lane = lax.broadcasted_iota(jnp.int32, block.shape, 1)
    return jnp.where((lane & 32) == 0, pltpu.roll(block, 96, 1), pltpu.roll(block, 32, 1))


def seen(prefix):
    row = lax.broadcasted_iota(jnp.int32, (SEQ_LEN, SEQ_LEN), 0)
    col = lax.broadcasted_iota(jnp.int32, (SEQ_LEN, SEQ_LEN), 1)
    return (col < prefix) | (col <= row)


def softmax(queries, keys, visible):
    scores = jnp.where(visible, dot_cols(queries, keys), far_below)
    weights = jnp.exp(scores - jnp.max(scores, axis=1, keepdims=True))
    return weights / jnp.sum(weights, axis=1, keepdims=True)


def attend_kernel(prefix_ref, packed_ref, cos_ref, sin_ref, qkv_ref, context_ref):
    width = context_ref.shape[1]
    visible = seen(prefix_ref[pl.program_id(0)])
    cosine = cos_ref[0]
    sine = sin_ref[0]
    for head in range(width // HEAD):
        at = pl.ds(head * HEAD, HEAD)
        at_k = pl.ds(width + head * HEAD, HEAD)
        at_v = pl.ds(2 * width + head * HEAD, HEAD)
        raw = packed_ref[:, at]
        queries = ((raw * cosine + swap_halves(raw) * sine) * scale).astype(BF16)
        raw = packed_ref[:, at_k]
        keys = (raw * cosine + swap_halves(raw) * sine).astype(BF16)
        values = packed_ref[:, at_v].astype(BF16)
        qkv_ref[:, at] = queries
        qkv_ref[:, at_k] = keys
        qkv_ref[:, at_v] = values
        probs = softmax(queries, keys, visible).astype(BF16)
        context_ref[:, at] = dot(probs, values).astype(BF16)


def attend_back_kernel(prefix_ref, qkv_ref, d_context_ref, cos_ref, sin_ref, d_packed_ref):
    width = d_context_ref.shape[1]
    visible = seen(prefix_ref[pl.program_id(0)])
    cosine = cos_ref[0]
    sine = sin_ref[0]
    for head in range(width // HEAD):
        at = pl.ds(head * HEAD, HEAD)
        at_k = pl.ds(width + head * HEAD, HEAD)
        at_v = pl.ds(2 * width + head * HEAD, HEAD)
        queries = qkv_ref[:, at]
        keys = qkv_ref[:, at_k]
        values = qkv_ref[:, at_v]
        d_context = d_context_ref[:, at]
        probs = softmax(queries, keys, visible)
        d_packed_ref[:, at_v] = dot_rows(probs.astype(BF16), d_context).astype(BF16)
        d_probs = dot_cols(d_context, values)
        inner = jnp.sum(probs * d_probs, axis=1, keepdims=True)
        d_scores = (probs * (d_probs - inner)).astype(BF16)
        grad = dot(d_scores, keys) * scale
        d_packed_ref[:, at] = (grad * cosine - swap_halves(grad) * sine).astype(BF16)
        grad = dot_rows(d_scores, queries)
        d_packed_ref[:, at_k] = (grad * cosine - swap_halves(grad) * sine).astype(BF16)


def by_sequence(width):
    return pl.BlockSpec((SEQ_LEN, width), lambda s: (s, 0))


TABLE = pl.BlockSpec((1, SEQ_LEN, HEAD), lambda s: (s, 0, 0))
SCALARS = pl.BlockSpec(memory_space=pltpu.SMEM)
PARAMS = pltpu.CompilerParams(vmem_limit_bytes=48 * 2**20)


def attend(prefix, packed, cosine, sine):
    rows, width = packed.shape[0], packed.shape[1] // 3
    return pl.pallas_call(
        attend_kernel,
        grid=(rows // SEQ_LEN,),
        in_specs=[SCALARS, by_sequence(3 * width), TABLE, TABLE],
        out_specs=[by_sequence(3 * width), by_sequence(width)],
        out_shape=[
            jax.ShapeDtypeStruct((rows, 3 * width), BF16),
            jax.ShapeDtypeStruct((rows, width), BF16),
        ],
        compiler_params=PARAMS,
    )(prefix, packed, cosine, sine)


def attend_back(prefix, qkv, d_context, cosine, sine):
    rows, width = d_context.shape
    return pl.pallas_call(
        attend_back_kernel,
        grid=(rows // SEQ_LEN,),
        in_specs=[SCALARS, by_sequence(3 * width), by_sequence(width), TABLE, TABLE],
        out_specs=by_sequence(3 * width),
        out_shape=jax.ShapeDtypeStruct((rows, 3 * width), BF16),
        compiler_params=PARAMS,
    )(prefix, qkv, d_context, cosine, sine)


def tables(prefix, start):
    place = jnp.arange(SEQ_LEN, dtype=jnp.int32)
    in_span = place[None, :] >= prefix[:, None]
    pos_one = jnp.where(in_span, start[:, None], place[None, :])
    pos_two = jnp.where(in_span, place[None, :] - prefix[:, None] + 1, 0)
    lane = jnp.arange(HEAD)
    freqs = 10000.0 ** (-2.0 * (lane % 32).astype(F32) / 64)
    place_of = jnp.where(lane[None, None, :] < 64, pos_one[:, :, None], pos_two[:, :, None])
    angles = place_of.astype(F32) * freqs
    sign = jnp.where(lane % 64 < 32, -1.0, 1.0)
    return jnp.cos(angles), jnp.sin(angles) * sign


def norm_parts(values):
    center = values - jnp.mean(values, axis=-1, keepdims=True)
    inverse = lax.rsqrt(jnp.mean(center * center, axis=-1, keepdims=True) + norm_eps)
    return center * inverse, inverse


def norm_back(normal, inverse, gain, grad):
    scaled = gain * grad
    return inverse * (
        scaled
        - jnp.mean(scaled, axis=-1, keepdims=True)
        - normal * jnp.mean(scaled * normal, axis=-1, keepdims=True)
    )


def gate_parts(gate):
    phi = 0.5 * (1.0 + lax.erf(gate * 0.7071067811865476))
    slope = phi + gate * jnp.exp(-0.5 * gate * gate) * 0.3989422804014327
    return gate * phi, slope


def here():
    return lax.axis_index("gy"), lax.axis_index("gx"), lax.axis_index("core")


def place(y, x, c):
    return (y * 2 + x) * 2 + c


def greet(peers):
    barrier = pltpu.get_barrier_semaphore()
    for peer in peers:
        pl.semaphore_signal(barrier, inc=1, device_id=peer, device_id_type=MESH)
    pl.semaphore_wait(barrier, len(peers))


def spread_block(cut, base, block_ref, out_ref, send, recv, local):
    rows = block_ref.shape[0]
    y, x, c = here()
    to_x, to_y, to_c = {"gx": 1 - x}, {"gy": 1 - y}, {"core": 1 - c}
    me, by_x, by_y, far = place(y, x, c), place(y, 1 - x, c), place(1 - y, x, c), place(1 - y, 1 - x, c)
    low, high = pl.ds(0, cut), pl.ds(cut, rows - cut)

    def push(k, src, dst, to):
        copy = pltpu.make_async_remote_copy(
            src_ref=src, dst_ref=dst, send_sem=send.at[base + k], recv_sem=recv.at[base + k], device_id=to, device_id_type=MESH
        )
        copy.start()
        return copy

    def landed(k, dst):
        pltpu.make_async_remote_copy(
            src_ref=dst, dst_ref=dst, send_sem=send.at[base + k], recv_sem=recv.at[base + k], device_id=to_c, device_id_type=MESH
        ).wait_recv()

    sent = [
        push(0, block_ref.at[low], out_ref.at[me, low], to_x),
        push(1, block_ref.at[high], out_ref.at[me, high], to_y),
        push(2, block_ref.at[high], out_ref.at[me, high], to_x),
        push(3, block_ref.at[low], out_ref.at[me, low], to_y),
        push(4, block_ref, out_ref.at[me], to_c),
    ]
    keep = pltpu.make_async_copy(block_ref, out_ref.at[me], local)
    keep.start()
    landed(0, out_ref.at[by_x, low])
    sent.append(push(5, out_ref.at[by_x, low], out_ref.at[by_x, low], to_y))
    sent.append(push(7, out_ref.at[by_x, low], out_ref.at[by_x, low], to_c))
    landed(1, out_ref.at[by_y, high])
    sent.append(push(6, out_ref.at[by_y, high], out_ref.at[by_y, high], to_x))
    sent.append(push(8, out_ref.at[by_y, high], out_ref.at[by_y, high], to_c))
    landed(2, out_ref.at[by_x, high])
    sent.append(push(9, out_ref.at[by_x, high], out_ref.at[by_x, high], to_c))
    landed(3, out_ref.at[by_y, low])
    sent.append(push(10, out_ref.at[by_y, low], out_ref.at[by_y, low], to_c))
    landed(5, out_ref.at[far, low])
    sent.append(push(11, out_ref.at[far, low], out_ref.at[far, low], to_c))
    landed(6, out_ref.at[far, high])
    sent.append(push(12, out_ref.at[far, high], out_ref.at[far, high], to_c))
    other, other_x, other_y, other_far = (
        place(y, x, 1 - c),
        place(y, 1 - x, 1 - c),
        place(1 - y, x, 1 - c),
        place(1 - y, 1 - x, 1 - c),
    )
    landed(4, out_ref.at[other])
    landed(7, out_ref.at[other_x, low])
    landed(8, out_ref.at[other_y, high])
    landed(9, out_ref.at[other_x, high])
    landed(10, out_ref.at[other_y, low])
    landed(11, out_ref.at[other_far, low])
    landed(12, out_ref.at[other_far, high])
    keep.wait()
    for copy in sent:
        copy.wait_send()


def gather_kernel(cut, block_ref, out_ref, send, recv, local):
    y, x, c = here()
    greet([{"gx": 1 - x}, {"gy": 1 - y}, {"core": 1 - c}])
    spread_block(cut, 0, block_ref, out_ref, send, recv, local)


ANY = pl.BlockSpec(memory_space=pl.ANY)


def group_gather(block):
    rows, width = block.shape
    return pl.pallas_call(
        functools.partial(gather_kernel, rows // 2),
        out_shape=jax.ShapeDtypeStruct((8, rows, width), block.dtype),
        in_specs=[ANY],
        out_specs=ANY,
        scratch_shapes=[pltpu.SemaphoreType.DMA((13,)), pltpu.SemaphoreType.DMA((13,)), pltpu.SemaphoreType.DMA],
        compiler_params=pltpu.CompilerParams(collective_id=9, has_side_effects=True),
        cost_estimate=pl.CostEstimate(flops=0, bytes_accessed=100 * 2**20, transcendentals=0),
    )(block)


def swap_peers(zs, kinds):
    y, x, c = here()
    z = lax.axis_index("z")
    found = []
    for k in range(1, 8):
        peer = ((y + k // 4) % 2, (x + k // 2 % 2) % 2, (c + k % 2) % 2)
        found.append((place(*peer), {"gy": peer[0], "gx": peer[1], "core": peer[2]}))
    if "line" in kinds:
        found += [((z + k) % zs, {"z": (z + k) % zs}) for k in range(1, zs)]
    return found


def swap_begin(zs, kinds, blocks, outs, send, recv, local):
    copies, comes, keeps = [], [], []
    found = swap_peers(zs, kinds)
    for i, kind in enumerate(kinds):
        me = lax.axis_index("z") if kind == "line" else place(*here())
        for k, (peer, name) in enumerate(found[7:] if kind == "line" else found[:7]):
            src = blocks[i].at[peer] if kind == "swap" else blocks[i]
            landing = outs[i].at[peer]
            sems = dict(send_sem=send.at[i, k], recv_sem=recv.at[i, k], device_id=name, device_id_type=MESH)
            copies.append(pltpu.make_async_remote_copy(src_ref=src, dst_ref=outs[i].at[me], **sems))
            comes.append(pltpu.make_async_remote_copy(src_ref=landing, dst_ref=landing, **sems))
            copies[-1].start()
        own = blocks[i].at[me] if kind == "swap" else blocks[i]
        keeps.append(pltpu.make_async_copy(own, outs[i].at[me], local.at[i]))
        keeps[-1].start()

    def finish():
        for come in comes:
            come.wait_recv()
        for copy in copies:
            copy.wait_send()
        for keep in keeps:
            keep.wait()

    return finish


SWAP_LEAD = {"swap": lambda zs: (), "group": lambda zs: (8,), "line": lambda zs: (zs,)}


def swap_shapes(zs, arrays, kinds):
    return [jax.ShapeDtypeStruct(SWAP_LEAD[k](zs) + a.shape, a.dtype) for a, k in zip(arrays, kinds)]


def swap_scratch(zs, kinds):
    n, most = len(kinds), max(7, zs - 1)
    return [
        pltpu.SemaphoreType.DMA((n, most)),
        pltpu.SemaphoreType.DMA((n, most)),
        pltpu.SemaphoreType.DMA((n,)),
    ]


SLAB = 16
ROWS = pl.BlockSpec(memory_space=pltpu.VMEM)
CHIP_COLS = 256


def by_rows(value, zs, piece):
    group = D // (zs * piece)
    order = [g * zs + z for z in range(zs) for g in range(group)]
    return jnp.concatenate([value[:, m * piece : (m + 1) * piece] for m in order], axis=1)


def in_order(value, zs, piece):
    group = D // (zs * piece)
    order = [z * group + g for g in range(group) for z in range(zs)]
    return jnp.concatenate([value[:, m * piece : (m + 1) * piece] for m in order], axis=1)


def first_norm(total, x, gains):
    normal, inverse = norm_parts(deep_alpha * x + total)
    first = normal * gains[0:1] + gains[1:2]
    return first, normal, inverse


def second_norm(total, first, grad, gains):
    normal, inverse = norm_parts(deep_alpha * first + total)
    return normal * gains[2:3] + gains[3:4], norm_back(normal, inverse, gains[2:3], grad), grad * normal


def first_back(total, d_pre_two, normal, inverse, gains):
    d_first = deep_alpha * d_pre_two + total
    return norm_back(normal, inverse, gains[0:1], d_first), d_first * normal, d_first


def fold_kernel(mode, across, zs, piece, n_aux, n_out, kinds, *refs):
    left_ref, right_ref, gains_ref = refs[:3]
    aux_refs = refs[3 : 3 + n_aux]
    refs = refs[3 + n_aux :]
    n_swap = len(kinds)
    swap_in, refs = refs[:n_swap], refs[n_swap:]
    spread = mode != "last"
    if spread:
        all_ref, refs = refs[0], refs[1:]
    outs, refs = refs[:n_out], refs[n_out:]
    swap_out, refs = refs[:n_swap], refs[n_swap:]
    aux, refs = refs[:n_aux], refs[n_aux:]
    left, right, part, got, near_x, near_y, from_x, from_y, block, acc, send, recv, local = refs[:13]
    rows, width = block.shape
    cut = near_x.shape[0]
    y, x, c = here()
    to_x, to_y, to_c = {"gx": 1 - x}, {"gy": 1 - y}, {"core": 1 - c}
    chips = [(1 - y, 1 - x), (y, 1 - x), (1 - y, x), (y, x)]
    low, high = pl.ds(0, cut), pl.ds(cut, rows - cut)

    def push(k, src, dst, to):
        copy = pltpu.make_async_remote_copy(
            src_ref=src, dst_ref=dst, send_sem=send.at[k], recv_sem=recv.at[k], device_id=to, device_id_type=MESH
        )
        copy.start()
        return copy

    def add(k, extra, start, size, offset=0):
        @pl.loop(0, size // SLAB)
        def _(step):
            at = pl.ds(pl.multiple_of(start + step * SLAB, SLAB), SLAB)
            of = pl.ds(pl.multiple_of(start - offset + step * SLAB, SLAB), SLAB)
            part[k, c, at] = (part[k, c, at].astype(F32) + extra[of].astype(F32)).astype(BF16)

    loads = [pltpu.make_async_copy(left_ref.at[a * 2 + b], left.at[k], local.at[k]) for k, (a, b) in enumerate(chips)]
    load_right = pltpu.make_async_copy(right_ref, right, local.at[4])
    load_aux = [pltpu.make_async_copy(r, v, local.at[5 + k]) for k, (r, v) in enumerate(zip(aux_refs, aux))]
    loads[0].start()
    load_right.start()
    for load in loads[1:] + load_aux:
        load.start()
    if n_swap:
        greet([name for _, name in swap_peers(1, kinds)])
        swap_finish = swap_begin(1, kinds, swap_in, swap_out, *refs[13:])
    else:
        greet([to_x, to_y, to_c])

    def product(k):
        loads[k].wait()

        @pl.loop(0, width // CHIP_COLS)
        def _(step):
            at = pl.ds(pl.multiple_of(step * CHIP_COLS, CHIP_COLS), CHIP_COLS)
            here_part = dot_cols(left[k], right[at]) if across else dot(left[k], right[:, at])
            part[k, 0, :, at] = here_part[:rows].astype(BF16)
            part[k, 1, :, at] = here_part[rows:].astype(BF16)

        return push(k, part.at[k, 1 - c], got.at[k], to_c)

    load_right.wait()
    sent = [product(0), product(1)]
    sent[0].wait_recv()
    add(0, got.at[0], 0, rows)
    far_x = push(4, part.at[0, c, low], near_x, to_x)
    far_y = push(5, part.at[0, c, high], near_y, to_y)
    sent.append(product(2))
    sent[1].wait_recv()
    add(1, got.at[1], 0, rows)
    plain_x = push(6, part.at[1, c, low], from_x.at[low], to_x)
    sent[2].wait_recv()
    add(2, got.at[2], 0, rows)
    plain_y = push(7, part.at[2, c, high], from_y.at[high], to_y)
    sent.append(product(3))
    far_y.wait_recv()
    add(1, near_y, cut, rows - cut, cut)
    more_x = push(8, part.at[1, c, high], from_x.at[high], to_x)
    far_x.wait_recv()
    add(2, near_x, 0, cut)
    more_y = push(9, part.at[2, c, low], from_y.at[low], to_y)
    sent[3].wait_recv()
    for load in load_aux:
        load.wait()
    plain_x.wait_recv()
    plain_y.wait_recv()
    more_x.wait_recv()
    more_y.wait_recv()
    gains = gains_ref[...]
    acc[...] = jnp.zeros_like(acc)

    @pl.loop(0, rows // SLAB)
    def _(step):
        at = pl.ds(pl.multiple_of(step * SLAB, SLAB), SLAB)
        total = part[3, c, at].astype(F32) + got[3, at].astype(F32) + from_x[at].astype(F32) + from_y[at].astype(F32)
        held = [a[at].astype(F32) for a in aux]
        if mode == "one":
            first, normal, inverse = first_norm(by_rows(total, zs, piece), held[0], gains)
            outs[0][at] = first
            outs[1][at] = normal
            outs[2][at] = jnp.broadcast_to(inverse, (SLAB, 128))
            block[at] = first.astype(BF16)
        elif mode == "back":
            d_pre, terms, d_first = first_back(total, held[0], held[1], held[2][:, 0:1], gains)
            outs[0][at] = d_pre
            block[at] = in_order(d_pre, zs, piece).astype(BF16)
            acc[0] += terms
            acc[1] += d_first
        else:
            outs[0][at] = in_order(deep_alpha * held[0] + total, zs, piece).astype(BF16)

    if mode == "back":
        outs[-1][0:1] = jnp.sum(acc[0], axis=0, keepdims=True)
        outs[-1][1:2] = jnp.sum(acc[1], axis=0, keepdims=True)
    for copy in sent + [far_x, far_y, plain_x, plain_y, more_x, more_y]:
        copy.wait_send()
    if n_swap:
        swap_finish()
    if spread:
        spread_block(cut, 10, block, all_ref, send, recv, local.at[4])


def group_fold(name, zs, mode, left, right, gains, aux, out_types, extras=(), kinds=()):
    across = mode != "one"
    rows, depth = left.shape[0] // 8, left.shape[1]
    width = gains.shape[1]
    cut = rows // 2
    spread = mode != "last"
    out_shape = [jax.ShapeDtypeStruct((8, rows, width), BF16)] * spread + out_types
    n, n_swap = len(aux), len(extras)
    n_sems = 23 if spread else 10
    return pl.pallas_call(
        functools.partial(fold_kernel, mode, across, zs, width // (8 * zs), n, len(out_types), kinds),
        out_shape=out_shape + swap_shapes(1, extras, kinds),
        in_specs=[ANY, ANY, ROWS] + [ANY] * (n + n_swap),
        out_specs=[ANY] * spread + [ROWS] * len(out_types) + [ANY] * n_swap,
        scratch_shapes=[pltpu.VMEM(a.shape, a.dtype) for a in aux]
        + [
            pltpu.VMEM((4, 2 * rows, depth), BF16),
            pltpu.VMEM(right.shape, BF16),
            pltpu.VMEM((4, 2, rows, width), BF16),
            pltpu.VMEM((4, rows, width), BF16),
            pltpu.VMEM((cut, width), BF16),
            pltpu.VMEM((rows - cut, width), BF16),
            pltpu.VMEM((rows, width), BF16),
            pltpu.VMEM((rows, width), BF16),
            pltpu.VMEM((rows, width), BF16),
            pltpu.VMEM((2, SLAB, width), F32),
            pltpu.SemaphoreType.DMA((n_sems,)),
            pltpu.SemaphoreType.DMA((n_sems,)),
            pltpu.SemaphoreType.DMA((5 + n,)),
        ]
        + (swap_scratch(1, kinds) if n_swap else []),
        compiler_params=pltpu.CompilerParams(
            collective_id=name, has_side_effects=True, vmem_limit_bytes=50 * 2**20
        ),
        cost_estimate=pl.CostEstimate(flops=0, bytes_accessed=(200 if spread else 110) * 2**20, transcendentals=0),
    )(left.reshape(4, 2 * rows, depth), right, gains, *aux, *extras)


def turn_kernel(
    zs, piece, x_ref, in_ref, out_ref, gains_ref, first_ref, grad_ref,
    all_ref, kept_ref, right_ref, result_ref, d_pre_ref, sums_ref, dw_ref,
    first, grad, w_in, kept, left, right, part, got, near_x, near_y, from_x, from_y, whole, dw, acc,
    fold_send, fold_recv, all_send, all_recv, line_send, line_recv, local, x_local
):
    rows = first.shape[0]
    tile = left.shape[2]
    wide = right.shape[2]
    y, x, c = here()
    z = lax.axis_index("z")
    to_x, to_y, to_c = {"gx": 1 - x}, {"gy": 1 - y}, {"core": 1 - c}
    chips = [(1 - y) * 2 + 1 - x, y * 2 + 1 - x, (1 - y) * 2 + x, y * 2 + x]
    me, by_x, by_y, far = place(y, x, c), place(y, 1 - x, c), place(1 - y, x, c), place(1 - y, 1 - x, c)
    other, other_x, other_y, other_far = (
        place(y, x, 1 - c),
        place(y, 1 - x, 1 - c),
        place(1 - y, x, 1 - c),
        place(1 - y, 1 - x, 1 - c),
    )
    half = rows // 2
    most = -(-half // (2 * SLAB)) * SLAB
    lows = [(0, most), (half, half - most)]
    highs = [(most, half - most), (2 * half - most, most)]
    top, bottom = pl.ds(0, half), pl.ds(half, half)
    sent = []

    def remote(sems, k, src, dst, to):
        return pltpu.make_async_remote_copy(
            src_ref=src,
            dst_ref=dst,
            send_sem=sems[0].at[k],
            recv_sem=sems[1].at[k],
            device_id=to,
            device_id_type=MESH,
        )

    def push(sems, k, src, dst, to):
        copy = remote(sems, k, src, dst, to)
        copy.start()
        sent.append(copy)

    def landed(sems, k, dst):
        remote(sems, k, dst, dst, to_c).wait_recv()

    folds, alls, lines = (fold_send, fold_recv), (all_send, all_recv), (line_send, line_recv)

    load_out = pltpu.make_async_copy(out_ref, right.at[z], local.at[0])
    load_in = pltpu.make_async_copy(in_ref, w_in, local.at[1])
    load_first = pltpu.make_async_copy(first_ref, first, local.at[2])
    load_grad = pltpu.make_async_copy(grad_ref, grad, local.at[3])

    def load_x(g):
        return pltpu.make_async_copy(x_ref.at[g], whole.at[g], x_local.at[g])

    load_out.start()
    load_in.start()
    for g in range(8):
        load_x(g).start()
    load_first.start()
    load_grad.start()

    barrier = pltpu.get_barrier_semaphore()
    for to in (to_x, to_y, to_c):
        pl.semaphore_signal(barrier, inc=1, device_id=to, device_id_type=MESH)

    @pl.when(z > 0)
    def _():
        pl.semaphore_signal(barrier, inc=1, device_id={"z": z - 1}, device_id_type=MESH)

    @pl.when(z < zs - 1)
    def _():
        pl.semaphore_signal(barrier, inc=1, device_id={"z": z + 1}, device_id_type=MESH)

    inside = (z > 0) & (z < zs - 1)

    @pl.when(inside)
    def _():
        pl.semaphore_wait(barrier, 5)

    @pl.when(jnp.logical_not(inside))
    def _():
        pl.semaphore_wait(barrier, 4)

    def shard_of(step, up):
        return z - step if up else z + step

    def hop(step, up):
        ref = right.at[shard_of(step, up)]
        return remote(lines, 2 * step + (0 if up else 1), ref, ref, {"z": z + 1 if up else z - 1})

    def sends(step, up):
        return (z >= step) & (z < zs - 1) if up else (z <= zs - 1 - step) & (z > 0)

    def gets(step, up):
        return z >= step + 1 if up else z <= zs - 2 - step

    def line_serve(step):
        for up in (True, False):

            @pl.when(gets(step - 1, up) & sends(step, up))
            def _(up=up):
                landed(lines, 2 * (step - 1) + (0 if up else 1), right.at[shard_of(step, up)])
                hop(step, up).start()

    def line_take(step):
        for up in (True, False):

            @pl.when(gets(step - 1, up) & jnp.logical_not(sends(step, up)))
            def _(up=up):
                landed(lines, 2 * (step - 1) + (0 if up else 1), right.at[shard_of(step, up)])

    load_out.wait()
    for up in (True, False):

        @pl.when(sends(0, up))
        def _(up=up):
            hop(0, up).start()


    load_in.wait()

    @pl.loop(0, 8)
    def _(g):
        @pl.when(g == 6)
        def _():
            line_serve(1)

        load_x(g).wait()
        projected = dot(whole[g], w_in[...])
        gate, up = projected[:, :tile], projected[:, tile:]
        act, slope = gate_parts(gate)
        left[g] = (act * up).astype(BF16)
        kept[g] = jnp.concatenate([up * slope, act], axis=1).astype(BF16)

    keep = pltpu.make_async_copy(kept, kept_ref, local.at[4])
    keep.start()

    def add(k, extra, start, offset, at):
        @pl.loop(0, half // SLAB)
        def _(step):
            row = pl.ds(pl.multiple_of(start + step * SLAB, SLAB), SLAB)
            of = pl.ds(pl.multiple_of(start - offset + step * SLAB, SLAB), SLAB)
            part[k, c, row, at] = (part[k, c, row, at].astype(F32) + extra[of, at].astype(F32)).astype(BF16)

    def chip_sum(k, at):
        add(k, got.at[k], 0, 0, at)
        add(k, got.at[k], half, 0, at)

    def product(k, block, at):
        found = dot(left[pl.ds(2 * chips[k], 2)].reshape(2 * rows, tile), right[block])
        part[k, 0, :, at] = found[:rows].astype(BF16)
        part[k, 1, :, at] = found[rows:].astype(BF16)

    def block_at(i):
        if i == 0:
            return z
        below = z < zs // 2
        near = jnp.where(below, z, zs - 1 - z)
        spot = jnp.where(i <= 2 * near, jnp.where(i % 2 == 1, near - (i + 1) // 2, near + i // 2), i)
        return jnp.where(below, spot, zs - 1 - spot)

    def block_cols(i):
        return pl.ds(pl.multiple_of(block_at(i) * wide, wide), wide)

    def fold_start(i):
        b, block, at = 8 * i, block_at(i), block_cols(i)
        rest = pl.ds(1, 3)
        product(0, block, at)
        push(folds, b, part.at[0, 1 - c, :, at], got.at[0, :, at], to_c)
        for k in (1, 2, 3):
            product(k, block, at)
        push(folds, b + 1, part.at[rest, 1 - c, :, at], got.at[rest, :, at], to_c)
        landed(folds, b, got.at[0, :, at])
        chip_sum(0, at)
        push(folds, b + 2, part.at[0, c, top, at], near_x.at[:, at], to_x)
        push(folds, b + 3, part.at[0, c, bottom, at], near_y.at[:, at], to_y)
        landed(folds, b + 1, got.at[rest, :, at])
        chip_sum(1, at)
        push(folds, b + 4, part.at[1, c, top, at], from_x.at[top, at], to_x)
        chip_sum(2, at)
        push(folds, b + 5, part.at[2, c, bottom, at], from_y.at[bottom, at], to_y)

    def fold_end(i):
        b, at = 8 * i, block_cols(i)
        landed(folds, b + 3, near_y.at[:, at])
        add(1, near_y, half, half, at)
        push(folds, b + 6, part.at[1, c, bottom, at], from_x.at[bottom, at], to_x)
        landed(folds, b + 2, near_x.at[:, at])
        add(2, near_x, 0, 0, at)
        push(folds, b + 7, part.at[2, c, top, at], from_y.at[top, at], to_y)

    gains = gains_ref[...]
    line_take(1)
    fold_start(0)
    fold_start(1)
    fold_end(0)
    for i in range(2, zs):
        if i < zs - 1:
            line_serve(i)
        fold_end(i - 1)
        line_take(i)
        fold_start(i)
    fold_end(zs - 1)
    carry = pltpu.make_async_copy(right, right_ref, local.at[5])
    carry.start()
    load_first.wait()
    load_grad.wait()
    acc[...] = jnp.zeros_like(acc)
    for i in range(zs):
        at = block_cols(i)
        landed(folds, 8 * i + 4, from_x.at[top, at])
        landed(folds, 8 * i + 5, from_y.at[bottom, at])
        landed(folds, 8 * i + 6, from_x.at[bottom, at])
        landed(folds, 8 * i + 7, from_y.at[top, at])

    def low(i):
        return pl.ds(*lows[i])

    def high(i):
        return pl.ds(*highs[i])

    def span(i):
        return pl.ds(i * half, half)

    def norm(i):
        @pl.loop(0, half // SLAB)
        def _(step):
            at = pl.ds(pl.multiple_of(i * half + step * SLAB, SLAB), SLAB)
            total = part[3, c, at].astype(F32) + got[3, at].astype(F32)
            total += from_x[at].astype(F32) + from_y[at].astype(F32)
            dy = grad[at].astype(F32)
            result, d_pre, terms = second_norm(total, first[at], dy, gains)
            result_ref[at] = in_order(result, zs, piece).astype(BF16)
            d_pre_ref[at] = d_pre
            whole[me, at] = d_pre.astype(BF16)
            acc[0] += terms
            acc[1] += dy

        b = 13 * i
        push(alls, b, whole.at[me, low(i)], whole.at[me, low(i)], to_x)
        push(alls, b + 1, whole.at[me, high(i)], whole.at[me, high(i)], to_y)
        push(alls, b + 2, whole.at[me, high(i)], whole.at[me, high(i)], to_x)
        push(alls, b + 3, whole.at[me, low(i)], whole.at[me, low(i)], to_y)
        push(alls, b + 4, whole.at[me, span(i)], whole.at[me, span(i)], to_c)

    def pass_on(i, k, slot, at, onward):
        ref = whole.at[slot, at]
        landed(alls, 13 * i + k, ref)
        for where, to in onward:
            push(alls, 13 * i + where, ref, ref, to)

    def spread_first(i):
        pass_on(i, 0, by_x, low(i), [(5, to_y), (7, to_c)])
        pass_on(i, 1, by_y, high(i), [(6, to_x), (8, to_c)])

    def spread_rest(i):
        pass_on(i, 2, by_x, high(i), [(9, to_c)])
        pass_on(i, 3, by_y, low(i), [(10, to_c)])

    def spread_far(i):
        pass_on(i, 5, far, low(i), [(11, to_c)])
        pass_on(i, 6, far, high(i), [(12, to_c)])

    outward = []

    def gradient(k, last=False, first_one=False):
        pair = pl.ds(2 * chips[k], 2)
        outward.append(pltpu.make_async_copy(whole.at[pair], all_ref.at[pair], local.at[6 + k]))
        outward[-1].start()

        @pl.loop(0, zs)
        def _(block):
            at = pl.ds(pl.multiple_of(block * wide, wide), wide)
            found = dot_rows(left[pair].reshape(2 * rows, tile), whole[pair, :, at].reshape(2 * rows, wide))
            if first_one:
                dw[block] = found
            elif last:
                dw_ref[block] = (dw[block] + found).astype(BF16)
            else:
                dw[block] += found

    norm(0)
    norm(1)
    spread_first(0)
    for i in (0, 1):
        landed(alls, 13 * i + 4, whole.at[other, span(i)])
    gradient(3, first_one=True)
    spread_rest(0)
    spread_first(1)
    spread_rest(1)
    for i in (0, 1):
        landed(alls, 13 * i + 7, whole.at[other_x, low(i)])
        landed(alls, 13 * i + 9, whole.at[other_x, high(i)])
    gradient(1)
    spread_far(0)
    for i in (0, 1):
        landed(alls, 13 * i + 8, whole.at[other_y, high(i)])
        landed(alls, 13 * i + 10, whole.at[other_y, low(i)])
    gradient(2)
    sums_ref[0:1] = jnp.sum(acc[0], axis=0, keepdims=True)
    sums_ref[1:2] = jnp.sum(acc[1], axis=0, keepdims=True)
    spread_far(1)
    for i in (0, 1):
        landed(alls, 13 * i + 11, whole.at[other_far, low(i)])
        landed(alls, 13 * i + 12, whole.at[other_far, high(i)])
    gradient(0, last=True)
    for copy in outward + [keep, carry]:
        copy.wait()
    for copy in sent:
        copy.wait_send()
    for step in range(zs - 1):
        for up in (True, False):

            @pl.when(sends(step, up))
            def _(step=step, up=up):
                hop(step, up).wait_send()


def turn(zs, x, w_in, w_out, gains, first, grad):
    rows = x.shape[0] // 8
    units, wide = w_out.shape
    width = gains.shape[1]
    half = rows // 2
    by_z = (zs, units, wide)
    return pl.pallas_call(
        functools.partial(turn_kernel, zs, width // (8 * zs)),
        out_shape=[
            jax.ShapeDtypeStruct((8, rows, width), BF16),
            jax.ShapeDtypeStruct((8, rows, 2 * units), BF16),
            jax.ShapeDtypeStruct(by_z, BF16),
            jax.ShapeDtypeStruct((rows, width), BF16),
            jax.ShapeDtypeStruct((rows, width), F32),
            jax.ShapeDtypeStruct((8, width), F32),
            jax.ShapeDtypeStruct(by_z, BF16),
        ],
        in_specs=[ANY, ANY, ANY, ROWS, ANY, ANY],
        out_specs=[ANY] * 3 + [ROWS] * 4,
        scratch_shapes=[
            pltpu.VMEM((rows, width), F32),
            pltpu.VMEM((rows, width), BF16),
            pltpu.VMEM(w_in.shape, BF16),
            pltpu.VMEM((8, rows, 2 * units), BF16),
            pltpu.VMEM((8, rows, units), BF16),
            pltpu.VMEM(by_z, BF16),
            pltpu.VMEM((4, 2, rows, width), BF16),
            pltpu.VMEM((4, rows, width), BF16),
            pltpu.VMEM((half, width), BF16),
            pltpu.VMEM((half, width), BF16),
            pltpu.VMEM((rows, width), BF16),
            pltpu.VMEM((rows, width), BF16),
            pltpu.VMEM((8, rows, width), BF16),
            pltpu.VMEM(by_z, F32),
            pltpu.VMEM((2, SLAB, width), F32),
            pltpu.SemaphoreType.DMA((8 * zs,)),
            pltpu.SemaphoreType.DMA((8 * zs,)),
            pltpu.SemaphoreType.DMA((26,)),
            pltpu.SemaphoreType.DMA((26,)),
            pltpu.SemaphoreType.DMA((2 * (zs - 1),)),
            pltpu.SemaphoreType.DMA((2 * (zs - 1),)),
            pltpu.SemaphoreType.DMA((10,)),
            pltpu.SemaphoreType.DMA((8,)),
        ],
        compiler_params=pltpu.CompilerParams(collective_id=1, has_side_effects=True, vmem_limit_bytes=60 * 2**20),
        cost_estimate=pl.CostEstimate(flops=0, bytes_accessed=380 * 2**20, transcendentals=0),
    )(x.reshape(8, rows, width), w_in, w_out, gains, first, grad)


def swap_kernel(zs, kinds, *refs):
    n = len(kinds)
    greet([name for _, name in swap_peers(zs, kinds)])
    swap_begin(zs, kinds, refs[:n], refs[n : 2 * n], *refs[2 * n :])()


def group_swap(name, zs, arrays, kinds):
    n = len(arrays)
    return pl.pallas_call(
        functools.partial(swap_kernel, zs, kinds),
        out_shape=swap_shapes(zs, arrays, kinds),
        in_specs=[ANY] * n,
        out_specs=[ANY] * n,
        scratch_shapes=swap_scratch(zs, kinds),
        compiler_params=pltpu.CompilerParams(collective_id=name, has_side_effects=True),
        cost_estimate=pl.CostEstimate(flops=0, bytes_accessed=50 * 2**20, transcendentals=0),
    )(*arrays)


def ff_kernel(x_ref, w_ref, hidden_ref, kept_ref):
    tile = hidden_ref.shape[1]
    projected = dot(x_ref[...], w_ref[...])
    gate, up = projected[:, :tile], projected[:, tile:]
    act, slope = gate_parts(gate)
    hidden_ref[...] = (act * up).astype(BF16)
    kept_ref[...] = jnp.concatenate([up * slope, act], axis=1).astype(BF16)


def ff_back_kernel(grad_ref, w_ref, kept_ref, out_ref):
    zs, _, wide = w_ref.shape
    d_hidden = dot_cols(grad_ref[:, :wide], w_ref[0])
    for z in range(1, zs):
        d_hidden += dot_cols(grad_ref[:, z * wide : (z + 1) * wide], w_ref[z])
    out_ref[...] = (jnp.concatenate([d_hidden, d_hidden], axis=1) * kept_ref[...].astype(F32)).astype(BF16)


FF_ROWS = 256


def ff_rows(width):
    return pl.BlockSpec((FF_ROWS, width), lambda i: (i, 0))


def ff_forward(x, w):
    rows, depth = x.shape
    wide = w.shape[1]
    return pl.pallas_call(
        ff_kernel,
        grid=(rows // FF_ROWS,),
        in_specs=[ff_rows(depth), pl.BlockSpec((depth, wide), lambda i: (0, 0))],
        out_specs=[ff_rows(wide // 2), ff_rows(wide)],
        out_shape=[jax.ShapeDtypeStruct((rows, wide // 2), BF16), jax.ShapeDtypeStruct((rows, wide), BF16)],
        compiler_params=PARAMS,
        cost_estimate=pl.CostEstimate(flops=2 * rows * depth * wide, bytes_accessed=20 * 2**20, transcendentals=0),
    )(x, w)


def ff_backward(grad, w, kept):
    rows, depth = grad.shape
    wide = kept.shape[1]
    return pl.pallas_call(
        ff_back_kernel,
        grid=(rows // FF_ROWS,),
        in_specs=[ff_rows(depth), pl.BlockSpec(w.shape, lambda i: (0, 0, 0)), ff_rows(wide)],
        out_specs=ff_rows(wide),
        out_shape=jax.ShapeDtypeStruct((rows, wide), BF16),
        compiler_params=PARAMS,
        cost_estimate=pl.CostEstimate(flops=rows * depth * wide, bytes_accessed=20 * 2**20, transcendentals=0),
    )(grad, w, kept)


def cut_kernel(in_ref, out_ref, in_blocks, out_blocks, wide):
    group, _, double = in_blocks.shape
    tile, ff = double // 2, out_ref.shape[1]
    span = group * tile
    odd = ff % 128
    live = lax.broadcasted_iota(jnp.int32, (in_ref.shape[0], span), 1) < ff
    wide[...] = jnp.zeros_like(wide)
    wide[:, : 2 * ff] = in_ref[...].astype(F32)
    gate = jnp.where(live, wide[:, :span], 0.0)
    up = pltpu.roll(wide[:, ff - odd : ff - odd + span], span - odd, 1)
    up = jnp.where(live, up, 0.0)
    wide[:, :span] = jnp.zeros_like(live, F32)
    wide[:, :ff] = out_ref[...].astype(F32)
    down = wide[:, :span]
    for g in range(group):
        at = slice(g * tile, (g + 1) * tile)
        in_blocks[g] = jnp.concatenate([gate[:, at], up[:, at]], axis=1).astype(BF16)
        out_blocks[g] = down[:, at].astype(BF16)


def cut_ff(w_in, w_out, group, tile):
    rows, ff = w_out.shape
    return pl.pallas_call(
        cut_kernel,
        grid=(rows // 16,),
        in_specs=[pl.BlockSpec((16, 2 * ff), lambda i: (i, 0)), pl.BlockSpec((16, ff), lambda i: (i, 0))],
        out_specs=[
            pl.BlockSpec((group, 16, 2 * tile), lambda i: (0, i, 0)),
            pl.BlockSpec((group, 16, tile), lambda i: (0, i, 0)),
        ],
        out_shape=[
            jax.ShapeDtypeStruct((group, rows, 2 * tile), BF16),
            jax.ShapeDtypeStruct((group, rows, tile), BF16),
        ],
        scratch_shapes=[pltpu.VMEM((16, -(-(ff + group * tile) // 128) * 128), F32)],
        compiler_params=PARAMS,
    )(w_in, w_out)


def join_kernel(in_blocks, out_blocks, in_ref, out_ref):
    group, _, double = in_blocks.shape
    tile, ff = double // 2, out_ref.shape[1]
    odd = ff % 128
    blocks = [in_blocks[g].astype(F32) for g in range(group)]
    gate = jnp.concatenate([block[:, :tile] for block in blocks], axis=1)
    up = jnp.concatenate([block[:, tile:] for block in blocks], axis=1)
    up = pltpu.roll(up, odd, 1)
    lane = lax.broadcasted_iota(jnp.int32, (up.shape[0], 128), 1)
    in_ref[:, : ff - odd] = gate[:, : ff - odd]
    in_ref[:, ff - odd : ff - odd + 128] = jnp.where(lane < odd, gate[:, ff - odd : ff - odd + 128], up[:, :128])
    in_ref[:, ff - odd + 128 :] = up[:, 128 : ff + odd]
    down = jnp.concatenate([out_blocks[g].astype(F32) for g in range(group)], axis=1)
    out_ref[...] = down[:, :ff]


def join_ff(in_blocks, out_blocks, ff):
    group, rows, tile = out_blocks.shape
    return pl.pallas_call(
        join_kernel,
        grid=(rows // 16,),
        in_specs=[
            pl.BlockSpec((group, 16, 2 * tile), lambda i: (0, i, 0)),
            pl.BlockSpec((group, 16, tile), lambda i: (0, i, 0)),
        ],
        out_specs=[pl.BlockSpec((16, 2 * ff), lambda i: (i, 0)), pl.BlockSpec((16, ff), lambda i: (i, 0))],
        out_shape=[jax.ShapeDtypeStruct((rows, 2 * ff), F32), jax.ShapeDtypeStruct((rows, ff), F32)],
        compiler_params=PARAMS,
    )(in_blocks, out_blocks)


def closing_kernel(zs, sum_ref, rows_ref, qkv_ref, dense_ref, total_ref, got, mine, lines, *refs):
    send, recv, local, line_send, line_recv = refs
    y, x, c = here()
    z = lax.axis_index("z")
    me = place(y, x, c)
    wide = got.shape[2]
    width = wide // 3
    piece = got.shape[1]
    found = swap_peers(zs, ("line",))
    greet([name for _, name in found])
    copies, comes = [], []
    for k, (peer, name) in enumerate(found[:7]):
        sems = dict(send_sem=send.at[k], recv_sem=recv.at[k], device_id=name, device_id_type=MESH)
        src = rows_ref.at[peer, :, pl.ds(0, wide)]
        copies.append(pltpu.make_async_remote_copy(src_ref=src, dst_ref=got.at[me], **sems))
        comes.append(pltpu.make_async_remote_copy(src_ref=got.at[peer], dst_ref=got.at[peer], **sems))
    for k, (peer, name) in enumerate(found[7:]):
        sems = dict(send_sem=line_send.at[k], recv_sem=line_recv.at[k], device_id=name, device_id_type=MESH)
        copies.append(pltpu.make_async_remote_copy(src_ref=sum_ref, dst_ref=lines.at[z], **sems))
        comes.append(pltpu.make_async_remote_copy(src_ref=lines.at[peer], dst_ref=lines.at[peer], **sems))
    for copy in copies:
        copy.start()
    keeps = [
        pltpu.make_async_copy(rows_ref.at[me, :, pl.ds(0, wide)], got.at[me], local.at[0]),
        pltpu.make_async_copy(sum_ref, lines.at[z], local.at[1]),
        pltpu.make_async_copy(rows_ref.at[:, :, pl.ds(wide, width)], mine, local.at[2]),
    ]
    for keep in keeps:
        keep.start()
    keeps[2].wait()
    for at in range(0, piece, 16):
        rows = jnp.concatenate([mine[g, at : at + 16] for g in range(8)], axis=1).astype(F32)
        dense_ref[at : at + 16] = rows
    for come in comes:
        come.wait_recv()
    for keep in keeps[:2]:
        keep.wait()
    for g in range(8):
        for j in range(3):
            at = pl.ds(j * D + g * width, width)
            qkv_ref[:, at] = got[g, :, j * width : (j + 1) * width].astype(F32)
    total = lines[0]
    for k in range(1, zs):
        total += lines[k]
    part = total[:, :piece]
    for k in range(1, zs):
        part = jnp.where(z == k, total[:, k * piece : (k + 1) * piece], part)
    total_ref[...] = part
    for copy in copies:
        copy.wait_send()


def closing(zs, sums, rows):
    _, piece, columns = rows.shape
    width = columns // 4
    return pl.pallas_call(
        functools.partial(closing_kernel, zs),
        out_shape=[
            jax.ShapeDtypeStruct((piece, 3 * D), F32),
            jax.ShapeDtypeStruct((piece, D), F32),
            jax.ShapeDtypeStruct((8, piece), F32),
        ],
        in_specs=[ROWS, ANY],
        out_specs=[ROWS] * 3,
        scratch_shapes=[
            pltpu.VMEM((8, piece, 3 * width), BF16),
            pltpu.VMEM((8, piece, width), BF16),
            pltpu.VMEM((zs, 8, width), F32),
            pltpu.SemaphoreType.DMA((7,)),
            pltpu.SemaphoreType.DMA((7,)),
            pltpu.SemaphoreType.DMA((3,)),
            pltpu.SemaphoreType.DMA((zs - 1,)),
            pltpu.SemaphoreType.DMA((zs - 1,)),
        ],
        compiler_params=pltpu.CompilerParams(collective_id=5, has_side_effects=True, vmem_limit_bytes=24 * 2**20),
        cost_estimate=pl.CostEstimate(flops=0, bytes_accessed=50 * 2**20, transcendentals=0),
    )(sums, rows)


def on_device(sizes, x_in, d_out, w_qkv, w_dense, w_in, w_out, gone, bone, gtwo, btwo, flags, span_start, span_len):
    gy, gx, cores, zs = sizes
    piece = w_qkv.shape[0]
    ff = w_out.shape[1]
    group = gy * gx * cores
    width = D // group
    tile = -(-ff // (group * 64)) * 64
    own = gy == 2

    def permute(array):
        lead = array.shape[:-1]
        return jnp.swapaxes(array.reshape(lead + (group, zs, piece)), -3, -2).reshape(lead + (D,))

    def restore(array):
        lead = array.shape[:-1]
        return jnp.swapaxes(array.reshape(lead + (zs, group, piece)), -3, -2).reshape(lead + (D,))

    def swap(name, arrays, kinds):
        if own:
            return group_swap(name, zs, arrays, kinds)
        ways = {
            "swap": lambda a: lax.all_to_all(a, GROUP, 0, 0, tiled=True),
            "group": lambda a: lax.all_gather(a, GROUP, axis=0),
            "line": lambda a: lax.all_gather(a, "z", axis=0),
        }
        return [ways[k](a) for a, k in zip(arrays, kinds)]

    def spread_rows(block):
        whole = group_gather(block) if own else lax.all_gather(block, GROUP, axis=0)
        return whole.reshape(group * block.shape[0], block.shape[1])

    rows_f32 = jax.ShapeDtypeStruct((SEQ_LEN, D), F32)
    rows_low = jax.ShapeDtypeStruct((SEQ_LEN, D), BF16)
    sums_type = jax.ShapeDtypeStruct((8, D), F32)

    def fold(partial):
        return lax.psum_scatter(partial.astype(BF16), GROUP, scatter_dimension=0, tiled=True).astype(F32)

    def stack_sums(*arrays):
        return jnp.pad(jnp.stack([jnp.sum(a, axis=0) for a in arrays]), ((0, 6), (0, 0)))

    def fold_one(left, right, x, gains):
        if own:
            kinds = [rows_f32, rows_f32, jax.ShapeDtypeStruct((SEQ_LEN, 128), F32)]
            whole, first, normal, inverse = group_fold(0, zs, "one", left, right, gains, [x], kinds)
            return whole.reshape(left.shape[0], D), first, normal, inverse
        first, normal, inverse = first_norm(permute(fold(dot(left, right))), x.astype(F32), gains)
        return spread_rows(first.astype(BF16)), first, normal, inverse

    def ff_turn(x, w_in, w_out, first, grad, gains):
        if own:
            whole, kept, w_out, result, d_pre, sums, d_out = turn(zs, x, w_in, w_out, gains, first, grad)
            rows = x.shape[0]
            return whole.reshape(rows, D), kept.reshape(rows, -1), w_out, result, d_pre, sums, d_out
        w_out = lax.all_gather(w_out, "z", axis=0)
        hidden, kept = ff_forward(x, w_in)
        grad = grad.astype(F32)
        right = jnp.swapaxes(w_out, 0, 1).reshape(-1, D)
        result, d_pre, terms = second_norm(fold(dot(hidden, right)), first, grad, gains)
        whole = spread_rows(d_pre.astype(BF16))
        d_out = jnp.swapaxes(dot_rows(hidden, whole).reshape(-1, zs, D // zs), 0, 1).astype(BF16)
        return whole, kept, w_out, restore(result.astype(BF16)), d_pre, stack_sums(terms, grad), d_out

    def fold_back(left, right, d_pre_two, normal, inverse, gains):
        if own:
            kinds = [rows_f32, sums_type]
            whole, d_pre, sums = group_fold(7, zs, "back", left, right, gains, [d_pre_two, normal, inverse], kinds)
            return whole.reshape(left.shape[0], D), d_pre, sums
        d_pre, terms, d_first = first_back(fold(dot_cols(left, right)), d_pre_two, normal, inverse, gains)
        return spread_rows(restore(d_pre).astype(BF16)), d_pre, stack_sums(terms, d_first)

    def fold_last(left, right, d_pre, gains, extras, kinds):
        if own:
            return group_fold(8, zs, "last", left, right, gains, [d_pre], [rows_low], extras, kinds)
        out = restore((deep_alpha * d_pre + fold(dot_cols(left, right))).astype(BF16))
        return [out] + swap(8, extras, kinds)

    def gather(block):
        return lax.all_gather(block, "z", axis=0, tiled=True)

    def scatter(partial):
        return lax.psum_scatter(partial.astype(BF16), "z", scatter_dimension=0, tiled=True)

    masked = jnp.max(flags) > 0
    prefix = jnp.where(masked, SEQ_LEN, SEQ_LEN - span_len[0])
    info = jnp.concatenate([gone, bone, gtwo, btwo, jnp.stack([prefix, span_start[0]]).astype(BF16)])
    info = jnp.pad(info[None, :], ((0, 15), (0, -info.shape[0] % 128)))

    qkv_blocks = jnp.moveaxis(w_qkv.reshape(piece, 3, group, width), 2, 0).reshape(group, piece, 3 * width)
    w_dense_part = gather(w_dense)
    qkv_blocks, info = swap(2, [qkv_blocks, info], ("swap", "group"))
    w_qkv_part = gather(qkv_blocks.reshape(group * piece, 3 * width))
    info = info[:, 0]
    place_info = info[:, 4 * piece : 4 * piece + 2].astype(jnp.int32)
    prefix, start = place_info[:, 0], place_info[:, 1]
    cosine, sine = tables(prefix, start)
    in_blocks, out_blocks = cut_ff(w_in, w_out, group, tile)
    x_perm = permute(x_in)
    x_next, qkv_blocks, cosine, sine = lax.optimization_barrier((x_perm, qkv_blocks, cosine, sine))
    x_all = spread_rows(x_next)
    in_blocks, out_blocks, x_all, w_dense_part = lax.optimization_barrier((in_blocks, out_blocks, x_all, w_dense_part))
    info = jnp.pad(info, ((0, -group % 16), (0, 0)))
    in_blocks, out_blocks, info = swap(3, [in_blocks, out_blocks, info], ("swap", "swap", "line"))
    w_in_part = gather(in_blocks.reshape(group * piece, 2 * tile))
    out_rows = out_blocks.reshape(group * piece, tile).T
    gains = info[:, :group, : 4 * piece].astype(F32).reshape(zs, group, 4, piece)
    gains = jnp.pad(jnp.transpose(gains, (2, 0, 1, 3)).reshape(4, D), ((0, 4), (0, 0)))
    w_qkv_part, x_all, cosine, sine, gains, out_rows = lax.optimization_barrier(
        (w_qkv_part, x_all, cosine, sine, gains, out_rows)
    )
    packed = dot(x_all, w_qkv_part)
    qkv, context = attend(prefix, packed, cosine, sine)
    first_all, first, normal_one, inverse_one = fold_one(context, w_dense_part, x_perm, gains)
    d_branch, kept, w_out_part, layer_out, d_pre_two, sums_two, d_w_out = ff_turn(
        first_all, w_in_part, out_rows, first, permute(d_out), gains
    )
    d_w_out = lax.psum_scatter(d_w_out, "z", scatter_dimension=0)
    d_projected = ff_backward(d_branch, w_out_part, kept)
    d_w_in = dot_rows(first_all, d_projected).astype(BF16)
    d_w_in, d_projected = lax.optimization_barrier((d_w_in, d_projected))
    d_w_in = scatter(d_w_in)
    d_attn, d_pre_one, sums_one = fold_back(d_projected, w_in_part, d_pre_two, normal_one, inverse_one, gains)
    d_attn, d_w_out = lax.optimization_barrier((d_attn, d_w_out))
    d_context = dot_cols(d_attn, w_dense_part).astype(BF16)
    d_packed = attend_back(prefix, qkv, d_context, cosine, sine)
    d_w_qkv = dot_rows(x_all, d_packed).astype(BF16)
    d_dense = dot_rows(context, d_attn).astype(BF16).reshape(zs, piece, group, width)
    d_dense = jnp.swapaxes(d_dense, 1, 2).reshape(D, width)
    d_w_qkv = jnp.concatenate([d_w_qkv, d_dense], axis=1)
    sums = jnp.concatenate([sums_one[:2], sums_two[:2], jnp.zeros((4, D), F32)])
    d_packed, d_w_qkv, d_w_in, sums = lax.optimization_barrier((d_packed, d_w_qkv, d_w_in, sums))
    d_w_qkv = scatter(d_w_qkv)
    d_w_in, d_w_out = d_w_in.reshape(group, piece, 2 * tile), d_w_out.T.reshape(group, piece, tile)
    d_input, d_w_in, d_w_out, sums = fold_last(
        d_packed, w_qkv_part, d_pre_one, gains, [d_w_in, d_w_out, sums], ("swap", "swap", "group")
    )
    sums = jnp.sum(sums, axis=0).reshape(8, zs, group, piece)
    sums = lax.dynamic_index_in_dim(sums, lax.axis_index(GROUP), 2, keepdims=False).reshape(8, width)
    out_in, out_out = join_ff(d_w_in, d_w_out, ff)
    out_in, out_out, d_input, d_w_qkv, sums = lax.optimization_barrier((out_in, out_out, d_input, d_w_qkv, sums))
    if own:
        out_qkv, out_dense, sums = closing(zs, sums, d_w_qkv.reshape(group, piece, 4 * width))
    else:
        out_dense = d_w_qkv[:, 3 * width :].reshape(group, piece, width)
        out_dense = jnp.swapaxes(out_dense, 0, 1).reshape(piece, D).astype(F32)
        d_w_qkv = d_w_qkv[:, : 3 * width].reshape(group, piece, 3 * width)
        d_w_qkv, sums = swap(5, [d_w_qkv, sums], ("swap", "line"))
        out_qkv = jnp.transpose(d_w_qkv.astype(F32).reshape(group, piece, 3, width), (1, 2, 0, 3))
        out_qkv = out_qkv.reshape(piece, 3 * D)
        sums = jnp.sum(sums, axis=0).reshape(8, zs, piece)
        sums = lax.dynamic_index_in_dim(sums, lax.axis_index("z"), 1, keepdims=False)
    return layer_out, d_input, out_qkv, out_dense, out_in, out_out, sums[0], sums[1], sums[2], sums[3]


def solution(mesh):
    grp, shard = mesh.shape["grp"], mesh.shape["shard"]
    sizes = (grp // 4, 2, 2, shard)
    inner = Mesh(mesh.devices.reshape(sizes), ALL)
    rows, flat = P(ALL, None), P(ALL)
    return jax.shard_map(
        functools.partial(on_device, sizes),
        mesh=inner,
        in_specs=(rows,) * 6 + (flat,) * 7,
        out_specs=(rows,) * 6 + (flat,) * 4,
        check_vma=False,
    )
```

```python
import functools

import jax
import jax.numpy as jnp
from jax import lax
from jax.experimental import pallas as pl
from jax.experimental.pallas import tpu as pltpu
from jax.sharding import Mesh
from jax.sharding import PartitionSpec as P

HEADS = 16
HEAD = 128
SEQ_LEN = 224
D = HEADS * HEAD
deep_alpha = 6.928203230275509
norm_eps = 1e-05
far_below = -1e30
scale = HEAD ** (-0.5)

ALL = ("gy", "gx", "core", "z")
GROUP = ("gy", "gx", "core")
MESH = pl.DeviceIdType.MESH
F32 = jnp.float32
BF16 = jnp.bfloat16


def dot(left, right):
    return jnp.dot(left, right, preferred_element_type=F32)


def dot_rows(left, right):
    return lax.dot_general(left, right, (((0,), (0,)), ((), ())), preferred_element_type=F32)


def dot_cols(left, right):
    return lax.dot_general(left, right, (((1,), (1,)), ((), ())), preferred_element_type=F32)


def swap_halves(block):
    lane = lax.broadcasted_iota(jnp.int32, block.shape, 1)
    return jnp.where((lane & 32) == 0, pltpu.roll(block, 96, 1), pltpu.roll(block, 32, 1))


def seen(prefix):
    row = lax.broadcasted_iota(jnp.int32, (SEQ_LEN, SEQ_LEN), 0)
    col = lax.broadcasted_iota(jnp.int32, (SEQ_LEN, SEQ_LEN), 1)
    return (col < prefix) | (col <= row)


def softmax(queries, keys, visible):
    scores = jnp.where(visible, dot_cols(queries, keys), far_below)
    weights = jnp.exp(scores - jnp.max(scores, axis=1, keepdims=True))
    return weights / jnp.sum(weights, axis=1, keepdims=True)


def attend_kernel(prefix_ref, packed_ref, cos_ref, sin_ref, qkv_ref, context_ref):
    width = context_ref.shape[1]
    visible = seen(prefix_ref[pl.program_id(0)])
    cosine = cos_ref[0]
    sine = sin_ref[0]
    for head in range(width // HEAD):
        at = pl.ds(head * HEAD, HEAD)
        at_k = pl.ds(width + head * HEAD, HEAD)
        at_v = pl.ds(2 * width + head * HEAD, HEAD)
        raw = packed_ref[:, at]
        queries = ((raw * cosine + swap_halves(raw) * sine) * scale).astype(BF16)
        raw = packed_ref[:, at_k]
        keys = (raw * cosine + swap_halves(raw) * sine).astype(BF16)
        values = packed_ref[:, at_v].astype(BF16)
        qkv_ref[:, at] = queries
        qkv_ref[:, at_k] = keys
        qkv_ref[:, at_v] = values
        probs = softmax(queries, keys, visible).astype(BF16)
        context_ref[:, at] = dot(probs, values).astype(BF16)


def attend_back_kernel(prefix_ref, qkv_ref, d_context_ref, cos_ref, sin_ref, d_packed_ref):
    width = d_context_ref.shape[1]
    visible = seen(prefix_ref[pl.program_id(0)])
    cosine = cos_ref[0]
    sine = sin_ref[0]
    for head in range(width // HEAD):
        at = pl.ds(head * HEAD, HEAD)
        at_k = pl.ds(width + head * HEAD, HEAD)
        at_v = pl.ds(2 * width + head * HEAD, HEAD)
        queries = qkv_ref[:, at]
        keys = qkv_ref[:, at_k]
        values = qkv_ref[:, at_v]
        d_context = d_context_ref[:, at]
        probs = softmax(queries, keys, visible)
        d_packed_ref[:, at_v] = dot_rows(probs.astype(BF16), d_context).astype(BF16)
        d_probs = dot_cols(d_context, values)
        inner = jnp.sum(probs * d_probs, axis=1, keepdims=True)
        d_scores = (probs * (d_probs - inner)).astype(BF16)
        grad = dot(d_scores, keys) * scale
        d_packed_ref[:, at] = (grad * cosine - swap_halves(grad) * sine).astype(BF16)
        grad = dot_rows(d_scores, queries)
        d_packed_ref[:, at_k] = (grad * cosine - swap_halves(grad) * sine).astype(BF16)


def by_sequence(width):
    return pl.BlockSpec((SEQ_LEN, width), lambda s: (s, 0))


TABLE = pl.BlockSpec((1, SEQ_LEN, HEAD), lambda s: (s, 0, 0))
SCALARS = pl.BlockSpec(memory_space=pltpu.SMEM)
PARAMS = pltpu.CompilerParams(vmem_limit_bytes=48 * 2**20)


def attend(prefix, packed, cosine, sine):
    rows, width = packed.shape[0], packed.shape[1] // 3
    return pl.pallas_call(
        attend_kernel,
        grid=(rows // SEQ_LEN,),
        in_specs=[SCALARS, by_sequence(3 * width), TABLE, TABLE],
        out_specs=[by_sequence(3 * width), by_sequence(width)],
        out_shape=[
            jax.ShapeDtypeStruct((rows, 3 * width), BF16),
            jax.ShapeDtypeStruct((rows, width), BF16),
        ],
        compiler_params=PARAMS,
    )(prefix, packed, cosine, sine)


def attend_back(prefix, qkv, d_context, cosine, sine):
    rows, width = d_context.shape
    return pl.pallas_call(
        attend_back_kernel,
        grid=(rows // SEQ_LEN,),
        in_specs=[SCALARS, by_sequence(3 * width), by_sequence(width), TABLE, TABLE],
        out_specs=by_sequence(3 * width),
        out_shape=jax.ShapeDtypeStruct((rows, 3 * width), BF16),
        compiler_params=PARAMS,
    )(prefix, qkv, d_context, cosine, sine)


def tables(prefix, start):
    place = jnp.arange(SEQ_LEN, dtype=jnp.int32)
    in_span = place[None, :] >= prefix[:, None]
    pos_one = jnp.where(in_span, start[:, None], place[None, :])
    pos_two = jnp.where(in_span, place[None, :] - prefix[:, None] + 1, 0)
    lane = jnp.arange(HEAD)
    freqs = 10000.0 ** (-2.0 * (lane % 32).astype(F32) / 64)
    place_of = jnp.where(lane[None, None, :] < 64, pos_one[:, :, None], pos_two[:, :, None])
    angles = place_of.astype(F32) * freqs
    sign = jnp.where(lane % 64 < 32, -1.0, 1.0)
    return jnp.cos(angles), jnp.sin(angles) * sign


def norm_parts(values):
    center = values - jnp.mean(values, axis=-1, keepdims=True)
    inverse = lax.rsqrt(jnp.mean(center * center, axis=-1, keepdims=True) + norm_eps)
    return center * inverse, inverse


def norm_back(normal, inverse, gain, grad):
    scaled = gain * grad
    return inverse * (
        scaled
        - jnp.mean(scaled, axis=-1, keepdims=True)
        - normal * jnp.mean(scaled * normal, axis=-1, keepdims=True)
    )


def gate_parts(gate):
    phi = 0.5 * (1.0 + lax.erf(gate * 0.7071067811865476))
    slope = phi + gate * jnp.exp(-0.5 * gate * gate) * 0.3989422804014327
    return gate * phi, slope


def here():
    return lax.axis_index("gy"), lax.axis_index("gx"), lax.axis_index("core")


def place(y, x, c):
    return (y * 2 + x) * 2 + c


def greet(peers):
    barrier = pltpu.get_barrier_semaphore()
    for peer in peers:
        pl.semaphore_signal(barrier, inc=1, device_id=peer, device_id_type=MESH)
    pl.semaphore_wait(barrier, len(peers))


def spread_block(cut, base, block_ref, out_ref, send, recv, local):
    rows = block_ref.shape[0]
    y, x, c = here()
    to_x, to_y, to_c = {"gx": 1 - x}, {"gy": 1 - y}, {"core": 1 - c}
    me, by_x, by_y, far = place(y, x, c), place(y, 1 - x, c), place(1 - y, x, c), place(1 - y, 1 - x, c)
    low, high = pl.ds(0, cut), pl.ds(cut, rows - cut)

    def push(k, src, dst, to):
        copy = pltpu.make_async_remote_copy(
            src_ref=src, dst_ref=dst, send_sem=send.at[base + k], recv_sem=recv.at[base + k], device_id=to, device_id_type=MESH
        )
        copy.start()
        return copy

    def landed(k, dst):
        pltpu.make_async_remote_copy(
            src_ref=dst, dst_ref=dst, send_sem=send.at[base + k], recv_sem=recv.at[base + k], device_id=to_c, device_id_type=MESH
        ).wait_recv()

    sent = [
        push(0, block_ref.at[low], out_ref.at[me, low], to_x),
        push(1, block_ref.at[high], out_ref.at[me, high], to_y),
        push(2, block_ref.at[high], out_ref.at[me, high], to_x),
        push(3, block_ref.at[low], out_ref.at[me, low], to_y),
        push(4, block_ref, out_ref.at[me], to_c),
    ]
    keep = pltpu.make_async_copy(block_ref, out_ref.at[me], local)
    keep.start()
    landed(0, out_ref.at[by_x, low])
    sent.append(push(5, out_ref.at[by_x, low], out_ref.at[by_x, low], to_y))
    sent.append(push(7, out_ref.at[by_x, low], out_ref.at[by_x, low], to_c))
    landed(1, out_ref.at[by_y, high])
    sent.append(push(6, out_ref.at[by_y, high], out_ref.at[by_y, high], to_x))
    sent.append(push(8, out_ref.at[by_y, high], out_ref.at[by_y, high], to_c))
    landed(2, out_ref.at[by_x, high])
    sent.append(push(9, out_ref.at[by_x, high], out_ref.at[by_x, high], to_c))
    landed(3, out_ref.at[by_y, low])
    sent.append(push(10, out_ref.at[by_y, low], out_ref.at[by_y, low], to_c))
    landed(5, out_ref.at[far, low])
    sent.append(push(11, out_ref.at[far, low], out_ref.at[far, low], to_c))
    landed(6, out_ref.at[far, high])
    sent.append(push(12, out_ref.at[far, high], out_ref.at[far, high], to_c))
    other, other_x, other_y, other_far = (
        place(y, x, 1 - c),
        place(y, 1 - x, 1 - c),
        place(1 - y, x, 1 - c),
        place(1 - y, 1 - x, 1 - c),
    )
    landed(4, out_ref.at[other])
    landed(7, out_ref.at[other_x, low])
    landed(8, out_ref.at[other_y, high])
    landed(9, out_ref.at[other_x, high])
    landed(10, out_ref.at[other_y, low])
    landed(11, out_ref.at[other_far, low])
    landed(12, out_ref.at[other_far, high])
    keep.wait()
    for copy in sent:
        copy.wait_send()


def gather_kernel(cut, block_ref, out_ref, send, recv, local):
    y, x, c = here()
    greet([{"gx": 1 - x}, {"gy": 1 - y}, {"core": 1 - c}])
    spread_block(cut, 0, block_ref, out_ref, send, recv, local)


ANY = pl.BlockSpec(memory_space=pl.ANY)


def group_gather(block):
    rows, width = block.shape
    return pl.pallas_call(
        functools.partial(gather_kernel, rows // 2),
        out_shape=jax.ShapeDtypeStruct((8, rows, width), block.dtype),
        in_specs=[ANY],
        out_specs=ANY,
        scratch_shapes=[pltpu.SemaphoreType.DMA((13,)), pltpu.SemaphoreType.DMA((13,)), pltpu.SemaphoreType.DMA],
        compiler_params=pltpu.CompilerParams(collective_id=9, has_side_effects=True),
        cost_estimate=pl.CostEstimate(flops=0, bytes_accessed=100 * 2**20, transcendentals=0),
    )(block)


def swap_peers(zs, kinds):
    y, x, c = here()
    z = lax.axis_index("z")
    found = []
    for k in range(1, 8):
        peer = ((y + k // 4) % 2, (x + k // 2 % 2) % 2, (c + k % 2) % 2)
        found.append((place(*peer), {"gy": peer[0], "gx": peer[1], "core": peer[2]}))
    if "line" in kinds:
        found += [((z + k) % zs, {"z": (z + k) % zs}) for k in range(1, zs)]
    return found


def swap_begin(zs, kinds, blocks, outs, send, recv, local):
    copies, comes, keeps = [], [], []
    found = swap_peers(zs, kinds)
    for i, kind in enumerate(kinds):
        me = lax.axis_index("z") if kind == "line" else place(*here())
        for k, (peer, name) in enumerate(found[7:] if kind == "line" else found[:7]):
            src = blocks[i].at[peer] if kind == "swap" else blocks[i]
            landing = outs[i].at[peer]
            sems = dict(send_sem=send.at[i, k], recv_sem=recv.at[i, k], device_id=name, device_id_type=MESH)
            copies.append(pltpu.make_async_remote_copy(src_ref=src, dst_ref=outs[i].at[me], **sems))
            comes.append(pltpu.make_async_remote_copy(src_ref=landing, dst_ref=landing, **sems))
            copies[-1].start()
        own = blocks[i].at[me] if kind == "swap" else blocks[i]
        keeps.append(pltpu.make_async_copy(own, outs[i].at[me], local.at[i]))
        keeps[-1].start()

    def finish():
        for come in comes:
            come.wait_recv()
        for copy in copies:
            copy.wait_send()
        for keep in keeps:
            keep.wait()

    return finish


SWAP_LEAD = {"swap": lambda zs: (), "group": lambda zs: (8,), "line": lambda zs: (zs,)}


def swap_shapes(zs, arrays, kinds):
    return [jax.ShapeDtypeStruct(SWAP_LEAD[k](zs) + a.shape, a.dtype) for a, k in zip(arrays, kinds)]


def swap_scratch(zs, kinds):
    n, most = len(kinds), max(7, zs - 1)
    return [
        pltpu.SemaphoreType.DMA((n, most)),
        pltpu.SemaphoreType.DMA((n, most)),
        pltpu.SemaphoreType.DMA((n,)),
    ]


SLAB = 16
ROWS = pl.BlockSpec(memory_space=pltpu.VMEM)
CHIP_COLS = 256


def by_rows(value, zs, piece):
    group = D // (zs * piece)
    order = [g * zs + z for z in range(zs) for g in range(group)]
    return jnp.concatenate([value[:, m * piece : (m + 1) * piece] for m in order], axis=1)


def in_order(value, zs, piece):
    group = D // (zs * piece)
    order = [z * group + g for g in range(group) for z in range(zs)]
    return jnp.concatenate([value[:, m * piece : (m + 1) * piece] for m in order], axis=1)


def first_norm(total, x, gains):
    normal, inverse = norm_parts(deep_alpha * x + total)
    first = normal * gains[0:1] + gains[1:2]
    return first, normal, inverse


def second_norm(total, first, grad, gains):
    normal, inverse = norm_parts(deep_alpha * first + total)
    return normal * gains[2:3] + gains[3:4], norm_back(normal, inverse, gains[2:3], grad), grad * normal


def first_back(total, d_pre_two, normal, inverse, gains):
    d_first = deep_alpha * d_pre_two + total
    return norm_back(normal, inverse, gains[0:1], d_first), d_first * normal, d_first


def fold_kernel(mode, across, zs, piece, n_aux, n_out, kinds, *refs):
    left_ref, right_ref, gains_ref = refs[:3]
    aux_refs = refs[3 : 3 + n_aux]
    refs = refs[3 + n_aux :]
    n_swap = len(kinds)
    swap_in, refs = refs[:n_swap], refs[n_swap:]
    spread = mode != "last"
    if spread:
        all_ref, refs = refs[0], refs[1:]
    outs, refs = refs[:n_out], refs[n_out:]
    swap_out, refs = refs[:n_swap], refs[n_swap:]
    aux, refs = refs[:n_aux], refs[n_aux:]
    left, right, part, got, near_x, near_y, from_x, from_y, block, acc, send, recv, local = refs[:13]
    rows, width = block.shape
    cut = near_x.shape[0]
    y, x, c = here()
    to_x, to_y, to_c = {"gx": 1 - x}, {"gy": 1 - y}, {"core": 1 - c}
    chips = [(1 - y, 1 - x), (y, 1 - x), (1 - y, x), (y, x)]
    low, high = pl.ds(0, cut), pl.ds(cut, rows - cut)

    def push(k, src, dst, to):
        copy = pltpu.make_async_remote_copy(
            src_ref=src, dst_ref=dst, send_sem=send.at[k], recv_sem=recv.at[k], device_id=to, device_id_type=MESH
        )
        copy.start()
        return copy

    def add(k, extra, start, size, offset=0):
        @pl.loop(0, size // SLAB)
        def _(step):
            at = pl.ds(pl.multiple_of(start + step * SLAB, SLAB), SLAB)
            of = pl.ds(pl.multiple_of(start - offset + step * SLAB, SLAB), SLAB)
            part[k, c, at] = (part[k, c, at].astype(F32) + extra[of].astype(F32)).astype(BF16)

    loads = [pltpu.make_async_copy(left_ref.at[a * 2 + b], left.at[k], local.at[k]) for k, (a, b) in enumerate(chips)]
    load_right = pltpu.make_async_copy(right_ref, right, local.at[4])
    load_aux = [pltpu.make_async_copy(r, v, local.at[5 + k]) for k, (r, v) in enumerate(zip(aux_refs, aux))]
    loads[0].start()
    load_right.start()
    for load in loads[1:] + load_aux:
        load.start()
    if n_swap:
        greet([name for _, name in swap_peers(1, kinds)])
        swap_finish = swap_begin(1, kinds, swap_in, swap_out, *refs[13:])
    else:
        greet([to_x, to_y, to_c])

    def product(k):
        loads[k].wait()

        @pl.loop(0, width // CHIP_COLS)
        def _(step):
            at = pl.ds(pl.multiple_of(step * CHIP_COLS, CHIP_COLS), CHIP_COLS)
            here_part = dot_cols(left[k], right[at]) if across else dot(left[k], right[:, at])
            part[k, 0, :, at] = here_part[:rows].astype(BF16)
            part[k, 1, :, at] = here_part[rows:].astype(BF16)

        return push(k, part.at[k, 1 - c], got.at[k], to_c)

    load_right.wait()
    sent = [product(0), product(1)]
    sent[0].wait_recv()
    add(0, got.at[0], 0, rows)
    far_x = push(4, part.at[0, c, low], near_x, to_x)
    far_y = push(5, part.at[0, c, high], near_y, to_y)
    sent.append(product(2))
    sent[1].wait_recv()
    add(1, got.at[1], 0, rows)
    plain_x = push(6, part.at[1, c, low], from_x.at[low], to_x)
    sent[2].wait_recv()
    add(2, got.at[2], 0, rows)
    plain_y = push(7, part.at[2, c, high], from_y.at[high], to_y)
    sent.append(product(3))
    far_y.wait_recv()
    add(1, near_y, cut, rows - cut, cut)
    more_x = push(8, part.at[1, c, high], from_x.at[high], to_x)
    far_x.wait_recv()
    add(2, near_x, 0, cut)
    more_y = push(9, part.at[2, c, low], from_y.at[low], to_y)
    sent[3].wait_recv()
    for load in load_aux:
        load.wait()
    plain_x.wait_recv()
    plain_y.wait_recv()
    more_x.wait_recv()
    more_y.wait_recv()
    gains = gains_ref[...]
    acc[...] = jnp.zeros_like(acc)

    @pl.loop(0, rows // SLAB)
    def _(step):
        at = pl.ds(pl.multiple_of(step * SLAB, SLAB), SLAB)
        total = part[3, c, at].astype(F32) + got[3, at].astype(F32) + from_x[at].astype(F32) + from_y[at].astype(F32)
        held = [a[at].astype(F32) for a in aux]
        if mode == "one":
            first, normal, inverse = first_norm(by_rows(total, zs, piece), by_rows(held[0], zs, piece), gains)
            outs[0][at] = first
            outs[1][at] = normal
            outs[2][at] = jnp.broadcast_to(inverse, (SLAB, 128))
            block[at] = first.astype(BF16)
        elif mode == "back":
            d_pre, terms, d_first = first_back(total, held[0], held[1], held[2][:, 0:1], gains)
            outs[0][at] = d_pre
            block[at] = in_order(d_pre, zs, piece).astype(BF16)
            acc[0] += terms
            acc[1] += d_first
        else:
            outs[0][at] = in_order(deep_alpha * held[0] + total, zs, piece).astype(BF16)

    if mode == "back":
        outs[-1][0:1] = jnp.sum(acc[0], axis=0, keepdims=True)
        outs[-1][1:2] = jnp.sum(acc[1], axis=0, keepdims=True)
    for copy in sent + [far_x, far_y, plain_x, plain_y, more_x, more_y]:
        copy.wait_send()
    if n_swap:
        swap_finish()
    if spread:
        spread_block(cut, 10, block, all_ref, send, recv, local.at[4])


def group_fold(name, zs, mode, left, right, gains, aux, out_types, extras=(), kinds=()):
    across = mode != "one"
    rows, depth = left.shape[0] // 8, left.shape[1]
    width = gains.shape[1]
    cut = rows // 2
    spread = mode != "last"
    out_shape = [jax.ShapeDtypeStruct((8, rows, width), BF16)] * spread + out_types
    n, n_swap = len(aux), len(extras)
    n_sems = 23 if spread else 10
    return pl.pallas_call(
        functools.partial(fold_kernel, mode, across, zs, width // (8 * zs), n, len(out_types), kinds),
        out_shape=out_shape + swap_shapes(1, extras, kinds),
        in_specs=[ANY, ANY, ROWS] + [ANY] * (n + n_swap),
        out_specs=[ANY] * spread + [ROWS] * len(out_types) + [ANY] * n_swap,
        scratch_shapes=[pltpu.VMEM(a.shape, a.dtype) for a in aux]
        + [
            pltpu.VMEM((4, 2 * rows, depth), BF16),
            pltpu.VMEM(right.shape, BF16),
            pltpu.VMEM((4, 2, rows, width), BF16),
            pltpu.VMEM((4, rows, width), BF16),
            pltpu.VMEM((cut, width), BF16),
            pltpu.VMEM((rows - cut, width), BF16),
            pltpu.VMEM((rows, width), BF16),
            pltpu.VMEM((rows, width), BF16),
            pltpu.VMEM((rows, width), BF16),
            pltpu.VMEM((2, SLAB, width), F32),
            pltpu.SemaphoreType.DMA((n_sems,)),
            pltpu.SemaphoreType.DMA((n_sems,)),
            pltpu.SemaphoreType.DMA((5 + n,)),
        ]
        + (swap_scratch(1, kinds) if n_swap else []),
        compiler_params=pltpu.CompilerParams(
            collective_id=name, has_side_effects=True, vmem_limit_bytes=50 * 2**20
        ),
        cost_estimate=pl.CostEstimate(flops=0, bytes_accessed=(200 if spread else 110) * 2**20, transcendentals=0),
    )(left.reshape(4, 2 * rows, depth), right, gains, *aux, *extras)


def turn_kernel(
    zs, piece, x_ref, in_ref, out_ref, gains_ref, first_ref, grad_ref,
    all_ref, kept_ref, right_ref, result_ref, d_pre_ref, sums_ref, dw_ref,
    first, grad, w_in, kept, left, right, part, got, near_x, near_y, from_x, from_y, whole, dw, acc,
    fold_send, fold_recv, all_send, all_recv, line_send, line_recv, local, x_local
):
    rows = first.shape[0]
    tile = left.shape[2]
    wide = right.shape[2]
    y, x, c = here()
    z = lax.axis_index("z")
    to_x, to_y, to_c = {"gx": 1 - x}, {"gy": 1 - y}, {"core": 1 - c}
    chips = [(1 - y) * 2 + 1 - x, y * 2 + 1 - x, (1 - y) * 2 + x, y * 2 + x]
    me, by_x, by_y, far = place(y, x, c), place(y, 1 - x, c), place(1 - y, x, c), place(1 - y, 1 - x, c)
    other, other_x, other_y, other_far = (
        place(y, x, 1 - c),
        place(y, 1 - x, 1 - c),
        place(1 - y, x, 1 - c),
        place(1 - y, 1 - x, 1 - c),
    )
    half = rows // 2
    most = -(-half // (2 * SLAB)) * SLAB
    lows = [(0, most), (half, half - most)]
    highs = [(most, half - most), (2 * half - most, most)]
    top, bottom = pl.ds(0, half), pl.ds(half, half)
    sent = []

    def remote(sems, k, src, dst, to):
        return pltpu.make_async_remote_copy(
            src_ref=src,
            dst_ref=dst,
            send_sem=sems[0].at[k],
            recv_sem=sems[1].at[k],
            device_id=to,
            device_id_type=MESH,
        )

    def push(sems, k, src, dst, to):
        copy = remote(sems, k, src, dst, to)
        copy.start()
        sent.append(copy)

    def landed(sems, k, dst):
        remote(sems, k, dst, dst, to_c).wait_recv()

    folds, alls, lines = (fold_send, fold_recv), (all_send, all_recv), (line_send, line_recv)

    load_out = pltpu.make_async_copy(out_ref, right.at[z], local.at[0])
    load_in = pltpu.make_async_copy(in_ref, w_in, local.at[1])
    load_first = pltpu.make_async_copy(first_ref, first, local.at[2])
    load_grad = pltpu.make_async_copy(grad_ref, grad, local.at[3])

    def load_x(g):
        return pltpu.make_async_copy(x_ref.at[g], whole.at[g], x_local.at[g])

    load_out.start()
    load_in.start()
    for g in range(8):
        load_x(g).start()
    load_first.start()
    load_grad.start()

    barrier = pltpu.get_barrier_semaphore()
    for to in (to_x, to_y, to_c):
        pl.semaphore_signal(barrier, inc=1, device_id=to, device_id_type=MESH)

    @pl.when(z > 0)
    def _():
        pl.semaphore_signal(barrier, inc=1, device_id={"z": z - 1}, device_id_type=MESH)

    @pl.when(z < zs - 1)
    def _():
        pl.semaphore_signal(barrier, inc=1, device_id={"z": z + 1}, device_id_type=MESH)

    inside = (z > 0) & (z < zs - 1)

    @pl.when(inside)
    def _():
        pl.semaphore_wait(barrier, 5)

    @pl.when(jnp.logical_not(inside))
    def _():
        pl.semaphore_wait(barrier, 4)

    def shard_of(step, up):
        return z - step if up else z + step

    def hop(step, up):
        ref = right.at[shard_of(step, up)]
        return remote(lines, 2 * step + (0 if up else 1), ref, ref, {"z": z + 1 if up else z - 1})

    def sends(step, up):
        return (z >= step) & (z < zs - 1) if up else (z <= zs - 1 - step) & (z > 0)

    def gets(step, up):
        return z >= step + 1 if up else z <= zs - 2 - step

    def line_serve(step):
        for up in (True, False):

            @pl.when(gets(step - 1, up) & sends(step, up))
            def _(up=up):
                landed(lines, 2 * (step - 1) + (0 if up else 1), right.at[shard_of(step, up)])
                hop(step, up).start()

    def line_take(step):
        for up in (True, False):

            @pl.when(gets(step - 1, up) & jnp.logical_not(sends(step, up)))
            def _(up=up):
                landed(lines, 2 * (step - 1) + (0 if up else 1), right.at[shard_of(step, up)])

    load_out.wait()
    for up in (True, False):

        @pl.when(sends(0, up))
        def _(up=up):
            hop(0, up).start()


    load_in.wait()

    @pl.loop(0, 8)
    def _(g):
        @pl.when(g == 6)
        def _():
            line_serve(1)

        load_x(g).wait()
        projected = dot(whole[g], w_in[...])
        gate, up = projected[:, :tile], projected[:, tile:]
        act, slope = gate_parts(gate)
        left[g] = (act * up).astype(BF16)
        kept[g] = jnp.concatenate([up * slope, act], axis=1).astype(BF16)

    keep = pltpu.make_async_copy(kept, kept_ref, local.at[4])
    keep.start()

    def add(k, extra, start, offset, at):
        @pl.loop(0, half // SLAB)
        def _(step):
            row = pl.ds(pl.multiple_of(start + step * SLAB, SLAB), SLAB)
            of = pl.ds(pl.multiple_of(start - offset + step * SLAB, SLAB), SLAB)
            part[k, c, row, at] = (part[k, c, row, at].astype(F32) + extra[of, at].astype(F32)).astype(BF16)

    def chip_sum(k, at):
        add(k, got.at[k], 0, 0, at)
        add(k, got.at[k], half, 0, at)

    def product(k, block, at):
        found = dot(left[pl.ds(2 * chips[k], 2)].reshape(2 * rows, tile), right[block])
        part[k, 0, :, at] = found[:rows].astype(BF16)
        part[k, 1, :, at] = found[rows:].astype(BF16)

    def block_at(i):
        if i == 0:
            return z
        below = z < zs // 2
        near = jnp.where(below, z, zs - 1 - z)
        spot = jnp.where(i <= 2 * near, jnp.where(i % 2 == 1, near - (i + 1) // 2, near + i // 2), i)
        return jnp.where(below, spot, zs - 1 - spot)

    def block_cols(i):
        return pl.ds(pl.multiple_of(block_at(i) * wide, wide), wide)

    def fold_start(i):
        b, block, at = 8 * i, block_at(i), block_cols(i)
        rest = pl.ds(1, 3)
        product(0, block, at)
        push(folds, b, part.at[0, 1 - c, :, at], got.at[0, :, at], to_c)
        for k in (1, 2, 3):
            product(k, block, at)
        push(folds, b + 1, part.at[rest, 1 - c, :, at], got.at[rest, :, at], to_c)
        landed(folds, b, got.at[0, :, at])
        chip_sum(0, at)
        push(folds, b + 2, part.at[0, c, top, at], near_x.at[:, at], to_x)
        push(folds, b + 3, part.at[0, c, bottom, at], near_y.at[:, at], to_y)
        landed(folds, b + 1, got.at[rest, :, at])
        chip_sum(1, at)
        push(folds, b + 4, part.at[1, c, top, at], from_x.at[top, at], to_x)
        chip_sum(2, at)
        push(folds, b + 5, part.at[2, c, bottom, at], from_y.at[bottom, at], to_y)

    def fold_end(i):
        b, at = 8 * i, block_cols(i)
        landed(folds, b + 3, near_y.at[:, at])
        add(1, near_y, half, half, at)
        push(folds, b + 6, part.at[1, c, bottom, at], from_x.at[bottom, at], to_x)
        landed(folds, b + 2, near_x.at[:, at])
        add(2, near_x, 0, 0, at)
        push(folds, b + 7, part.at[2, c, top, at], from_y.at[top, at], to_y)

    gains = gains_ref[...]
    line_take(1)
    fold_start(0)
    fold_start(1)
    fold_end(0)
    for i in range(2, zs):
        if i < zs - 1:
            line_serve(i)
        fold_end(i - 1)
        line_take(i)
        fold_start(i)
    fold_end(zs - 1)
    carry = pltpu.make_async_copy(right, right_ref, local.at[5])
    carry.start()
    load_first.wait()
    load_grad.wait()
    acc[...] = jnp.zeros_like(acc)
    for i in range(zs):
        at = block_cols(i)
        landed(folds, 8 * i + 4, from_x.at[top, at])
        landed(folds, 8 * i + 5, from_y.at[bottom, at])
        landed(folds, 8 * i + 6, from_x.at[bottom, at])
        landed(folds, 8 * i + 7, from_y.at[top, at])

    def low(i):
        return pl.ds(*lows[i])

    def high(i):
        return pl.ds(*highs[i])

    def span(i):
        return pl.ds(i * half, half)

    def norm(i):
        @pl.loop(0, half // SLAB)
        def _(step):
            at = pl.ds(pl.multiple_of(i * half + step * SLAB, SLAB), SLAB)
            total = part[3, c, at].astype(F32) + got[3, at].astype(F32)
            total += from_x[at].astype(F32) + from_y[at].astype(F32)
            dy = by_rows(grad[at].astype(F32), zs, piece)
            result, d_pre, terms = second_norm(total, first[at], dy, gains)
            result_ref[at] = in_order(result, zs, piece).astype(BF16)
            d_pre_ref[at] = d_pre
            whole[me, at] = d_pre.astype(BF16)
            acc[0] += terms
            acc[1] += dy

        b = 13 * i
        push(alls, b, whole.at[me, low(i)], whole.at[me, low(i)], to_x)
        push(alls, b + 1, whole.at[me, high(i)], whole.at[me, high(i)], to_y)
        push(alls, b + 2, whole.at[me, high(i)], whole.at[me, high(i)], to_x)
        push(alls, b + 3, whole.at[me, low(i)], whole.at[me, low(i)], to_y)
        push(alls, b + 4, whole.at[me, span(i)], whole.at[me, span(i)], to_c)

    def pass_on(i, k, slot, at, onward):
        ref = whole.at[slot, at]
        landed(alls, 13 * i + k, ref)
        for where, to in onward:
            push(alls, 13 * i + where, ref, ref, to)

    def spread_first(i):
        pass_on(i, 0, by_x, low(i), [(5, to_y), (7, to_c)])
        pass_on(i, 1, by_y, high(i), [(6, to_x), (8, to_c)])

    def spread_rest(i):
        pass_on(i, 2, by_x, high(i), [(9, to_c)])
        pass_on(i, 3, by_y, low(i), [(10, to_c)])

    def spread_far(i):
        pass_on(i, 5, far, low(i), [(11, to_c)])
        pass_on(i, 6, far, high(i), [(12, to_c)])

    outward = []

    def gradient(k, last=False, first_one=False):
        pair = pl.ds(2 * chips[k], 2)
        outward.append(pltpu.make_async_copy(whole.at[pair], all_ref.at[pair], local.at[6 + k]))
        outward[-1].start()

        @pl.loop(0, zs)
        def _(block):
            at = pl.ds(pl.multiple_of(block * wide, wide), wide)
            found = dot_rows(left[pair].reshape(2 * rows, tile), whole[pair, :, at].reshape(2 * rows, wide))
            if first_one:
                dw[block] = found
            elif last:
                dw_ref[block] = (dw[block] + found).astype(BF16)
            else:
                dw[block] += found

    norm(0)
    norm(1)
    spread_first(0)
    for i in (0, 1):
        landed(alls, 13 * i + 4, whole.at[other, span(i)])
    gradient(3, first_one=True)
    spread_rest(0)
    spread_first(1)
    spread_rest(1)
    for i in (0, 1):
        landed(alls, 13 * i + 7, whole.at[other_x, low(i)])
        landed(alls, 13 * i + 9, whole.at[other_x, high(i)])
    gradient(1)
    spread_far(0)
    for i in (0, 1):
        landed(alls, 13 * i + 8, whole.at[other_y, high(i)])
        landed(alls, 13 * i + 10, whole.at[other_y, low(i)])
    gradient(2)
    sums_ref[0:1] = jnp.sum(acc[0], axis=0, keepdims=True)
    sums_ref[1:2] = jnp.sum(acc[1], axis=0, keepdims=True)
    spread_far(1)
    for i in (0, 1):
        landed(alls, 13 * i + 11, whole.at[other_far, low(i)])
        landed(alls, 13 * i + 12, whole.at[other_far, high(i)])
    gradient(0, last=True)
    for copy in outward + [keep, carry]:
        copy.wait()
    for copy in sent:
        copy.wait_send()
    for step in range(zs - 1):
        for up in (True, False):

            @pl.when(sends(step, up))
            def _(step=step, up=up):
                hop(step, up).wait_send()


def turn(zs, x, w_in, w_out, gains, first, grad):
    rows = x.shape[0] // 8
    units, wide = w_out.shape
    width = gains.shape[1]
    half = rows // 2
    by_z = (zs, units, wide)
    return pl.pallas_call(
        functools.partial(turn_kernel, zs, width // (8 * zs)),
        out_shape=[
            jax.ShapeDtypeStruct((8, rows, width), BF16),
            jax.ShapeDtypeStruct((8, rows, 2 * units), BF16),
            jax.ShapeDtypeStruct(by_z, BF16),
            jax.ShapeDtypeStruct((rows, width), BF16),
            jax.ShapeDtypeStruct((rows, width), F32),
            jax.ShapeDtypeStruct((8, width), F32),
            jax.ShapeDtypeStruct(by_z, BF16),
        ],
        in_specs=[ANY, ANY, ANY, ROWS, ANY, ANY],
        out_specs=[ANY] * 3 + [ROWS] * 4,
        scratch_shapes=[
            pltpu.VMEM((rows, width), F32),
            pltpu.VMEM((rows, width), BF16),
            pltpu.VMEM(w_in.shape, BF16),
            pltpu.VMEM((8, rows, 2 * units), BF16),
            pltpu.VMEM((8, rows, units), BF16),
            pltpu.VMEM(by_z, BF16),
            pltpu.VMEM((4, 2, rows, width), BF16),
            pltpu.VMEM((4, rows, width), BF16),
            pltpu.VMEM((half, width), BF16),
            pltpu.VMEM((half, width), BF16),
            pltpu.VMEM((rows, width), BF16),
            pltpu.VMEM((rows, width), BF16),
            pltpu.VMEM((8, rows, width), BF16),
            pltpu.VMEM(by_z, F32),
            pltpu.VMEM((2, SLAB, width), F32),
            pltpu.SemaphoreType.DMA((8 * zs,)),
            pltpu.SemaphoreType.DMA((8 * zs,)),
            pltpu.SemaphoreType.DMA((26,)),
            pltpu.SemaphoreType.DMA((26,)),
            pltpu.SemaphoreType.DMA((2 * (zs - 1),)),
            pltpu.SemaphoreType.DMA((2 * (zs - 1),)),
            pltpu.SemaphoreType.DMA((10,)),
            pltpu.SemaphoreType.DMA((8,)),
        ],
        compiler_params=pltpu.CompilerParams(collective_id=1, has_side_effects=True, vmem_limit_bytes=60 * 2**20),
        cost_estimate=pl.CostEstimate(flops=0, bytes_accessed=380 * 2**20, transcendentals=0),
    )(x.reshape(8, rows, width), w_in, w_out, gains, first, grad)


def swap_kernel(zs, kinds, *refs):
    n = len(kinds)
    greet([name for _, name in swap_peers(zs, kinds)])
    swap_begin(zs, kinds, refs[:n], refs[n : 2 * n], *refs[2 * n :])()


def group_swap(name, zs, arrays, kinds):
    n = len(arrays)
    return pl.pallas_call(
        functools.partial(swap_kernel, zs, kinds),
        out_shape=swap_shapes(zs, arrays, kinds),
        in_specs=[ANY] * n,
        out_specs=[ANY] * n,
        scratch_shapes=swap_scratch(zs, kinds),
        compiler_params=pltpu.CompilerParams(collective_id=name, has_side_effects=True),
        cost_estimate=pl.CostEstimate(flops=0, bytes_accessed=50 * 2**20, transcendentals=0),
    )(*arrays)


def ff_kernel(x_ref, w_ref, hidden_ref, kept_ref):
    tile = hidden_ref.shape[1]
    projected = dot(x_ref[...], w_ref[...])
    gate, up = projected[:, :tile], projected[:, tile:]
    act, slope = gate_parts(gate)
    hidden_ref[...] = (act * up).astype(BF16)
    kept_ref[...] = jnp.concatenate([up * slope, act], axis=1).astype(BF16)


def ff_back_kernel(grad_ref, w_ref, kept_ref, out_ref):
    zs, _, wide = w_ref.shape
    d_hidden = dot_cols(grad_ref[:, :wide], w_ref[0])
    for z in range(1, zs):
        d_hidden += dot_cols(grad_ref[:, z * wide : (z + 1) * wide], w_ref[z])
    out_ref[...] = (jnp.concatenate([d_hidden, d_hidden], axis=1) * kept_ref[...].astype(F32)).astype(BF16)


FF_ROWS = 256


def ff_rows(width):
    return pl.BlockSpec((FF_ROWS, width), lambda i: (i, 0))


def ff_forward(x, w):
    rows, depth = x.shape
    wide = w.shape[1]
    return pl.pallas_call(
        ff_kernel,
        grid=(rows // FF_ROWS,),
        in_specs=[ff_rows(depth), pl.BlockSpec((depth, wide), lambda i: (0, 0))],
        out_specs=[ff_rows(wide // 2), ff_rows(wide)],
        out_shape=[jax.ShapeDtypeStruct((rows, wide // 2), BF16), jax.ShapeDtypeStruct((rows, wide), BF16)],
        compiler_params=PARAMS,
        cost_estimate=pl.CostEstimate(flops=2 * rows * depth * wide, bytes_accessed=20 * 2**20, transcendentals=0),
    )(x, w)


def ff_backward(grad, w, kept):
    rows, depth = grad.shape
    wide = kept.shape[1]
    return pl.pallas_call(
        ff_back_kernel,
        grid=(rows // FF_ROWS,),
        in_specs=[ff_rows(depth), pl.BlockSpec(w.shape, lambda i: (0, 0, 0)), ff_rows(wide)],
        out_specs=ff_rows(wide),
        out_shape=jax.ShapeDtypeStruct((rows, wide), BF16),
        compiler_params=PARAMS,
        cost_estimate=pl.CostEstimate(flops=rows * depth * wide, bytes_accessed=20 * 2**20, transcendentals=0),
    )(grad, w, kept)


def cut_kernel(in_ref, out_ref, in_blocks, out_blocks, wide):
    group, _, double = in_blocks.shape
    tile, ff = double // 2, out_ref.shape[1]
    span = group * tile
    odd = ff % 128
    live = lax.broadcasted_iota(jnp.int32, (in_ref.shape[0], span), 1) < ff
    wide[...] = jnp.zeros_like(wide)
    wide[:, : 2 * ff] = in_ref[...].astype(F32)
    gate = jnp.where(live, wide[:, :span], 0.0)
    up = pltpu.roll(wide[:, ff - odd : ff - odd + span], span - odd, 1)
    up = jnp.where(live, up, 0.0)
    wide[:, :span] = jnp.zeros_like(live, F32)
    wide[:, :ff] = out_ref[...].astype(F32)
    down = wide[:, :span]
    for g in range(group):
        at = slice(g * tile, (g + 1) * tile)
        in_blocks[g] = jnp.concatenate([gate[:, at], up[:, at]], axis=1).astype(BF16)
        out_blocks[g] = down[:, at].astype(BF16)


def cut_ff(w_in, w_out, group, tile):
    rows, ff = w_out.shape
    return pl.pallas_call(
        cut_kernel,
        grid=(rows // 16,),
        in_specs=[pl.BlockSpec((16, 2 * ff), lambda i: (i, 0)), pl.BlockSpec((16, ff), lambda i: (i, 0))],
        out_specs=[
            pl.BlockSpec((group, 16, 2 * tile), lambda i: (0, i, 0)),
            pl.BlockSpec((group, 16, tile), lambda i: (0, i, 0)),
        ],
        out_shape=[
            jax.ShapeDtypeStruct((group, rows, 2 * tile), BF16),
            jax.ShapeDtypeStruct((group, rows, tile), BF16),
        ],
        scratch_shapes=[pltpu.VMEM((16, -(-(ff + group * tile) // 128) * 128), F32)],
        compiler_params=PARAMS,
    )(w_in, w_out)


def join_kernel(in_blocks, out_blocks, in_ref, out_ref):
    group, _, double = in_blocks.shape
    tile, ff = double // 2, out_ref.shape[1]
    odd = ff % 128
    blocks = [in_blocks[g].astype(F32) for g in range(group)]
    gate = jnp.concatenate([block[:, :tile] for block in blocks], axis=1)
    up = jnp.concatenate([block[:, tile:] for block in blocks], axis=1)
    up = pltpu.roll(up, odd, 1)
    lane = lax.broadcasted_iota(jnp.int32, (up.shape[0], 128), 1)
    in_ref[:, : ff - odd] = gate[:, : ff - odd]
    in_ref[:, ff - odd : ff - odd + 128] = jnp.where(lane < odd, gate[:, ff - odd : ff - odd + 128], up[:, :128])
    in_ref[:, ff - odd + 128 :] = up[:, 128 : ff + odd]
    down = jnp.concatenate([out_blocks[g].astype(F32) for g in range(group)], axis=1)
    out_ref[...] = down[:, :ff]


def join_ff(in_blocks, out_blocks, ff):
    group, rows, tile = out_blocks.shape
    return pl.pallas_call(
        join_kernel,
        grid=(rows // 16,),
        in_specs=[
            pl.BlockSpec((group, 16, 2 * tile), lambda i: (0, i, 0)),
            pl.BlockSpec((group, 16, tile), lambda i: (0, i, 0)),
        ],
        out_specs=[pl.BlockSpec((16, 2 * ff), lambda i: (i, 0)), pl.BlockSpec((16, ff), lambda i: (i, 0))],
        out_shape=[jax.ShapeDtypeStruct((rows, 2 * ff), F32), jax.ShapeDtypeStruct((rows, ff), F32)],
        compiler_params=PARAMS,
    )(in_blocks, out_blocks)


def closing_kernel(zs, sum_ref, rows_ref, qkv_ref, dense_ref, total_ref, got, mine, lines, *refs):
    send, recv, local, line_send, line_recv = refs
    y, x, c = here()
    z = lax.axis_index("z")
    me = place(y, x, c)
    wide = got.shape[2]
    width = wide // 3
    piece = got.shape[1]
    found = swap_peers(zs, ("line",))
    greet([name for _, name in found])
    copies, comes = [], []
    for k, (peer, name) in enumerate(found[:7]):
        sems = dict(send_sem=send.at[k], recv_sem=recv.at[k], device_id=name, device_id_type=MESH)
        src = rows_ref.at[peer, :, pl.ds(0, wide)]
        copies.append(pltpu.make_async_remote_copy(src_ref=src, dst_ref=got.at[me], **sems))
        comes.append(pltpu.make_async_remote_copy(src_ref=got.at[peer], dst_ref=got.at[peer], **sems))
    for k, (peer, name) in enumerate(found[7:]):
        sems = dict(send_sem=line_send.at[k], recv_sem=line_recv.at[k], device_id=name, device_id_type=MESH)
        copies.append(pltpu.make_async_remote_copy(src_ref=sum_ref, dst_ref=lines.at[z], **sems))
        comes.append(pltpu.make_async_remote_copy(src_ref=lines.at[peer], dst_ref=lines.at[peer], **sems))
    for copy in copies:
        copy.start()
    keeps = [
        pltpu.make_async_copy(rows_ref.at[me, :, pl.ds(0, wide)], got.at[me], local.at[0]),
        pltpu.make_async_copy(sum_ref, lines.at[z], local.at[1]),
        pltpu.make_async_copy(rows_ref.at[:, :, pl.ds(wide, width)], mine, local.at[2]),
    ]
    for keep in keeps:
        keep.start()
    keeps[2].wait()
    for at in range(0, piece, 16):
        rows = jnp.concatenate([mine[g, at : at + 16] for g in range(8)], axis=1).astype(F32)
        dense_ref[at : at + 16] = rows
    for come in comes:
        come.wait_recv()
    for keep in keeps[:2]:
        keep.wait()
    for g in range(8):
        for j in range(3):
            at = pl.ds(j * D + g * width, width)
            qkv_ref[:, at] = got[g, :, j * width : (j + 1) * width].astype(F32)
    total = lines[0]
    for k in range(1, zs):
        total += lines[k]
    part = total[:, :piece]
    for k in range(1, zs):
        part = jnp.where(z == k, total[:, k * piece : (k + 1) * piece], part)
    total_ref[...] = part
    for copy in copies:
        copy.wait_send()


def closing(zs, sums, rows):
    _, piece, columns = rows.shape
    width = columns // 4
    return pl.pallas_call(
        functools.partial(closing_kernel, zs),
        out_shape=[
            jax.ShapeDtypeStruct((piece, 3 * D), F32),
            jax.ShapeDtypeStruct((piece, D), F32),
            jax.ShapeDtypeStruct((8, piece), F32),
        ],
        in_specs=[ROWS, ANY],
        out_specs=[ROWS] * 3,
        scratch_shapes=[
            pltpu.VMEM((8, piece, 3 * width), BF16),
            pltpu.VMEM((8, piece, width), BF16),
            pltpu.VMEM((zs, 8, width), F32),
            pltpu.SemaphoreType.DMA((7,)),
            pltpu.SemaphoreType.DMA((7,)),
            pltpu.SemaphoreType.DMA((3,)),
            pltpu.SemaphoreType.DMA((zs - 1,)),
            pltpu.SemaphoreType.DMA((zs - 1,)),
        ],
        compiler_params=pltpu.CompilerParams(collective_id=5, has_side_effects=True, vmem_limit_bytes=24 * 2**20),
        cost_estimate=pl.CostEstimate(flops=0, bytes_accessed=50 * 2**20, transcendentals=0),
    )(sums, rows)


def on_device(sizes, x_in, d_out, w_qkv, w_dense, w_in, w_out, gone, bone, gtwo, btwo, flags, span_start, span_len):
    gy, gx, cores, zs = sizes
    piece = w_qkv.shape[0]
    ff = w_out.shape[1]
    group = gy * gx * cores
    width = D // group
    tile = -(-ff // (group * 64)) * 64
    own = gy == 2

    def permute(array):
        lead = array.shape[:-1]
        return jnp.swapaxes(array.reshape(lead + (group, zs, piece)), -3, -2).reshape(lead + (D,))

    def restore(array):
        lead = array.shape[:-1]
        return jnp.swapaxes(array.reshape(lead + (zs, group, piece)), -3, -2).reshape(lead + (D,))

    def swap(name, arrays, kinds):
        if own:
            return group_swap(name, zs, arrays, kinds)
        ways = {
            "swap": lambda a: lax.all_to_all(a, GROUP, 0, 0, tiled=True),
            "group": lambda a: lax.all_gather(a, GROUP, axis=0),
            "line": lambda a: lax.all_gather(a, "z", axis=0),
        }
        return [ways[k](a) for a, k in zip(arrays, kinds)]

    def spread_rows(block):
        whole = group_gather(block) if own else lax.all_gather(block, GROUP, axis=0)
        return whole.reshape(group * block.shape[0], block.shape[1])

    rows_f32 = jax.ShapeDtypeStruct((SEQ_LEN, D), F32)
    rows_low = jax.ShapeDtypeStruct((SEQ_LEN, D), BF16)
    sums_type = jax.ShapeDtypeStruct((8, D), F32)

    def fold(partial):
        return lax.psum_scatter(partial.astype(BF16), GROUP, scatter_dimension=0, tiled=True).astype(F32)

    def stack_sums(*arrays):
        return jnp.pad(jnp.stack([jnp.sum(a, axis=0) for a in arrays]), ((0, 6), (0, 0)))

    def fold_one(left, right, x, gains):
        if own:
            kinds = [rows_f32, rows_f32, jax.ShapeDtypeStruct((SEQ_LEN, 128), F32)]
            whole, first, normal, inverse = group_fold(0, zs, "one", left, right, gains, [x], kinds)
            return whole.reshape(left.shape[0], D), first, normal, inverse
        first, normal, inverse = first_norm(permute(fold(dot(left, right))), permute(x).astype(F32), gains)
        return spread_rows(first.astype(BF16)), first, normal, inverse

    def ff_turn(x, w_in, w_out, first, grad, gains):
        if own:
            whole, kept, w_out, result, d_pre, sums, d_out = turn(zs, x, w_in, w_out, gains, first, grad)
            rows = x.shape[0]
            return whole.reshape(rows, D), kept.reshape(rows, -1), w_out, result, d_pre, sums, d_out
        w_out = lax.all_gather(w_out, "z", axis=0)
        hidden, kept = ff_forward(x, w_in)
        grad = permute(grad).astype(F32)
        right = jnp.swapaxes(w_out, 0, 1).reshape(-1, D)
        result, d_pre, terms = second_norm(fold(dot(hidden, right)), first, grad, gains)
        whole = spread_rows(d_pre.astype(BF16))
        d_out = jnp.swapaxes(dot_rows(hidden, whole).reshape(-1, zs, D // zs), 0, 1).astype(BF16)
        return whole, kept, w_out, restore(result.astype(BF16)), d_pre, stack_sums(terms, grad), d_out

    def fold_back(left, right, d_pre_two, normal, inverse, gains):
        if own:
            kinds = [rows_f32, sums_type]
            whole, d_pre, sums = group_fold(7, zs, "back", left, right, gains, [d_pre_two, normal, inverse], kinds)
            return whole.reshape(left.shape[0], D), d_pre, sums
        d_pre, terms, d_first = first_back(fold(dot_cols(left, right)), d_pre_two, normal, inverse, gains)
        return spread_rows(restore(d_pre).astype(BF16)), d_pre, stack_sums(terms, d_first)

    def fold_last(left, right, d_pre, gains, extras, kinds):
        if own:
            return group_fold(8, zs, "last", left, right, gains, [d_pre], [rows_low], extras, kinds)
        out = restore((deep_alpha * d_pre + fold(dot_cols(left, right))).astype(BF16))
        return [out] + swap(8, extras, kinds)

    def gather(block):
        return lax.all_gather(block, "z", axis=0, tiled=True)

    def scatter(partial):
        return lax.psum_scatter(partial.astype(BF16), "z", scatter_dimension=0, tiled=True)

    masked = jnp.max(flags) > 0
    prefix = jnp.where(masked, SEQ_LEN, SEQ_LEN - span_len[0])
    info = jnp.concatenate([gone, bone, gtwo, btwo, jnp.stack([prefix, span_start[0]]).astype(BF16)])
    info = jnp.pad(info[None, :], ((0, 15), (0, -info.shape[0] % 128)))

    qkv_blocks = jnp.moveaxis(w_qkv.reshape(piece, 3, group, width), 2, 0).reshape(group, piece, 3 * width)
    w_dense_part = gather(w_dense)
    qkv_blocks, info = swap(2, [qkv_blocks, info], ("swap", "group"))
    w_qkv_part = gather(qkv_blocks.reshape(group * piece, 3 * width))
    info = info[:, 0]
    place_info = info[:, 4 * piece : 4 * piece + 2].astype(jnp.int32)
    prefix, start = place_info[:, 0], place_info[:, 1]
    cosine, sine = tables(prefix, start)
    in_blocks, out_blocks = cut_ff(w_in, w_out, group, tile)
    in_blocks, out_blocks, qkv_blocks = lax.optimization_barrier((in_blocks, out_blocks, qkv_blocks))
    info = jnp.pad(info, ((0, -group % 16), (0, 0)))
    in_blocks, out_blocks, info = swap(3, [in_blocks, out_blocks, info], ("swap", "swap", "line"))
    w_in_part = gather(in_blocks.reshape(group * piece, 2 * tile))
    out_rows = out_blocks.reshape(group * piece, tile).T
    x_next, in_blocks, w_dense_part = lax.optimization_barrier((permute(x_in), in_blocks, w_dense_part))
    x_all = spread_rows(x_next)
    gains = info[:, :group, : 4 * piece].astype(F32).reshape(zs, group, 4, piece)
    gains = jnp.pad(jnp.transpose(gains, (2, 0, 1, 3)).reshape(4, D), ((0, 4), (0, 0)))
    w_qkv_part, x_all, cosine, sine, gains = lax.optimization_barrier((w_qkv_part, x_all, cosine, sine, gains))
    packed = dot(x_all, w_qkv_part)
    qkv, context = attend(prefix, packed, cosine, sine)
    first_all, first, normal_one, inverse_one = fold_one(context, w_dense_part, x_in, gains)
    d_branch, kept, w_out_part, layer_out, d_pre_two, sums_two, d_w_out = ff_turn(
        first_all, w_in_part, out_rows, first, d_out, gains
    )
    d_w_out = lax.psum_scatter(d_w_out, "z", scatter_dimension=0)
    d_projected = ff_backward(d_branch, w_out_part, kept)
    d_w_in = dot_rows(first_all, d_projected).astype(BF16)
    d_w_in, d_projected = lax.optimization_barrier((d_w_in, d_projected))
    d_w_in = scatter(d_w_in)
    d_attn, d_pre_one, sums_one = fold_back(d_projected, w_in_part, d_pre_two, normal_one, inverse_one, gains)
    d_attn, d_w_out = lax.optimization_barrier((d_attn, d_w_out))
    d_context = dot_cols(d_attn, w_dense_part).astype(BF16)
    d_packed = attend_back(prefix, qkv, d_context, cosine, sine)
    d_w_qkv = dot_rows(x_all, d_packed).astype(BF16)
    d_dense = dot_rows(context, d_attn).astype(BF16).reshape(zs, piece, group, width)
    d_dense = jnp.swapaxes(d_dense, 1, 2).reshape(D, width)
    d_w_qkv = jnp.concatenate([d_w_qkv, d_dense], axis=1)
    sums = jnp.concatenate([sums_one[:2], sums_two[:2], jnp.zeros((4, D), F32)])
    d_packed, d_w_qkv, d_w_in, sums = lax.optimization_barrier((d_packed, d_w_qkv, d_w_in, sums))
    d_w_qkv = scatter(d_w_qkv)
    d_w_in, d_w_out = d_w_in.reshape(group, piece, 2 * tile), d_w_out.T.reshape(group, piece, tile)
    d_input, d_w_in, d_w_out, sums = fold_last(
        d_packed, w_qkv_part, d_pre_one, gains, [d_w_in, d_w_out, sums], ("swap", "swap", "group")
    )
    sums = jnp.sum(sums, axis=0).reshape(8, zs, group, piece)
    sums = lax.dynamic_index_in_dim(sums, lax.axis_index(GROUP), 2, keepdims=False).reshape(8, width)
    out_in, out_out = join_ff(d_w_in, d_w_out, ff)
    out_in, out_out, d_input, d_w_qkv, sums = lax.optimization_barrier((out_in, out_out, d_input, d_w_qkv, sums))
    if own:
        out_qkv, out_dense, sums = closing(zs, sums, d_w_qkv.reshape(group, piece, 4 * width))
    else:
        out_dense = d_w_qkv[:, 3 * width :].reshape(group, piece, width)
        out_dense = jnp.swapaxes(out_dense, 0, 1).reshape(piece, D).astype(F32)
        d_w_qkv = d_w_qkv[:, : 3 * width].reshape(group, piece, 3 * width)
        d_w_qkv, sums = swap(5, [d_w_qkv, sums], ("swap", "line"))
        out_qkv = jnp.transpose(d_w_qkv.astype(F32).reshape(group, piece, 3, width), (1, 2, 0, 3))
        out_qkv = out_qkv.reshape(piece, 3 * D)
        sums = jnp.sum(sums, axis=0).reshape(8, zs, piece)
        sums = lax.dynamic_index_in_dim(sums, lax.axis_index("z"), 1, keepdims=False)
    return layer_out, d_input, out_qkv, out_dense, out_in, out_out, sums[0], sums[1], sums[2], sums[3]


def solution(mesh):
    grp, shard = mesh.shape["grp"], mesh.shape["shard"]
    sizes = (grp // 4, 2, 2, shard)
    inner = Mesh(mesh.devices.reshape(sizes), ALL)
    rows, flat = P(ALL, None), P(ALL)
    return jax.shard_map(
        functools.partial(on_device, sizes),
        mesh=inner,
        in_specs=(rows,) * 6 + (flat,) * 7,
        out_specs=(rows,) * 6 + (flat,) * 4,
        check_vma=False,
    )
```

```python
import functools

import jax
import jax.numpy as jnp
from jax import lax
from jax.experimental import pallas as pl
from jax.experimental.pallas import tpu as pltpu
from jax.sharding import Mesh
from jax.sharding import PartitionSpec as P

HEADS = 16
HEAD = 128
SEQ_LEN = 224
D = HEADS * HEAD
deep_alpha = 6.928203230275509
norm_eps = 1e-05
far_below = -1e30
scale = HEAD ** (-0.5)

ALL = ("gy", "gx", "core", "z")
GROUP = ("gy", "gx", "core")
MESH = pl.DeviceIdType.MESH
F32 = jnp.float32
BF16 = jnp.bfloat16


def dot(left, right):
    return jnp.dot(left, right, preferred_element_type=F32)


def dot_rows(left, right):
    return lax.dot_general(left, right, (((0,), (0,)), ((), ())), preferred_element_type=F32)


def dot_cols(left, right):
    return lax.dot_general(left, right, (((1,), (1,)), ((), ())), preferred_element_type=F32)


def swap_halves(block):
    lane = lax.broadcasted_iota(jnp.int32, block.shape, 1)
    return jnp.where((lane & 32) == 0, pltpu.roll(block, 96, 1), pltpu.roll(block, 32, 1))


def seen(prefix):
    row = lax.broadcasted_iota(jnp.int32, (SEQ_LEN, SEQ_LEN), 0)
    col = lax.broadcasted_iota(jnp.int32, (SEQ_LEN, SEQ_LEN), 1)
    return (col < prefix) | (col <= row)


def softmax(queries, keys, visible):
    scores = jnp.where(visible, dot_cols(queries, keys), far_below)
    weights = jnp.exp(scores - jnp.max(scores, axis=1, keepdims=True))
    return weights / jnp.sum(weights, axis=1, keepdims=True)


def attend_kernel(prefix_ref, packed_ref, cos_ref, sin_ref, qkv_ref, context_ref):
    width = context_ref.shape[1]
    visible = seen(prefix_ref[pl.program_id(0)])
    cosine = cos_ref[0]
    sine = sin_ref[0]
    for head in range(width // HEAD):
        at = pl.ds(head * HEAD, HEAD)
        at_k = pl.ds(width + head * HEAD, HEAD)
        at_v = pl.ds(2 * width + head * HEAD, HEAD)
        raw = packed_ref[:, at]
        queries = ((raw * cosine + swap_halves(raw) * sine) * scale).astype(BF16)
        raw = packed_ref[:, at_k]
        keys = (raw * cosine + swap_halves(raw) * sine).astype(BF16)
        values = packed_ref[:, at_v].astype(BF16)
        qkv_ref[:, at] = queries
        qkv_ref[:, at_k] = keys
        qkv_ref[:, at_v] = values
        probs = softmax(queries, keys, visible).astype(BF16)
        context_ref[:, at] = dot(probs, values).astype(BF16)


def attend_back_kernel(prefix_ref, qkv_ref, d_context_ref, cos_ref, sin_ref, d_packed_ref):
    width = d_context_ref.shape[1]
    visible = seen(prefix_ref[pl.program_id(0)])
    cosine = cos_ref[0]
    sine = sin_ref[0]
    for head in range(width // HEAD):
        at = pl.ds(head * HEAD, HEAD)
        at_k = pl.ds(width + head * HEAD, HEAD)
        at_v = pl.ds(2 * width + head * HEAD, HEAD)
        queries = qkv_ref[:, at]
        keys = qkv_ref[:, at_k]
        values = qkv_ref[:, at_v]
        d_context = d_context_ref[:, at]
        probs = softmax(queries, keys, visible)
        d_packed_ref[:, at_v] = dot_rows(probs.astype(BF16), d_context).astype(BF16)
        d_probs = dot_cols(d_context, values)
        inner = jnp.sum(probs * d_probs, axis=1, keepdims=True)
        d_scores = (probs * (d_probs - inner)).astype(BF16)
        grad = dot(d_scores, keys) * scale
        d_packed_ref[:, at] = (grad * cosine - swap_halves(grad) * sine).astype(BF16)
        grad = dot_rows(d_scores, queries)
        d_packed_ref[:, at_k] = (grad * cosine - swap_halves(grad) * sine).astype(BF16)


def by_sequence(width):
    return pl.BlockSpec((SEQ_LEN, width), lambda s: (s, 0))


TABLE = pl.BlockSpec((1, SEQ_LEN, HEAD), lambda s: (s, 0, 0))
SCALARS = pl.BlockSpec(memory_space=pltpu.SMEM)
PARAMS = pltpu.CompilerParams(vmem_limit_bytes=48 * 2**20)


def attend(prefix, packed, cosine, sine):
    rows, width = packed.shape[0], packed.shape[1] // 3
    return pl.pallas_call(
        attend_kernel,
        grid=(rows // SEQ_LEN,),
        in_specs=[SCALARS, by_sequence(3 * width), TABLE, TABLE],
        out_specs=[by_sequence(3 * width), by_sequence(width)],
        out_shape=[
            jax.ShapeDtypeStruct((rows, 3 * width), BF16),
            jax.ShapeDtypeStruct((rows, width), BF16),
        ],
        compiler_params=PARAMS,
    )(prefix, packed, cosine, sine)


def attend_back(prefix, qkv, d_context, cosine, sine):
    rows, width = d_context.shape
    return pl.pallas_call(
        attend_back_kernel,
        grid=(rows // SEQ_LEN,),
        in_specs=[SCALARS, by_sequence(3 * width), by_sequence(width), TABLE, TABLE],
        out_specs=by_sequence(3 * width),
        out_shape=jax.ShapeDtypeStruct((rows, 3 * width), BF16),
        compiler_params=PARAMS,
    )(prefix, qkv, d_context, cosine, sine)


def tables(prefix, start):
    place = jnp.arange(SEQ_LEN, dtype=jnp.int32)
    in_span = place[None, :] >= prefix[:, None]
    pos_one = jnp.where(in_span, start[:, None], place[None, :])
    pos_two = jnp.where(in_span, place[None, :] - prefix[:, None] + 1, 0)
    lane = jnp.arange(HEAD)
    freqs = 10000.0 ** (-2.0 * (lane % 32).astype(F32) / 64)
    place_of = jnp.where(lane[None, None, :] < 64, pos_one[:, :, None], pos_two[:, :, None])
    angles = place_of.astype(F32) * freqs
    sign = jnp.where(lane % 64 < 32, -1.0, 1.0)
    return jnp.cos(angles), jnp.sin(angles) * sign


def norm_parts(values):
    center = values - jnp.mean(values, axis=-1, keepdims=True)
    inverse = lax.rsqrt(jnp.mean(center * center, axis=-1, keepdims=True) + norm_eps)
    return center * inverse, inverse


def norm_back(normal, inverse, gain, grad):
    scaled = gain * grad
    return inverse * (
        scaled
        - jnp.mean(scaled, axis=-1, keepdims=True)
        - normal * jnp.mean(scaled * normal, axis=-1, keepdims=True)
    )


def gate_parts(gate):
    phi = 0.5 * (1.0 + lax.erf(gate * 0.7071067811865476))
    slope = phi + gate * jnp.exp(-0.5 * gate * gate) * 0.3989422804014327
    return gate * phi, slope


def here():
    return lax.axis_index("gy"), lax.axis_index("gx"), lax.axis_index("core")


def place(y, x, c):
    return (y * 2 + x) * 2 + c


def greet(peers):
    barrier = pltpu.get_barrier_semaphore()
    for peer in peers:
        pl.semaphore_signal(barrier, inc=1, device_id=peer, device_id_type=MESH)
    pl.semaphore_wait(barrier, len(peers))


def spread_block(cut, base, block_ref, out_ref, send, recv, local):
    rows = block_ref.shape[0]
    y, x, c = here()
    to_x, to_y, to_c = {"gx": 1 - x}, {"gy": 1 - y}, {"core": 1 - c}
    me, by_x, by_y, far = place(y, x, c), place(y, 1 - x, c), place(1 - y, x, c), place(1 - y, 1 - x, c)
    low, high = pl.ds(0, cut), pl.ds(cut, rows - cut)

    def push(k, src, dst, to):
        copy = pltpu.make_async_remote_copy(
            src_ref=src, dst_ref=dst, send_sem=send.at[base + k], recv_sem=recv.at[base + k], device_id=to, device_id_type=MESH
        )
        copy.start()
        return copy

    def landed(k, dst):
        pltpu.make_async_remote_copy(
            src_ref=dst, dst_ref=dst, send_sem=send.at[base + k], recv_sem=recv.at[base + k], device_id=to_c, device_id_type=MESH
        ).wait_recv()

    sent = [
        push(0, block_ref.at[low], out_ref.at[me, low], to_x),
        push(1, block_ref.at[high], out_ref.at[me, high], to_y),
        push(2, block_ref.at[high], out_ref.at[me, high], to_x),
        push(3, block_ref.at[low], out_ref.at[me, low], to_y),
        push(4, block_ref, out_ref.at[me], to_c),
    ]
    keep = pltpu.make_async_copy(block_ref, out_ref.at[me], local)
    keep.start()
    landed(0, out_ref.at[by_x, low])
    sent.append(push(5, out_ref.at[by_x, low], out_ref.at[by_x, low], to_y))
    sent.append(push(7, out_ref.at[by_x, low], out_ref.at[by_x, low], to_c))
    landed(1, out_ref.at[by_y, high])
    sent.append(push(6, out_ref.at[by_y, high], out_ref.at[by_y, high], to_x))
    sent.append(push(8, out_ref.at[by_y, high], out_ref.at[by_y, high], to_c))
    landed(2, out_ref.at[by_x, high])
    sent.append(push(9, out_ref.at[by_x, high], out_ref.at[by_x, high], to_c))
    landed(3, out_ref.at[by_y, low])
    sent.append(push(10, out_ref.at[by_y, low], out_ref.at[by_y, low], to_c))
    landed(5, out_ref.at[far, low])
    sent.append(push(11, out_ref.at[far, low], out_ref.at[far, low], to_c))
    landed(6, out_ref.at[far, high])
    sent.append(push(12, out_ref.at[far, high], out_ref.at[far, high], to_c))
    other, other_x, other_y, other_far = (
        place(y, x, 1 - c),
        place(y, 1 - x, 1 - c),
        place(1 - y, x, 1 - c),
        place(1 - y, 1 - x, 1 - c),
    )
    landed(4, out_ref.at[other])
    landed(7, out_ref.at[other_x, low])
    landed(8, out_ref.at[other_y, high])
    landed(9, out_ref.at[other_x, high])
    landed(10, out_ref.at[other_y, low])
    landed(11, out_ref.at[other_far, low])
    landed(12, out_ref.at[other_far, high])
    keep.wait()
    for copy in sent:
        copy.wait_send()


def gather_kernel(cut, block_ref, out_ref, send, recv, local):
    y, x, c = here()
    greet([{"gx": 1 - x}, {"gy": 1 - y}, {"core": 1 - c}])
    spread_block(cut, 0, block_ref, out_ref, send, recv, local)


ANY = pl.BlockSpec(memory_space=pl.ANY)


def group_gather(block):
    rows, width = block.shape
    return pl.pallas_call(
        functools.partial(gather_kernel, rows // 2),
        out_shape=jax.ShapeDtypeStruct((8, rows, width), block.dtype),
        in_specs=[ANY],
        out_specs=ANY,
        scratch_shapes=[pltpu.SemaphoreType.DMA((13,)), pltpu.SemaphoreType.DMA((13,)), pltpu.SemaphoreType.DMA],
        compiler_params=pltpu.CompilerParams(collective_id=9, has_side_effects=True),
        cost_estimate=pl.CostEstimate(flops=0, bytes_accessed=100 * 2**20, transcendentals=0),
    )(block)


def swap_peers(zs, kinds):
    y, x, c = here()
    z = lax.axis_index("z")
    found = []
    for k in range(1, 8):
        peer = ((y + k // 4) % 2, (x + k // 2 % 2) % 2, (c + k % 2) % 2)
        found.append((place(*peer), {"gy": peer[0], "gx": peer[1], "core": peer[2]}))
    if "line" in kinds:
        found += [((z + k) % zs, {"z": (z + k) % zs}) for k in range(1, zs)]
    return found


def swap_begin(zs, kinds, blocks, outs, send, recv, local):
    copies, comes, keeps = [], [], []
    found = swap_peers(zs, kinds)
    for i, kind in enumerate(kinds):
        me = lax.axis_index("z") if kind == "line" else place(*here())
        for k, (peer, name) in enumerate(found[7:] if kind == "line" else found[:7]):
            src = blocks[i].at[peer] if kind == "swap" else blocks[i]
            landing = outs[i].at[peer]
            sems = dict(send_sem=send.at[i, k], recv_sem=recv.at[i, k], device_id=name, device_id_type=MESH)
            copies.append(pltpu.make_async_remote_copy(src_ref=src, dst_ref=outs[i].at[me], **sems))
            comes.append(pltpu.make_async_remote_copy(src_ref=landing, dst_ref=landing, **sems))
            copies[-1].start()
        own = blocks[i].at[me] if kind == "swap" else blocks[i]
        keeps.append(pltpu.make_async_copy(own, outs[i].at[me], local.at[i]))
        keeps[-1].start()

    def finish():
        for come in comes:
            come.wait_recv()
        for copy in copies:
            copy.wait_send()
        for keep in keeps:
            keep.wait()

    return finish


SWAP_LEAD = {"swap": lambda zs: (), "group": lambda zs: (8,), "line": lambda zs: (zs,)}


def swap_shapes(zs, arrays, kinds):
    return [jax.ShapeDtypeStruct(SWAP_LEAD[k](zs) + a.shape, a.dtype) for a, k in zip(arrays, kinds)]


def swap_scratch(zs, kinds):
    n, most = len(kinds), max(7, zs - 1)
    return [
        pltpu.SemaphoreType.DMA((n, most)),
        pltpu.SemaphoreType.DMA((n, most)),
        pltpu.SemaphoreType.DMA((n,)),
    ]


SLAB = 16
ROWS = pl.BlockSpec(memory_space=pltpu.VMEM)
CHIP_COLS = 256


def by_rows(value, zs, piece):
    group = D // (zs * piece)
    order = [g * zs + z for z in range(zs) for g in range(group)]
    return jnp.concatenate([value[:, m * piece : (m + 1) * piece] for m in order], axis=1)


def in_order(value, zs, piece):
    group = D // (zs * piece)
    order = [z * group + g for g in range(group) for z in range(zs)]
    return jnp.concatenate([value[:, m * piece : (m + 1) * piece] for m in order], axis=1)


def first_norm(values, gains):
    normal, inverse = norm_parts(values)
    first = normal * gains[0:1] + gains[1:2]
    return first, normal, inverse


def second_norm(total, first, grad, gains):
    normal, inverse = norm_parts(deep_alpha * first + total)
    return normal * gains[2:3] + gains[3:4], norm_back(normal, inverse, gains[2:3], grad), grad * normal


def first_back(total, d_pre_two, normal, inverse, gains):
    d_first = deep_alpha * d_pre_two + total
    return norm_back(normal, inverse, gains[0:1], d_first), d_first * normal, d_first


def fold_kernel(mode, across, zs, piece, n_aux, n_out, kinds, *refs):
    left_ref, right_ref, gains_ref = refs[:3]
    aux_refs = refs[3 : 3 + n_aux]
    refs = refs[3 + n_aux :]
    n_swap = len(kinds)
    swap_in, refs = refs[:n_swap], refs[n_swap:]
    spread = mode != "last"
    if spread:
        all_ref, refs = refs[0], refs[1:]
    outs, refs = refs[:n_out], refs[n_out:]
    swap_out, refs = refs[:n_swap], refs[n_swap:]
    aux, refs = refs[:n_aux], refs[n_aux:]
    left, right, part, got, near_x, near_y, from_x, from_y, block, acc, send, recv, local = refs[:13]
    rows, width = block.shape
    cut = near_x.shape[0]
    y, x, c = here()
    to_x, to_y, to_c = {"gx": 1 - x}, {"gy": 1 - y}, {"core": 1 - c}
    chips = [(1 - y, 1 - x), (y, 1 - x), (1 - y, x), (y, x)]
    low, high = pl.ds(0, cut), pl.ds(cut, rows - cut)

    def push(k, src, dst, to):
        copy = pltpu.make_async_remote_copy(
            src_ref=src, dst_ref=dst, send_sem=send.at[k], recv_sem=recv.at[k], device_id=to, device_id_type=MESH
        )
        copy.start()
        return copy

    def add(k, extra, start, size, offset=0):
        @pl.loop(0, size // SLAB)
        def _(step):
            at = pl.ds(pl.multiple_of(start + step * SLAB, SLAB), SLAB)
            of = pl.ds(pl.multiple_of(start - offset + step * SLAB, SLAB), SLAB)
            part[k, c, at] = (part[k, c, at].astype(F32) + extra[of].astype(F32)).astype(BF16)

    loads = [pltpu.make_async_copy(left_ref.at[a * 2 + b], left.at[k], local.at[k]) for k, (a, b) in enumerate(chips)]
    load_right = pltpu.make_async_copy(right_ref, right, local.at[4])
    load_aux = [pltpu.make_async_copy(r, v, local.at[5 + k]) for k, (r, v) in enumerate(zip(aux_refs, aux))]
    loads[0].start()
    load_right.start()
    for load in loads[1:] + load_aux:
        load.start()
    if n_swap:
        greet([name for _, name in swap_peers(1, kinds)])
        swap_finish = swap_begin(1, kinds, swap_in, swap_out, *refs[13:])
    else:
        greet([to_x, to_y, to_c])

    def product(k):
        loads[k].wait()

        @pl.loop(0, width // CHIP_COLS)
        def _(step):
            at = pl.ds(pl.multiple_of(step * CHIP_COLS, CHIP_COLS), CHIP_COLS)
            here_part = dot_cols(left[k], right[at]) if across else dot(left[k], right[:, at])
            part[k, 0, :, at] = here_part[:rows].astype(BF16)
            part[k, 1, :, at] = here_part[rows:].astype(BF16)

        return push(k, part.at[k, 1 - c], got.at[k], to_c)

    load_right.wait()
    sent = [product(0), product(1)]
    sent[0].wait_recv()
    add(0, got.at[0], 0, rows)
    far_x = push(4, part.at[0, c, low], near_x, to_x)
    far_y = push(5, part.at[0, c, high], near_y, to_y)
    sent.append(product(2))
    sent[1].wait_recv()
    add(1, got.at[1], 0, rows)
    plain_x = push(6, part.at[1, c, low], from_x.at[low], to_x)
    sent[2].wait_recv()
    add(2, got.at[2], 0, rows)
    plain_y = push(7, part.at[2, c, high], from_y.at[high], to_y)
    sent.append(product(3))
    far_y.wait_recv()
    add(1, near_y, cut, rows - cut, cut)
    more_x = push(8, part.at[1, c, high], from_x.at[high], to_x)
    far_x.wait_recv()
    add(2, near_x, 0, cut)
    more_y = push(9, part.at[2, c, low], from_y.at[low], to_y)
    sent[3].wait_recv()
    for load in load_aux:
        load.wait()
    plain_x.wait_recv()
    plain_y.wait_recv()
    more_x.wait_recv()
    more_y.wait_recv()
    gains = gains_ref[...]
    acc[...] = jnp.zeros_like(acc)

    @pl.loop(0, rows // SLAB)
    def _(step):
        at = pl.ds(pl.multiple_of(step * SLAB, SLAB), SLAB)
        total = part[3, c, at].astype(F32) + got[3, at].astype(F32) + from_x[at].astype(F32) + from_y[at].astype(F32)
        held = [a[at].astype(F32) for a in aux]
        if mode == "one":
            first, normal, inverse = first_norm(by_rows(deep_alpha * held[0] + total, zs, piece), gains)
            outs[0][at] = first
            outs[1][at] = normal
            outs[2][at] = jnp.broadcast_to(inverse, (SLAB, 128))
            block[at] = first.astype(BF16)
        elif mode == "back":
            d_pre, terms, d_first = first_back(total, held[0], held[1], held[2][:, 0:1], gains)
            outs[0][at] = d_pre
            block[at] = in_order(d_pre, zs, piece).astype(BF16)
            acc[0] += terms
            acc[1] += d_first
        else:
            outs[0][at] = in_order(deep_alpha * held[0] + total, zs, piece).astype(BF16)

    if mode == "back":
        outs[-1][0:1] = jnp.sum(acc[0], axis=0, keepdims=True)
        outs[-1][1:2] = jnp.sum(acc[1], axis=0, keepdims=True)
    for copy in sent + [far_x, far_y, plain_x, plain_y, more_x, more_y]:
        copy.wait_send()
    if n_swap:
        swap_finish()
    if spread:
        spread_block(cut, 10, block, all_ref, send, recv, local.at[4])


def group_fold(name, zs, mode, left, right, gains, aux, out_types, extras=(), kinds=()):
    across = mode != "one"
    rows, depth = left.shape[0] // 8, left.shape[1]
    width = gains.shape[1]
    cut = rows // 2
    spread = mode != "last"
    out_shape = [jax.ShapeDtypeStruct((8, rows, width), BF16)] * spread + out_types
    n, n_swap = len(aux), len(extras)
    n_sems = 23 if spread else 10
    return pl.pallas_call(
        functools.partial(fold_kernel, mode, across, zs, width // (8 * zs), n, len(out_types), kinds),
        out_shape=out_shape + swap_shapes(1, extras, kinds),
        in_specs=[ANY, ANY, ROWS] + [ANY] * (n + n_swap),
        out_specs=[ANY] * spread + [ROWS] * len(out_types) + [ANY] * n_swap,
        scratch_shapes=[pltpu.VMEM(a.shape, a.dtype) for a in aux]
        + [
            pltpu.VMEM((4, 2 * rows, depth), BF16),
            pltpu.VMEM(right.shape, BF16),
            pltpu.VMEM((4, 2, rows, width), BF16),
            pltpu.VMEM((4, rows, width), BF16),
            pltpu.VMEM((cut, width), BF16),
            pltpu.VMEM((rows - cut, width), BF16),
            pltpu.VMEM((rows, width), BF16),
            pltpu.VMEM((rows, width), BF16),
            pltpu.VMEM((rows, width), BF16),
            pltpu.VMEM((2, SLAB, width), F32),
            pltpu.SemaphoreType.DMA((n_sems,)),
            pltpu.SemaphoreType.DMA((n_sems,)),
            pltpu.SemaphoreType.DMA((5 + n,)),
        ]
        + (swap_scratch(1, kinds) if n_swap else []),
        compiler_params=pltpu.CompilerParams(
            collective_id=name, has_side_effects=True, vmem_limit_bytes=50 * 2**20
        ),
        cost_estimate=pl.CostEstimate(flops=0, bytes_accessed=(200 if spread else 110) * 2**20, transcendentals=0),
    )(left.reshape(4, 2 * rows, depth), right, gains, *aux, *extras)


def turn_kernel(
    zs, piece, x_ref, in_ref, out_ref, gains_ref, first_ref, grad_ref,
    all_ref, kept_ref, right_ref, result_ref, d_pre_ref, sums_ref, dw_ref,
    first, grad, w_in, kept, left, right, part, got, near_x, near_y, from_x, from_y, whole, dw, acc,
    fold_send, fold_recv, all_send, all_recv, line_send, line_recv, local, x_local
):
    rows = first.shape[0]
    tile = left.shape[2]
    wide = right.shape[2]
    y, x, c = here()
    z = lax.axis_index("z")
    to_x, to_y, to_c = {"gx": 1 - x}, {"gy": 1 - y}, {"core": 1 - c}
    chips = [(1 - y) * 2 + 1 - x, y * 2 + 1 - x, (1 - y) * 2 + x, y * 2 + x]
    me, by_x, by_y, far = place(y, x, c), place(y, 1 - x, c), place(1 - y, x, c), place(1 - y, 1 - x, c)
    other, other_x, other_y, other_far = (
        place(y, x, 1 - c),
        place(y, 1 - x, 1 - c),
        place(1 - y, x, 1 - c),
        place(1 - y, 1 - x, 1 - c),
    )
    half = rows // 2
    most = -(-half // (2 * SLAB)) * SLAB
    lows = [(0, most), (half, half - most)]
    highs = [(most, half - most), (2 * half - most, most)]
    top, bottom = pl.ds(0, half), pl.ds(half, half)
    sent = []

    def remote(sems, k, src, dst, to):
        return pltpu.make_async_remote_copy(
            src_ref=src,
            dst_ref=dst,
            send_sem=sems[0].at[k],
            recv_sem=sems[1].at[k],
            device_id=to,
            device_id_type=MESH,
        )

    def push(sems, k, src, dst, to):
        copy = remote(sems, k, src, dst, to)
        copy.start()
        sent.append(copy)

    def landed(sems, k, dst):
        remote(sems, k, dst, dst, to_c).wait_recv()

    folds, alls, lines = (fold_send, fold_recv), (all_send, all_recv), (line_send, line_recv)

    load_out = pltpu.make_async_copy(out_ref, right.at[z], local.at[0])
    load_in = pltpu.make_async_copy(in_ref, w_in, local.at[1])
    load_first = pltpu.make_async_copy(first_ref, first, local.at[2])
    load_grad = pltpu.make_async_copy(grad_ref, grad, local.at[3])

    def load_x(g):
        return pltpu.make_async_copy(x_ref.at[g], whole.at[g], x_local.at[g])

    load_out.start()
    load_in.start()
    for g in range(8):
        load_x(g).start()
    load_first.start()
    load_grad.start()

    barrier = pltpu.get_barrier_semaphore()
    for to in (to_x, to_y, to_c):
        pl.semaphore_signal(barrier, inc=1, device_id=to, device_id_type=MESH)

    @pl.when(z > 0)
    def _():
        pl.semaphore_signal(barrier, inc=1, device_id={"z": z - 1}, device_id_type=MESH)

    @pl.when(z < zs - 1)
    def _():
        pl.semaphore_signal(barrier, inc=1, device_id={"z": z + 1}, device_id_type=MESH)

    inside = (z > 0) & (z < zs - 1)

    @pl.when(inside)
    def _():
        pl.semaphore_wait(barrier, 5)

    @pl.when(jnp.logical_not(inside))
    def _():
        pl.semaphore_wait(barrier, 4)

    def shard_of(step, up):
        return z - step if up else z + step

    def hop(step, up):
        ref = right.at[shard_of(step, up)]
        return remote(lines, 2 * step + (0 if up else 1), ref, ref, {"z": z + 1 if up else z - 1})

    def sends(step, up):
        return (z >= step) & (z < zs - 1) if up else (z <= zs - 1 - step) & (z > 0)

    def gets(step, up):
        return z >= step + 1 if up else z <= zs - 2 - step

    def line_serve(step):
        for up in (True, False):

            @pl.when(gets(step - 1, up) & sends(step, up))
            def _(up=up):
                landed(lines, 2 * (step - 1) + (0 if up else 1), right.at[shard_of(step, up)])
                hop(step, up).start()

    def line_take(step):
        for up in (True, False):

            @pl.when(gets(step - 1, up) & jnp.logical_not(sends(step, up)))
            def _(up=up):
                landed(lines, 2 * (step - 1) + (0 if up else 1), right.at[shard_of(step, up)])

    load_out.wait()
    for up in (True, False):

        @pl.when(sends(0, up))
        def _(up=up):
            hop(0, up).start()


    load_in.wait()

    @pl.loop(0, 8)
    def _(g):
        @pl.when(g == 6)
        def _():
            line_serve(1)

        load_x(g).wait()
        projected = dot(whole[g], w_in[...])
        gate, up = projected[:, :tile], projected[:, tile:]
        act, slope = gate_parts(gate)
        left[g] = (act * up).astype(BF16)
        kept[g] = jnp.concatenate([up * slope, act], axis=1).astype(BF16)

    keep = pltpu.make_async_copy(kept, kept_ref, local.at[4])
    keep.start()

    def add(k, extra, start, offset, at):
        @pl.loop(0, half // SLAB)
        def _(step):
            row = pl.ds(pl.multiple_of(start + step * SLAB, SLAB), SLAB)
            of = pl.ds(pl.multiple_of(start - offset + step * SLAB, SLAB), SLAB)
            part[k, c, row, at] = (part[k, c, row, at].astype(F32) + extra[of, at].astype(F32)).astype(BF16)

    def chip_sum(k, at):
        add(k, got.at[k], 0, 0, at)
        add(k, got.at[k], half, 0, at)

    def product(k, block, at):
        found = dot(left[pl.ds(2 * chips[k], 2)].reshape(2 * rows, tile), right[block])
        part[k, 0, :, at] = found[:rows].astype(BF16)
        part[k, 1, :, at] = found[rows:].astype(BF16)

    def block_at(i):
        if i == 0:
            return z
        below = z < zs // 2
        near = jnp.where(below, z, zs - 1 - z)
        spot = jnp.where(i <= 2 * near, jnp.where(i % 2 == 1, near - (i + 1) // 2, near + i // 2), i)
        return jnp.where(below, spot, zs - 1 - spot)

    def block_cols(i):
        return pl.ds(pl.multiple_of(block_at(i) * wide, wide), wide)

    def fold_start(i):
        b, block, at = 8 * i, block_at(i), block_cols(i)
        rest = pl.ds(1, 3)
        product(0, block, at)
        push(folds, b, part.at[0, 1 - c, :, at], got.at[0, :, at], to_c)
        for k in (1, 2, 3):
            product(k, block, at)
        push(folds, b + 1, part.at[rest, 1 - c, :, at], got.at[rest, :, at], to_c)
        landed(folds, b, got.at[0, :, at])
        chip_sum(0, at)
        push(folds, b + 2, part.at[0, c, top, at], near_x.at[:, at], to_x)
        push(folds, b + 3, part.at[0, c, bottom, at], near_y.at[:, at], to_y)
        landed(folds, b + 1, got.at[rest, :, at])
        chip_sum(1, at)
        push(folds, b + 4, part.at[1, c, top, at], from_x.at[top, at], to_x)
        chip_sum(2, at)
        push(folds, b + 5, part.at[2, c, bottom, at], from_y.at[bottom, at], to_y)

    def fold_end(i):
        b, at = 8 * i, block_cols(i)
        landed(folds, b + 3, near_y.at[:, at])
        add(1, near_y, half, half, at)
        push(folds, b + 6, part.at[1, c, bottom, at], from_x.at[bottom, at], to_x)
        landed(folds, b + 2, near_x.at[:, at])
        add(2, near_x, 0, 0, at)
        push(folds, b + 7, part.at[2, c, top, at], from_y.at[top, at], to_y)

    gains = gains_ref[...]
    def reorder(ref, how):
        @pl.loop(0, rows // SLAB)
        def _(step):
            at = pl.ds(pl.multiple_of(step * SLAB, SLAB), SLAB)
            ref[at] = how(ref[at].astype(F32), zs, piece).astype(BF16)

    line_take(1)
    fold_start(0)
    fold_start(1)
    fold_end(0)
    for i in range(2, zs):
        if i < zs - 1:
            line_serve(i)
        fold_end(i - 1)
        if i == 2:
            load_grad.wait()
            reorder(grad, by_rows)
        line_take(i)
        fold_start(i)
    fold_end(zs - 1)
    carry = pltpu.make_async_copy(right, right_ref, local.at[5])
    carry.start()
    load_first.wait()
    acc[...] = jnp.zeros_like(acc)
    for i in range(zs):
        at = block_cols(i)
        landed(folds, 8 * i + 4, from_x.at[top, at])
        landed(folds, 8 * i + 5, from_y.at[bottom, at])
        landed(folds, 8 * i + 6, from_x.at[bottom, at])
        landed(folds, 8 * i + 7, from_y.at[top, at])

    def low(i):
        return pl.ds(*lows[i])

    def high(i):
        return pl.ds(*highs[i])

    def span(i):
        return pl.ds(i * half, half)

    def norm(i):
        @pl.loop(0, half // SLAB)
        def _(step):
            at = pl.ds(pl.multiple_of(i * half + step * SLAB, SLAB), SLAB)
            total = part[3, c, at].astype(F32) + got[3, at].astype(F32)
            total += from_x[at].astype(F32) + from_y[at].astype(F32)
            dy = grad[at].astype(F32)
            result, d_pre, terms = second_norm(total, first[at], dy, gains)
            result_ref[at] = result.astype(BF16)
            d_pre_ref[at] = d_pre
            whole[me, at] = d_pre.astype(BF16)
            acc[0] += terms
            acc[1] += dy

        b = 13 * i
        push(alls, b, whole.at[me, low(i)], whole.at[me, low(i)], to_x)
        push(alls, b + 1, whole.at[me, high(i)], whole.at[me, high(i)], to_y)
        push(alls, b + 2, whole.at[me, high(i)], whole.at[me, high(i)], to_x)
        push(alls, b + 3, whole.at[me, low(i)], whole.at[me, low(i)], to_y)
        push(alls, b + 4, whole.at[me, span(i)], whole.at[me, span(i)], to_c)

    def pass_on(i, k, slot, at, onward):
        ref = whole.at[slot, at]
        landed(alls, 13 * i + k, ref)
        for where, to in onward:
            push(alls, 13 * i + where, ref, ref, to)

    def spread_first(i):
        pass_on(i, 0, by_x, low(i), [(5, to_y), (7, to_c)])
        pass_on(i, 1, by_y, high(i), [(6, to_x), (8, to_c)])

    def spread_rest(i):
        pass_on(i, 2, by_x, high(i), [(9, to_c)])
        pass_on(i, 3, by_y, low(i), [(10, to_c)])

    def spread_far(i):
        pass_on(i, 5, far, low(i), [(11, to_c)])
        pass_on(i, 6, far, high(i), [(12, to_c)])

    outward = []

    def gradient(k, last=False, first_one=False):
        pair = pl.ds(2 * chips[k], 2)
        outward.append(pltpu.make_async_copy(whole.at[pair], all_ref.at[pair], local.at[6 + k]))
        outward[-1].start()

        @pl.loop(0, zs)
        def _(block):
            at = pl.ds(pl.multiple_of(block * wide, wide), wide)
            found = dot_rows(left[pair].reshape(2 * rows, tile), whole[pair, :, at].reshape(2 * rows, wide))
            if first_one:
                dw[block] = found
            elif last:
                dw_ref[block] = (dw[block] + found).astype(BF16)
            else:
                dw[block] += found

    norm(0)
    norm(1)
    reorder(result_ref, in_order)
    spread_first(0)
    for i in (0, 1):
        landed(alls, 13 * i + 4, whole.at[other, span(i)])
    gradient(3, first_one=True)
    spread_rest(0)
    spread_first(1)
    spread_rest(1)
    for i in (0, 1):
        landed(alls, 13 * i + 7, whole.at[other_x, low(i)])
        landed(alls, 13 * i + 9, whole.at[other_x, high(i)])
    gradient(1)
    spread_far(0)
    for i in (0, 1):
        landed(alls, 13 * i + 8, whole.at[other_y, high(i)])
        landed(alls, 13 * i + 10, whole.at[other_y, low(i)])
    gradient(2)
    sums_ref[0:1] = jnp.sum(acc[0], axis=0, keepdims=True)
    sums_ref[1:2] = jnp.sum(acc[1], axis=0, keepdims=True)
    spread_far(1)
    for i in (0, 1):
        landed(alls, 13 * i + 11, whole.at[other_far, low(i)])
        landed(alls, 13 * i + 12, whole.at[other_far, high(i)])
    gradient(0, last=True)
    for copy in outward + [keep, carry]:
        copy.wait()
    for copy in sent:
        copy.wait_send()
    for step in range(zs - 1):
        for up in (True, False):

            @pl.when(sends(step, up))
            def _(step=step, up=up):
                hop(step, up).wait_send()


def turn(zs, x, w_in, w_out, gains, first, grad):
    rows = x.shape[0] // 8
    units, wide = w_out.shape
    width = gains.shape[1]
    half = rows // 2
    by_z = (zs, units, wide)
    return pl.pallas_call(
        functools.partial(turn_kernel, zs, width // (8 * zs)),
        out_shape=[
            jax.ShapeDtypeStruct((8, rows, width), BF16),
            jax.ShapeDtypeStruct((8, rows, 2 * units), BF16),
            jax.ShapeDtypeStruct(by_z, BF16),
            jax.ShapeDtypeStruct((rows, width), BF16),
            jax.ShapeDtypeStruct((rows, width), F32),
            jax.ShapeDtypeStruct((8, width), F32),
            jax.ShapeDtypeStruct(by_z, BF16),
        ],
        in_specs=[ANY, ANY, ANY, ROWS, ANY, ANY],
        out_specs=[ANY] * 3 + [ROWS] * 4,
        scratch_shapes=[
            pltpu.VMEM((rows, width), F32),
            pltpu.VMEM((rows, width), BF16),
            pltpu.VMEM(w_in.shape, BF16),
            pltpu.VMEM((8, rows, 2 * units), BF16),
            pltpu.VMEM((8, rows, units), BF16),
            pltpu.VMEM(by_z, BF16),
            pltpu.VMEM((4, 2, rows, width), BF16),
            pltpu.VMEM((4, rows, width), BF16),
            pltpu.VMEM((half, width), BF16),
            pltpu.VMEM((half, width), BF16),
            pltpu.VMEM((rows, width), BF16),
            pltpu.VMEM((rows, width), BF16),
            pltpu.VMEM((8, rows, width), BF16),
            pltpu.VMEM(by_z, F32),
            pltpu.VMEM((2, SLAB, width), F32),
            pltpu.SemaphoreType.DMA((8 * zs,)),
            pltpu.SemaphoreType.DMA((8 * zs,)),
            pltpu.SemaphoreType.DMA((26,)),
            pltpu.SemaphoreType.DMA((26,)),
            pltpu.SemaphoreType.DMA((2 * (zs - 1),)),
            pltpu.SemaphoreType.DMA((2 * (zs - 1),)),
            pltpu.SemaphoreType.DMA((10,)),
            pltpu.SemaphoreType.DMA((8,)),
        ],
        compiler_params=pltpu.CompilerParams(collective_id=1, has_side_effects=True, vmem_limit_bytes=60 * 2**20),
        cost_estimate=pl.CostEstimate(flops=0, bytes_accessed=380 * 2**20, transcendentals=0),
    )(x.reshape(8, rows, width), w_in, w_out, gains, first, grad)


def swap_kernel(zs, kinds, *refs):
    n = len(kinds)
    greet([name for _, name in swap_peers(zs, kinds)])
    swap_begin(zs, kinds, refs[:n], refs[n : 2 * n], *refs[2 * n :])()


def group_swap(name, zs, arrays, kinds):
    n = len(arrays)
    return pl.pallas_call(
        functools.partial(swap_kernel, zs, kinds),
        out_shape=swap_shapes(zs, arrays, kinds),
        in_specs=[ANY] * n,
        out_specs=[ANY] * n,
        scratch_shapes=swap_scratch(zs, kinds),
        compiler_params=pltpu.CompilerParams(collective_id=name, has_side_effects=True),
        cost_estimate=pl.CostEstimate(flops=0, bytes_accessed=50 * 2**20, transcendentals=0),
    )(*arrays)


def ff_kernel(x_ref, w_ref, hidden_ref, kept_ref):
    tile = hidden_ref.shape[1]
    projected = dot(x_ref[...], w_ref[...])
    gate, up = projected[:, :tile], projected[:, tile:]
    act, slope = gate_parts(gate)
    hidden_ref[...] = (act * up).astype(BF16)
    kept_ref[...] = jnp.concatenate([up * slope, act], axis=1).astype(BF16)


def ff_back_kernel(grad_ref, w_ref, kept_ref, out_ref):
    zs, _, wide = w_ref.shape
    d_hidden = dot_cols(grad_ref[:, :wide], w_ref[0])
    for z in range(1, zs):
        d_hidden += dot_cols(grad_ref[:, z * wide : (z + 1) * wide], w_ref[z])
    out_ref[...] = (jnp.concatenate([d_hidden, d_hidden], axis=1) * kept_ref[...].astype(F32)).astype(BF16)


FF_ROWS = 256


def ff_rows(width):
    return pl.BlockSpec((FF_ROWS, width), lambda i: (i, 0))


def ff_forward(x, w):
    rows, depth = x.shape
    wide = w.shape[1]
    return pl.pallas_call(
        ff_kernel,
        grid=(rows // FF_ROWS,),
        in_specs=[ff_rows(depth), pl.BlockSpec((depth, wide), lambda i: (0, 0))],
        out_specs=[ff_rows(wide // 2), ff_rows(wide)],
        out_shape=[jax.ShapeDtypeStruct((rows, wide // 2), BF16), jax.ShapeDtypeStruct((rows, wide), BF16)],
        compiler_params=PARAMS,
        cost_estimate=pl.CostEstimate(flops=2 * rows * depth * wide, bytes_accessed=20 * 2**20, transcendentals=0),
    )(x, w)


def ff_backward(grad, w, kept):
    rows, depth = grad.shape
    wide = kept.shape[1]
    return pl.pallas_call(
        ff_back_kernel,
        grid=(rows // FF_ROWS,),
        in_specs=[ff_rows(depth), pl.BlockSpec(w.shape, lambda i: (0, 0, 0)), ff_rows(wide)],
        out_specs=ff_rows(wide),
        out_shape=jax.ShapeDtypeStruct((rows, wide), BF16),
        compiler_params=PARAMS,
        cost_estimate=pl.CostEstimate(flops=rows * depth * wide, bytes_accessed=20 * 2**20, transcendentals=0),
    )(grad, w, kept)


def cut_kernel(in_ref, out_ref, in_blocks, out_blocks, wide):
    group, _, double = in_blocks.shape
    tile, ff = double // 2, out_ref.shape[1]
    span = group * tile
    odd = ff % 128
    live = lax.broadcasted_iota(jnp.int32, (in_ref.shape[0], span), 1) < ff
    wide[...] = jnp.zeros_like(wide)
    wide[:, : 2 * ff] = in_ref[...].astype(F32)
    gate = jnp.where(live, wide[:, :span], 0.0)
    up = pltpu.roll(wide[:, ff - odd : ff - odd + span], span - odd, 1)
    up = jnp.where(live, up, 0.0)
    wide[:, :span] = jnp.zeros_like(live, F32)
    wide[:, :ff] = out_ref[...].astype(F32)
    down = wide[:, :span]
    for g in range(group):
        at = slice(g * tile, (g + 1) * tile)
        in_blocks[g] = jnp.concatenate([gate[:, at], up[:, at]], axis=1).astype(BF16)
        out_blocks[g] = down[:, at].astype(BF16)


def cut_ff(w_in, w_out, group, tile):
    rows, ff = w_out.shape
    return pl.pallas_call(
        cut_kernel,
        grid=(rows // 16,),
        in_specs=[pl.BlockSpec((16, 2 * ff), lambda i: (i, 0)), pl.BlockSpec((16, ff), lambda i: (i, 0))],
        out_specs=[
            pl.BlockSpec((group, 16, 2 * tile), lambda i: (0, i, 0)),
            pl.BlockSpec((group, 16, tile), lambda i: (0, i, 0)),
        ],
        out_shape=[
            jax.ShapeDtypeStruct((group, rows, 2 * tile), BF16),
            jax.ShapeDtypeStruct((group, rows, tile), BF16),
        ],
        scratch_shapes=[pltpu.VMEM((16, -(-(ff + group * tile) // 128) * 128), F32)],
        compiler_params=PARAMS,
    )(w_in, w_out)


def join_kernel(in_blocks, out_blocks, in_ref, out_ref):
    group, _, double = in_blocks.shape
    tile, ff = double // 2, out_ref.shape[1]
    odd = ff % 128
    blocks = [in_blocks[g].astype(F32) for g in range(group)]
    gate = jnp.concatenate([block[:, :tile] for block in blocks], axis=1)
    up = jnp.concatenate([block[:, tile:] for block in blocks], axis=1)
    up = pltpu.roll(up, odd, 1)
    lane = lax.broadcasted_iota(jnp.int32, (up.shape[0], 128), 1)
    in_ref[:, : ff - odd] = gate[:, : ff - odd]
    in_ref[:, ff - odd : ff - odd + 128] = jnp.where(lane < odd, gate[:, ff - odd : ff - odd + 128], up[:, :128])
    in_ref[:, ff - odd + 128 :] = up[:, 128 : ff + odd]
    down = jnp.concatenate([out_blocks[g].astype(F32) for g in range(group)], axis=1)
    out_ref[...] = down[:, :ff]


def join_ff(in_blocks, out_blocks, ff):
    group, rows, tile = out_blocks.shape
    return pl.pallas_call(
        join_kernel,
        grid=(rows // 16,),
        in_specs=[
            pl.BlockSpec((group, 16, 2 * tile), lambda i: (0, i, 0)),
            pl.BlockSpec((group, 16, tile), lambda i: (0, i, 0)),
        ],
        out_specs=[pl.BlockSpec((16, 2 * ff), lambda i: (i, 0)), pl.BlockSpec((16, ff), lambda i: (i, 0))],
        out_shape=[jax.ShapeDtypeStruct((rows, 2 * ff), F32), jax.ShapeDtypeStruct((rows, ff), F32)],
        compiler_params=PARAMS,
    )(in_blocks, out_blocks)


def closing_kernel(zs, sum_ref, rows_ref, qkv_ref, dense_ref, total_ref, got, mine, lines, *refs):
    send, recv, local, line_send, line_recv = refs
    y, x, c = here()
    z = lax.axis_index("z")
    me = place(y, x, c)
    wide = got.shape[2]
    width = wide // 3
    piece = got.shape[1]
    found = swap_peers(zs, ("line",))
    greet([name for _, name in found])
    copies, comes = [], []
    for k, (peer, name) in enumerate(found[:7]):
        sems = dict(send_sem=send.at[k], recv_sem=recv.at[k], device_id=name, device_id_type=MESH)
        src = rows_ref.at[peer, :, pl.ds(0, wide)]
        copies.append(pltpu.make_async_remote_copy(src_ref=src, dst_ref=got.at[me], **sems))
        comes.append(pltpu.make_async_remote_copy(src_ref=got.at[peer], dst_ref=got.at[peer], **sems))
    for k, (peer, name) in enumerate(found[7:]):
        sems = dict(send_sem=line_send.at[k], recv_sem=line_recv.at[k], device_id=name, device_id_type=MESH)
        copies.append(pltpu.make_async_remote_copy(src_ref=sum_ref, dst_ref=lines.at[z], **sems))
        comes.append(pltpu.make_async_remote_copy(src_ref=lines.at[peer], dst_ref=lines.at[peer], **sems))
    for copy in copies:
        copy.start()
    keeps = [
        pltpu.make_async_copy(rows_ref.at[me, :, pl.ds(0, wide)], got.at[me], local.at[0]),
        pltpu.make_async_copy(sum_ref, lines.at[z], local.at[1]),
        pltpu.make_async_copy(rows_ref.at[:, :, pl.ds(wide, width)], mine, local.at[2]),
    ]
    for keep in keeps:
        keep.start()
    keeps[2].wait()
    for at in range(0, piece, 16):
        rows = jnp.concatenate([mine[g, at : at + 16] for g in range(8)], axis=1).astype(F32)
        dense_ref[at : at + 16] = rows
    for come in comes:
        come.wait_recv()
    for keep in keeps[:2]:
        keep.wait()
    for g in range(8):
        for j in range(3):
            at = pl.ds(j * D + g * width, width)
            qkv_ref[:, at] = got[g, :, j * width : (j + 1) * width].astype(F32)
    total = lines[0]
    for k in range(1, zs):
        total += lines[k]
    part = total[:, :piece]
    for k in range(1, zs):
        part = jnp.where(z == k, total[:, k * piece : (k + 1) * piece], part)
    total_ref[...] = part
    for copy in copies:
        copy.wait_send()


def closing(zs, sums, rows):
    _, piece, columns = rows.shape
    width = columns // 4
    return pl.pallas_call(
        functools.partial(closing_kernel, zs),
        out_shape=[
            jax.ShapeDtypeStruct((piece, 3 * D), F32),
            jax.ShapeDtypeStruct((piece, D), F32),
            jax.ShapeDtypeStruct((8, piece), F32),
        ],
        in_specs=[ROWS, ANY],
        out_specs=[ROWS] * 3,
        scratch_shapes=[
            pltpu.VMEM((8, piece, 3 * width), BF16),
            pltpu.VMEM((8, piece, width), BF16),
            pltpu.VMEM((zs, 8, width), F32),
            pltpu.SemaphoreType.DMA((7,)),
            pltpu.SemaphoreType.DMA((7,)),
            pltpu.SemaphoreType.DMA((3,)),
            pltpu.SemaphoreType.DMA((zs - 1,)),
            pltpu.SemaphoreType.DMA((zs - 1,)),
        ],
        compiler_params=pltpu.CompilerParams(collective_id=5, has_side_effects=True, vmem_limit_bytes=24 * 2**20),
        cost_estimate=pl.CostEstimate(flops=0, bytes_accessed=50 * 2**20, transcendentals=0),
    )(sums, rows)


def on_device(sizes, x_in, d_out, w_qkv, w_dense, w_in, w_out, gone, bone, gtwo, btwo, flags, span_start, span_len):
    gy, gx, cores, zs = sizes
    piece = w_qkv.shape[0]
    ff = w_out.shape[1]
    group = gy * gx * cores
    width = D // group
    tile = -(-ff // (group * 64)) * 64
    own = gy == 2

    def permute(array):
        lead = array.shape[:-1]
        return jnp.swapaxes(array.reshape(lead + (group, zs, piece)), -3, -2).reshape(lead + (D,))

    def restore(array):
        lead = array.shape[:-1]
        return jnp.swapaxes(array.reshape(lead + (zs, group, piece)), -3, -2).reshape(lead + (D,))

    def swap(name, arrays, kinds):
        if own:
            return group_swap(name, zs, arrays, kinds)
        ways = {
            "swap": lambda a: lax.all_to_all(a, GROUP, 0, 0, tiled=True),
            "group": lambda a: lax.all_gather(a, GROUP, axis=0),
            "line": lambda a: lax.all_gather(a, "z", axis=0),
        }
        return [ways[k](a) for a, k in zip(arrays, kinds)]

    def spread_rows(block):
        whole = group_gather(block) if own else lax.all_gather(block, GROUP, axis=0)
        return whole.reshape(group * block.shape[0], block.shape[1])

    rows_f32 = jax.ShapeDtypeStruct((SEQ_LEN, D), F32)
    rows_low = jax.ShapeDtypeStruct((SEQ_LEN, D), BF16)
    sums_type = jax.ShapeDtypeStruct((8, D), F32)

    def fold(partial):
        return lax.psum_scatter(partial.astype(BF16), GROUP, scatter_dimension=0, tiled=True).astype(F32)

    def stack_sums(*arrays):
        return jnp.pad(jnp.stack([jnp.sum(a, axis=0) for a in arrays]), ((0, 6), (0, 0)))

    def fold_one(left, right, x, gains):
        if own:
            kinds = [rows_f32, rows_f32, jax.ShapeDtypeStruct((SEQ_LEN, 128), F32)]
            whole, first, normal, inverse = group_fold(0, zs, "one", left, right, gains, [x], kinds)
            return whole.reshape(left.shape[0], D), first, normal, inverse
        first, normal, inverse = first_norm(permute(deep_alpha * x.astype(F32) + fold(dot(left, right))), gains)
        return spread_rows(first.astype(BF16)), first, normal, inverse

    def ff_turn(x, w_in, w_out, first, grad, gains):
        if own:
            whole, kept, w_out, result, d_pre, sums, d_out = turn(zs, x, w_in, w_out, gains, first, grad)
            rows = x.shape[0]
            return whole.reshape(rows, D), kept.reshape(rows, -1), w_out, result, d_pre, sums, d_out
        w_out = lax.all_gather(w_out, "z", axis=0)
        hidden, kept = ff_forward(x, w_in)
        grad = permute(grad).astype(F32)
        right = jnp.swapaxes(w_out, 0, 1).reshape(-1, D)
        result, d_pre, terms = second_norm(fold(dot(hidden, right)), first, grad, gains)
        whole = spread_rows(d_pre.astype(BF16))
        d_out = jnp.swapaxes(dot_rows(hidden, whole).reshape(-1, zs, D // zs), 0, 1).astype(BF16)
        return whole, kept, w_out, restore(result.astype(BF16)), d_pre, stack_sums(terms, grad), d_out

    def fold_back(left, right, d_pre_two, normal, inverse, gains):
        if own:
            kinds = [rows_f32, sums_type]
            whole, d_pre, sums = group_fold(7, zs, "back", left, right, gains, [d_pre_two, normal, inverse], kinds)
            return whole.reshape(left.shape[0], D), d_pre, sums
        d_pre, terms, d_first = first_back(fold(dot_cols(left, right)), d_pre_two, normal, inverse, gains)
        return spread_rows(restore(d_pre).astype(BF16)), d_pre, stack_sums(terms, d_first)

    def fold_last(left, right, d_pre, gains, extras, kinds):
        if own:
            return group_fold(8, zs, "last", left, right, gains, [d_pre], [rows_low], extras, kinds)
        out = restore((deep_alpha * d_pre + fold(dot_cols(left, right))).astype(BF16))
        return [out] + swap(8, extras, kinds)

    def gather(block):
        return lax.all_gather(block, "z", axis=0, tiled=True)

    def scatter(partial):
        return lax.psum_scatter(partial.astype(BF16), "z", scatter_dimension=0, tiled=True)

    masked = jnp.max(flags) > 0
    prefix = jnp.where(masked, SEQ_LEN, SEQ_LEN - span_len[0])
    info = jnp.concatenate([gone, bone, gtwo, btwo, jnp.stack([prefix, span_start[0]]).astype(BF16)])
    info = jnp.pad(info[None, :], ((0, 15), (0, -info.shape[0] % 128)))

    qkv_blocks = jnp.moveaxis(w_qkv.reshape(piece, 3, group, width), 2, 0).reshape(group, piece, 3 * width)
    w_dense_part = gather(w_dense)
    qkv_blocks, info = swap(2, [qkv_blocks, info], ("swap", "group"))
    w_qkv_part = gather(qkv_blocks.reshape(group * piece, 3 * width))
    info = info[:, 0]
    place_info = info[:, 4 * piece : 4 * piece + 2].astype(jnp.int32)
    prefix, start = place_info[:, 0], place_info[:, 1]
    cosine, sine = tables(prefix, start)
    in_blocks, out_blocks = cut_ff(w_in, w_out, group, tile)
    in_blocks, out_blocks, qkv_blocks = lax.optimization_barrier((in_blocks, out_blocks, qkv_blocks))
    info = jnp.pad(info, ((0, -group % 16), (0, 0)))
    in_blocks, out_blocks, info = swap(3, [in_blocks, out_blocks, info], ("swap", "swap", "line"))
    w_in_part = gather(in_blocks.reshape(group * piece, 2 * tile))
    out_rows = out_blocks.reshape(group * piece, tile).T
    x_next, in_blocks, w_dense_part = lax.optimization_barrier((permute(x_in), in_blocks, w_dense_part))
    x_all = spread_rows(x_next)
    gains = info[:, :group, : 4 * piece].astype(F32).reshape(zs, group, 4, piece)
    gains = jnp.pad(jnp.transpose(gains, (2, 0, 1, 3)).reshape(4, D), ((0, 4), (0, 0)))
    w_qkv_part, x_all, cosine, sine, gains = lax.optimization_barrier((w_qkv_part, x_all, cosine, sine, gains))
    packed = dot(x_all, w_qkv_part)
    qkv, context = attend(prefix, packed, cosine, sine)
    first_all, first, normal_one, inverse_one = fold_one(context, w_dense_part, x_in, gains)
    d_branch, kept, w_out_part, layer_out, d_pre_two, sums_two, d_w_out = ff_turn(
        first_all, w_in_part, out_rows, first, d_out, gains
    )
    d_w_out = lax.psum_scatter(d_w_out, "z", scatter_dimension=0)
    d_projected = ff_backward(d_branch, w_out_part, kept)
    d_w_in = dot_rows(first_all, d_projected).astype(BF16)
    d_w_in, d_projected = lax.optimization_barrier((d_w_in, d_projected))
    d_w_in = scatter(d_w_in)
    d_attn, d_pre_one, sums_one = fold_back(d_projected, w_in_part, d_pre_two, normal_one, inverse_one, gains)
    d_attn, d_w_out = lax.optimization_barrier((d_attn, d_w_out))
    d_context = dot_cols(d_attn, w_dense_part).astype(BF16)
    d_packed = attend_back(prefix, qkv, d_context, cosine, sine)
    d_w_qkv = dot_rows(x_all, d_packed).astype(BF16)
    d_dense = dot_rows(context, d_attn).astype(BF16).reshape(zs, piece, group, width)
    d_dense = jnp.swapaxes(d_dense, 1, 2).reshape(D, width)
    d_w_qkv = jnp.concatenate([d_w_qkv, d_dense], axis=1)
    sums = jnp.concatenate([sums_one[:2], sums_two[:2], jnp.zeros((4, D), F32)])
    d_packed, d_w_qkv, d_w_in, sums = lax.optimization_barrier((d_packed, d_w_qkv, d_w_in, sums))
    d_w_qkv = scatter(d_w_qkv)
    d_w_in, d_w_out = d_w_in.reshape(group, piece, 2 * tile), d_w_out.T.reshape(group, piece, tile)
    d_input, d_w_in, d_w_out, sums = fold_last(
        d_packed, w_qkv_part, d_pre_one, gains, [d_w_in, d_w_out, sums], ("swap", "swap", "group")
    )
    sums = jnp.sum(sums, axis=0).reshape(8, zs, group, piece)
    sums = lax.dynamic_index_in_dim(sums, lax.axis_index(GROUP), 2, keepdims=False).reshape(8, width)
    out_in, out_out = join_ff(d_w_in, d_w_out, ff)
    out_in, out_out, d_input, d_w_qkv, sums = lax.optimization_barrier((out_in, out_out, d_input, d_w_qkv, sums))
    if own:
        out_qkv, out_dense, sums = closing(zs, sums, d_w_qkv.reshape(group, piece, 4 * width))
    else:
        out_dense = d_w_qkv[:, 3 * width :].reshape(group, piece, width)
        out_dense = jnp.swapaxes(out_dense, 0, 1).reshape(piece, D).astype(F32)
        d_w_qkv = d_w_qkv[:, : 3 * width].reshape(group, piece, 3 * width)
        d_w_qkv, sums = swap(5, [d_w_qkv, sums], ("swap", "line"))
        out_qkv = jnp.transpose(d_w_qkv.astype(F32).reshape(group, piece, 3, width), (1, 2, 0, 3))
        out_qkv = out_qkv.reshape(piece, 3 * D)
        sums = jnp.sum(sums, axis=0).reshape(8, zs, piece)
        sums = lax.dynamic_index_in_dim(sums, lax.axis_index("z"), 1, keepdims=False)
    return layer_out, d_input, out_qkv, out_dense, out_in, out_out, sums[0], sums[1], sums[2], sums[3]


def solution(mesh):
    grp, shard = mesh.shape["grp"], mesh.shape["shard"]
    sizes = (grp // 4, 2, 2, shard)
    inner = Mesh(mesh.devices.reshape(sizes), ALL)
    rows, flat = P(ALL, None), P(ALL)
    return jax.shard_map(
        functools.partial(on_device, sizes),
        mesh=inner,
        in_specs=(rows,) * 6 + (flat,) * 7,
        out_specs=(rows,) * 6 + (flat,) * 4,
        check_vma=False,
    )
```

```python
import functools

import jax
import jax.numpy as jnp
from jax import lax
from jax.experimental import pallas as pl
from jax.experimental.pallas import tpu as pltpu
from jax.sharding import Mesh
from jax.sharding import PartitionSpec as P

HEADS = 16
HEAD = 128
SEQ_LEN = 224
D = HEADS * HEAD
deep_alpha = 6.928203230275509
norm_eps = 1e-05
far_below = -1e30
scale = HEAD ** (-0.5)

ALL = ("gy", "gx", "core", "z")
GROUP = ("gy", "gx", "core")
MESH = pl.DeviceIdType.MESH
F32 = jnp.float32
BF16 = jnp.bfloat16


def dot(left, right):
    return jnp.dot(left, right, preferred_element_type=F32)


def dot_rows(left, right):
    return lax.dot_general(left, right, (((0,), (0,)), ((), ())), preferred_element_type=F32)


def dot_cols(left, right):
    return lax.dot_general(left, right, (((1,), (1,)), ((), ())), preferred_element_type=F32)


def swap_halves(block):
    lane = lax.broadcasted_iota(jnp.int32, block.shape, 1)
    return jnp.where((lane & 32) == 0, pltpu.roll(block, 96, 1), pltpu.roll(block, 32, 1))


def seen(prefix):
    row = lax.broadcasted_iota(jnp.int32, (SEQ_LEN, SEQ_LEN), 0)
    col = lax.broadcasted_iota(jnp.int32, (SEQ_LEN, SEQ_LEN), 1)
    return (col < prefix) | (col <= row)


def softmax(queries, keys, visible):
    scores = jnp.where(visible, dot_cols(queries, keys), far_below)
    weights = jnp.exp(scores - jnp.max(scores, axis=1, keepdims=True))
    return weights / jnp.sum(weights, axis=1, keepdims=True)


def attend_kernel(prefix_ref, packed_ref, cos_ref, sin_ref, qkv_ref, context_ref):
    width = context_ref.shape[1]
    visible = seen(prefix_ref[pl.program_id(0)])
    cosine = cos_ref[0]
    sine = sin_ref[0]
    for head in range(width // HEAD):
        at = pl.ds(head * HEAD, HEAD)
        at_k = pl.ds(width + head * HEAD, HEAD)
        at_v = pl.ds(2 * width + head * HEAD, HEAD)
        raw = packed_ref[:, at]
        queries = ((raw * cosine + swap_halves(raw) * sine) * scale).astype(BF16)
        raw = packed_ref[:, at_k]
        keys = (raw * cosine + swap_halves(raw) * sine).astype(BF16)
        values = packed_ref[:, at_v].astype(BF16)
        qkv_ref[:, at] = queries
        qkv_ref[:, at_k] = keys
        qkv_ref[:, at_v] = values
        probs = softmax(queries, keys, visible).astype(BF16)
        context_ref[:, at] = dot(probs, values).astype(BF16)


def attend_back_kernel(prefix_ref, qkv_ref, d_context_ref, cos_ref, sin_ref, d_packed_ref):
    width = d_context_ref.shape[1]
    visible = seen(prefix_ref[pl.program_id(0)])
    cosine = cos_ref[0]
    sine = sin_ref[0]
    for head in range(width // HEAD):
        at = pl.ds(head * HEAD, HEAD)
        at_k = pl.ds(width + head * HEAD, HEAD)
        at_v = pl.ds(2 * width + head * HEAD, HEAD)
        queries = qkv_ref[:, at]
        keys = qkv_ref[:, at_k]
        values = qkv_ref[:, at_v]
        d_context = d_context_ref[:, at]
        probs = softmax(queries, keys, visible)
        d_packed_ref[:, at_v] = dot_rows(probs.astype(BF16), d_context).astype(BF16)
        d_probs = dot_cols(d_context, values)
        inner = jnp.sum(probs * d_probs, axis=1, keepdims=True)
        d_scores = (probs * (d_probs - inner)).astype(BF16)
        grad = dot(d_scores, keys) * scale
        d_packed_ref[:, at] = (grad * cosine - swap_halves(grad) * sine).astype(BF16)
        grad = dot_rows(d_scores, queries)
        d_packed_ref[:, at_k] = (grad * cosine - swap_halves(grad) * sine).astype(BF16)


def by_sequence(width):
    return pl.BlockSpec((SEQ_LEN, width), lambda s: (s, 0))


TABLE = pl.BlockSpec((1, SEQ_LEN, HEAD), lambda s: (s, 0, 0))
SCALARS = pl.BlockSpec(memory_space=pltpu.SMEM)
PARAMS = pltpu.CompilerParams(vmem_limit_bytes=48 * 2**20)


def attend(prefix, packed, cosine, sine):
    rows, width = packed.shape[0], packed.shape[1] // 3
    return pl.pallas_call(
        attend_kernel,
        grid=(rows // SEQ_LEN,),
        in_specs=[SCALARS, by_sequence(3 * width), TABLE, TABLE],
        out_specs=[by_sequence(3 * width), by_sequence(width)],
        out_shape=[
            jax.ShapeDtypeStruct((rows, 3 * width), BF16),
            jax.ShapeDtypeStruct((rows, width), BF16),
        ],
        compiler_params=PARAMS,
    )(prefix, packed, cosine, sine)


def attend_back(prefix, qkv, d_context, cosine, sine):
    rows, width = d_context.shape
    return pl.pallas_call(
        attend_back_kernel,
        grid=(rows // SEQ_LEN,),
        in_specs=[SCALARS, by_sequence(3 * width), by_sequence(width), TABLE, TABLE],
        out_specs=by_sequence(3 * width),
        out_shape=jax.ShapeDtypeStruct((rows, 3 * width), BF16),
        compiler_params=PARAMS,
    )(prefix, qkv, d_context, cosine, sine)


def tables(prefix, start):
    place = jnp.arange(SEQ_LEN, dtype=jnp.int32)
    in_span = place[None, :] >= prefix[:, None]
    pos_one = jnp.where(in_span, start[:, None], place[None, :])
    pos_two = jnp.where(in_span, place[None, :] - prefix[:, None] + 1, 0)
    lane = jnp.arange(HEAD)
    freqs = 10000.0 ** (-2.0 * (lane % 32).astype(F32) / 64)
    place_of = jnp.where(lane[None, None, :] < 64, pos_one[:, :, None], pos_two[:, :, None])
    angles = place_of.astype(F32) * freqs
    sign = jnp.where(lane % 64 < 32, -1.0, 1.0)
    return jnp.cos(angles), jnp.sin(angles) * sign


def norm_parts(values):
    center = values - jnp.mean(values, axis=-1, keepdims=True)
    inverse = lax.rsqrt(jnp.mean(center * center, axis=-1, keepdims=True) + norm_eps)
    return center * inverse, inverse


def norm_back(normal, inverse, gain, grad):
    scaled = gain * grad
    return inverse * (
        scaled
        - jnp.mean(scaled, axis=-1, keepdims=True)
        - normal * jnp.mean(scaled * normal, axis=-1, keepdims=True)
    )


def gate_parts(gate):
    phi = 0.5 * (1.0 + lax.erf(gate * 0.7071067811865476))
    slope = phi + gate * jnp.exp(-0.5 * gate * gate) * 0.3989422804014327
    return gate * phi, slope


def here():
    return lax.axis_index("gy"), lax.axis_index("gx"), lax.axis_index("core")


def place(y, x, c):
    return (y * 2 + x) * 2 + c


def greet(peers):
    barrier = pltpu.get_barrier_semaphore()
    for peer in peers:
        pl.semaphore_signal(barrier, inc=1, device_id=peer, device_id_type=MESH)
    pl.semaphore_wait(barrier, len(peers))


def spread_block(cut, base, block_ref, out_ref, send, recv, local):
    rows = block_ref.shape[0]
    y, x, c = here()
    to_x, to_y, to_c = {"gx": 1 - x}, {"gy": 1 - y}, {"core": 1 - c}
    me, by_x, by_y, far = place(y, x, c), place(y, 1 - x, c), place(1 - y, x, c), place(1 - y, 1 - x, c)
    low, high = pl.ds(0, cut), pl.ds(cut, rows - cut)

    def push(k, src, dst, to):
        copy = pltpu.make_async_remote_copy(
            src_ref=src, dst_ref=dst, send_sem=send.at[base + k], recv_sem=recv.at[base + k], device_id=to, device_id_type=MESH
        )
        copy.start()
        return copy

    def landed(k, dst):
        pltpu.make_async_remote_copy(
            src_ref=dst, dst_ref=dst, send_sem=send.at[base + k], recv_sem=recv.at[base + k], device_id=to_c, device_id_type=MESH
        ).wait_recv()

    sent = [
        push(0, block_ref.at[low], out_ref.at[me, low], to_x),
        push(1, block_ref.at[high], out_ref.at[me, high], to_y),
        push(2, block_ref.at[high], out_ref.at[me, high], to_x),
        push(3, block_ref.at[low], out_ref.at[me, low], to_y),
        push(4, block_ref, out_ref.at[me], to_c),
    ]
    keep = pltpu.make_async_copy(block_ref, out_ref.at[me], local)
    keep.start()
    landed(0, out_ref.at[by_x, low])
    sent.append(push(5, out_ref.at[by_x, low], out_ref.at[by_x, low], to_y))
    sent.append(push(7, out_ref.at[by_x, low], out_ref.at[by_x, low], to_c))
    landed(1, out_ref.at[by_y, high])
    sent.append(push(6, out_ref.at[by_y, high], out_ref.at[by_y, high], to_x))
    sent.append(push(8, out_ref.at[by_y, high], out_ref.at[by_y, high], to_c))
    landed(2, out_ref.at[by_x, high])
    sent.append(push(9, out_ref.at[by_x, high], out_ref.at[by_x, high], to_c))
    landed(3, out_ref.at[by_y, low])
    sent.append(push(10, out_ref.at[by_y, low], out_ref.at[by_y, low], to_c))
    landed(5, out_ref.at[far, low])
    sent.append(push(11, out_ref.at[far, low], out_ref.at[far, low], to_c))
    landed(6, out_ref.at[far, high])
    sent.append(push(12, out_ref.at[far, high], out_ref.at[far, high], to_c))
    other, other_x, other_y, other_far = (
        place(y, x, 1 - c),
        place(y, 1 - x, 1 - c),
        place(1 - y, x, 1 - c),
        place(1 - y, 1 - x, 1 - c),
    )
    landed(4, out_ref.at[other])
    landed(7, out_ref.at[other_x, low])
    landed(8, out_ref.at[other_y, high])
    landed(9, out_ref.at[other_x, high])
    landed(10, out_ref.at[other_y, low])
    landed(11, out_ref.at[other_far, low])
    landed(12, out_ref.at[other_far, high])
    keep.wait()
    for copy in sent:
        copy.wait_send()


ANY = pl.BlockSpec(memory_space=pl.ANY)


def swap_peers(zs, kinds):
    y, x, c = here()
    z = lax.axis_index("z")
    found = []
    for k in range(1, 8):
        peer = ((y + k // 4) % 2, (x + k // 2 % 2) % 2, (c + k % 2) % 2)
        found.append((place(*peer), {"gy": peer[0], "gx": peer[1], "core": peer[2]}))
    if "line" in kinds:
        found += [((z + k) % zs, {"z": (z + k) % zs}) for k in range(1, zs)]
    return found


def swap_begin(zs, kinds, blocks, outs, send, recv, local):
    copies, comes, keeps = [], [], []
    found = swap_peers(zs, kinds)
    for i, kind in enumerate(kinds):
        me = lax.axis_index("z") if kind == "line" else place(*here())
        for k, (peer, name) in enumerate(found[7:] if kind == "line" else found[:7]):
            src = blocks[i].at[peer] if kind == "swap" else blocks[i]
            landing = outs[i].at[peer]
            sems = dict(send_sem=send.at[i, k], recv_sem=recv.at[i, k], device_id=name, device_id_type=MESH)
            copies.append(pltpu.make_async_remote_copy(src_ref=src, dst_ref=outs[i].at[me], **sems))
            comes.append(pltpu.make_async_remote_copy(src_ref=landing, dst_ref=landing, **sems))
            copies[-1].start()
        own = blocks[i].at[me] if kind == "swap" else blocks[i]
        keeps.append(pltpu.make_async_copy(own, outs[i].at[me], local.at[i]))
        keeps[-1].start()

    def finish():
        for come in comes:
            come.wait_recv()
        for copy in copies:
            copy.wait_send()
        for keep in keeps:
            keep.wait()

    return finish


SWAP_LEAD = {"swap": lambda zs: (), "group": lambda zs: (8,), "line": lambda zs: (zs,)}


def swap_shapes(zs, arrays, kinds):
    return [jax.ShapeDtypeStruct(SWAP_LEAD[k](zs) + a.shape, a.dtype) for a, k in zip(arrays, kinds)]


def swap_scratch(zs, kinds):
    n, most = len(kinds), max(7, zs - 1)
    return [
        pltpu.SemaphoreType.DMA((n, most)),
        pltpu.SemaphoreType.DMA((n, most)),
        pltpu.SemaphoreType.DMA((n,)),
    ]


SLAB = 16
ROWS = pl.BlockSpec(memory_space=pltpu.VMEM)
CHIP_COLS = 256


def by_rows(value, zs, piece):
    group = D // (zs * piece)
    order = [g * zs + z for z in range(zs) for g in range(group)]
    return jnp.concatenate([value[:, m * piece : (m + 1) * piece] for m in order], axis=1)


def in_order(value, zs, piece):
    group = D // (zs * piece)
    order = [z * group + g for g in range(group) for z in range(zs)]
    return jnp.concatenate([value[:, m * piece : (m + 1) * piece] for m in order], axis=1)


def first_norm(values, gains):
    normal, inverse = norm_parts(values)
    first = normal * gains[0:1] + gains[1:2]
    return first, normal, inverse


def second_norm(total, first, grad, gains):
    normal, inverse = norm_parts(deep_alpha * first + total)
    return normal * gains[2:3] + gains[3:4], norm_back(normal, inverse, gains[2:3], grad), grad * normal


def first_back(total, d_pre_two, normal, inverse, gains):
    d_first = deep_alpha * d_pre_two + total
    return norm_back(normal, inverse, gains[0:1], d_first), d_first * normal, d_first


def fold_kernel(mode, across, zs, piece, n_aux, n_out, kinds, *refs):
    left_ref, right_ref, gains_ref = refs[:3]
    aux_refs = refs[3 : 3 + n_aux]
    refs = refs[3 + n_aux :]
    n_swap = len(kinds)
    swap_in, refs = refs[:n_swap], refs[n_swap:]
    spread = mode != "last"
    if spread:
        all_ref, refs = refs[0], refs[1:]
    outs, refs = refs[:n_out], refs[n_out:]
    swap_out, refs = refs[:n_swap], refs[n_swap:]
    aux, refs = refs[:n_aux], refs[n_aux:]
    left, right, part, got, near_x, near_y, from_x, from_y, block, acc, send, recv, local = refs[:13]
    rows, width = block.shape
    cut = near_x.shape[0]
    y, x, c = here()
    to_x, to_y, to_c = {"gx": 1 - x}, {"gy": 1 - y}, {"core": 1 - c}
    chips = [(1 - y, 1 - x), (y, 1 - x), (1 - y, x), (y, x)]
    low, high = pl.ds(0, cut), pl.ds(cut, rows - cut)

    def push(k, src, dst, to):
        copy = pltpu.make_async_remote_copy(
            src_ref=src, dst_ref=dst, send_sem=send.at[k], recv_sem=recv.at[k], device_id=to, device_id_type=MESH
        )
        copy.start()
        return copy

    def add(k, extra, start, size, offset=0):
        @pl.loop(0, size // SLAB)
        def _(step):
            at = pl.ds(pl.multiple_of(start + step * SLAB, SLAB), SLAB)
            of = pl.ds(pl.multiple_of(start - offset + step * SLAB, SLAB), SLAB)
            part[k, c, at] = (part[k, c, at].astype(F32) + extra[of].astype(F32)).astype(BF16)

    loads = [pltpu.make_async_copy(left_ref.at[a * 2 + b], left.at[k], local.at[k]) for k, (a, b) in enumerate(chips)]
    load_right = pltpu.make_async_copy(right_ref, right, local.at[4])
    load_aux = [pltpu.make_async_copy(r, v, local.at[5 + k]) for k, (r, v) in enumerate(zip(aux_refs, aux))]
    loads[0].start()
    load_right.start()
    for load in loads[1:] + load_aux:
        load.start()
    if n_swap:
        greet([name for _, name in swap_peers(1, kinds)])
        swap_finish = swap_begin(1, kinds, swap_in, swap_out, *refs[13:])
    else:
        greet([to_x, to_y, to_c])

    def product(k):
        loads[k].wait()

        @pl.loop(0, width // CHIP_COLS)
        def _(step):
            at = pl.ds(pl.multiple_of(step * CHIP_COLS, CHIP_COLS), CHIP_COLS)
            here_part = dot_cols(left[k], right[at]) if across else dot(left[k], right[:, at])
            part[k, 0, :, at] = here_part[:rows].astype(BF16)
            part[k, 1, :, at] = here_part[rows:].astype(BF16)

        return push(k, part.at[k, 1 - c], got.at[k], to_c)

    load_right.wait()
    sent = [product(0), product(1)]
    sent[0].wait_recv()
    add(0, got.at[0], 0, rows)
    far_x = push(4, part.at[0, c, low], near_x, to_x)
    far_y = push(5, part.at[0, c, high], near_y, to_y)
    sent.append(product(2))
    sent[1].wait_recv()
    add(1, got.at[1], 0, rows)
    plain_x = push(6, part.at[1, c, low], from_x.at[low], to_x)
    sent[2].wait_recv()
    add(2, got.at[2], 0, rows)
    plain_y = push(7, part.at[2, c, high], from_y.at[high], to_y)
    sent.append(product(3))
    far_y.wait_recv()
    add(1, near_y, cut, rows - cut, cut)
    more_x = push(8, part.at[1, c, high], from_x.at[high], to_x)
    far_x.wait_recv()
    add(2, near_x, 0, cut)
    more_y = push(9, part.at[2, c, low], from_y.at[low], to_y)
    sent[3].wait_recv()
    for load in load_aux:
        load.wait()
    plain_x.wait_recv()
    plain_y.wait_recv()
    more_x.wait_recv()
    more_y.wait_recv()
    gains = gains_ref[...]
    acc[...] = jnp.zeros_like(acc)

    @pl.loop(0, rows // SLAB)
    def _(step):
        at = pl.ds(pl.multiple_of(step * SLAB, SLAB), SLAB)
        total = part[3, c, at].astype(F32) + got[3, at].astype(F32) + from_x[at].astype(F32) + from_y[at].astype(F32)
        held = [a[at].astype(F32) for a in aux]
        if mode == "one":
            first, normal, inverse = first_norm(by_rows(deep_alpha * held[0] + total, zs, piece), gains)
            outs[0][at] = first
            outs[1][at] = normal
            outs[2][at] = jnp.broadcast_to(inverse, (SLAB, 128))
            block[at] = first.astype(BF16)
        elif mode == "back":
            d_pre, terms, d_first = first_back(total, held[0], held[1], held[2][:, 0:1], gains)
            outs[0][at] = d_pre
            block[at] = in_order(d_pre, zs, piece).astype(BF16)
            acc[0] += terms
            acc[1] += d_first
        else:
            outs[0][at] = in_order(deep_alpha * held[0] + total, zs, piece).astype(BF16)

    if mode == "back":
        outs[-1][0:1] = jnp.sum(acc[0], axis=0, keepdims=True)
        outs[-1][1:2] = jnp.sum(acc[1], axis=0, keepdims=True)
    for copy in sent + [far_x, far_y, plain_x, plain_y, more_x, more_y]:
        copy.wait_send()
    if n_swap:
        swap_finish()
    if spread:
        spread_block(cut, 10, block, all_ref, send, recv, local.at[4])


def group_fold(name, zs, mode, left, right, gains, aux, out_types, extras=(), kinds=()):
    across = mode != "one"
    rows, depth = left.shape[0] // 8, left.shape[1]
    width = gains.shape[1]
    cut = rows // 2
    spread = mode != "last"
    out_shape = [jax.ShapeDtypeStruct((8, rows, width), BF16)] * spread + out_types
    n, n_swap = len(aux), len(extras)
    n_sems = 23 if spread else 10
    return pl.pallas_call(
        functools.partial(fold_kernel, mode, across, zs, width // (8 * zs), n, len(out_types), kinds),
        out_shape=out_shape + swap_shapes(1, extras, kinds),
        in_specs=[ANY, ANY, ROWS] + [ANY] * (n + n_swap),
        out_specs=[ANY] * spread + [ROWS] * len(out_types) + [ANY] * n_swap,
        scratch_shapes=[pltpu.VMEM(a.shape, a.dtype) for a in aux]
        + [
            pltpu.VMEM((4, 2 * rows, depth), BF16),
            pltpu.VMEM(right.shape, BF16),
            pltpu.VMEM((4, 2, rows, width), BF16),
            pltpu.VMEM((4, rows, width), BF16),
            pltpu.VMEM((cut, width), BF16),
            pltpu.VMEM((rows - cut, width), BF16),
            pltpu.VMEM((rows, width), BF16),
            pltpu.VMEM((rows, width), BF16),
            pltpu.VMEM((rows, width), BF16),
            pltpu.VMEM((2, SLAB, width), F32),
            pltpu.SemaphoreType.DMA((n_sems,)),
            pltpu.SemaphoreType.DMA((n_sems,)),
            pltpu.SemaphoreType.DMA((5 + n,)),
        ]
        + (swap_scratch(1, kinds) if n_swap else []),
        compiler_params=pltpu.CompilerParams(
            collective_id=name, has_side_effects=True, vmem_limit_bytes=50 * 2**20
        ),
        cost_estimate=pl.CostEstimate(flops=0, bytes_accessed=(200 if spread else 110) * 2**20, transcendentals=0),
    )(left.reshape(4, 2 * rows, depth), right, gains, *aux, *extras)


def turn_kernel(
    zs, piece, x_ref, in_ref, out_ref, gains_ref, first_ref, grad_ref,
    all_ref, kept_ref, right_ref, result_ref, d_pre_ref, sums_ref, dw_ref,
    first, grad, w_in, kept, left, right, part, got, near_x, near_y, from_x, from_y, whole, dw, acc,
    fold_send, fold_recv, all_send, all_recv, line_send, line_recv, local, x_local
):
    rows = first.shape[0]
    tile = left.shape[2]
    wide = right.shape[2]
    y, x, c = here()
    z = lax.axis_index("z")
    to_x, to_y, to_c = {"gx": 1 - x}, {"gy": 1 - y}, {"core": 1 - c}
    chips = [(1 - y) * 2 + 1 - x, y * 2 + 1 - x, (1 - y) * 2 + x, y * 2 + x]
    me, by_x, by_y, far = place(y, x, c), place(y, 1 - x, c), place(1 - y, x, c), place(1 - y, 1 - x, c)
    other, other_x, other_y, other_far = (
        place(y, x, 1 - c),
        place(y, 1 - x, 1 - c),
        place(1 - y, x, 1 - c),
        place(1 - y, 1 - x, 1 - c),
    )
    half = rows // 2
    most = -(-half // (2 * SLAB)) * SLAB
    lows = [(0, most), (half, half - most)]
    highs = [(most, half - most), (2 * half - most, most)]
    top, bottom = pl.ds(0, half), pl.ds(half, half)
    sent = []

    def remote(sems, k, src, dst, to):
        return pltpu.make_async_remote_copy(
            src_ref=src,
            dst_ref=dst,
            send_sem=sems[0].at[k],
            recv_sem=sems[1].at[k],
            device_id=to,
            device_id_type=MESH,
        )

    def push(sems, k, src, dst, to):
        copy = remote(sems, k, src, dst, to)
        copy.start()
        sent.append(copy)

    def landed(sems, k, dst):
        remote(sems, k, dst, dst, to_c).wait_recv()

    folds, alls, lines = (fold_send, fold_recv), (all_send, all_recv), (line_send, line_recv)

    load_out = pltpu.make_async_copy(out_ref, right.at[z], local.at[0])
    load_in = pltpu.make_async_copy(in_ref, w_in, local.at[1])
    load_first = pltpu.make_async_copy(first_ref, first, local.at[2])
    load_grad = pltpu.make_async_copy(grad_ref, grad, local.at[3])

    def load_x(g):
        return pltpu.make_async_copy(x_ref.at[g], whole.at[g], x_local.at[g])

    load_out.start()
    load_in.start()
    for g in range(8):
        load_x(g).start()
    load_first.start()
    load_grad.start()

    barrier = pltpu.get_barrier_semaphore()
    for to in (to_x, to_y, to_c):
        pl.semaphore_signal(barrier, inc=1, device_id=to, device_id_type=MESH)

    @pl.when(z > 0)
    def _():
        pl.semaphore_signal(barrier, inc=1, device_id={"z": z - 1}, device_id_type=MESH)

    @pl.when(z < zs - 1)
    def _():
        pl.semaphore_signal(barrier, inc=1, device_id={"z": z + 1}, device_id_type=MESH)

    inside = (z > 0) & (z < zs - 1)

    @pl.when(inside)
    def _():
        pl.semaphore_wait(barrier, 5)

    @pl.when(jnp.logical_not(inside))
    def _():
        pl.semaphore_wait(barrier, 4)

    def shard_of(step, up):
        return z - step if up else z + step

    def hop(step, up):
        ref = right.at[shard_of(step, up)]
        return remote(lines, 2 * step + (0 if up else 1), ref, ref, {"z": z + 1 if up else z - 1})

    def sends(step, up):
        return (z >= step) & (z < zs - 1) if up else (z <= zs - 1 - step) & (z > 0)

    def gets(step, up):
        return z >= step + 1 if up else z <= zs - 2 - step

    def line_serve(step):
        for up in (True, False):

            @pl.when(gets(step - 1, up) & sends(step, up))
            def _(up=up):
                landed(lines, 2 * (step - 1) + (0 if up else 1), right.at[shard_of(step, up)])
                hop(step, up).start()

    def line_take(step):
        for up in (True, False):

            @pl.when(gets(step - 1, up) & jnp.logical_not(sends(step, up)))
            def _(up=up):
                landed(lines, 2 * (step - 1) + (0 if up else 1), right.at[shard_of(step, up)])

    load_out.wait()
    for up in (True, False):

        @pl.when(sends(0, up))
        def _(up=up):
            hop(0, up).start()


    load_in.wait()

    @pl.loop(0, 8)
    def _(g):
        @pl.when(g == 6)
        def _():
            line_serve(1)

        load_x(g).wait()
        projected = dot(whole[g], w_in[...])
        gate, up = projected[:, :tile], projected[:, tile:]
        act, slope = gate_parts(gate)
        left[g] = (act * up).astype(BF16)
        kept[g] = jnp.concatenate([up * slope, act], axis=1).astype(BF16)

    keep = pltpu.make_async_copy(kept, kept_ref, local.at[4])
    keep.start()

    def add(k, extra, start, offset, at):
        @pl.loop(0, half // SLAB)
        def _(step):
            row = pl.ds(pl.multiple_of(start + step * SLAB, SLAB), SLAB)
            of = pl.ds(pl.multiple_of(start - offset + step * SLAB, SLAB), SLAB)
            part[k, c, row, at] = (part[k, c, row, at].astype(F32) + extra[of, at].astype(F32)).astype(BF16)

    def chip_sum(k, at):
        add(k, got.at[k], 0, 0, at)
        add(k, got.at[k], half, 0, at)

    def product(k, block, at):
        found = dot(left[pl.ds(2 * chips[k], 2)].reshape(2 * rows, tile), right[block])
        part[k, 0, :, at] = found[:rows].astype(BF16)
        part[k, 1, :, at] = found[rows:].astype(BF16)

    def block_at(i):
        if i == 0:
            return z
        below = z < zs // 2
        near = jnp.where(below, z, zs - 1 - z)
        spot = jnp.where(i <= 2 * near, jnp.where(i % 2 == 1, near - (i + 1) // 2, near + i // 2), i)
        return jnp.where(below, spot, zs - 1 - spot)

    def block_cols(i):
        return pl.ds(pl.multiple_of(block_at(i) * wide, wide), wide)

    def fold_start(i):
        b, block, at = 8 * i, block_at(i), block_cols(i)
        rest = pl.ds(1, 3)
        product(0, block, at)
        push(folds, b, part.at[0, 1 - c, :, at], got.at[0, :, at], to_c)
        for k in (1, 2, 3):
            product(k, block, at)
        push(folds, b + 1, part.at[rest, 1 - c, :, at], got.at[rest, :, at], to_c)
        landed(folds, b, got.at[0, :, at])
        chip_sum(0, at)
        push(folds, b + 2, part.at[0, c, top, at], near_x.at[:, at], to_x)
        push(folds, b + 3, part.at[0, c, bottom, at], near_y.at[:, at], to_y)
        landed(folds, b + 1, got.at[rest, :, at])
        chip_sum(1, at)
        push(folds, b + 4, part.at[1, c, top, at], from_x.at[top, at], to_x)
        chip_sum(2, at)
        push(folds, b + 5, part.at[2, c, bottom, at], from_y.at[bottom, at], to_y)

    def fold_end(i):
        b, at = 8 * i, block_cols(i)
        landed(folds, b + 3, near_y.at[:, at])
        add(1, near_y, half, half, at)
        push(folds, b + 6, part.at[1, c, bottom, at], from_x.at[bottom, at], to_x)
        landed(folds, b + 2, near_x.at[:, at])
        add(2, near_x, 0, 0, at)
        push(folds, b + 7, part.at[2, c, top, at], from_y.at[top, at], to_y)

    gains = gains_ref[...]
    line_take(1)
    fold_start(0)
    fold_start(1)
    fold_end(0)
    for i in range(2, zs):
        if i < zs - 1:
            line_serve(i)
        fold_end(i - 1)
        line_take(i)
        fold_start(i)
    fold_end(zs - 1)
    carry = pltpu.make_async_copy(right, right_ref, local.at[5])
    carry.start()
    load_first.wait()
    load_grad.wait()
    acc[...] = jnp.zeros_like(acc)
    for i in range(zs):
        at = block_cols(i)
        landed(folds, 8 * i + 4, from_x.at[top, at])
        landed(folds, 8 * i + 5, from_y.at[bottom, at])
        landed(folds, 8 * i + 6, from_x.at[bottom, at])
        landed(folds, 8 * i + 7, from_y.at[top, at])

    def low(i):
        return pl.ds(*lows[i])

    def high(i):
        return pl.ds(*highs[i])

    def span(i):
        return pl.ds(i * half, half)

    def norm(i):
        @pl.loop(0, half // SLAB)
        def _(step):
            at = pl.ds(pl.multiple_of(i * half + step * SLAB, SLAB), SLAB)
            total = part[3, c, at].astype(F32) + got[3, at].astype(F32)
            total += from_x[at].astype(F32) + from_y[at].astype(F32)
            dy = grad[at].astype(F32)
            result, d_pre, terms = second_norm(total, first[at], dy, gains)
            result_ref[at] = result.astype(BF16)
            d_pre_ref[at] = d_pre
            whole[me, at] = d_pre.astype(BF16)
            acc[0] += terms
            acc[1] += dy

        b = 13 * i
        push(alls, b, whole.at[me, low(i)], whole.at[me, low(i)], to_x)
        push(alls, b + 1, whole.at[me, high(i)], whole.at[me, high(i)], to_y)
        push(alls, b + 2, whole.at[me, high(i)], whole.at[me, high(i)], to_x)
        push(alls, b + 3, whole.at[me, low(i)], whole.at[me, low(i)], to_y)
        push(alls, b + 4, whole.at[me, span(i)], whole.at[me, span(i)], to_c)

    def pass_on(i, k, slot, at, onward):
        ref = whole.at[slot, at]
        landed(alls, 13 * i + k, ref)
        for where, to in onward:
            push(alls, 13 * i + where, ref, ref, to)

    def spread_first(i):
        pass_on(i, 0, by_x, low(i), [(5, to_y), (7, to_c)])
        pass_on(i, 1, by_y, high(i), [(6, to_x), (8, to_c)])

    def spread_rest(i):
        pass_on(i, 2, by_x, high(i), [(9, to_c)])
        pass_on(i, 3, by_y, low(i), [(10, to_c)])

    def spread_far(i):
        pass_on(i, 5, far, low(i), [(11, to_c)])
        pass_on(i, 6, far, high(i), [(12, to_c)])

    outward = []

    def gradient(k, last=False, first_one=False):
        pair = pl.ds(2 * chips[k], 2)
        outward.append(pltpu.make_async_copy(whole.at[pair], all_ref.at[pair], local.at[6 + k]))
        outward[-1].start()

        @pl.loop(0, zs)
        def _(block):
            at = pl.ds(pl.multiple_of(block * wide, wide), wide)
            found = dot_rows(left[pair].reshape(2 * rows, tile), whole[pair, :, at].reshape(2 * rows, wide))
            if first_one:
                dw[block] = found
            elif last:
                dw_ref[block] = (dw[block] + found).astype(BF16)
            else:
                dw[block] += found

    norm(0)
    norm(1)
    spread_first(0)
    for i in (0, 1):
        landed(alls, 13 * i + 4, whole.at[other, span(i)])
    gradient(3, first_one=True)
    spread_rest(0)
    spread_first(1)
    spread_rest(1)
    for i in (0, 1):
        landed(alls, 13 * i + 7, whole.at[other_x, low(i)])
        landed(alls, 13 * i + 9, whole.at[other_x, high(i)])
    gradient(1)
    spread_far(0)
    for i in (0, 1):
        landed(alls, 13 * i + 8, whole.at[other_y, high(i)])
        landed(alls, 13 * i + 10, whole.at[other_y, low(i)])
    gradient(2)
    sums_ref[0:1] = jnp.sum(acc[0], axis=0, keepdims=True)
    sums_ref[1:2] = jnp.sum(acc[1], axis=0, keepdims=True)
    spread_far(1)
    for i in (0, 1):
        landed(alls, 13 * i + 11, whole.at[other_far, low(i)])
        landed(alls, 13 * i + 12, whole.at[other_far, high(i)])
    gradient(0, last=True)
    for copy in outward + [keep, carry]:
        copy.wait()
    for copy in sent:
        copy.wait_send()
    for step in range(zs - 1):
        for up in (True, False):

            @pl.when(sends(step, up))
            def _(step=step, up=up):
                hop(step, up).wait_send()


def turn(zs, x, w_in, w_out, gains, first, grad):
    rows = x.shape[0] // 8
    units, wide = w_out.shape
    width = gains.shape[1]
    half = rows // 2
    by_z = (zs, units, wide)
    return pl.pallas_call(
        functools.partial(turn_kernel, zs, width // (8 * zs)),
        out_shape=[
            jax.ShapeDtypeStruct((8, rows, width), BF16),
            jax.ShapeDtypeStruct((8, rows, 2 * units), BF16),
            jax.ShapeDtypeStruct(by_z, BF16),
            jax.ShapeDtypeStruct((rows, width), BF16),
            jax.ShapeDtypeStruct((rows, width), F32),
            jax.ShapeDtypeStruct((8, width), F32),
            jax.ShapeDtypeStruct(by_z, BF16),
        ],
        in_specs=[ANY, ANY, ANY, ROWS, ANY, ANY],
        out_specs=[ANY] * 3 + [ROWS] * 4,
        scratch_shapes=[
            pltpu.VMEM((rows, width), F32),
            pltpu.VMEM((rows, width), BF16),
            pltpu.VMEM(w_in.shape, BF16),
            pltpu.VMEM((8, rows, 2 * units), BF16),
            pltpu.VMEM((8, rows, units), BF16),
            pltpu.VMEM(by_z, BF16),
            pltpu.VMEM((4, 2, rows, width), BF16),
            pltpu.VMEM((4, rows, width), BF16),
            pltpu.VMEM((half, width), BF16),
            pltpu.VMEM((half, width), BF16),
            pltpu.VMEM((rows, width), BF16),
            pltpu.VMEM((rows, width), BF16),
            pltpu.VMEM((8, rows, width), BF16),
            pltpu.VMEM(by_z, F32),
            pltpu.VMEM((2, SLAB, width), F32),
            pltpu.SemaphoreType.DMA((8 * zs,)),
            pltpu.SemaphoreType.DMA((8 * zs,)),
            pltpu.SemaphoreType.DMA((26,)),
            pltpu.SemaphoreType.DMA((26,)),
            pltpu.SemaphoreType.DMA((2 * (zs - 1),)),
            pltpu.SemaphoreType.DMA((2 * (zs - 1),)),
            pltpu.SemaphoreType.DMA((10,)),
            pltpu.SemaphoreType.DMA((8,)),
        ],
        compiler_params=pltpu.CompilerParams(collective_id=1, has_side_effects=True, vmem_limit_bytes=60 * 2**20),
        cost_estimate=pl.CostEstimate(flops=0, bytes_accessed=380 * 2**20, transcendentals=0),
    )(x.reshape(8, rows, width), w_in, w_out, gains, first, grad)


def swap_kernel(zs, kinds, *refs):
    n = len(kinds)
    greet([name for _, name in swap_peers(zs, kinds)])
    swap_begin(zs, kinds, refs[:n], refs[n : 2 * n], *refs[2 * n :])()


def group_swap(name, zs, arrays, kinds):
    n = len(arrays)
    return pl.pallas_call(
        functools.partial(swap_kernel, zs, kinds),
        out_shape=swap_shapes(zs, arrays, kinds),
        in_specs=[ANY] * n,
        out_specs=[ANY] * n,
        scratch_shapes=swap_scratch(zs, kinds),
        compiler_params=pltpu.CompilerParams(collective_id=name, has_side_effects=True),
        cost_estimate=pl.CostEstimate(flops=0, bytes_accessed=50 * 2**20, transcendentals=0),
    )(*arrays)


def enter_kernel(zs, kinds, x_ref, *refs):
    n = len(kinds)
    blocks, x_all, outs, sems = refs[:n], refs[n], refs[n + 1 : 2 * n + 1], refs[2 * n + 1 :]
    greet([name for _, name in swap_peers(zs, kinds)])
    finish = swap_begin(zs, kinds, blocks, outs, *sems[:3])
    spread_block(x_ref.shape[0] // 2, 0, x_ref, x_all, *sems[3:])
    finish()


def enter(zs, x, arrays, kinds):
    n = len(arrays)
    return pl.pallas_call(
        functools.partial(enter_kernel, zs, kinds),
        out_shape=[jax.ShapeDtypeStruct((8,) + x.shape, x.dtype)] + swap_shapes(zs, arrays, kinds),
        in_specs=[ANY] * (n + 1),
        out_specs=[ANY] * (n + 1),
        scratch_shapes=swap_scratch(zs, kinds)
        + [pltpu.SemaphoreType.DMA((13,)), pltpu.SemaphoreType.DMA((13,)), pltpu.SemaphoreType.DMA],
        compiler_params=pltpu.CompilerParams(collective_id=3, has_side_effects=True),
        cost_estimate=pl.CostEstimate(flops=0, bytes_accessed=150 * 2**20, transcendentals=0),
    )(x, *arrays)


def ff_kernel(x_ref, w_ref, hidden_ref, kept_ref):
    tile = hidden_ref.shape[1]
    projected = dot(x_ref[...], w_ref[...])
    gate, up = projected[:, :tile], projected[:, tile:]
    act, slope = gate_parts(gate)
    hidden_ref[...] = (act * up).astype(BF16)
    kept_ref[...] = jnp.concatenate([up * slope, act], axis=1).astype(BF16)


def ff_back_kernel(grad_ref, w_ref, kept_ref, out_ref):
    zs, _, wide = w_ref.shape
    d_hidden = dot_cols(grad_ref[:, :wide], w_ref[0])
    for z in range(1, zs):
        d_hidden += dot_cols(grad_ref[:, z * wide : (z + 1) * wide], w_ref[z])
    out_ref[...] = (jnp.concatenate([d_hidden, d_hidden], axis=1) * kept_ref[...].astype(F32)).astype(BF16)


FF_ROWS = 256


def ff_rows(width):
    return pl.BlockSpec((FF_ROWS, width), lambda i: (i, 0))


def ff_forward(x, w):
    rows, depth = x.shape
    wide = w.shape[1]
    return pl.pallas_call(
        ff_kernel,
        grid=(rows // FF_ROWS,),
        in_specs=[ff_rows(depth), pl.BlockSpec((depth, wide), lambda i: (0, 0))],
        out_specs=[ff_rows(wide // 2), ff_rows(wide)],
        out_shape=[jax.ShapeDtypeStruct((rows, wide // 2), BF16), jax.ShapeDtypeStruct((rows, wide), BF16)],
        compiler_params=PARAMS,
        cost_estimate=pl.CostEstimate(flops=2 * rows * depth * wide, bytes_accessed=20 * 2**20, transcendentals=0),
    )(x, w)


def ff_backward(grad, w, kept):
    rows, depth = grad.shape
    wide = kept.shape[1]
    return pl.pallas_call(
        ff_back_kernel,
        grid=(rows // FF_ROWS,),
        in_specs=[ff_rows(depth), pl.BlockSpec(w.shape, lambda i: (0, 0, 0)), ff_rows(wide)],
        out_specs=ff_rows(wide),
        out_shape=jax.ShapeDtypeStruct((rows, wide), BF16),
        compiler_params=PARAMS,
        cost_estimate=pl.CostEstimate(flops=rows * depth * wide, bytes_accessed=20 * 2**20, transcendentals=0),
    )(grad, w, kept)


def cut_kernel(in_ref, out_ref, in_blocks, out_blocks, wide):
    group, _, double = in_blocks.shape
    tile, ff = double // 2, out_ref.shape[1]
    span = group * tile
    odd = ff % 128
    live = lax.broadcasted_iota(jnp.int32, (in_ref.shape[0], span), 1) < ff
    wide[...] = jnp.zeros_like(wide)
    wide[:, : 2 * ff] = in_ref[...].astype(F32)
    gate = jnp.where(live, wide[:, :span], 0.0)
    up = pltpu.roll(wide[:, ff - odd : ff - odd + span], span - odd, 1)
    up = jnp.where(live, up, 0.0)
    wide[:, :span] = jnp.zeros_like(live, F32)
    wide[:, :ff] = out_ref[...].astype(F32)
    down = wide[:, :span]
    for g in range(group):
        at = slice(g * tile, (g + 1) * tile)
        in_blocks[g] = jnp.concatenate([gate[:, at], up[:, at]], axis=1).astype(BF16)
        out_blocks[g] = down[:, at].astype(BF16)


def cut_ff(w_in, w_out, group, tile):
    rows, ff = w_out.shape
    return pl.pallas_call(
        cut_kernel,
        grid=(rows // 16,),
        in_specs=[pl.BlockSpec((16, 2 * ff), lambda i: (i, 0)), pl.BlockSpec((16, ff), lambda i: (i, 0))],
        out_specs=[
            pl.BlockSpec((group, 16, 2 * tile), lambda i: (0, i, 0)),
            pl.BlockSpec((group, 16, tile), lambda i: (0, i, 0)),
        ],
        out_shape=[
            jax.ShapeDtypeStruct((group, rows, 2 * tile), BF16),
            jax.ShapeDtypeStruct((group, rows, tile), BF16),
        ],
        scratch_shapes=[pltpu.VMEM((16, -(-(ff + group * tile) // 128) * 128), F32)],
        compiler_params=PARAMS,
    )(w_in, w_out)


def join_kernel(in_blocks, out_blocks, in_ref, out_ref):
    group, _, double = in_blocks.shape
    tile, ff = double // 2, out_ref.shape[1]
    odd = ff % 128
    blocks = [in_blocks[g].astype(F32) for g in range(group)]
    gate = jnp.concatenate([block[:, :tile] for block in blocks], axis=1)
    up = jnp.concatenate([block[:, tile:] for block in blocks], axis=1)
    up = pltpu.roll(up, odd, 1)
    lane = lax.broadcasted_iota(jnp.int32, (up.shape[0], 128), 1)
    in_ref[:, : ff - odd] = gate[:, : ff - odd]
    in_ref[:, ff - odd : ff - odd + 128] = jnp.where(lane < odd, gate[:, ff - odd : ff - odd + 128], up[:, :128])
    in_ref[:, ff - odd + 128 :] = up[:, 128 : ff + odd]
    down = jnp.concatenate([out_blocks[g].astype(F32) for g in range(group)], axis=1)
    out_ref[...] = down[:, :ff]


def join_ff(in_blocks, out_blocks, ff):
    group, rows, tile = out_blocks.shape
    return pl.pallas_call(
        join_kernel,
        grid=(rows // 16,),
        in_specs=[
            pl.BlockSpec((group, 16, 2 * tile), lambda i: (0, i, 0)),
            pl.BlockSpec((group, 16, tile), lambda i: (0, i, 0)),
        ],
        out_specs=[pl.BlockSpec((16, 2 * ff), lambda i: (i, 0)), pl.BlockSpec((16, ff), lambda i: (i, 0))],
        out_shape=[jax.ShapeDtypeStruct((rows, 2 * ff), F32), jax.ShapeDtypeStruct((rows, ff), F32)],
        compiler_params=PARAMS,
    )(in_blocks, out_blocks)


def closing_kernel(zs, sum_ref, rows_ref, qkv_ref, dense_ref, total_ref, got, mine, lines, *refs):
    send, recv, local, line_send, line_recv = refs
    y, x, c = here()
    z = lax.axis_index("z")
    me = place(y, x, c)
    wide = got.shape[2]
    width = wide // 3
    piece = got.shape[1]
    found = swap_peers(zs, ("line",))
    greet([name for _, name in found])
    copies, comes = [], []
    for k, (peer, name) in enumerate(found[:7]):
        sems = dict(send_sem=send.at[k], recv_sem=recv.at[k], device_id=name, device_id_type=MESH)
        src = rows_ref.at[peer, :, pl.ds(0, wide)]
        copies.append(pltpu.make_async_remote_copy(src_ref=src, dst_ref=got.at[me], **sems))
        comes.append(pltpu.make_async_remote_copy(src_ref=got.at[peer], dst_ref=got.at[peer], **sems))
    for k, (peer, name) in enumerate(found[7:]):
        sems = dict(send_sem=line_send.at[k], recv_sem=line_recv.at[k], device_id=name, device_id_type=MESH)
        copies.append(pltpu.make_async_remote_copy(src_ref=sum_ref, dst_ref=lines.at[z], **sems))
        comes.append(pltpu.make_async_remote_copy(src_ref=lines.at[peer], dst_ref=lines.at[peer], **sems))
    for copy in copies:
        copy.start()
    keeps = [
        pltpu.make_async_copy(rows_ref.at[me, :, pl.ds(0, wide)], got.at[me], local.at[0]),
        pltpu.make_async_copy(sum_ref, lines.at[z], local.at[1]),
        pltpu.make_async_copy(rows_ref.at[:, :, pl.ds(wide, width)], mine, local.at[2]),
    ]
    for keep in keeps:
        keep.start()
    keeps[2].wait()
    for at in range(0, piece, 16):
        rows = jnp.concatenate([mine[g, at : at + 16] for g in range(8)], axis=1).astype(F32)
        dense_ref[at : at + 16] = rows
    for come in comes:
        come.wait_recv()
    for keep in keeps[:2]:
        keep.wait()
    for g in range(8):
        for j in range(3):
            at = pl.ds(j * D + g * width, width)
            qkv_ref[:, at] = got[g, :, j * width : (j + 1) * width].astype(F32)
    total = lines[0]
    for k in range(1, zs):
        total += lines[k]
    part = total[:, :piece]
    for k in range(1, zs):
        part = jnp.where(z == k, total[:, k * piece : (k + 1) * piece], part)
    total_ref[...] = part
    for copy in copies:
        copy.wait_send()


def closing(zs, sums, rows):
    _, piece, columns = rows.shape
    width = columns // 4
    return pl.pallas_call(
        functools.partial(closing_kernel, zs),
        out_shape=[
            jax.ShapeDtypeStruct((piece, 3 * D), F32),
            jax.ShapeDtypeStruct((piece, D), F32),
            jax.ShapeDtypeStruct((8, piece), F32),
        ],
        in_specs=[ROWS, ANY],
        out_specs=[ROWS] * 3,
        scratch_shapes=[
            pltpu.VMEM((8, piece, 3 * width), BF16),
            pltpu.VMEM((8, piece, width), BF16),
            pltpu.VMEM((zs, 8, width), F32),
            pltpu.SemaphoreType.DMA((7,)),
            pltpu.SemaphoreType.DMA((7,)),
            pltpu.SemaphoreType.DMA((3,)),
            pltpu.SemaphoreType.DMA((zs - 1,)),
            pltpu.SemaphoreType.DMA((zs - 1,)),
        ],
        compiler_params=pltpu.CompilerParams(collective_id=5, has_side_effects=True, vmem_limit_bytes=24 * 2**20),
        cost_estimate=pl.CostEstimate(flops=0, bytes_accessed=50 * 2**20, transcendentals=0),
    )(sums, rows)


def on_device(sizes, x_in, d_out, w_qkv, w_dense, w_in, w_out, gone, bone, gtwo, btwo, flags, span_start, span_len):
    gy, gx, cores, zs = sizes
    piece = w_qkv.shape[0]
    ff = w_out.shape[1]
    group = gy * gx * cores
    width = D // group
    tile = -(-ff // (group * 64)) * 64
    own = gy == 2

    def permute(array):
        lead = array.shape[:-1]
        return jnp.swapaxes(array.reshape(lead + (group, zs, piece)), -3, -2).reshape(lead + (D,))

    def restore(array):
        lead = array.shape[:-1]
        return jnp.swapaxes(array.reshape(lead + (zs, group, piece)), -3, -2).reshape(lead + (D,))

    def swap(name, arrays, kinds):
        if own:
            return group_swap(name, zs, arrays, kinds)
        ways = {
            "swap": lambda a: lax.all_to_all(a, GROUP, 0, 0, tiled=True),
            "group": lambda a: lax.all_gather(a, GROUP, axis=0),
            "line": lambda a: lax.all_gather(a, "z", axis=0),
        }
        return [ways[k](a) for a, k in zip(arrays, kinds)]

    def spread_rows(block):
        return lax.all_gather(block, GROUP, axis=0, tiled=True)

    rows_f32 = jax.ShapeDtypeStruct((SEQ_LEN, D), F32)
    rows_low = jax.ShapeDtypeStruct((SEQ_LEN, D), BF16)
    sums_type = jax.ShapeDtypeStruct((8, D), F32)

    def fold(partial):
        return lax.psum_scatter(partial.astype(BF16), GROUP, scatter_dimension=0, tiled=True).astype(F32)

    def stack_sums(*arrays):
        return jnp.pad(jnp.stack([jnp.sum(a, axis=0) for a in arrays]), ((0, 6), (0, 0)))

    def fold_one(left, right, x, gains):
        if own:
            kinds = [rows_f32, rows_f32, jax.ShapeDtypeStruct((SEQ_LEN, 128), F32)]
            whole, first, normal, inverse = group_fold(0, zs, "one", left, right, gains, [x], kinds)
            return whole.reshape(left.shape[0], D), first, normal, inverse
        first, normal, inverse = first_norm(permute(deep_alpha * x.astype(F32) + fold(dot(left, right))), gains)
        return spread_rows(first.astype(BF16)), first, normal, inverse

    def ff_turn(x, w_in, w_out, first, grad, gains):
        if own:
            whole, kept, w_out, result, d_pre, sums, d_out = turn(zs, x, w_in, w_out, gains, first, grad)
            rows = x.shape[0]
            return whole.reshape(rows, D), kept.reshape(rows, -1), w_out, result, d_pre, sums, d_out
        w_out = lax.all_gather(w_out, "z", axis=0)
        hidden, kept = ff_forward(x, w_in)
        grad = grad.astype(F32)
        right = jnp.swapaxes(w_out, 0, 1).reshape(-1, D)
        result, d_pre, terms = second_norm(fold(dot(hidden, right)), first, grad, gains)
        whole = spread_rows(d_pre.astype(BF16))
        d_out = jnp.swapaxes(dot_rows(hidden, whole).reshape(-1, zs, D // zs), 0, 1).astype(BF16)
        return whole, kept, w_out, result.astype(BF16), d_pre, stack_sums(terms, grad), d_out

    def fold_back(left, right, d_pre_two, normal, inverse, gains):
        if own:
            kinds = [rows_f32, sums_type]
            whole, d_pre, sums = group_fold(7, zs, "back", left, right, gains, [d_pre_two, normal, inverse], kinds)
            return whole.reshape(left.shape[0], D), d_pre, sums
        d_pre, terms, d_first = first_back(fold(dot_cols(left, right)), d_pre_two, normal, inverse, gains)
        return spread_rows(restore(d_pre).astype(BF16)), d_pre, stack_sums(terms, d_first)

    def fold_last(left, right, d_pre, gains, extras, kinds):
        if own:
            return group_fold(8, zs, "last", left, right, gains, [d_pre], [rows_low], extras, kinds)
        out = restore((deep_alpha * d_pre + fold(dot_cols(left, right))).astype(BF16))
        return [out] + swap(8, extras, kinds)

    def gather(block):
        return lax.all_gather(block, "z", axis=0, tiled=True)

    def scatter(partial):
        return lax.psum_scatter(partial.astype(BF16), "z", scatter_dimension=0, tiled=True)

    masked = jnp.max(flags) > 0
    prefix = jnp.where(masked, SEQ_LEN, SEQ_LEN - span_len[0])
    info = jnp.concatenate([gone, bone, gtwo, btwo, jnp.stack([prefix, span_start[0]]).astype(BF16)])
    info = jnp.pad(info[None, :], ((0, 15), (0, -info.shape[0] % 128)))

    qkv_blocks = jnp.moveaxis(w_qkv.reshape(piece, 3, group, width), 2, 0).reshape(group, piece, 3 * width)
    w_dense_part = gather(w_dense)
    qkv_blocks, info = swap(2, [qkv_blocks, info], ("swap", "group"))
    w_qkv_part = gather(qkv_blocks.reshape(group * piece, 3 * width))
    info = info[:, 0]
    place_info = info[:, 4 * piece : 4 * piece + 2].astype(jnp.int32)
    prefix, start = place_info[:, 0], place_info[:, 1]
    cosine, sine = tables(prefix, start)
    in_blocks, out_blocks = cut_ff(w_in, w_out, group, tile)
    info = jnp.pad(info, ((0, -group % 16), (0, 0)))
    x_perm = permute(x_in)
    grad_two = permute(d_out)
    in_blocks, out_blocks, x_perm, qkv_blocks, w_dense_part, cosine, sine, grad_two = lax.optimization_barrier(
        (in_blocks, out_blocks, x_perm, qkv_blocks, w_dense_part, cosine, sine, grad_two)
    )
    swapped, kinds = [in_blocks, out_blocks, info], ("swap", "swap", "line")
    if own:
        x_all, in_blocks, out_blocks, info = enter(zs, x_perm, swapped, kinds)
        x_all = x_all.reshape(group * SEQ_LEN, D)
    else:
        x_all = spread_rows(x_perm)
        in_blocks, out_blocks, info = swap(3, swapped, kinds)
    w_in_part = gather(in_blocks.reshape(group * piece, 2 * tile))
    out_rows = out_blocks.reshape(group * piece, tile).T
    gains = info[:, :group, : 4 * piece].astype(F32).reshape(zs, group, 4, piece)
    gains = jnp.pad(jnp.transpose(gains, (2, 0, 1, 3)).reshape(4, D), ((0, 4), (0, 0)))
    w_qkv_part, x_all, gains, out_rows = lax.optimization_barrier((w_qkv_part, x_all, gains, out_rows))
    packed = dot(x_all, w_qkv_part)
    qkv, context = attend(prefix, packed, cosine, sine)
    first_all, first, normal_one, inverse_one = fold_one(context, w_dense_part, x_in, gains)
    d_branch, kept, w_out_part, layer_out, d_pre_two, sums_two, d_w_out = ff_turn(
        first_all, w_in_part, out_rows, first, grad_two, gains
    )
    layer_out = restore(layer_out)
    d_w_out = lax.psum_scatter(d_w_out, "z", scatter_dimension=0)
    d_projected = ff_backward(d_branch, w_out_part, kept)
    d_w_in = dot_rows(first_all, d_projected).astype(BF16)
    d_w_in, d_projected = lax.optimization_barrier((d_w_in, d_projected))
    d_w_in = scatter(d_w_in)
    d_attn, d_pre_one, sums_one = fold_back(d_projected, w_in_part, d_pre_two, normal_one, inverse_one, gains)
    d_attn, d_w_out = lax.optimization_barrier((d_attn, d_w_out))
    d_context = dot_cols(d_attn, w_dense_part).astype(BF16)
    d_packed = attend_back(prefix, qkv, d_context, cosine, sine)
    d_w_qkv = dot_rows(x_all, d_packed).astype(BF16)
    d_dense = dot_rows(context, d_attn).astype(BF16).reshape(zs, piece, group, width)
    d_dense = jnp.swapaxes(d_dense, 1, 2).reshape(D, width)
    d_w_qkv = jnp.concatenate([d_w_qkv, d_dense], axis=1)
    sums = jnp.concatenate([sums_one[:2], sums_two[:2], jnp.zeros((4, D), F32)])
    d_packed, d_w_qkv, d_w_in, sums = lax.optimization_barrier((d_packed, d_w_qkv, d_w_in, sums))
    d_w_qkv = scatter(d_w_qkv)
    d_w_in, d_w_out = d_w_in.reshape(group, piece, 2 * tile), d_w_out.T.reshape(group, piece, tile)
    d_input, d_w_in, d_w_out, sums = fold_last(
        d_packed, w_qkv_part, d_pre_one, gains, [d_w_in, d_w_out, sums], ("swap", "swap", "group")
    )
    sums = jnp.sum(sums, axis=0).reshape(8, zs, group, piece)
    sums = lax.dynamic_index_in_dim(sums, lax.axis_index(GROUP), 2, keepdims=False).reshape(8, width)
    out_in, out_out = join_ff(d_w_in, d_w_out, ff)
    out_in, out_out, d_input, d_w_qkv, sums = lax.optimization_barrier((out_in, out_out, d_input, d_w_qkv, sums))
    if own:
        out_qkv, out_dense, sums = closing(zs, sums, d_w_qkv.reshape(group, piece, 4 * width))
    else:
        out_dense = d_w_qkv[:, 3 * width :].reshape(group, piece, width)
        out_dense = jnp.swapaxes(out_dense, 0, 1).reshape(piece, D).astype(F32)
        d_w_qkv = d_w_qkv[:, : 3 * width].reshape(group, piece, 3 * width)
        d_w_qkv, sums = swap(5, [d_w_qkv, sums], ("swap", "line"))
        out_qkv = jnp.transpose(d_w_qkv.astype(F32).reshape(group, piece, 3, width), (1, 2, 0, 3))
        out_qkv = out_qkv.reshape(piece, 3 * D)
        sums = jnp.sum(sums, axis=0).reshape(8, zs, piece)
        sums = lax.dynamic_index_in_dim(sums, lax.axis_index("z"), 1, keepdims=False)
    return layer_out, d_input, out_qkv, out_dense, out_in, out_out, sums[0], sums[1], sums[2], sums[3]


def solution(mesh):
    grp, shard = mesh.shape["grp"], mesh.shape["shard"]
    sizes = (grp // 4, 2, 2, shard)
    inner = Mesh(mesh.devices.reshape(sizes), ALL)
    rows, flat = P(ALL, None), P(ALL)
    return jax.shard_map(
        functools.partial(on_device, sizes),
        mesh=inner,
        in_specs=(rows,) * 6 + (flat,) * 7,
        out_specs=(rows,) * 6 + (flat,) * 4,
        check_vma=False,
    )
```

```python
import functools

import jax
import jax.numpy as jnp
from jax import lax
from jax.experimental import pallas as pl
from jax.experimental.pallas import tpu as pltpu
from jax.sharding import Mesh
from jax.sharding import PartitionSpec as P

HEADS = 16
HEAD = 128
SEQ_LEN = 224
D = HEADS * HEAD
deep_alpha = 6.928203230275509
norm_eps = 1e-05
far_below = -1e30
scale = HEAD ** (-0.5)

ALL = ("gy", "gx", "core", "z")
GROUP = ("gy", "gx", "core")
MESH = pl.DeviceIdType.MESH
F32 = jnp.float32
BF16 = jnp.bfloat16


def dot(left, right):
    return jnp.dot(left, right, preferred_element_type=F32)


def dot_rows(left, right):
    return lax.dot_general(left, right, (((0,), (0,)), ((), ())), preferred_element_type=F32)


def dot_cols(left, right):
    return lax.dot_general(left, right, (((1,), (1,)), ((), ())), preferred_element_type=F32)


def swap_halves(block):
    lane = lax.broadcasted_iota(jnp.int32, block.shape, 1)
    return jnp.where((lane & 32) == 0, pltpu.roll(block, 96, 1), pltpu.roll(block, 32, 1))


def seen(prefix):
    row = lax.broadcasted_iota(jnp.int32, (SEQ_LEN, SEQ_LEN), 0)
    col = lax.broadcasted_iota(jnp.int32, (SEQ_LEN, SEQ_LEN), 1)
    return (col < prefix) | (col <= row)


def softmax(queries, keys, visible):
    scores = jnp.where(visible, dot_cols(queries, keys), far_below)
    weights = jnp.exp(scores - jnp.max(scores, axis=1, keepdims=True))
    return weights / jnp.sum(weights, axis=1, keepdims=True)


def attend_kernel(prefix_ref, packed_ref, cos_ref, sin_ref, qkv_ref, context_ref):
    width = context_ref.shape[1]
    visible = seen(prefix_ref[pl.program_id(0)])
    cosine = cos_ref[0]
    sine = sin_ref[0]
    for head in range(width // HEAD):
        at = pl.ds(head * HEAD, HEAD)
        at_k = pl.ds(width + head * HEAD, HEAD)
        at_v = pl.ds(2 * width + head * HEAD, HEAD)
        raw = packed_ref[:, at]
        queries = ((raw * cosine + swap_halves(raw) * sine) * scale).astype(BF16)
        raw = packed_ref[:, at_k]
        keys = (raw * cosine + swap_halves(raw) * sine).astype(BF16)
        values = packed_ref[:, at_v].astype(BF16)
        qkv_ref[:, at] = queries
        qkv_ref[:, at_k] = keys
        qkv_ref[:, at_v] = values
        probs = softmax(queries, keys, visible).astype(BF16)
        context_ref[:, at] = dot(probs, values).astype(BF16)


def attend_back_kernel(prefix_ref, qkv_ref, d_context_ref, cos_ref, sin_ref, d_packed_ref):
    width = d_context_ref.shape[1]
    visible = seen(prefix_ref[pl.program_id(0)])
    cosine = cos_ref[0]
    sine = sin_ref[0]
    for head in range(width // HEAD):
        at = pl.ds(head * HEAD, HEAD)
        at_k = pl.ds(width + head * HEAD, HEAD)
        at_v = pl.ds(2 * width + head * HEAD, HEAD)
        queries = qkv_ref[:, at]
        keys = qkv_ref[:, at_k]
        values = qkv_ref[:, at_v]
        d_context = d_context_ref[:, at]
        probs = softmax(queries, keys, visible)
        d_packed_ref[:, at_v] = dot_rows(probs.astype(BF16), d_context).astype(BF16)
        d_probs = dot_cols(d_context, values)
        inner = jnp.sum(probs * d_probs, axis=1, keepdims=True)
        d_scores = (probs * (d_probs - inner)).astype(BF16)
        grad = dot(d_scores, keys) * scale
        d_packed_ref[:, at] = (grad * cosine - swap_halves(grad) * sine).astype(BF16)
        grad = dot_rows(d_scores, queries)
        d_packed_ref[:, at_k] = (grad * cosine - swap_halves(grad) * sine).astype(BF16)


def by_sequence(width):
    return pl.BlockSpec((SEQ_LEN, width), lambda s: (s, 0))


TABLE = pl.BlockSpec((1, SEQ_LEN, HEAD), lambda s: (s, 0, 0))
SCALARS = pl.BlockSpec(memory_space=pltpu.SMEM)
PARAMS = pltpu.CompilerParams(vmem_limit_bytes=48 * 2**20)


def attend(prefix, packed, cosine, sine):
    rows, width = packed.shape[0], packed.shape[1] // 3
    return pl.pallas_call(
        attend_kernel,
        grid=(rows // SEQ_LEN,),
        in_specs=[SCALARS, by_sequence(3 * width), TABLE, TABLE],
        out_specs=[by_sequence(3 * width), by_sequence(width)],
        out_shape=[
            jax.ShapeDtypeStruct((rows, 3 * width), BF16),
            jax.ShapeDtypeStruct((rows, width), BF16),
        ],
        compiler_params=PARAMS,
    )(prefix, packed, cosine, sine)


def attend_back(prefix, qkv, d_context, cosine, sine):
    rows, width = d_context.shape
    return pl.pallas_call(
        attend_back_kernel,
        grid=(rows // SEQ_LEN,),
        in_specs=[SCALARS, by_sequence(3 * width), by_sequence(width), TABLE, TABLE],
        out_specs=by_sequence(3 * width),
        out_shape=jax.ShapeDtypeStruct((rows, 3 * width), BF16),
        compiler_params=PARAMS,
    )(prefix, qkv, d_context, cosine, sine)


def tables(prefix, start):
    place = jnp.arange(SEQ_LEN, dtype=jnp.int32)
    in_span = place[None, :] >= prefix[:, None]
    pos_one = jnp.where(in_span, start[:, None], place[None, :])
    pos_two = jnp.where(in_span, place[None, :] - prefix[:, None] + 1, 0)
    lane = jnp.arange(HEAD)
    freqs = 10000.0 ** (-2.0 * (lane % 32).astype(F32) / 64)
    place_of = jnp.where(lane[None, None, :] < 64, pos_one[:, :, None], pos_two[:, :, None])
    angles = place_of.astype(F32) * freqs
    sign = jnp.where(lane % 64 < 32, -1.0, 1.0)
    return jnp.cos(angles), jnp.sin(angles) * sign


def norm_parts(values):
    center = values - jnp.mean(values, axis=-1, keepdims=True)
    inverse = lax.rsqrt(jnp.mean(center * center, axis=-1, keepdims=True) + norm_eps)
    return center * inverse, inverse


def norm_back(normal, inverse, gain, grad):
    scaled = gain * grad
    return inverse * (
        scaled
        - jnp.mean(scaled, axis=-1, keepdims=True)
        - normal * jnp.mean(scaled * normal, axis=-1, keepdims=True)
    )


def gate_parts(gate):
    phi = 0.5 * (1.0 + lax.erf(gate * 0.7071067811865476))
    slope = phi + gate * jnp.exp(-0.5 * gate * gate) * 0.3989422804014327
    return gate * phi, slope


def here():
    return lax.axis_index("gy"), lax.axis_index("gx"), lax.axis_index("core")


def place(y, x, c):
    return (y * 2 + x) * 2 + c


def greet(peers):
    barrier = pltpu.get_barrier_semaphore()
    for peer in peers:
        pl.semaphore_signal(barrier, inc=1, device_id=peer, device_id_type=MESH)
    pl.semaphore_wait(barrier, len(peers))


def spread_block(cut, base, block_ref, out_ref, send, recv, local):
    rows = block_ref.shape[0]
    y, x, c = here()
    to_x, to_y, to_c = {"gx": 1 - x}, {"gy": 1 - y}, {"core": 1 - c}
    me, by_x, by_y, far = place(y, x, c), place(y, 1 - x, c), place(1 - y, x, c), place(1 - y, 1 - x, c)
    low, high = pl.ds(0, cut), pl.ds(cut, rows - cut)

    def push(k, src, dst, to):
        copy = pltpu.make_async_remote_copy(
            src_ref=src, dst_ref=dst, send_sem=send.at[base + k], recv_sem=recv.at[base + k], device_id=to, device_id_type=MESH
        )
        copy.start()
        return copy

    def landed(k, dst):
        pltpu.make_async_remote_copy(
            src_ref=dst, dst_ref=dst, send_sem=send.at[base + k], recv_sem=recv.at[base + k], device_id=to_c, device_id_type=MESH
        ).wait_recv()

    sent = [
        push(0, block_ref.at[low], out_ref.at[me, low], to_x),
        push(1, block_ref.at[high], out_ref.at[me, high], to_y),
        push(2, block_ref.at[high], out_ref.at[me, high], to_x),
        push(3, block_ref.at[low], out_ref.at[me, low], to_y),
        push(4, block_ref, out_ref.at[me], to_c),
    ]
    keep = pltpu.make_async_copy(block_ref, out_ref.at[me], local)
    keep.start()
    landed(0, out_ref.at[by_x, low])
    sent.append(push(5, out_ref.at[by_x, low], out_ref.at[by_x, low], to_y))
    sent.append(push(7, out_ref.at[by_x, low], out_ref.at[by_x, low], to_c))
    landed(1, out_ref.at[by_y, high])
    sent.append(push(6, out_ref.at[by_y, high], out_ref.at[by_y, high], to_x))
    sent.append(push(8, out_ref.at[by_y, high], out_ref.at[by_y, high], to_c))
    landed(2, out_ref.at[by_x, high])
    sent.append(push(9, out_ref.at[by_x, high], out_ref.at[by_x, high], to_c))
    landed(3, out_ref.at[by_y, low])
    sent.append(push(10, out_ref.at[by_y, low], out_ref.at[by_y, low], to_c))
    landed(5, out_ref.at[far, low])
    sent.append(push(11, out_ref.at[far, low], out_ref.at[far, low], to_c))
    landed(6, out_ref.at[far, high])
    sent.append(push(12, out_ref.at[far, high], out_ref.at[far, high], to_c))
    other, other_x, other_y, other_far = (
        place(y, x, 1 - c),
        place(y, 1 - x, 1 - c),
        place(1 - y, x, 1 - c),
        place(1 - y, 1 - x, 1 - c),
    )
    landed(4, out_ref.at[other])
    landed(7, out_ref.at[other_x, low])
    landed(8, out_ref.at[other_y, high])
    landed(9, out_ref.at[other_x, high])
    landed(10, out_ref.at[other_y, low])
    landed(11, out_ref.at[other_far, low])
    landed(12, out_ref.at[other_far, high])
    keep.wait()
    for copy in sent:
        copy.wait_send()


ANY = pl.BlockSpec(memory_space=pl.ANY)


def swap_peers(zs, kinds):
    y, x, c = here()
    z = lax.axis_index("z")
    found = []
    for k in range(1, 8):
        peer = ((y + k // 4) % 2, (x + k // 2 % 2) % 2, (c + k % 2) % 2)
        found.append((place(*peer), {"gy": peer[0], "gx": peer[1], "core": peer[2]}))
    if "line" in kinds:
        found += [((z + k) % zs, {"z": (z + k) % zs}) for k in range(1, zs)]
    return found


def swap_begin(zs, kinds, blocks, outs, send, recv, local):
    copies, comes, keeps = [], [], []
    found = swap_peers(zs, kinds)
    for i, kind in enumerate(kinds):
        me = lax.axis_index("z") if kind == "line" else place(*here())
        for k, (peer, name) in enumerate(found[7:] if kind == "line" else found[:7]):
            src = blocks[i].at[peer] if kind == "swap" else blocks[i]
            landing = outs[i].at[peer]
            sems = dict(send_sem=send.at[i, k], recv_sem=recv.at[i, k], device_id=name, device_id_type=MESH)
            copies.append(pltpu.make_async_remote_copy(src_ref=src, dst_ref=outs[i].at[me], **sems))
            comes.append(pltpu.make_async_remote_copy(src_ref=landing, dst_ref=landing, **sems))
            copies[-1].start()
        own = blocks[i].at[me] if kind == "swap" else blocks[i]
        keeps.append(pltpu.make_async_copy(own, outs[i].at[me], local.at[i]))
        keeps[-1].start()

    def finish():
        for come in comes:
            come.wait_recv()
        for copy in copies:
            copy.wait_send()
        for keep in keeps:
            keep.wait()

    return finish


SWAP_LEAD = {"swap": lambda zs: (), "group": lambda zs: (8,), "line": lambda zs: (zs,)}


def swap_shapes(zs, arrays, kinds):
    return [jax.ShapeDtypeStruct(SWAP_LEAD[k](zs) + a.shape, a.dtype) for a, k in zip(arrays, kinds)]


def swap_scratch(zs, kinds):
    n, most = len(kinds), max(7, zs - 1)
    return [
        pltpu.SemaphoreType.DMA((n, most)),
        pltpu.SemaphoreType.DMA((n, most)),
        pltpu.SemaphoreType.DMA((n,)),
    ]


SLAB = 16
ROWS = pl.BlockSpec(memory_space=pltpu.VMEM)
CHIP_COLS = 256


def by_rows(value, zs, piece):
    group = D // (zs * piece)
    order = [g * zs + z for z in range(zs) for g in range(group)]
    return jnp.concatenate([value[:, m * piece : (m + 1) * piece] for m in order], axis=1)


def in_order(value, zs, piece):
    group = D // (zs * piece)
    order = [z * group + g for g in range(group) for z in range(zs)]
    return jnp.concatenate([value[:, m * piece : (m + 1) * piece] for m in order], axis=1)


def first_norm(values, gains):
    normal, inverse = norm_parts(values)
    first = normal * gains[0:1] + gains[1:2]
    return first, normal, inverse


def second_norm(total, first, grad, gains):
    normal, inverse = norm_parts(deep_alpha * first + total)
    return normal * gains[2:3] + gains[3:4], norm_back(normal, inverse, gains[2:3], grad), grad * normal


def first_back(total, d_pre_two, normal, inverse, gains):
    d_first = deep_alpha * d_pre_two + total
    return norm_back(normal, inverse, gains[0:1], d_first), d_first * normal, d_first


def fold_kernel(mode, across, zs, piece, n_aux, n_out, kinds, *refs):
    left_ref, right_ref, gains_ref = refs[:3]
    aux_refs = refs[3 : 3 + n_aux]
    refs = refs[3 + n_aux :]
    n_swap = len(kinds)
    swap_in, refs = refs[:n_swap], refs[n_swap:]
    spread = mode != "last"
    if spread:
        all_ref, refs = refs[0], refs[1:]
    outs, refs = refs[:n_out], refs[n_out:]
    swap_out, refs = refs[:n_swap], refs[n_swap:]
    aux, refs = refs[:n_aux], refs[n_aux:]
    left, right, part, got, near_x, near_y, from_x, from_y, block, acc, send, recv, local = refs[:13]
    rows, width = block.shape
    cut = near_x.shape[0]
    y, x, c = here()
    to_x, to_y, to_c = {"gx": 1 - x}, {"gy": 1 - y}, {"core": 1 - c}
    chips = [(1 - y, 1 - x), (y, 1 - x), (1 - y, x), (y, x)]
    low, high = pl.ds(0, cut), pl.ds(cut, rows - cut)

    def push(k, src, dst, to):
        copy = pltpu.make_async_remote_copy(
            src_ref=src, dst_ref=dst, send_sem=send.at[k], recv_sem=recv.at[k], device_id=to, device_id_type=MESH
        )
        copy.start()
        return copy

    def add(k, extra, start, size, offset=0):
        @pl.loop(0, size // SLAB)
        def _(step):
            at = pl.ds(pl.multiple_of(start + step * SLAB, SLAB), SLAB)
            of = pl.ds(pl.multiple_of(start - offset + step * SLAB, SLAB), SLAB)
            part[k, c, at] = (part[k, c, at].astype(F32) + extra[of].astype(F32)).astype(BF16)

    loads = [pltpu.make_async_copy(left_ref.at[a * 2 + b], left.at[k], local.at[k]) for k, (a, b) in enumerate(chips)]
    load_right = pltpu.make_async_copy(right_ref, right, local.at[4])
    load_aux = [pltpu.make_async_copy(r, v, local.at[5 + k]) for k, (r, v) in enumerate(zip(aux_refs, aux))]
    loads[0].start()
    load_right.start()
    for load in loads[1:] + load_aux:
        load.start()
    if n_swap:
        greet([name for _, name in swap_peers(1, kinds)])
        swap_finish = swap_begin(1, kinds, swap_in, swap_out, *refs[13:])
    else:
        greet([to_x, to_y, to_c])

    def product(k):
        loads[k].wait()

        @pl.loop(0, width // CHIP_COLS)
        def _(step):
            at = pl.ds(pl.multiple_of(step * CHIP_COLS, CHIP_COLS), CHIP_COLS)
            here_part = dot_cols(left[k], right[at]) if across else dot(left[k], right[:, at])
            part[k, 0, :, at] = here_part[:rows].astype(BF16)
            part[k, 1, :, at] = here_part[rows:].astype(BF16)

        return push(k, part.at[k, 1 - c], got.at[k], to_c)

    load_right.wait()
    sent = [product(0), product(1)]
    sent[0].wait_recv()
    add(0, got.at[0], 0, rows)
    far_x = push(4, part.at[0, c, low], near_x, to_x)
    far_y = push(5, part.at[0, c, high], near_y, to_y)
    sent.append(product(2))
    sent[1].wait_recv()
    add(1, got.at[1], 0, rows)
    plain_x = push(6, part.at[1, c, low], from_x.at[low], to_x)
    sent[2].wait_recv()
    add(2, got.at[2], 0, rows)
    plain_y = push(7, part.at[2, c, high], from_y.at[high], to_y)
    sent.append(product(3))
    far_y.wait_recv()
    add(1, near_y, cut, rows - cut, cut)
    more_x = push(8, part.at[1, c, high], from_x.at[high], to_x)
    far_x.wait_recv()
    add(2, near_x, 0, cut)
    more_y = push(9, part.at[2, c, low], from_y.at[low], to_y)
    sent[3].wait_recv()
    for load in load_aux:
        load.wait()
    plain_x.wait_recv()
    plain_y.wait_recv()
    more_x.wait_recv()
    more_y.wait_recv()
    gains = gains_ref[...]
    acc[...] = jnp.zeros_like(acc)

    @pl.loop(0, rows // SLAB)
    def _(step):
        at = pl.ds(pl.multiple_of(step * SLAB, SLAB), SLAB)
        total = part[3, c, at].astype(F32) + got[3, at].astype(F32) + from_x[at].astype(F32) + from_y[at].astype(F32)
        held = [a[at].astype(F32) for a in aux]
        if mode == "one":
            first, normal, inverse = first_norm(by_rows(deep_alpha * held[0] + total, zs, piece), gains)
            outs[0][at] = first
            outs[1][at] = normal
            outs[2][at] = jnp.broadcast_to(inverse, (SLAB, 128))
            block[at] = first.astype(BF16)
        elif mode == "back":
            d_pre, terms, d_first = first_back(total, held[0], held[1], held[2][:, 0:1], gains)
            outs[0][at] = d_pre
            block[at] = in_order(d_pre, zs, piece).astype(BF16)
            acc[0] += terms
            acc[1] += d_first
        else:
            outs[0][at] = in_order(deep_alpha * held[0] + total, zs, piece).astype(BF16)

    if mode == "back":
        outs[-1][0:1] = jnp.sum(acc[0], axis=0, keepdims=True)
        outs[-1][1:2] = jnp.sum(acc[1], axis=0, keepdims=True)
    for copy in sent + [far_x, far_y, plain_x, plain_y, more_x, more_y]:
        copy.wait_send()
    if n_swap:
        swap_finish()
    if spread:
        spread_block(cut, 10, block, all_ref, send, recv, local.at[4])


def group_fold(name, zs, mode, left, right, gains, aux, out_types, extras=(), kinds=()):
    across = mode != "one"
    rows, depth = left.shape[0] // 8, left.shape[1]
    width = gains.shape[1]
    cut = rows // 2
    spread = mode != "last"
    out_shape = [jax.ShapeDtypeStruct((8, rows, width), BF16)] * spread + out_types
    n, n_swap = len(aux), len(extras)
    n_sems = 23 if spread else 10
    return pl.pallas_call(
        functools.partial(fold_kernel, mode, across, zs, width // (8 * zs), n, len(out_types), kinds),
        out_shape=out_shape + swap_shapes(1, extras, kinds),
        in_specs=[ANY, ANY, ROWS] + [ANY] * (n + n_swap),
        out_specs=[ANY] * spread + [ROWS] * len(out_types) + [ANY] * n_swap,
        scratch_shapes=[pltpu.VMEM(a.shape, a.dtype) for a in aux]
        + [
            pltpu.VMEM((4, 2 * rows, depth), BF16),
            pltpu.VMEM(right.shape, BF16),
            pltpu.VMEM((4, 2, rows, width), BF16),
            pltpu.VMEM((4, rows, width), BF16),
            pltpu.VMEM((cut, width), BF16),
            pltpu.VMEM((rows - cut, width), BF16),
            pltpu.VMEM((rows, width), BF16),
            pltpu.VMEM((rows, width), BF16),
            pltpu.VMEM((rows, width), BF16),
            pltpu.VMEM((2, SLAB, width), F32),
            pltpu.SemaphoreType.DMA((n_sems,)),
            pltpu.SemaphoreType.DMA((n_sems,)),
            pltpu.SemaphoreType.DMA((5 + n,)),
        ]
        + (swap_scratch(1, kinds) if n_swap else []),
        compiler_params=pltpu.CompilerParams(
            collective_id=name, has_side_effects=True, vmem_limit_bytes=50 * 2**20
        ),
        cost_estimate=pl.CostEstimate(flops=0, bytes_accessed=(200 if spread else 110) * 2**20, transcendentals=0),
    )(left.reshape(4, 2 * rows, depth), right, gains, *aux, *extras)


def turn_kernel(
    zs, piece, x_ref, in_ref, out_ref, gains_ref, first_ref, grad_ref,
    all_ref, kept_ref, right_ref, result_ref, d_pre_ref, sums_ref, dw_ref,
    first, grad, w_in, kept, left, right, part, got, near_x, near_y, from_x, from_y, whole, dw, acc,
    fold_send, fold_recv, all_send, all_recv, line_send, line_recv, local, x_local
):
    rows = first.shape[0]
    tile = left.shape[2]
    wide = right.shape[2]
    y, x, c = here()
    z = lax.axis_index("z")
    to_x, to_y, to_c = {"gx": 1 - x}, {"gy": 1 - y}, {"core": 1 - c}
    chips = [(1 - y) * 2 + 1 - x, y * 2 + 1 - x, (1 - y) * 2 + x, y * 2 + x]
    me, by_x, by_y, far = place(y, x, c), place(y, 1 - x, c), place(1 - y, x, c), place(1 - y, 1 - x, c)
    other, other_x, other_y, other_far = (
        place(y, x, 1 - c),
        place(y, 1 - x, 1 - c),
        place(1 - y, x, 1 - c),
        place(1 - y, 1 - x, 1 - c),
    )
    half = rows // 2
    most = -(-half // (2 * SLAB)) * SLAB
    lows = [(0, most), (half, half - most)]
    highs = [(most, half - most), (2 * half - most, most)]
    top, bottom = pl.ds(0, half), pl.ds(half, half)
    sent = []

    def remote(sems, k, src, dst, to):
        return pltpu.make_async_remote_copy(
            src_ref=src,
            dst_ref=dst,
            send_sem=sems[0].at[k],
            recv_sem=sems[1].at[k],
            device_id=to,
            device_id_type=MESH,
        )

    def push(sems, k, src, dst, to):
        copy = remote(sems, k, src, dst, to)
        copy.start()
        sent.append(copy)

    def landed(sems, k, dst):
        remote(sems, k, dst, dst, to_c).wait_recv()

    folds, alls, lines = (fold_send, fold_recv), (all_send, all_recv), (line_send, line_recv)

    load_out = pltpu.make_async_copy(out_ref, right.at[z], local.at[0])
    load_in = pltpu.make_async_copy(in_ref, w_in, local.at[1])
    load_first = pltpu.make_async_copy(first_ref, first, local.at[2])
    load_grad = pltpu.make_async_copy(grad_ref, grad, local.at[3])

    def load_x(g):
        return pltpu.make_async_copy(x_ref.at[g], whole.at[g], x_local.at[g])

    load_out.start()
    load_in.start()
    for g in range(8):
        load_x(g).start()
    load_first.start()
    load_grad.start()

    barrier = pltpu.get_barrier_semaphore()
    for to in (to_x, to_y, to_c):
        pl.semaphore_signal(barrier, inc=1, device_id=to, device_id_type=MESH)

    @pl.when(z > 0)
    def _():
        pl.semaphore_signal(barrier, inc=1, device_id={"z": z - 1}, device_id_type=MESH)

    @pl.when(z < zs - 1)
    def _():
        pl.semaphore_signal(barrier, inc=1, device_id={"z": z + 1}, device_id_type=MESH)

    inside = (z > 0) & (z < zs - 1)

    @pl.when(inside)
    def _():
        pl.semaphore_wait(barrier, 5)

    @pl.when(jnp.logical_not(inside))
    def _():
        pl.semaphore_wait(barrier, 4)

    def shard_of(step, up):
        return z - step if up else z + step

    def hop(step, up):
        ref = right.at[shard_of(step, up)]
        return remote(lines, 2 * step + (0 if up else 1), ref, ref, {"z": z + 1 if up else z - 1})

    def sends(step, up):
        return (z >= step) & (z < zs - 1) if up else (z <= zs - 1 - step) & (z > 0)

    def gets(step, up):
        return z >= step + 1 if up else z <= zs - 2 - step

    def line_serve(step):
        for up in (True, False):

            @pl.when(gets(step - 1, up) & sends(step, up))
            def _(up=up):
                landed(lines, 2 * (step - 1) + (0 if up else 1), right.at[shard_of(step, up)])
                hop(step, up).start()

    def line_take(step):
        for up in (True, False):

            @pl.when(gets(step - 1, up) & jnp.logical_not(sends(step, up)))
            def _(up=up):
                landed(lines, 2 * (step - 1) + (0 if up else 1), right.at[shard_of(step, up)])

    load_out.wait()
    for up in (True, False):

        @pl.when(sends(0, up))
        def _(up=up):
            hop(0, up).start()


    load_in.wait()

    @pl.loop(0, 8)
    def _(g):
        @pl.when(g == 6)
        def _():
            line_serve(1)

        load_x(g).wait()
        projected = dot(whole[g], w_in[...])
        gate, up = projected[:, :tile], projected[:, tile:]
        act, slope = gate_parts(gate)
        left[g] = (act * up).astype(BF16)
        kept[g] = jnp.concatenate([up * slope, act], axis=1).astype(BF16)

    keep = pltpu.make_async_copy(kept, kept_ref, local.at[4])
    keep.start()

    def add(k, extra, start, offset, at):
        @pl.loop(0, half // SLAB)
        def _(step):
            row = pl.ds(pl.multiple_of(start + step * SLAB, SLAB), SLAB)
            of = pl.ds(pl.multiple_of(start - offset + step * SLAB, SLAB), SLAB)
            part[k, c, row, at] = (part[k, c, row, at].astype(F32) + extra[of, at].astype(F32)).astype(BF16)

    def chip_sum(k, at):
        add(k, got.at[k], 0, 0, at)
        add(k, got.at[k], half, 0, at)

    def product(k, block, at):
        found = dot(left[pl.ds(2 * chips[k], 2)].reshape(2 * rows, tile), right[block])
        part[k, 0, :, at] = found[:rows].astype(BF16)
        part[k, 1, :, at] = found[rows:].astype(BF16)

    def block_at(i):
        if i == 0:
            return z
        below = z < zs // 2
        near = jnp.where(below, z, zs - 1 - z)
        spot = jnp.where(i <= 2 * near, jnp.where(i % 2 == 1, near - (i + 1) // 2, near + i // 2), i)
        return jnp.where(below, spot, zs - 1 - spot)

    def block_cols(i):
        return pl.ds(pl.multiple_of(block_at(i) * wide, wide), wide)

    def fold_start(i):
        b, block, at = 8 * i, block_at(i), block_cols(i)
        rest = pl.ds(1, 3)
        product(0, block, at)
        push(folds, b, part.at[0, 1 - c, :, at], got.at[0, :, at], to_c)
        for k in (1, 2, 3):
            product(k, block, at)
        push(folds, b + 1, part.at[rest, 1 - c, :, at], got.at[rest, :, at], to_c)
        landed(folds, b, got.at[0, :, at])
        chip_sum(0, at)
        push(folds, b + 2, part.at[0, c, top, at], near_x.at[:, at], to_x)
        push(folds, b + 3, part.at[0, c, bottom, at], near_y.at[:, at], to_y)
        landed(folds, b + 1, got.at[rest, :, at])
        chip_sum(1, at)
        push(folds, b + 4, part.at[1, c, top, at], from_x.at[top, at], to_x)
        chip_sum(2, at)
        push(folds, b + 5, part.at[2, c, bottom, at], from_y.at[bottom, at], to_y)

    def fold_end(i):
        b, at = 8 * i, block_cols(i)
        landed(folds, b + 3, near_y.at[:, at])
        add(1, near_y, half, half, at)
        push(folds, b + 6, part.at[1, c, bottom, at], from_x.at[bottom, at], to_x)
        landed(folds, b + 2, near_x.at[:, at])
        add(2, near_x, 0, 0, at)
        push(folds, b + 7, part.at[2, c, top, at], from_y.at[top, at], to_y)

    gains = gains_ref[...]
    line_take(1)
    fold_start(0)
    fold_start(1)
    fold_end(0)
    for i in range(2, zs):
        if i < zs - 1:
            line_serve(i)
        fold_end(i - 1)
        line_take(i)
        fold_start(i)
    fold_end(zs - 1)
    carry = pltpu.make_async_copy(right, right_ref, local.at[5])
    carry.start()
    load_first.wait()
    load_grad.wait()
    acc[...] = jnp.zeros_like(acc)
    for i in range(zs):
        at = block_cols(i)
        landed(folds, 8 * i + 4, from_x.at[top, at])
        landed(folds, 8 * i + 5, from_y.at[bottom, at])
        landed(folds, 8 * i + 6, from_x.at[bottom, at])
        landed(folds, 8 * i + 7, from_y.at[top, at])

    def low(i):
        return pl.ds(*lows[i])

    def high(i):
        return pl.ds(*highs[i])

    def span(i):
        return pl.ds(i * half, half)

    def norm(i):
        @pl.loop(0, half // SLAB)
        def _(step):
            at = pl.ds(pl.multiple_of(i * half + step * SLAB, SLAB), SLAB)
            total = part[3, c, at].astype(F32) + got[3, at].astype(F32)
            total += from_x[at].astype(F32) + from_y[at].astype(F32)
            dy = grad[at].astype(F32)
            result, d_pre, terms = second_norm(total, first[at], dy, gains)
            result_ref[at] = result.astype(BF16)
            d_pre_ref[at] = d_pre
            whole[me, at] = d_pre.astype(BF16)
            acc[0] += terms
            acc[1] += dy

        b = 13 * i
        push(alls, b, whole.at[me, low(i)], whole.at[me, low(i)], to_x)
        push(alls, b + 1, whole.at[me, high(i)], whole.at[me, high(i)], to_y)
        push(alls, b + 2, whole.at[me, high(i)], whole.at[me, high(i)], to_x)
        push(alls, b + 3, whole.at[me, low(i)], whole.at[me, low(i)], to_y)
        push(alls, b + 4, whole.at[me, span(i)], whole.at[me, span(i)], to_c)

    def pass_on(i, k, slot, at, onward):
        ref = whole.at[slot, at]
        landed(alls, 13 * i + k, ref)
        for where, to in onward:
            push(alls, 13 * i + where, ref, ref, to)

    def spread_first(i):
        pass_on(i, 0, by_x, low(i), [(5, to_y), (7, to_c)])
        pass_on(i, 1, by_y, high(i), [(6, to_x), (8, to_c)])

    def spread_rest(i):
        pass_on(i, 2, by_x, high(i), [(9, to_c)])
        pass_on(i, 3, by_y, low(i), [(10, to_c)])

    def spread_far(i):
        pass_on(i, 5, far, low(i), [(11, to_c)])
        pass_on(i, 6, far, high(i), [(12, to_c)])

    outward = []

    def gradient(k, last=False, first_one=False):
        pair = pl.ds(2 * chips[k], 2)
        outward.append(pltpu.make_async_copy(whole.at[pair], all_ref.at[pair], local.at[6 + k]))
        outward[-1].start()

        @pl.loop(0, zs)
        def _(block):
            at = pl.ds(pl.multiple_of(block * wide, wide), wide)
            found = dot_rows(left[pair].reshape(2 * rows, tile), whole[pair, :, at].reshape(2 * rows, wide))
            if first_one:
                dw[block] = found
            elif last:
                dw_ref[block] = (dw[block] + found).astype(BF16)
            else:
                dw[block] += found

    norm(0)
    norm(1)
    spread_first(0)
    for i in (0, 1):
        landed(alls, 13 * i + 4, whole.at[other, span(i)])
    gradient(3, first_one=True)
    spread_rest(0)
    spread_first(1)
    spread_rest(1)
    for i in (0, 1):
        landed(alls, 13 * i + 7, whole.at[other_x, low(i)])
        landed(alls, 13 * i + 9, whole.at[other_x, high(i)])
    gradient(1)
    spread_far(0)
    for i in (0, 1):
        landed(alls, 13 * i + 8, whole.at[other_y, high(i)])
        landed(alls, 13 * i + 10, whole.at[other_y, low(i)])
    gradient(2)
    sums_ref[0:1] = jnp.sum(acc[0], axis=0, keepdims=True)
    sums_ref[1:2] = jnp.sum(acc[1], axis=0, keepdims=True)
    spread_far(1)
    for i in (0, 1):
        landed(alls, 13 * i + 11, whole.at[other_far, low(i)])
        landed(alls, 13 * i + 12, whole.at[other_far, high(i)])
    gradient(0, last=True)
    for copy in outward + [keep, carry]:
        copy.wait()
    for copy in sent:
        copy.wait_send()
    for step in range(zs - 1):
        for up in (True, False):

            @pl.when(sends(step, up))
            def _(step=step, up=up):
                hop(step, up).wait_send()


def turn(zs, x, w_in, w_out, gains, first, grad):
    rows = x.shape[0] // 8
    units, wide = w_out.shape
    width = gains.shape[1]
    half = rows // 2
    by_z = (zs, units, wide)
    return pl.pallas_call(
        functools.partial(turn_kernel, zs, width // (8 * zs)),
        out_shape=[
            jax.ShapeDtypeStruct((8, rows, width), BF16),
            jax.ShapeDtypeStruct((8, rows, 2 * units), BF16),
            jax.ShapeDtypeStruct(by_z, BF16),
            jax.ShapeDtypeStruct((rows, width), BF16),
            jax.ShapeDtypeStruct((rows, width), F32),
            jax.ShapeDtypeStruct((8, width), F32),
            jax.ShapeDtypeStruct(by_z, BF16),
        ],
        in_specs=[ANY, ANY, ANY, ROWS, ANY, ANY],
        out_specs=[ANY] * 3 + [ROWS] * 4,
        scratch_shapes=[
            pltpu.VMEM((rows, width), F32),
            pltpu.VMEM((rows, width), BF16),
            pltpu.VMEM(w_in.shape, BF16),
            pltpu.VMEM((8, rows, 2 * units), BF16),
            pltpu.VMEM((8, rows, units), BF16),
            pltpu.VMEM(by_z, BF16),
            pltpu.VMEM((4, 2, rows, width), BF16),
            pltpu.VMEM((4, rows, width), BF16),
            pltpu.VMEM((half, width), BF16),
            pltpu.VMEM((half, width), BF16),
            pltpu.VMEM((rows, width), BF16),
            pltpu.VMEM((rows, width), BF16),
            pltpu.VMEM((8, rows, width), BF16),
            pltpu.VMEM(by_z, F32),
            pltpu.VMEM((2, SLAB, width), F32),
            pltpu.SemaphoreType.DMA((8 * zs,)),
            pltpu.SemaphoreType.DMA((8 * zs,)),
            pltpu.SemaphoreType.DMA((26,)),
            pltpu.SemaphoreType.DMA((26,)),
            pltpu.SemaphoreType.DMA((2 * (zs - 1),)),
            pltpu.SemaphoreType.DMA((2 * (zs - 1),)),
            pltpu.SemaphoreType.DMA((10,)),
            pltpu.SemaphoreType.DMA((8,)),
        ],
        compiler_params=pltpu.CompilerParams(collective_id=1, has_side_effects=True, vmem_limit_bytes=60 * 2**20),
        cost_estimate=pl.CostEstimate(flops=0, bytes_accessed=380 * 2**20, transcendentals=0),
    )(x.reshape(8, rows, width), w_in, w_out, gains, first, grad)


def swap_kernel(zs, kinds, *refs):
    n = len(kinds)
    greet([name for _, name in swap_peers(zs, kinds)])
    swap_begin(zs, kinds, refs[:n], refs[n : 2 * n], *refs[2 * n :])()


def group_swap(name, zs, arrays, kinds):
    n = len(arrays)
    return pl.pallas_call(
        functools.partial(swap_kernel, zs, kinds),
        out_shape=swap_shapes(zs, arrays, kinds),
        in_specs=[ANY] * n,
        out_specs=[ANY] * n,
        scratch_shapes=swap_scratch(zs, kinds),
        compiler_params=pltpu.CompilerParams(collective_id=name, has_side_effects=True),
        cost_estimate=pl.CostEstimate(flops=0, bytes_accessed=50 * 2**20, transcendentals=0),
    )(*arrays)


def enter_kernel(zs, kinds, x_ref, grad_ref, *refs):
    n = len(kinds)
    blocks, x_all, grad_out, outs, refs = refs[:n], refs[n], refs[n + 1], refs[n + 2 : 2 * n + 2], refs[2 * n + 2 :]
    x_rows, sems = refs[0], refs[1:]
    rows, width = x_ref.shape
    greet([name for _, name in swap_peers(zs, kinds)])
    finish = swap_begin(zs, kinds, blocks, outs, *sems[:3])
    for ref, out in ((x_ref, x_rows), (grad_ref, grad_out)):

        @pl.loop(0, rows // SLAB)
        def _(step, ref=ref, out=out):
            at = pl.ds(pl.multiple_of(step * SLAB, SLAB), SLAB)
            out[at] = by_rows(ref[at].astype(F32), zs, width // (8 * zs)).astype(BF16)

    spread_block(rows // 2, 0, x_rows, x_all, *sems[3:])
    finish()


def enter(zs, x, grad, arrays, kinds):
    n = len(arrays)
    return pl.pallas_call(
        functools.partial(enter_kernel, zs, kinds),
        out_shape=[jax.ShapeDtypeStruct((8,) + x.shape, x.dtype), jax.ShapeDtypeStruct(grad.shape, grad.dtype)]
        + swap_shapes(zs, arrays, kinds),
        in_specs=[ROWS] * 2 + [ANY] * n,
        out_specs=[ANY, ROWS] + [ANY] * n,
        scratch_shapes=[pltpu.VMEM(x.shape, x.dtype)]
        + swap_scratch(zs, kinds)
        + [pltpu.SemaphoreType.DMA((13,)), pltpu.SemaphoreType.DMA((13,)), pltpu.SemaphoreType.DMA],
        compiler_params=pltpu.CompilerParams(collective_id=3, has_side_effects=True, vmem_limit_bytes=24 * 2**20),
        cost_estimate=pl.CostEstimate(flops=0, bytes_accessed=150 * 2**20, transcendentals=0),
    )(x, grad, *arrays)


def ff_kernel(x_ref, w_ref, hidden_ref, kept_ref):
    tile = hidden_ref.shape[1]
    projected = dot(x_ref[...], w_ref[...])
    gate, up = projected[:, :tile], projected[:, tile:]
    act, slope = gate_parts(gate)
    hidden_ref[...] = (act * up).astype(BF16)
    kept_ref[...] = jnp.concatenate([up * slope, act], axis=1).astype(BF16)


def ff_back_kernel(grad_ref, w_ref, kept_ref, out_ref):
    zs, _, wide = w_ref.shape
    d_hidden = dot_cols(grad_ref[:, :wide], w_ref[0])
    for z in range(1, zs):
        d_hidden += dot_cols(grad_ref[:, z * wide : (z + 1) * wide], w_ref[z])
    out_ref[...] = (jnp.concatenate([d_hidden, d_hidden], axis=1) * kept_ref[...].astype(F32)).astype(BF16)


FF_ROWS = 256


def ff_rows(width):
    return pl.BlockSpec((FF_ROWS, width), lambda i: (i, 0))


def ff_forward(x, w):
    rows, depth = x.shape
    wide = w.shape[1]
    return pl.pallas_call(
        ff_kernel,
        grid=(rows // FF_ROWS,),
        in_specs=[ff_rows(depth), pl.BlockSpec((depth, wide), lambda i: (0, 0))],
        out_specs=[ff_rows(wide // 2), ff_rows(wide)],
        out_shape=[jax.ShapeDtypeStruct((rows, wide // 2), BF16), jax.ShapeDtypeStruct((rows, wide), BF16)],
        compiler_params=PARAMS,
        cost_estimate=pl.CostEstimate(flops=2 * rows * depth * wide, bytes_accessed=20 * 2**20, transcendentals=0),
    )(x, w)


def ff_backward(grad, w, kept):
    rows, depth = grad.shape
    wide = kept.shape[1]
    return pl.pallas_call(
        ff_back_kernel,
        grid=(rows // FF_ROWS,),
        in_specs=[ff_rows(depth), pl.BlockSpec(w.shape, lambda i: (0, 0, 0)), ff_rows(wide)],
        out_specs=ff_rows(wide),
        out_shape=jax.ShapeDtypeStruct((rows, wide), BF16),
        compiler_params=PARAMS,
        cost_estimate=pl.CostEstimate(flops=rows * depth * wide, bytes_accessed=20 * 2**20, transcendentals=0),
    )(grad, w, kept)


def cut_kernel(in_ref, out_ref, in_blocks, out_blocks, wide):
    group, _, double = in_blocks.shape
    tile, ff = double // 2, out_ref.shape[1]
    span = group * tile
    odd = ff % 128
    live = lax.broadcasted_iota(jnp.int32, (in_ref.shape[0], span), 1) < ff
    wide[...] = jnp.zeros_like(wide)
    wide[:, : 2 * ff] = in_ref[...].astype(F32)
    gate = jnp.where(live, wide[:, :span], 0.0)
    up = pltpu.roll(wide[:, ff - odd : ff - odd + span], span - odd, 1)
    up = jnp.where(live, up, 0.0)
    wide[:, :span] = jnp.zeros_like(live, F32)
    wide[:, :ff] = out_ref[...].astype(F32)
    down = wide[:, :span]
    for g in range(group):
        at = slice(g * tile, (g + 1) * tile)
        in_blocks[g] = jnp.concatenate([gate[:, at], up[:, at]], axis=1).astype(BF16)
        out_blocks[g] = down[:, at].astype(BF16)


def cut_ff(w_in, w_out, group, tile):
    rows, ff = w_out.shape
    return pl.pallas_call(
        cut_kernel,
        grid=(rows // 16,),
        in_specs=[pl.BlockSpec((16, 2 * ff), lambda i: (i, 0)), pl.BlockSpec((16, ff), lambda i: (i, 0))],
        out_specs=[
            pl.BlockSpec((group, 16, 2 * tile), lambda i: (0, i, 0)),
            pl.BlockSpec((group, 16, tile), lambda i: (0, i, 0)),
        ],
        out_shape=[
            jax.ShapeDtypeStruct((group, rows, 2 * tile), BF16),
            jax.ShapeDtypeStruct((group, rows, tile), BF16),
        ],
        scratch_shapes=[pltpu.VMEM((16, -(-(ff + group * tile) // 128) * 128), F32)],
        compiler_params=PARAMS,
    )(w_in, w_out)


def join_kernel(in_blocks, out_blocks, in_ref, out_ref):
    group, _, double = in_blocks.shape
    tile, ff = double // 2, out_ref.shape[1]
    odd = ff % 128
    blocks = [in_blocks[g].astype(F32) for g in range(group)]
    gate = jnp.concatenate([block[:, :tile] for block in blocks], axis=1)
    up = jnp.concatenate([block[:, tile:] for block in blocks], axis=1)
    up = pltpu.roll(up, odd, 1)
    lane = lax.broadcasted_iota(jnp.int32, (up.shape[0], 128), 1)
    in_ref[:, : ff - odd] = gate[:, : ff - odd]
    in_ref[:, ff - odd : ff - odd + 128] = jnp.where(lane < odd, gate[:, ff - odd : ff - odd + 128], up[:, :128])
    in_ref[:, ff - odd + 128 :] = up[:, 128 : ff + odd]
    down = jnp.concatenate([out_blocks[g].astype(F32) for g in range(group)], axis=1)
    out_ref[...] = down[:, :ff]


def join_ff(in_blocks, out_blocks, ff):
    group, rows, tile = out_blocks.shape
    return pl.pallas_call(
        join_kernel,
        grid=(rows // 16,),
        in_specs=[
            pl.BlockSpec((group, 16, 2 * tile), lambda i: (0, i, 0)),
            pl.BlockSpec((group, 16, tile), lambda i: (0, i, 0)),
        ],
        out_specs=[pl.BlockSpec((16, 2 * ff), lambda i: (i, 0)), pl.BlockSpec((16, ff), lambda i: (i, 0))],
        out_shape=[jax.ShapeDtypeStruct((rows, 2 * ff), F32), jax.ShapeDtypeStruct((rows, ff), F32)],
        compiler_params=PARAMS,
    )(in_blocks, out_blocks)


def closing_kernel(zs, sum_ref, rows_ref, qkv_ref, dense_ref, total_ref, got, mine, lines, *refs):
    send, recv, local, line_send, line_recv = refs
    y, x, c = here()
    z = lax.axis_index("z")
    me = place(y, x, c)
    wide = got.shape[2]
    width = wide // 3
    piece = got.shape[1]
    found = swap_peers(zs, ("line",))
    greet([name for _, name in found])
    copies, comes = [], []
    for k, (peer, name) in enumerate(found[:7]):
        sems = dict(send_sem=send.at[k], recv_sem=recv.at[k], device_id=name, device_id_type=MESH)
        src = rows_ref.at[peer, :, pl.ds(0, wide)]
        copies.append(pltpu.make_async_remote_copy(src_ref=src, dst_ref=got.at[me], **sems))
        comes.append(pltpu.make_async_remote_copy(src_ref=got.at[peer], dst_ref=got.at[peer], **sems))
    for k, (peer, name) in enumerate(found[7:]):
        sems = dict(send_sem=line_send.at[k], recv_sem=line_recv.at[k], device_id=name, device_id_type=MESH)
        copies.append(pltpu.make_async_remote_copy(src_ref=sum_ref, dst_ref=lines.at[z], **sems))
        comes.append(pltpu.make_async_remote_copy(src_ref=lines.at[peer], dst_ref=lines.at[peer], **sems))
    for copy in copies:
        copy.start()
    keeps = [
        pltpu.make_async_copy(rows_ref.at[me, :, pl.ds(0, wide)], got.at[me], local.at[0]),
        pltpu.make_async_copy(sum_ref, lines.at[z], local.at[1]),
        pltpu.make_async_copy(rows_ref.at[:, :, pl.ds(wide, width)], mine, local.at[2]),
    ]
    for keep in keeps:
        keep.start()
    keeps[2].wait()
    for at in range(0, piece, 16):
        rows = jnp.concatenate([mine[g, at : at + 16] for g in range(8)], axis=1).astype(F32)
        dense_ref[at : at + 16] = rows
    for come in comes:
        come.wait_recv()
    for keep in keeps[:2]:
        keep.wait()
    for g in range(8):
        for j in range(3):
            at = pl.ds(j * D + g * width, width)
            qkv_ref[:, at] = got[g, :, j * width : (j + 1) * width].astype(F32)
    total = lines[0]
    for k in range(1, zs):
        total += lines[k]
    part = total[:, :piece]
    for k in range(1, zs):
        part = jnp.where(z == k, total[:, k * piece : (k + 1) * piece], part)
    total_ref[...] = part
    for copy in copies:
        copy.wait_send()


def closing(zs, sums, rows):
    _, piece, columns = rows.shape
    width = columns // 4
    return pl.pallas_call(
        functools.partial(closing_kernel, zs),
        out_shape=[
            jax.ShapeDtypeStruct((piece, 3 * D), F32),
            jax.ShapeDtypeStruct((piece, D), F32),
            jax.ShapeDtypeStruct((8, piece), F32),
        ],
        in_specs=[ROWS, ANY],
        out_specs=[ROWS] * 3,
        scratch_shapes=[
            pltpu.VMEM((8, piece, 3 * width), BF16),
            pltpu.VMEM((8, piece, width), BF16),
            pltpu.VMEM((zs, 8, width), F32),
            pltpu.SemaphoreType.DMA((7,)),
            pltpu.SemaphoreType.DMA((7,)),
            pltpu.SemaphoreType.DMA((3,)),
            pltpu.SemaphoreType.DMA((zs - 1,)),
            pltpu.SemaphoreType.DMA((zs - 1,)),
        ],
        compiler_params=pltpu.CompilerParams(collective_id=5, has_side_effects=True, vmem_limit_bytes=24 * 2**20),
        cost_estimate=pl.CostEstimate(flops=0, bytes_accessed=50 * 2**20, transcendentals=0),
    )(sums, rows)


def on_device(sizes, x_in, d_out, w_qkv, w_dense, w_in, w_out, gone, bone, gtwo, btwo, flags, span_start, span_len):
    gy, gx, cores, zs = sizes
    piece = w_qkv.shape[0]
    ff = w_out.shape[1]
    group = gy * gx * cores
    width = D // group
    tile = -(-ff // (group * 64)) * 64
    own = gy == 2

    def permute(array):
        lead = array.shape[:-1]
        return jnp.swapaxes(array.reshape(lead + (group, zs, piece)), -3, -2).reshape(lead + (D,))

    def restore(array):
        lead = array.shape[:-1]
        return jnp.swapaxes(array.reshape(lead + (zs, group, piece)), -3, -2).reshape(lead + (D,))

    def swap(name, arrays, kinds):
        if own:
            return group_swap(name, zs, arrays, kinds)
        ways = {
            "swap": lambda a: lax.all_to_all(a, GROUP, 0, 0, tiled=True),
            "group": lambda a: lax.all_gather(a, GROUP, axis=0),
            "line": lambda a: lax.all_gather(a, "z", axis=0),
        }
        return [ways[k](a) for a, k in zip(arrays, kinds)]

    def spread_rows(block):
        return lax.all_gather(block, GROUP, axis=0, tiled=True)

    rows_f32 = jax.ShapeDtypeStruct((SEQ_LEN, D), F32)
    rows_low = jax.ShapeDtypeStruct((SEQ_LEN, D), BF16)
    sums_type = jax.ShapeDtypeStruct((8, D), F32)

    def fold(partial):
        return lax.psum_scatter(partial.astype(BF16), GROUP, scatter_dimension=0, tiled=True).astype(F32)

    def stack_sums(*arrays):
        return jnp.pad(jnp.stack([jnp.sum(a, axis=0) for a in arrays]), ((0, 6), (0, 0)))

    def fold_one(left, right, x, gains):
        if own:
            kinds = [rows_f32, rows_f32, jax.ShapeDtypeStruct((SEQ_LEN, 128), F32)]
            whole, first, normal, inverse = group_fold(0, zs, "one", left, right, gains, [x], kinds)
            return whole.reshape(left.shape[0], D), first, normal, inverse
        first, normal, inverse = first_norm(permute(deep_alpha * x.astype(F32) + fold(dot(left, right))), gains)
        return spread_rows(first.astype(BF16)), first, normal, inverse

    def ff_turn(x, w_in, w_out, first, grad, gains):
        if own:
            whole, kept, w_out, result, d_pre, sums, d_out = turn(zs, x, w_in, w_out, gains, first, grad)
            rows = x.shape[0]
            return whole.reshape(rows, D), kept.reshape(rows, -1), w_out, result, d_pre, sums, d_out
        w_out = lax.all_gather(w_out, "z", axis=0)
        hidden, kept = ff_forward(x, w_in)
        grad = grad.astype(F32)
        right = jnp.swapaxes(w_out, 0, 1).reshape(-1, D)
        result, d_pre, terms = second_norm(fold(dot(hidden, right)), first, grad, gains)
        whole = spread_rows(d_pre.astype(BF16))
        d_out = jnp.swapaxes(dot_rows(hidden, whole).reshape(-1, zs, D // zs), 0, 1).astype(BF16)
        return whole, kept, w_out, result.astype(BF16), d_pre, stack_sums(terms, grad), d_out

    def fold_back(left, right, d_pre_two, normal, inverse, gains):
        if own:
            kinds = [rows_f32, sums_type]
            whole, d_pre, sums = group_fold(7, zs, "back", left, right, gains, [d_pre_two, normal, inverse], kinds)
            return whole.reshape(left.shape[0], D), d_pre, sums
        d_pre, terms, d_first = first_back(fold(dot_cols(left, right)), d_pre_two, normal, inverse, gains)
        return spread_rows(restore(d_pre).astype(BF16)), d_pre, stack_sums(terms, d_first)

    def fold_last(left, right, d_pre, gains, extras, kinds):
        if own:
            return group_fold(8, zs, "last", left, right, gains, [d_pre], [rows_low], extras, kinds)
        out = restore((deep_alpha * d_pre + fold(dot_cols(left, right))).astype(BF16))
        return [out] + swap(8, extras, kinds)

    def gather(block):
        return lax.all_gather(block, "z", axis=0, tiled=True)

    def scatter(partial):
        return lax.psum_scatter(partial.astype(BF16), "z", scatter_dimension=0, tiled=True)

    masked = jnp.max(flags) > 0
    prefix = jnp.where(masked, SEQ_LEN, SEQ_LEN - span_len[0])
    info = jnp.concatenate([gone, bone, gtwo, btwo, jnp.stack([prefix, span_start[0]]).astype(BF16)])
    info = jnp.pad(info[None, :], ((0, 15), (0, -info.shape[0] % 128)))

    qkv_blocks = jnp.moveaxis(w_qkv.reshape(piece, 3, group, width), 2, 0).reshape(group, piece, 3 * width)
    w_dense_part = gather(w_dense)
    qkv_blocks, info = swap(2, [qkv_blocks, info], ("swap", "group"))
    w_qkv_part = gather(qkv_blocks.reshape(group * piece, 3 * width))
    info = info[:, 0]
    place_info = info[:, 4 * piece : 4 * piece + 2].astype(jnp.int32)
    prefix, start = place_info[:, 0], place_info[:, 1]
    cosine, sine = tables(prefix, start)
    in_blocks, out_blocks = cut_ff(w_in, w_out, group, tile)
    info = jnp.pad(info, ((0, -group % 16), (0, 0)))
    in_blocks, out_blocks, qkv_blocks, w_dense_part, cosine, sine = lax.optimization_barrier(
        (in_blocks, out_blocks, qkv_blocks, w_dense_part, cosine, sine)
    )
    swapped, kinds = [in_blocks, out_blocks, info], ("swap", "swap", "line")
    if own:
        x_all, grad_two, in_blocks, out_blocks, info = enter(zs, x_in, d_out, swapped, kinds)
        x_all = x_all.reshape(group * SEQ_LEN, D)
    else:
        x_all, grad_two = spread_rows(permute(x_in)), permute(d_out)
        in_blocks, out_blocks, info = swap(3, swapped, kinds)
    w_in_part = gather(in_blocks.reshape(group * piece, 2 * tile))
    out_rows = out_blocks.reshape(group * piece, tile).T
    gains = info[:, :group, : 4 * piece].astype(F32).reshape(zs, group, 4, piece)
    gains = jnp.pad(jnp.transpose(gains, (2, 0, 1, 3)).reshape(4, D), ((0, 4), (0, 0)))
    w_qkv_part, x_all, gains, out_rows = lax.optimization_barrier((w_qkv_part, x_all, gains, out_rows))
    packed = dot(x_all, w_qkv_part)
    qkv, context = attend(prefix, packed, cosine, sine)
    first_all, first, normal_one, inverse_one = fold_one(context, w_dense_part, x_in, gains)
    d_branch, kept, w_out_part, layer_out, d_pre_two, sums_two, d_w_out = ff_turn(
        first_all, w_in_part, out_rows, first, grad_two, gains
    )
    layer_out = restore(layer_out)
    d_w_out = lax.psum_scatter(d_w_out, "z", scatter_dimension=0)
    d_projected = ff_backward(d_branch, w_out_part, kept)
    d_w_in = dot_rows(first_all, d_projected).astype(BF16)
    d_w_in, d_projected = lax.optimization_barrier((d_w_in, d_projected))
    d_w_in = scatter(d_w_in)
    d_attn, d_pre_one, sums_one = fold_back(d_projected, w_in_part, d_pre_two, normal_one, inverse_one, gains)
    d_attn, d_w_out = lax.optimization_barrier((d_attn, d_w_out))
    d_context = dot_cols(d_attn, w_dense_part).astype(BF16)
    d_packed = attend_back(prefix, qkv, d_context, cosine, sine)
    d_w_qkv = dot_rows(x_all, d_packed).astype(BF16)
    d_dense = dot_rows(context, d_attn).astype(BF16).reshape(zs, piece, group, width)
    d_dense = jnp.swapaxes(d_dense, 1, 2).reshape(D, width)
    d_w_qkv = jnp.concatenate([d_w_qkv, d_dense], axis=1)
    sums = jnp.concatenate([sums_one[:2], sums_two[:2], jnp.zeros((4, D), F32)])
    d_packed, d_w_qkv, d_w_in, sums = lax.optimization_barrier((d_packed, d_w_qkv, d_w_in, sums))
    d_w_qkv = scatter(d_w_qkv)
    d_w_in, d_w_out = d_w_in.reshape(group, piece, 2 * tile), d_w_out.T.reshape(group, piece, tile)
    d_input, d_w_in, d_w_out, sums = fold_last(
        d_packed, w_qkv_part, d_pre_one, gains, [d_w_in, d_w_out, sums], ("swap", "swap", "group")
    )
    sums = jnp.sum(sums, axis=0).reshape(8, zs, group, piece)
    sums = lax.dynamic_index_in_dim(sums, lax.axis_index(GROUP), 2, keepdims=False).reshape(8, width)
    out_in, out_out = join_ff(d_w_in, d_w_out, ff)
    out_in, out_out, d_input, d_w_qkv, sums = lax.optimization_barrier((out_in, out_out, d_input, d_w_qkv, sums))
    if own:
        out_qkv, out_dense, sums = closing(zs, sums, d_w_qkv.reshape(group, piece, 4 * width))
    else:
        out_dense = d_w_qkv[:, 3 * width :].reshape(group, piece, width)
        out_dense = jnp.swapaxes(out_dense, 0, 1).reshape(piece, D).astype(F32)
        d_w_qkv = d_w_qkv[:, : 3 * width].reshape(group, piece, 3 * width)
        d_w_qkv, sums = swap(5, [d_w_qkv, sums], ("swap", "line"))
        out_qkv = jnp.transpose(d_w_qkv.astype(F32).reshape(group, piece, 3, width), (1, 2, 0, 3))
        out_qkv = out_qkv.reshape(piece, 3 * D)
        sums = jnp.sum(sums, axis=0).reshape(8, zs, piece)
        sums = lax.dynamic_index_in_dim(sums, lax.axis_index("z"), 1, keepdims=False)
    return layer_out, d_input, out_qkv, out_dense, out_in, out_out, sums[0], sums[1], sums[2], sums[3]


def solution(mesh):
    grp, shard = mesh.shape["grp"], mesh.shape["shard"]
    sizes = (grp // 4, 2, 2, shard)
    inner = Mesh(mesh.devices.reshape(sizes), ALL)
    rows, flat = P(ALL, None), P(ALL)
    return jax.shard_map(
        functools.partial(on_device, sizes),
        mesh=inner,
        in_specs=(rows,) * 6 + (flat,) * 7,
        out_specs=(rows,) * 6 + (flat,) * 4,
        check_vma=False,
    )
```

```python
import functools

import jax
import jax.numpy as jnp
from jax import lax
from jax.experimental import pallas as pl
from jax.experimental.pallas import tpu as pltpu
from jax.sharding import Mesh
from jax.sharding import PartitionSpec as P

HEADS = 16
HEAD = 128
SEQ_LEN = 224
D = HEADS * HEAD
deep_alpha = 6.928203230275509
norm_eps = 1e-05
far_below = -1e30
scale = HEAD ** (-0.5)

ALL = ("gy", "gx", "core", "z")
GROUP = ("gy", "gx", "core")
MESH = pl.DeviceIdType.MESH
F32 = jnp.float32
BF16 = jnp.bfloat16


def dot(left, right):
    return jnp.dot(left, right, preferred_element_type=F32)


def dot_rows(left, right):
    return lax.dot_general(left, right, (((0,), (0,)), ((), ())), preferred_element_type=F32)


def dot_cols(left, right):
    return lax.dot_general(left, right, (((1,), (1,)), ((), ())), preferred_element_type=F32)


def swap_halves(block):
    lane = lax.broadcasted_iota(jnp.int32, block.shape, 1)
    return jnp.where((lane & 32) == 0, pltpu.roll(block, 96, 1), pltpu.roll(block, 32, 1))


def seen(prefix):
    row = lax.broadcasted_iota(jnp.int32, (SEQ_LEN, SEQ_LEN), 0)
    col = lax.broadcasted_iota(jnp.int32, (SEQ_LEN, SEQ_LEN), 1)
    return (col < prefix) | (col <= row)


def softmax(queries, keys, visible):
    scores = jnp.where(visible, dot_cols(queries, keys), far_below)
    weights = jnp.exp(scores - jnp.max(scores, axis=1, keepdims=True))
    return weights / jnp.sum(weights, axis=1, keepdims=True)


def attend_kernel(prefix_ref, packed_ref, cos_ref, sin_ref, qkv_ref, context_ref):
    width = context_ref.shape[1]
    visible = seen(prefix_ref[pl.program_id(0)])
    cosine = cos_ref[0]
    sine = sin_ref[0]
    for head in range(width // HEAD):
        at = pl.ds(head * HEAD, HEAD)
        at_k = pl.ds(width + head * HEAD, HEAD)
        at_v = pl.ds(2 * width + head * HEAD, HEAD)
        raw = packed_ref[:, at]
        queries = ((raw * cosine + swap_halves(raw) * sine) * scale).astype(BF16)
        raw = packed_ref[:, at_k]
        keys = (raw * cosine + swap_halves(raw) * sine).astype(BF16)
        values = packed_ref[:, at_v].astype(BF16)
        qkv_ref[:, at] = queries
        qkv_ref[:, at_k] = keys
        qkv_ref[:, at_v] = values
        probs = softmax(queries, keys, visible).astype(BF16)
        context_ref[:, at] = dot(probs, values).astype(BF16)


def attend_back_kernel(prefix_ref, qkv_ref, d_context_ref, cos_ref, sin_ref, d_packed_ref):
    width = d_context_ref.shape[1]
    visible = seen(prefix_ref[pl.program_id(0)])
    cosine = cos_ref[0]
    sine = sin_ref[0]
    for head in range(width // HEAD):
        at = pl.ds(head * HEAD, HEAD)
        at_k = pl.ds(width + head * HEAD, HEAD)
        at_v = pl.ds(2 * width + head * HEAD, HEAD)
        queries = qkv_ref[:, at]
        keys = qkv_ref[:, at_k]
        values = qkv_ref[:, at_v]
        d_context = d_context_ref[:, at]
        probs = softmax(queries, keys, visible)
        d_packed_ref[:, at_v] = dot_rows(probs.astype(BF16), d_context).astype(BF16)
        d_probs = dot_cols(d_context, values)
        inner = jnp.sum(probs * d_probs, axis=1, keepdims=True)
        d_scores = (probs * (d_probs - inner)).astype(BF16)
        grad = dot(d_scores, keys) * scale
        d_packed_ref[:, at] = (grad * cosine - swap_halves(grad) * sine).astype(BF16)
        grad = dot_rows(d_scores, queries)
        d_packed_ref[:, at_k] = (grad * cosine - swap_halves(grad) * sine).astype(BF16)


def by_sequence(width):
    return pl.BlockSpec((SEQ_LEN, width), lambda s: (s, 0))


TABLE = pl.BlockSpec((1, SEQ_LEN, HEAD), lambda s: (s, 0, 0))
SCALARS = pl.BlockSpec(memory_space=pltpu.SMEM)
PARAMS = pltpu.CompilerParams(vmem_limit_bytes=56 * 2**20)


def attend(prefix, packed, cosine, sine):
    rows, width = packed.shape[0], packed.shape[1] // 3
    return pl.pallas_call(
        attend_kernel,
        grid=(rows // SEQ_LEN,),
        in_specs=[SCALARS, by_sequence(3 * width), TABLE, TABLE],
        out_specs=[by_sequence(3 * width), by_sequence(width)],
        out_shape=[
            jax.ShapeDtypeStruct((rows, 3 * width), BF16),
            jax.ShapeDtypeStruct((rows, width), BF16),
        ],
        compiler_params=PARAMS,
    )(prefix, packed, cosine, sine)


def attend_back(prefix, qkv, d_context, cosine, sine):
    rows, width = d_context.shape
    return pl.pallas_call(
        attend_back_kernel,
        grid=(rows // SEQ_LEN,),
        in_specs=[SCALARS, by_sequence(3 * width), by_sequence(width), TABLE, TABLE],
        out_specs=by_sequence(3 * width),
        out_shape=jax.ShapeDtypeStruct((rows, 3 * width), BF16),
        compiler_params=PARAMS,
    )(prefix, qkv, d_context, cosine, sine)


def tables(prefix, start):
    place = jnp.arange(SEQ_LEN, dtype=jnp.int32)
    in_span = place[None, :] >= prefix[:, None]
    pos_one = jnp.where(in_span, start[:, None], place[None, :])
    pos_two = jnp.where(in_span, place[None, :] - prefix[:, None] + 1, 0)
    lane = jnp.arange(HEAD)
    freqs = 10000.0 ** (-2.0 * (lane % 32).astype(F32) / 64)
    place_of = jnp.where(lane[None, None, :] < 64, pos_one[:, :, None], pos_two[:, :, None])
    angles = place_of.astype(F32) * freqs
    sign = jnp.where(lane % 64 < 32, -1.0, 1.0)
    return jnp.cos(angles), jnp.sin(angles) * sign


def norm_parts(values):
    center = values - jnp.mean(values, axis=-1, keepdims=True)
    inverse = lax.rsqrt(jnp.mean(center * center, axis=-1, keepdims=True) + norm_eps)
    return center * inverse, inverse


def norm_back(normal, inverse, gain, grad):
    scaled = gain * grad
    return inverse * (
        scaled
        - jnp.mean(scaled, axis=-1, keepdims=True)
        - normal * jnp.mean(scaled * normal, axis=-1, keepdims=True)
    )


def gate_parts(gate):
    phi = 0.5 * (1.0 + lax.erf(gate * 0.7071067811865476))
    slope = phi + gate * jnp.exp(-0.5 * gate * gate) * 0.3989422804014327
    return gate * phi, slope


def here():
    return lax.axis_index("gy"), lax.axis_index("gx"), lax.axis_index("core")


def place(y, x, c):
    return (y * 2 + x) * 2 + c


def greet(peers):
    barrier = pltpu.get_barrier_semaphore()
    for peer in peers:
        pl.semaphore_signal(barrier, inc=1, device_id=peer, device_id_type=MESH)
    pl.semaphore_wait(barrier, len(peers))


def spread_block(cut, base, block_ref, out_ref, send, recv, local):
    rows = block_ref.shape[0]
    y, x, c = here()
    to_x, to_y, to_c = {"gx": 1 - x}, {"gy": 1 - y}, {"core": 1 - c}
    me, by_x, by_y, far = place(y, x, c), place(y, 1 - x, c), place(1 - y, x, c), place(1 - y, 1 - x, c)
    low, high = pl.ds(0, cut), pl.ds(cut, rows - cut)

    def push(k, src, dst, to):
        copy = pltpu.make_async_remote_copy(
            src_ref=src, dst_ref=dst, send_sem=send.at[base + k], recv_sem=recv.at[base + k], device_id=to, device_id_type=MESH
        )
        copy.start()
        return copy

    def landed(k, dst):
        pltpu.make_async_remote_copy(
            src_ref=dst, dst_ref=dst, send_sem=send.at[base + k], recv_sem=recv.at[base + k], device_id=to_c, device_id_type=MESH
        ).wait_recv()

    sent = [
        push(0, block_ref.at[low], out_ref.at[me, low], to_x),
        push(1, block_ref.at[high], out_ref.at[me, high], to_y),
        push(2, block_ref.at[high], out_ref.at[me, high], to_x),
        push(3, block_ref.at[low], out_ref.at[me, low], to_y),
        push(4, block_ref, out_ref.at[me], to_c),
    ]
    keep = pltpu.make_async_copy(block_ref, out_ref.at[me], local)
    keep.start()
    landed(0, out_ref.at[by_x, low])
    sent.append(push(5, out_ref.at[by_x, low], out_ref.at[by_x, low], to_y))
    sent.append(push(7, out_ref.at[by_x, low], out_ref.at[by_x, low], to_c))
    landed(1, out_ref.at[by_y, high])
    sent.append(push(6, out_ref.at[by_y, high], out_ref.at[by_y, high], to_x))
    sent.append(push(8, out_ref.at[by_y, high], out_ref.at[by_y, high], to_c))
    landed(2, out_ref.at[by_x, high])
    sent.append(push(9, out_ref.at[by_x, high], out_ref.at[by_x, high], to_c))
    landed(3, out_ref.at[by_y, low])
    sent.append(push(10, out_ref.at[by_y, low], out_ref.at[by_y, low], to_c))
    landed(5, out_ref.at[far, low])
    sent.append(push(11, out_ref.at[far, low], out_ref.at[far, low], to_c))
    landed(6, out_ref.at[far, high])
    sent.append(push(12, out_ref.at[far, high], out_ref.at[far, high], to_c))
    other, other_x, other_y, other_far = (
        place(y, x, 1 - c),
        place(y, 1 - x, 1 - c),
        place(1 - y, x, 1 - c),
        place(1 - y, 1 - x, 1 - c),
    )
    landed(4, out_ref.at[other])
    landed(7, out_ref.at[other_x, low])
    landed(8, out_ref.at[other_y, high])
    landed(9, out_ref.at[other_x, high])
    landed(10, out_ref.at[other_y, low])
    landed(11, out_ref.at[other_far, low])
    landed(12, out_ref.at[other_far, high])
    keep.wait()
    for copy in sent:
        copy.wait_send()


ANY = pl.BlockSpec(memory_space=pl.ANY)


def swap_peers(zs, kinds):
    y, x, c = here()
    z = lax.axis_index("z")
    found = []
    for k in range(1, 8):
        peer = ((y + k // 4) % 2, (x + k // 2 % 2) % 2, (c + k % 2) % 2)
        found.append((place(*peer), {"gy": peer[0], "gx": peer[1], "core": peer[2]}))
    if "line" in kinds:
        found += [((z + k) % zs, {"z": (z + k) % zs}) for k in range(1, zs)]
    return found


def swap_begin(zs, kinds, blocks, outs, send, recv, local):
    copies, comes, keeps = [], [], []
    found = swap_peers(zs, kinds)
    for i, kind in enumerate(kinds):
        me = lax.axis_index("z") if kind == "line" else place(*here())
        for k, (peer, name) in enumerate(found[7:] if kind == "line" else found[:7]):
            src = blocks[i].at[peer] if kind == "swap" else blocks[i]
            landing = outs[i].at[peer]
            sems = dict(send_sem=send.at[i, k], recv_sem=recv.at[i, k], device_id=name, device_id_type=MESH)
            copies.append(pltpu.make_async_remote_copy(src_ref=src, dst_ref=outs[i].at[me], **sems))
            comes.append(pltpu.make_async_remote_copy(src_ref=landing, dst_ref=landing, **sems))
            copies[-1].start()
        own = blocks[i].at[me] if kind == "swap" else blocks[i]
        keeps.append(pltpu.make_async_copy(own, outs[i].at[me], local.at[i]))
        keeps[-1].start()

    def finish():
        for come in comes:
            come.wait_recv()
        for copy in copies:
            copy.wait_send()
        for keep in keeps:
            keep.wait()

    return finish


SWAP_LEAD = {"swap": lambda zs: (), "group": lambda zs: (8,), "line": lambda zs: (zs,)}


def swap_shapes(zs, arrays, kinds):
    return [jax.ShapeDtypeStruct(SWAP_LEAD[k](zs) + a.shape, a.dtype) for a, k in zip(arrays, kinds)]


def swap_scratch(zs, kinds):
    n, most = len(kinds), max(7, zs - 1)
    return [
        pltpu.SemaphoreType.DMA((n, most)),
        pltpu.SemaphoreType.DMA((n, most)),
        pltpu.SemaphoreType.DMA((n,)),
    ]


SLAB = 16
ROWS = pl.BlockSpec(memory_space=pltpu.VMEM)
CHIP_COLS = 256


def by_rows(value, zs, piece):
    group = D // (zs * piece)
    order = [g * zs + z for z in range(zs) for g in range(group)]
    return jnp.concatenate([value[:, m * piece : (m + 1) * piece] for m in order], axis=1)


def in_order(value, zs, piece):
    group = D // (zs * piece)
    order = [z * group + g for g in range(group) for z in range(zs)]
    return jnp.concatenate([value[:, m * piece : (m + 1) * piece] for m in order], axis=1)


def first_norm(values, gains):
    normal, inverse = norm_parts(values)
    first = normal * gains[0:1] + gains[1:2]
    return first, normal, inverse


def second_norm(total, first, grad, gains):
    normal, inverse = norm_parts(deep_alpha * first + total)
    return normal * gains[2:3] + gains[3:4], norm_back(normal, inverse, gains[2:3], grad), grad * normal


def first_back(total, d_pre_two, normal, inverse, gains):
    d_first = deep_alpha * d_pre_two + total
    return norm_back(normal, inverse, gains[0:1], d_first), d_first * normal, d_first


def fold_kernel(mode, across, zs, piece, n_aux, n_out, kinds, *refs):
    left_ref, right_ref, gains_ref = refs[:3]
    aux_refs = refs[3 : 3 + n_aux]
    refs = refs[3 + n_aux :]
    n_swap = len(kinds)
    swap_in, refs = refs[:n_swap], refs[n_swap:]
    spread = mode != "last"
    if spread:
        all_ref, refs = refs[0], refs[1:]
    outs, refs = refs[:n_out], refs[n_out:]
    swap_out, refs = refs[:n_swap], refs[n_swap:]
    aux, refs = refs[:n_aux], refs[n_aux:]
    left, right, part, got, near_x, near_y, from_x, from_y, block, acc, send, recv, local = refs[:13]
    rows, width = block.shape
    cut = near_x.shape[0]
    y, x, c = here()
    to_x, to_y, to_c = {"gx": 1 - x}, {"gy": 1 - y}, {"core": 1 - c}
    chips = [(1 - y, 1 - x), (y, 1 - x), (1 - y, x), (y, x)]
    low, high = pl.ds(0, cut), pl.ds(cut, rows - cut)

    def push(k, src, dst, to):
        copy = pltpu.make_async_remote_copy(
            src_ref=src, dst_ref=dst, send_sem=send.at[k], recv_sem=recv.at[k], device_id=to, device_id_type=MESH
        )
        copy.start()
        return copy

    def add(k, extra, start, size, offset=0):
        @pl.loop(0, size // SLAB)
        def _(step):
            at = pl.ds(pl.multiple_of(start + step * SLAB, SLAB), SLAB)
            of = pl.ds(pl.multiple_of(start - offset + step * SLAB, SLAB), SLAB)
            part[k, c, at] = (part[k, c, at].astype(F32) + extra[of].astype(F32)).astype(BF16)

    loads = [pltpu.make_async_copy(left_ref.at[a * 2 + b], left.at[k], local.at[k]) for k, (a, b) in enumerate(chips)]
    load_right = pltpu.make_async_copy(right_ref, right, local.at[4])
    load_aux = [pltpu.make_async_copy(r, v, local.at[5 + k]) for k, (r, v) in enumerate(zip(aux_refs, aux))]
    loads[0].start()
    load_right.start()
    for load in loads[1:] + load_aux:
        load.start()
    if n_swap:
        greet([name for _, name in swap_peers(1, kinds)])
        swap_finish = swap_begin(1, kinds, swap_in, swap_out, *refs[13:])
    else:
        greet([to_x, to_y, to_c])

    def product(k):
        loads[k].wait()

        @pl.loop(0, width // CHIP_COLS)
        def _(step):
            at = pl.ds(pl.multiple_of(step * CHIP_COLS, CHIP_COLS), CHIP_COLS)
            here_part = dot_cols(left[k], right[at]) if across else dot(left[k], right[:, at])
            part[k, 0, :, at] = here_part[:rows].astype(BF16)
            part[k, 1, :, at] = here_part[rows:].astype(BF16)

        return push(k, part.at[k, 1 - c], got.at[k], to_c)

    load_right.wait()
    sent = [product(0), product(1)]
    sent[0].wait_recv()
    add(0, got.at[0], 0, rows)
    far_x = push(4, part.at[0, c, low], near_x, to_x)
    far_y = push(5, part.at[0, c, high], near_y, to_y)
    sent.append(product(2))
    sent[1].wait_recv()
    add(1, got.at[1], 0, rows)
    plain_x = push(6, part.at[1, c, low], from_x.at[low], to_x)
    sent[2].wait_recv()
    add(2, got.at[2], 0, rows)
    plain_y = push(7, part.at[2, c, high], from_y.at[high], to_y)
    sent.append(product(3))
    far_y.wait_recv()
    add(1, near_y, cut, rows - cut, cut)
    more_x = push(8, part.at[1, c, high], from_x.at[high], to_x)
    far_x.wait_recv()
    add(2, near_x, 0, cut)
    more_y = push(9, part.at[2, c, low], from_y.at[low], to_y)
    sent[3].wait_recv()
    for load in load_aux:
        load.wait()
    plain_x.wait_recv()
    plain_y.wait_recv()
    more_x.wait_recv()
    more_y.wait_recv()
    gains = gains_ref[...]
    acc[...] = jnp.zeros_like(acc)

    @pl.loop(0, rows // SLAB)
    def _(step):
        at = pl.ds(pl.multiple_of(step * SLAB, SLAB), SLAB)
        total = part[3, c, at].astype(F32) + got[3, at].astype(F32) + from_x[at].astype(F32) + from_y[at].astype(F32)
        held = [a[at].astype(F32) for a in aux]
        if mode == "one":
            first, normal, inverse = first_norm(by_rows(deep_alpha * held[0] + total, zs, piece), gains)
            outs[0][at] = first
            outs[1][at] = normal
            outs[2][at] = jnp.broadcast_to(inverse, (SLAB, 128))
            block[at] = first.astype(BF16)
        elif mode == "back":
            d_pre, terms, d_first = first_back(total, held[0], held[1], held[2][:, 0:1], gains)
            outs[0][at] = d_pre
            block[at] = in_order(d_pre, zs, piece).astype(BF16)
            acc[0] += terms
            acc[1] += d_first
        else:
            outs[0][at] = in_order(deep_alpha * held[0] + total, zs, piece).astype(BF16)

    if mode == "back":
        outs[-1][0:1] = jnp.sum(acc[0], axis=0, keepdims=True)
        outs[-1][1:2] = jnp.sum(acc[1], axis=0, keepdims=True)
    for copy in sent + [far_x, far_y, plain_x, plain_y, more_x, more_y]:
        copy.wait_send()
    if n_swap:
        swap_finish()
    if spread:
        spread_block(cut, 10, block, all_ref, send, recv, local.at[4])


def group_fold(name, zs, mode, left, right, gains, aux, out_types, extras=(), kinds=()):
    across = mode != "one"
    rows, depth = left.shape[0] // 8, left.shape[1]
    width = gains.shape[1]
    cut = rows // 2
    spread = mode != "last"
    out_shape = [jax.ShapeDtypeStruct((8, rows, width), BF16)] * spread + out_types
    n, n_swap = len(aux), len(extras)
    n_sems = 23 if spread else 10
    return pl.pallas_call(
        functools.partial(fold_kernel, mode, across, zs, width // (8 * zs), n, len(out_types), kinds),
        out_shape=out_shape + swap_shapes(1, extras, kinds),
        in_specs=[ANY, ANY, ROWS] + [ANY] * (n + n_swap),
        out_specs=[ANY] * spread + [ROWS] * len(out_types) + [ANY] * n_swap,
        scratch_shapes=[pltpu.VMEM(a.shape, a.dtype) for a in aux]
        + [
            pltpu.VMEM((4, 2 * rows, depth), BF16),
            pltpu.VMEM(right.shape, BF16),
            pltpu.VMEM((4, 2, rows, width), BF16),
            pltpu.VMEM((4, rows, width), BF16),
            pltpu.VMEM((cut, width), BF16),
            pltpu.VMEM((rows - cut, width), BF16),
            pltpu.VMEM((rows, width), BF16),
            pltpu.VMEM((rows, width), BF16),
            pltpu.VMEM((rows, width), BF16),
            pltpu.VMEM((2, SLAB, width), F32),
            pltpu.SemaphoreType.DMA((n_sems,)),
            pltpu.SemaphoreType.DMA((n_sems,)),
            pltpu.SemaphoreType.DMA((5 + n,)),
        ]
        + (swap_scratch(1, kinds) if n_swap else []),
        compiler_params=pltpu.CompilerParams(
            collective_id=name, has_side_effects=True, vmem_limit_bytes=50 * 2**20
        ),
        cost_estimate=pl.CostEstimate(flops=0, bytes_accessed=(200 if spread else 110) * 2**20, transcendentals=0),
    )(left.reshape(4, 2 * rows, depth), right, gains, *aux, *extras)


def turn_kernel(
    zs, piece, x_ref, in_ref, out_ref, gains_ref, first_ref, grad_ref,
    all_ref, kept_ref, right_ref, result_ref, d_pre_ref, sums_ref, dw_ref,
    first, grad, w_in, kept, left, right, part, got, near_x, near_y, from_x, from_y, whole, dw, acc,
    fold_send, fold_recv, all_send, all_recv, line_send, line_recv, local, x_local
):
    rows = first.shape[0]
    tile = left.shape[2]
    wide = right.shape[2]
    y, x, c = here()
    z = lax.axis_index("z")
    to_x, to_y, to_c = {"gx": 1 - x}, {"gy": 1 - y}, {"core": 1 - c}
    chips = [(1 - y) * 2 + 1 - x, y * 2 + 1 - x, (1 - y) * 2 + x, y * 2 + x]
    me, by_x, by_y, far = place(y, x, c), place(y, 1 - x, c), place(1 - y, x, c), place(1 - y, 1 - x, c)
    other, other_x, other_y, other_far = (
        place(y, x, 1 - c),
        place(y, 1 - x, 1 - c),
        place(1 - y, x, 1 - c),
        place(1 - y, 1 - x, 1 - c),
    )
    half = rows // 2
    most = -(-half // (2 * SLAB)) * SLAB
    lows = [(0, most), (half, half - most)]
    highs = [(most, half - most), (2 * half - most, most)]
    top, bottom = pl.ds(0, half), pl.ds(half, half)
    sent = []

    def remote(sems, k, src, dst, to):
        return pltpu.make_async_remote_copy(
            src_ref=src,
            dst_ref=dst,
            send_sem=sems[0].at[k],
            recv_sem=sems[1].at[k],
            device_id=to,
            device_id_type=MESH,
        )

    def push(sems, k, src, dst, to):
        copy = remote(sems, k, src, dst, to)
        copy.start()
        sent.append(copy)

    def landed(sems, k, dst):
        remote(sems, k, dst, dst, to_c).wait_recv()

    folds, alls, lines = (fold_send, fold_recv), (all_send, all_recv), (line_send, line_recv)

    load_out = pltpu.make_async_copy(out_ref, right.at[z], local.at[0])
    load_in = pltpu.make_async_copy(in_ref, w_in, local.at[1])
    load_first = pltpu.make_async_copy(first_ref, first, local.at[2])
    load_grad = pltpu.make_async_copy(grad_ref, grad, local.at[3])

    def load_x(g):
        return pltpu.make_async_copy(x_ref.at[g], whole.at[g], x_local.at[g])

    load_out.start()

    barrier = pltpu.get_barrier_semaphore()
    for to in (to_x, to_y, to_c):
        pl.semaphore_signal(barrier, inc=1, device_id=to, device_id_type=MESH)

    @pl.when(z > 0)
    def _():
        pl.semaphore_signal(barrier, inc=1, device_id={"z": z - 1}, device_id_type=MESH)

    @pl.when(z < zs - 1)
    def _():
        pl.semaphore_signal(barrier, inc=1, device_id={"z": z + 1}, device_id_type=MESH)

    inside = (z > 0) & (z < zs - 1)

    @pl.when(inside)
    def _():
        pl.semaphore_wait(barrier, 5)

    @pl.when(jnp.logical_not(inside))
    def _():
        pl.semaphore_wait(barrier, 4)

    def shard_of(step, up):
        return z - step if up else z + step

    def hop(step, up):
        ref = right.at[shard_of(step, up)]
        return remote(lines, 2 * step + (0 if up else 1), ref, ref, {"z": z + 1 if up else z - 1})

    def sends(step, up):
        return (z >= step) & (z < zs - 1) if up else (z <= zs - 1 - step) & (z > 0)

    def gets(step, up):
        return z >= step + 1 if up else z <= zs - 2 - step

    def line_serve(step):
        for up in (True, False):

            @pl.when(gets(step - 1, up) & sends(step, up))
            def _(up=up):
                landed(lines, 2 * (step - 1) + (0 if up else 1), right.at[shard_of(step, up)])
                hop(step, up).start()

    def line_take(step):
        for up in (True, False):

            @pl.when(gets(step - 1, up) & jnp.logical_not(sends(step, up)))
            def _(up=up):
                landed(lines, 2 * (step - 1) + (0 if up else 1), right.at[shard_of(step, up)])

    load_out.wait()
    for up in (True, False):

        @pl.when(sends(0, up))
        def _(up=up):
            hop(0, up).start()

    load_in.start()
    for g in range(8):
        load_x(g).start()


    load_in.wait()

    @pl.loop(0, 8)
    def _(g):
        @pl.when(g == 6)
        def _():
            line_serve(1)

        load_x(g).wait()
        projected = dot(whole[g], w_in[...])
        gate, up = projected[:, :tile], projected[:, tile:]
        act, slope = gate_parts(gate)
        left[g] = (act * up).astype(BF16)
        kept[g] = jnp.concatenate([up * slope, act], axis=1).astype(BF16)

    load_first.start()
    load_grad.start()
    keep = pltpu.make_async_copy(kept, kept_ref, local.at[4])
    keep.start()

    def add(k, extra, start, offset, at):
        @pl.loop(0, half // SLAB)
        def _(step):
            row = pl.ds(pl.multiple_of(start + step * SLAB, SLAB), SLAB)
            of = pl.ds(pl.multiple_of(start - offset + step * SLAB, SLAB), SLAB)
            part[k, c, row, at] = (part[k, c, row, at].astype(F32) + extra[of, at].astype(F32)).astype(BF16)

    def chip_sum(k, at):
        add(k, got.at[k], 0, 0, at)
        add(k, got.at[k], half, 0, at)

    def product(k, block, at):
        found = dot(left[pl.ds(2 * chips[k], 2)].reshape(2 * rows, tile), right[block])
        part[k, 0, :, at] = found[:rows].astype(BF16)
        part[k, 1, :, at] = found[rows:].astype(BF16)

    def block_at(i):
        if i == 0:
            return z
        below = z < zs // 2
        near = jnp.where(below, z, zs - 1 - z)
        spot = jnp.where(i <= 2 * near, jnp.where(i % 2 == 1, near - (i + 1) // 2, near + i // 2), i)
        return jnp.where(below, spot, zs - 1 - spot)

    def block_cols(i):
        return pl.ds(pl.multiple_of(block_at(i) * wide, wide), wide)

    def fold_start(i):
        b, block, at = 8 * i, block_at(i), block_cols(i)
        rest = pl.ds(1, 3)
        product(0, block, at)
        push(folds, b, part.at[0, 1 - c, :, at], got.at[0, :, at], to_c)
        for k in (1, 2, 3):
            product(k, block, at)
        push(folds, b + 1, part.at[rest, 1 - c, :, at], got.at[rest, :, at], to_c)
        landed(folds, b, got.at[0, :, at])
        chip_sum(0, at)
        push(folds, b + 2, part.at[0, c, top, at], near_x.at[:, at], to_x)
        push(folds, b + 3, part.at[0, c, bottom, at], near_y.at[:, at], to_y)
        landed(folds, b + 1, got.at[rest, :, at])
        chip_sum(1, at)
        push(folds, b + 4, part.at[1, c, top, at], from_x.at[top, at], to_x)
        chip_sum(2, at)
        push(folds, b + 5, part.at[2, c, bottom, at], from_y.at[bottom, at], to_y)

    def fold_end(i):
        b, at = 8 * i, block_cols(i)
        landed(folds, b + 3, near_y.at[:, at])
        add(1, near_y, half, half, at)
        push(folds, b + 6, part.at[1, c, bottom, at], from_x.at[bottom, at], to_x)
        landed(folds, b + 2, near_x.at[:, at])
        add(2, near_x, 0, 0, at)
        push(folds, b + 7, part.at[2, c, top, at], from_y.at[top, at], to_y)

    gains = gains_ref[...]
    line_take(1)
    fold_start(0)
    fold_start(1)
    fold_end(0)
    for i in range(2, zs):
        if i < zs - 1:
            line_serve(i)
        fold_end(i - 1)
        line_take(i)
        fold_start(i)
    fold_end(zs - 1)
    carry = pltpu.make_async_copy(right, right_ref, local.at[5])
    carry.start()
    load_first.wait()
    load_grad.wait()
    acc[...] = jnp.zeros_like(acc)
    for i in range(zs):
        at = block_cols(i)
        landed(folds, 8 * i + 4, from_x.at[top, at])
        landed(folds, 8 * i + 5, from_y.at[bottom, at])
        landed(folds, 8 * i + 6, from_x.at[bottom, at])
        landed(folds, 8 * i + 7, from_y.at[top, at])

    def low(i):
        return pl.ds(*lows[i])

    def high(i):
        return pl.ds(*highs[i])

    def span(i):
        return pl.ds(i * half, half)

    def norm(i):
        @pl.loop(0, half // SLAB)
        def _(step):
            at = pl.ds(pl.multiple_of(i * half + step * SLAB, SLAB), SLAB)
            total = part[3, c, at].astype(F32) + got[3, at].astype(F32)
            total += from_x[at].astype(F32) + from_y[at].astype(F32)
            dy = grad[at].astype(F32)
            result, d_pre, terms = second_norm(total, first[at], dy, gains)
            result_ref[at] = result.astype(BF16)
            d_pre_ref[at] = d_pre
            whole[me, at] = d_pre.astype(BF16)
            acc[0] += terms
            acc[1] += dy

        b = 13 * i
        push(alls, b, whole.at[me, low(i)], whole.at[me, low(i)], to_x)
        push(alls, b + 1, whole.at[me, high(i)], whole.at[me, high(i)], to_y)
        push(alls, b + 2, whole.at[me, high(i)], whole.at[me, high(i)], to_x)
        push(alls, b + 3, whole.at[me, low(i)], whole.at[me, low(i)], to_y)
        push(alls, b + 4, whole.at[me, span(i)], whole.at[me, span(i)], to_c)

    def pass_on(i, k, slot, at, onward):
        ref = whole.at[slot, at]
        landed(alls, 13 * i + k, ref)
        for where, to in onward:
            push(alls, 13 * i + where, ref, ref, to)

    def spread_first(i):
        pass_on(i, 0, by_x, low(i), [(5, to_y), (7, to_c)])
        pass_on(i, 1, by_y, high(i), [(6, to_x), (8, to_c)])

    def spread_rest(i):
        pass_on(i, 2, by_x, high(i), [(9, to_c)])
        pass_on(i, 3, by_y, low(i), [(10, to_c)])

    def spread_far(i):
        pass_on(i, 5, far, low(i), [(11, to_c)])
        pass_on(i, 6, far, high(i), [(12, to_c)])

    outward = []

    def gradient(k, last=False, first_one=False):
        pair = pl.ds(2 * chips[k], 2)
        outward.append(pltpu.make_async_copy(whole.at[pair], all_ref.at[pair], local.at[6 + k]))
        outward[-1].start()

        @pl.loop(0, zs)
        def _(block):
            at = pl.ds(pl.multiple_of(block * wide, wide), wide)
            found = dot_rows(left[pair].reshape(2 * rows, tile), whole[pair, :, at].reshape(2 * rows, wide))
            if first_one:
                dw[block] = found
            elif last:
                dw_ref[block] = (dw[block] + found).astype(BF16)
            else:
                dw[block] += found

    norm(0)
    norm(1)
    spread_first(0)
    for i in (0, 1):
        landed(alls, 13 * i + 4, whole.at[other, span(i)])
    gradient(3, first_one=True)
    spread_rest(0)
    spread_first(1)
    spread_rest(1)
    for i in (0, 1):
        landed(alls, 13 * i + 7, whole.at[other_x, low(i)])
        landed(alls, 13 * i + 9, whole.at[other_x, high(i)])
    gradient(1)
    spread_far(0)
    for i in (0, 1):
        landed(alls, 13 * i + 8, whole.at[other_y, high(i)])
        landed(alls, 13 * i + 10, whole.at[other_y, low(i)])
    gradient(2)
    sums_ref[0:1] = jnp.sum(acc[0], axis=0, keepdims=True)
    sums_ref[1:2] = jnp.sum(acc[1], axis=0, keepdims=True)
    spread_far(1)
    for i in (0, 1):
        landed(alls, 13 * i + 11, whole.at[other_far, low(i)])
        landed(alls, 13 * i + 12, whole.at[other_far, high(i)])
    gradient(0, last=True)
    for copy in outward + [keep, carry]:
        copy.wait()
    for copy in sent:
        copy.wait_send()
    for step in range(zs - 1):
        for up in (True, False):

            @pl.when(sends(step, up))
            def _(step=step, up=up):
                hop(step, up).wait_send()


def turn(zs, x, w_in, w_out, gains, first, grad):
    rows = x.shape[0] // 8
    units, wide = w_out.shape
    width = gains.shape[1]
    half = rows // 2
    by_z = (zs, units, wide)
    return pl.pallas_call(
        functools.partial(turn_kernel, zs, width // (8 * zs)),
        out_shape=[
            jax.ShapeDtypeStruct((8, rows, width), BF16),
            jax.ShapeDtypeStruct((8, rows, 2 * units), BF16),
            jax.ShapeDtypeStruct(by_z, BF16),
            jax.ShapeDtypeStruct((rows, width), BF16),
            jax.ShapeDtypeStruct((rows, width), F32),
            jax.ShapeDtypeStruct((8, width), F32),
            jax.ShapeDtypeStruct(by_z, BF16),
        ],
        in_specs=[ANY, ANY, ANY, ROWS, ANY, ANY],
        out_specs=[ANY] * 3 + [ROWS] * 4,
        scratch_shapes=[
            pltpu.VMEM((rows, width), F32),
            pltpu.VMEM((rows, width), BF16),
            pltpu.VMEM(w_in.shape, BF16),
            pltpu.VMEM((8, rows, 2 * units), BF16),
            pltpu.VMEM((8, rows, units), BF16),
            pltpu.VMEM(by_z, BF16),
            pltpu.VMEM((4, 2, rows, width), BF16),
            pltpu.VMEM((4, rows, width), BF16),
            pltpu.VMEM((half, width), BF16),
            pltpu.VMEM((half, width), BF16),
            pltpu.VMEM((rows, width), BF16),
            pltpu.VMEM((rows, width), BF16),
            pltpu.VMEM((8, rows, width), BF16),
            pltpu.VMEM(by_z, F32),
            pltpu.VMEM((2, SLAB, width), F32),
            pltpu.SemaphoreType.DMA((8 * zs,)),
            pltpu.SemaphoreType.DMA((8 * zs,)),
            pltpu.SemaphoreType.DMA((26,)),
            pltpu.SemaphoreType.DMA((26,)),
            pltpu.SemaphoreType.DMA((2 * (zs - 1),)),
            pltpu.SemaphoreType.DMA((2 * (zs - 1),)),
            pltpu.SemaphoreType.DMA((10,)),
            pltpu.SemaphoreType.DMA((8,)),
        ],
        compiler_params=pltpu.CompilerParams(collective_id=1, has_side_effects=True, vmem_limit_bytes=60 * 2**20),
        cost_estimate=pl.CostEstimate(flops=0, bytes_accessed=380 * 2**20, transcendentals=0),
    )(x.reshape(8, rows, width), w_in, w_out, gains, first, grad)


def swap_kernel(zs, kinds, *refs):
    n = len(kinds)
    greet([name for _, name in swap_peers(zs, kinds)])
    swap_begin(zs, kinds, refs[:n], refs[n : 2 * n], *refs[2 * n :])()


def group_swap(name, zs, arrays, kinds):
    n = len(arrays)
    return pl.pallas_call(
        functools.partial(swap_kernel, zs, kinds),
        out_shape=swap_shapes(zs, arrays, kinds),
        in_specs=[ANY] * n,
        out_specs=[ANY] * n,
        scratch_shapes=swap_scratch(zs, kinds),
        compiler_params=pltpu.CompilerParams(collective_id=name, has_side_effects=True),
        cost_estimate=pl.CostEstimate(flops=0, bytes_accessed=50 * 2**20, transcendentals=0),
    )(*arrays)


def enter_kernel(zs, kinds, x_ref, grad_ref, *refs):
    n = len(kinds)
    blocks, x_all, grad_out, outs, refs = refs[:n], refs[n], refs[n + 1], refs[n + 2 : 2 * n + 2], refs[2 * n + 2 :]
    x_rows, sems = refs[0], refs[1:]
    rows, width = x_ref.shape
    greet([name for _, name in swap_peers(zs, kinds)])
    finish = swap_begin(zs, kinds, blocks, outs, *sems[:3])
    for ref, out in ((x_ref, x_rows), (grad_ref, grad_out)):

        @pl.loop(0, rows // SLAB)
        def _(step, ref=ref, out=out):
            at = pl.ds(pl.multiple_of(step * SLAB, SLAB), SLAB)
            out[at] = by_rows(ref[at].astype(F32), zs, width // (8 * zs)).astype(BF16)

    spread_block(rows // 2, 0, x_rows, x_all, *sems[3:])
    finish()


def enter(zs, x, grad, arrays, kinds):
    n = len(arrays)
    return pl.pallas_call(
        functools.partial(enter_kernel, zs, kinds),
        out_shape=[jax.ShapeDtypeStruct((8,) + x.shape, x.dtype), jax.ShapeDtypeStruct(grad.shape, grad.dtype)]
        + swap_shapes(zs, arrays, kinds),
        in_specs=[ROWS] * 2 + [ANY] * n,
        out_specs=[ANY, ROWS] + [ANY] * n,
        scratch_shapes=[pltpu.VMEM(x.shape, x.dtype)]
        + swap_scratch(zs, kinds)
        + [pltpu.SemaphoreType.DMA((13,)), pltpu.SemaphoreType.DMA((13,)), pltpu.SemaphoreType.DMA],
        compiler_params=pltpu.CompilerParams(collective_id=3, has_side_effects=True, vmem_limit_bytes=56 * 2**20),
        cost_estimate=pl.CostEstimate(flops=0, bytes_accessed=150 * 2**20, transcendentals=0),
    )(x, grad, *arrays)


def ff_kernel(x_ref, w_ref, hidden_ref, kept_ref):
    tile = hidden_ref.shape[1]
    projected = dot(x_ref[...], w_ref[...])
    gate, up = projected[:, :tile], projected[:, tile:]
    act, slope = gate_parts(gate)
    hidden_ref[...] = (act * up).astype(BF16)
    kept_ref[...] = jnp.concatenate([up * slope, act], axis=1).astype(BF16)


def ff_back_kernel(grad_ref, w_ref, kept_ref, out_ref):
    zs, _, wide = w_ref.shape
    d_hidden = dot_cols(grad_ref[:, :wide], w_ref[0])
    for z in range(1, zs):
        d_hidden += dot_cols(grad_ref[:, z * wide : (z + 1) * wide], w_ref[z])
    out_ref[...] = (jnp.concatenate([d_hidden, d_hidden], axis=1) * kept_ref[...].astype(F32)).astype(BF16)


FF_ROWS = 256


def ff_rows(width):
    return pl.BlockSpec((FF_ROWS, width), lambda i: (i, 0))


def ff_forward(x, w):
    rows, depth = x.shape
    wide = w.shape[1]
    return pl.pallas_call(
        ff_kernel,
        grid=(rows // FF_ROWS,),
        in_specs=[ff_rows(depth), pl.BlockSpec((depth, wide), lambda i: (0, 0))],
        out_specs=[ff_rows(wide // 2), ff_rows(wide)],
        out_shape=[jax.ShapeDtypeStruct((rows, wide // 2), BF16), jax.ShapeDtypeStruct((rows, wide), BF16)],
        compiler_params=PARAMS,
        cost_estimate=pl.CostEstimate(flops=2 * rows * depth * wide, bytes_accessed=20 * 2**20, transcendentals=0),
    )(x, w)


def ff_backward(grad, w, kept):
    rows, depth = grad.shape
    wide = kept.shape[1]
    return pl.pallas_call(
        ff_back_kernel,
        grid=(rows // FF_ROWS,),
        in_specs=[ff_rows(depth), pl.BlockSpec(w.shape, lambda i: (0, 0, 0)), ff_rows(wide)],
        out_specs=ff_rows(wide),
        out_shape=jax.ShapeDtypeStruct((rows, wide), BF16),
        compiler_params=PARAMS,
        cost_estimate=pl.CostEstimate(flops=rows * depth * wide, bytes_accessed=20 * 2**20, transcendentals=0),
    )(grad, w, kept)


def cut_kernel(in_ref, out_ref, in_blocks, out_blocks, wide):
    group, _, double = in_blocks.shape
    tile, ff = double // 2, out_ref.shape[1]
    span = group * tile
    odd = ff % 128
    live = lax.broadcasted_iota(jnp.int32, (in_ref.shape[0], span), 1) < ff
    wide[...] = jnp.zeros_like(wide)
    wide[:, : 2 * ff] = in_ref[...].astype(F32)
    gate = jnp.where(live, wide[:, :span], 0.0)
    up = pltpu.roll(wide[:, ff - odd : ff - odd + span], span - odd, 1)
    up = jnp.where(live, up, 0.0)
    wide[:, :span] = jnp.zeros_like(live, F32)
    wide[:, :ff] = out_ref[...].astype(F32)
    down = wide[:, :span]
    for g in range(group):
        at = slice(g * tile, (g + 1) * tile)
        in_blocks[g] = jnp.concatenate([gate[:, at], up[:, at]], axis=1).astype(BF16)
        out_blocks[g] = down[:, at].astype(BF16)


def cut_ff(w_in, w_out, group, tile):
    rows, ff = w_out.shape
    return pl.pallas_call(
        cut_kernel,
        grid=(rows // 16,),
        in_specs=[pl.BlockSpec((16, 2 * ff), lambda i: (i, 0)), pl.BlockSpec((16, ff), lambda i: (i, 0))],
        out_specs=[
            pl.BlockSpec((group, 16, 2 * tile), lambda i: (0, i, 0)),
            pl.BlockSpec((group, 16, tile), lambda i: (0, i, 0)),
        ],
        out_shape=[
            jax.ShapeDtypeStruct((group, rows, 2 * tile), BF16),
            jax.ShapeDtypeStruct((group, rows, tile), BF16),
        ],
        scratch_shapes=[pltpu.VMEM((16, -(-(ff + group * tile) // 128) * 128), F32)],
        compiler_params=PARAMS,
    )(w_in, w_out)


def join_kernel(in_blocks, out_blocks, in_ref, out_ref):
    group, _, double = in_blocks.shape
    tile, ff = double // 2, out_ref.shape[1]
    odd = ff % 128
    blocks = [in_blocks[g].astype(F32) for g in range(group)]
    gate = jnp.concatenate([block[:, :tile] for block in blocks], axis=1)
    up = jnp.concatenate([block[:, tile:] for block in blocks], axis=1)
    up = pltpu.roll(up, odd, 1)
    lane = lax.broadcasted_iota(jnp.int32, (up.shape[0], 128), 1)
    in_ref[:, : ff - odd] = gate[:, : ff - odd]
    in_ref[:, ff - odd : ff - odd + 128] = jnp.where(lane < odd, gate[:, ff - odd : ff - odd + 128], up[:, :128])
    in_ref[:, ff - odd + 128 :] = up[:, 128 : ff + odd]
    down = jnp.concatenate([out_blocks[g].astype(F32) for g in range(group)], axis=1)
    out_ref[...] = down[:, :ff]


def join_ff(in_blocks, out_blocks, ff):
    group, rows, tile = out_blocks.shape
    return pl.pallas_call(
        join_kernel,
        grid=(rows // 16,),
        in_specs=[
            pl.BlockSpec((group, 16, 2 * tile), lambda i: (0, i, 0)),
            pl.BlockSpec((group, 16, tile), lambda i: (0, i, 0)),
        ],
        out_specs=[pl.BlockSpec((16, 2 * ff), lambda i: (i, 0)), pl.BlockSpec((16, ff), lambda i: (i, 0))],
        out_shape=[jax.ShapeDtypeStruct((rows, 2 * ff), F32), jax.ShapeDtypeStruct((rows, ff), F32)],
        compiler_params=PARAMS,
    )(in_blocks, out_blocks)


def closing_kernel(zs, sum_ref, rows_ref, qkv_ref, dense_ref, total_ref, got, mine, lines, *refs):
    send, recv, local, line_send, line_recv = refs
    y, x, c = here()
    z = lax.axis_index("z")
    me = place(y, x, c)
    wide = got.shape[2]
    width = wide // 3
    piece = got.shape[1]
    found = swap_peers(zs, ("line",))
    greet([name for _, name in found])
    copies, comes = [], []
    for k, (peer, name) in enumerate(found[:7]):
        sems = dict(send_sem=send.at[k], recv_sem=recv.at[k], device_id=name, device_id_type=MESH)
        src = rows_ref.at[peer, :, pl.ds(0, wide)]
        copies.append(pltpu.make_async_remote_copy(src_ref=src, dst_ref=got.at[me], **sems))
        comes.append(pltpu.make_async_remote_copy(src_ref=got.at[peer], dst_ref=got.at[peer], **sems))
    for k, (peer, name) in enumerate(found[7:]):
        sems = dict(send_sem=line_send.at[k], recv_sem=line_recv.at[k], device_id=name, device_id_type=MESH)
        copies.append(pltpu.make_async_remote_copy(src_ref=sum_ref, dst_ref=lines.at[z], **sems))
        comes.append(pltpu.make_async_remote_copy(src_ref=lines.at[peer], dst_ref=lines.at[peer], **sems))
    for copy in copies:
        copy.start()
    keeps = [
        pltpu.make_async_copy(rows_ref.at[me, :, pl.ds(0, wide)], got.at[me], local.at[0]),
        pltpu.make_async_copy(sum_ref, lines.at[z], local.at[1]),
        pltpu.make_async_copy(rows_ref.at[:, :, pl.ds(wide, width)], mine, local.at[2]),
    ]
    for keep in keeps:
        keep.start()
    keeps[2].wait()
    for at in range(0, piece, 16):
        rows = jnp.concatenate([mine[g, at : at + 16] for g in range(8)], axis=1).astype(F32)
        dense_ref[at : at + 16] = rows
    for come in comes:
        come.wait_recv()
    for keep in keeps[:2]:
        keep.wait()
    for g in range(8):
        for j in range(3):
            at = pl.ds(j * D + g * width, width)
            qkv_ref[:, at] = got[g, :, j * width : (j + 1) * width].astype(F32)
    total = lines[0]
    for k in range(1, zs):
        total += lines[k]
    part = total[:, :piece]
    for k in range(1, zs):
        part = jnp.where(z == k, total[:, k * piece : (k + 1) * piece], part)
    total_ref[...] = part
    for copy in copies:
        copy.wait_send()


def closing(zs, sums, rows):
    _, piece, columns = rows.shape
    width = columns // 4
    return pl.pallas_call(
        functools.partial(closing_kernel, zs),
        out_shape=[
            jax.ShapeDtypeStruct((piece, 3 * D), F32),
            jax.ShapeDtypeStruct((piece, D), F32),
            jax.ShapeDtypeStruct((8, piece), F32),
        ],
        in_specs=[ROWS, ANY],
        out_specs=[ROWS] * 3,
        scratch_shapes=[
            pltpu.VMEM((8, piece, 3 * width), BF16),
            pltpu.VMEM((8, piece, width), BF16),
            pltpu.VMEM((zs, 8, width), F32),
            pltpu.SemaphoreType.DMA((7,)),
            pltpu.SemaphoreType.DMA((7,)),
            pltpu.SemaphoreType.DMA((3,)),
            pltpu.SemaphoreType.DMA((zs - 1,)),
            pltpu.SemaphoreType.DMA((zs - 1,)),
        ],
        compiler_params=pltpu.CompilerParams(collective_id=5, has_side_effects=True, vmem_limit_bytes=56 * 2**20),
        cost_estimate=pl.CostEstimate(flops=0, bytes_accessed=50 * 2**20, transcendentals=0),
    )(sums, rows)


def on_device(sizes, x_in, d_out, w_qkv, w_dense, w_in, w_out, gone, bone, gtwo, btwo, flags, span_start, span_len):
    gy, gx, cores, zs = sizes
    piece = w_qkv.shape[0]
    ff = w_out.shape[1]
    group = gy * gx * cores
    width = D // group
    tile = -(-ff // (group * 64)) * 64
    own = gy == 2

    def permute(array):
        lead = array.shape[:-1]
        return jnp.swapaxes(array.reshape(lead + (group, zs, piece)), -3, -2).reshape(lead + (D,))

    def restore(array):
        lead = array.shape[:-1]
        return jnp.swapaxes(array.reshape(lead + (zs, group, piece)), -3, -2).reshape(lead + (D,))

    def swap(name, arrays, kinds):
        if own:
            return group_swap(name, zs, arrays, kinds)
        ways = {
            "swap": lambda a: lax.all_to_all(a, GROUP, 0, 0, tiled=True),
            "group": lambda a: lax.all_gather(a, GROUP, axis=0),
            "line": lambda a: lax.all_gather(a, "z", axis=0),
        }
        return [ways[k](a) for a, k in zip(arrays, kinds)]

    def spread_rows(block):
        return lax.all_gather(block, GROUP, axis=0, tiled=True)

    rows_f32 = jax.ShapeDtypeStruct((SEQ_LEN, D), F32)
    rows_low = jax.ShapeDtypeStruct((SEQ_LEN, D), BF16)
    sums_type = jax.ShapeDtypeStruct((8, D), F32)

    def fold(partial):
        return lax.psum_scatter(partial.astype(BF16), GROUP, scatter_dimension=0, tiled=True).astype(F32)

    def stack_sums(*arrays):
        return jnp.pad(jnp.stack([jnp.sum(a, axis=0) for a in arrays]), ((0, 6), (0, 0)))

    def fold_one(left, right, x, gains):
        if own:
            kinds = [rows_f32, rows_f32, jax.ShapeDtypeStruct((SEQ_LEN, 128), F32)]
            whole, first, normal, inverse = group_fold(0, zs, "one", left, right, gains, [x], kinds)
            return whole.reshape(left.shape[0], D), first, normal, inverse
        first, normal, inverse = first_norm(permute(deep_alpha * x.astype(F32) + fold(dot(left, right))), gains)
        return spread_rows(first.astype(BF16)), first, normal, inverse

    def ff_turn(x, w_in, w_out, first, grad, gains):
        if own:
            whole, kept, w_out, result, d_pre, sums, d_out = turn(zs, x, w_in, w_out, gains, first, grad)
            rows = x.shape[0]
            return whole.reshape(rows, D), kept.reshape(rows, -1), w_out, result, d_pre, sums, d_out
        w_out = lax.all_gather(w_out, "z", axis=0)
        hidden, kept = ff_forward(x, w_in)
        grad = grad.astype(F32)
        right = jnp.swapaxes(w_out, 0, 1).reshape(-1, D)
        result, d_pre, terms = second_norm(fold(dot(hidden, right)), first, grad, gains)
        whole = spread_rows(d_pre.astype(BF16))
        d_out = jnp.swapaxes(dot_rows(hidden, whole).reshape(-1, zs, D // zs), 0, 1).astype(BF16)
        return whole, kept, w_out, result.astype(BF16), d_pre, stack_sums(terms, grad), d_out

    def fold_back(left, right, d_pre_two, normal, inverse, gains):
        if own:
            kinds = [rows_f32, sums_type]
            whole, d_pre, sums = group_fold(7, zs, "back", left, right, gains, [d_pre_two, normal, inverse], kinds)
            return whole.reshape(left.shape[0], D), d_pre, sums
        d_pre, terms, d_first = first_back(fold(dot_cols(left, right)), d_pre_two, normal, inverse, gains)
        return spread_rows(restore(d_pre).astype(BF16)), d_pre, stack_sums(terms, d_first)

    def fold_last(left, right, d_pre, gains, extras, kinds):
        if own:
            return group_fold(8, zs, "last", left, right, gains, [d_pre], [rows_low], extras, kinds)
        out = restore((deep_alpha * d_pre + fold(dot_cols(left, right))).astype(BF16))
        return [out] + swap(8, extras, kinds)

    def gather(block):
        return lax.all_gather(block, "z", axis=0, tiled=True)

    def scatter(partial):
        return lax.psum_scatter(partial.astype(BF16), "z", scatter_dimension=0, tiled=True)

    masked = jnp.max(flags) > 0
    prefix = jnp.where(masked, SEQ_LEN, SEQ_LEN - span_len[0])
    info = jnp.concatenate([gone, bone, gtwo, btwo, jnp.stack([prefix, span_start[0]]).astype(BF16)])
    info = jnp.pad(info[None, :], ((0, 15), (0, -info.shape[0] % 128)))

    qkv_blocks = jnp.moveaxis(w_qkv.reshape(piece, 3, group, width), 2, 0).reshape(group, piece, 3 * width)
    w_dense_part = gather(w_dense)
    qkv_blocks, info = swap(2, [qkv_blocks, info], ("swap", "group"))
    w_qkv_part = gather(qkv_blocks.reshape(group * piece, 3 * width))
    info = info[:, 0]
    place_info = info[:, 4 * piece : 4 * piece + 2].astype(jnp.int32)
    prefix, start = place_info[:, 0], place_info[:, 1]
    cosine, sine = tables(prefix, start)
    in_blocks, out_blocks = cut_ff(w_in, w_out, group, tile)
    info = jnp.pad(info, ((0, -group % 16), (0, 0)))
    in_blocks, out_blocks, qkv_blocks, w_dense_part, cosine, sine = lax.optimization_barrier(
        (in_blocks, out_blocks, qkv_blocks, w_dense_part, cosine, sine)
    )
    swapped, kinds = [in_blocks, out_blocks, info], ("swap", "swap", "line")
    if own:
        x_all, grad_two, in_blocks, out_blocks, info = enter(zs, x_in, d_out, swapped, kinds)
        x_all = x_all.reshape(group * SEQ_LEN, D)
    else:
        x_all, grad_two = spread_rows(permute(x_in)), permute(d_out)
        in_blocks, out_blocks, info = swap(3, swapped, kinds)
    w_in_part = gather(in_blocks.reshape(group * piece, 2 * tile))
    out_rows = out_blocks.reshape(group * piece, tile).T
    gains = info[:, :group, : 4 * piece].astype(F32).reshape(zs, group, 4, piece)
    gains = jnp.pad(jnp.transpose(gains, (2, 0, 1, 3)).reshape(4, D), ((0, 4), (0, 0)))
    w_qkv_part, x_all, gains, out_rows = lax.optimization_barrier((w_qkv_part, x_all, gains, out_rows))
    packed = dot(x_all, w_qkv_part)
    qkv, context = attend(prefix, packed, cosine, sine)
    first_all, first, normal_one, inverse_one = fold_one(context, w_dense_part, x_in, gains)
    d_branch, kept, w_out_part, layer_out, d_pre_two, sums_two, d_w_out = ff_turn(
        first_all, w_in_part, out_rows, first, grad_two, gains
    )
    layer_out = restore(layer_out)
    d_w_out = lax.psum_scatter(d_w_out, "z", scatter_dimension=0)
    d_projected = ff_backward(d_branch, w_out_part, kept)
    d_w_in = dot_rows(first_all, d_projected).astype(BF16)
    d_w_in, d_projected = lax.optimization_barrier((d_w_in, d_projected))
    d_w_in = scatter(d_w_in)
    d_attn, d_pre_one, sums_one = fold_back(d_projected, w_in_part, d_pre_two, normal_one, inverse_one, gains)
    d_attn, d_w_out = lax.optimization_barrier((d_attn, d_w_out))
    d_context = dot_cols(d_attn, w_dense_part).astype(BF16)
    d_packed = attend_back(prefix, qkv, d_context, cosine, sine)
    d_w_qkv = dot_rows(x_all, d_packed).astype(BF16)
    d_dense = dot_rows(context, d_attn).astype(BF16).reshape(zs, piece, group, width)
    d_dense = jnp.swapaxes(d_dense, 1, 2).reshape(D, width)
    d_w_qkv = jnp.concatenate([d_w_qkv, d_dense], axis=1)
    sums = jnp.concatenate([sums_one[:2], sums_two[:2], jnp.zeros((4, D), F32)])
    d_packed, d_w_qkv, d_w_in, sums = lax.optimization_barrier((d_packed, d_w_qkv, d_w_in, sums))
    d_w_qkv = scatter(d_w_qkv)
    d_w_in, d_w_out = d_w_in.reshape(group, piece, 2 * tile), d_w_out.T.reshape(group, piece, tile)
    d_input, d_w_in, d_w_out, sums = fold_last(
        d_packed, w_qkv_part, d_pre_one, gains, [d_w_in, d_w_out, sums], ("swap", "swap", "group")
    )
    sums = jnp.sum(sums, axis=0).reshape(8, zs, group, piece)
    sums = lax.dynamic_index_in_dim(sums, lax.axis_index(GROUP), 2, keepdims=False).reshape(8, width)
    out_in, out_out = join_ff(d_w_in, d_w_out, ff)
    out_in, out_out, d_input, d_w_qkv, sums = lax.optimization_barrier((out_in, out_out, d_input, d_w_qkv, sums))
    if own:
        out_qkv, out_dense, sums = closing(zs, sums, d_w_qkv.reshape(group, piece, 4 * width))
    else:
        out_dense = d_w_qkv[:, 3 * width :].reshape(group, piece, width)
        out_dense = jnp.swapaxes(out_dense, 0, 1).reshape(piece, D).astype(F32)
        d_w_qkv = d_w_qkv[:, : 3 * width].reshape(group, piece, 3 * width)
        d_w_qkv, sums = swap(5, [d_w_qkv, sums], ("swap", "line"))
        out_qkv = jnp.transpose(d_w_qkv.astype(F32).reshape(group, piece, 3, width), (1, 2, 0, 3))
        out_qkv = out_qkv.reshape(piece, 3 * D)
        sums = jnp.sum(sums, axis=0).reshape(8, zs, piece)
        sums = lax.dynamic_index_in_dim(sums, lax.axis_index("z"), 1, keepdims=False)
    return layer_out, d_input, out_qkv, out_dense, out_in, out_out, sums[0], sums[1], sums[2], sums[3]


def solution(mesh):
    grp, shard = mesh.shape["grp"], mesh.shape["shard"]
    sizes = (grp // 4, 2, 2, shard)
    inner = Mesh(mesh.devices.reshape(sizes), ALL)
    rows, flat = P(ALL, None), P(ALL)
    return jax.shard_map(
        functools.partial(on_device, sizes),
        mesh=inner,
        in_specs=(rows,) * 6 + (flat,) * 7,
        out_specs=(rows,) * 6 + (flat,) * 4,
        check_vma=False,
    )
```

```python
import functools

import jax
import jax.numpy as jnp
from jax import lax
from jax.experimental import pallas as pl
from jax.experimental.pallas import tpu as pltpu
from jax.experimental.layout import Layout, with_layout_constraint
from jax.sharding import Mesh
from jax.sharding import PartitionSpec as P

HEADS = 16
HEAD = 128
SEQ_LEN = 224
D = HEADS * HEAD
deep_alpha = 6.928203230275509
norm_eps = 1e-05
far_below = -1e30
scale = HEAD ** (-0.5)

ALL = ("gy", "gx", "core", "z")
GROUP = ("gy", "gx", "core")
MESH = pl.DeviceIdType.MESH
F32 = jnp.float32
BF16 = jnp.bfloat16


def dot(left, right):
    return jnp.dot(left, right, preferred_element_type=F32)


def dot_rows(left, right):
    return lax.dot_general(left, right, (((0,), (0,)), ((), ())), preferred_element_type=F32)


def dot_cols(left, right):
    return lax.dot_general(left, right, (((1,), (1,)), ((), ())), preferred_element_type=F32)


def swap_halves(block):
    lane = lax.broadcasted_iota(jnp.int32, block.shape, 1)
    return jnp.where((lane & 32) == 0, pltpu.roll(block, 96, 1), pltpu.roll(block, 32, 1))


def seen(prefix):
    row = lax.broadcasted_iota(jnp.int32, (SEQ_LEN, SEQ_LEN), 0)
    col = lax.broadcasted_iota(jnp.int32, (SEQ_LEN, SEQ_LEN), 1)
    return (col < prefix) | (col <= row)


def softmax(queries, keys, visible):
    scores = jnp.where(visible, dot_cols(queries, keys), far_below)
    weights = jnp.exp(scores - jnp.max(scores, axis=1, keepdims=True))
    return weights / jnp.sum(weights, axis=1, keepdims=True)


def attend_kernel(prefix_ref, packed_ref, cos_ref, sin_ref, qkv_ref, context_ref):
    width = context_ref.shape[1]
    visible = seen(prefix_ref[pl.program_id(0)])
    cosine = cos_ref[0]
    sine = sin_ref[0]
    for head in range(width // HEAD):
        at = pl.ds(head * HEAD, HEAD)
        at_k = pl.ds(width + head * HEAD, HEAD)
        at_v = pl.ds(2 * width + head * HEAD, HEAD)
        raw = packed_ref[:, at]
        queries = ((raw * cosine + swap_halves(raw) * sine) * scale).astype(BF16)
        raw = packed_ref[:, at_k]
        keys = (raw * cosine + swap_halves(raw) * sine).astype(BF16)
        values = packed_ref[:, at_v].astype(BF16)
        qkv_ref[:, at] = queries
        qkv_ref[:, at_k] = keys
        qkv_ref[:, at_v] = values
        probs = softmax(queries, keys, visible).astype(BF16)
        context_ref[:, at] = dot(probs, values).astype(BF16)


def attend_back_kernel(prefix_ref, qkv_ref, d_context_ref, cos_ref, sin_ref, d_packed_ref):
    width = d_context_ref.shape[1]
    visible = seen(prefix_ref[pl.program_id(0)])
    cosine = cos_ref[0]
    sine = sin_ref[0]
    for head in range(width // HEAD):
        at = pl.ds(head * HEAD, HEAD)
        at_k = pl.ds(width + head * HEAD, HEAD)
        at_v = pl.ds(2 * width + head * HEAD, HEAD)
        queries = qkv_ref[:, at]
        keys = qkv_ref[:, at_k]
        values = qkv_ref[:, at_v]
        d_context = d_context_ref[:, at]
        probs = softmax(queries, keys, visible)
        d_packed_ref[:, at_v] = dot_rows(probs.astype(BF16), d_context).astype(BF16)
        d_probs = dot_cols(d_context, values)
        inner = jnp.sum(probs * d_probs, axis=1, keepdims=True)
        d_scores = (probs * (d_probs - inner)).astype(BF16)
        grad = dot(d_scores, keys) * scale
        d_packed_ref[:, at] = (grad * cosine - swap_halves(grad) * sine).astype(BF16)
        grad = dot_rows(d_scores, queries)
        d_packed_ref[:, at_k] = (grad * cosine - swap_halves(grad) * sine).astype(BF16)


def by_sequence(width):
    return pl.BlockSpec((SEQ_LEN, width), lambda s: (s, 0))


TABLE = pl.BlockSpec((1, SEQ_LEN, HEAD), lambda s: (s, 0, 0))
SCALARS = pl.BlockSpec(memory_space=pltpu.SMEM)
PARAMS = pltpu.CompilerParams(vmem_limit_bytes=56 * 2**20)
SMALL = pltpu.CompilerParams(vmem_limit_bytes=24 * 2**20)


def attend(prefix, packed, cosine, sine):
    rows, width = packed.shape[0], packed.shape[1] // 3
    return pl.pallas_call(
        attend_kernel,
        grid=(rows // SEQ_LEN,),
        in_specs=[SCALARS, by_sequence(3 * width), TABLE, TABLE],
        out_specs=[by_sequence(3 * width), by_sequence(width)],
        out_shape=[
            jax.ShapeDtypeStruct((rows, 3 * width), BF16),
            jax.ShapeDtypeStruct((rows, width), BF16),
        ],
        compiler_params=PARAMS,
    )(prefix, packed, cosine, sine)


def attend_back(prefix, qkv, d_context, cosine, sine):
    rows, width = d_context.shape
    return pl.pallas_call(
        attend_back_kernel,
        grid=(rows // SEQ_LEN,),
        in_specs=[SCALARS, by_sequence(3 * width), by_sequence(width), TABLE, TABLE],
        out_specs=by_sequence(3 * width),
        out_shape=jax.ShapeDtypeStruct((rows, 3 * width), BF16),
        compiler_params=PARAMS,
    )(prefix, qkv, d_context, cosine, sine)


def tables(prefix, start):
    place = jnp.arange(SEQ_LEN, dtype=jnp.int32)
    in_span = place[None, :] >= prefix[:, None]
    pos_one = jnp.where(in_span, start[:, None], place[None, :])
    pos_two = jnp.where(in_span, place[None, :] - prefix[:, None] + 1, 0)
    lane = jnp.arange(HEAD)
    freqs = 10000.0 ** (-2.0 * (lane % 32).astype(F32) / 64)
    place_of = jnp.where(lane[None, None, :] < 64, pos_one[:, :, None], pos_two[:, :, None])
    angles = place_of.astype(F32) * freqs
    sign = jnp.where(lane % 64 < 32, -1.0, 1.0)
    return jnp.cos(angles), jnp.sin(angles) * sign


def norm_parts(values):
    center = values - jnp.mean(values, axis=-1, keepdims=True)
    inverse = lax.rsqrt(jnp.mean(center * center, axis=-1, keepdims=True) + norm_eps)
    return center * inverse, inverse


def norm_back(normal, inverse, gain, grad):
    scaled = gain * grad
    return inverse * (
        scaled
        - jnp.mean(scaled, axis=-1, keepdims=True)
        - normal * jnp.mean(scaled * normal, axis=-1, keepdims=True)
    )


def gate_parts(gate):
    phi = 0.5 * (1.0 + lax.erf(gate * 0.7071067811865476))
    slope = phi + gate * jnp.exp(-0.5 * gate * gate) * 0.3989422804014327
    return gate * phi, slope


def here():
    return lax.axis_index("gy"), lax.axis_index("gx"), lax.axis_index("core")


def place(y, x, c):
    return (y * 2 + x) * 2 + c


def greet(peers):
    barrier = pltpu.get_barrier_semaphore()
    for peer in peers:
        pl.semaphore_signal(barrier, inc=1, device_id=peer, device_id_type=MESH)
    pl.semaphore_wait(barrier, len(peers))


def spread_block(cut, base, block_ref, out_ref, send, recv, local):
    rows = block_ref.shape[0]
    y, x, c = here()
    to_x, to_y, to_c = {"gx": 1 - x}, {"gy": 1 - y}, {"core": 1 - c}
    me, by_x, by_y, far = place(y, x, c), place(y, 1 - x, c), place(1 - y, x, c), place(1 - y, 1 - x, c)
    low, high = pl.ds(0, cut), pl.ds(cut, rows - cut)

    def push(k, src, dst, to):
        copy = pltpu.make_async_remote_copy(
            src_ref=src, dst_ref=dst, send_sem=send.at[base + k], recv_sem=recv.at[base + k], device_id=to, device_id_type=MESH
        )
        copy.start()
        return copy

    def landed(k, dst):
        pltpu.make_async_remote_copy(
            src_ref=dst, dst_ref=dst, send_sem=send.at[base + k], recv_sem=recv.at[base + k], device_id=to_c, device_id_type=MESH
        ).wait_recv()

    sent = [
        push(0, block_ref.at[low], out_ref.at[me, low], to_x),
        push(1, block_ref.at[high], out_ref.at[me, high], to_y),
        push(2, block_ref.at[high], out_ref.at[me, high], to_x),
        push(3, block_ref.at[low], out_ref.at[me, low], to_y),
        push(4, block_ref, out_ref.at[me], to_c),
    ]
    keep = pltpu.make_async_copy(block_ref, out_ref.at[me], local)
    keep.start()
    landed(0, out_ref.at[by_x, low])
    sent.append(push(5, out_ref.at[by_x, low], out_ref.at[by_x, low], to_y))
    sent.append(push(7, out_ref.at[by_x, low], out_ref.at[by_x, low], to_c))
    landed(1, out_ref.at[by_y, high])
    sent.append(push(6, out_ref.at[by_y, high], out_ref.at[by_y, high], to_x))
    sent.append(push(8, out_ref.at[by_y, high], out_ref.at[by_y, high], to_c))
    landed(2, out_ref.at[by_x, high])
    sent.append(push(9, out_ref.at[by_x, high], out_ref.at[by_x, high], to_c))
    landed(3, out_ref.at[by_y, low])
    sent.append(push(10, out_ref.at[by_y, low], out_ref.at[by_y, low], to_c))
    landed(5, out_ref.at[far, low])
    sent.append(push(11, out_ref.at[far, low], out_ref.at[far, low], to_c))
    landed(6, out_ref.at[far, high])
    sent.append(push(12, out_ref.at[far, high], out_ref.at[far, high], to_c))
    other, other_x, other_y, other_far = (
        place(y, x, 1 - c),
        place(y, 1 - x, 1 - c),
        place(1 - y, x, 1 - c),
        place(1 - y, 1 - x, 1 - c),
    )
    landed(4, out_ref.at[other])
    landed(7, out_ref.at[other_x, low])
    landed(8, out_ref.at[other_y, high])
    landed(9, out_ref.at[other_x, high])
    landed(10, out_ref.at[other_y, low])
    landed(11, out_ref.at[other_far, low])
    landed(12, out_ref.at[other_far, high])
    keep.wait()
    for copy in sent:
        copy.wait_send()


ANY = pl.BlockSpec(memory_space=pl.ANY)


def swap_peers(zs, kinds):
    y, x, c = here()
    z = lax.axis_index("z")
    found = []
    for k in range(1, 8):
        peer = ((y + k // 4) % 2, (x + k // 2 % 2) % 2, (c + k % 2) % 2)
        found.append((place(*peer), {"gy": peer[0], "gx": peer[1], "core": peer[2]}))
    if "line" in kinds:
        found += [((z + k) % zs, {"z": (z + k) % zs}) for k in range(1, zs)]
    return found


def swap_begin(zs, kinds, blocks, outs, send, recv, local):
    copies, comes, keeps = [], [], []
    found = swap_peers(zs, kinds)
    for i, kind in enumerate(kinds):
        me = lax.axis_index("z") if kind == "line" else place(*here())
        for k, (peer, name) in enumerate(found[7:] if kind == "line" else found[:7]):
            src = blocks[i].at[peer] if kind == "swap" else blocks[i]
            landing = outs[i].at[peer]
            sems = dict(send_sem=send.at[i, k], recv_sem=recv.at[i, k], device_id=name, device_id_type=MESH)
            copies.append(pltpu.make_async_remote_copy(src_ref=src, dst_ref=outs[i].at[me], **sems))
            comes.append(pltpu.make_async_remote_copy(src_ref=landing, dst_ref=landing, **sems))
            copies[-1].start()
        own = blocks[i].at[me] if kind == "swap" else blocks[i]
        keeps.append(pltpu.make_async_copy(own, outs[i].at[me], local.at[i]))
        keeps[-1].start()

    def finish():
        for come in comes:
            come.wait_recv()
        for copy in copies:
            copy.wait_send()
        for keep in keeps:
            keep.wait()

    return finish


SWAP_LEAD = {"swap": lambda zs: (), "group": lambda zs: (8,), "line": lambda zs: (zs,)}


def swap_shapes(zs, arrays, kinds):
    return [jax.ShapeDtypeStruct(SWAP_LEAD[k](zs) + a.shape, a.dtype) for a, k in zip(arrays, kinds)]


def swap_scratch(zs, kinds):
    n, most = len(kinds), max(7, zs - 1)
    return [
        pltpu.SemaphoreType.DMA((n, most)),
        pltpu.SemaphoreType.DMA((n, most)),
        pltpu.SemaphoreType.DMA((n,)),
    ]


SLAB = 16
ROWS = pl.BlockSpec(memory_space=pltpu.VMEM)
CHIP_COLS = 256


def by_rows(value, zs, piece):
    group = D // (zs * piece)
    order = [g * zs + z for z in range(zs) for g in range(group)]
    return jnp.concatenate([value[:, m * piece : (m + 1) * piece] for m in order], axis=1)


def in_order(value, zs, piece):
    group = D // (zs * piece)
    order = [z * group + g for g in range(group) for z in range(zs)]
    return jnp.concatenate([value[:, m * piece : (m + 1) * piece] for m in order], axis=1)


def first_norm(values, gains):
    normal, inverse = norm_parts(values)
    first = normal * gains[0:1] + gains[1:2]
    return first, normal, inverse


def second_norm(total, first, grad, gains):
    normal, inverse = norm_parts(deep_alpha * first + total)
    return normal * gains[2:3] + gains[3:4], norm_back(normal, inverse, gains[2:3], grad), grad * normal


def first_back(total, d_pre_two, normal, inverse, gains):
    d_first = deep_alpha * d_pre_two + total
    return norm_back(normal, inverse, gains[0:1], d_first), d_first * normal, d_first


def fold_kernel(mode, across, zs, piece, n_aux, n_out, kinds, *refs):
    left_ref, right_ref, gains_ref = refs[:3]
    aux_refs = refs[3 : 3 + n_aux]
    refs = refs[3 + n_aux :]
    n_swap = len(kinds)
    swap_in, refs = refs[:n_swap], refs[n_swap:]
    spread = mode != "last"
    if spread:
        all_ref, refs = refs[0], refs[1:]
    out_refs, refs = refs[:n_out], refs[n_out:]
    swap_out, refs = refs[:n_swap], refs[n_swap:]
    aux, refs = refs[:n_aux], refs[n_aux:]
    outs, refs = refs[:n_out], refs[n_out:]
    left, right, part, got, near_x, near_y, from_x, from_y, block, acc, send, recv, local = refs[:13]
    rows, width = block.shape
    cut = near_x.shape[0]
    y, x, c = here()
    to_x, to_y, to_c = {"gx": 1 - x}, {"gy": 1 - y}, {"core": 1 - c}
    chips = [(1 - y, 1 - x), (y, 1 - x), (1 - y, x), (y, x)]
    low, high = pl.ds(0, cut), pl.ds(cut, rows - cut)

    def push(k, src, dst, to):
        copy = pltpu.make_async_remote_copy(
            src_ref=src, dst_ref=dst, send_sem=send.at[k], recv_sem=recv.at[k], device_id=to, device_id_type=MESH
        )
        copy.start()
        return copy

    def add(k, extra, start, size, offset=0):
        @pl.loop(0, size // SLAB)
        def _(step):
            at = pl.ds(pl.multiple_of(start + step * SLAB, SLAB), SLAB)
            of = pl.ds(pl.multiple_of(start - offset + step * SLAB, SLAB), SLAB)
            part[k, c, at] = (part[k, c, at].astype(F32) + extra[of].astype(F32)).astype(BF16)

    loads = [pltpu.make_async_copy(left_ref.at[a * 2 + b], left.at[k], local.at[k]) for k, (a, b) in enumerate(chips)]
    load_right = pltpu.make_async_copy(right_ref, right, local.at[4])
    load_aux = [pltpu.make_async_copy(r, v, local.at[5 + k]) for k, (r, v) in enumerate(zip(aux_refs, aux))]
    loads[0].start()
    load_right.start()
    for load in loads[1:] + load_aux:
        load.start()
    if n_swap:
        greet([name for _, name in swap_peers(1, kinds)])
        swap_finish = swap_begin(1, kinds, swap_in, swap_out, *refs[13:])
    else:
        greet([to_x, to_y, to_c])

    def product(k):
        loads[k].wait()

        @pl.loop(0, width // CHIP_COLS)
        def _(step):
            at = pl.ds(pl.multiple_of(step * CHIP_COLS, CHIP_COLS), CHIP_COLS)
            here_part = dot_cols(left[k], right[at]) if across else dot(left[k], right[:, at])
            part[k, 0, :, at] = here_part[:rows].astype(BF16)
            part[k, 1, :, at] = here_part[rows:].astype(BF16)

        return push(k, part.at[k, 1 - c], got.at[k], to_c)

    load_right.wait()
    sent = [product(0), product(1)]
    sent[0].wait_recv()
    add(0, got.at[0], 0, rows)
    far_x = push(4, part.at[0, c, low], near_x, to_x)
    far_y = push(5, part.at[0, c, high], near_y, to_y)
    sent.append(product(2))
    sent[1].wait_recv()
    add(1, got.at[1], 0, rows)
    plain_x = push(6, part.at[1, c, low], from_x.at[low], to_x)
    sent[2].wait_recv()
    add(2, got.at[2], 0, rows)
    plain_y = push(7, part.at[2, c, high], from_y.at[high], to_y)
    sent.append(product(3))
    far_y.wait_recv()
    add(1, near_y, cut, rows - cut, cut)
    more_x = push(8, part.at[1, c, high], from_x.at[high], to_x)
    far_x.wait_recv()
    add(2, near_x, 0, cut)
    more_y = push(9, part.at[2, c, low], from_y.at[low], to_y)
    sent[3].wait_recv()
    for load in load_aux:
        load.wait()
    plain_x.wait_recv()
    plain_y.wait_recv()
    more_x.wait_recv()
    more_y.wait_recv()
    gains = gains_ref[...]
    acc[...] = jnp.zeros_like(acc)

    @pl.loop(0, rows // SLAB)
    def _(step):
        at = pl.ds(pl.multiple_of(step * SLAB, SLAB), SLAB)
        total = part[3, c, at].astype(F32) + got[3, at].astype(F32) + from_x[at].astype(F32) + from_y[at].astype(F32)
        held = [a[at].astype(F32) for a in aux]
        if mode == "one":
            first, normal, inverse = first_norm(by_rows(deep_alpha * held[0] + total, zs, piece), gains)
            outs[0][at] = first
            outs[1][at] = normal
            outs[2][at] = jnp.broadcast_to(inverse, (SLAB, 128))
            block[at] = first.astype(BF16)
        elif mode == "back":
            d_pre, terms, d_first = first_back(total, held[0], held[1], held[2][:, 0:1], gains)
            outs[0][at] = d_pre
            block[at] = in_order(d_pre, zs, piece).astype(BF16)
            acc[0] += terms
            acc[1] += d_first
        else:
            outs[0][at] = in_order(deep_alpha * held[0] + total, zs, piece).astype(BF16)

    if mode == "back":
        outs[-1][0:1] = jnp.sum(acc[0], axis=0, keepdims=True)
        outs[-1][1:2] = jnp.sum(acc[1], axis=0, keepdims=True)
    stores = [pltpu.make_async_copy(v, r, local.at[5 + n_aux + k]) for k, (v, r) in enumerate(zip(outs, out_refs))]
    for store in stores:
        store.start()
    for copy in sent + [far_x, far_y, plain_x, plain_y, more_x, more_y]:
        copy.wait_send()
    if n_swap:
        swap_finish()
    if spread:
        spread_block(cut, 10, block, all_ref, send, recv, local.at[4])
    for store in stores:
        store.wait()


def group_fold(name, zs, mode, left, right, gains, aux, out_types, extras=(), kinds=()):
    across = mode != "one"
    rows, depth = left.shape[0] // 8, left.shape[1]
    width = gains.shape[1]
    cut = rows // 2
    spread = mode != "last"
    out_shape = [jax.ShapeDtypeStruct((8, rows, width), BF16)] * spread + out_types
    n, n_swap = len(aux), len(extras)
    n_sems = 23 if spread else 10
    return pl.pallas_call(
        functools.partial(fold_kernel, mode, across, zs, width // (8 * zs), n, len(out_types), kinds),
        out_shape=out_shape + swap_shapes(1, extras, kinds),
        in_specs=[ANY, ANY, ROWS] + [ANY] * (n + n_swap),
        out_specs=[ANY] * (spread + len(out_types) + n_swap),
        scratch_shapes=[pltpu.VMEM(a.shape, a.dtype) for a in list(aux) + out_types]
        + [
            pltpu.VMEM((4, 2 * rows, depth), BF16),
            pltpu.VMEM(right.shape, BF16),
            pltpu.VMEM((4, 2, rows, width), BF16),
            pltpu.VMEM((4, rows, width), BF16),
            pltpu.VMEM((cut, width), BF16),
            pltpu.VMEM((rows - cut, width), BF16),
            pltpu.VMEM((rows, width), BF16),
            pltpu.VMEM((rows, width), BF16),
            pltpu.VMEM((rows, width), BF16),
            pltpu.VMEM((2, SLAB, width), F32),
            pltpu.SemaphoreType.DMA((n_sems,)),
            pltpu.SemaphoreType.DMA((n_sems,)),
            pltpu.SemaphoreType.DMA((5 + n + len(out_types),)),
        ]
        + (swap_scratch(1, kinds) if n_swap else []),
        compiler_params=pltpu.CompilerParams(
            collective_id=name, has_side_effects=True, vmem_limit_bytes=50 * 2**20
        ),
        cost_estimate=pl.CostEstimate(flops=0, bytes_accessed=(200 if spread else 110) * 2**20, transcendentals=0),
    )(left.reshape(4, 2 * rows, depth), right, gains, *aux, *extras)


def turn_kernel(
    zs, piece, x_ref, in_ref, out_ref, gains_ref, first_ref, grad_ref,
    all_ref, kept_ref, right_ref, result_out, d_pre_out, sums_ref, dw_out, result_ref, d_pre_ref, dw_ref,
    first, grad, w_in, kept, left, right, part, got, near_x, near_y, from_x, from_y, whole, dw, acc,
    fold_send, fold_recv, all_send, all_recv, line_send, line_recv, local, x_local
):
    rows = first.shape[0]
    tile = left.shape[2]
    wide = right.shape[2]
    y, x, c = here()
    z = lax.axis_index("z")
    to_x, to_y, to_c = {"gx": 1 - x}, {"gy": 1 - y}, {"core": 1 - c}
    chips = [(1 - y) * 2 + 1 - x, y * 2 + 1 - x, (1 - y) * 2 + x, y * 2 + x]
    me, by_x, by_y, far = place(y, x, c), place(y, 1 - x, c), place(1 - y, x, c), place(1 - y, 1 - x, c)
    other, other_x, other_y, other_far = (
        place(y, x, 1 - c),
        place(y, 1 - x, 1 - c),
        place(1 - y, x, 1 - c),
        place(1 - y, 1 - x, 1 - c),
    )
    half = rows // 2
    most = -(-half // (2 * SLAB)) * SLAB
    lows = [(0, most), (half, half - most)]
    highs = [(most, half - most), (2 * half - most, most)]
    top, bottom = pl.ds(0, half), pl.ds(half, half)
    sent = []

    def remote(sems, k, src, dst, to):
        return pltpu.make_async_remote_copy(
            src_ref=src,
            dst_ref=dst,
            send_sem=sems[0].at[k],
            recv_sem=sems[1].at[k],
            device_id=to,
            device_id_type=MESH,
        )

    def push(sems, k, src, dst, to):
        copy = remote(sems, k, src, dst, to)
        copy.start()
        sent.append(copy)

    def landed(sems, k, dst):
        remote(sems, k, dst, dst, to_c).wait_recv()

    folds, alls, lines = (fold_send, fold_recv), (all_send, all_recv), (line_send, line_recv)

    load_out = pltpu.make_async_copy(out_ref, right.at[z], local.at[0])
    load_in = pltpu.make_async_copy(in_ref, w_in, local.at[1])
    load_first = pltpu.make_async_copy(first_ref, first, local.at[2])
    load_grad = pltpu.make_async_copy(grad_ref, grad, local.at[3])

    def load_x(g):
        return pltpu.make_async_copy(x_ref.at[g], whole.at[g], x_local.at[g])

    load_out.start()

    barrier = pltpu.get_barrier_semaphore()
    for to in (to_x, to_y, to_c):
        pl.semaphore_signal(barrier, inc=1, device_id=to, device_id_type=MESH)

    @pl.when(z > 0)
    def _():
        pl.semaphore_signal(barrier, inc=1, device_id={"z": z - 1}, device_id_type=MESH)

    @pl.when(z < zs - 1)
    def _():
        pl.semaphore_signal(barrier, inc=1, device_id={"z": z + 1}, device_id_type=MESH)

    inside = (z > 0) & (z < zs - 1)

    @pl.when(inside)
    def _():
        pl.semaphore_wait(barrier, 5)

    @pl.when(jnp.logical_not(inside))
    def _():
        pl.semaphore_wait(barrier, 4)

    def shard_of(step, up):
        return z - step if up else z + step

    def hop(step, up):
        ref = right.at[shard_of(step, up)]
        return remote(lines, 2 * step + (0 if up else 1), ref, ref, {"z": z + 1 if up else z - 1})

    def sends(step, up):
        return (z >= step) & (z < zs - 1) if up else (z <= zs - 1 - step) & (z > 0)

    def gets(step, up):
        return z >= step + 1 if up else z <= zs - 2 - step

    def line_serve(step):
        for up in (True, False):

            @pl.when(gets(step - 1, up) & sends(step, up))
            def _(up=up):
                landed(lines, 2 * (step - 1) + (0 if up else 1), right.at[shard_of(step, up)])
                hop(step, up).start()

    def line_take(step):
        for up in (True, False):

            @pl.when(gets(step - 1, up) & jnp.logical_not(sends(step, up)))
            def _(up=up):
                landed(lines, 2 * (step - 1) + (0 if up else 1), right.at[shard_of(step, up)])

    load_out.wait()
    for up in (True, False):

        @pl.when(sends(0, up))
        def _(up=up):
            hop(0, up).start()

    load_in.start()
    for g in range(8):
        load_x(g).start()


    load_in.wait()

    @pl.loop(0, 8)
    def _(g):
        @pl.when(g == 6)
        def _():
            line_serve(1)

        load_x(g).wait()
        projected = dot(whole[g], w_in[...])
        gate, up = projected[:, :tile], projected[:, tile:]
        act, slope = gate_parts(gate)
        left[g] = (act * up).astype(BF16)
        kept[g] = jnp.concatenate([up * slope, act], axis=1).astype(BF16)

    load_first.start()
    load_grad.start()
    keep = pltpu.make_async_copy(kept, kept_ref, local.at[4])
    keep.start()

    def add(k, extra, start, offset, at):
        @pl.loop(0, half // SLAB)
        def _(step):
            row = pl.ds(pl.multiple_of(start + step * SLAB, SLAB), SLAB)
            of = pl.ds(pl.multiple_of(start - offset + step * SLAB, SLAB), SLAB)
            part[k, c, row, at] = (part[k, c, row, at].astype(F32) + extra[of, at].astype(F32)).astype(BF16)

    def chip_sum(k, at):
        add(k, got.at[k], 0, 0, at)
        add(k, got.at[k], half, 0, at)

    def product(k, block, at):
        found = dot(left[pl.ds(2 * chips[k], 2)].reshape(2 * rows, tile), right[block])
        part[k, 0, :, at] = found[:rows].astype(BF16)
        part[k, 1, :, at] = found[rows:].astype(BF16)

    def block_at(i):
        if i == 0:
            return z
        below = z < zs // 2
        near = jnp.where(below, z, zs - 1 - z)
        spot = jnp.where(i <= 2 * near, jnp.where(i % 2 == 1, near - (i + 1) // 2, near + i // 2), i)
        return jnp.where(below, spot, zs - 1 - spot)

    def block_cols(i):
        return pl.ds(pl.multiple_of(block_at(i) * wide, wide), wide)

    def fold_start(i):
        b, block, at = 8 * i, block_at(i), block_cols(i)
        rest = pl.ds(1, 3)
        product(0, block, at)
        push(folds, b, part.at[0, 1 - c, :, at], got.at[0, :, at], to_c)
        for k in (1, 2, 3):
            product(k, block, at)
        push(folds, b + 1, part.at[rest, 1 - c, :, at], got.at[rest, :, at], to_c)
        landed(folds, b, got.at[0, :, at])
        chip_sum(0, at)
        push(folds, b + 2, part.at[0, c, top, at], near_x.at[:, at], to_x)
        push(folds, b + 3, part.at[0, c, bottom, at], near_y.at[:, at], to_y)
        landed(folds, b + 1, got.at[rest, :, at])
        chip_sum(1, at)
        push(folds, b + 4, part.at[1, c, top, at], from_x.at[top, at], to_x)
        chip_sum(2, at)
        push(folds, b + 5, part.at[2, c, bottom, at], from_y.at[bottom, at], to_y)

    def fold_end(i):
        b, at = 8 * i, block_cols(i)
        landed(folds, b + 3, near_y.at[:, at])
        add(1, near_y, half, half, at)
        push(folds, b + 6, part.at[1, c, bottom, at], from_x.at[bottom, at], to_x)
        landed(folds, b + 2, near_x.at[:, at])
        add(2, near_x, 0, 0, at)
        push(folds, b + 7, part.at[2, c, top, at], from_y.at[top, at], to_y)

    gains = gains_ref[...]
    line_take(1)
    fold_start(0)
    fold_start(1)
    fold_end(0)
    for i in range(2, zs):
        if i < zs - 1:
            line_serve(i)
        fold_end(i - 1)
        line_take(i)
        fold_start(i)
    fold_end(zs - 1)
    carry = pltpu.make_async_copy(right, right_ref, local.at[5])
    carry.start()
    load_first.wait()
    load_grad.wait()
    acc[...] = jnp.zeros_like(acc)
    for i in range(zs):
        at = block_cols(i)
        landed(folds, 8 * i + 4, from_x.at[top, at])
        landed(folds, 8 * i + 5, from_y.at[bottom, at])
        landed(folds, 8 * i + 6, from_x.at[bottom, at])
        landed(folds, 8 * i + 7, from_y.at[top, at])

    def low(i):
        return pl.ds(*lows[i])

    def high(i):
        return pl.ds(*highs[i])

    def span(i):
        return pl.ds(i * half, half)

    def norm(i):
        @pl.loop(0, half // SLAB)
        def _(step):
            at = pl.ds(pl.multiple_of(i * half + step * SLAB, SLAB), SLAB)
            total = part[3, c, at].astype(F32) + got[3, at].astype(F32)
            total += from_x[at].astype(F32) + from_y[at].astype(F32)
            dy = grad[at].astype(F32)
            result, d_pre, terms = second_norm(total, first[at], dy, gains)
            result_ref[at] = result.astype(BF16)
            d_pre_ref[at] = d_pre
            whole[me, at] = d_pre.astype(BF16)
            acc[0] += terms
            acc[1] += dy

        b = 13 * i
        push(alls, b, whole.at[me, low(i)], whole.at[me, low(i)], to_x)
        push(alls, b + 1, whole.at[me, high(i)], whole.at[me, high(i)], to_y)
        push(alls, b + 2, whole.at[me, high(i)], whole.at[me, high(i)], to_x)
        push(alls, b + 3, whole.at[me, low(i)], whole.at[me, low(i)], to_y)
        push(alls, b + 4, whole.at[me, span(i)], whole.at[me, span(i)], to_c)

    def pass_on(i, k, slot, at, onward):
        ref = whole.at[slot, at]
        landed(alls, 13 * i + k, ref)
        for where, to in onward:
            push(alls, 13 * i + where, ref, ref, to)

    def spread_first(i):
        pass_on(i, 0, by_x, low(i), [(5, to_y), (7, to_c)])
        pass_on(i, 1, by_y, high(i), [(6, to_x), (8, to_c)])

    def spread_rest(i):
        pass_on(i, 2, by_x, high(i), [(9, to_c)])
        pass_on(i, 3, by_y, low(i), [(10, to_c)])

    def spread_far(i):
        pass_on(i, 5, far, low(i), [(11, to_c)])
        pass_on(i, 6, far, high(i), [(12, to_c)])

    outward = []

    def gradient(k, last=False, first_one=False):
        pair = pl.ds(2 * chips[k], 2)
        outward.append(pltpu.make_async_copy(whole.at[pair], all_ref.at[pair], local.at[6 + k]))
        outward[-1].start()

        @pl.loop(0, zs)
        def _(block):
            at = pl.ds(pl.multiple_of(block * wide, wide), wide)
            found = dot_rows(left[pair].reshape(2 * rows, tile), whole[pair, :, at].reshape(2 * rows, wide))
            if first_one:
                dw[block] = found
            elif last:
                dw_ref[block] = (dw[block] + found).astype(BF16)
                pltpu.make_async_copy(dw_ref.at[block], dw_out.at[block], x_local.at[block]).start()
            else:
                dw[block] += found

    norm(0)
    norm(1)
    stores = [
        pltpu.make_async_copy(result_ref, result_out, local.at[10]),
        pltpu.make_async_copy(d_pre_ref, d_pre_out, local.at[11]),
    ]
    for store in stores:
        store.start()
    spread_first(0)
    for i in (0, 1):
        landed(alls, 13 * i + 4, whole.at[other, span(i)])
    gradient(3, first_one=True)
    spread_rest(0)
    spread_first(1)
    spread_rest(1)
    for i in (0, 1):
        landed(alls, 13 * i + 7, whole.at[other_x, low(i)])
        landed(alls, 13 * i + 9, whole.at[other_x, high(i)])
    gradient(1)
    spread_far(0)
    for i in (0, 1):
        landed(alls, 13 * i + 8, whole.at[other_y, high(i)])
        landed(alls, 13 * i + 10, whole.at[other_y, low(i)])
    gradient(2)
    sums_ref[0:1] = jnp.sum(acc[0], axis=0, keepdims=True)
    sums_ref[1:2] = jnp.sum(acc[1], axis=0, keepdims=True)
    spread_far(1)
    for i in (0, 1):
        landed(alls, 13 * i + 11, whole.at[other_far, low(i)])
        landed(alls, 13 * i + 12, whole.at[other_far, high(i)])
    gradient(0, last=True)
    for block in range(zs):
        pltpu.make_async_copy(dw_ref.at[block], dw_out.at[block], x_local.at[block]).wait()
    for copy in outward + [keep, carry] + stores:
        copy.wait()
    for copy in sent:
        copy.wait_send()
    for step in range(zs - 1):
        for up in (True, False):

            @pl.when(sends(step, up))
            def _(step=step, up=up):
                hop(step, up).wait_send()


def turn(zs, x, w_in, w_out, gains, first, grad):
    rows = x.shape[0] // 8
    units, wide = w_out.shape
    width = gains.shape[1]
    half = rows // 2
    by_z = (zs, units, wide)
    return pl.pallas_call(
        functools.partial(turn_kernel, zs, width // (8 * zs)),
        out_shape=[
            jax.ShapeDtypeStruct((8, rows, width), BF16),
            jax.ShapeDtypeStruct((8, rows, 2 * units), BF16),
            jax.ShapeDtypeStruct(by_z, BF16),
            jax.ShapeDtypeStruct((rows, width), BF16),
            jax.ShapeDtypeStruct((rows, width), F32),
            jax.ShapeDtypeStruct((8, width), F32),
            jax.ShapeDtypeStruct(by_z, BF16),
        ],
        in_specs=[ANY, ANY, ANY, ROWS, ANY, ANY],
        out_specs=[ANY] * 5 + [ROWS, ANY],
        scratch_shapes=[
            pltpu.VMEM((rows, width), BF16),
            pltpu.VMEM((rows, width), F32),
            pltpu.VMEM(by_z, BF16),
            pltpu.VMEM((rows, width), F32),
            pltpu.VMEM((rows, width), BF16),
            pltpu.VMEM(w_in.shape, BF16),
            pltpu.VMEM((8, rows, 2 * units), BF16),
            pltpu.VMEM((8, rows, units), BF16),
            pltpu.VMEM(by_z, BF16),
            pltpu.VMEM((4, 2, rows, width), BF16),
            pltpu.VMEM((4, rows, width), BF16),
            pltpu.VMEM((half, width), BF16),
            pltpu.VMEM((half, width), BF16),
            pltpu.VMEM((rows, width), BF16),
            pltpu.VMEM((rows, width), BF16),
            pltpu.VMEM((8, rows, width), BF16),
            pltpu.VMEM(by_z, F32),
            pltpu.VMEM((2, SLAB, width), F32),
            pltpu.SemaphoreType.DMA((8 * zs,)),
            pltpu.SemaphoreType.DMA((8 * zs,)),
            pltpu.SemaphoreType.DMA((26,)),
            pltpu.SemaphoreType.DMA((26,)),
            pltpu.SemaphoreType.DMA((2 * (zs - 1),)),
            pltpu.SemaphoreType.DMA((2 * (zs - 1),)),
            pltpu.SemaphoreType.DMA((12,)),
            pltpu.SemaphoreType.DMA((8,)),
        ],
        compiler_params=pltpu.CompilerParams(collective_id=1, has_side_effects=True, vmem_limit_bytes=60 * 2**20),
        cost_estimate=pl.CostEstimate(flops=0, bytes_accessed=380 * 2**20, transcendentals=0),
    )(x.reshape(8, rows, width), w_in, w_out, gains, first, grad)


def swap_kernel(zs, kinds, *refs):
    n = len(kinds)
    greet([name for _, name in swap_peers(zs, kinds)])
    swap_begin(zs, kinds, refs[:n], refs[n : 2 * n], *refs[2 * n :])()


def group_swap(name, zs, arrays, kinds):
    n = len(arrays)
    return pl.pallas_call(
        functools.partial(swap_kernel, zs, kinds),
        out_shape=swap_shapes(zs, arrays, kinds),
        in_specs=[ANY] * n,
        out_specs=[ANY] * n,
        scratch_shapes=swap_scratch(zs, kinds),
        compiler_params=pltpu.CompilerParams(collective_id=name, has_side_effects=True),
        cost_estimate=pl.CostEstimate(flops=0, bytes_accessed=50 * 2**20, transcendentals=0),
    )(*arrays)


def enter_kernel(zs, kinds, x_ref, grad_ref, *refs):
    n = len(kinds)
    blocks, x_all, grad_out, outs, refs = refs[:n], refs[n], refs[n + 1], refs[n + 2 : 2 * n + 2], refs[2 * n + 2 :]
    x_rows, sems = refs[0], refs[1:]
    rows, width = x_ref.shape
    greet([name for _, name in swap_peers(zs, kinds)])
    finish = swap_begin(zs, kinds, blocks, outs, *sems[:3])
    for ref, out in ((x_ref, x_rows), (grad_ref, grad_out)):

        @pl.loop(0, rows // SLAB)
        def _(step, ref=ref, out=out):
            at = pl.ds(pl.multiple_of(step * SLAB, SLAB), SLAB)
            out[at] = by_rows(ref[at].astype(F32), zs, width // (8 * zs)).astype(BF16)

    spread_block(rows // 2, 0, x_rows, x_all, *sems[3:])
    finish()


def enter(zs, x, grad, arrays, kinds):
    n = len(arrays)
    return pl.pallas_call(
        functools.partial(enter_kernel, zs, kinds),
        out_shape=[jax.ShapeDtypeStruct((8,) + x.shape, x.dtype), jax.ShapeDtypeStruct(grad.shape, grad.dtype)]
        + swap_shapes(zs, arrays, kinds),
        in_specs=[ROWS] * 2 + [ANY] * n,
        out_specs=[ANY, ROWS] + [ANY] * n,
        scratch_shapes=[pltpu.VMEM(x.shape, x.dtype)]
        + swap_scratch(zs, kinds)
        + [pltpu.SemaphoreType.DMA((13,)), pltpu.SemaphoreType.DMA((13,)), pltpu.SemaphoreType.DMA],
        compiler_params=pltpu.CompilerParams(collective_id=3, has_side_effects=True, vmem_limit_bytes=56 * 2**20),
        cost_estimate=pl.CostEstimate(flops=0, bytes_accessed=150 * 2**20, transcendentals=0),
    )(x, grad, *arrays)


def ff_kernel(x_ref, w_ref, hidden_ref, kept_ref):
    tile = hidden_ref.shape[1]
    projected = dot(x_ref[...], w_ref[...])
    gate, up = projected[:, :tile], projected[:, tile:]
    act, slope = gate_parts(gate)
    hidden_ref[...] = (act * up).astype(BF16)
    kept_ref[...] = jnp.concatenate([up * slope, act], axis=1).astype(BF16)


def ff_back_kernel(grad_ref, w_ref, kept_ref, out_ref):
    zs, _, wide = w_ref.shape
    d_hidden = dot_cols(grad_ref[:, :wide], w_ref[0])
    for z in range(1, zs):
        d_hidden += dot_cols(grad_ref[:, z * wide : (z + 1) * wide], w_ref[z])
    out_ref[...] = (jnp.concatenate([d_hidden, d_hidden], axis=1) * kept_ref[...].astype(F32)).astype(BF16)


FF_ROWS = 256


def ff_rows(width):
    return pl.BlockSpec((FF_ROWS, width), lambda i: (i, 0))


def ff_forward(x, w):
    rows, depth = x.shape
    wide = w.shape[1]
    return pl.pallas_call(
        ff_kernel,
        grid=(rows // FF_ROWS,),
        in_specs=[ff_rows(depth), pl.BlockSpec((depth, wide), lambda i: (0, 0))],
        out_specs=[ff_rows(wide // 2), ff_rows(wide)],
        out_shape=[jax.ShapeDtypeStruct((rows, wide // 2), BF16), jax.ShapeDtypeStruct((rows, wide), BF16)],
        compiler_params=PARAMS,
        cost_estimate=pl.CostEstimate(flops=2 * rows * depth * wide, bytes_accessed=20 * 2**20, transcendentals=0),
    )(x, w)


def ff_backward(grad, w, kept):
    rows, depth = grad.shape
    wide = kept.shape[1]
    return pl.pallas_call(
        ff_back_kernel,
        grid=(rows // FF_ROWS,),
        in_specs=[ff_rows(depth), pl.BlockSpec(w.shape, lambda i: (0, 0, 0)), ff_rows(wide)],
        out_specs=ff_rows(wide),
        out_shape=jax.ShapeDtypeStruct((rows, wide), BF16),
        compiler_params=PARAMS,
        cost_estimate=pl.CostEstimate(flops=rows * depth * wide, bytes_accessed=20 * 2**20, transcendentals=0),
    )(grad, w, kept)


def cut_kernel(in_ref, out_ref, in_blocks, out_blocks, wide):
    group, _, double = in_blocks.shape
    tile, ff = double // 2, out_ref.shape[1]
    span = group * tile
    odd = ff % 128
    live = lax.broadcasted_iota(jnp.int32, (in_ref.shape[0], span), 1) < ff
    wide[...] = jnp.zeros_like(wide)
    wide[:, : 2 * ff] = in_ref[...].astype(F32)
    gate = jnp.where(live, wide[:, :span], 0.0)
    up = pltpu.roll(wide[:, ff - odd : ff - odd + span], span - odd, 1)
    up = jnp.where(live, up, 0.0)
    wide[:, :span] = jnp.zeros_like(live, F32)
    wide[:, :ff] = out_ref[...].astype(F32)
    down = wide[:, :span]
    for g in range(group):
        at = slice(g * tile, (g + 1) * tile)
        in_blocks[g] = jnp.concatenate([gate[:, at], up[:, at]], axis=1).astype(BF16)
        out_blocks[g] = down[:, at].astype(BF16)


def cut_ff(w_in, w_out, group, tile):
    rows, ff = w_out.shape
    return pl.pallas_call(
        cut_kernel,
        grid=(rows // 16,),
        in_specs=[pl.BlockSpec((16, 2 * ff), lambda i: (i, 0)), pl.BlockSpec((16, ff), lambda i: (i, 0))],
        out_specs=[
            pl.BlockSpec((group, 16, 2 * tile), lambda i: (0, i, 0)),
            pl.BlockSpec((group, 16, tile), lambda i: (0, i, 0)),
        ],
        out_shape=[
            jax.ShapeDtypeStruct((group, rows, 2 * tile), BF16),
            jax.ShapeDtypeStruct((group, rows, tile), BF16),
        ],
        scratch_shapes=[pltpu.VMEM((16, -(-(ff + group * tile) // 128) * 128), F32)],
        compiler_params=SMALL,
    )(w_in, w_out)


def join_kernel(in_blocks, out_blocks, in_ref, out_ref):
    group, _, double = in_blocks.shape
    tile, ff = double // 2, out_ref.shape[1]
    odd = ff % 128
    blocks = [in_blocks[g].astype(F32) for g in range(group)]
    gate = jnp.concatenate([block[:, :tile] for block in blocks], axis=1)
    up = jnp.concatenate([block[:, tile:] for block in blocks], axis=1)
    up = pltpu.roll(up, odd, 1)
    lane = lax.broadcasted_iota(jnp.int32, (up.shape[0], 128), 1)
    in_ref[:, : ff - odd] = gate[:, : ff - odd]
    in_ref[:, ff - odd : ff - odd + 128] = jnp.where(lane < odd, gate[:, ff - odd : ff - odd + 128], up[:, :128])
    in_ref[:, ff - odd + 128 :] = up[:, 128 : ff + odd]
    down = jnp.concatenate([out_blocks[g].astype(F32) for g in range(group)], axis=1)
    out_ref[...] = down[:, :ff]


def join_ff(in_blocks, out_blocks, ff):
    group, rows, tile = out_blocks.shape
    return pl.pallas_call(
        join_kernel,
        grid=(rows // 16,),
        in_specs=[
            pl.BlockSpec((group, 16, 2 * tile), lambda i: (0, i, 0)),
            pl.BlockSpec((group, 16, tile), lambda i: (0, i, 0)),
        ],
        out_specs=[pl.BlockSpec((16, 2 * ff), lambda i: (i, 0)), pl.BlockSpec((16, ff), lambda i: (i, 0))],
        out_shape=[jax.ShapeDtypeStruct((rows, 2 * ff), F32), jax.ShapeDtypeStruct((rows, ff), F32)],
        compiler_params=SMALL,
    )(in_blocks, out_blocks)


def closing_kernel(zs, sum_ref, rows_ref, qkv_ref, dense_ref, total_ref, got, mine, lines, *refs):
    send, recv, local, line_send, line_recv = refs
    y, x, c = here()
    z = lax.axis_index("z")
    me = place(y, x, c)
    wide = got.shape[2]
    width = wide // 3
    piece = got.shape[1]
    found = swap_peers(zs, ("line",))
    greet([name for _, name in found])
    copies, comes = [], []
    for k, (peer, name) in enumerate(found[:7]):
        sems = dict(send_sem=send.at[k], recv_sem=recv.at[k], device_id=name, device_id_type=MESH)
        src = rows_ref.at[peer, :, pl.ds(0, wide)]
        copies.append(pltpu.make_async_remote_copy(src_ref=src, dst_ref=got.at[me], **sems))
        comes.append(pltpu.make_async_remote_copy(src_ref=got.at[peer], dst_ref=got.at[peer], **sems))
    for k, (peer, name) in enumerate(found[7:]):
        sems = dict(send_sem=line_send.at[k], recv_sem=line_recv.at[k], device_id=name, device_id_type=MESH)
        copies.append(pltpu.make_async_remote_copy(src_ref=sum_ref, dst_ref=lines.at[z], **sems))
        comes.append(pltpu.make_async_remote_copy(src_ref=lines.at[peer], dst_ref=lines.at[peer], **sems))
    for copy in copies:
        copy.start()
    keeps = [
        pltpu.make_async_copy(rows_ref.at[me, :, pl.ds(0, wide)], got.at[me], local.at[0]),
        pltpu.make_async_copy(sum_ref, lines.at[z], local.at[1]),
        pltpu.make_async_copy(rows_ref.at[:, :, pl.ds(wide, width)], mine, local.at[2]),
    ]
    for keep in keeps:
        keep.start()
    keeps[2].wait()
    for at in range(0, piece, 16):
        rows = jnp.concatenate([mine[g, at : at + 16] for g in range(8)], axis=1).astype(F32)
        dense_ref[at : at + 16] = rows
    for come in comes:
        come.wait_recv()
    for keep in keeps[:2]:
        keep.wait()
    for g in range(8):
        for j in range(3):
            at = pl.ds(j * D + g * width, width)
            qkv_ref[:, at] = got[g, :, j * width : (j + 1) * width].astype(F32)
    total = lines[0]
    for k in range(1, zs):
        total += lines[k]
    part = total[:, :piece]
    for k in range(1, zs):
        part = jnp.where(z == k, total[:, k * piece : (k + 1) * piece], part)
    total_ref[...] = part
    for copy in copies:
        copy.wait_send()


def closing(zs, sums, rows):
    _, piece, columns = rows.shape
    width = columns // 4
    return pl.pallas_call(
        functools.partial(closing_kernel, zs),
        out_shape=[
            jax.ShapeDtypeStruct((piece, 3 * D), F32),
            jax.ShapeDtypeStruct((piece, D), F32),
            jax.ShapeDtypeStruct((8, piece), F32),
        ],
        in_specs=[ROWS, ANY],
        out_specs=[ROWS] * 3,
        scratch_shapes=[
            pltpu.VMEM((8, piece, 3 * width), BF16),
            pltpu.VMEM((8, piece, width), BF16),
            pltpu.VMEM((zs, 8, width), F32),
            pltpu.SemaphoreType.DMA((7,)),
            pltpu.SemaphoreType.DMA((7,)),
            pltpu.SemaphoreType.DMA((3,)),
            pltpu.SemaphoreType.DMA((zs - 1,)),
            pltpu.SemaphoreType.DMA((zs - 1,)),
        ],
        compiler_params=pltpu.CompilerParams(collective_id=5, has_side_effects=True, vmem_limit_bytes=24 * 2**20),
        cost_estimate=pl.CostEstimate(flops=0, bytes_accessed=50 * 2**20, transcendentals=0),
    )(sums, rows)


def on_device(sizes, x_in, d_out, w_qkv, w_dense, w_in, w_out, gone, bone, gtwo, btwo, flags, span_start, span_len):
    gy, gx, cores, zs = sizes
    piece = w_qkv.shape[0]
    ff = w_out.shape[1]
    group = gy * gx * cores
    width = D // group
    tile = -(-ff // (group * 64)) * 64
    own = gy == 2

    def permute(array):
        lead = array.shape[:-1]
        return jnp.swapaxes(array.reshape(lead + (group, zs, piece)), -3, -2).reshape(lead + (D,))

    def restore(array):
        lead = array.shape[:-1]
        return jnp.swapaxes(array.reshape(lead + (zs, group, piece)), -3, -2).reshape(lead + (D,))

    def swap(name, arrays, kinds):
        if own:
            return group_swap(name, zs, arrays, kinds)
        ways = {
            "swap": lambda a: lax.all_to_all(a, GROUP, 0, 0, tiled=True),
            "group": lambda a: lax.all_gather(a, GROUP, axis=0),
            "line": lambda a: lax.all_gather(a, "z", axis=0),
        }
        return [ways[k](a) for a, k in zip(arrays, kinds)]

    def spread_rows(block):
        return lax.all_gather(block, GROUP, axis=0, tiled=True)

    rows_f32 = jax.ShapeDtypeStruct((SEQ_LEN, D), F32)
    rows_low = jax.ShapeDtypeStruct((SEQ_LEN, D), BF16)
    sums_type = jax.ShapeDtypeStruct((8, D), F32)

    def fold(partial):
        return lax.psum_scatter(partial.astype(BF16), GROUP, scatter_dimension=0, tiled=True).astype(F32)

    def stack_sums(*arrays):
        return jnp.pad(jnp.stack([jnp.sum(a, axis=0) for a in arrays]), ((0, 6), (0, 0)))

    def fold_one(left, right, x, gains):
        if own:
            kinds = [rows_f32, rows_f32, jax.ShapeDtypeStruct((SEQ_LEN, 128), F32)]
            whole, first, normal, inverse = group_fold(0, zs, "one", left, right, gains, [x], kinds)
            return whole.reshape(left.shape[0], D), first, normal, inverse
        first, normal, inverse = first_norm(permute(deep_alpha * x.astype(F32) + fold(dot(left, right))), gains)
        return spread_rows(first.astype(BF16)), first, normal, inverse

    def ff_turn(x, w_in, w_out, first, grad, gains):
        if own:
            whole, kept, w_out, result, d_pre, sums, d_out = turn(zs, x, w_in, w_out, gains, first, grad)
            rows = x.shape[0]
            return whole.reshape(rows, D), kept.reshape(rows, -1), w_out, result, d_pre, sums, d_out
        w_out = lax.all_gather(w_out, "z", axis=0)
        hidden, kept = ff_forward(x, w_in)
        grad = grad.astype(F32)
        right = jnp.swapaxes(w_out, 0, 1).reshape(-1, D)
        result, d_pre, terms = second_norm(fold(dot(hidden, right)), first, grad, gains)
        whole = spread_rows(d_pre.astype(BF16))
        d_out = jnp.swapaxes(dot_rows(hidden, whole).reshape(-1, zs, D // zs), 0, 1).astype(BF16)
        return whole, kept, w_out, result.astype(BF16), d_pre, stack_sums(terms, grad), d_out

    def fold_back(left, right, d_pre_two, normal, inverse, gains):
        if own:
            kinds = [rows_f32, sums_type]
            whole, d_pre, sums = group_fold(7, zs, "back", left, right, gains, [d_pre_two, normal, inverse], kinds)
            return whole.reshape(left.shape[0], D), d_pre, sums
        d_pre, terms, d_first = first_back(fold(dot_cols(left, right)), d_pre_two, normal, inverse, gains)
        return spread_rows(restore(d_pre).astype(BF16)), d_pre, stack_sums(terms, d_first)

    def fold_last(left, right, d_pre, gains, extras, kinds):
        if own:
            return group_fold(8, zs, "last", left, right, gains, [d_pre], [rows_low], extras, kinds)
        out = restore((deep_alpha * d_pre + fold(dot_cols(left, right))).astype(BF16))
        return [out] + swap(8, extras, kinds)

    def gather(block):
        return lax.all_gather(block, "z", axis=0, tiled=True)

    def scatter(partial):
        return lax.psum_scatter(partial.astype(BF16), "z", scatter_dimension=0, tiled=True)

    masked = jnp.max(flags) > 0
    prefix = jnp.where(masked, SEQ_LEN, SEQ_LEN - span_len[0])
    info = jnp.concatenate([gone, bone, gtwo, btwo, jnp.stack([prefix, span_start[0]]).astype(BF16)])
    info = jnp.pad(info[None, :], ((0, 15), (0, -info.shape[0] % 128)))

    qkv_blocks = jnp.moveaxis(w_qkv.reshape(piece, 3, group, width), 2, 0).reshape(group, piece, 3 * width)
    w_dense_part = gather(w_dense)
    qkv_blocks, info = swap(2, [qkv_blocks, info], ("swap", "group"))
    w_qkv_part = gather(qkv_blocks.reshape(group * piece, 3 * width))
    info = info[:, 0]
    place_info = info[:, 4 * piece : 4 * piece + 2].astype(jnp.int32)
    prefix, start = place_info[:, 0], place_info[:, 1]
    cosine, sine = tables(prefix, start)
    in_blocks, out_blocks = cut_ff(w_in, w_out, group, tile)
    info = jnp.pad(info, ((0, -group % 16), (0, 0)))
    in_blocks, out_blocks, qkv_blocks, w_dense_part, cosine, sine = lax.optimization_barrier(
        (in_blocks, out_blocks, qkv_blocks, w_dense_part, cosine, sine)
    )
    swapped, kinds = [in_blocks, out_blocks, info], ("swap", "swap", "line")
    if own:
        x_all, grad_two, in_blocks, out_blocks, info = enter(zs, x_in, d_out, swapped, kinds)
        x_all = x_all.reshape(group * SEQ_LEN, D)
    else:
        x_all, grad_two = spread_rows(permute(x_in)), permute(d_out)
        in_blocks, out_blocks, info = swap(3, swapped, kinds)
    w_in_part = gather(in_blocks.reshape(group * piece, 2 * tile))
    out_rows = out_blocks.reshape(group * piece, tile).T
    gains = info[:, :group, : 4 * piece].astype(F32).reshape(zs, group, 4, piece)
    gains = jnp.pad(jnp.transpose(gains, (2, 0, 1, 3)).reshape(4, D), ((0, 4), (0, 0)))
    w_qkv_part, x_all, gains, out_rows = lax.optimization_barrier((w_qkv_part, x_all, gains, out_rows))
    packed = dot(x_all, w_qkv_part)
    qkv, context = attend(prefix, packed, cosine, sine)
    first_all, first, normal_one, inverse_one = fold_one(context, w_dense_part, x_in, gains)
    d_branch, kept, w_out_part, layer_out, d_pre_two, sums_two, d_w_out = ff_turn(
        first_all, w_in_part, out_rows, first, grad_two, gains
    )
    layer_out = restore(layer_out)
    d_w_out = lax.psum_scatter(d_w_out, "z", scatter_dimension=0)
    d_projected = ff_backward(d_branch, w_out_part, kept)
    d_w_in = dot_rows(first_all, d_projected).astype(BF16)
    d_w_in, d_projected = lax.optimization_barrier((d_w_in, d_projected))
    d_w_in = scatter(d_w_in)
    d_attn, d_pre_one, sums_one = fold_back(d_projected, w_in_part, d_pre_two, normal_one, inverse_one, gains)
    d_attn, d_w_out = lax.optimization_barrier((d_attn, d_w_out))
    d_context = dot_cols(d_attn, w_dense_part).astype(BF16)
    d_packed = attend_back(prefix, qkv, d_context, cosine, sine)
    d_w_qkv = dot_rows(x_all, d_packed).astype(BF16)
    d_dense = dot_rows(context, d_attn).astype(BF16).reshape(zs, piece, group, width)
    d_dense = jnp.swapaxes(d_dense, 1, 2).reshape(D, width)
    d_w_qkv = with_layout_constraint(jnp.concatenate([d_w_qkv, d_dense], axis=1), Layout((0, 1)))
    sums = jnp.concatenate([sums_one[:2], sums_two[:2], jnp.zeros((4, D), F32)])
    d_packed, d_w_qkv, d_w_in, sums = lax.optimization_barrier((d_packed, d_w_qkv, d_w_in, sums))
    d_w_qkv = scatter(d_w_qkv)
    d_w_in, d_w_out = d_w_in.reshape(group, piece, 2 * tile), d_w_out.T.reshape(group, piece, tile)
    d_input, d_w_in, d_w_out, sums = fold_last(
        d_packed, w_qkv_part, d_pre_one, gains, [d_w_in, d_w_out, sums], ("swap", "swap", "group")
    )
    sums = jnp.sum(sums, axis=0).reshape(8, zs, group, piece)
    sums = lax.dynamic_index_in_dim(sums, lax.axis_index(GROUP), 2, keepdims=False).reshape(8, width)
    out_in, out_out = join_ff(d_w_in, d_w_out, ff)
    out_in, out_out, d_input, d_w_qkv, sums = lax.optimization_barrier((out_in, out_out, d_input, d_w_qkv, sums))
    if own:
        out_qkv, out_dense, sums = closing(zs, sums, d_w_qkv.reshape(group, piece, 4 * width))
    else:
        out_dense = d_w_qkv[:, 3 * width :].reshape(group, piece, width)
        out_dense = jnp.swapaxes(out_dense, 0, 1).reshape(piece, D).astype(F32)
        d_w_qkv = d_w_qkv[:, : 3 * width].reshape(group, piece, 3 * width)
        d_w_qkv, sums = swap(5, [d_w_qkv, sums], ("swap", "line"))
        out_qkv = jnp.transpose(d_w_qkv.astype(F32).reshape(group, piece, 3, width), (1, 2, 0, 3))
        out_qkv = out_qkv.reshape(piece, 3 * D)
        sums = jnp.sum(sums, axis=0).reshape(8, zs, piece)
        sums = lax.dynamic_index_in_dim(sums, lax.axis_index("z"), 1, keepdims=False)
    return layer_out, d_input, out_qkv, out_dense, out_in, out_out, sums[0], sums[1], sums[2], sums[3]


def solution(mesh):
    grp, shard = mesh.shape["grp"], mesh.shape["shard"]
    sizes = (grp // 4, 2, 2, shard)
    inner = Mesh(mesh.devices.reshape(sizes), ALL)
    rows, flat = P(ALL, None), P(ALL)
    return jax.shard_map(
        functools.partial(on_device, sizes),
        mesh=inner,
        in_specs=(rows,) * 6 + (flat,) * 7,
        out_specs=(rows,) * 6 + (flat,) * 4,
        check_vma=False,
    )
```

```python
import functools

import jax
import jax.numpy as jnp
from jax import lax
from jax.experimental import pallas as pl
from jax.experimental.pallas import tpu as pltpu
from jax.experimental.layout import Layout, with_layout_constraint
from jax.sharding import Mesh
from jax.sharding import PartitionSpec as P

HEADS = 16
HEAD = 128
SEQ_LEN = 224
D = HEADS * HEAD
deep_alpha = 6.928203230275509
norm_eps = 1e-05
far_below = -1e30
scale = HEAD ** (-0.5)

ALL = ("gy", "gx", "core", "z")
GROUP = ("gy", "gx", "core")
MESH = pl.DeviceIdType.MESH
F32 = jnp.float32
BF16 = jnp.bfloat16


def dot(left, right):
    return jnp.dot(left, right, preferred_element_type=F32)


def dot_rows(left, right):
    return lax.dot_general(left, right, (((0,), (0,)), ((), ())), preferred_element_type=F32)


def dot_cols(left, right):
    return lax.dot_general(left, right, (((1,), (1,)), ((), ())), preferred_element_type=F32)


def swap_halves(block):
    lane = lax.broadcasted_iota(jnp.int32, block.shape, 1)
    return jnp.where((lane & 32) == 0, pltpu.roll(block, 96, 1), pltpu.roll(block, 32, 1))


def seen(prefix):
    row = lax.broadcasted_iota(jnp.int32, (SEQ_LEN, SEQ_LEN), 0)
    col = lax.broadcasted_iota(jnp.int32, (SEQ_LEN, SEQ_LEN), 1)
    return (col < prefix) | (col <= row)


def softmax(queries, keys, visible):
    scores = jnp.where(visible, dot_cols(queries, keys), far_below)
    weights = jnp.exp(scores - jnp.max(scores, axis=1, keepdims=True))
    return weights / jnp.sum(weights, axis=1, keepdims=True)


def attend_kernel(prefix_ref, packed_ref, cos_ref, sin_ref, qkv_ref, context_ref):
    width = context_ref.shape[1]
    visible = seen(prefix_ref[pl.program_id(0)])
    cosine = cos_ref[0]
    sine = sin_ref[0]
    for head in range(width // HEAD):
        at = pl.ds(head * HEAD, HEAD)
        at_k = pl.ds(width + head * HEAD, HEAD)
        at_v = pl.ds(2 * width + head * HEAD, HEAD)
        raw = packed_ref[:, at]
        queries = ((raw * cosine + swap_halves(raw) * sine) * scale).astype(BF16)
        raw = packed_ref[:, at_k]
        keys = (raw * cosine + swap_halves(raw) * sine).astype(BF16)
        values = packed_ref[:, at_v].astype(BF16)
        qkv_ref[:, at] = queries
        qkv_ref[:, at_k] = keys
        qkv_ref[:, at_v] = values
        probs = softmax(queries, keys, visible).astype(BF16)
        context_ref[:, at] = dot(probs, values).astype(BF16)


def attend_back_kernel(prefix_ref, qkv_ref, d_context_ref, cos_ref, sin_ref, d_packed_ref):
    width = d_context_ref.shape[1]
    visible = seen(prefix_ref[pl.program_id(0)])
    cosine = cos_ref[0]
    sine = sin_ref[0]
    for head in range(width // HEAD):
        at = pl.ds(head * HEAD, HEAD)
        at_k = pl.ds(width + head * HEAD, HEAD)
        at_v = pl.ds(2 * width + head * HEAD, HEAD)
        queries = qkv_ref[:, at]
        keys = qkv_ref[:, at_k]
        values = qkv_ref[:, at_v]
        d_context = d_context_ref[:, at]
        probs = softmax(queries, keys, visible)
        d_packed_ref[:, at_v] = dot_rows(probs.astype(BF16), d_context).astype(BF16)
        d_probs = dot_cols(d_context, values)
        inner = jnp.sum(probs * d_probs, axis=1, keepdims=True)
        d_scores = (probs * (d_probs - inner)).astype(BF16)
        grad = dot(d_scores, keys) * scale
        d_packed_ref[:, at] = (grad * cosine - swap_halves(grad) * sine).astype(BF16)
        grad = dot_rows(d_scores, queries)
        d_packed_ref[:, at_k] = (grad * cosine - swap_halves(grad) * sine).astype(BF16)


def by_sequence(width):
    return pl.BlockSpec((SEQ_LEN, width), lambda s: (s, 0))


TABLE = pl.BlockSpec((1, SEQ_LEN, HEAD), lambda s: (s, 0, 0))
SCALARS = pl.BlockSpec(memory_space=pltpu.SMEM)
PARAMS = pltpu.CompilerParams(vmem_limit_bytes=56 * 2**20)
SMALL = pltpu.CompilerParams(vmem_limit_bytes=24 * 2**20)


def attend(prefix, packed, cosine, sine):
    rows, width = packed.shape[0], packed.shape[1] // 3
    return pl.pallas_call(
        attend_kernel,
        grid=(rows // SEQ_LEN,),
        in_specs=[SCALARS, by_sequence(3 * width), TABLE, TABLE],
        out_specs=[by_sequence(3 * width), by_sequence(width)],
        out_shape=[
            jax.ShapeDtypeStruct((rows, 3 * width), BF16),
            jax.ShapeDtypeStruct((rows, width), BF16),
        ],
        compiler_params=PARAMS,
    )(prefix, packed, cosine, sine)


def attend_back(prefix, qkv, d_context, cosine, sine):
    rows, width = d_context.shape
    return pl.pallas_call(
        attend_back_kernel,
        grid=(rows // SEQ_LEN,),
        in_specs=[SCALARS, by_sequence(3 * width), by_sequence(width), TABLE, TABLE],
        out_specs=by_sequence(3 * width),
        out_shape=jax.ShapeDtypeStruct((rows, 3 * width), BF16),
        compiler_params=PARAMS,
    )(prefix, qkv, d_context, cosine, sine)


def tables(prefix, start):
    place = jnp.arange(SEQ_LEN, dtype=jnp.int32)
    in_span = place[None, :] >= prefix[:, None]
    pos_one = jnp.where(in_span, start[:, None], place[None, :])
    pos_two = jnp.where(in_span, place[None, :] - prefix[:, None] + 1, 0)
    lane = jnp.arange(HEAD)
    freqs = 10000.0 ** (-2.0 * (lane % 32).astype(F32) / 64)
    place_of = jnp.where(lane[None, None, :] < 64, pos_one[:, :, None], pos_two[:, :, None])
    angles = place_of.astype(F32) * freqs
    sign = jnp.where(lane % 64 < 32, -1.0, 1.0)
    return jnp.cos(angles), jnp.sin(angles) * sign


def norm_parts(values):
    center = values - jnp.mean(values, axis=-1, keepdims=True)
    inverse = lax.rsqrt(jnp.mean(center * center, axis=-1, keepdims=True) + norm_eps)
    return center * inverse, inverse


def norm_back(normal, inverse, gain, grad):
    scaled = gain * grad
    return inverse * (
        scaled
        - jnp.mean(scaled, axis=-1, keepdims=True)
        - normal * jnp.mean(scaled * normal, axis=-1, keepdims=True)
    )


def gate_parts(gate):
    phi = 0.5 * (1.0 + lax.erf(gate * 0.7071067811865476))
    slope = phi + gate * jnp.exp(-0.5 * gate * gate) * 0.3989422804014327
    return gate * phi, slope


def here():
    return lax.axis_index("gy"), lax.axis_index("gx"), lax.axis_index("core")


def place(y, x, c):
    return (y * 2 + x) * 2 + c


def greet(peers):
    barrier = pltpu.get_barrier_semaphore()
    for peer in peers:
        pl.semaphore_signal(barrier, inc=1, device_id=peer, device_id_type=MESH)
    pl.semaphore_wait(barrier, len(peers))


def spread_block(cut, base, block_ref, out_ref, send, recv, local):
    rows = block_ref.shape[0]
    y, x, c = here()
    to_x, to_y, to_c = {"gx": 1 - x}, {"gy": 1 - y}, {"core": 1 - c}
    me, by_x, by_y, far = place(y, x, c), place(y, 1 - x, c), place(1 - y, x, c), place(1 - y, 1 - x, c)
    low, high = pl.ds(0, cut), pl.ds(cut, rows - cut)

    def push(k, src, dst, to):
        copy = pltpu.make_async_remote_copy(
            src_ref=src, dst_ref=dst, send_sem=send.at[base + k], recv_sem=recv.at[base + k], device_id=to, device_id_type=MESH
        )
        copy.start()
        return copy

    def landed(k, dst):
        pltpu.make_async_remote_copy(
            src_ref=dst, dst_ref=dst, send_sem=send.at[base + k], recv_sem=recv.at[base + k], device_id=to_c, device_id_type=MESH
        ).wait_recv()

    sent = [
        push(0, block_ref.at[low], out_ref.at[me, low], to_x),
        push(1, block_ref.at[high], out_ref.at[me, high], to_y),
        push(2, block_ref.at[high], out_ref.at[me, high], to_x),
        push(3, block_ref.at[low], out_ref.at[me, low], to_y),
        push(4, block_ref, out_ref.at[me], to_c),
    ]
    keep = pltpu.make_async_copy(block_ref, out_ref.at[me], local)
    keep.start()
    landed(0, out_ref.at[by_x, low])
    sent.append(push(5, out_ref.at[by_x, low], out_ref.at[by_x, low], to_y))
    sent.append(push(7, out_ref.at[by_x, low], out_ref.at[by_x, low], to_c))
    landed(1, out_ref.at[by_y, high])
    sent.append(push(6, out_ref.at[by_y, high], out_ref.at[by_y, high], to_x))
    sent.append(push(8, out_ref.at[by_y, high], out_ref.at[by_y, high], to_c))
    landed(2, out_ref.at[by_x, high])
    sent.append(push(9, out_ref.at[by_x, high], out_ref.at[by_x, high], to_c))
    landed(3, out_ref.at[by_y, low])
    sent.append(push(10, out_ref.at[by_y, low], out_ref.at[by_y, low], to_c))
    landed(5, out_ref.at[far, low])
    sent.append(push(11, out_ref.at[far, low], out_ref.at[far, low], to_c))
    landed(6, out_ref.at[far, high])
    sent.append(push(12, out_ref.at[far, high], out_ref.at[far, high], to_c))
    other, other_x, other_y, other_far = (
        place(y, x, 1 - c),
        place(y, 1 - x, 1 - c),
        place(1 - y, x, 1 - c),
        place(1 - y, 1 - x, 1 - c),
    )
    landed(4, out_ref.at[other])
    landed(7, out_ref.at[other_x, low])
    landed(8, out_ref.at[other_y, high])
    landed(9, out_ref.at[other_x, high])
    landed(10, out_ref.at[other_y, low])
    landed(11, out_ref.at[other_far, low])
    landed(12, out_ref.at[other_far, high])
    keep.wait()
    for copy in sent:
        copy.wait_send()


ANY = pl.BlockSpec(memory_space=pl.ANY)


def swap_peers(zs, kinds):
    y, x, c = here()
    z = lax.axis_index("z")
    found = []
    for k in range(1, 8):
        peer = ((y + k // 4) % 2, (x + k // 2 % 2) % 2, (c + k % 2) % 2)
        found.append((place(*peer), {"gy": peer[0], "gx": peer[1], "core": peer[2]}))
    if "line" in kinds:
        found += [((z + k) % zs, {"z": (z + k) % zs}) for k in range(1, zs)]
    return found


def swap_begin(zs, kinds, blocks, outs, send, recv, local):
    copies, comes, keeps = [], [], []
    found = swap_peers(zs, kinds)
    for i, kind in enumerate(kinds):
        me = lax.axis_index("z") if kind == "line" else place(*here())
        for k, (peer, name) in enumerate(found[7:] if kind == "line" else found[:7]):
            src = blocks[i].at[peer] if kind == "swap" else blocks[i]
            landing = outs[i].at[peer]
            sems = dict(send_sem=send.at[i, k], recv_sem=recv.at[i, k], device_id=name, device_id_type=MESH)
            copies.append(pltpu.make_async_remote_copy(src_ref=src, dst_ref=outs[i].at[me], **sems))
            comes.append(pltpu.make_async_remote_copy(src_ref=landing, dst_ref=landing, **sems))
            copies[-1].start()
        own = blocks[i].at[me] if kind == "swap" else blocks[i]
        keeps.append(pltpu.make_async_copy(own, outs[i].at[me], local.at[i]))
        keeps[-1].start()

    def finish():
        for come in comes:
            come.wait_recv()
        for copy in copies:
            copy.wait_send()
        for keep in keeps:
            keep.wait()

    return finish


SWAP_LEAD = {"swap": lambda zs: (), "group": lambda zs: (8,), "line": lambda zs: (zs,)}


def swap_shapes(zs, arrays, kinds):
    return [jax.ShapeDtypeStruct(SWAP_LEAD[k](zs) + a.shape, a.dtype) for a, k in zip(arrays, kinds)]


def swap_scratch(zs, kinds):
    n, most = len(kinds), max(7, zs - 1)
    return [
        pltpu.SemaphoreType.DMA((n, most)),
        pltpu.SemaphoreType.DMA((n, most)),
        pltpu.SemaphoreType.DMA((n,)),
    ]


SLAB = 16
ROWS = pl.BlockSpec(memory_space=pltpu.VMEM)
CHIP_COLS = 256


def by_rows(value, zs, piece):
    group = D // (zs * piece)
    order = [g * zs + z for z in range(zs) for g in range(group)]
    return jnp.concatenate([value[:, m * piece : (m + 1) * piece] for m in order], axis=1)


def in_order(value, zs, piece):
    group = D // (zs * piece)
    order = [z * group + g for g in range(group) for z in range(zs)]
    return jnp.concatenate([value[:, m * piece : (m + 1) * piece] for m in order], axis=1)


def first_norm(values, gains):
    normal, inverse = norm_parts(values)
    first = normal * gains[0:1] + gains[1:2]
    return first, normal, inverse


def second_norm(total, first, grad, gains):
    normal, inverse = norm_parts(deep_alpha * first + total)
    return normal * gains[2:3] + gains[3:4], norm_back(normal, inverse, gains[2:3], grad), grad * normal


def first_back(total, d_pre_two, normal, inverse, gains):
    d_first = deep_alpha * d_pre_two + total
    return norm_back(normal, inverse, gains[0:1], d_first), d_first * normal, d_first


def fold_kernel(mode, across, zs, piece, n_aux, n_out, kinds, *refs):
    left_ref, right_ref, gains_ref = refs[:3]
    aux_refs = refs[3 : 3 + n_aux]
    refs = refs[3 + n_aux :]
    n_swap = len(kinds)
    swap_in, refs = refs[:n_swap], refs[n_swap:]
    spread = mode != "last"
    if spread:
        all_ref, refs = refs[0], refs[1:]
    out_refs, refs = refs[:n_out], refs[n_out:]
    swap_out, refs = refs[:n_swap], refs[n_swap:]
    aux, refs = refs[:n_aux], refs[n_aux:]
    outs, refs = refs[:n_out], refs[n_out:]
    left, right, part, got, near_x, near_y, from_x, from_y, block, acc, send, recv, local = refs[:13]
    rows, width = block.shape
    cut = near_x.shape[0]
    y, x, c = here()
    to_x, to_y, to_c = {"gx": 1 - x}, {"gy": 1 - y}, {"core": 1 - c}
    chips = [(1 - y, 1 - x), (y, 1 - x), (1 - y, x), (y, x)]
    low, high = pl.ds(0, cut), pl.ds(cut, rows - cut)

    def push(k, src, dst, to):
        copy = pltpu.make_async_remote_copy(
            src_ref=src, dst_ref=dst, send_sem=send.at[k], recv_sem=recv.at[k], device_id=to, device_id_type=MESH
        )
        copy.start()
        return copy

    def add(k, extra, start, size, offset=0):
        @pl.loop(0, size // SLAB)
        def _(step):
            at = pl.ds(pl.multiple_of(start + step * SLAB, SLAB), SLAB)
            of = pl.ds(pl.multiple_of(start - offset + step * SLAB, SLAB), SLAB)
            part[k, c, at] = (part[k, c, at].astype(F32) + extra[of].astype(F32)).astype(BF16)

    loads = [pltpu.make_async_copy(left_ref.at[a * 2 + b], left.at[k], local.at[k]) for k, (a, b) in enumerate(chips)]
    load_right = pltpu.make_async_copy(right_ref, right, local.at[4])
    load_aux = [pltpu.make_async_copy(r, v, local.at[5 + k]) for k, (r, v) in enumerate(zip(aux_refs, aux))]
    loads[0].start()
    load_right.start()
    for load in loads[1:] + load_aux:
        load.start()
    if n_swap:
        greet([name for _, name in swap_peers(1, kinds)])
        swap_finish = swap_begin(1, kinds, swap_in, swap_out, *refs[13:])
    else:
        greet([to_x, to_y, to_c])

    def product(k):
        loads[k].wait()

        @pl.loop(0, width // CHIP_COLS)
        def _(step):
            at = pl.ds(pl.multiple_of(step * CHIP_COLS, CHIP_COLS), CHIP_COLS)
            here_part = dot_cols(left[k], right[at]) if across else dot(left[k], right[:, at])
            part[k, 0, :, at] = here_part[:rows].astype(BF16)
            part[k, 1, :, at] = here_part[rows:].astype(BF16)

        return push(k, part.at[k, 1 - c], got.at[k], to_c)

    load_right.wait()
    sent = [product(0), product(1)]
    sent[0].wait_recv()
    add(0, got.at[0], 0, rows)
    far_x = push(4, part.at[0, c, low], near_x, to_x)
    far_y = push(5, part.at[0, c, high], near_y, to_y)
    sent.append(product(2))
    sent[1].wait_recv()
    add(1, got.at[1], 0, rows)
    plain_x = push(6, part.at[1, c, low], from_x.at[low], to_x)
    sent[2].wait_recv()
    add(2, got.at[2], 0, rows)
    plain_y = push(7, part.at[2, c, high], from_y.at[high], to_y)
    sent.append(product(3))
    far_y.wait_recv()
    add(1, near_y, cut, rows - cut, cut)
    more_x = push(8, part.at[1, c, high], from_x.at[high], to_x)
    far_x.wait_recv()
    add(2, near_x, 0, cut)
    more_y = push(9, part.at[2, c, low], from_y.at[low], to_y)
    sent[3].wait_recv()
    for load in load_aux:
        load.wait()
    plain_x.wait_recv()
    plain_y.wait_recv()
    more_x.wait_recv()
    more_y.wait_recv()
    gains = gains_ref[...]
    acc[...] = jnp.zeros_like(acc)

    @pl.loop(0, rows // SLAB)
    def _(step):
        at = pl.ds(pl.multiple_of(step * SLAB, SLAB), SLAB)
        total = part[3, c, at].astype(F32) + got[3, at].astype(F32) + from_x[at].astype(F32) + from_y[at].astype(F32)
        held = [a[at].astype(F32) for a in aux]
        if mode == "one":
            first, normal, inverse = first_norm(by_rows(deep_alpha * held[0] + total, zs, piece), gains)
            outs[0][at] = first
            outs[1][at] = normal
            outs[2][at] = jnp.broadcast_to(inverse, (SLAB, 128))
            block[at] = first.astype(BF16)
        elif mode == "back":
            d_pre, terms, d_first = first_back(total, held[0], held[1], held[2][:, 0:1], gains)
            outs[0][at] = d_pre
            block[at] = in_order(d_pre, zs, piece).astype(BF16)
            acc[0] += terms
            acc[1] += d_first
        else:
            outs[0][at] = in_order(deep_alpha * held[0] + total, zs, piece).astype(BF16)

    if mode == "back":
        outs[-1][0:1] = jnp.sum(acc[0], axis=0, keepdims=True)
        outs[-1][1:2] = jnp.sum(acc[1], axis=0, keepdims=True)
    stores = [pltpu.make_async_copy(v, r, local.at[5 + n_aux + k]) for k, (v, r) in enumerate(zip(outs, out_refs))]
    for store in stores:
        store.start()
    for copy in sent + [far_x, far_y, plain_x, plain_y, more_x, more_y]:
        copy.wait_send()
    if n_swap:
        swap_finish()
    if spread:
        spread_block(cut, 10, block, all_ref, send, recv, local.at[4])
    for store in stores:
        store.wait()


def group_fold(name, zs, mode, left, right, gains, aux, out_types, extras=(), kinds=()):
    across = mode != "one"
    rows, depth = left.shape[0] // 8, left.shape[1]
    width = gains.shape[1]
    cut = rows // 2
    spread = mode != "last"
    out_shape = [jax.ShapeDtypeStruct((8, rows, width), BF16)] * spread + out_types
    n, n_swap = len(aux), len(extras)
    n_sems = 23 if spread else 10
    return pl.pallas_call(
        functools.partial(fold_kernel, mode, across, zs, width // (8 * zs), n, len(out_types), kinds),
        out_shape=out_shape + swap_shapes(1, extras, kinds),
        in_specs=[ANY, ANY, ROWS] + [ANY] * (n + n_swap),
        out_specs=[ANY] * (spread + len(out_types) + n_swap),
        scratch_shapes=[pltpu.VMEM(a.shape, a.dtype) for a in list(aux) + out_types]
        + [
            pltpu.VMEM((4, 2 * rows, depth), BF16),
            pltpu.VMEM(right.shape, BF16),
            pltpu.VMEM((4, 2, rows, width), BF16),
            pltpu.VMEM((4, rows, width), BF16),
            pltpu.VMEM((cut, width), BF16),
            pltpu.VMEM((rows - cut, width), BF16),
            pltpu.VMEM((rows, width), BF16),
            pltpu.VMEM((rows, width), BF16),
            pltpu.VMEM((rows, width), BF16),
            pltpu.VMEM((2, SLAB, width), F32),
            pltpu.SemaphoreType.DMA((n_sems,)),
            pltpu.SemaphoreType.DMA((n_sems,)),
            pltpu.SemaphoreType.DMA((5 + n + len(out_types),)),
        ]
        + (swap_scratch(1, kinds) if n_swap else []),
        compiler_params=pltpu.CompilerParams(
            collective_id=name, has_side_effects=True, vmem_limit_bytes=50 * 2**20
        ),
        cost_estimate=pl.CostEstimate(flops=0, bytes_accessed=(200 if spread else 110) * 2**20, transcendentals=0),
    )(left.reshape(4, 2 * rows, depth), right, gains, *aux, *extras)


def turn_kernel(
    zs, piece, x_ref, in_ref, out_ref, gains_ref, first_ref, grad_ref,
    all_ref, kept_ref, right_ref, result_out, d_pre_out, sums_ref, dw_out, result_ref, d_pre_ref, dw_ref,
    first, grad, w_in, kept, left, right, part, got, near_x, near_y, from_x, from_y, whole, dw, acc,
    fold_send, fold_recv, all_send, all_recv, line_send, line_recv, local, x_local
):
    rows = first.shape[0]
    tile = left.shape[2]
    wide = right.shape[2]
    y, x, c = here()
    z = lax.axis_index("z")
    to_x, to_y, to_c = {"gx": 1 - x}, {"gy": 1 - y}, {"core": 1 - c}
    chips = [(1 - y) * 2 + 1 - x, y * 2 + 1 - x, (1 - y) * 2 + x, y * 2 + x]
    me, by_x, by_y, far = place(y, x, c), place(y, 1 - x, c), place(1 - y, x, c), place(1 - y, 1 - x, c)
    other, other_x, other_y, other_far = (
        place(y, x, 1 - c),
        place(y, 1 - x, 1 - c),
        place(1 - y, x, 1 - c),
        place(1 - y, 1 - x, 1 - c),
    )
    half = rows // 2
    most = -(-half // (2 * SLAB)) * SLAB
    lows = [(0, most), (half, half - most)]
    highs = [(most, half - most), (2 * half - most, most)]
    top, bottom = pl.ds(0, half), pl.ds(half, half)
    sent = []

    def remote(sems, k, src, dst, to):
        return pltpu.make_async_remote_copy(
            src_ref=src,
            dst_ref=dst,
            send_sem=sems[0].at[k],
            recv_sem=sems[1].at[k],
            device_id=to,
            device_id_type=MESH,
        )

    def push(sems, k, src, dst, to):
        copy = remote(sems, k, src, dst, to)
        copy.start()
        sent.append(copy)

    def landed(sems, k, dst):
        remote(sems, k, dst, dst, to_c).wait_recv()

    folds, alls, lines = (fold_send, fold_recv), (all_send, all_recv), (line_send, line_recv)

    load_out = pltpu.make_async_copy(out_ref, right.at[z], local.at[0])
    load_in = pltpu.make_async_copy(in_ref, w_in, local.at[1])
    load_first = pltpu.make_async_copy(first_ref, first, local.at[2])
    load_grad = pltpu.make_async_copy(grad_ref, grad, local.at[3])

    def load_x(g):
        return pltpu.make_async_copy(x_ref.at[g], whole.at[g], x_local.at[g])

    load_out.start()

    barrier = pltpu.get_barrier_semaphore()
    for to in (to_x, to_y, to_c):
        pl.semaphore_signal(barrier, inc=1, device_id=to, device_id_type=MESH)

    @pl.when(z > 0)
    def _():
        pl.semaphore_signal(barrier, inc=1, device_id={"z": z - 1}, device_id_type=MESH)

    @pl.when(z < zs - 1)
    def _():
        pl.semaphore_signal(barrier, inc=1, device_id={"z": z + 1}, device_id_type=MESH)

    inside = (z > 0) & (z < zs - 1)

    @pl.when(inside)
    def _():
        pl.semaphore_wait(barrier, 5)

    @pl.when(jnp.logical_not(inside))
    def _():
        pl.semaphore_wait(barrier, 4)

    def shard_of(step, up):
        return z - step if up else z + step

    def hop(step, up):
        ref = right.at[shard_of(step, up)]
        return remote(lines, 2 * step + (0 if up else 1), ref, ref, {"z": z + 1 if up else z - 1})

    def sends(step, up):
        return (z >= step) & (z < zs - 1) if up else (z <= zs - 1 - step) & (z > 0)

    def gets(step, up):
        return z >= step + 1 if up else z <= zs - 2 - step

    def line_serve(step):
        for up in (True, False):

            @pl.when(gets(step - 1, up) & sends(step, up))
            def _(up=up):
                landed(lines, 2 * (step - 1) + (0 if up else 1), right.at[shard_of(step, up)])
                hop(step, up).start()

    def line_take(step):
        for up in (True, False):

            @pl.when(gets(step - 1, up) & jnp.logical_not(sends(step, up)))
            def _(up=up):
                landed(lines, 2 * (step - 1) + (0 if up else 1), right.at[shard_of(step, up)])

    load_out.wait()
    for up in (True, False):

        @pl.when(sends(0, up))
        def _(up=up):
            hop(0, up).start()

    load_in.start()
    for g in range(8):
        load_x(g).start()


    load_in.wait()

    @pl.loop(0, 8)
    def _(g):
        @pl.when(g == 6)
        def _():
            line_serve(1)

        load_x(g).wait()
        projected = dot(whole[g], w_in[...])
        gate, up = projected[:, :tile], projected[:, tile:]
        act, slope = gate_parts(gate)
        left[g] = (act * up).astype(BF16)
        kept[g] = jnp.concatenate([up * slope, act], axis=1).astype(BF16)

    load_first.start()
    load_grad.start()
    keep = pltpu.make_async_copy(kept, kept_ref, local.at[4])
    keep.start()

    def add(k, extra, start, offset, at):
        @pl.loop(0, half // SLAB)
        def _(step):
            row = pl.ds(pl.multiple_of(start + step * SLAB, SLAB), SLAB)
            of = pl.ds(pl.multiple_of(start - offset + step * SLAB, SLAB), SLAB)
            part[k, c, row, at] = (part[k, c, row, at].astype(F32) + extra[of, at].astype(F32)).astype(BF16)

    def chip_sum(k, at):
        add(k, got.at[k], 0, 0, at)
        add(k, got.at[k], half, 0, at)

    def product(k, block, at):
        found = dot(left[pl.ds(2 * chips[k], 2)].reshape(2 * rows, tile), right[block])
        part[k, 0, :, at] = found[:rows].astype(BF16)
        part[k, 1, :, at] = found[rows:].astype(BF16)

    def block_at(i):
        if i == 0:
            return z
        below = z < zs // 2
        near = jnp.where(below, z, zs - 1 - z)
        spot = jnp.where(i <= 2 * near, jnp.where(i % 2 == 1, near - (i + 1) // 2, near + i // 2), i)
        return jnp.where(below, spot, zs - 1 - spot)

    def block_cols(i):
        return pl.ds(pl.multiple_of(block_at(i) * wide, wide), wide)

    def fold_start(i):
        b, block, at = 8 * i, block_at(i), block_cols(i)
        rest = pl.ds(1, 3)
        product(0, block, at)
        push(folds, b, part.at[0, 1 - c, :, at], got.at[0, :, at], to_c)
        for k in (1, 2, 3):
            product(k, block, at)
        push(folds, b + 1, part.at[rest, 1 - c, :, at], got.at[rest, :, at], to_c)
        landed(folds, b, got.at[0, :, at])
        chip_sum(0, at)
        push(folds, b + 2, part.at[0, c, top, at], near_x.at[:, at], to_x)
        push(folds, b + 3, part.at[0, c, bottom, at], near_y.at[:, at], to_y)
        landed(folds, b + 1, got.at[rest, :, at])
        chip_sum(1, at)
        push(folds, b + 4, part.at[1, c, top, at], from_x.at[top, at], to_x)
        chip_sum(2, at)
        push(folds, b + 5, part.at[2, c, bottom, at], from_y.at[bottom, at], to_y)

    def fold_end(i):
        b, at = 8 * i, block_cols(i)
        landed(folds, b + 3, near_y.at[:, at])
        add(1, near_y, half, half, at)
        push(folds, b + 6, part.at[1, c, bottom, at], from_x.at[bottom, at], to_x)
        landed(folds, b + 2, near_x.at[:, at])
        add(2, near_x, 0, 0, at)
        push(folds, b + 7, part.at[2, c, top, at], from_y.at[top, at], to_y)

    gains = gains_ref[...]
    line_take(1)
    fold_start(0)
    fold_start(1)
    fold_end(0)
    for i in range(2, zs):
        if i < zs - 1:
            line_serve(i)
        fold_end(i - 1)
        line_take(i)
        fold_start(i)
    fold_end(zs - 1)
    carry = pltpu.make_async_copy(right, right_ref, local.at[5])
    carry.start()
    load_first.wait()
    load_grad.wait()
    acc[...] = jnp.zeros_like(acc)
    for i in range(zs):
        at = block_cols(i)
        landed(folds, 8 * i + 4, from_x.at[top, at])
        landed(folds, 8 * i + 5, from_y.at[bottom, at])
        landed(folds, 8 * i + 6, from_x.at[bottom, at])
        landed(folds, 8 * i + 7, from_y.at[top, at])

    def low(i):
        return pl.ds(*lows[i])

    def high(i):
        return pl.ds(*highs[i])

    def span(i):
        return pl.ds(i * half, half)

    def norm(i):
        @pl.loop(0, half // SLAB)
        def _(step):
            at = pl.ds(pl.multiple_of(i * half + step * SLAB, SLAB), SLAB)
            total = part[3, c, at].astype(F32) + got[3, at].astype(F32)
            total += from_x[at].astype(F32) + from_y[at].astype(F32)
            dy = grad[at].astype(F32)
            result, d_pre, terms = second_norm(total, first[at], dy, gains)
            result_ref[at] = result.astype(BF16)
            d_pre_ref[at] = d_pre
            whole[me, at] = d_pre.astype(BF16)
            acc[0] += terms
            acc[1] += dy

        b = 13 * i
        push(alls, b, whole.at[me, low(i)], whole.at[me, low(i)], to_x)
        push(alls, b + 1, whole.at[me, high(i)], whole.at[me, high(i)], to_y)
        push(alls, b + 2, whole.at[me, high(i)], whole.at[me, high(i)], to_x)
        push(alls, b + 3, whole.at[me, low(i)], whole.at[me, low(i)], to_y)
        push(alls, b + 4, whole.at[me, span(i)], whole.at[me, span(i)], to_c)

    def pass_on(i, k, slot, at, onward):
        ref = whole.at[slot, at]
        landed(alls, 13 * i + k, ref)
        for where, to in onward:
            push(alls, 13 * i + where, ref, ref, to)

    def spread_first(i):
        pass_on(i, 0, by_x, low(i), [(5, to_y), (7, to_c)])
        pass_on(i, 1, by_y, high(i), [(6, to_x), (8, to_c)])

    def spread_rest(i):
        pass_on(i, 2, by_x, high(i), [(9, to_c)])
        pass_on(i, 3, by_y, low(i), [(10, to_c)])

    def spread_far(i):
        pass_on(i, 5, far, low(i), [(11, to_c)])
        pass_on(i, 6, far, high(i), [(12, to_c)])

    outward = []

    def gradient(k, last=False, first_one=False):
        pair = pl.ds(2 * chips[k], 2)
        outward.append(pltpu.make_async_copy(whole.at[pair], all_ref.at[pair], local.at[6 + k]))
        outward[-1].start()

        @pl.loop(0, zs)
        def _(block):
            at = pl.ds(pl.multiple_of(block * wide, wide), wide)
            found = dot_rows(left[pair].reshape(2 * rows, tile), whole[pair, :, at].reshape(2 * rows, wide))
            if first_one:
                dw[block] = found
            elif last:
                dw_ref[block] = (dw[block] + found).astype(BF16)
                pltpu.make_async_copy(dw_ref.at[block], dw_out.at[block], x_local.at[block]).start()
            else:
                dw[block] += found

    norm(0)
    norm(1)
    stores = [
        pltpu.make_async_copy(result_ref, result_out, local.at[10]),
        pltpu.make_async_copy(d_pre_ref, d_pre_out, local.at[11]),
    ]
    for store in stores:
        store.start()
    spread_first(0)
    for i in (0, 1):
        landed(alls, 13 * i + 4, whole.at[other, span(i)])
    gradient(3, first_one=True)
    spread_rest(0)
    spread_first(1)
    spread_rest(1)
    for i in (0, 1):
        landed(alls, 13 * i + 7, whole.at[other_x, low(i)])
        landed(alls, 13 * i + 9, whole.at[other_x, high(i)])
    gradient(1)
    spread_far(0)
    for i in (0, 1):
        landed(alls, 13 * i + 8, whole.at[other_y, high(i)])
        landed(alls, 13 * i + 10, whole.at[other_y, low(i)])
    gradient(2)
    sums_ref[0:1] = jnp.sum(acc[0], axis=0, keepdims=True)
    sums_ref[1:2] = jnp.sum(acc[1], axis=0, keepdims=True)
    spread_far(1)
    for i in (0, 1):
        landed(alls, 13 * i + 11, whole.at[other_far, low(i)])
        landed(alls, 13 * i + 12, whole.at[other_far, high(i)])
    gradient(0, last=True)
    for block in range(zs):
        pltpu.make_async_copy(dw_ref.at[block], dw_out.at[block], x_local.at[block]).wait()
    for copy in outward + [keep, carry] + stores:
        copy.wait()
    for copy in sent:
        copy.wait_send()
    for step in range(zs - 1):
        for up in (True, False):

            @pl.when(sends(step, up))
            def _(step=step, up=up):
                hop(step, up).wait_send()


def turn(zs, x, w_in, w_out, gains, first, grad):
    rows = x.shape[0] // 8
    units, wide = w_out.shape
    width = gains.shape[1]
    half = rows // 2
    by_z = (zs, units, wide)
    return pl.pallas_call(
        functools.partial(turn_kernel, zs, width // (8 * zs)),
        out_shape=[
            jax.ShapeDtypeStruct((8, rows, width), BF16),
            jax.ShapeDtypeStruct((8, rows, 2 * units), BF16),
            jax.ShapeDtypeStruct(by_z, BF16),
            jax.ShapeDtypeStruct((rows, width), BF16),
            jax.ShapeDtypeStruct((rows, width), F32),
            jax.ShapeDtypeStruct((8, width), F32),
            jax.ShapeDtypeStruct(by_z, BF16),
        ],
        in_specs=[ANY, ANY, ANY, ROWS, ANY, ANY],
        out_specs=[ANY] * 5 + [ROWS, ANY],
        scratch_shapes=[
            pltpu.VMEM((rows, width), BF16),
            pltpu.VMEM((rows, width), F32),
            pltpu.VMEM(by_z, BF16),
            pltpu.VMEM((rows, width), F32),
            pltpu.VMEM((rows, width), BF16),
            pltpu.VMEM(w_in.shape, BF16),
            pltpu.VMEM((8, rows, 2 * units), BF16),
            pltpu.VMEM((8, rows, units), BF16),
            pltpu.VMEM(by_z, BF16),
            pltpu.VMEM((4, 2, rows, width), BF16),
            pltpu.VMEM((4, rows, width), BF16),
            pltpu.VMEM((half, width), BF16),
            pltpu.VMEM((half, width), BF16),
            pltpu.VMEM((rows, width), BF16),
            pltpu.VMEM((rows, width), BF16),
            pltpu.VMEM((8, rows, width), BF16),
            pltpu.VMEM(by_z, F32),
            pltpu.VMEM((2, SLAB, width), F32),
            pltpu.SemaphoreType.DMA((8 * zs,)),
            pltpu.SemaphoreType.DMA((8 * zs,)),
            pltpu.SemaphoreType.DMA((26,)),
            pltpu.SemaphoreType.DMA((26,)),
            pltpu.SemaphoreType.DMA((2 * (zs - 1),)),
            pltpu.SemaphoreType.DMA((2 * (zs - 1),)),
            pltpu.SemaphoreType.DMA((12,)),
            pltpu.SemaphoreType.DMA((8,)),
        ],
        compiler_params=pltpu.CompilerParams(collective_id=1, has_side_effects=True, vmem_limit_bytes=60 * 2**20),
        cost_estimate=pl.CostEstimate(flops=0, bytes_accessed=380 * 2**20, transcendentals=0),
    )(x.reshape(8, rows, width), w_in, w_out, gains, first, grad)


def swap_kernel(zs, kinds, *refs):
    n = len(kinds)
    greet([name for _, name in swap_peers(zs, kinds)])
    swap_begin(zs, kinds, refs[:n], refs[n : 2 * n], *refs[2 * n :])()


def group_swap(name, zs, arrays, kinds):
    n = len(arrays)
    return pl.pallas_call(
        functools.partial(swap_kernel, zs, kinds),
        out_shape=swap_shapes(zs, arrays, kinds),
        in_specs=[ANY] * n,
        out_specs=[ANY] * n,
        scratch_shapes=swap_scratch(zs, kinds),
        compiler_params=pltpu.CompilerParams(collective_id=name, has_side_effects=True),
        cost_estimate=pl.CostEstimate(flops=0, bytes_accessed=50 * 2**20, transcendentals=0),
    )(*arrays)


def enter_kernel(zs, kinds, x_ref, grad_ref, *refs):
    n = len(kinds)
    blocks, x_all, grad_out, outs, refs = refs[:n], refs[n], refs[n + 1], refs[n + 2 : 2 * n + 2], refs[2 * n + 2 :]
    x_rows, sems = refs[0], refs[1:]
    rows, width = x_ref.shape
    greet([name for _, name in swap_peers(zs, kinds)])
    finish = swap_begin(zs, kinds, blocks, outs, *sems[:3])
    for ref, out in ((x_ref, x_rows), (grad_ref, grad_out)):

        @pl.loop(0, rows // SLAB)
        def _(step, ref=ref, out=out):
            at = pl.ds(pl.multiple_of(step * SLAB, SLAB), SLAB)
            out[at] = by_rows(ref[at].astype(F32), zs, width // (8 * zs)).astype(BF16)

    spread_block(rows // 2, 0, x_rows, x_all, *sems[3:])
    finish()


def enter(zs, x, grad, arrays, kinds):
    n = len(arrays)
    return pl.pallas_call(
        functools.partial(enter_kernel, zs, kinds),
        out_shape=[jax.ShapeDtypeStruct((8,) + x.shape, x.dtype), jax.ShapeDtypeStruct(grad.shape, grad.dtype)]
        + swap_shapes(zs, arrays, kinds),
        in_specs=[ROWS] * 2 + [ANY] * n,
        out_specs=[ANY, ROWS] + [ANY] * n,
        scratch_shapes=[pltpu.VMEM(x.shape, x.dtype)]
        + swap_scratch(zs, kinds)
        + [pltpu.SemaphoreType.DMA((13,)), pltpu.SemaphoreType.DMA((13,)), pltpu.SemaphoreType.DMA],
        compiler_params=pltpu.CompilerParams(collective_id=3, has_side_effects=True, vmem_limit_bytes=56 * 2**20),
        cost_estimate=pl.CostEstimate(flops=0, bytes_accessed=150 * 2**20, transcendentals=0),
    )(x, grad, *arrays)


def ff_kernel(x_ref, w_ref, hidden_ref, kept_ref):
    tile = hidden_ref.shape[1]
    projected = dot(x_ref[...], w_ref[...])
    gate, up = projected[:, :tile], projected[:, tile:]
    act, slope = gate_parts(gate)
    hidden_ref[...] = (act * up).astype(BF16)
    kept_ref[...] = jnp.concatenate([up * slope, act], axis=1).astype(BF16)


def ff_back_kernel(grad_ref, w_ref, kept_ref, out_ref):
    zs, _, wide = w_ref.shape
    d_hidden = dot_cols(grad_ref[:, :wide], w_ref[0])
    for z in range(1, zs):
        d_hidden += dot_cols(grad_ref[:, z * wide : (z + 1) * wide], w_ref[z])
    out_ref[...] = (jnp.concatenate([d_hidden, d_hidden], axis=1) * kept_ref[...].astype(F32)).astype(BF16)


FF_ROWS = 256


def ff_rows(width):
    return pl.BlockSpec((FF_ROWS, width), lambda i: (i, 0))


def ff_forward(x, w):
    rows, depth = x.shape
    wide = w.shape[1]
    return pl.pallas_call(
        ff_kernel,
        grid=(rows // FF_ROWS,),
        in_specs=[ff_rows(depth), pl.BlockSpec((depth, wide), lambda i: (0, 0))],
        out_specs=[ff_rows(wide // 2), ff_rows(wide)],
        out_shape=[jax.ShapeDtypeStruct((rows, wide // 2), BF16), jax.ShapeDtypeStruct((rows, wide), BF16)],
        compiler_params=PARAMS,
        cost_estimate=pl.CostEstimate(flops=2 * rows * depth * wide, bytes_accessed=20 * 2**20, transcendentals=0),
    )(x, w)


def ff_backward(grad, w, kept):
    rows, depth = grad.shape
    wide = kept.shape[1]
    return pl.pallas_call(
        ff_back_kernel,
        grid=(rows // FF_ROWS,),
        in_specs=[ff_rows(depth), pl.BlockSpec(w.shape, lambda i: (0, 0, 0)), ff_rows(wide)],
        out_specs=ff_rows(wide),
        out_shape=jax.ShapeDtypeStruct((rows, wide), BF16),
        compiler_params=PARAMS,
        cost_estimate=pl.CostEstimate(flops=rows * depth * wide, bytes_accessed=20 * 2**20, transcendentals=0),
    )(grad, w, kept)


def cut_kernel(in_ref, out_ref, in_blocks, out_blocks, wide):
    group, _, double = in_blocks.shape
    tile, ff = double // 2, out_ref.shape[1]
    span = group * tile
    odd = ff % 128
    live = lax.broadcasted_iota(jnp.int32, (in_ref.shape[0], span), 1) < ff
    wide[...] = jnp.zeros_like(wide)
    wide[:, : 2 * ff] = in_ref[...].astype(F32)
    gate = jnp.where(live, wide[:, :span], 0.0)
    up = pltpu.roll(wide[:, ff - odd : ff - odd + span], span - odd, 1)
    up = jnp.where(live, up, 0.0)
    wide[:, :span] = jnp.zeros_like(live, F32)
    wide[:, :ff] = out_ref[...].astype(F32)
    down = wide[:, :span]
    for g in range(group):
        at = slice(g * tile, (g + 1) * tile)
        in_blocks[g] = jnp.concatenate([gate[:, at], up[:, at]], axis=1).astype(BF16)
        out_blocks[g] = down[:, at].astype(BF16)


def cut_ff(w_in, w_out, group, tile):
    rows, ff = w_out.shape
    return pl.pallas_call(
        cut_kernel,
        grid=(rows // 16,),
        in_specs=[pl.BlockSpec((16, 2 * ff), lambda i: (i, 0)), pl.BlockSpec((16, ff), lambda i: (i, 0))],
        out_specs=[
            pl.BlockSpec((group, 16, 2 * tile), lambda i: (0, i, 0)),
            pl.BlockSpec((group, 16, tile), lambda i: (0, i, 0)),
        ],
        out_shape=[
            jax.ShapeDtypeStruct((group, rows, 2 * tile), BF16),
            jax.ShapeDtypeStruct((group, rows, tile), BF16),
        ],
        scratch_shapes=[pltpu.VMEM((16, -(-(ff + group * tile) // 128) * 128), F32)],
        compiler_params=SMALL,
    )(w_in, w_out)


def join_kernel(in_blocks, out_blocks, in_ref, out_ref):
    group, _, double = in_blocks.shape
    tile, ff = double // 2, out_ref.shape[1]
    odd = ff % 128
    blocks = [in_blocks[g].astype(F32) for g in range(group)]
    gate = jnp.concatenate([block[:, :tile] for block in blocks], axis=1)
    up = jnp.concatenate([block[:, tile:] for block in blocks], axis=1)
    up = pltpu.roll(up, odd, 1)
    lane = lax.broadcasted_iota(jnp.int32, (up.shape[0], 128), 1)
    in_ref[:, : ff - odd] = gate[:, : ff - odd]
    in_ref[:, ff - odd : ff - odd + 128] = jnp.where(lane < odd, gate[:, ff - odd : ff - odd + 128], up[:, :128])
    in_ref[:, ff - odd + 128 :] = up[:, 128 : ff + odd]
    down = jnp.concatenate([out_blocks[g].astype(F32) for g in range(group)], axis=1)
    out_ref[...] = down[:, :ff]


def join_ff(in_blocks, out_blocks, ff):
    group, rows, tile = out_blocks.shape
    return pl.pallas_call(
        join_kernel,
        grid=(rows // 16,),
        in_specs=[
            pl.BlockSpec((group, 16, 2 * tile), lambda i: (0, i, 0)),
            pl.BlockSpec((group, 16, tile), lambda i: (0, i, 0)),
        ],
        out_specs=[pl.BlockSpec((16, 2 * ff), lambda i: (i, 0)), pl.BlockSpec((16, ff), lambda i: (i, 0))],
        out_shape=[jax.ShapeDtypeStruct((rows, 2 * ff), F32), jax.ShapeDtypeStruct((rows, ff), F32)],
        compiler_params=SMALL,
    )(in_blocks, out_blocks)


def closing_kernel(zs, sum_ref, rows_ref, qkv_ref, total_ref, got, lines, *refs):
    send, recv, local, line_send, line_recv = refs
    y, x, c = here()
    z = lax.axis_index("z")
    me = place(y, x, c)
    wide = got.shape[2]
    width = wide // 3
    piece = got.shape[1]
    found = swap_peers(zs, ("line",))
    greet([name for _, name in found])
    copies, comes = [], []
    for k, (peer, name) in enumerate(found[:7]):
        sems = dict(send_sem=send.at[k], recv_sem=recv.at[k], device_id=name, device_id_type=MESH)
        copies.append(pltpu.make_async_remote_copy(src_ref=rows_ref.at[peer], dst_ref=got.at[me], **sems))
        comes.append(pltpu.make_async_remote_copy(src_ref=got.at[peer], dst_ref=got.at[peer], **sems))
    for k, (peer, name) in enumerate(found[7:]):
        sems = dict(send_sem=line_send.at[k], recv_sem=line_recv.at[k], device_id=name, device_id_type=MESH)
        copies.append(pltpu.make_async_remote_copy(src_ref=sum_ref, dst_ref=lines.at[z], **sems))
        comes.append(pltpu.make_async_remote_copy(src_ref=lines.at[peer], dst_ref=lines.at[peer], **sems))
    for copy in copies:
        copy.start()
    keeps = [
        pltpu.make_async_copy(rows_ref.at[me], got.at[me], local.at[0]),
        pltpu.make_async_copy(sum_ref, lines.at[z], local.at[1]),
    ]
    for keep in keeps:
        keep.start()
    for come in comes:
        come.wait_recv()
    for keep in keeps:
        keep.wait()
    for g in range(8):
        for j in range(3):
            at = pl.ds(j * D + g * width, width)
            qkv_ref[:, at] = got[g, :, j * width : (j + 1) * width].astype(F32)
    total = lines[0]
    for k in range(1, zs):
        total += lines[k]
    part = total[:, :piece]
    for k in range(1, zs):
        part = jnp.where(z == k, total[:, k * piece : (k + 1) * piece], part)
    total_ref[...] = part
    for copy in copies:
        copy.wait_send()


def closing(zs, sums, rows):
    _, piece, columns = rows.shape
    width = columns // 3
    return pl.pallas_call(
        functools.partial(closing_kernel, zs),
        out_shape=[
            jax.ShapeDtypeStruct((piece, 3 * D), F32),
            jax.ShapeDtypeStruct((8, piece), F32),
        ],
        in_specs=[ROWS, ANY],
        out_specs=[ROWS] * 2,
        scratch_shapes=[
            pltpu.VMEM((8, piece, 3 * width), BF16),
            pltpu.VMEM((zs, 8, width), F32),
            pltpu.SemaphoreType.DMA((7,)),
            pltpu.SemaphoreType.DMA((7,)),
            pltpu.SemaphoreType.DMA((2,)),
            pltpu.SemaphoreType.DMA((zs - 1,)),
            pltpu.SemaphoreType.DMA((zs - 1,)),
        ],
        compiler_params=pltpu.CompilerParams(collective_id=5, has_side_effects=True, vmem_limit_bytes=24 * 2**20),
        cost_estimate=pl.CostEstimate(flops=0, bytes_accessed=50 * 2**20, transcendentals=0),
    )(sums, rows)


def on_device(sizes, x_in, d_out, w_qkv, w_dense, w_in, w_out, gone, bone, gtwo, btwo, flags, span_start, span_len):
    gy, gx, cores, zs = sizes
    piece = w_qkv.shape[0]
    ff = w_out.shape[1]
    group = gy * gx * cores
    width = D // group
    tile = -(-ff // (group * 64)) * 64
    own = gy == 2

    def permute(array):
        lead = array.shape[:-1]
        return jnp.swapaxes(array.reshape(lead + (group, zs, piece)), -3, -2).reshape(lead + (D,))

    def restore(array):
        lead = array.shape[:-1]
        return jnp.swapaxes(array.reshape(lead + (zs, group, piece)), -3, -2).reshape(lead + (D,))

    def swap(name, arrays, kinds):
        if own:
            return group_swap(name, zs, arrays, kinds)
        ways = {
            "swap": lambda a: lax.all_to_all(a, GROUP, 0, 0, tiled=True),
            "group": lambda a: lax.all_gather(a, GROUP, axis=0),
            "line": lambda a: lax.all_gather(a, "z", axis=0),
        }
        return [ways[k](a) for a, k in zip(arrays, kinds)]

    def spread_rows(block):
        return lax.all_gather(block, GROUP, axis=0, tiled=True)

    rows_f32 = jax.ShapeDtypeStruct((SEQ_LEN, D), F32)
    rows_low = jax.ShapeDtypeStruct((SEQ_LEN, D), BF16)
    sums_type = jax.ShapeDtypeStruct((8, D), F32)

    def fold(partial):
        return lax.psum_scatter(partial.astype(BF16), GROUP, scatter_dimension=0, tiled=True).astype(F32)

    def stack_sums(*arrays):
        return jnp.pad(jnp.stack([jnp.sum(a, axis=0) for a in arrays]), ((0, 6), (0, 0)))

    def fold_one(left, right, x, gains):
        if own:
            kinds = [rows_f32, rows_f32, jax.ShapeDtypeStruct((SEQ_LEN, 128), F32)]
            whole, first, normal, inverse = group_fold(0, zs, "one", left, right, gains, [x], kinds)
            return whole.reshape(left.shape[0], D), first, normal, inverse
        first, normal, inverse = first_norm(permute(deep_alpha * x.astype(F32) + fold(dot(left, right))), gains)
        return spread_rows(first.astype(BF16)), first, normal, inverse

    def ff_turn(x, w_in, w_out, first, grad, gains):
        if own:
            whole, kept, w_out, result, d_pre, sums, d_out = turn(zs, x, w_in, w_out, gains, first, grad)
            rows = x.shape[0]
            return whole.reshape(rows, D), kept.reshape(rows, -1), w_out, result, d_pre, sums, d_out
        w_out = lax.all_gather(w_out, "z", axis=0)
        hidden, kept = ff_forward(x, w_in)
        grad = grad.astype(F32)
        right = jnp.swapaxes(w_out, 0, 1).reshape(-1, D)
        result, d_pre, terms = second_norm(fold(dot(hidden, right)), first, grad, gains)
        whole = spread_rows(d_pre.astype(BF16))
        d_out = jnp.swapaxes(dot_rows(hidden, whole).reshape(-1, zs, D // zs), 0, 1).astype(BF16)
        return whole, kept, w_out, result.astype(BF16), d_pre, stack_sums(terms, grad), d_out

    def fold_back(left, right, d_pre_two, normal, inverse, gains):
        if own:
            kinds = [rows_f32, sums_type]
            whole, d_pre, sums = group_fold(7, zs, "back", left, right, gains, [d_pre_two, normal, inverse], kinds)
            return whole.reshape(left.shape[0], D), d_pre, sums
        d_pre, terms, d_first = first_back(fold(dot_cols(left, right)), d_pre_two, normal, inverse, gains)
        return spread_rows(restore(d_pre).astype(BF16)), d_pre, stack_sums(terms, d_first)

    def fold_last(left, right, d_pre, gains, extras, kinds):
        if own:
            return group_fold(8, zs, "last", left, right, gains, [d_pre], [rows_low], extras, kinds)
        out = restore((deep_alpha * d_pre + fold(dot_cols(left, right))).astype(BF16))
        return [out] + swap(8, extras, kinds)

    def gather(block):
        return lax.all_gather(block, "z", axis=0, tiled=True)

    def scatter(partial):
        return lax.psum_scatter(partial.astype(BF16), "z", scatter_dimension=0, tiled=True)

    masked = jnp.max(flags) > 0
    prefix = jnp.where(masked, SEQ_LEN, SEQ_LEN - span_len[0])
    info = jnp.concatenate([gone, bone, gtwo, btwo, jnp.stack([prefix, span_start[0]]).astype(BF16)])
    info = jnp.pad(info[None, :], ((0, 15), (0, -info.shape[0] % 128)))

    qkv_blocks = jnp.moveaxis(w_qkv.reshape(piece, 3, group, width), 2, 0).reshape(group, piece, 3 * width)
    w_dense_part = gather(w_dense)
    qkv_blocks, info = swap(2, [qkv_blocks, info], ("swap", "group"))
    w_qkv_part = gather(qkv_blocks.reshape(group * piece, 3 * width))
    info = info[:, 0]
    place_info = info[:, 4 * piece : 4 * piece + 2].astype(jnp.int32)
    prefix, start = place_info[:, 0], place_info[:, 1]
    cosine, sine = tables(prefix, start)
    in_blocks, out_blocks = cut_ff(w_in, w_out, group, tile)
    info = jnp.pad(info, ((0, -group % 16), (0, 0)))
    in_blocks, out_blocks, qkv_blocks, w_dense_part, cosine, sine = lax.optimization_barrier(
        (in_blocks, out_blocks, qkv_blocks, w_dense_part, cosine, sine)
    )
    swapped, kinds = [in_blocks, out_blocks, info], ("swap", "swap", "line")
    if own:
        x_all, grad_two, in_blocks, out_blocks, info = enter(zs, x_in, d_out, swapped, kinds)
        x_all = x_all.reshape(group * SEQ_LEN, D)
    else:
        x_all, grad_two = spread_rows(permute(x_in)), permute(d_out)
        in_blocks, out_blocks, info = swap(3, swapped, kinds)
    w_in_part = gather(in_blocks.reshape(group * piece, 2 * tile))
    out_rows = out_blocks.reshape(group * piece, tile).T
    gains = info[:, :group, : 4 * piece].astype(F32).reshape(zs, group, 4, piece)
    gains = jnp.pad(jnp.transpose(gains, (2, 0, 1, 3)).reshape(4, D), ((0, 4), (0, 0)))
    w_qkv_part, x_all, gains, out_rows = lax.optimization_barrier((w_qkv_part, x_all, gains, out_rows))
    packed = dot(x_all, w_qkv_part)
    qkv, context = attend(prefix, packed, cosine, sine)
    first_all, first, normal_one, inverse_one = fold_one(context, w_dense_part, x_in, gains)
    d_branch, kept, w_out_part, layer_out, d_pre_two, sums_two, d_w_out = ff_turn(
        first_all, w_in_part, out_rows, first, grad_two, gains
    )
    layer_out = restore(layer_out)
    d_w_out = lax.psum_scatter(d_w_out, "z", scatter_dimension=0)
    d_projected = ff_backward(d_branch, w_out_part, kept)
    d_w_in = dot_rows(first_all, d_projected).astype(BF16)
    d_w_in, d_projected = lax.optimization_barrier((d_w_in, d_projected))
    d_w_in = scatter(d_w_in)
    d_attn, d_pre_one, sums_one = fold_back(d_projected, w_in_part, d_pre_two, normal_one, inverse_one, gains)
    d_attn, d_w_out = lax.optimization_barrier((d_attn, d_w_out))
    d_context = dot_cols(d_attn, w_dense_part).astype(BF16)
    d_packed = attend_back(prefix, qkv, d_context, cosine, sine)
    d_w_qkv = dot_rows(x_all, d_packed).astype(BF16)
    sums = jnp.concatenate([sums_one[:2], sums_two[:2], jnp.zeros((4, D), F32)])
    d_w_qkv = with_layout_constraint(d_w_qkv, Layout((0, 1)))
    d_packed, d_w_qkv, d_w_in, sums, d_attn = lax.optimization_barrier((d_packed, d_w_qkv, d_w_in, sums, d_attn))
    d_w_qkv = scatter(d_w_qkv)
    d_dense = dot_rows(context, d_attn).astype(BF16)
    d_dense, d_packed = lax.optimization_barrier((d_dense, d_packed))
    d_dense = scatter(d_dense)
    d_w_in, d_w_out = d_w_in.reshape(group, piece, 2 * tile), d_w_out.T.reshape(group, piece, tile)
    d_input, d_w_in, d_w_out, sums = fold_last(
        d_packed, w_qkv_part, d_pre_one, gains, [d_w_in, d_w_out, sums], ("swap", "swap", "group")
    )
    sums = jnp.sum(sums, axis=0).reshape(8, zs, group, piece)
    sums = lax.dynamic_index_in_dim(sums, lax.axis_index(GROUP), 2, keepdims=False).reshape(8, width)
    out_in, out_out = join_ff(d_w_in, d_w_out, ff)
    out_in, out_out, d_input, d_w_qkv, sums = lax.optimization_barrier((out_in, out_out, d_input, d_w_qkv, sums))
    if own:
        out_qkv, sums = closing(zs, sums, d_w_qkv.reshape(group, piece, 3 * width))
    else:
        d_w_qkv, sums = swap(5, [d_w_qkv.reshape(group, piece, 3 * width), sums], ("swap", "line"))
        out_qkv = jnp.transpose(d_w_qkv.astype(F32).reshape(group, piece, 3, width), (1, 2, 0, 3))
        out_qkv = out_qkv.reshape(piece, 3 * D)
        sums = jnp.sum(sums, axis=0).reshape(8, zs, piece)
        sums = lax.dynamic_index_in_dim(sums, lax.axis_index("z"), 1, keepdims=False)
    out_qkv, sums, d_dense = lax.optimization_barrier((out_qkv, sums, d_dense))
    out_dense = d_dense.astype(F32)
    return layer_out, d_input, out_qkv, out_dense, out_in, out_out, sums[0], sums[1], sums[2], sums[3]


def solution(mesh):
    grp, shard = mesh.shape["grp"], mesh.shape["shard"]
    sizes = (grp // 4, 2, 2, shard)
    inner = Mesh(mesh.devices.reshape(sizes), ALL)
    rows, flat = P(ALL, None), P(ALL)
    return jax.shard_map(
        functools.partial(on_device, sizes),
        mesh=inner,
        in_specs=(rows,) * 6 + (flat,) * 7,
        out_specs=(rows,) * 6 + (flat,) * 4,
        check_vma=False,
    )
```

```python
import functools

import jax
import jax.numpy as jnp
from jax import lax
from jax.experimental import pallas as pl
from jax.experimental.pallas import tpu as pltpu
from jax.experimental.layout import Layout, with_layout_constraint
from jax.sharding import Mesh
from jax.sharding import PartitionSpec as P

HEADS = 16
HEAD = 128
SEQ_LEN = 224
D = HEADS * HEAD
deep_alpha = 6.928203230275509
norm_eps = 1e-05
far_below = -1e30
scale = HEAD ** (-0.5)

ALL = ("gy", "gx", "core", "z")
GROUP = ("gy", "gx", "core")
MESH = pl.DeviceIdType.MESH
F32 = jnp.float32
BF16 = jnp.bfloat16


def dot(left, right):
    return jnp.dot(left, right, preferred_element_type=F32)


def dot_rows(left, right):
    return lax.dot_general(left, right, (((0,), (0,)), ((), ())), preferred_element_type=F32)


def dot_cols(left, right):
    return lax.dot_general(left, right, (((1,), (1,)), ((), ())), preferred_element_type=F32)


def swap_halves(block):
    lane = lax.broadcasted_iota(jnp.int32, block.shape, 1)
    return jnp.where((lane & 32) == 0, pltpu.roll(block, 96, 1), pltpu.roll(block, 32, 1))


def seen(prefix):
    row = lax.broadcasted_iota(jnp.int32, (SEQ_LEN, SEQ_LEN), 0)
    col = lax.broadcasted_iota(jnp.int32, (SEQ_LEN, SEQ_LEN), 1)
    return (col < prefix) | (col <= row)


def softmax(queries, keys, visible):
    scores = jnp.where(visible, dot_cols(queries, keys), far_below)
    weights = jnp.exp(scores - jnp.max(scores, axis=1, keepdims=True))
    return weights / jnp.sum(weights, axis=1, keepdims=True)


def attend_kernel(prefix_ref, packed_ref, cos_ref, sin_ref, qkv_ref, context_ref):
    width = context_ref.shape[1]
    visible = seen(prefix_ref[pl.program_id(0)])
    cosine = cos_ref[0]
    sine = sin_ref[0]
    for head in range(width // HEAD):
        at = pl.ds(head * HEAD, HEAD)
        at_k = pl.ds(width + head * HEAD, HEAD)
        at_v = pl.ds(2 * width + head * HEAD, HEAD)
        raw = packed_ref[:, at]
        queries = ((raw * cosine + swap_halves(raw) * sine) * scale).astype(BF16)
        raw = packed_ref[:, at_k]
        keys = (raw * cosine + swap_halves(raw) * sine).astype(BF16)
        values = packed_ref[:, at_v].astype(BF16)
        qkv_ref[:, at] = queries
        qkv_ref[:, at_k] = keys
        qkv_ref[:, at_v] = values
        probs = softmax(queries, keys, visible).astype(BF16)
        context_ref[:, at] = dot(probs, values).astype(BF16)


def attend_back_kernel(prefix_ref, qkv_ref, d_context_ref, cos_ref, sin_ref, d_packed_ref):
    width = d_context_ref.shape[1]
    visible = seen(prefix_ref[pl.program_id(0)])
    cosine = cos_ref[0]
    sine = sin_ref[0]
    for head in range(width // HEAD):
        at = pl.ds(head * HEAD, HEAD)
        at_k = pl.ds(width + head * HEAD, HEAD)
        at_v = pl.ds(2 * width + head * HEAD, HEAD)
        queries = qkv_ref[:, at]
        keys = qkv_ref[:, at_k]
        values = qkv_ref[:, at_v]
        d_context = d_context_ref[:, at]
        probs = softmax(queries, keys, visible)
        d_packed_ref[:, at_v] = dot_rows(probs.astype(BF16), d_context).astype(BF16)
        d_probs = dot_cols(d_context, values)
        inner = jnp.sum(probs * d_probs, axis=1, keepdims=True)
        d_scores = (probs * (d_probs - inner)).astype(BF16)
        grad = dot(d_scores, keys) * scale
        d_packed_ref[:, at] = (grad * cosine - swap_halves(grad) * sine).astype(BF16)
        grad = dot_rows(d_scores, queries)
        d_packed_ref[:, at_k] = (grad * cosine - swap_halves(grad) * sine).astype(BF16)


def by_sequence(width):
    return pl.BlockSpec((SEQ_LEN, width), lambda s: (s, 0))


TABLE = pl.BlockSpec((1, SEQ_LEN, HEAD), lambda s: (s, 0, 0))
SCALARS = pl.BlockSpec(memory_space=pltpu.SMEM)
PARAMS = pltpu.CompilerParams(vmem_limit_bytes=56 * 2**20)
SMALL = pltpu.CompilerParams(vmem_limit_bytes=24 * 2**20)


def attend(prefix, packed, cosine, sine):
    rows, width = packed.shape[0], packed.shape[1] // 3
    return pl.pallas_call(
        attend_kernel,
        grid=(rows // SEQ_LEN,),
        in_specs=[SCALARS, by_sequence(3 * width), TABLE, TABLE],
        out_specs=[by_sequence(3 * width), by_sequence(width)],
        out_shape=[
            jax.ShapeDtypeStruct((rows, 3 * width), BF16),
            jax.ShapeDtypeStruct((rows, width), BF16),
        ],
        compiler_params=PARAMS,
    )(prefix, packed, cosine, sine)


def attend_back(prefix, qkv, d_context, cosine, sine):
    rows, width = d_context.shape
    return pl.pallas_call(
        attend_back_kernel,
        grid=(rows // SEQ_LEN,),
        in_specs=[SCALARS, by_sequence(3 * width), by_sequence(width), TABLE, TABLE],
        out_specs=by_sequence(3 * width),
        out_shape=jax.ShapeDtypeStruct((rows, 3 * width), BF16),
        compiler_params=PARAMS,
    )(prefix, qkv, d_context, cosine, sine)


def tables(prefix, start):
    place = jnp.arange(SEQ_LEN, dtype=jnp.int32)
    in_span = place[None, :] >= prefix[:, None]
    pos_one = jnp.where(in_span, start[:, None], place[None, :])
    pos_two = jnp.where(in_span, place[None, :] - prefix[:, None] + 1, 0)
    lane = jnp.arange(HEAD)
    freqs = 10000.0 ** (-2.0 * (lane % 32).astype(F32) / 64)
    place_of = jnp.where(lane[None, None, :] < 64, pos_one[:, :, None], pos_two[:, :, None])
    angles = place_of.astype(F32) * freqs
    sign = jnp.where(lane % 64 < 32, -1.0, 1.0)
    return jnp.cos(angles), jnp.sin(angles) * sign


def norm_parts(values):
    center = values - jnp.mean(values, axis=-1, keepdims=True)
    inverse = lax.rsqrt(jnp.mean(center * center, axis=-1, keepdims=True) + norm_eps)
    return center * inverse, inverse


def norm_back(normal, inverse, gain, grad):
    scaled = gain * grad
    return inverse * (
        scaled
        - jnp.mean(scaled, axis=-1, keepdims=True)
        - normal * jnp.mean(scaled * normal, axis=-1, keepdims=True)
    )


def gate_parts(gate):
    phi = 0.5 * (1.0 + lax.erf(gate * 0.7071067811865476))
    slope = phi + gate * jnp.exp(-0.5 * gate * gate) * 0.3989422804014327
    return gate * phi, slope


def here():
    return lax.axis_index("gy"), lax.axis_index("gx"), lax.axis_index("core")


def place(y, x, c):
    return (y * 2 + x) * 2 + c


def greet(peers):
    barrier = pltpu.get_barrier_semaphore()
    for peer in peers:
        pl.semaphore_signal(barrier, inc=1, device_id=peer, device_id_type=MESH)
    pl.semaphore_wait(barrier, len(peers))


def spread_block(cut, base, block_ref, out_ref, send, recv, local):
    rows = block_ref.shape[0]
    y, x, c = here()
    to_x, to_y, to_c = {"gx": 1 - x}, {"gy": 1 - y}, {"core": 1 - c}
    me, by_x, by_y, far = place(y, x, c), place(y, 1 - x, c), place(1 - y, x, c), place(1 - y, 1 - x, c)
    low, high = pl.ds(0, cut), pl.ds(cut, rows - cut)

    def push(k, src, dst, to):
        copy = pltpu.make_async_remote_copy(
            src_ref=src, dst_ref=dst, send_sem=send.at[base + k], recv_sem=recv.at[base + k], device_id=to, device_id_type=MESH
        )
        copy.start()
        return copy

    def landed(k, dst):
        pltpu.make_async_remote_copy(
            src_ref=dst, dst_ref=dst, send_sem=send.at[base + k], recv_sem=recv.at[base + k], device_id=to_c, device_id_type=MESH
        ).wait_recv()

    sent = [
        push(0, block_ref.at[low], out_ref.at[me, low], to_x),
        push(1, block_ref.at[high], out_ref.at[me, high], to_y),
        push(2, block_ref.at[high], out_ref.at[me, high], to_x),
        push(3, block_ref.at[low], out_ref.at[me, low], to_y),
        push(4, block_ref, out_ref.at[me], to_c),
    ]
    keep = pltpu.make_async_copy(block_ref, out_ref.at[me], local)
    keep.start()
    landed(0, out_ref.at[by_x, low])
    sent.append(push(5, out_ref.at[by_x, low], out_ref.at[by_x, low], to_y))
    sent.append(push(7, out_ref.at[by_x, low], out_ref.at[by_x, low], to_c))
    landed(1, out_ref.at[by_y, high])
    sent.append(push(6, out_ref.at[by_y, high], out_ref.at[by_y, high], to_x))
    sent.append(push(8, out_ref.at[by_y, high], out_ref.at[by_y, high], to_c))
    landed(2, out_ref.at[by_x, high])
    sent.append(push(9, out_ref.at[by_x, high], out_ref.at[by_x, high], to_c))
    landed(3, out_ref.at[by_y, low])
    sent.append(push(10, out_ref.at[by_y, low], out_ref.at[by_y, low], to_c))
    landed(5, out_ref.at[far, low])
    sent.append(push(11, out_ref.at[far, low], out_ref.at[far, low], to_c))
    landed(6, out_ref.at[far, high])
    sent.append(push(12, out_ref.at[far, high], out_ref.at[far, high], to_c))
    other, other_x, other_y, other_far = (
        place(y, x, 1 - c),
        place(y, 1 - x, 1 - c),
        place(1 - y, x, 1 - c),
        place(1 - y, 1 - x, 1 - c),
    )
    landed(4, out_ref.at[other])
    landed(7, out_ref.at[other_x, low])
    landed(8, out_ref.at[other_y, high])
    landed(9, out_ref.at[other_x, high])
    landed(10, out_ref.at[other_y, low])
    landed(11, out_ref.at[other_far, low])
    landed(12, out_ref.at[other_far, high])
    keep.wait()
    for copy in sent:
        copy.wait_send()


ANY = pl.BlockSpec(memory_space=pl.ANY)


def swap_peers(zs, kinds):
    y, x, c = here()
    z = lax.axis_index("z")
    found = []
    for k in range(1, 8):
        peer = ((y + k // 4) % 2, (x + k // 2 % 2) % 2, (c + k % 2) % 2)
        found.append((place(*peer), {"gy": peer[0], "gx": peer[1], "core": peer[2]}))
    if "line" in kinds:
        found += [((z + k) % zs, {"z": (z + k) % zs}) for k in range(1, zs)]
    return found


def swap_begin(zs, kinds, blocks, outs, send, recv, local):
    copies, comes, keeps = [], [], []
    found = swap_peers(zs, kinds)
    for i, kind in enumerate(kinds):
        me = lax.axis_index("z") if kind == "line" else place(*here())
        for k, (peer, name) in enumerate(found[7:] if kind == "line" else found[:7]):
            src = blocks[i].at[peer] if kind == "swap" else blocks[i]
            landing = outs[i].at[peer]
            sems = dict(send_sem=send.at[i, k], recv_sem=recv.at[i, k], device_id=name, device_id_type=MESH)
            copies.append(pltpu.make_async_remote_copy(src_ref=src, dst_ref=outs[i].at[me], **sems))
            comes.append(pltpu.make_async_remote_copy(src_ref=landing, dst_ref=landing, **sems))
            copies[-1].start()
        own = blocks[i].at[me] if kind == "swap" else blocks[i]
        keeps.append(pltpu.make_async_copy(own, outs[i].at[me], local.at[i]))
        keeps[-1].start()

    def finish():
        for come in comes:
            come.wait_recv()
        for copy in copies:
            copy.wait_send()
        for keep in keeps:
            keep.wait()

    return finish


SWAP_LEAD = {"swap": lambda zs: (), "group": lambda zs: (8,), "line": lambda zs: (zs,)}


def swap_shapes(zs, arrays, kinds):
    return [jax.ShapeDtypeStruct(SWAP_LEAD[k](zs) + a.shape, a.dtype) for a, k in zip(arrays, kinds)]


def swap_scratch(zs, kinds):
    n, most = len(kinds), max(7, zs - 1)
    return [
        pltpu.SemaphoreType.DMA((n, most)),
        pltpu.SemaphoreType.DMA((n, most)),
        pltpu.SemaphoreType.DMA((n,)),
    ]


SLAB = 16
ROWS = pl.BlockSpec(memory_space=pltpu.VMEM)
CHIP_COLS = 256


def by_rows(value, zs, piece):
    group = D // (zs * piece)
    order = [g * zs + z for z in range(zs) for g in range(group)]
    return jnp.concatenate([value[:, m * piece : (m + 1) * piece] for m in order], axis=1)


def in_order(value, zs, piece):
    group = D // (zs * piece)
    order = [z * group + g for g in range(group) for z in range(zs)]
    return jnp.concatenate([value[:, m * piece : (m + 1) * piece] for m in order], axis=1)


def first_norm(values, gains):
    normal, inverse = norm_parts(values)
    first = normal * gains[0:1] + gains[1:2]
    return first, normal, inverse


def second_norm(total, first, grad, gains):
    normal, inverse = norm_parts(deep_alpha * first + total)
    return normal * gains[2:3] + gains[3:4], norm_back(normal, inverse, gains[2:3], grad), grad * normal


def first_back(total, d_pre_two, normal, inverse, gains):
    d_first = deep_alpha * d_pre_two + total
    return norm_back(normal, inverse, gains[0:1], d_first), d_first * normal, d_first


def fold_kernel(mode, across, zs, piece, n_aux, n_out, kinds, *refs):
    left_ref, right_ref, gains_ref = refs[:3]
    aux_refs = refs[3 : 3 + n_aux]
    refs = refs[3 + n_aux :]
    n_swap = len(kinds)
    swap_in, refs = refs[:n_swap], refs[n_swap:]
    spread = mode != "last"
    if spread:
        all_ref, refs = refs[0], refs[1:]
    out_refs, refs = refs[:n_out], refs[n_out:]
    swap_out, refs = refs[:n_swap], refs[n_swap:]
    aux, refs = refs[:n_aux], refs[n_aux:]
    outs, refs = refs[:n_out], refs[n_out:]
    left, right, part, got, near_x, near_y, from_x, from_y, block, acc, send, recv, local = refs[:13]
    rows, width = block.shape
    cut = near_x.shape[0]
    y, x, c = here()
    to_x, to_y, to_c = {"gx": 1 - x}, {"gy": 1 - y}, {"core": 1 - c}
    chips = [(1 - y, 1 - x), (y, 1 - x), (1 - y, x), (y, x)]
    low, high = pl.ds(0, cut), pl.ds(cut, rows - cut)

    def push(k, src, dst, to):
        copy = pltpu.make_async_remote_copy(
            src_ref=src, dst_ref=dst, send_sem=send.at[k], recv_sem=recv.at[k], device_id=to, device_id_type=MESH
        )
        copy.start()
        return copy

    def add(k, extra, start, size, offset=0):
        @pl.loop(0, size // SLAB)
        def _(step):
            at = pl.ds(pl.multiple_of(start + step * SLAB, SLAB), SLAB)
            of = pl.ds(pl.multiple_of(start - offset + step * SLAB, SLAB), SLAB)
            part[k, c, at] = (part[k, c, at].astype(F32) + extra[of].astype(F32)).astype(BF16)

    loads = [pltpu.make_async_copy(left_ref.at[a * 2 + b], left.at[k], local.at[k]) for k, (a, b) in enumerate(chips)]
    load_right = pltpu.make_async_copy(right_ref, right, local.at[4])
    load_aux = [pltpu.make_async_copy(r, v, local.at[5 + k]) for k, (r, v) in enumerate(zip(aux_refs, aux))]
    loads[0].start()
    load_right.start()
    for load in loads[1:] + load_aux:
        load.start()
    if n_swap:
        greet([name for _, name in swap_peers(1, kinds)])
        swap_finish = swap_begin(1, kinds, swap_in, swap_out, *refs[13:])
    else:
        greet([to_x, to_y, to_c])

    def product(k):
        loads[k].wait()

        @pl.loop(0, width // CHIP_COLS)
        def _(step):
            at = pl.ds(pl.multiple_of(step * CHIP_COLS, CHIP_COLS), CHIP_COLS)
            here_part = dot_cols(left[k], right[at]) if across else dot(left[k], right[:, at])
            part[k, 0, :, at] = here_part[:rows].astype(BF16)
            part[k, 1, :, at] = here_part[rows:].astype(BF16)

        return push(k, part.at[k, 1 - c], got.at[k], to_c)

    load_right.wait()
    sent = [product(0), product(1)]
    sent[0].wait_recv()
    add(0, got.at[0], 0, rows)
    far_x = push(4, part.at[0, c, low], near_x, to_x)
    far_y = push(5, part.at[0, c, high], near_y, to_y)
    sent.append(product(2))
    sent[1].wait_recv()
    add(1, got.at[1], 0, rows)
    plain_x = push(6, part.at[1, c, low], from_x.at[low], to_x)
    sent[2].wait_recv()
    add(2, got.at[2], 0, rows)
    plain_y = push(7, part.at[2, c, high], from_y.at[high], to_y)
    sent.append(product(3))
    far_y.wait_recv()
    add(1, near_y, cut, rows - cut, cut)
    more_x = push(8, part.at[1, c, high], from_x.at[high], to_x)
    far_x.wait_recv()
    add(2, near_x, 0, cut)
    more_y = push(9, part.at[2, c, low], from_y.at[low], to_y)
    sent[3].wait_recv()
    for load in load_aux:
        load.wait()
    plain_x.wait_recv()
    plain_y.wait_recv()
    more_x.wait_recv()
    more_y.wait_recv()
    gains = gains_ref[...]
    acc[...] = jnp.zeros_like(acc)

    @pl.loop(0, rows // SLAB)
    def _(step):
        at = pl.ds(pl.multiple_of(step * SLAB, SLAB), SLAB)
        total = part[3, c, at].astype(F32) + got[3, at].astype(F32) + from_x[at].astype(F32) + from_y[at].astype(F32)
        held = [a[at].astype(F32) for a in aux]
        if mode == "one":
            first, normal, inverse = first_norm(by_rows(deep_alpha * held[0] + total, zs, piece), gains)
            outs[0][at] = first
            outs[1][at] = normal
            outs[2][at] = jnp.broadcast_to(inverse, (SLAB, 128))
            block[at] = first.astype(BF16)
        elif mode == "back":
            d_pre, terms, d_first = first_back(total, held[0], held[1], held[2][:, 0:1], gains)
            outs[0][at] = d_pre
            block[at] = in_order(d_pre, zs, piece).astype(BF16)
            acc[0] += terms
            acc[1] += d_first
        else:
            outs[0][at] = in_order(deep_alpha * held[0] + total, zs, piece).astype(BF16)

    if mode == "back":
        outs[-1][0:1] = jnp.sum(acc[0], axis=0, keepdims=True)
        outs[-1][1:2] = jnp.sum(acc[1], axis=0, keepdims=True)
    stores = [pltpu.make_async_copy(v, r, local.at[5 + n_aux + k]) for k, (v, r) in enumerate(zip(outs, out_refs))]
    for store in stores:
        store.start()
    for copy in sent + [far_x, far_y, plain_x, plain_y, more_x, more_y]:
        copy.wait_send()
    if n_swap:
        swap_finish()
    if spread:
        spread_block(cut, 10, block, all_ref, send, recv, local.at[4])
    for store in stores:
        store.wait()


def group_fold(name, zs, mode, left, right, gains, aux, out_types, extras=(), kinds=()):
    across = mode != "one"
    rows, depth = left.shape[0] // 8, left.shape[1]
    width = gains.shape[1]
    cut = rows // 2
    spread = mode != "last"
    out_shape = [jax.ShapeDtypeStruct((8, rows, width), BF16)] * spread + out_types
    n, n_swap = len(aux), len(extras)
    n_sems = 23 if spread else 10
    return pl.pallas_call(
        functools.partial(fold_kernel, mode, across, zs, width // (8 * zs), n, len(out_types), kinds),
        out_shape=out_shape + swap_shapes(1, extras, kinds),
        in_specs=[ANY, ANY, ROWS] + [ANY] * (n + n_swap),
        out_specs=[ANY] * (spread + len(out_types) + n_swap),
        scratch_shapes=[pltpu.VMEM(a.shape, a.dtype) for a in list(aux) + out_types]
        + [
            pltpu.VMEM((4, 2 * rows, depth), BF16),
            pltpu.VMEM(right.shape, BF16),
            pltpu.VMEM((4, 2, rows, width), BF16),
            pltpu.VMEM((4, rows, width), BF16),
            pltpu.VMEM((cut, width), BF16),
            pltpu.VMEM((rows - cut, width), BF16),
            pltpu.VMEM((rows, width), BF16),
            pltpu.VMEM((rows, width), BF16),
            pltpu.VMEM((rows, width), BF16),
            pltpu.VMEM((2, SLAB, width), F32),
            pltpu.SemaphoreType.DMA((n_sems,)),
            pltpu.SemaphoreType.DMA((n_sems,)),
            pltpu.SemaphoreType.DMA((5 + n + len(out_types),)),
        ]
        + (swap_scratch(1, kinds) if n_swap else []),
        compiler_params=pltpu.CompilerParams(
            collective_id=name, has_side_effects=True, vmem_limit_bytes=50 * 2**20
        ),
        cost_estimate=pl.CostEstimate(flops=0, bytes_accessed=(200 if spread else 110) * 2**20, transcendentals=0),
    )(left.reshape(4, 2 * rows, depth), right, gains, *aux, *extras)


def turn_kernel(
    zs, piece, x_ref, in_ref, out_ref, gains_ref, first_ref, grad_ref,
    all_ref, kept_ref, right_ref, result_out, d_pre_out, sums_ref, dw_out, result_ref, d_pre_ref, dw_ref,
    first, grad, w_in, kept, left, right, part, got, near_x, near_y, from_x, from_y, whole, dw, acc,
    fold_send, fold_recv, all_send, all_recv, line_send, line_recv, local, x_local
):
    rows = first.shape[0]
    tile = left.shape[2]
    wide = right.shape[2]
    y, x, c = here()
    z = lax.axis_index("z")
    to_x, to_y, to_c = {"gx": 1 - x}, {"gy": 1 - y}, {"core": 1 - c}
    chips = [(1 - y) * 2 + 1 - x, y * 2 + 1 - x, (1 - y) * 2 + x, y * 2 + x]
    me, by_x, by_y, far = place(y, x, c), place(y, 1 - x, c), place(1 - y, x, c), place(1 - y, 1 - x, c)
    other, other_x, other_y, other_far = (
        place(y, x, 1 - c),
        place(y, 1 - x, 1 - c),
        place(1 - y, x, 1 - c),
        place(1 - y, 1 - x, 1 - c),
    )
    half = rows // 2
    most = -(-half // (2 * SLAB)) * SLAB
    lows = [(0, most), (half, half - most)]
    highs = [(most, half - most), (2 * half - most, most)]
    top, bottom = pl.ds(0, half), pl.ds(half, half)
    sent = []

    def remote(sems, k, src, dst, to):
        return pltpu.make_async_remote_copy(
            src_ref=src,
            dst_ref=dst,
            send_sem=sems[0].at[k],
            recv_sem=sems[1].at[k],
            device_id=to,
            device_id_type=MESH,
        )

    def push(sems, k, src, dst, to):
        copy = remote(sems, k, src, dst, to)
        copy.start()
        sent.append(copy)

    def landed(sems, k, dst):
        remote(sems, k, dst, dst, to_c).wait_recv()

    folds, alls, lines = (fold_send, fold_recv), (all_send, all_recv), (line_send, line_recv)

    load_out = pltpu.make_async_copy(out_ref, right.at[z], local.at[0])
    load_in = pltpu.make_async_copy(in_ref, w_in, local.at[1])
    load_first = pltpu.make_async_copy(first_ref, first, local.at[2])
    load_grad = pltpu.make_async_copy(grad_ref, grad, local.at[3])

    def load_x(g):
        return pltpu.make_async_copy(x_ref.at[g], whole.at[g], x_local.at[g])


    barrier = pltpu.get_barrier_semaphore()
    for to in (to_x, to_y, to_c):
        pl.semaphore_signal(barrier, inc=1, device_id=to, device_id_type=MESH)

    @pl.when(z > 0)
    def _():
        pl.semaphore_signal(barrier, inc=1, device_id={"z": z - 1}, device_id_type=MESH)

    @pl.when(z < zs - 1)
    def _():
        pl.semaphore_signal(barrier, inc=1, device_id={"z": z + 1}, device_id_type=MESH)

    inside = (z > 0) & (z < zs - 1)

    @pl.when(inside)
    def _():
        pl.semaphore_wait(barrier, 5)

    @pl.when(jnp.logical_not(inside))
    def _():
        pl.semaphore_wait(barrier, 4)

    def shard_of(step, up):
        return z - step if up else z + step

    def hop(step, up):
        ref = right.at[shard_of(step, up)]
        src = ref if step else out_ref
        return remote(lines, 2 * step + (0 if up else 1), src, ref, {"z": z + 1 if up else z - 1})

    def sends(step, up):
        return (z >= step) & (z < zs - 1) if up else (z <= zs - 1 - step) & (z > 0)

    def gets(step, up):
        return z >= step + 1 if up else z <= zs - 2 - step

    def line_serve(step):
        for up in (True, False):

            @pl.when(gets(step - 1, up) & sends(step, up))
            def _(up=up):
                landed(lines, 2 * (step - 1) + (0 if up else 1), right.at[shard_of(step, up)])
                hop(step, up).start()

    def line_take(step):
        for up in (True, False):

            @pl.when(gets(step - 1, up) & jnp.logical_not(sends(step, up)))
            def _(up=up):
                landed(lines, 2 * (step - 1) + (0 if up else 1), right.at[shard_of(step, up)])

    for up in (True, False):

        @pl.when(sends(0, up))
        def _(up=up):
            hop(0, up).start()

    load_in.start()
    load_out.start()
    for g in range(8):
        load_x(g).start()


    load_in.wait()
    load_out.wait()

    @pl.loop(0, 8)
    def _(g):
        @pl.when(g == 6)
        def _():
            line_serve(1)

        load_x(g).wait()
        projected = dot(whole[g], w_in[...])
        gate, up = projected[:, :tile], projected[:, tile:]
        act, slope = gate_parts(gate)
        left[g] = (act * up).astype(BF16)
        kept[g] = jnp.concatenate([up * slope, act], axis=1).astype(BF16)

    load_first.start()
    load_grad.start()
    keep = pltpu.make_async_copy(kept, kept_ref, local.at[4])
    keep.start()

    def add(k, extra, start, offset, at):
        @pl.loop(0, half // SLAB)
        def _(step):
            row = pl.ds(pl.multiple_of(start + step * SLAB, SLAB), SLAB)
            of = pl.ds(pl.multiple_of(start - offset + step * SLAB, SLAB), SLAB)
            part[k, c, row, at] = (part[k, c, row, at].astype(F32) + extra[of, at].astype(F32)).astype(BF16)

    def chip_sum(k, at):
        add(k, got.at[k], 0, 0, at)
        add(k, got.at[k], half, 0, at)

    def product(k, block, at):
        found = dot(left[pl.ds(2 * chips[k], 2)].reshape(2 * rows, tile), right[block])
        part[k, 0, :, at] = found[:rows].astype(BF16)
        part[k, 1, :, at] = found[rows:].astype(BF16)

    def block_at(i):
        if i == 0:
            return z
        below = z < zs // 2
        near = jnp.where(below, z, zs - 1 - z)
        spot = jnp.where(i <= 2 * near, jnp.where(i % 2 == 1, near - (i + 1) // 2, near + i // 2), i)
        return jnp.where(below, spot, zs - 1 - spot)

    def block_cols(i):
        return pl.ds(pl.multiple_of(block_at(i) * wide, wide), wide)

    def fold_start(i):
        b, block, at = 8 * i, block_at(i), block_cols(i)
        rest = pl.ds(1, 3)
        product(0, block, at)
        push(folds, b, part.at[0, 1 - c, :, at], got.at[0, :, at], to_c)
        for k in (1, 2, 3):
            product(k, block, at)
        push(folds, b + 1, part.at[rest, 1 - c, :, at], got.at[rest, :, at], to_c)
        landed(folds, b, got.at[0, :, at])
        chip_sum(0, at)
        push(folds, b + 2, part.at[0, c, top, at], near_x.at[:, at], to_x)
        push(folds, b + 3, part.at[0, c, bottom, at], near_y.at[:, at], to_y)
        landed(folds, b + 1, got.at[rest, :, at])
        chip_sum(1, at)
        push(folds, b + 4, part.at[1, c, top, at], from_x.at[top, at], to_x)
        chip_sum(2, at)
        push(folds, b + 5, part.at[2, c, bottom, at], from_y.at[bottom, at], to_y)

    def fold_end(i):
        b, at = 8 * i, block_cols(i)
        landed(folds, b + 3, near_y.at[:, at])
        add(1, near_y, half, half, at)
        push(folds, b + 6, part.at[1, c, bottom, at], from_x.at[bottom, at], to_x)
        landed(folds, b + 2, near_x.at[:, at])
        add(2, near_x, 0, 0, at)
        push(folds, b + 7, part.at[2, c, top, at], from_y.at[top, at], to_y)

    gains = gains_ref[...]
    line_take(1)
    fold_start(0)
    fold_start(1)
    fold_end(0)
    for i in range(2, zs):
        if i < zs - 1:
            line_serve(i)
        fold_end(i - 1)
        line_take(i)
        fold_start(i)
    fold_end(zs - 1)
    carry = pltpu.make_async_copy(right, right_ref, local.at[5])
    carry.start()
    load_first.wait()
    load_grad.wait()
    acc[...] = jnp.zeros_like(acc)
    for i in range(zs):
        at = block_cols(i)
        landed(folds, 8 * i + 4, from_x.at[top, at])
        landed(folds, 8 * i + 5, from_y.at[bottom, at])
        landed(folds, 8 * i + 6, from_x.at[bottom, at])
        landed(folds, 8 * i + 7, from_y.at[top, at])

    def low(i):
        return pl.ds(*lows[i])

    def high(i):
        return pl.ds(*highs[i])

    def span(i):
        return pl.ds(i * half, half)

    def norm(i):
        @pl.loop(0, half // SLAB)
        def _(step):
            at = pl.ds(pl.multiple_of(i * half + step * SLAB, SLAB), SLAB)
            total = part[3, c, at].astype(F32) + got[3, at].astype(F32)
            total += from_x[at].astype(F32) + from_y[at].astype(F32)
            dy = grad[at].astype(F32)
            result, d_pre, terms = second_norm(total, first[at], dy, gains)
            result_ref[at] = result.astype(BF16)
            d_pre_ref[at] = d_pre
            whole[me, at] = d_pre.astype(BF16)
            acc[0] += terms
            acc[1] += dy

        b = 13 * i
        push(alls, b, whole.at[me, low(i)], whole.at[me, low(i)], to_x)
        push(alls, b + 1, whole.at[me, high(i)], whole.at[me, high(i)], to_y)
        push(alls, b + 2, whole.at[me, high(i)], whole.at[me, high(i)], to_x)
        push(alls, b + 3, whole.at[me, low(i)], whole.at[me, low(i)], to_y)
        push(alls, b + 4, whole.at[me, span(i)], whole.at[me, span(i)], to_c)

    def pass_on(i, k, slot, at, onward):
        ref = whole.at[slot, at]
        landed(alls, 13 * i + k, ref)
        for where, to in onward:
            push(alls, 13 * i + where, ref, ref, to)

    def spread_first(i):
        pass_on(i, 0, by_x, low(i), [(5, to_y), (7, to_c)])
        pass_on(i, 1, by_y, high(i), [(6, to_x), (8, to_c)])

    def spread_rest(i):
        pass_on(i, 2, by_x, high(i), [(9, to_c)])
        pass_on(i, 3, by_y, low(i), [(10, to_c)])

    def spread_far(i):
        pass_on(i, 5, far, low(i), [(11, to_c)])
        pass_on(i, 6, far, high(i), [(12, to_c)])

    outward = []

    def gradient(k, some=None, last=False, first_one=False):
        pair = pl.ds(2 * chips[k], 2)
        some = pl.ds(0, rows) if some is None else some
        if last or some.size == rows:
            outward.append(pltpu.make_async_copy(whole.at[pair], all_ref.at[pair], local.at[6 + k]))
            outward[-1].start()

        @pl.loop(0, zs)
        def _(block):
            at = pl.ds(pl.multiple_of(block * wide, wide), wide)
            tokens = 2 * some.size
            found = dot_rows(left[pair, some].reshape(tokens, tile), whole[pair, some, at].reshape(tokens, wide))
            if first_one:
                dw[block] = found
            elif last:
                dw_ref[block] = (dw[block] + found).astype(BF16)
                pltpu.make_async_copy(dw_ref.at[block], dw_out.at[block], x_local.at[block]).start()
            else:
                dw[block] += found

    norm(0)
    norm(1)
    stores = [
        pltpu.make_async_copy(result_ref, result_out, local.at[10]),
        pltpu.make_async_copy(d_pre_ref, d_pre_out, local.at[11]),
    ]
    for store in stores:
        store.start()
    spread_first(0)
    for i in (0, 1):
        landed(alls, 13 * i + 4, whole.at[other, span(i)])
    gradient(3, first_one=True)
    spread_rest(0)
    spread_first(1)
    spread_rest(1)
    for i in (0, 1):
        landed(alls, 13 * i + 7, whole.at[other_x, low(i)])
        landed(alls, 13 * i + 9, whole.at[other_x, high(i)])
    gradient(1)
    spread_far(0)
    for i in (0, 1):
        landed(alls, 13 * i + 8, whole.at[other_y, high(i)])
        landed(alls, 13 * i + 10, whole.at[other_y, low(i)])
    gradient(2)
    sums_ref[0:1] = jnp.sum(acc[0], axis=0, keepdims=True)
    sums_ref[1:2] = jnp.sum(acc[1], axis=0, keepdims=True)
    landed(alls, 11, whole.at[other_far, low(0)])
    landed(alls, 12, whole.at[other_far, high(0)])
    gradient(0, some=span(0))
    spread_far(1)
    landed(alls, 13 + 11, whole.at[other_far, low(1)])
    landed(alls, 13 + 12, whole.at[other_far, high(1)])
    gradient(0, some=span(1), last=True)
    for block in range(zs):
        pltpu.make_async_copy(dw_ref.at[block], dw_out.at[block], x_local.at[block]).wait()
    for copy in outward + [keep, carry] + stores:
        copy.wait()
    for copy in sent:
        copy.wait_send()
    for step in range(zs - 1):
        for up in (True, False):

            @pl.when(sends(step, up))
            def _(step=step, up=up):
                hop(step, up).wait_send()


def turn(zs, x, w_in, w_out, gains, first, grad):
    rows = x.shape[0] // 8
    units, wide = w_out.shape
    width = gains.shape[1]
    half = rows // 2
    by_z = (zs, units, wide)
    return pl.pallas_call(
        functools.partial(turn_kernel, zs, width // (8 * zs)),
        out_shape=[
            jax.ShapeDtypeStruct((8, rows, width), BF16),
            jax.ShapeDtypeStruct((8, rows, 2 * units), BF16),
            jax.ShapeDtypeStruct(by_z, BF16),
            jax.ShapeDtypeStruct((rows, width), BF16),
            jax.ShapeDtypeStruct((rows, width), F32),
            jax.ShapeDtypeStruct((8, width), F32),
            jax.ShapeDtypeStruct(by_z, BF16),
        ],
        in_specs=[ANY, ANY, ANY, ROWS, ANY, ANY],
        out_specs=[ANY] * 5 + [ROWS, ANY],
        scratch_shapes=[
            pltpu.VMEM((rows, width), BF16),
            pltpu.VMEM((rows, width), F32),
            pltpu.VMEM(by_z, BF16),
            pltpu.VMEM((rows, width), F32),
            pltpu.VMEM((rows, width), BF16),
            pltpu.VMEM(w_in.shape, BF16),
            pltpu.VMEM((8, rows, 2 * units), BF16),
            pltpu.VMEM((8, rows, units), BF16),
            pltpu.VMEM(by_z, BF16),
            pltpu.VMEM((4, 2, rows, width), BF16),
            pltpu.VMEM((4, rows, width), BF16),
            pltpu.VMEM((half, width), BF16),
            pltpu.VMEM((half, width), BF16),
            pltpu.VMEM((rows, width), BF16),
            pltpu.VMEM((rows, width), BF16),
            pltpu.VMEM((8, rows, width), BF16),
            pltpu.VMEM(by_z, F32),
            pltpu.VMEM((2, SLAB, width), F32),
            pltpu.SemaphoreType.DMA((8 * zs,)),
            pltpu.SemaphoreType.DMA((8 * zs,)),
            pltpu.SemaphoreType.DMA((26,)),
            pltpu.SemaphoreType.DMA((26,)),
            pltpu.SemaphoreType.DMA((2 * (zs - 1),)),
            pltpu.SemaphoreType.DMA((2 * (zs - 1),)),
            pltpu.SemaphoreType.DMA((12,)),
            pltpu.SemaphoreType.DMA((8,)),
        ],
        compiler_params=pltpu.CompilerParams(collective_id=1, has_side_effects=True, vmem_limit_bytes=60 * 2**20),
        cost_estimate=pl.CostEstimate(flops=0, bytes_accessed=380 * 2**20, transcendentals=0),
    )(x.reshape(8, rows, width), w_in, w_out, gains, first, grad)


def swap_kernel(zs, kinds, *refs):
    n = len(kinds)
    greet([name for _, name in swap_peers(zs, kinds)])
    swap_begin(zs, kinds, refs[:n], refs[n : 2 * n], *refs[2 * n :])()


def group_swap(name, zs, arrays, kinds):
    n = len(arrays)
    return pl.pallas_call(
        functools.partial(swap_kernel, zs, kinds),
        out_shape=swap_shapes(zs, arrays, kinds),
        in_specs=[ANY] * n,
        out_specs=[ANY] * n,
        scratch_shapes=swap_scratch(zs, kinds),
        compiler_params=pltpu.CompilerParams(collective_id=name, has_side_effects=True),
        cost_estimate=pl.CostEstimate(flops=0, bytes_accessed=50 * 2**20, transcendentals=0),
    )(*arrays)


def enter_kernel(zs, kinds, x_ref, grad_ref, *refs):
    n = len(kinds)
    blocks, x_all, grad_out, outs, refs = refs[:n], refs[n], refs[n + 1], refs[n + 2 : 2 * n + 2], refs[2 * n + 2 :]
    x_rows, sems = refs[0], refs[1:]
    rows, width = x_ref.shape
    greet([name for _, name in swap_peers(zs, kinds)])
    finish = swap_begin(zs, kinds, blocks, outs, *sems[:3])
    for ref, out in ((x_ref, x_rows), (grad_ref, grad_out)):

        @pl.loop(0, rows // SLAB)
        def _(step, ref=ref, out=out):
            at = pl.ds(pl.multiple_of(step * SLAB, SLAB), SLAB)
            out[at] = by_rows(ref[at].astype(F32), zs, width // (8 * zs)).astype(BF16)

    spread_block(rows // 2, 0, x_rows, x_all, *sems[3:])
    finish()


def enter(zs, x, grad, arrays, kinds):
    n = len(arrays)
    return pl.pallas_call(
        functools.partial(enter_kernel, zs, kinds),
        out_shape=[jax.ShapeDtypeStruct((8,) + x.shape, x.dtype), jax.ShapeDtypeStruct(grad.shape, grad.dtype)]
        + swap_shapes(zs, arrays, kinds),
        in_specs=[ROWS] * 2 + [ANY] * n,
        out_specs=[ANY, ROWS] + [ANY] * n,
        scratch_shapes=[pltpu.VMEM(x.shape, x.dtype)]
        + swap_scratch(zs, kinds)
        + [pltpu.SemaphoreType.DMA((13,)), pltpu.SemaphoreType.DMA((13,)), pltpu.SemaphoreType.DMA],
        compiler_params=pltpu.CompilerParams(collective_id=3, has_side_effects=True, vmem_limit_bytes=56 * 2**20),
        cost_estimate=pl.CostEstimate(flops=0, bytes_accessed=150 * 2**20, transcendentals=0),
    )(x, grad, *arrays)


def ff_kernel(x_ref, w_ref, hidden_ref, kept_ref):
    tile = hidden_ref.shape[1]
    projected = dot(x_ref[...], w_ref[...])
    gate, up = projected[:, :tile], projected[:, tile:]
    act, slope = gate_parts(gate)
    hidden_ref[...] = (act * up).astype(BF16)
    kept_ref[...] = jnp.concatenate([up * slope, act], axis=1).astype(BF16)


def ff_back_kernel(grad_ref, w_ref, kept_ref, out_ref):
    zs, _, wide = w_ref.shape
    d_hidden = dot_cols(grad_ref[:, :wide], w_ref[0])
    for z in range(1, zs):
        d_hidden += dot_cols(grad_ref[:, z * wide : (z + 1) * wide], w_ref[z])
    out_ref[...] = (jnp.concatenate([d_hidden, d_hidden], axis=1) * kept_ref[...].astype(F32)).astype(BF16)


FF_ROWS = 256


def ff_rows(width):
    return pl.BlockSpec((FF_ROWS, width), lambda i: (i, 0))


def ff_forward(x, w):
    rows, depth = x.shape
    wide = w.shape[1]
    return pl.pallas_call(
        ff_kernel,
        grid=(rows // FF_ROWS,),
        in_specs=[ff_rows(depth), pl.BlockSpec((depth, wide), lambda i: (0, 0))],
        out_specs=[ff_rows(wide // 2), ff_rows(wide)],
        out_shape=[jax.ShapeDtypeStruct((rows, wide // 2), BF16), jax.ShapeDtypeStruct((rows, wide), BF16)],
        compiler_params=PARAMS,
        cost_estimate=pl.CostEstimate(flops=2 * rows * depth * wide, bytes_accessed=20 * 2**20, transcendentals=0),
    )(x, w)


def ff_backward(grad, w, kept):
    rows, depth = grad.shape
    wide = kept.shape[1]
    return pl.pallas_call(
        ff_back_kernel,
        grid=(rows // FF_ROWS,),
        in_specs=[ff_rows(depth), pl.BlockSpec(w.shape, lambda i: (0, 0, 0)), ff_rows(wide)],
        out_specs=ff_rows(wide),
        out_shape=jax.ShapeDtypeStruct((rows, wide), BF16),
        compiler_params=PARAMS,
        cost_estimate=pl.CostEstimate(flops=rows * depth * wide, bytes_accessed=20 * 2**20, transcendentals=0),
    )(grad, w, kept)


def cut_kernel(in_ref, out_ref, in_blocks, out_blocks, wide):
    group, _, double = in_blocks.shape
    tile, ff = double // 2, out_ref.shape[1]
    span = group * tile
    odd = ff % 128
    live = lax.broadcasted_iota(jnp.int32, (in_ref.shape[0], span), 1) < ff
    wide[...] = jnp.zeros_like(wide)
    wide[:, : 2 * ff] = in_ref[...].astype(F32)
    gate = jnp.where(live, wide[:, :span], 0.0)
    up = pltpu.roll(wide[:, ff - odd : ff - odd + span], span - odd, 1)
    up = jnp.where(live, up, 0.0)
    wide[:, :span] = jnp.zeros_like(live, F32)
    wide[:, :ff] = out_ref[...].astype(F32)
    down = wide[:, :span]
    for g in range(group):
        at = slice(g * tile, (g + 1) * tile)
        in_blocks[g] = jnp.concatenate([gate[:, at], up[:, at]], axis=1).astype(BF16)
        out_blocks[g] = down[:, at].astype(BF16)


def cut_ff(w_in, w_out, group, tile):
    rows, ff = w_out.shape
    return pl.pallas_call(
        cut_kernel,
        grid=(rows // 16,),
        in_specs=[pl.BlockSpec((16, 2 * ff), lambda i: (i, 0)), pl.BlockSpec((16, ff), lambda i: (i, 0))],
        out_specs=[
            pl.BlockSpec((group, 16, 2 * tile), lambda i: (0, i, 0)),
            pl.BlockSpec((group, 16, tile), lambda i: (0, i, 0)),
        ],
        out_shape=[
            jax.ShapeDtypeStruct((group, rows, 2 * tile), BF16),
            jax.ShapeDtypeStruct((group, rows, tile), BF16),
        ],
        scratch_shapes=[pltpu.VMEM((16, -(-(ff + group * tile) // 128) * 128), F32)],
        compiler_params=SMALL,
    )(w_in, w_out)


def join_kernel(in_blocks, out_blocks, in_ref, out_ref):
    group, _, double = in_blocks.shape
    tile, ff = double // 2, out_ref.shape[1]
    odd = ff % 128
    blocks = [in_blocks[g].astype(F32) for g in range(group)]
    gate = jnp.concatenate([block[:, :tile] for block in blocks], axis=1)
    up = jnp.concatenate([block[:, tile:] for block in blocks], axis=1)
    up = pltpu.roll(up, odd, 1)
    lane = lax.broadcasted_iota(jnp.int32, (up.shape[0], 128), 1)
    in_ref[:, : ff - odd] = gate[:, : ff - odd]
    in_ref[:, ff - odd : ff - odd + 128] = jnp.where(lane < odd, gate[:, ff - odd : ff - odd + 128], up[:, :128])
    in_ref[:, ff - odd + 128 :] = up[:, 128 : ff + odd]
    down = jnp.concatenate([out_blocks[g].astype(F32) for g in range(group)], axis=1)
    out_ref[...] = down[:, :ff]


def join_ff(in_blocks, out_blocks, ff):
    group, rows, tile = out_blocks.shape
    return pl.pallas_call(
        join_kernel,
        grid=(rows // 16,),
        in_specs=[
            pl.BlockSpec((group, 16, 2 * tile), lambda i: (0, i, 0)),
            pl.BlockSpec((group, 16, tile), lambda i: (0, i, 0)),
        ],
        out_specs=[pl.BlockSpec((16, 2 * ff), lambda i: (i, 0)), pl.BlockSpec((16, ff), lambda i: (i, 0))],
        out_shape=[jax.ShapeDtypeStruct((rows, 2 * ff), F32), jax.ShapeDtypeStruct((rows, ff), F32)],
        compiler_params=SMALL,
    )(in_blocks, out_blocks)


def closing_kernel(zs, sum_ref, rows_ref, qkv_ref, total_ref, got, lines, *refs):
    send, recv, local, line_send, line_recv = refs
    y, x, c = here()
    z = lax.axis_index("z")
    me = place(y, x, c)
    wide = got.shape[2]
    width = wide // 3
    piece = got.shape[1]
    found = swap_peers(zs, ("line",))
    greet([name for _, name in found])
    copies, comes = [], []
    for k, (peer, name) in enumerate(found[:7]):
        sems = dict(send_sem=send.at[k], recv_sem=recv.at[k], device_id=name, device_id_type=MESH)
        copies.append(pltpu.make_async_remote_copy(src_ref=rows_ref.at[peer], dst_ref=got.at[me], **sems))
        comes.append(pltpu.make_async_remote_copy(src_ref=got.at[peer], dst_ref=got.at[peer], **sems))
    for k, (peer, name) in enumerate(found[7:]):
        sems = dict(send_sem=line_send.at[k], recv_sem=line_recv.at[k], device_id=name, device_id_type=MESH)
        copies.append(pltpu.make_async_remote_copy(src_ref=sum_ref, dst_ref=lines.at[z], **sems))
        comes.append(pltpu.make_async_remote_copy(src_ref=lines.at[peer], dst_ref=lines.at[peer], **sems))
    for copy in copies:
        copy.start()
    keeps = [
        pltpu.make_async_copy(rows_ref.at[me], got.at[me], local.at[0]),
        pltpu.make_async_copy(sum_ref, lines.at[z], local.at[1]),
    ]
    for keep in keeps:
        keep.start()
    for come in comes:
        come.wait_recv()
    for keep in keeps:
        keep.wait()
    for g in range(8):
        for j in range(3):
            at = pl.ds(j * D + g * width, width)
            qkv_ref[:, at] = got[g, :, j * width : (j + 1) * width].astype(F32)
    total = lines[0]
    for k in range(1, zs):
        total += lines[k]
    part = total[:, :piece]
    for k in range(1, zs):
        part = jnp.where(z == k, total[:, k * piece : (k + 1) * piece], part)
    total_ref[...] = part
    for copy in copies:
        copy.wait_send()


def closing(zs, sums, rows):
    _, piece, columns = rows.shape
    width = columns // 3
    return pl.pallas_call(
        functools.partial(closing_kernel, zs),
        out_shape=[
            jax.ShapeDtypeStruct((piece, 3 * D), F32),
            jax.ShapeDtypeStruct((8, piece), F32),
        ],
        in_specs=[ROWS, ANY],
        out_specs=[ROWS] * 2,
        scratch_shapes=[
            pltpu.VMEM((8, piece, 3 * width), BF16),
            pltpu.VMEM((zs, 8, width), F32),
            pltpu.SemaphoreType.DMA((7,)),
            pltpu.SemaphoreType.DMA((7,)),
            pltpu.SemaphoreType.DMA((2,)),
            pltpu.SemaphoreType.DMA((zs - 1,)),
            pltpu.SemaphoreType.DMA((zs - 1,)),
        ],
        compiler_params=pltpu.CompilerParams(collective_id=5, has_side_effects=True, vmem_limit_bytes=24 * 2**20),
        cost_estimate=pl.CostEstimate(flops=0, bytes_accessed=50 * 2**20, transcendentals=0),
    )(sums, rows)


def on_device(sizes, x_in, d_out, w_qkv, w_dense, w_in, w_out, gone, bone, gtwo, btwo, flags, span_start, span_len):
    gy, gx, cores, zs = sizes
    piece = w_qkv.shape[0]
    ff = w_out.shape[1]
    group = gy * gx * cores
    width = D // group
    tile = -(-ff // (group * 64)) * 64
    own = gy == 2

    def permute(array):
        lead = array.shape[:-1]
        return jnp.swapaxes(array.reshape(lead + (group, zs, piece)), -3, -2).reshape(lead + (D,))

    def restore(array):
        lead = array.shape[:-1]
        return jnp.swapaxes(array.reshape(lead + (zs, group, piece)), -3, -2).reshape(lead + (D,))

    def swap(name, arrays, kinds):
        if own:
            return group_swap(name, zs, arrays, kinds)
        ways = {
            "swap": lambda a: lax.all_to_all(a, GROUP, 0, 0, tiled=True),
            "group": lambda a: lax.all_gather(a, GROUP, axis=0),
            "line": lambda a: lax.all_gather(a, "z", axis=0),
        }
        return [ways[k](a) for a, k in zip(arrays, kinds)]

    def spread_rows(block):
        return lax.all_gather(block, GROUP, axis=0, tiled=True)

    rows_f32 = jax.ShapeDtypeStruct((SEQ_LEN, D), F32)
    rows_low = jax.ShapeDtypeStruct((SEQ_LEN, D), BF16)
    sums_type = jax.ShapeDtypeStruct((8, D), F32)

    def fold(partial):
        return lax.psum_scatter(partial.astype(BF16), GROUP, scatter_dimension=0, tiled=True).astype(F32)

    def stack_sums(*arrays):
        return jnp.pad(jnp.stack([jnp.sum(a, axis=0) for a in arrays]), ((0, 6), (0, 0)))

    def fold_one(left, right, x, gains):
        if own:
            kinds = [rows_f32, rows_f32, jax.ShapeDtypeStruct((SEQ_LEN, 128), F32)]
            whole, first, normal, inverse = group_fold(0, zs, "one", left, right, gains, [x], kinds)
            return whole.reshape(left.shape[0], D), first, normal, inverse
        first, normal, inverse = first_norm(permute(deep_alpha * x.astype(F32) + fold(dot(left, right))), gains)
        return spread_rows(first.astype(BF16)), first, normal, inverse

    def ff_turn(x, w_in, w_out, first, grad, gains):
        if own:
            whole, kept, w_out, result, d_pre, sums, d_out = turn(zs, x, w_in, w_out, gains, first, grad)
            rows = x.shape[0]
            return whole.reshape(rows, D), kept.reshape(rows, -1), w_out, result, d_pre, sums, d_out
        w_out = lax.all_gather(w_out, "z", axis=0)
        hidden, kept = ff_forward(x, w_in)
        grad = grad.astype(F32)
        right = jnp.swapaxes(w_out, 0, 1).reshape(-1, D)
        result, d_pre, terms = second_norm(fold(dot(hidden, right)), first, grad, gains)
        whole = spread_rows(d_pre.astype(BF16))
        d_out = jnp.swapaxes(dot_rows(hidden, whole).reshape(-1, zs, D // zs), 0, 1).astype(BF16)
        return whole, kept, w_out, result.astype(BF16), d_pre, stack_sums(terms, grad), d_out

    def fold_back(left, right, d_pre_two, normal, inverse, gains):
        if own:
            kinds = [rows_f32, sums_type]
            whole, d_pre, sums = group_fold(7, zs, "back", left, right, gains, [d_pre_two, normal, inverse], kinds)
            return whole.reshape(left.shape[0], D), d_pre, sums
        d_pre, terms, d_first = first_back(fold(dot_cols(left, right)), d_pre_two, normal, inverse, gains)
        return spread_rows(restore(d_pre).astype(BF16)), d_pre, stack_sums(terms, d_first)

    def fold_last(left, right, d_pre, gains, extras, kinds):
        if own:
            return group_fold(8, zs, "last", left, right, gains, [d_pre], [rows_low], extras, kinds)
        out = restore((deep_alpha * d_pre + fold(dot_cols(left, right))).astype(BF16))
        return [out] + swap(8, extras, kinds)

    def gather(block):
        return lax.all_gather(block, "z", axis=0, tiled=True)

    def scatter(partial):
        return lax.psum_scatter(partial.astype(BF16), "z", scatter_dimension=0, tiled=True)

    masked = jnp.max(flags) > 0
    prefix = jnp.where(masked, SEQ_LEN, SEQ_LEN - span_len[0])
    info = jnp.concatenate([gone, bone, gtwo, btwo, jnp.stack([prefix, span_start[0]]).astype(BF16)])
    info = jnp.pad(info[None, :], ((0, 15), (0, -info.shape[0] % 128)))

    qkv_blocks = jnp.moveaxis(w_qkv.reshape(piece, 3, group, width), 2, 0).reshape(group, piece, 3 * width)
    w_dense_part = gather(w_dense)
    qkv_blocks, info = swap(2, [qkv_blocks, info], ("swap", "group"))
    w_qkv_part = gather(qkv_blocks.reshape(group * piece, 3 * width))
    info = info[:, 0]
    place_info = info[:, 4 * piece : 4 * piece + 2].astype(jnp.int32)
    prefix, start = place_info[:, 0], place_info[:, 1]
    cosine, sine = tables(prefix, start)
    in_blocks, out_blocks = cut_ff(w_in, w_out, group, tile)
    info = jnp.pad(info, ((0, -group % 16), (0, 0)))
    in_blocks, out_blocks, qkv_blocks, w_dense_part, cosine, sine = lax.optimization_barrier(
        (in_blocks, out_blocks, qkv_blocks, w_dense_part, cosine, sine)
    )
    swapped, kinds = [in_blocks, out_blocks, info], ("swap", "swap", "line")
    if own:
        x_all, grad_two, in_blocks, out_blocks, info = enter(zs, x_in, d_out, swapped, kinds)
        x_all = x_all.reshape(group * SEQ_LEN, D)
    else:
        x_all, grad_two = spread_rows(permute(x_in)), permute(d_out)
        in_blocks, out_blocks, info = swap(3, swapped, kinds)
    w_in_part = gather(in_blocks.reshape(group * piece, 2 * tile))
    out_rows = out_blocks.reshape(group * piece, tile).T
    gains = info[:, :group, : 4 * piece].astype(F32).reshape(zs, group, 4, piece)
    gains = jnp.pad(jnp.transpose(gains, (2, 0, 1, 3)).reshape(4, D), ((0, 4), (0, 0)))
    w_qkv_part, x_all, gains, out_rows = lax.optimization_barrier((w_qkv_part, x_all, gains, out_rows))
    packed = dot(x_all, w_qkv_part)
    qkv, context = attend(prefix, packed, cosine, sine)
    first_all, first, normal_one, inverse_one = fold_one(context, w_dense_part, x_in, gains)
    d_branch, kept, w_out_part, layer_out, d_pre_two, sums_two, d_w_out = ff_turn(
        first_all, w_in_part, out_rows, first, grad_two, gains
    )
    layer_out = restore(layer_out)
    d_w_out = lax.psum_scatter(d_w_out, "z", scatter_dimension=0)
    d_projected = ff_backward(d_branch, w_out_part, kept)
    d_w_in = dot_rows(first_all, d_projected).astype(BF16)
    d_w_in, d_projected = lax.optimization_barrier((d_w_in, d_projected))
    d_w_in = scatter(d_w_in)
    d_attn, d_pre_one, sums_one = fold_back(d_projected, w_in_part, d_pre_two, normal_one, inverse_one, gains)
    d_attn, d_w_out = lax.optimization_barrier((d_attn, d_w_out))
    d_context = dot_cols(d_attn, w_dense_part).astype(BF16)
    d_packed = attend_back(prefix, qkv, d_context, cosine, sine)
    d_w_qkv = dot_rows(x_all, d_packed).astype(BF16)
    sums = jnp.concatenate([sums_one[:2], sums_two[:2], jnp.zeros((4, D), F32)])
    d_w_qkv = with_layout_constraint(d_w_qkv, Layout((0, 1)))
    d_dense = dot_rows(context, d_attn).astype(BF16)
    d_packed, d_w_qkv, d_w_in, sums, d_dense = lax.optimization_barrier((d_packed, d_w_qkv, d_w_in, sums, d_dense))
    d_w_qkv = scatter(d_w_qkv)
    d_dense = scatter(d_dense)
    d_w_in, d_w_out = d_w_in.reshape(group, piece, 2 * tile), d_w_out.T.reshape(group, piece, tile)
    d_input, d_w_in, d_w_out, sums = fold_last(
        d_packed, w_qkv_part, d_pre_one, gains, [d_w_in, d_w_out, sums], ("swap", "swap", "group")
    )
    sums = jnp.sum(sums, axis=0).reshape(8, zs, group, piece)
    sums = lax.dynamic_index_in_dim(sums, lax.axis_index(GROUP), 2, keepdims=False).reshape(8, width)
    out_in, out_out = join_ff(d_w_in, d_w_out, ff)
    out_in, out_out, d_input, d_w_qkv, sums = lax.optimization_barrier((out_in, out_out, d_input, d_w_qkv, sums))
    if own:
        out_qkv, sums = closing(zs, sums, d_w_qkv.reshape(group, piece, 3 * width))
    else:
        d_w_qkv, sums = swap(5, [d_w_qkv.reshape(group, piece, 3 * width), sums], ("swap", "line"))
        out_qkv = jnp.transpose(d_w_qkv.astype(F32).reshape(group, piece, 3, width), (1, 2, 0, 3))
        out_qkv = out_qkv.reshape(piece, 3 * D)
        sums = jnp.sum(sums, axis=0).reshape(8, zs, piece)
        sums = lax.dynamic_index_in_dim(sums, lax.axis_index("z"), 1, keepdims=False)
    out_dense = d_dense.astype(F32)
    return layer_out, d_input, out_qkv, out_dense, out_in, out_out, sums[0], sums[1], sums[2], sums[3]


def solution(mesh):
    grp, shard = mesh.shape["grp"], mesh.shape["shard"]
    sizes = (grp // 4, 2, 2, shard)
    inner = Mesh(mesh.devices.reshape(sizes), ALL)
    rows, flat = P(ALL, None), P(ALL)
    return jax.shard_map(
        functools.partial(on_device, sizes),
        mesh=inner,
        in_specs=(rows,) * 6 + (flat,) * 7,
        out_specs=(rows,) * 6 + (flat,) * 4,
        check_vma=False,
    )
```

```python
import functools

import jax
import jax.numpy as jnp
from jax import lax
from jax.experimental import pallas as pl
from jax.experimental.pallas import tpu as pltpu
from jax.experimental.layout import Layout, with_layout_constraint
from jax.sharding import Mesh
from jax.sharding import PartitionSpec as P

HEADS = 16
HEAD = 128
SEQ_LEN = 224
D = HEADS * HEAD
deep_alpha = 6.928203230275509
norm_eps = 1e-05
far_below = -1e30
scale = HEAD ** (-0.5)

ALL = ("gy", "gx", "core", "z")
GROUP = ("gy", "gx", "core")
MESH = pl.DeviceIdType.MESH
F32 = jnp.float32
BF16 = jnp.bfloat16


def dot(left, right):
    return jnp.dot(left, right, preferred_element_type=F32)


def dot_rows(left, right):
    return lax.dot_general(left, right, (((0,), (0,)), ((), ())), preferred_element_type=F32)


def dot_cols(left, right):
    return lax.dot_general(left, right, (((1,), (1,)), ((), ())), preferred_element_type=F32)


def swap_halves(block):
    lane = lax.broadcasted_iota(jnp.int32, block.shape, 1)
    return jnp.where((lane & 32) == 0, pltpu.roll(block, 96, 1), pltpu.roll(block, 32, 1))


def seen(prefix):
    row = lax.broadcasted_iota(jnp.int32, (SEQ_LEN, SEQ_LEN), 0)
    col = lax.broadcasted_iota(jnp.int32, (SEQ_LEN, SEQ_LEN), 1)
    return (col < prefix) | (col <= row)


def softmax(queries, keys, visible):
    scores = jnp.where(visible, dot_cols(queries, keys), far_below)
    weights = jnp.exp(scores - jnp.max(scores, axis=1, keepdims=True))
    return weights / jnp.sum(weights, axis=1, keepdims=True)


def attend_kernel(prefix_ref, packed_ref, cos_ref, sin_ref, qkv_ref, context_ref):
    width = context_ref.shape[1]
    visible = seen(prefix_ref[pl.program_id(0)])
    cosine = cos_ref[0]
    sine = sin_ref[0]
    for head in range(width // HEAD):
        at = pl.ds(head * HEAD, HEAD)
        at_k = pl.ds(width + head * HEAD, HEAD)
        at_v = pl.ds(2 * width + head * HEAD, HEAD)
        raw = packed_ref[:, at]
        queries = ((raw * cosine + swap_halves(raw) * sine) * scale).astype(BF16)
        raw = packed_ref[:, at_k]
        keys = (raw * cosine + swap_halves(raw) * sine).astype(BF16)
        values = packed_ref[:, at_v].astype(BF16)
        qkv_ref[:, at] = queries
        qkv_ref[:, at_k] = keys
        qkv_ref[:, at_v] = values
        probs = softmax(queries, keys, visible).astype(BF16)
        context_ref[:, at] = dot(probs, values).astype(BF16)


def attend_back_kernel(prefix_ref, qkv_ref, d_context_ref, cos_ref, sin_ref, d_packed_ref):
    width = d_context_ref.shape[1]
    visible = seen(prefix_ref[pl.program_id(0)])
    cosine = cos_ref[0]
    sine = sin_ref[0]
    for head in range(width // HEAD):
        at = pl.ds(head * HEAD, HEAD)
        at_k = pl.ds(width + head * HEAD, HEAD)
        at_v = pl.ds(2 * width + head * HEAD, HEAD)
        queries = qkv_ref[:, at]
        keys = qkv_ref[:, at_k]
        values = qkv_ref[:, at_v]
        d_context = d_context_ref[:, at]
        probs = softmax(queries, keys, visible)
        d_packed_ref[:, at_v] = dot_rows(probs.astype(BF16), d_context).astype(BF16)
        d_probs = dot_cols(d_context, values)
        inner = jnp.sum(probs * d_probs, axis=1, keepdims=True)
        d_scores = (probs * (d_probs - inner)).astype(BF16)
        grad = dot(d_scores, keys) * scale
        d_packed_ref[:, at] = (grad * cosine - swap_halves(grad) * sine).astype(BF16)
        grad = dot_rows(d_scores, queries)
        d_packed_ref[:, at_k] = (grad * cosine - swap_halves(grad) * sine).astype(BF16)


def by_sequence(width):
    return pl.BlockSpec((SEQ_LEN, width), lambda s: (s, 0))


TABLE = pl.BlockSpec((1, SEQ_LEN, HEAD), lambda s: (s, 0, 0))
SCALARS = pl.BlockSpec(memory_space=pltpu.SMEM)
PARAMS = pltpu.CompilerParams(vmem_limit_bytes=56 * 2**20)
SMALL = pltpu.CompilerParams(vmem_limit_bytes=24 * 2**20)


def attend(prefix, packed, cosine, sine):
    rows, width = packed.shape[0], packed.shape[1] // 3
    return pl.pallas_call(
        attend_kernel,
        grid=(rows // SEQ_LEN,),
        in_specs=[SCALARS, by_sequence(3 * width), TABLE, TABLE],
        out_specs=[by_sequence(3 * width), by_sequence(width)],
        out_shape=[
            jax.ShapeDtypeStruct((rows, 3 * width), BF16),
            jax.ShapeDtypeStruct((rows, width), BF16),
        ],
        compiler_params=PARAMS,
    )(prefix, packed, cosine, sine)


def attend_back(prefix, qkv, d_context, cosine, sine):
    rows, width = d_context.shape
    return pl.pallas_call(
        attend_back_kernel,
        grid=(rows // SEQ_LEN,),
        in_specs=[SCALARS, by_sequence(3 * width), by_sequence(width), TABLE, TABLE],
        out_specs=by_sequence(3 * width),
        out_shape=jax.ShapeDtypeStruct((rows, 3 * width), BF16),
        compiler_params=PARAMS,
    )(prefix, qkv, d_context, cosine, sine)


def tables(prefix, start):
    place = jnp.arange(SEQ_LEN, dtype=jnp.int32)
    in_span = place[None, :] >= prefix[:, None]
    pos_one = jnp.where(in_span, start[:, None], place[None, :])
    pos_two = jnp.where(in_span, place[None, :] - prefix[:, None] + 1, 0)
    lane = jnp.arange(HEAD)
    freqs = 10000.0 ** (-2.0 * (lane % 32).astype(F32) / 64)
    place_of = jnp.where(lane[None, None, :] < 64, pos_one[:, :, None], pos_two[:, :, None])
    angles = place_of.astype(F32) * freqs
    sign = jnp.where(lane % 64 < 32, -1.0, 1.0)
    return jnp.cos(angles), jnp.sin(angles) * sign


def norm_parts(values):
    center = values - jnp.mean(values, axis=-1, keepdims=True)
    inverse = lax.rsqrt(jnp.mean(center * center, axis=-1, keepdims=True) + norm_eps)
    return center * inverse, inverse


def norm_back(normal, inverse, gain, grad):
    scaled = gain * grad
    return inverse * (
        scaled
        - jnp.mean(scaled, axis=-1, keepdims=True)
        - normal * jnp.mean(scaled * normal, axis=-1, keepdims=True)
    )


def gate_parts(gate):
    phi = 0.5 * (1.0 + lax.erf(gate * 0.7071067811865476))
    slope = phi + gate * jnp.exp(-0.5 * gate * gate) * 0.3989422804014327
    return gate * phi, slope


def here():
    return lax.axis_index("gy"), lax.axis_index("gx"), lax.axis_index("core")


def place(y, x, c):
    return (y * 2 + x) * 2 + c


def greet(peers):
    barrier = pltpu.get_barrier_semaphore()
    for peer in peers:
        pl.semaphore_signal(barrier, inc=1, device_id=peer, device_id_type=MESH)
    pl.semaphore_wait(barrier, len(peers))


def spread_block(cut, base, block_ref, out_ref, send, recv, local):
    rows = block_ref.shape[0]
    y, x, c = here()
    to_x, to_y, to_c = {"gx": 1 - x}, {"gy": 1 - y}, {"core": 1 - c}
    me, by_x, by_y, far = place(y, x, c), place(y, 1 - x, c), place(1 - y, x, c), place(1 - y, 1 - x, c)
    low, high = pl.ds(0, cut), pl.ds(cut, rows - cut)

    def push(k, src, dst, to):
        copy = pltpu.make_async_remote_copy(
            src_ref=src, dst_ref=dst, send_sem=send.at[base + k], recv_sem=recv.at[base + k], device_id=to, device_id_type=MESH
        )
        copy.start()
        return copy

    def landed(k, dst):
        pltpu.make_async_remote_copy(
            src_ref=dst, dst_ref=dst, send_sem=send.at[base + k], recv_sem=recv.at[base + k], device_id=to_c, device_id_type=MESH
        ).wait_recv()

    sent = [
        push(0, block_ref.at[low], out_ref.at[me, low], to_x),
        push(1, block_ref.at[high], out_ref.at[me, high], to_y),
        push(2, block_ref.at[high], out_ref.at[me, high], to_x),
        push(3, block_ref.at[low], out_ref.at[me, low], to_y),
        push(4, block_ref, out_ref.at[me], to_c),
    ]
    keep = pltpu.make_async_copy(block_ref, out_ref.at[me], local)
    keep.start()
    landed(0, out_ref.at[by_x, low])
    sent.append(push(5, out_ref.at[by_x, low], out_ref.at[by_x, low], to_y))
    sent.append(push(7, out_ref.at[by_x, low], out_ref.at[by_x, low], to_c))
    landed(1, out_ref.at[by_y, high])
    sent.append(push(6, out_ref.at[by_y, high], out_ref.at[by_y, high], to_x))
    sent.append(push(8, out_ref.at[by_y, high], out_ref.at[by_y, high], to_c))
    landed(2, out_ref.at[by_x, high])
    sent.append(push(9, out_ref.at[by_x, high], out_ref.at[by_x, high], to_c))
    landed(3, out_ref.at[by_y, low])
    sent.append(push(10, out_ref.at[by_y, low], out_ref.at[by_y, low], to_c))
    landed(5, out_ref.at[far, low])
    sent.append(push(11, out_ref.at[far, low], out_ref.at[far, low], to_c))
    landed(6, out_ref.at[far, high])
    sent.append(push(12, out_ref.at[far, high], out_ref.at[far, high], to_c))
    other, other_x, other_y, other_far = (
        place(y, x, 1 - c),
        place(y, 1 - x, 1 - c),
        place(1 - y, x, 1 - c),
        place(1 - y, 1 - x, 1 - c),
    )
    landed(4, out_ref.at[other])
    landed(7, out_ref.at[other_x, low])
    landed(8, out_ref.at[other_y, high])
    landed(9, out_ref.at[other_x, high])
    landed(10, out_ref.at[other_y, low])
    landed(11, out_ref.at[other_far, low])
    landed(12, out_ref.at[other_far, high])
    keep.wait()
    for copy in sent:
        copy.wait_send()


ANY = pl.BlockSpec(memory_space=pl.ANY)


def swap_peers(zs, kinds):
    y, x, c = here()
    z = lax.axis_index("z")
    found = []
    for k in range(1, 8):
        peer = ((y + k // 4) % 2, (x + k // 2 % 2) % 2, (c + k % 2) % 2)
        found.append((place(*peer), {"gy": peer[0], "gx": peer[1], "core": peer[2]}))
    if "line" in kinds:
        found += [((z + k) % zs, {"z": (z + k) % zs}) for k in range(1, zs)]
    return found


def swap_begin(zs, kinds, blocks, outs, send, recv, local):
    copies, comes, keeps = [], [], []
    found = swap_peers(zs, kinds)
    for i, kind in enumerate(kinds):
        me = lax.axis_index("z") if kind == "line" else place(*here())
        for k, (peer, name) in enumerate(found[7:] if kind == "line" else found[:7]):
            src = blocks[i].at[peer] if kind == "swap" else blocks[i]
            landing = outs[i].at[peer]
            sems = dict(send_sem=send.at[i, k], recv_sem=recv.at[i, k], device_id=name, device_id_type=MESH)
            copies.append(pltpu.make_async_remote_copy(src_ref=src, dst_ref=outs[i].at[me], **sems))
            comes.append(pltpu.make_async_remote_copy(src_ref=landing, dst_ref=landing, **sems))
            copies[-1].start()
        own = blocks[i].at[me] if kind == "swap" else blocks[i]
        keeps.append(pltpu.make_async_copy(own, outs[i].at[me], local.at[i]))
        keeps[-1].start()

    def finish():
        for come in comes:
            come.wait_recv()
        for copy in copies:
            copy.wait_send()
        for keep in keeps:
            keep.wait()

    return finish


SWAP_LEAD = {"swap": lambda zs: (), "group": lambda zs: (8,), "line": lambda zs: (zs,)}


def swap_shapes(zs, arrays, kinds):
    return [jax.ShapeDtypeStruct(SWAP_LEAD[k](zs) + a.shape, a.dtype) for a, k in zip(arrays, kinds)]


def swap_scratch(zs, kinds):
    n, most = len(kinds), max(7, zs - 1)
    return [
        pltpu.SemaphoreType.DMA((n, most)),
        pltpu.SemaphoreType.DMA((n, most)),
        pltpu.SemaphoreType.DMA((n,)),
    ]


SLAB = 16
ROWS = pl.BlockSpec(memory_space=pltpu.VMEM)
CHIP_COLS = 256


def by_rows(value, zs, piece):
    group = D // (zs * piece)
    order = [g * zs + z for z in range(zs) for g in range(group)]
    return jnp.concatenate([value[:, m * piece : (m + 1) * piece] for m in order], axis=1)


def in_order(value, zs, piece):
    group = D // (zs * piece)
    order = [z * group + g for g in range(group) for z in range(zs)]
    return jnp.concatenate([value[:, m * piece : (m + 1) * piece] for m in order], axis=1)


def first_norm(values, gains):
    normal, inverse = norm_parts(values)
    first = normal * gains[0:1] + gains[1:2]
    return first, normal, inverse


def second_norm(total, first, grad, gains):
    normal, inverse = norm_parts(deep_alpha * first + total)
    return normal * gains[2:3] + gains[3:4], norm_back(normal, inverse, gains[2:3], grad), grad * normal


def first_back(total, d_pre_two, normal, inverse, gains):
    d_first = deep_alpha * d_pre_two + total
    return norm_back(normal, inverse, gains[0:1], d_first), d_first * normal, d_first


def fold_kernel(mode, across, zs, piece, n_aux, n_out, kinds, *refs):
    left_ref, right_ref, gains_ref = refs[:3]
    aux_refs = refs[3 : 3 + n_aux]
    refs = refs[3 + n_aux :]
    n_swap = len(kinds)
    swap_in, refs = refs[:n_swap], refs[n_swap:]
    spread = mode != "last"
    if spread:
        all_ref, refs = refs[0], refs[1:]
    out_refs, refs = refs[:n_out], refs[n_out:]
    swap_out, refs = refs[:n_swap], refs[n_swap:]
    aux, refs = refs[:n_aux], refs[n_aux:]
    outs, refs = refs[:n_out], refs[n_out:]
    left, right, part, got, near_x, near_y, from_x, from_y, block, acc, send, recv, local = refs[:13]
    rows, width = block.shape
    cut = near_x.shape[0]
    y, x, c = here()
    to_x, to_y, to_c = {"gx": 1 - x}, {"gy": 1 - y}, {"core": 1 - c}
    chips = [(1 - y, 1 - x), (y, 1 - x), (1 - y, x), (y, x)]
    low, high = pl.ds(0, cut), pl.ds(cut, rows - cut)

    def push(k, src, dst, to):
        copy = pltpu.make_async_remote_copy(
            src_ref=src, dst_ref=dst, send_sem=send.at[k], recv_sem=recv.at[k], device_id=to, device_id_type=MESH
        )
        copy.start()
        return copy

    def add(k, extra, start, size, offset=0):
        @pl.loop(0, size // SLAB)
        def _(step):
            at = pl.ds(pl.multiple_of(start + step * SLAB, SLAB), SLAB)
            of = pl.ds(pl.multiple_of(start - offset + step * SLAB, SLAB), SLAB)
            part[k, c, at] = (part[k, c, at].astype(F32) + extra[of].astype(F32)).astype(BF16)

    loads = [pltpu.make_async_copy(left_ref.at[a * 2 + b], left.at[k], local.at[k]) for k, (a, b) in enumerate(chips)]
    load_right = pltpu.make_async_copy(right_ref, right, local.at[4])
    load_aux = [pltpu.make_async_copy(r, v, local.at[5 + k]) for k, (r, v) in enumerate(zip(aux_refs, aux))]
    loads[0].start()
    load_right.start()
    for load in loads[1:] + load_aux:
        load.start()
    if n_swap:
        greet([name for _, name in swap_peers(1, kinds)])
        swap_finish = swap_begin(1, kinds, swap_in, swap_out, *refs[13:])
    else:
        greet([to_x, to_y, to_c])

    def product(k):
        loads[k].wait()

        @pl.loop(0, width // CHIP_COLS)
        def _(step):
            at = pl.ds(pl.multiple_of(step * CHIP_COLS, CHIP_COLS), CHIP_COLS)
            here_part = dot_cols(left[k], right[at]) if across else dot(left[k], right[:, at])
            part[k, 0, :, at] = here_part[:rows].astype(BF16)
            part[k, 1, :, at] = here_part[rows:].astype(BF16)

        return push(k, part.at[k, 1 - c], got.at[k], to_c)

    load_right.wait()
    sent = [product(0), product(1)]
    sent[0].wait_recv()
    add(0, got.at[0], 0, rows)
    far_x = push(4, part.at[0, c, low], near_x, to_x)
    far_y = push(5, part.at[0, c, high], near_y, to_y)
    sent.append(product(2))
    sent[1].wait_recv()
    add(1, got.at[1], 0, rows)
    plain_x = push(6, part.at[1, c, low], from_x.at[low], to_x)
    sent[2].wait_recv()
    add(2, got.at[2], 0, rows)
    plain_y = push(7, part.at[2, c, high], from_y.at[high], to_y)
    sent.append(product(3))
    far_y.wait_recv()
    add(1, near_y, cut, rows - cut, cut)
    more_x = push(8, part.at[1, c, high], from_x.at[high], to_x)
    far_x.wait_recv()
    add(2, near_x, 0, cut)
    more_y = push(9, part.at[2, c, low], from_y.at[low], to_y)
    sent[3].wait_recv()
    for load in load_aux:
        load.wait()
    plain_x.wait_recv()
    plain_y.wait_recv()
    more_x.wait_recv()
    more_y.wait_recv()
    gains = gains_ref[...]
    acc[...] = jnp.zeros_like(acc)

    @pl.loop(0, rows // SLAB)
    def _(step):
        at = pl.ds(pl.multiple_of(step * SLAB, SLAB), SLAB)
        total = part[3, c, at].astype(F32) + got[3, at].astype(F32) + from_x[at].astype(F32) + from_y[at].astype(F32)
        held = [a[at].astype(F32) for a in aux]
        if mode == "one":
            first, normal, inverse = first_norm(by_rows(deep_alpha * held[0] + total, zs, piece), gains)
            outs[0][at] = first
            outs[1][at] = normal
            outs[2][at] = jnp.broadcast_to(inverse, (SLAB, 128))
            block[at] = first.astype(BF16)
        elif mode == "back":
            d_pre, terms, d_first = first_back(total, held[0], held[1], held[2][:, 0:1], gains)
            outs[0][at] = d_pre
            block[at] = in_order(d_pre, zs, piece).astype(BF16)
            acc[0] += terms
            acc[1] += d_first
        else:
            outs[0][at] = in_order(deep_alpha * held[0] + total, zs, piece).astype(BF16)

    if mode == "back":
        outs[-1][0:1] = jnp.sum(acc[0], axis=0, keepdims=True)
        outs[-1][1:2] = jnp.sum(acc[1], axis=0, keepdims=True)
    stores = [pltpu.make_async_copy(v, r, local.at[5 + n_aux + k]) for k, (v, r) in enumerate(zip(outs, out_refs))]
    for store in stores:
        store.start()
    for copy in sent + [far_x, far_y, plain_x, plain_y, more_x, more_y]:
        copy.wait_send()
    if n_swap:
        swap_finish()
    if spread:
        spread_block(cut, 10, block, all_ref, send, recv, local.at[4])
    for store in stores:
        store.wait()


def group_fold(name, zs, mode, left, right, gains, aux, out_types, extras=(), kinds=()):
    across = mode != "one"
    rows, depth = left.shape[0] // 8, left.shape[1]
    width = gains.shape[1]
    cut = rows // 2
    spread = mode != "last"
    out_shape = [jax.ShapeDtypeStruct((8, rows, width), BF16)] * spread + out_types
    n, n_swap = len(aux), len(extras)
    n_sems = 23 if spread else 10
    return pl.pallas_call(
        functools.partial(fold_kernel, mode, across, zs, width // (8 * zs), n, len(out_types), kinds),
        out_shape=out_shape + swap_shapes(1, extras, kinds),
        in_specs=[ANY, ANY, ROWS] + [ANY] * (n + n_swap),
        out_specs=[ANY] * (spread + len(out_types) + n_swap),
        scratch_shapes=[pltpu.VMEM(a.shape, a.dtype) for a in list(aux) + out_types]
        + [
            pltpu.VMEM((4, 2 * rows, depth), BF16),
            pltpu.VMEM(right.shape, BF16),
            pltpu.VMEM((4, 2, rows, width), BF16),
            pltpu.VMEM((4, rows, width), BF16),
            pltpu.VMEM((cut, width), BF16),
            pltpu.VMEM((rows - cut, width), BF16),
            pltpu.VMEM((rows, width), BF16),
            pltpu.VMEM((rows, width), BF16),
            pltpu.VMEM((rows, width), BF16),
            pltpu.VMEM((2, SLAB, width), F32),
            pltpu.SemaphoreType.DMA((n_sems,)),
            pltpu.SemaphoreType.DMA((n_sems,)),
            pltpu.SemaphoreType.DMA((5 + n + len(out_types),)),
        ]
        + (swap_scratch(1, kinds) if n_swap else []),
        compiler_params=pltpu.CompilerParams(
            collective_id=name, has_side_effects=True, vmem_limit_bytes=50 * 2**20
        ),
        cost_estimate=pl.CostEstimate(flops=0, bytes_accessed=(200 if spread else 110) * 2**20, transcendentals=0),
    )(left.reshape(4, 2 * rows, depth), right, gains, *aux, *extras)


def turn_kernel(
    zs, piece, x_ref, in_ref, out_ref, gains_ref, first_ref, grad_ref,
    all_ref, kept_ref, right_ref, result_out, d_pre_out, sums_ref, dw_out, result_ref, d_pre_ref, dw_ref,
    first, grad, w_in, kept, left, right, part, got, near_x, near_y, from_x, from_y, whole, dw, acc,
    fold_send, fold_recv, all_send, all_recv, line_send, line_recv, local, x_local
):
    rows = first.shape[0]
    tile = left.shape[2]
    wide = right.shape[2]
    y, x, c = here()
    z = lax.axis_index("z")
    to_x, to_y, to_c = {"gx": 1 - x}, {"gy": 1 - y}, {"core": 1 - c}
    chips = [(1 - y) * 2 + 1 - x, y * 2 + 1 - x, (1 - y) * 2 + x, y * 2 + x]
    me, by_x, by_y, far = place(y, x, c), place(y, 1 - x, c), place(1 - y, x, c), place(1 - y, 1 - x, c)
    other, other_x, other_y, other_far = (
        place(y, x, 1 - c),
        place(y, 1 - x, 1 - c),
        place(1 - y, x, 1 - c),
        place(1 - y, 1 - x, 1 - c),
    )
    half = rows // 2
    most = -(-half // (2 * SLAB)) * SLAB
    lows = [(0, most), (half, half - most)]
    highs = [(most, half - most), (2 * half - most, most)]
    top, bottom = pl.ds(0, half), pl.ds(half, half)
    sent = []

    def remote(sems, k, src, dst, to):
        return pltpu.make_async_remote_copy(
            src_ref=src,
            dst_ref=dst,
            send_sem=sems[0].at[k],
            recv_sem=sems[1].at[k],
            device_id=to,
            device_id_type=MESH,
        )

    def push(sems, k, src, dst, to):
        copy = remote(sems, k, src, dst, to)
        copy.start()
        sent.append(copy)

    def landed(sems, k, dst):
        remote(sems, k, dst, dst, to_c).wait_recv()

    folds, alls, lines = (fold_send, fold_recv), (all_send, all_recv), (line_send, line_recv)

    load_out = pltpu.make_async_copy(out_ref, right.at[z], local.at[0])
    load_in = pltpu.make_async_copy(in_ref, w_in, local.at[1])
    load_first = pltpu.make_async_copy(first_ref, first, local.at[2])
    load_grad = pltpu.make_async_copy(grad_ref, grad, local.at[3])

    def load_x(g):
        return pltpu.make_async_copy(x_ref.at[g], whole.at[g], x_local.at[g])


    barrier = pltpu.get_barrier_semaphore()
    for to in (to_x, to_y, to_c):
        pl.semaphore_signal(barrier, inc=1, device_id=to, device_id_type=MESH)

    @pl.when(z > 0)
    def _():
        pl.semaphore_signal(barrier, inc=1, device_id={"z": z - 1}, device_id_type=MESH)

    @pl.when(z < zs - 1)
    def _():
        pl.semaphore_signal(barrier, inc=1, device_id={"z": z + 1}, device_id_type=MESH)

    inside = (z > 0) & (z < zs - 1)

    @pl.when(inside)
    def _():
        pl.semaphore_wait(barrier, 5)

    @pl.when(jnp.logical_not(inside))
    def _():
        pl.semaphore_wait(barrier, 4)

    def shard_of(step, up):
        return z - step if up else z + step

    def hop(step, up):
        ref = right.at[shard_of(step, up)]
        src = ref if step else out_ref
        return remote(lines, 2 * step + (0 if up else 1), src, ref, {"z": z + 1 if up else z - 1})

    def sends(step, up):
        return (z >= step) & (z < zs - 1) if up else (z <= zs - 1 - step) & (z > 0)

    def gets(step, up):
        return z >= step + 1 if up else z <= zs - 2 - step

    def line_serve(step):
        for up in (True, False):

            @pl.when(gets(step - 1, up) & sends(step, up))
            def _(up=up):
                landed(lines, 2 * (step - 1) + (0 if up else 1), right.at[shard_of(step, up)])
                hop(step, up).start()

    def line_take(step):
        for up in (True, False):

            @pl.when(gets(step - 1, up) & jnp.logical_not(sends(step, up)))
            def _(up=up):
                landed(lines, 2 * (step - 1) + (0 if up else 1), right.at[shard_of(step, up)])

    for up in (True, False):

        @pl.when(sends(0, up))
        def _(up=up):
            hop(0, up).start()

    load_in.start()
    load_out.start()
    for g in range(8):
        load_x(g).start()


    load_in.wait()
    load_out.wait()

    @pl.loop(0, 8)
    def _(g):
        @pl.when(g == 6)
        def _():
            line_serve(1)

        load_x(g).wait()
        projected = dot(whole[g], w_in[...])
        gate, up = projected[:, :tile], projected[:, tile:]
        act, slope = gate_parts(gate)
        left[g] = (act * up).astype(BF16)
        kept[g] = jnp.concatenate([up * slope, act], axis=1).astype(BF16)

    load_first.start()
    load_grad.start()
    keep = pltpu.make_async_copy(kept, kept_ref, local.at[4])
    keep.start()

    def add(k, extra, start, offset, at):
        @pl.loop(0, half // SLAB)
        def _(step):
            row = pl.ds(pl.multiple_of(start + step * SLAB, SLAB), SLAB)
            of = pl.ds(pl.multiple_of(start - offset + step * SLAB, SLAB), SLAB)
            part[k, c, row, at] = (part[k, c, row, at].astype(F32) + extra[of, at].astype(F32)).astype(BF16)

    def chip_sum(k, at):
        add(k, got.at[k], 0, 0, at)
        add(k, got.at[k], half, 0, at)

    def product(k, block, at):
        found = dot(left[pl.ds(2 * chips[k], 2)].reshape(2 * rows, tile), right[block])
        part[k, 0, :, at] = found[:rows].astype(BF16)
        part[k, 1, :, at] = found[rows:].astype(BF16)

    def block_at(i):
        if i == 0:
            return z
        below = z < zs // 2
        near = jnp.where(below, z, zs - 1 - z)
        spot = jnp.where(i <= 2 * near, jnp.where(i % 2 == 1, near - (i + 1) // 2, near + i // 2), i)
        return jnp.where(below, spot, zs - 1 - spot)

    def block_cols(i):
        return pl.ds(pl.multiple_of(block_at(i) * wide, wide), wide)

    def fold_start(i):
        b, block, at = 8 * i, block_at(i), block_cols(i)
        rest = pl.ds(1, 3)
        product(0, block, at)
        push(folds, b, part.at[0, 1 - c, :, at], got.at[0, :, at], to_c)
        for k in (1, 2, 3):
            product(k, block, at)
        push(folds, b + 1, part.at[rest, 1 - c, :, at], got.at[rest, :, at], to_c)
        landed(folds, b, got.at[0, :, at])
        chip_sum(0, at)
        push(folds, b + 2, part.at[0, c, top, at], near_x.at[:, at], to_x)
        push(folds, b + 3, part.at[0, c, bottom, at], near_y.at[:, at], to_y)
        landed(folds, b + 1, got.at[rest, :, at])
        chip_sum(1, at)
        push(folds, b + 4, part.at[1, c, top, at], from_x.at[top, at], to_x)
        chip_sum(2, at)
        push(folds, b + 5, part.at[2, c, bottom, at], from_y.at[bottom, at], to_y)

    def fold_end(i):
        b, at = 8 * i, block_cols(i)
        landed(folds, b + 3, near_y.at[:, at])
        add(1, near_y, half, half, at)
        push(folds, b + 6, part.at[1, c, bottom, at], from_x.at[bottom, at], to_x)
        landed(folds, b + 2, near_x.at[:, at])
        add(2, near_x, 0, 0, at)
        push(folds, b + 7, part.at[2, c, top, at], from_y.at[top, at], to_y)

    gains = gains_ref[...]
    line_take(1)
    fold_start(0)
    fold_start(1)
    fold_end(0)
    for i in range(2, zs):
        if i < zs - 1:
            line_serve(i)
        fold_end(i - 1)
        line_take(i)
        fold_start(i)
    fold_end(zs - 1)
    carry = pltpu.make_async_copy(right, right_ref, local.at[5])
    carry.start()
    load_first.wait()
    load_grad.wait()
    acc[...] = jnp.zeros_like(acc)
    for i in range(zs):
        at = block_cols(i)
        landed(folds, 8 * i + 4, from_x.at[top, at])
        landed(folds, 8 * i + 5, from_y.at[bottom, at])
        landed(folds, 8 * i + 6, from_x.at[bottom, at])
        landed(folds, 8 * i + 7, from_y.at[top, at])

    def low(i):
        return pl.ds(*lows[i])

    def high(i):
        return pl.ds(*highs[i])

    def span(i):
        return pl.ds(i * half, half)

    def norm(i):
        @pl.loop(0, half // SLAB)
        def _(step):
            at = pl.ds(pl.multiple_of(i * half + step * SLAB, SLAB), SLAB)
            total = part[3, c, at].astype(F32) + got[3, at].astype(F32)
            total += from_x[at].astype(F32) + from_y[at].astype(F32)
            dy = grad[at].astype(F32)
            result, d_pre, terms = second_norm(total, first[at], dy, gains)
            result_ref[at] = result.astype(BF16)
            d_pre_ref[at] = d_pre
            whole[me, at] = d_pre.astype(BF16)
            acc[0] += terms
            acc[1] += dy

        b = 13 * i
        push(alls, b, whole.at[me, low(i)], whole.at[me, low(i)], to_x)
        push(alls, b + 1, whole.at[me, high(i)], whole.at[me, high(i)], to_y)
        push(alls, b + 2, whole.at[me, high(i)], whole.at[me, high(i)], to_x)
        push(alls, b + 3, whole.at[me, low(i)], whole.at[me, low(i)], to_y)
        push(alls, b + 4, whole.at[me, span(i)], whole.at[me, span(i)], to_c)

    def pass_on(i, k, slot, at, onward):
        ref = whole.at[slot, at]
        landed(alls, 13 * i + k, ref)
        for where, to in onward:
            push(alls, 13 * i + where, ref, ref, to)

    def spread_first(i):
        pass_on(i, 0, by_x, low(i), [(5, to_y), (7, to_c)])
        pass_on(i, 1, by_y, high(i), [(6, to_x), (8, to_c)])

    def spread_rest(i):
        pass_on(i, 2, by_x, high(i), [(9, to_c)])
        pass_on(i, 3, by_y, low(i), [(10, to_c)])

    def spread_far(i):
        pass_on(i, 5, far, low(i), [(11, to_c)])
        pass_on(i, 6, far, high(i), [(12, to_c)])

    outward = []

    def gradient(k, some=None, last=False, first_one=False):
        pair = pl.ds(2 * chips[k], 2)
        some = pl.ds(0, rows) if some is None else some
        if last or some.size == rows:
            outward.append(pltpu.make_async_copy(whole.at[pair], all_ref.at[pair], local.at[6 + k]))
            outward[-1].start()

        @pl.loop(0, zs)
        def _(block):
            at = pl.ds(pl.multiple_of(block * wide, wide), wide)
            tokens = 2 * some.size
            found = dot_rows(left[pair, some].reshape(tokens, tile), whole[pair, some, at].reshape(tokens, wide))
            if first_one:
                dw[block] = found
            elif last:
                dw_ref[block] = (dw[block] + found).astype(BF16)
                pltpu.make_async_copy(dw_ref.at[block], dw_out.at[block], x_local.at[block]).start()
            else:
                dw[block] += found

    norm(0)
    norm(1)
    stores = [
        pltpu.make_async_copy(result_ref, result_out, local.at[10]),
        pltpu.make_async_copy(d_pre_ref, d_pre_out, local.at[11]),
    ]
    for store in stores:
        store.start()
    spread_first(0)
    for i in (0, 1):
        landed(alls, 13 * i + 4, whole.at[other, span(i)])
    gradient(3, first_one=True)
    spread_rest(0)
    spread_first(1)
    spread_rest(1)
    for i in (0, 1):
        landed(alls, 13 * i + 7, whole.at[other_x, low(i)])
        landed(alls, 13 * i + 9, whole.at[other_x, high(i)])
    gradient(1)
    spread_far(0)
    for i in (0, 1):
        landed(alls, 13 * i + 8, whole.at[other_y, high(i)])
        landed(alls, 13 * i + 10, whole.at[other_y, low(i)])
    gradient(2)
    sums_ref[0:1] = jnp.sum(acc[0], axis=0, keepdims=True)
    sums_ref[1:2] = jnp.sum(acc[1], axis=0, keepdims=True)
    landed(alls, 11, whole.at[other_far, low(0)])
    landed(alls, 12, whole.at[other_far, high(0)])
    gradient(0, some=span(0))
    spread_far(1)
    landed(alls, 13 + 11, whole.at[other_far, low(1)])
    landed(alls, 13 + 12, whole.at[other_far, high(1)])
    gradient(0, some=span(1), last=True)
    for block in range(zs):
        pltpu.make_async_copy(dw_ref.at[block], dw_out.at[block], x_local.at[block]).wait()
    for copy in outward + [keep, carry] + stores:
        copy.wait()
    for copy in sent:
        copy.wait_send()
    for step in range(zs - 1):
        for up in (True, False):

            @pl.when(sends(step, up))
            def _(step=step, up=up):
                hop(step, up).wait_send()


def turn(zs, x, w_in, w_out, gains, first, grad):
    rows = x.shape[0] // 8
    units, wide = w_out.shape
    width = gains.shape[1]
    half = rows // 2
    by_z = (zs, units, wide)
    return pl.pallas_call(
        functools.partial(turn_kernel, zs, width // (8 * zs)),
        out_shape=[
            jax.ShapeDtypeStruct((8, rows, width), BF16),
            jax.ShapeDtypeStruct((8, rows, 2 * units), BF16),
            jax.ShapeDtypeStruct(by_z, BF16),
            jax.ShapeDtypeStruct((rows, width), BF16),
            jax.ShapeDtypeStruct((rows, width), F32),
            jax.ShapeDtypeStruct((8, width), F32),
            jax.ShapeDtypeStruct(by_z, BF16),
        ],
        in_specs=[ANY, ANY, ANY, ROWS, ANY, ANY],
        out_specs=[ANY] * 5 + [ROWS, ANY],
        scratch_shapes=[
            pltpu.VMEM((rows, width), BF16),
            pltpu.VMEM((rows, width), F32),
            pltpu.VMEM(by_z, BF16),
            pltpu.VMEM((rows, width), F32),
            pltpu.VMEM((rows, width), BF16),
            pltpu.VMEM(w_in.shape, BF16),
            pltpu.VMEM((8, rows, 2 * units), BF16),
            pltpu.VMEM((8, rows, units), BF16),
            pltpu.VMEM(by_z, BF16),
            pltpu.VMEM((4, 2, rows, width), BF16),
            pltpu.VMEM((4, rows, width), BF16),
            pltpu.VMEM((half, width), BF16),
            pltpu.VMEM((half, width), BF16),
            pltpu.VMEM((rows, width), BF16),
            pltpu.VMEM((rows, width), BF16),
            pltpu.VMEM((8, rows, width), BF16),
            pltpu.VMEM(by_z, F32),
            pltpu.VMEM((2, SLAB, width), F32),
            pltpu.SemaphoreType.DMA((8 * zs,)),
            pltpu.SemaphoreType.DMA((8 * zs,)),
            pltpu.SemaphoreType.DMA((26,)),
            pltpu.SemaphoreType.DMA((26,)),
            pltpu.SemaphoreType.DMA((2 * (zs - 1),)),
            pltpu.SemaphoreType.DMA((2 * (zs - 1),)),
            pltpu.SemaphoreType.DMA((12,)),
            pltpu.SemaphoreType.DMA((8,)),
        ],
        compiler_params=pltpu.CompilerParams(collective_id=1, has_side_effects=True, vmem_limit_bytes=60 * 2**20),
        cost_estimate=pl.CostEstimate(flops=0, bytes_accessed=380 * 2**20, transcendentals=0),
    )(x.reshape(8, rows, width), w_in, w_out, gains, first, grad)


def swap_kernel(zs, kinds, *refs):
    n = len(kinds)
    greet([name for _, name in swap_peers(zs, kinds)])
    swap_begin(zs, kinds, refs[:n], refs[n : 2 * n], *refs[2 * n :])()


def group_swap(name, zs, arrays, kinds):
    n = len(arrays)
    return pl.pallas_call(
        functools.partial(swap_kernel, zs, kinds),
        out_shape=swap_shapes(zs, arrays, kinds),
        in_specs=[ANY] * n,
        out_specs=[ANY] * n,
        scratch_shapes=swap_scratch(zs, kinds),
        compiler_params=pltpu.CompilerParams(collective_id=name, has_side_effects=True),
        cost_estimate=pl.CostEstimate(flops=0, bytes_accessed=50 * 2**20, transcendentals=0),
    )(*arrays)


def enter_kernel(zs, kinds, x_ref, grad_ref, *refs):
    n = len(kinds)
    blocks, x_all, grad_out, outs, refs = refs[:n], refs[n], refs[n + 1], refs[n + 2 : 2 * n + 2], refs[2 * n + 2 :]
    x_rows, sems = refs[0], refs[1:]
    rows, width = x_ref.shape
    greet([name for _, name in swap_peers(zs, kinds)])
    finish = swap_begin(zs, kinds, blocks, outs, *sems[:3])
    for ref, out in ((x_ref, x_rows), (grad_ref, grad_out)):

        @pl.loop(0, rows // SLAB)
        def _(step, ref=ref, out=out):
            at = pl.ds(pl.multiple_of(step * SLAB, SLAB), SLAB)
            out[at] = by_rows(ref[at].astype(F32), zs, width // (8 * zs)).astype(BF16)

    spread_block(rows // 2, 0, x_rows, x_all, *sems[3:])
    finish()


def enter(zs, x, grad, arrays, kinds):
    n = len(arrays)
    return pl.pallas_call(
        functools.partial(enter_kernel, zs, kinds),
        out_shape=[jax.ShapeDtypeStruct((8,) + x.shape, x.dtype), jax.ShapeDtypeStruct(grad.shape, grad.dtype)]
        + swap_shapes(zs, arrays, kinds),
        in_specs=[ROWS] * 2 + [ANY] * n,
        out_specs=[ANY, ROWS] + [ANY] * n,
        scratch_shapes=[pltpu.VMEM(x.shape, x.dtype)]
        + swap_scratch(zs, kinds)
        + [pltpu.SemaphoreType.DMA((13,)), pltpu.SemaphoreType.DMA((13,)), pltpu.SemaphoreType.DMA],
        compiler_params=pltpu.CompilerParams(collective_id=3, has_side_effects=True, vmem_limit_bytes=56 * 2**20),
        cost_estimate=pl.CostEstimate(flops=0, bytes_accessed=150 * 2**20, transcendentals=0),
    )(x, grad, *arrays)


def ff_kernel(x_ref, w_ref, hidden_ref, kept_ref):
    tile = hidden_ref.shape[1]
    projected = dot(x_ref[...], w_ref[...])
    gate, up = projected[:, :tile], projected[:, tile:]
    act, slope = gate_parts(gate)
    hidden_ref[...] = (act * up).astype(BF16)
    kept_ref[...] = jnp.concatenate([up * slope, act], axis=1).astype(BF16)


def ff_back_kernel(grad_ref, w_ref, kept_ref, out_ref):
    zs, _, wide = w_ref.shape
    d_hidden = dot_cols(grad_ref[:, :wide], w_ref[0])
    for z in range(1, zs):
        d_hidden += dot_cols(grad_ref[:, z * wide : (z + 1) * wide], w_ref[z])
    out_ref[...] = (jnp.concatenate([d_hidden, d_hidden], axis=1) * kept_ref[...].astype(F32)).astype(BF16)


FF_ROWS = 256


def ff_rows(width):
    return pl.BlockSpec((FF_ROWS, width), lambda i: (i, 0))


def ff_forward(x, w):
    rows, depth = x.shape
    wide = w.shape[1]
    return pl.pallas_call(
        ff_kernel,
        grid=(rows // FF_ROWS,),
        in_specs=[ff_rows(depth), pl.BlockSpec((depth, wide), lambda i: (0, 0))],
        out_specs=[ff_rows(wide // 2), ff_rows(wide)],
        out_shape=[jax.ShapeDtypeStruct((rows, wide // 2), BF16), jax.ShapeDtypeStruct((rows, wide), BF16)],
        compiler_params=PARAMS,
        cost_estimate=pl.CostEstimate(flops=2 * rows * depth * wide, bytes_accessed=20 * 2**20, transcendentals=0),
    )(x, w)


def ff_backward(grad, w, kept):
    rows, depth = grad.shape
    wide = kept.shape[1]
    return pl.pallas_call(
        ff_back_kernel,
        grid=(rows // FF_ROWS,),
        in_specs=[ff_rows(depth), pl.BlockSpec(w.shape, lambda i: (0, 0, 0)), ff_rows(wide)],
        out_specs=ff_rows(wide),
        out_shape=jax.ShapeDtypeStruct((rows, wide), BF16),
        compiler_params=PARAMS,
        cost_estimate=pl.CostEstimate(flops=rows * depth * wide, bytes_accessed=20 * 2**20, transcendentals=0),
    )(grad, w, kept)


def cut_kernel(in_ref, out_ref, in_blocks, out_blocks, wide):
    group, _, double = in_blocks.shape
    tile, ff = double // 2, out_ref.shape[1]
    span = group * tile
    odd = ff % 128
    live = lax.broadcasted_iota(jnp.int32, (in_ref.shape[0], span), 1) < ff
    wide[...] = jnp.zeros_like(wide)
    wide[:, : 2 * ff] = in_ref[...].astype(F32)
    gate = jnp.where(live, wide[:, :span], 0.0)
    up = pltpu.roll(wide[:, ff - odd : ff - odd + span], span - odd, 1)
    up = jnp.where(live, up, 0.0)
    wide[:, :span] = jnp.zeros_like(live, F32)
    wide[:, :ff] = out_ref[...].astype(F32)
    down = wide[:, :span]
    for g in range(group):
        at = slice(g * tile, (g + 1) * tile)
        in_blocks[g] = jnp.concatenate([gate[:, at], up[:, at]], axis=1).astype(BF16)
        out_blocks[g] = down[:, at].astype(BF16)


def cut_ff(w_in, w_out, group, tile):
    rows, ff = w_out.shape
    return pl.pallas_call(
        cut_kernel,
        grid=(rows // 16,),
        in_specs=[pl.BlockSpec((16, 2 * ff), lambda i: (i, 0)), pl.BlockSpec((16, ff), lambda i: (i, 0))],
        out_specs=[
            pl.BlockSpec((group, 16, 2 * tile), lambda i: (0, i, 0)),
            pl.BlockSpec((group, 16, tile), lambda i: (0, i, 0)),
        ],
        out_shape=[
            jax.ShapeDtypeStruct((group, rows, 2 * tile), BF16),
            jax.ShapeDtypeStruct((group, rows, tile), BF16),
        ],
        scratch_shapes=[pltpu.VMEM((16, -(-(ff + group * tile) // 128) * 128), F32)],
        compiler_params=SMALL,
    )(w_in, w_out)


def join_kernel(in_blocks, out_blocks, in_ref, out_ref):
    group, _, double = in_blocks.shape
    tile, ff = double // 2, out_ref.shape[1]
    odd = ff % 128
    blocks = [in_blocks[g].astype(F32) for g in range(group)]
    gate = jnp.concatenate([block[:, :tile] for block in blocks], axis=1)
    up = jnp.concatenate([block[:, tile:] for block in blocks], axis=1)
    up = pltpu.roll(up, odd, 1)
    lane = lax.broadcasted_iota(jnp.int32, (up.shape[0], 128), 1)
    in_ref[:, : ff - odd] = gate[:, : ff - odd]
    in_ref[:, ff - odd : ff - odd + 128] = jnp.where(lane < odd, gate[:, ff - odd : ff - odd + 128], up[:, :128])
    in_ref[:, ff - odd + 128 :] = up[:, 128 : ff + odd]
    down = jnp.concatenate([out_blocks[g].astype(F32) for g in range(group)], axis=1)
    out_ref[...] = down[:, :ff]


def join_ff(in_blocks, out_blocks, ff):
    group, rows, tile = out_blocks.shape
    return pl.pallas_call(
        join_kernel,
        grid=(rows // 16,),
        in_specs=[
            pl.BlockSpec((group, 16, 2 * tile), lambda i: (0, i, 0)),
            pl.BlockSpec((group, 16, tile), lambda i: (0, i, 0)),
        ],
        out_specs=[pl.BlockSpec((16, 2 * ff), lambda i: (i, 0)), pl.BlockSpec((16, ff), lambda i: (i, 0))],
        out_shape=[jax.ShapeDtypeStruct((rows, 2 * ff), F32), jax.ShapeDtypeStruct((rows, ff), F32)],
        compiler_params=SMALL,
    )(in_blocks, out_blocks)


def closing_kernel(zs, sum_ref, rows_ref, qkv_ref, total_ref, got, lines, *refs):
    send, recv, local, line_send, line_recv = refs
    y, x, c = here()
    z = lax.axis_index("z")
    me = place(y, x, c)
    wide = got.shape[2]
    width = wide // 3
    piece = got.shape[1]
    found = swap_peers(zs, ("line",))
    greet([name for _, name in found])
    copies, comes = [], []
    for k, (peer, name) in enumerate(found[:7]):
        sems = dict(send_sem=send.at[k], recv_sem=recv.at[k], device_id=name, device_id_type=MESH)
        copies.append(pltpu.make_async_remote_copy(src_ref=rows_ref.at[peer], dst_ref=got.at[me], **sems))
        comes.append(pltpu.make_async_remote_copy(src_ref=got.at[peer], dst_ref=got.at[peer], **sems))
    for k, (peer, name) in enumerate(found[7:]):
        sems = dict(send_sem=line_send.at[k], recv_sem=line_recv.at[k], device_id=name, device_id_type=MESH)
        copies.append(pltpu.make_async_remote_copy(src_ref=sum_ref, dst_ref=lines.at[z], **sems))
        comes.append(pltpu.make_async_remote_copy(src_ref=lines.at[peer], dst_ref=lines.at[peer], **sems))
    for copy in copies:
        copy.start()
    keeps = [
        pltpu.make_async_copy(rows_ref.at[me], got.at[me], local.at[0]),
        pltpu.make_async_copy(sum_ref, lines.at[z], local.at[1]),
    ]
    for keep in keeps:
        keep.start()
    for come in comes:
        come.wait_recv()
    for keep in keeps:
        keep.wait()
    for g in range(8):
        for j in range(3):
            at = pl.ds(j * D + g * width, width)
            qkv_ref[:, at] = got[g, :, j * width : (j + 1) * width].astype(F32)
    total = lines[0]
    for k in range(1, zs):
        total += lines[k]
    part = total[:, :piece]
    for k in range(1, zs):
        part = jnp.where(z == k, total[:, k * piece : (k + 1) * piece], part)
    total_ref[...] = part
    for copy in copies:
        copy.wait_send()


def closing(zs, sums, rows):
    _, piece, columns = rows.shape
    width = columns // 3
    return pl.pallas_call(
        functools.partial(closing_kernel, zs),
        out_shape=[
            jax.ShapeDtypeStruct((piece, 3 * D), F32),
            jax.ShapeDtypeStruct((8, piece), F32),
        ],
        in_specs=[ROWS, ANY],
        out_specs=[ROWS] * 2,
        scratch_shapes=[
            pltpu.VMEM((8, piece, 3 * width), BF16),
            pltpu.VMEM((zs, 8, width), F32),
            pltpu.SemaphoreType.DMA((7,)),
            pltpu.SemaphoreType.DMA((7,)),
            pltpu.SemaphoreType.DMA((2,)),
            pltpu.SemaphoreType.DMA((zs - 1,)),
            pltpu.SemaphoreType.DMA((zs - 1,)),
        ],
        compiler_params=pltpu.CompilerParams(collective_id=5, has_side_effects=True, vmem_limit_bytes=24 * 2**20),
        cost_estimate=pl.CostEstimate(flops=0, bytes_accessed=50 * 2**20, transcendentals=0),
    )(sums, rows)


def on_device(sizes, x_in, d_out, w_qkv, w_dense, w_in, w_out, gone, bone, gtwo, btwo, flags, span_start, span_len):
    gy, gx, cores, zs = sizes
    piece = w_qkv.shape[0]
    ff = w_out.shape[1]
    group = gy * gx * cores
    width = D // group
    tile = -(-ff // (group * 64)) * 64
    own = gy == 2

    def permute(array):
        lead = array.shape[:-1]
        return jnp.swapaxes(array.reshape(lead + (group, zs, piece)), -3, -2).reshape(lead + (D,))

    def restore(array):
        lead = array.shape[:-1]
        return jnp.swapaxes(array.reshape(lead + (zs, group, piece)), -3, -2).reshape(lead + (D,))

    def swap(name, arrays, kinds):
        if own:
            return group_swap(name, zs, arrays, kinds)
        ways = {
            "swap": lambda a: lax.all_to_all(a, GROUP, 0, 0, tiled=True),
            "group": lambda a: lax.all_gather(a, GROUP, axis=0),
            "line": lambda a: lax.all_gather(a, "z", axis=0),
        }
        return [ways[k](a) for a, k in zip(arrays, kinds)]

    def spread_rows(block):
        return lax.all_gather(block, GROUP, axis=0, tiled=True)

    rows_f32 = jax.ShapeDtypeStruct((SEQ_LEN, D), F32)
    rows_low = jax.ShapeDtypeStruct((SEQ_LEN, D), BF16)
    sums_type = jax.ShapeDtypeStruct((8, D), F32)

    def fold(partial):
        return lax.psum_scatter(partial.astype(BF16), GROUP, scatter_dimension=0, tiled=True).astype(F32)

    def stack_sums(*arrays):
        return jnp.pad(jnp.stack([jnp.sum(a, axis=0) for a in arrays]), ((0, 6), (0, 0)))

    def fold_one(left, right, x, gains):
        if own:
            kinds = [rows_f32, rows_f32, jax.ShapeDtypeStruct((SEQ_LEN, 128), F32)]
            whole, first, normal, inverse = group_fold(0, zs, "one", left, right, gains, [x], kinds)
            return whole.reshape(left.shape[0], D), first, normal, inverse
        first, normal, inverse = first_norm(permute(deep_alpha * x.astype(F32) + fold(dot(left, right))), gains)
        return spread_rows(first.astype(BF16)), first, normal, inverse

    def ff_turn(x, w_in, w_out, first, grad, gains):
        if own:
            whole, kept, w_out, result, d_pre, sums, d_out = turn(zs, x, w_in, w_out, gains, first, grad)
            rows = x.shape[0]
            return whole.reshape(rows, D), kept.reshape(rows, -1), w_out, result, d_pre, sums, d_out
        w_out = lax.all_gather(w_out, "z", axis=0)
        hidden, kept = ff_forward(x, w_in)
        grad = grad.astype(F32)
        right = jnp.swapaxes(w_out, 0, 1).reshape(-1, D)
        result, d_pre, terms = second_norm(fold(dot(hidden, right)), first, grad, gains)
        whole = spread_rows(d_pre.astype(BF16))
        d_out = jnp.swapaxes(dot_rows(hidden, whole).reshape(-1, zs, D // zs), 0, 1).astype(BF16)
        return whole, kept, w_out, result.astype(BF16), d_pre, stack_sums(terms, grad), d_out

    def fold_back(left, right, d_pre_two, normal, inverse, gains):
        if own:
            kinds = [rows_f32, sums_type]
            whole, d_pre, sums = group_fold(7, zs, "back", left, right, gains, [d_pre_two, normal, inverse], kinds)
            return whole.reshape(left.shape[0], D), d_pre, sums
        d_pre, terms, d_first = first_back(fold(dot_cols(left, right)), d_pre_two, normal, inverse, gains)
        return spread_rows(restore(d_pre).astype(BF16)), d_pre, stack_sums(terms, d_first)

    def fold_last(left, right, d_pre, gains, extras, kinds):
        if own:
            return group_fold(8, zs, "last", left, right, gains, [d_pre], [rows_low], extras, kinds)
        out = restore((deep_alpha * d_pre + fold(dot_cols(left, right))).astype(BF16))
        return [out] + swap(8, extras, kinds)

    def gather(block):
        return lax.all_gather(block, "z", axis=0, tiled=True)

    def scatter(partial):
        return lax.psum_scatter(partial.astype(BF16), "z", scatter_dimension=0, tiled=True)

    masked = jnp.max(flags) > 0
    prefix = jnp.where(masked, SEQ_LEN, SEQ_LEN - span_len[0])
    info = jnp.concatenate([gone, bone, gtwo, btwo, jnp.stack([prefix, span_start[0]]).astype(BF16)])
    info = jnp.pad(info[None, :], ((0, 15), (0, -info.shape[0] % 128)))

    qkv_blocks = jnp.moveaxis(w_qkv.reshape(piece, 3, group, width), 2, 0).reshape(group, piece, 3 * width)
    w_dense_part = gather(w_dense)
    qkv_blocks, info = swap(2, [qkv_blocks, info], ("swap", "group"))
    w_qkv_part = gather(qkv_blocks.reshape(group * piece, 3 * width))
    info = info[:, 0]
    place_info = info[:, 4 * piece : 4 * piece + 2].astype(jnp.int32)
    prefix, start = place_info[:, 0], place_info[:, 1]
    cosine, sine = tables(prefix, start)
    in_blocks, out_blocks = cut_ff(w_in, w_out, group, tile)
    info = jnp.pad(info, ((0, -group % 16), (0, 0)))
    in_blocks, out_blocks, qkv_blocks, w_dense_part, cosine, sine = lax.optimization_barrier(
        (in_blocks, out_blocks, qkv_blocks, w_dense_part, cosine, sine)
    )
    swapped, kinds = [in_blocks, out_blocks, info], ("swap", "swap", "line")
    if own:
        x_all, grad_two, in_blocks, out_blocks, info = enter(zs, x_in, d_out, swapped, kinds)
        x_all = x_all.reshape(group * SEQ_LEN, D)
    else:
        x_all, grad_two = spread_rows(permute(x_in)), permute(d_out)
        in_blocks, out_blocks, info = swap(3, swapped, kinds)
    w_in_part = gather(in_blocks.reshape(group * piece, 2 * tile))
    out_rows = out_blocks.reshape(group * piece, tile).T
    gains = info[:, :group, : 4 * piece].astype(F32).reshape(zs, group, 4, piece)
    gains = jnp.pad(jnp.transpose(gains, (2, 0, 1, 3)).reshape(4, D), ((0, 4), (0, 0)))
    w_qkv_part, x_all, gains, out_rows = lax.optimization_barrier((w_qkv_part, x_all, gains, out_rows))
    packed = dot(x_all, w_qkv_part)
    qkv, context = attend(prefix, packed, cosine, sine)
    first_all, first, normal_one, inverse_one = fold_one(context, w_dense_part, x_in, gains)
    d_branch, kept, w_out_part, layer_out, d_pre_two, sums_two, d_w_out = ff_turn(
        first_all, w_in_part, out_rows, first, grad_two, gains
    )
    layer_out = restore(layer_out)
    d_w_out = lax.psum_scatter(d_w_out, "z", scatter_dimension=0)
    d_projected = ff_backward(d_branch, w_out_part, kept)
    d_w_in = dot_rows(first_all, d_projected).astype(BF16)
    d_w_in, d_projected = lax.optimization_barrier((d_w_in, d_projected))
    d_w_in = scatter(d_w_in)
    d_attn, d_pre_one, sums_one = fold_back(d_projected, w_in_part, d_pre_two, normal_one, inverse_one, gains)
    d_attn, d_w_out = lax.optimization_barrier((d_attn, d_w_out))
    d_context = dot_cols(d_attn, w_dense_part).astype(BF16)
    d_packed = attend_back(prefix, qkv, d_context, cosine, sine)
    d_w_qkv = dot_rows(x_all, d_packed).astype(BF16)
    sums = jnp.concatenate([sums_one[:2], sums_two[:2], jnp.zeros((4, D), F32)])
    d_w_qkv = with_layout_constraint(d_w_qkv, Layout((0, 1)))
    d_dense = dot_rows(context, d_attn).astype(BF16)
    d_packed, d_w_qkv, d_w_in, sums, d_dense = lax.optimization_barrier((d_packed, d_w_qkv, d_w_in, sums, d_dense))
    d_w_qkv = scatter(d_w_qkv)
    d_dense = scatter(d_dense)
    d_w_in, d_w_out = d_w_in.reshape(group, piece, 2 * tile), d_w_out.T.reshape(group, piece, tile)
    d_input, d_w_in, d_w_out, sums = fold_last(
        d_packed, w_qkv_part, d_pre_one, gains, [d_w_in, d_w_out, sums], ("swap", "swap", "group")
    )
    sums = jnp.sum(sums, axis=0).reshape(8, zs, group, piece)
    sums = lax.dynamic_index_in_dim(sums, lax.axis_index(GROUP), 2, keepdims=False).reshape(8, width)
    out_in, out_out = join_ff(d_w_in, d_w_out, ff)
    out_in, out_out, d_input, d_w_qkv, sums = lax.optimization_barrier((out_in, out_out, d_input, d_w_qkv, sums))
    if own:
        out_qkv, sums = closing(zs, sums, d_w_qkv.reshape(group, piece, 3 * width))
    else:
        d_w_qkv, sums = swap(5, [d_w_qkv.reshape(group, piece, 3 * width), sums], ("swap", "line"))
        out_qkv = jnp.transpose(d_w_qkv.astype(F32).reshape(group, piece, 3, width), (1, 2, 0, 3))
        out_qkv = out_qkv.reshape(piece, 3 * D)
        sums = jnp.sum(sums, axis=0).reshape(8, zs, piece)
        sums = lax.dynamic_index_in_dim(sums, lax.axis_index("z"), 1, keepdims=False)
    out_qkv, sums, d_dense = lax.optimization_barrier((out_qkv, sums, d_dense))
    out_dense = d_dense.astype(F32)
    return layer_out, d_input, out_qkv, out_dense, out_in, out_out, sums[0], sums[1], sums[2], sums[3]


def solution(mesh):
    grp, shard = mesh.shape["grp"], mesh.shape["shard"]
    sizes = (grp // 4, 2, 2, shard)
    inner = Mesh(mesh.devices.reshape(sizes), ALL)
    rows, flat = P(ALL, None), P(ALL)
    return jax.shard_map(
        functools.partial(on_device, sizes),
        mesh=inner,
        in_specs=(rows,) * 6 + (flat,) * 7,
        out_specs=(rows,) * 6 + (flat,) * 4,
        check_vma=False,
    )
```

```python
import functools

import jax
import jax.numpy as jnp
from jax import lax
from jax.experimental import pallas as pl
from jax.experimental.pallas import tpu as pltpu
from jax.experimental.layout import Layout, with_layout_constraint
from jax.sharding import Mesh
from jax.sharding import PartitionSpec as P

HEADS = 16
HEAD = 128
SEQ_LEN = 224
D = HEADS * HEAD
deep_alpha = 6.928203230275509
norm_eps = 1e-05
far_below = -1e30
scale = HEAD ** (-0.5)

ALL = ("gy", "gx", "core", "z")
GROUP = ("gy", "gx", "core")
MESH = pl.DeviceIdType.MESH
F32 = jnp.float32
BF16 = jnp.bfloat16


def dot(left, right):
    return jnp.dot(left, right, preferred_element_type=F32)


def dot_rows(left, right):
    return lax.dot_general(left, right, (((0,), (0,)), ((), ())), preferred_element_type=F32)


def dot_cols(left, right):
    return lax.dot_general(left, right, (((1,), (1,)), ((), ())), preferred_element_type=F32)


def swap_halves(block):
    lane = lax.broadcasted_iota(jnp.int32, block.shape, 1)
    return jnp.where((lane & 32) == 0, pltpu.roll(block, 96, 1), pltpu.roll(block, 32, 1))


def seen(prefix):
    row = lax.broadcasted_iota(jnp.int32, (SEQ_LEN, SEQ_LEN), 0)
    col = lax.broadcasted_iota(jnp.int32, (SEQ_LEN, SEQ_LEN), 1)
    return (col < prefix) | (col <= row)


def softmax(queries, keys, visible):
    scores = jnp.where(visible, dot_cols(queries, keys), far_below)
    weights = jnp.exp(scores - jnp.max(scores, axis=1, keepdims=True))
    return weights / jnp.sum(weights, axis=1, keepdims=True)


def attend_kernel(prefix_ref, packed_ref, cos_ref, sin_ref, qkv_ref, context_ref):
    width = context_ref.shape[1]
    visible = seen(prefix_ref[pl.program_id(0)])
    cosine = cos_ref[0]
    sine = sin_ref[0]
    for head in range(width // HEAD):
        at = pl.ds(head * HEAD, HEAD)
        at_k = pl.ds(width + head * HEAD, HEAD)
        at_v = pl.ds(2 * width + head * HEAD, HEAD)
        raw = packed_ref[:, at]
        queries = ((raw * cosine + swap_halves(raw) * sine) * scale).astype(BF16)
        raw = packed_ref[:, at_k]
        keys = (raw * cosine + swap_halves(raw) * sine).astype(BF16)
        values = packed_ref[:, at_v].astype(BF16)
        qkv_ref[:, at] = queries
        qkv_ref[:, at_k] = keys
        qkv_ref[:, at_v] = values
        probs = softmax(queries, keys, visible).astype(BF16)
        context_ref[:, at] = dot(probs, values).astype(BF16)


def attend_back_kernel(prefix_ref, qkv_ref, d_context_ref, cos_ref, sin_ref, d_packed_ref):
    width = d_context_ref.shape[1]
    visible = seen(prefix_ref[pl.program_id(0)])
    cosine = cos_ref[0]
    sine = sin_ref[0]
    for head in range(width // HEAD):
        at = pl.ds(head * HEAD, HEAD)
        at_k = pl.ds(width + head * HEAD, HEAD)
        at_v = pl.ds(2 * width + head * HEAD, HEAD)
        queries = qkv_ref[:, at]
        keys = qkv_ref[:, at_k]
        values = qkv_ref[:, at_v]
        d_context = d_context_ref[:, at]
        probs = softmax(queries, keys, visible)
        d_packed_ref[:, at_v] = dot_rows(probs.astype(BF16), d_context).astype(BF16)
        d_probs = dot_cols(d_context, values)
        inner = jnp.sum(probs * d_probs, axis=1, keepdims=True)
        d_scores = (probs * (d_probs - inner)).astype(BF16)
        grad = dot(d_scores, keys) * scale
        d_packed_ref[:, at] = (grad * cosine - swap_halves(grad) * sine).astype(BF16)
        grad = dot_rows(d_scores, queries)
        d_packed_ref[:, at_k] = (grad * cosine - swap_halves(grad) * sine).astype(BF16)


def by_sequence(width):
    return pl.BlockSpec((SEQ_LEN, width), lambda s: (s, 0))


TABLE = pl.BlockSpec((1, SEQ_LEN, HEAD), lambda s: (s, 0, 0))
SCALARS = pl.BlockSpec(memory_space=pltpu.SMEM)
PARAMS = pltpu.CompilerParams(vmem_limit_bytes=56 * 2**20)
SMALL = pltpu.CompilerParams(vmem_limit_bytes=24 * 2**20)


def attend(prefix, packed, cosine, sine):
    rows, width = packed.shape[0], packed.shape[1] // 3
    return pl.pallas_call(
        attend_kernel,
        grid=(rows // SEQ_LEN,),
        in_specs=[SCALARS, by_sequence(3 * width), TABLE, TABLE],
        out_specs=[by_sequence(3 * width), by_sequence(width)],
        out_shape=[
            jax.ShapeDtypeStruct((rows, 3 * width), BF16),
            jax.ShapeDtypeStruct((rows, width), BF16),
        ],
        compiler_params=PARAMS,
    )(prefix, packed, cosine, sine)


def attend_back(prefix, qkv, d_context, cosine, sine):
    rows, width = d_context.shape
    return pl.pallas_call(
        attend_back_kernel,
        grid=(rows // SEQ_LEN,),
        in_specs=[SCALARS, by_sequence(3 * width), by_sequence(width), TABLE, TABLE],
        out_specs=by_sequence(3 * width),
        out_shape=jax.ShapeDtypeStruct((rows, 3 * width), BF16),
        compiler_params=PARAMS,
    )(prefix, qkv, d_context, cosine, sine)


def tables(prefix, start):
    place = jnp.arange(SEQ_LEN, dtype=jnp.int32)
    in_span = place[None, :] >= prefix[:, None]
    pos_one = jnp.where(in_span, start[:, None], place[None, :])
    pos_two = jnp.where(in_span, place[None, :] - prefix[:, None] + 1, 0)
    lane = jnp.arange(HEAD)
    freqs = 10000.0 ** (-2.0 * (lane % 32).astype(F32) / 64)
    place_of = jnp.where(lane[None, None, :] < 64, pos_one[:, :, None], pos_two[:, :, None])
    angles = place_of.astype(F32) * freqs
    sign = jnp.where(lane % 64 < 32, -1.0, 1.0)
    return jnp.cos(angles), jnp.sin(angles) * sign


def norm_parts(values):
    center = values - jnp.mean(values, axis=-1, keepdims=True)
    inverse = lax.rsqrt(jnp.mean(center * center, axis=-1, keepdims=True) + norm_eps)
    return center * inverse, inverse


def norm_back(normal, inverse, gain, grad):
    scaled = gain * grad
    return inverse * (
        scaled
        - jnp.mean(scaled, axis=-1, keepdims=True)
        - normal * jnp.mean(scaled * normal, axis=-1, keepdims=True)
    )


def gate_parts(gate):
    phi = 0.5 * (1.0 + lax.erf(gate * 0.7071067811865476))
    slope = phi + gate * jnp.exp(-0.5 * gate * gate) * 0.3989422804014327
    return gate * phi, slope


def here():
    return lax.axis_index("gy"), lax.axis_index("gx"), lax.axis_index("core")


def place(y, x, c):
    return (y * 2 + x) * 2 + c


def greet(peers):
    barrier = pltpu.get_barrier_semaphore()
    for peer in peers:
        pl.semaphore_signal(barrier, inc=1, device_id=peer, device_id_type=MESH)
    pl.semaphore_wait(barrier, len(peers))


def spread_block(cut, base, block_ref, out_ref, send, recv, local):
    rows = block_ref.shape[0]
    y, x, c = here()
    to_x, to_y, to_c = {"gx": 1 - x}, {"gy": 1 - y}, {"core": 1 - c}
    me, by_x, by_y, far = place(y, x, c), place(y, 1 - x, c), place(1 - y, x, c), place(1 - y, 1 - x, c)
    low, high = pl.ds(0, cut), pl.ds(cut, rows - cut)

    def push(k, src, dst, to):
        copy = pltpu.make_async_remote_copy(
            src_ref=src, dst_ref=dst, send_sem=send.at[base + k], recv_sem=recv.at[base + k], device_id=to, device_id_type=MESH
        )
        copy.start()
        return copy

    def landed(k, dst):
        pltpu.make_async_remote_copy(
            src_ref=dst, dst_ref=dst, send_sem=send.at[base + k], recv_sem=recv.at[base + k], device_id=to_c, device_id_type=MESH
        ).wait_recv()

    sent = [
        push(0, block_ref.at[low], out_ref.at[me, low], to_x),
        push(1, block_ref.at[high], out_ref.at[me, high], to_y),
        push(2, block_ref.at[high], out_ref.at[me, high], to_x),
        push(3, block_ref.at[low], out_ref.at[me, low], to_y),
        push(4, block_ref, out_ref.at[me], to_c),
    ]
    keep = pltpu.make_async_copy(block_ref, out_ref.at[me], local)
    keep.start()
    landed(0, out_ref.at[by_x, low])
    sent.append(push(5, out_ref.at[by_x, low], out_ref.at[by_x, low], to_y))
    sent.append(push(7, out_ref.at[by_x, low], out_ref.at[by_x, low], to_c))
    landed(1, out_ref.at[by_y, high])
    sent.append(push(6, out_ref.at[by_y, high], out_ref.at[by_y, high], to_x))
    sent.append(push(8, out_ref.at[by_y, high], out_ref.at[by_y, high], to_c))
    landed(2, out_ref.at[by_x, high])
    sent.append(push(9, out_ref.at[by_x, high], out_ref.at[by_x, high], to_c))
    landed(3, out_ref.at[by_y, low])
    sent.append(push(10, out_ref.at[by_y, low], out_ref.at[by_y, low], to_c))
    landed(5, out_ref.at[far, low])
    sent.append(push(11, out_ref.at[far, low], out_ref.at[far, low], to_c))
    landed(6, out_ref.at[far, high])
    sent.append(push(12, out_ref.at[far, high], out_ref.at[far, high], to_c))
    other, other_x, other_y, other_far = (
        place(y, x, 1 - c),
        place(y, 1 - x, 1 - c),
        place(1 - y, x, 1 - c),
        place(1 - y, 1 - x, 1 - c),
    )
    landed(4, out_ref.at[other])
    landed(7, out_ref.at[other_x, low])
    landed(8, out_ref.at[other_y, high])
    landed(9, out_ref.at[other_x, high])
    landed(10, out_ref.at[other_y, low])
    landed(11, out_ref.at[other_far, low])
    landed(12, out_ref.at[other_far, high])
    keep.wait()
    for copy in sent:
        copy.wait_send()


ANY = pl.BlockSpec(memory_space=pl.ANY)


def swap_peers(zs, kinds):
    y, x, c = here()
    z = lax.axis_index("z")
    found = []
    for k in range(1, 8):
        peer = ((y + k // 4) % 2, (x + k // 2 % 2) % 2, (c + k % 2) % 2)
        found.append((place(*peer), {"gy": peer[0], "gx": peer[1], "core": peer[2]}))
    if "line" in kinds:
        found += [((z + k) % zs, {"z": (z + k) % zs}) for k in range(1, zs)]
    return found


def swap_begin(zs, kinds, blocks, outs, send, recv, local):
    copies, comes, keeps = [], [], []
    found = swap_peers(zs, kinds)
    for i, kind in enumerate(kinds):
        me = lax.axis_index("z") if kind == "line" else place(*here())
        for k, (peer, name) in enumerate(found[7:] if kind == "line" else found[:7]):
            src = blocks[i].at[peer] if kind == "swap" else blocks[i]
            landing = outs[i].at[peer]
            sems = dict(send_sem=send.at[i, k], recv_sem=recv.at[i, k], device_id=name, device_id_type=MESH)
            copies.append(pltpu.make_async_remote_copy(src_ref=src, dst_ref=outs[i].at[me], **sems))
            comes.append(pltpu.make_async_remote_copy(src_ref=landing, dst_ref=landing, **sems))
            copies[-1].start()
        own = blocks[i].at[me] if kind == "swap" else blocks[i]
        keeps.append(pltpu.make_async_copy(own, outs[i].at[me], local.at[i]))
        keeps[-1].start()

    def finish():
        for come in comes:
            come.wait_recv()
        for copy in copies:
            copy.wait_send()
        for keep in keeps:
            keep.wait()

    return finish


SWAP_LEAD = {"swap": lambda zs: (), "group": lambda zs: (8,), "line": lambda zs: (zs,)}


def swap_shapes(zs, arrays, kinds):
    return [jax.ShapeDtypeStruct(SWAP_LEAD[k](zs) + a.shape, a.dtype) for a, k in zip(arrays, kinds)]


def swap_scratch(zs, kinds):
    n, most = len(kinds), max(7, zs - 1)
    return [
        pltpu.SemaphoreType.DMA((n, most)),
        pltpu.SemaphoreType.DMA((n, most)),
        pltpu.SemaphoreType.DMA((n,)),
    ]


SLAB = 16
ROWS = pl.BlockSpec(memory_space=pltpu.VMEM)
CHIP_COLS = 256


def by_rows(value, zs, piece):
    group = D // (zs * piece)
    order = [g * zs + z for z in range(zs) for g in range(group)]
    return jnp.concatenate([value[:, m * piece : (m + 1) * piece] for m in order], axis=1)


def in_order(value, zs, piece):
    group = D // (zs * piece)
    order = [z * group + g for g in range(group) for z in range(zs)]
    return jnp.concatenate([value[:, m * piece : (m + 1) * piece] for m in order], axis=1)


def first_norm(values, gains):
    normal, inverse = norm_parts(values)
    first = normal * gains[0:1] + gains[1:2]
    return first, normal, inverse


def second_norm(total, first, grad, gains):
    normal, inverse = norm_parts(deep_alpha * first + total)
    return normal * gains[2:3] + gains[3:4], norm_back(normal, inverse, gains[2:3], grad), grad * normal


def first_back(total, d_pre_two, normal, inverse, gains):
    d_first = deep_alpha * d_pre_two + total
    return norm_back(normal, inverse, gains[0:1], d_first), d_first * normal, d_first


def fold_kernel(mode, across, zs, piece, n_aux, n_out, kinds, *refs):
    left_ref, right_ref, gains_ref = refs[:3]
    aux_refs = refs[3 : 3 + n_aux]
    refs = refs[3 + n_aux :]
    n_swap = len(kinds)
    swap_in, refs = refs[:n_swap], refs[n_swap:]
    spread = mode != "last"
    if spread:
        all_ref, refs = refs[0], refs[1:]
    out_refs, refs = refs[:n_out], refs[n_out:]
    swap_out, refs = refs[:n_swap], refs[n_swap:]
    aux, refs = refs[:n_aux], refs[n_aux:]
    outs, refs = refs[:n_out], refs[n_out:]
    left, right, part, got, near_x, near_y, from_x, from_y, block, acc, send, recv, local = refs[:13]
    rows, width = block.shape
    cut = near_x.shape[0]
    y, x, c = here()
    to_x, to_y, to_c = {"gx": 1 - x}, {"gy": 1 - y}, {"core": 1 - c}
    chips = [(1 - y, 1 - x), (y, 1 - x), (1 - y, x), (y, x)]
    low, high = pl.ds(0, cut), pl.ds(cut, rows - cut)

    def push(k, src, dst, to):
        copy = pltpu.make_async_remote_copy(
            src_ref=src, dst_ref=dst, send_sem=send.at[k], recv_sem=recv.at[k], device_id=to, device_id_type=MESH
        )
        copy.start()
        return copy

    def add(k, extra, start, size, offset=0):
        @pl.loop(0, size // SLAB)
        def _(step):
            at = pl.ds(pl.multiple_of(start + step * SLAB, SLAB), SLAB)
            of = pl.ds(pl.multiple_of(start - offset + step * SLAB, SLAB), SLAB)
            part[k, c, at] = (part[k, c, at].astype(F32) + extra[of].astype(F32)).astype(BF16)

    loads = [pltpu.make_async_copy(left_ref.at[a * 2 + b], left.at[k], local.at[k]) for k, (a, b) in enumerate(chips)]
    load_right = pltpu.make_async_copy(right_ref, right, local.at[4])
    load_aux = [pltpu.make_async_copy(r, v, local.at[5 + k]) for k, (r, v) in enumerate(zip(aux_refs, aux))]
    loads[0].start()
    load_right.start()
    for load in loads[1:] + load_aux:
        load.start()
    if n_swap:
        greet([name for _, name in swap_peers(1, kinds)])
        swap_finish = swap_begin(1, kinds, swap_in, swap_out, *refs[13:])
    else:
        greet([to_x, to_y, to_c])

    def product(k):
        loads[k].wait()

        @pl.loop(0, width // CHIP_COLS)
        def _(step):
            at = pl.ds(pl.multiple_of(step * CHIP_COLS, CHIP_COLS), CHIP_COLS)
            here_part = dot_cols(left[k], right[at]) if across else dot(left[k], right[:, at])
            part[k, 0, :, at] = here_part[:rows].astype(BF16)
            part[k, 1, :, at] = here_part[rows:].astype(BF16)

        return push(k, part.at[k, 1 - c], got.at[k], to_c)

    load_right.wait()
    sent = [product(0), product(1)]
    sent[0].wait_recv()
    add(0, got.at[0], 0, rows)
    far_x = push(4, part.at[0, c, low], near_x, to_x)
    far_y = push(5, part.at[0, c, high], near_y, to_y)
    sent.append(product(2))
    sent[1].wait_recv()
    add(1, got.at[1], 0, rows)
    plain_x = push(6, part.at[1, c, low], from_x.at[low], to_x)
    sent[2].wait_recv()
    add(2, got.at[2], 0, rows)
    plain_y = push(7, part.at[2, c, high], from_y.at[high], to_y)
    sent.append(product(3))
    far_y.wait_recv()
    add(1, near_y, cut, rows - cut, cut)
    more_x = push(8, part.at[1, c, high], from_x.at[high], to_x)
    far_x.wait_recv()
    add(2, near_x, 0, cut)
    more_y = push(9, part.at[2, c, low], from_y.at[low], to_y)
    sent[3].wait_recv()
    for load in load_aux:
        load.wait()
    plain_x.wait_recv()
    plain_y.wait_recv()
    more_x.wait_recv()
    more_y.wait_recv()
    gains = gains_ref[...]
    acc[...] = jnp.zeros_like(acc)

    @pl.loop(0, rows // SLAB)
    def _(step):
        at = pl.ds(pl.multiple_of(step * SLAB, SLAB), SLAB)
        total = part[3, c, at].astype(F32) + got[3, at].astype(F32) + from_x[at].astype(F32) + from_y[at].astype(F32)
        held = [a[at].astype(F32) for a in aux]
        if mode == "one":
            first, normal, inverse = first_norm(by_rows(deep_alpha * held[0] + total, zs, piece), gains)
            outs[0][at] = first
            outs[1][at] = normal
            outs[2][at] = jnp.broadcast_to(inverse, (SLAB, 128))
            block[at] = first.astype(BF16)
        elif mode == "back":
            d_pre, terms, d_first = first_back(total, held[0], held[1], held[2][:, 0:1], gains)
            outs[0][at] = d_pre
            block[at] = in_order(d_pre, zs, piece).astype(BF16)
            acc[0] += terms
            acc[1] += d_first
        else:
            outs[0][at] = in_order(deep_alpha * held[0] + total, zs, piece).astype(BF16)

    if mode == "back":
        outs[-1][0:1] = jnp.sum(acc[0], axis=0, keepdims=True)
        outs[-1][1:2] = jnp.sum(acc[1], axis=0, keepdims=True)
    stores = [pltpu.make_async_copy(v, r, local.at[5 + n_aux + k]) for k, (v, r) in enumerate(zip(outs, out_refs))]
    for store in stores:
        store.start()
    for copy in sent + [far_x, far_y, plain_x, plain_y, more_x, more_y]:
        copy.wait_send()
    if n_swap:
        swap_finish()
    if spread:
        spread_block(cut, 10, block, all_ref, send, recv, local.at[4])
    for store in stores:
        store.wait()


def group_fold(name, zs, mode, left, right, gains, aux, out_types, extras=(), kinds=()):
    across = mode != "one"
    rows, depth = left.shape[0] // 8, left.shape[1]
    width = gains.shape[1]
    cut = rows // 2
    spread = mode != "last"
    out_shape = [jax.ShapeDtypeStruct((8, rows, width), BF16)] * spread + out_types
    n, n_swap = len(aux), len(extras)
    n_sems = 23 if spread else 10
    return pl.pallas_call(
        functools.partial(fold_kernel, mode, across, zs, width // (8 * zs), n, len(out_types), kinds),
        out_shape=out_shape + swap_shapes(1, extras, kinds),
        in_specs=[ANY, ANY, ROWS] + [ANY] * (n + n_swap),
        out_specs=[ANY] * (spread + len(out_types) + n_swap),
        scratch_shapes=[pltpu.VMEM(a.shape, a.dtype) for a in list(aux) + out_types]
        + [
            pltpu.VMEM((4, 2 * rows, depth), BF16),
            pltpu.VMEM(right.shape, BF16),
            pltpu.VMEM((4, 2, rows, width), BF16),
            pltpu.VMEM((4, rows, width), BF16),
            pltpu.VMEM((cut, width), BF16),
            pltpu.VMEM((rows - cut, width), BF16),
            pltpu.VMEM((rows, width), BF16),
            pltpu.VMEM((rows, width), BF16),
            pltpu.VMEM((rows, width), BF16),
            pltpu.VMEM((2, SLAB, width), F32),
            pltpu.SemaphoreType.DMA((n_sems,)),
            pltpu.SemaphoreType.DMA((n_sems,)),
            pltpu.SemaphoreType.DMA((5 + n + len(out_types),)),
        ]
        + (swap_scratch(1, kinds) if n_swap else []),
        compiler_params=pltpu.CompilerParams(
            collective_id=name, has_side_effects=True, vmem_limit_bytes=50 * 2**20
        ),
        cost_estimate=pl.CostEstimate(flops=0, bytes_accessed=(200 if spread else 110) * 2**20, transcendentals=0),
    )(left.reshape(4, 2 * rows, depth), right, gains, *aux, *extras)


def turn_kernel(
    zs, piece, x_ref, in_ref, out_ref, gains_ref, first_ref, grad_ref,
    all_ref, kept_ref, right_ref, result_out, d_pre_out, sums_ref, dw_out, result_ref, d_pre_ref, dw_ref,
    first, grad, w_in, kept, left, right, part, got, near_x, near_y, from_x, from_y, whole, dw, acc,
    fold_send, fold_recv, all_send, all_recv, line_send, line_recv, local, x_local
):
    rows = first.shape[0]
    tile = left.shape[2]
    wide = right.shape[2]
    y, x, c = here()
    z = lax.axis_index("z")
    to_x, to_y, to_c = {"gx": 1 - x}, {"gy": 1 - y}, {"core": 1 - c}
    chips = [(1 - y) * 2 + 1 - x, y * 2 + 1 - x, (1 - y) * 2 + x, y * 2 + x]
    me, by_x, by_y, far = place(y, x, c), place(y, 1 - x, c), place(1 - y, x, c), place(1 - y, 1 - x, c)
    other, other_x, other_y, other_far = (
        place(y, x, 1 - c),
        place(y, 1 - x, 1 - c),
        place(1 - y, x, 1 - c),
        place(1 - y, 1 - x, 1 - c),
    )
    half = rows // 2
    most = -(-half // (2 * SLAB)) * SLAB
    lows = [(0, most), (half, half - most)]
    highs = [(most, half - most), (2 * half - most, most)]
    top, bottom = pl.ds(0, half), pl.ds(half, half)
    sent = []

    def remote(sems, k, src, dst, to):
        return pltpu.make_async_remote_copy(
            src_ref=src,
            dst_ref=dst,
            send_sem=sems[0].at[k],
            recv_sem=sems[1].at[k],
            device_id=to,
            device_id_type=MESH,
        )

    def push(sems, k, src, dst, to):
        copy = remote(sems, k, src, dst, to)
        copy.start()
        sent.append(copy)

    def landed(sems, k, dst):
        remote(sems, k, dst, dst, to_c).wait_recv()

    folds, alls, lines = (fold_send, fold_recv), (all_send, all_recv), (line_send, line_recv)

    load_out = pltpu.make_async_copy(out_ref, right.at[z], local.at[0])
    load_in = pltpu.make_async_copy(in_ref, w_in, local.at[1])
    load_first = pltpu.make_async_copy(first_ref, first, local.at[2])
    load_grad = pltpu.make_async_copy(grad_ref, grad, local.at[3])

    def load_x(g):
        return pltpu.make_async_copy(x_ref.at[g], whole.at[g], x_local.at[g])


    barrier = pltpu.get_barrier_semaphore()
    for to in (to_x, to_y, to_c):
        pl.semaphore_signal(barrier, inc=1, device_id=to, device_id_type=MESH)

    @pl.when(z > 0)
    def _():
        pl.semaphore_signal(barrier, inc=1, device_id={"z": z - 1}, device_id_type=MESH)

    @pl.when(z < zs - 1)
    def _():
        pl.semaphore_signal(barrier, inc=1, device_id={"z": z + 1}, device_id_type=MESH)

    inside = (z > 0) & (z < zs - 1)

    @pl.when(inside)
    def _():
        pl.semaphore_wait(barrier, 5)

    @pl.when(jnp.logical_not(inside))
    def _():
        pl.semaphore_wait(barrier, 4)

    def shard_of(step, up):
        return z - step if up else z + step

    def hop(step, up):
        ref = right.at[shard_of(step, up)]
        src = ref if step else out_ref
        return remote(lines, 2 * step + (0 if up else 1), src, ref, {"z": z + 1 if up else z - 1})

    def sends(step, up):
        return (z >= step) & (z < zs - 1) if up else (z <= zs - 1 - step) & (z > 0)

    def gets(step, up):
        return z >= step + 1 if up else z <= zs - 2 - step

    def line_serve(step):
        for up in (True, False):

            @pl.when(gets(step - 1, up) & sends(step, up))
            def _(up=up):
                landed(lines, 2 * (step - 1) + (0 if up else 1), right.at[shard_of(step, up)])
                hop(step, up).start()

    def line_take(step):
        for up in (True, False):

            @pl.when(gets(step - 1, up) & jnp.logical_not(sends(step, up)))
            def _(up=up):
                landed(lines, 2 * (step - 1) + (0 if up else 1), right.at[shard_of(step, up)])

    for up in (True, False):

        @pl.when(sends(0, up))
        def _(up=up):
            hop(0, up).start()

    load_in.start()
    load_out.start()
    for g in range(8):
        load_x(g).start()


    load_in.wait()
    load_out.wait()

    @pl.loop(0, 8)
    def _(g):
        @pl.when(g == 6)
        def _():
            line_serve(1)

        load_x(g).wait()
        projected = dot(whole[g], w_in[...])
        gate, up = projected[:, :tile], projected[:, tile:]
        act, slope = gate_parts(gate)
        left[g] = (act * up).astype(BF16)
        kept[g] = jnp.concatenate([up * slope, act], axis=1).astype(BF16)

    load_first.start()
    load_grad.start()
    keep = pltpu.make_async_copy(kept, kept_ref, local.at[4])
    keep.start()

    def add(k, extra, start, offset, at):
        @pl.loop(0, half // SLAB)
        def _(step):
            row = pl.ds(pl.multiple_of(start + step * SLAB, SLAB), SLAB)
            of = pl.ds(pl.multiple_of(start - offset + step * SLAB, SLAB), SLAB)
            part[k, c, row, at] = (part[k, c, row, at].astype(F32) + extra[of, at].astype(F32)).astype(BF16)

    def chip_sum(k, at):
        add(k, got.at[k], 0, 0, at)
        add(k, got.at[k], half, 0, at)

    def product(k, block, at):
        found = dot(left[pl.ds(2 * chips[k], 2)].reshape(2 * rows, tile), right[block])
        part[k, 0, :, at] = found[:rows].astype(BF16)
        part[k, 1, :, at] = found[rows:].astype(BF16)

    def block_at(i):
        if i == 0:
            return z
        below = z < zs // 2
        near = jnp.where(below, z, zs - 1 - z)
        spot = jnp.where(i <= 2 * near, jnp.where(i % 2 == 1, near - (i + 1) // 2, near + i // 2), i)
        return jnp.where(below, spot, zs - 1 - spot)

    def block_cols(i):
        return pl.ds(pl.multiple_of(block_at(i) * wide, wide), wide)

    def fold_start(i):
        b, block, at = 8 * i, block_at(i), block_cols(i)
        rest = pl.ds(1, 3)
        product(0, block, at)
        push(folds, b, part.at[0, 1 - c, :, at], got.at[0, :, at], to_c)
        product(1, block, at)
        landed(folds, b, got.at[0, :, at])
        chip_sum(0, at)
        push(folds, b + 2, part.at[0, c, top, at], near_x.at[:, at], to_x)
        push(folds, b + 3, part.at[0, c, bottom, at], near_y.at[:, at], to_y)
        product(2, block, at)
        product(3, block, at)
        push(folds, b + 1, part.at[rest, 1 - c, :, at], got.at[rest, :, at], to_c)
        landed(folds, b + 1, got.at[rest, :, at])
        chip_sum(1, at)
        push(folds, b + 4, part.at[1, c, top, at], from_x.at[top, at], to_x)
        chip_sum(2, at)
        push(folds, b + 5, part.at[2, c, bottom, at], from_y.at[bottom, at], to_y)

    def fold_end(i):
        b, at = 8 * i, block_cols(i)
        landed(folds, b + 3, near_y.at[:, at])
        add(1, near_y, half, half, at)
        push(folds, b + 6, part.at[1, c, bottom, at], from_x.at[bottom, at], to_x)
        landed(folds, b + 2, near_x.at[:, at])
        add(2, near_x, 0, 0, at)
        push(folds, b + 7, part.at[2, c, top, at], from_y.at[top, at], to_y)

    gains = gains_ref[...]
    line_take(1)
    fold_start(0)
    fold_start(1)
    fold_end(0)
    for i in range(2, zs):
        if i < zs - 1:
            line_serve(i)
        fold_end(i - 1)
        line_take(i)
        fold_start(i)
    fold_end(zs - 1)
    carry = pltpu.make_async_copy(right, right_ref, local.at[5])
    carry.start()
    load_first.wait()
    load_grad.wait()
    acc[...] = jnp.zeros_like(acc)
    for i in range(zs):
        at = block_cols(i)
        landed(folds, 8 * i + 4, from_x.at[top, at])
        landed(folds, 8 * i + 5, from_y.at[bottom, at])
        landed(folds, 8 * i + 6, from_x.at[bottom, at])
        landed(folds, 8 * i + 7, from_y.at[top, at])

    def low(i):
        return pl.ds(*lows[i])

    def high(i):
        return pl.ds(*highs[i])

    def span(i):
        return pl.ds(i * half, half)

    def norm(i):
        @pl.loop(0, half // SLAB)
        def _(step):
            at = pl.ds(pl.multiple_of(i * half + step * SLAB, SLAB), SLAB)
            total = part[3, c, at].astype(F32) + got[3, at].astype(F32)
            total += from_x[at].astype(F32) + from_y[at].astype(F32)
            dy = grad[at].astype(F32)
            result, d_pre, terms = second_norm(total, first[at], dy, gains)
            result_ref[at] = result.astype(BF16)
            d_pre_ref[at] = d_pre
            whole[me, at] = d_pre.astype(BF16)
            acc[0] += terms
            acc[1] += dy

        b = 13 * i
        push(alls, b, whole.at[me, low(i)], whole.at[me, low(i)], to_x)
        push(alls, b + 1, whole.at[me, high(i)], whole.at[me, high(i)], to_y)
        push(alls, b + 2, whole.at[me, high(i)], whole.at[me, high(i)], to_x)
        push(alls, b + 3, whole.at[me, low(i)], whole.at[me, low(i)], to_y)
        push(alls, b + 4, whole.at[me, span(i)], whole.at[me, span(i)], to_c)

    def pass_on(i, k, slot, at, onward):
        ref = whole.at[slot, at]
        landed(alls, 13 * i + k, ref)
        for where, to in onward:
            push(alls, 13 * i + where, ref, ref, to)

    def spread_first(i):
        pass_on(i, 0, by_x, low(i), [(5, to_y), (7, to_c)])
        pass_on(i, 1, by_y, high(i), [(6, to_x), (8, to_c)])

    def spread_rest(i):
        pass_on(i, 2, by_x, high(i), [(9, to_c)])
        pass_on(i, 3, by_y, low(i), [(10, to_c)])

    def spread_far(i):
        pass_on(i, 5, far, low(i), [(11, to_c)])
        pass_on(i, 6, far, high(i), [(12, to_c)])

    outward = []

    def gradient(k, some=None, last=False, first_one=False):
        pair = pl.ds(2 * chips[k], 2)
        some = pl.ds(0, rows) if some is None else some
        if last or some.size == rows:
            outward.append(pltpu.make_async_copy(whole.at[pair], all_ref.at[pair], local.at[6 + k]))
            outward[-1].start()

        @pl.loop(0, zs)
        def _(block):
            at = pl.ds(pl.multiple_of(block * wide, wide), wide)
            tokens = 2 * some.size
            found = dot_rows(left[pair, some].reshape(tokens, tile), whole[pair, some, at].reshape(tokens, wide))
            if first_one:
                dw[block] = found
            elif last:
                dw_ref[block] = (dw[block] + found).astype(BF16)
                pltpu.make_async_copy(dw_ref.at[block], dw_out.at[block], x_local.at[block]).start()
            else:
                dw[block] += found

    norm(0)
    norm(1)
    stores = [
        pltpu.make_async_copy(result_ref, result_out, local.at[10]),
        pltpu.make_async_copy(d_pre_ref, d_pre_out, local.at[11]),
    ]
    for store in stores:
        store.start()
    spread_first(0)
    for i in (0, 1):
        landed(alls, 13 * i + 4, whole.at[other, span(i)])
    gradient(3, first_one=True)
    spread_rest(0)
    spread_first(1)
    spread_rest(1)
    for i in (0, 1):
        landed(alls, 13 * i + 7, whole.at[other_x, low(i)])
        landed(alls, 13 * i + 9, whole.at[other_x, high(i)])
    gradient(1)
    spread_far(0)
    for i in (0, 1):
        landed(alls, 13 * i + 8, whole.at[other_y, high(i)])
        landed(alls, 13 * i + 10, whole.at[other_y, low(i)])
    gradient(2)
    sums_ref[0:1] = jnp.sum(acc[0], axis=0, keepdims=True)
    sums_ref[1:2] = jnp.sum(acc[1], axis=0, keepdims=True)
    landed(alls, 11, whole.at[other_far, low(0)])
    landed(alls, 12, whole.at[other_far, high(0)])
    gradient(0, some=span(0))
    spread_far(1)
    landed(alls, 13 + 11, whole.at[other_far, low(1)])
    landed(alls, 13 + 12, whole.at[other_far, high(1)])
    gradient(0, some=span(1), last=True)
    for block in range(zs):
        pltpu.make_async_copy(dw_ref.at[block], dw_out.at[block], x_local.at[block]).wait()
    for copy in outward + [keep, carry] + stores:
        copy.wait()
    for copy in sent:
        copy.wait_send()
    for step in range(zs - 1):
        for up in (True, False):

            @pl.when(sends(step, up))
            def _(step=step, up=up):
                hop(step, up).wait_send()


def turn(zs, x, w_in, w_out, gains, first, grad):
    rows = x.shape[0] // 8
    units, wide = w_out.shape
    width = gains.shape[1]
    half = rows // 2
    by_z = (zs, units, wide)
    return pl.pallas_call(
        functools.partial(turn_kernel, zs, width // (8 * zs)),
        out_shape=[
            jax.ShapeDtypeStruct((8, rows, width), BF16),
            jax.ShapeDtypeStruct((8, rows, 2 * units), BF16),
            jax.ShapeDtypeStruct(by_z, BF16),
            jax.ShapeDtypeStruct((rows, width), BF16),
            jax.ShapeDtypeStruct((rows, width), F32),
            jax.ShapeDtypeStruct((8, width), F32),
            jax.ShapeDtypeStruct(by_z, BF16),
        ],
        in_specs=[ANY, ANY, ANY, ROWS, ANY, ANY],
        out_specs=[ANY] * 5 + [ROWS, ANY],
        scratch_shapes=[
            pltpu.VMEM((rows, width), BF16),
            pltpu.VMEM((rows, width), F32),
            pltpu.VMEM(by_z, BF16),
            pltpu.VMEM((rows, width), F32),
            pltpu.VMEM((rows, width), BF16),
            pltpu.VMEM(w_in.shape, BF16),
            pltpu.VMEM((8, rows, 2 * units), BF16),
            pltpu.VMEM((8, rows, units), BF16),
            pltpu.VMEM(by_z, BF16),
            pltpu.VMEM((4, 2, rows, width), BF16),
            pltpu.VMEM((4, rows, width), BF16),
            pltpu.VMEM((half, width), BF16),
            pltpu.VMEM((half, width), BF16),
            pltpu.VMEM((rows, width), BF16),
            pltpu.VMEM((rows, width), BF16),
            pltpu.VMEM((8, rows, width), BF16),
            pltpu.VMEM(by_z, F32),
            pltpu.VMEM((2, SLAB, width), F32),
            pltpu.SemaphoreType.DMA((8 * zs,)),
            pltpu.SemaphoreType.DMA((8 * zs,)),
            pltpu.SemaphoreType.DMA((26,)),
            pltpu.SemaphoreType.DMA((26,)),
            pltpu.SemaphoreType.DMA((2 * (zs - 1),)),
            pltpu.SemaphoreType.DMA((2 * (zs - 1),)),
            pltpu.SemaphoreType.DMA((12,)),
            pltpu.SemaphoreType.DMA((8,)),
        ],
        compiler_params=pltpu.CompilerParams(collective_id=1, has_side_effects=True, vmem_limit_bytes=60 * 2**20),
        cost_estimate=pl.CostEstimate(flops=0, bytes_accessed=380 * 2**20, transcendentals=0),
    )(x.reshape(8, rows, width), w_in, w_out, gains, first, grad)


def swap_kernel(zs, kinds, *refs):
    n = len(kinds)
    greet([name for _, name in swap_peers(zs, kinds)])
    swap_begin(zs, kinds, refs[:n], refs[n : 2 * n], *refs[2 * n :])()


def group_swap(name, zs, arrays, kinds):
    n = len(arrays)
    return pl.pallas_call(
        functools.partial(swap_kernel, zs, kinds),
        out_shape=swap_shapes(zs, arrays, kinds),
        in_specs=[ANY] * n,
        out_specs=[ANY] * n,
        scratch_shapes=swap_scratch(zs, kinds),
        compiler_params=pltpu.CompilerParams(collective_id=name, has_side_effects=True),
        cost_estimate=pl.CostEstimate(flops=0, bytes_accessed=50 * 2**20, transcendentals=0),
    )(*arrays)


def enter_kernel(zs, kinds, x_ref, grad_ref, *refs):
    n = len(kinds)
    blocks, x_all, grad_out, outs, refs = refs[:n], refs[n], refs[n + 1], refs[n + 2 : 2 * n + 2], refs[2 * n + 2 :]
    x_rows, sems = refs[0], refs[1:]
    rows, width = x_ref.shape
    greet([name for _, name in swap_peers(zs, kinds)])
    finish = swap_begin(zs, kinds, blocks, outs, *sems[:3])
    for ref, out in ((x_ref, x_rows), (grad_ref, grad_out)):

        @pl.loop(0, rows // SLAB)
        def _(step, ref=ref, out=out):
            at = pl.ds(pl.multiple_of(step * SLAB, SLAB), SLAB)
            out[at] = by_rows(ref[at].astype(F32), zs, width // (8 * zs)).astype(BF16)

    spread_block(rows // 2, 0, x_rows, x_all, *sems[3:])
    finish()


def enter(zs, x, grad, arrays, kinds):
    n = len(arrays)
    return pl.pallas_call(
        functools.partial(enter_kernel, zs, kinds),
        out_shape=[jax.ShapeDtypeStruct((8,) + x.shape, x.dtype), jax.ShapeDtypeStruct(grad.shape, grad.dtype)]
        + swap_shapes(zs, arrays, kinds),
        in_specs=[ROWS] * 2 + [ANY] * n,
        out_specs=[ANY, ROWS] + [ANY] * n,
        scratch_shapes=[pltpu.VMEM(x.shape, x.dtype)]
        + swap_scratch(zs, kinds)
        + [pltpu.SemaphoreType.DMA((13,)), pltpu.SemaphoreType.DMA((13,)), pltpu.SemaphoreType.DMA],
        compiler_params=pltpu.CompilerParams(collective_id=3, has_side_effects=True, vmem_limit_bytes=56 * 2**20),
        cost_estimate=pl.CostEstimate(flops=0, bytes_accessed=150 * 2**20, transcendentals=0),
    )(x, grad, *arrays)


def ff_kernel(x_ref, w_ref, hidden_ref, kept_ref):
    tile = hidden_ref.shape[1]
    projected = dot(x_ref[...], w_ref[...])
    gate, up = projected[:, :tile], projected[:, tile:]
    act, slope = gate_parts(gate)
    hidden_ref[...] = (act * up).astype(BF16)
    kept_ref[...] = jnp.concatenate([up * slope, act], axis=1).astype(BF16)


def ff_back_kernel(grad_ref, w_ref, kept_ref, out_ref):
    zs, _, wide = w_ref.shape
    d_hidden = dot_cols(grad_ref[:, :wide], w_ref[0])
    for z in range(1, zs):
        d_hidden += dot_cols(grad_ref[:, z * wide : (z + 1) * wide], w_ref[z])
    out_ref[...] = (jnp.concatenate([d_hidden, d_hidden], axis=1) * kept_ref[...].astype(F32)).astype(BF16)


FF_ROWS = 256


def ff_rows(width):
    return pl.BlockSpec((FF_ROWS, width), lambda i: (i, 0))


def ff_forward(x, w):
    rows, depth = x.shape
    wide = w.shape[1]
    return pl.pallas_call(
        ff_kernel,
        grid=(rows // FF_ROWS,),
        in_specs=[ff_rows(depth), pl.BlockSpec((depth, wide), lambda i: (0, 0))],
        out_specs=[ff_rows(wide // 2), ff_rows(wide)],
        out_shape=[jax.ShapeDtypeStruct((rows, wide // 2), BF16), jax.ShapeDtypeStruct((rows, wide), BF16)],
        compiler_params=PARAMS,
        cost_estimate=pl.CostEstimate(flops=2 * rows * depth * wide, bytes_accessed=20 * 2**20, transcendentals=0),
    )(x, w)


def ff_backward(grad, w, kept):
    rows, depth = grad.shape
    wide = kept.shape[1]
    return pl.pallas_call(
        ff_back_kernel,
        grid=(rows // FF_ROWS,),
        in_specs=[ff_rows(depth), pl.BlockSpec(w.shape, lambda i: (0, 0, 0)), ff_rows(wide)],
        out_specs=ff_rows(wide),
        out_shape=jax.ShapeDtypeStruct((rows, wide), BF16),
        compiler_params=PARAMS,
        cost_estimate=pl.CostEstimate(flops=rows * depth * wide, bytes_accessed=20 * 2**20, transcendentals=0),
    )(grad, w, kept)


def cut_kernel(in_ref, out_ref, in_blocks, out_blocks, wide):
    group, _, double = in_blocks.shape
    tile, ff = double // 2, out_ref.shape[1]
    span = group * tile
    odd = ff % 128
    live = lax.broadcasted_iota(jnp.int32, (in_ref.shape[0], span), 1) < ff
    wide[...] = jnp.zeros_like(wide)
    wide[:, : 2 * ff] = in_ref[...].astype(F32)
    gate = jnp.where(live, wide[:, :span], 0.0)
    up = pltpu.roll(wide[:, ff - odd : ff - odd + span], span - odd, 1)
    up = jnp.where(live, up, 0.0)
    wide[:, :span] = jnp.zeros_like(live, F32)
    wide[:, :ff] = out_ref[...].astype(F32)
    down = wide[:, :span]
    for g in range(group):
        at = slice(g * tile, (g + 1) * tile)
        in_blocks[g] = jnp.concatenate([gate[:, at], up[:, at]], axis=1).astype(BF16)
        out_blocks[g] = down[:, at].astype(BF16)


def cut_ff(w_in, w_out, group, tile):
    rows, ff = w_out.shape
    return pl.pallas_call(
        cut_kernel,
        grid=(rows // 16,),
        in_specs=[pl.BlockSpec((16, 2 * ff), lambda i: (i, 0)), pl.BlockSpec((16, ff), lambda i: (i, 0))],
        out_specs=[
            pl.BlockSpec((group, 16, 2 * tile), lambda i: (0, i, 0)),
            pl.BlockSpec((group, 16, tile), lambda i: (0, i, 0)),
        ],
        out_shape=[
            jax.ShapeDtypeStruct((group, rows, 2 * tile), BF16),
            jax.ShapeDtypeStruct((group, rows, tile), BF16),
        ],
        scratch_shapes=[pltpu.VMEM((16, -(-(ff + group * tile) // 128) * 128), F32)],
        compiler_params=SMALL,
    )(w_in, w_out)


def join_kernel(in_blocks, out_blocks, in_ref, out_ref):
    group, _, double = in_blocks.shape
    tile, ff = double // 2, out_ref.shape[1]
    odd = ff % 128
    blocks = [in_blocks[g].astype(F32) for g in range(group)]
    gate = jnp.concatenate([block[:, :tile] for block in blocks], axis=1)
    up = jnp.concatenate([block[:, tile:] for block in blocks], axis=1)
    up = pltpu.roll(up, odd, 1)
    lane = lax.broadcasted_iota(jnp.int32, (up.shape[0], 128), 1)
    in_ref[:, : ff - odd] = gate[:, : ff - odd]
    in_ref[:, ff - odd : ff - odd + 128] = jnp.where(lane < odd, gate[:, ff - odd : ff - odd + 128], up[:, :128])
    in_ref[:, ff - odd + 128 :] = up[:, 128 : ff + odd]
    down = jnp.concatenate([out_blocks[g].astype(F32) for g in range(group)], axis=1)
    out_ref[...] = down[:, :ff]


def join_ff(in_blocks, out_blocks, ff):
    group, rows, tile = out_blocks.shape
    return pl.pallas_call(
        join_kernel,
        grid=(rows // 16,),
        in_specs=[
            pl.BlockSpec((group, 16, 2 * tile), lambda i: (0, i, 0)),
            pl.BlockSpec((group, 16, tile), lambda i: (0, i, 0)),
        ],
        out_specs=[pl.BlockSpec((16, 2 * ff), lambda i: (i, 0)), pl.BlockSpec((16, ff), lambda i: (i, 0))],
        out_shape=[jax.ShapeDtypeStruct((rows, 2 * ff), F32), jax.ShapeDtypeStruct((rows, ff), F32)],
        compiler_params=SMALL,
    )(in_blocks, out_blocks)


def closing_kernel(zs, sum_ref, rows_ref, qkv_ref, total_ref, got, lines, *refs):
    send, recv, local, line_send, line_recv = refs
    y, x, c = here()
    z = lax.axis_index("z")
    me = place(y, x, c)
    wide = got.shape[2]
    width = wide // 3
    piece = got.shape[1]
    found = swap_peers(zs, ("line",))
    greet([name for _, name in found])
    copies, comes = [], []
    for k, (peer, name) in enumerate(found[:7]):
        sems = dict(send_sem=send.at[k], recv_sem=recv.at[k], device_id=name, device_id_type=MESH)
        copies.append(pltpu.make_async_remote_copy(src_ref=rows_ref.at[peer], dst_ref=got.at[me], **sems))
        comes.append(pltpu.make_async_remote_copy(src_ref=got.at[peer], dst_ref=got.at[peer], **sems))
    for k, (peer, name) in enumerate(found[7:]):
        sems = dict(send_sem=line_send.at[k], recv_sem=line_recv.at[k], device_id=name, device_id_type=MESH)
        copies.append(pltpu.make_async_remote_copy(src_ref=sum_ref, dst_ref=lines.at[z], **sems))
        comes.append(pltpu.make_async_remote_copy(src_ref=lines.at[peer], dst_ref=lines.at[peer], **sems))
    for copy in copies:
        copy.start()
    keeps = [
        pltpu.make_async_copy(rows_ref.at[me], got.at[me], local.at[0]),
        pltpu.make_async_copy(sum_ref, lines.at[z], local.at[1]),
    ]
    for keep in keeps:
        keep.start()
    for come in comes:
        come.wait_recv()
    for keep in keeps:
        keep.wait()
    for g in range(8):
        for j in range(3):
            at = pl.ds(j * D + g * width, width)
            qkv_ref[:, at] = got[g, :, j * width : (j + 1) * width].astype(F32)
    total = lines[0]
    for k in range(1, zs):
        total += lines[k]
    part = total[:, :piece]
    for k in range(1, zs):
        part = jnp.where(z == k, total[:, k * piece : (k + 1) * piece], part)
    total_ref[...] = part
    for copy in copies:
        copy.wait_send()


def closing(zs, sums, rows):
    _, piece, columns = rows.shape
    width = columns // 3
    return pl.pallas_call(
        functools.partial(closing_kernel, zs),
        out_shape=[
            jax.ShapeDtypeStruct((piece, 3 * D), F32),
            jax.ShapeDtypeStruct((8, piece), F32),
        ],
        in_specs=[ROWS, ANY],
        out_specs=[ROWS] * 2,
        scratch_shapes=[
            pltpu.VMEM((8, piece, 3 * width), BF16),
            pltpu.VMEM((zs, 8, width), F32),
            pltpu.SemaphoreType.DMA((7,)),
            pltpu.SemaphoreType.DMA((7,)),
            pltpu.SemaphoreType.DMA((2,)),
            pltpu.SemaphoreType.DMA((zs - 1,)),
            pltpu.SemaphoreType.DMA((zs - 1,)),
        ],
        compiler_params=pltpu.CompilerParams(collective_id=5, has_side_effects=True, vmem_limit_bytes=24 * 2**20),
        cost_estimate=pl.CostEstimate(flops=0, bytes_accessed=50 * 2**20, transcendentals=0),
    )(sums, rows)


def on_device(sizes, x_in, d_out, w_qkv, w_dense, w_in, w_out, gone, bone, gtwo, btwo, flags, span_start, span_len):
    gy, gx, cores, zs = sizes
    piece = w_qkv.shape[0]
    ff = w_out.shape[1]
    group = gy * gx * cores
    width = D // group
    tile = -(-ff // (group * 64)) * 64
    own = gy == 2

    def permute(array):
        lead = array.shape[:-1]
        return jnp.swapaxes(array.reshape(lead + (group, zs, piece)), -3, -2).reshape(lead + (D,))

    def restore(array):
        lead = array.shape[:-1]
        return jnp.swapaxes(array.reshape(lead + (zs, group, piece)), -3, -2).reshape(lead + (D,))

    def swap(name, arrays, kinds):
        if own:
            return group_swap(name, zs, arrays, kinds)
        ways = {
            "swap": lambda a: lax.all_to_all(a, GROUP, 0, 0, tiled=True),
            "group": lambda a: lax.all_gather(a, GROUP, axis=0),
            "line": lambda a: lax.all_gather(a, "z", axis=0),
        }
        return [ways[k](a) for a, k in zip(arrays, kinds)]

    def spread_rows(block):
        return lax.all_gather(block, GROUP, axis=0, tiled=True)

    rows_f32 = jax.ShapeDtypeStruct((SEQ_LEN, D), F32)
    rows_low = jax.ShapeDtypeStruct((SEQ_LEN, D), BF16)
    sums_type = jax.ShapeDtypeStruct((8, D), F32)

    def fold(partial):
        return lax.psum_scatter(partial.astype(BF16), GROUP, scatter_dimension=0, tiled=True).astype(F32)

    def stack_sums(*arrays):
        return jnp.pad(jnp.stack([jnp.sum(a, axis=0) for a in arrays]), ((0, 6), (0, 0)))

    def fold_one(left, right, x, gains):
        if own:
            kinds = [rows_f32, rows_f32, jax.ShapeDtypeStruct((SEQ_LEN, 128), F32)]
            whole, first, normal, inverse = group_fold(0, zs, "one", left, right, gains, [x], kinds)
            return whole.reshape(left.shape[0], D), first, normal, inverse
        first, normal, inverse = first_norm(permute(deep_alpha * x.astype(F32) + fold(dot(left, right))), gains)
        return spread_rows(first.astype(BF16)), first, normal, inverse

    def ff_turn(x, w_in, w_out, first, grad, gains):
        if own:
            whole, kept, w_out, result, d_pre, sums, d_out = turn(zs, x, w_in, w_out, gains, first, grad)
            rows = x.shape[0]
            return whole.reshape(rows, D), kept.reshape(rows, -1), w_out, result, d_pre, sums, d_out
        w_out = lax.all_gather(w_out, "z", axis=0)
        hidden, kept = ff_forward(x, w_in)
        grad = grad.astype(F32)
        right = jnp.swapaxes(w_out, 0, 1).reshape(-1, D)
        result, d_pre, terms = second_norm(fold(dot(hidden, right)), first, grad, gains)
        whole = spread_rows(d_pre.astype(BF16))
        d_out = jnp.swapaxes(dot_rows(hidden, whole).reshape(-1, zs, D // zs), 0, 1).astype(BF16)
        return whole, kept, w_out, result.astype(BF16), d_pre, stack_sums(terms, grad), d_out

    def fold_back(left, right, d_pre_two, normal, inverse, gains):
        if own:
            kinds = [rows_f32, sums_type]
            whole, d_pre, sums = group_fold(7, zs, "back", left, right, gains, [d_pre_two, normal, inverse], kinds)
            return whole.reshape(left.shape[0], D), d_pre, sums
        d_pre, terms, d_first = first_back(fold(dot_cols(left, right)), d_pre_two, normal, inverse, gains)
        return spread_rows(restore(d_pre).astype(BF16)), d_pre, stack_sums(terms, d_first)

    def fold_last(left, right, d_pre, gains, extras, kinds):
        if own:
            return group_fold(8, zs, "last", left, right, gains, [d_pre], [rows_low], extras, kinds)
        out = restore((deep_alpha * d_pre + fold(dot_cols(left, right))).astype(BF16))
        return [out] + swap(8, extras, kinds)

    def gather(block):
        return lax.all_gather(block, "z", axis=0, tiled=True)

    def scatter(partial):
        return lax.psum_scatter(partial.astype(BF16), "z", scatter_dimension=0, tiled=True)

    masked = jnp.max(flags) > 0
    prefix = jnp.where(masked, SEQ_LEN, SEQ_LEN - span_len[0])
    info = jnp.concatenate([gone, bone, gtwo, btwo, jnp.stack([prefix, span_start[0]]).astype(BF16)])
    info = jnp.pad(info[None, :], ((0, 15), (0, -info.shape[0] % 128)))

    qkv_blocks = jnp.moveaxis(w_qkv.reshape(piece, 3, group, width), 2, 0).reshape(group, piece, 3 * width)
    w_dense_part = gather(w_dense)
    qkv_blocks, info = swap(2, [qkv_blocks, info], ("swap", "group"))
    w_qkv_part = gather(qkv_blocks.reshape(group * piece, 3 * width))
    info = info[:, 0]
    place_info = info[:, 4 * piece : 4 * piece + 2].astype(jnp.int32)
    prefix, start = place_info[:, 0], place_info[:, 1]
    cosine, sine = tables(prefix, start)
    in_blocks, out_blocks = cut_ff(w_in, w_out, group, tile)
    info = jnp.pad(info, ((0, -group % 16), (0, 0)))
    in_blocks, out_blocks, qkv_blocks, w_dense_part, cosine, sine = lax.optimization_barrier(
        (in_blocks, out_blocks, qkv_blocks, w_dense_part, cosine, sine)
    )
    swapped, kinds = [in_blocks, out_blocks, info], ("swap", "swap", "line")
    if own:
        x_all, grad_two, in_blocks, out_blocks, info = enter(zs, x_in, d_out, swapped, kinds)
        x_all = x_all.reshape(group * SEQ_LEN, D)
    else:
        x_all, grad_two = spread_rows(permute(x_in)), permute(d_out)
        in_blocks, out_blocks, info = swap(3, swapped, kinds)
    w_in_part = gather(in_blocks.reshape(group * piece, 2 * tile))
    out_rows = out_blocks.reshape(group * piece, tile).T
    gains = info[:, :group, : 4 * piece].astype(F32).reshape(zs, group, 4, piece)
    gains = jnp.pad(jnp.transpose(gains, (2, 0, 1, 3)).reshape(4, D), ((0, 4), (0, 0)))
    w_qkv_part, x_all, gains, out_rows = lax.optimization_barrier((w_qkv_part, x_all, gains, out_rows))
    packed = dot(x_all, w_qkv_part)
    qkv, context = attend(prefix, packed, cosine, sine)
    first_all, first, normal_one, inverse_one = fold_one(context, w_dense_part, x_in, gains)
    d_branch, kept, w_out_part, layer_out, d_pre_two, sums_two, d_w_out = ff_turn(
        first_all, w_in_part, out_rows, first, grad_two, gains
    )
    layer_out = restore(layer_out)
    d_w_out = lax.psum_scatter(d_w_out, "z", scatter_dimension=0)
    d_projected = ff_backward(d_branch, w_out_part, kept)
    d_w_in = dot_rows(first_all, d_projected).astype(BF16)
    d_w_in, d_projected = lax.optimization_barrier((d_w_in, d_projected))
    d_w_in = scatter(d_w_in)
    d_attn, d_pre_one, sums_one = fold_back(d_projected, w_in_part, d_pre_two, normal_one, inverse_one, gains)
    d_attn, d_w_out = lax.optimization_barrier((d_attn, d_w_out))
    d_context = dot_cols(d_attn, w_dense_part).astype(BF16)
    d_packed = attend_back(prefix, qkv, d_context, cosine, sine)
    d_w_qkv = dot_rows(x_all, d_packed).astype(BF16)
    sums = jnp.concatenate([sums_one[:2], sums_two[:2], jnp.zeros((4, D), F32)])
    d_w_qkv = with_layout_constraint(d_w_qkv, Layout((0, 1)))
    d_dense = dot_rows(context, d_attn).astype(BF16)
    d_packed, d_w_qkv, d_w_in, sums, d_dense = lax.optimization_barrier((d_packed, d_w_qkv, d_w_in, sums, d_dense))
    d_w_qkv = scatter(d_w_qkv)
    d_dense = scatter(d_dense)
    d_w_in, d_w_out = d_w_in.reshape(group, piece, 2 * tile), d_w_out.T.reshape(group, piece, tile)
    d_input, d_w_in, d_w_out, sums = fold_last(
        d_packed, w_qkv_part, d_pre_one, gains, [d_w_in, d_w_out, sums], ("swap", "swap", "group")
    )
    sums = jnp.sum(sums, axis=0).reshape(8, zs, group, piece)
    sums = lax.dynamic_index_in_dim(sums, lax.axis_index(GROUP), 2, keepdims=False).reshape(8, width)
    out_in, out_out = join_ff(d_w_in, d_w_out, ff)
    out_in, out_out, d_input, d_w_qkv, sums = lax.optimization_barrier((out_in, out_out, d_input, d_w_qkv, sums))
    if own:
        out_qkv, sums = closing(zs, sums, d_w_qkv.reshape(group, piece, 3 * width))
    else:
        d_w_qkv, sums = swap(5, [d_w_qkv.reshape(group, piece, 3 * width), sums], ("swap", "line"))
        out_qkv = jnp.transpose(d_w_qkv.astype(F32).reshape(group, piece, 3, width), (1, 2, 0, 3))
        out_qkv = out_qkv.reshape(piece, 3 * D)
        sums = jnp.sum(sums, axis=0).reshape(8, zs, piece)
        sums = lax.dynamic_index_in_dim(sums, lax.axis_index("z"), 1, keepdims=False)
    out_qkv, sums, d_dense = lax.optimization_barrier((out_qkv, sums, d_dense))
    out_dense = d_dense.astype(F32)
    return layer_out, d_input, out_qkv, out_dense, out_in, out_out, sums[0], sums[1], sums[2], sums[3]


def solution(mesh):
    grp, shard = mesh.shape["grp"], mesh.shape["shard"]
    sizes = (grp // 4, 2, 2, shard)
    inner = Mesh(mesh.devices.reshape(sizes), ALL)
    rows, flat = P(ALL, None), P(ALL)
    return jax.shard_map(
        functools.partial(on_device, sizes),
        mesh=inner,
        in_specs=(rows,) * 6 + (flat,) * 7,
        out_specs=(rows,) * 6 + (flat,) * 4,
        check_vma=False,
    )
```
